32 devices in a mesh: dp: 16 (over z, y, x), own: 2 (over core).
Axes of the slice: x: 2, y: 2, z: 4, core: 2. Of those that a mesh axis runs over, the one named last changes fastest.
Arguments:
- tokens: bfloat16 [32, 577, 768], P(('dp', 'own')), may hold values from -6 to 6
- cotangent: bfloat16 [32, 577, 768], P(('dp', 'own')), may hold values from -6 to 6
- selected: int32 [32, 577], P(('dp', 'own')), may hold values from 0 to 1, as said below
- packing: int32 [32, 256], P(('dp', 'own')), may hold values from 0 to 255, each once within a row
- segments: int32 [32, 256], P(('dp', 'own')), may hold values from 0 to 7, never falling along the last dimension, each value on 1 to 64 neighbouring positions
- blocks: float32 [768, 12, 768], P('dp', 'own')
- left_stat: float32 [768, 12, 768], P('dp', 'own'), as said below
- right_stat: float32 [768, 12, 768], P('dp', 'own'), as said below
- left_root: float32 [768, 12, 768], P('dp', 'own')
- right_root: float32 [768, 12, 768], P('dp', 'own')
- vectors: float32 [5, 768], replicated
- moment: float32 [5, 768], replicated
Outputs:
- mixed: bfloat16 [32, 577, 768], P(('dp', 'own'))
- grad_tokens: bfloat16 [32, 577, 768], P(('dp', 'own'))
- block_grads: float32 [768, 12, 768], P('dp', 'own')
- left_stats: float32 [768, 12, 768], P('dp', 'own')
- right_stats: float32 [768, 12, 768], P('dp', 'own')
- new_blocks: float32 [768, 12, 768], P('dp', 'own')
- vector_grads: float32 [5, 768], replicated
- vector_moment: float32 [5, 768], replicated
- new_vectors: float32 [5, 768], replicated
The draws below stay inside these ranges and needn't reach their ends.
Inputs may be any that keep to these rules, and one draw needn't show every extreme that they name: `selected`: each row holds exactly 256 ones. `packing`: each row is a permutation of 0 to 255. `segments`: ids never fall along a row; each id covers 1 to 64 positions, one exactly 64. `left_stat`: symmetric in the first and last index for each block. `right_stat`: symmetric in the first and last index for each block.
All inputs are finite; a program needn't handle non-finite values.
Results may differ from the reference program's by a relative error of at most 0.011.
Values may be sent and summed in bfloat16 or wider, within the bound.
No kernel may reach another device: no remote copies, remote signals or barrier semaphores. Data moves between devices by JAX's collectives and lax.ppermute only.
A program may use at most 256 MiB of HBM per device.

```python
import math
import jax
import jax.numpy as jnp
import numpy as np
from jax import lax

D = 768
HEAD_DIM = 64
FF = 3072
S = 577
CAP = 256
ROWS_DEV = 1
NB = 12
GROUPS = 32
ROWS = 32
M = 256
SELECTED = 8192
TOKENS_ALL = 18464
N_DP = 16
N_OWN = 2


def gradient_sizes():
    selected_root = math.sqrt(SELECTED)
    every_root = math.sqrt(TOKENS_ALL)
    up_blocks = FF // D
    entry_sizes = [0.8 * selected_root] * 3 + [0.15 * selected_root]
    entry_sizes = entry_sizes + [0.35 * every_root] * up_blocks + [0.6 * every_root] * up_blocks
    return jnp.array(entry_sizes, jnp.float32)


def identity_table():
    return (jnp.arange(D)[:, None] == jnp.arange(D)[None, :]).astype(jnp.float32)


def statistics(key):
    squared = gradient_sizes() ** 2
    first_key, second_key = jax.random.split(key)
    diagonal = D * squared[None, :] * jax.random.uniform(first_key, (D, NB), jnp.float32, 1.0, 4.0)
    jitter = jnp.clip(jax.random.normal(second_key, (D, NB, D), jnp.float32), -4.0, 4.0)
    off_diag = (jitter + jnp.transpose(jitter, (2, 1, 0))) * (0.4 * 0.7071 * math.sqrt(D)) * squared[None, :, None]
    identity = identity_table()
    return off_diag * (1.0 - identity)[:, None, :] + diagonal[:, :, None] * identity[:, None, :]


def root_matrix(key, diagonal):
    jitter = jnp.clip(jax.random.normal(key, (D, NB, D), jnp.float32), -4.0, 4.0)
    off_diag = jitter * (0.4 / math.sqrt(D)) * jnp.sqrt(diagonal[:, :, None] * jnp.transpose(diagonal)[None, :, :])
    identity = identity_table()
    return off_diag * (1.0 - identity)[:, None, :] + diagonal[:, :, None] * identity[:, None, :]


def draw_selected(key, part):
    key = jax.random.fold_in(key, 1)
    positions = jnp.broadcast_to(jnp.arange(S, dtype=jnp.int32)[None, :], (ROWS, S))
    shuffled = jax.random.permutation(key, positions, axis=1, independent=True)
    return (shuffled < CAP).astype(jnp.int32)


def draw_blocks(key, part):
    key = jax.random.fold_in(key, 2)
    number = jnp.arange(NB)
    block_scale = jnp.where(number == 3, (D // 32) ** (-0.5), D ** (-0.5))
    block_scale = jnp.where(number >= 4 + FF // D, FF ** (-0.5), block_scale)
    jitter = jnp.clip(jax.random.normal(key, (D, NB, D), jnp.float32), -4.0, 4.0)
    return jitter * block_scale[None, :, None]


def draw_left_stat(key, part):
    key = jax.random.fold_in(key, 3)
    return statistics(key)


def draw_right_stat(key, part):
    key = jax.random.fold_in(key, 4)
    return statistics(key)


def draw_left_root(key, part):
    key = jax.random.fold_in(key, 5)
    first_key, second_key = jax.random.split(key)
    rising = 3.0 ** (jnp.arange(D, dtype=jnp.float32) / (D - 1))
    factor = jnp.exp(jax.random.uniform(first_key, (D, NB), jnp.float32, 0.0, math.log(4.0)))
    return root_matrix(second_key, rising[:, None] * factor)


def draw_right_root(key, part):
    key = jax.random.fold_in(key, 6)
    first_key, second_key = jax.random.split(key)
    factor = jnp.exp(jax.random.uniform(first_key, (D, NB), jnp.float32, 0.0, math.log(10.0)))
    return root_matrix(second_key, factor)


def draw_vectors(key, part):
    key = jax.random.fold_in(key, 7)
    key_list = jax.random.split(key, 5)
    rising = 0.7 + 0.6 * jnp.arange(D, dtype=jnp.float32) / (D - 1)
    gain_one = rising * jax.random.uniform(key_list[0], (D,), jnp.float32, 0.8, 1.25)
    bias_one = 0.3 * jnp.clip(jax.random.normal(key_list[1], (D,), jnp.float32), -4.0, 4.0)
    router = jnp.clip(jax.random.normal(key_list[2], (D,), jnp.float32), -4.0, 4.0) * D ** (-0.5)
    gain_two = rising * jax.random.uniform(key_list[3], (D,), jnp.float32, 0.8, 1.25)
    bias_two = 0.3 * jnp.clip(jax.random.normal(key_list[4], (D,), jnp.float32), -4.0, 4.0)
    return jnp.stack([gain_one, bias_one, router, gain_two, bias_two])


def draw_moment(key, part):
    key = jax.random.fold_in(key, 8)
    selected_root = math.sqrt(SELECTED)
    every_root = math.sqrt(TOKENS_ALL)
    row_sizes = jnp.array([0.7 * selected_root, 0.7 * selected_root, 7.0 * selected_root, 0.7 * every_root, 0.7 * every_root], jnp.float32)
    jitter = jnp.clip(jax.random.normal(key, (5, D), jnp.float32), -4.0, 4.0)
    return jitter * row_sizes[:, None]


def shard_levels(own_key, extent, cuts, smallest, high):
    loudness = 1.0
    for dim, blocks in cuts:
        draws = jax.random.uniform(jax.random.fold_in(jax.random.fold_in(own_key, 6), dim), (blocks,), jnp.float32, smallest / len(cuts), high / len(cuts))
        loudness = loudness * jnp.repeat(jnp.exp(draws), extent[dim] // blocks).reshape((-1,) + (1,) * (len(extent) - 1 - dim))
    return loudness


def length_profile(amount, total, reach, skew):
    loads = [(1 << 20) // math.isqrt(grade ** skew) + 1 for grade in range(2, amount + 1)]
    surplus, counts = total - reach - (amount - 1), [1] * (amount - 1)
    while surplus > 0:
        movable = [i for i in range(amount - 1) if counts[i] < reach]
        whole, remaining = sum([loads[i] for i in movable]), surplus
        for i in movable:
            addition = min(reach - counts[i], max(1, remaining * loads[i] // whole), surplus)
            counts[i] = counts[i] + addition
            surplus = surplus - addition
    return np.array([reach] + counts)


def uneven(rng, amount, total, limit, lean):
    if amount == 2:
        one = jax.random.randint(rng, (), max(1, total - limit), min(limit, total - 1) + 1)
        return jnp.stack([one, total - one])
    tallies = jnp.asarray(length_profile(amount, total, limit, lean), jnp.int32)
    pairs = (amount - 1) // 2
    donor, receiver = tallies[1:1 + 2 * pairs:2], tallies[2:2 + 2 * pairs:2]
    margin = jnp.minimum(donor - 1, limit - receiver)
    passed = jax.random.randint(jax.random.fold_in(rng, 1), (pairs,), 0, 1 << 20) % (margin + 1)
    tallies = tallies.at[1:1 + 2 * pairs:2].set(donor - passed).at[2:2 + 2 * pairs:2].set(receiver + passed)
    return tallies[jax.random.permutation(jax.random.fold_in(rng, 2), amount)]


def bell_draw(own_key, extent, scale, reach, pieces=(), kind=jnp.bfloat16):
    values = scale * jax.random.normal(own_key, extent, jnp.float32)
    if pieces:
        values = values * shard_levels(own_key, extent, pieces, -0.22, 0.18)
    return jnp.clip(values, -reach, reach).astype(kind)


def setup_inputs(seed: int = 0) -> dict:
    seeds = jax.random.split(jax.random.key(seed), 13)
    return {
        "tokens": bell_draw(seeds[0], (ROWS, S, D), 1.0, 6.0, ((0, 32),)),
        "cotangent": bell_draw(seeds[1], (ROWS, S, D), 1.0, 6.0, ((0, 32),)),
        "selected": draw_selected(jax.random.fold_in(seeds[12], 71), 0),
        "packing": jax.vmap(lambda own: jax.random.permutation(own, M))(jax.random.split(seeds[3], GROUPS)).reshape((GROUPS, M)).astype(jnp.int32),
        "segments": jax.vmap(lambda own: jnp.searchsorted(jnp.cumsum(uneven(own, 8, M, M // 4, 0)), jnp.arange(M), side="right"))(jax.random.split(seeds[4], GROUPS)).reshape((GROUPS, M)).astype(jnp.int32),
        "blocks": draw_blocks(jax.random.fold_in(seeds[12], 71), 0),
        "left_stat": draw_left_stat(jax.random.fold_in(seeds[12], 71), 0),
        "right_stat": draw_right_stat(jax.random.fold_in(seeds[12], 71), 0),
        "left_root": draw_left_root(jax.random.fold_in(seeds[12], 71), 0),
        "right_root": draw_right_root(jax.random.fold_in(seeds[12], 71), 0),
        "vectors": draw_vectors(jax.random.fold_in(seeds[12], 71), 0),
        "moment": draw_moment(jax.random.fold_in(seeds[12], 71), 0),
    }


norm_eps = 1e-06
block_rate = 0.03
vector_rate = 0.04
highest = lax.Precision.HIGHEST

@jax.custom_vjp
def low(v):
    return lax.optimization_barrier(v.astype(jnp.bfloat16)).astype(jnp.float32)

@jax.custom_vjp
def low_back(v):
    return v

def low_keep(v):
    return (low(v), None)

def low_pass(kept, grad):
    return (grad,)

def back_keep(v):
    return (v, None)

def back_low(kept, grad):
    return (low(grad),)
low.defvjp(low_keep, low_pass)
low_back.defvjp(back_keep, back_low)

def layer_norm(values, norm_gain, norm_bias):
    center = values - lax.optimization_barrier(jnp.mean(values, axis=-1, keepdims=True))
    spread = lax.optimization_barrier(jnp.mean(center * center, axis=-1, keepdims=True))
    return center * lax.rsqrt(spread + norm_eps) * norm_gain + norm_bias

def slot_table(chosen, packing_row):
    before = (jnp.cumsum(chosen) - 1).astype(jnp.int32)
    safe_index = jnp.clip(before, 0, M - 1).astype(jnp.int32)
    return jnp.where(chosen == 1, packing_row[safe_index], -1).astype(jnp.int32)

def source_table(slot_index):
    targets = jnp.where(slot_index >= 0, slot_index, M).astype(jnp.int32)
    tokens_here = jnp.arange(slot_index.shape[0], dtype=jnp.int32)
    return jnp.zeros((M,), jnp.int32).at[targets].set(tokens_here, mode='drop')

def reorder(buffers):
    grid_view = buffers.reshape(N_DP, N_OWN, N_DP, M // N_DP, D)
    return jnp.transpose(grid_view, (2, 1, 0, 3, 4)).reshape(N_DP * N_OWN, M, D)

def attend(buffer, segment, w_query, w_key, w_value, w_out):
    buffer = low_back(buffer)
    head_count = D // HEAD_DIM

    def project(matrix):
        made = low_back(low(jnp.dot(buffer, matrix, precision=highest)))
        return made.reshape(M, head_count, HEAD_DIM)
    query_rows = project(w_query)
    key_rows = project(w_key)
    value_rows = project(w_value)
    scores = jnp.einsum('qhd,khd->hqk', query_rows, key_rows, precision=highest) * HEAD_DIM ** (-0.5)
    scores = low_back(scores)
    same_segment = segment[:, None] == segment[None, :]
    scores = jnp.where(same_segment[None, :, :], scores, -1e+30)
    shares = low(jax.nn.softmax(scores, axis=-1))
    context = jnp.einsum('hqk,khd->qhd', shares, value_rows, precision=highest).reshape(M, D)
    context = low_back(low(context))
    return low(jnp.dot(context, w_out, precision=highest))

def reference(tokens, cotangent, selected, packing, segments, blocks, left_stat, right_stat, left_root, right_root, vectors, moment):
    devices = N_DP * N_OWN
    token_count = ROWS_DEV * S
    up_blocks = FF // D
    inputs = tokens.astype(jnp.float32).reshape(devices, token_count, D)
    chosen = selected.reshape(devices, token_count)
    slot_index = jax.vmap(slot_table)(chosen, packing)
    sources = jax.vmap(source_table)(slot_index)

    def forward(inputs, blocks, vectors):
        matrices = low(blocks)
        w_query = matrices[:, 0, :]
        w_key = matrices[:, 1, :]
        w_value = matrices[:, 2, :]
        w_out = matrices[:, 3, :]
        w_up = jnp.concatenate([matrices[:, 4 + position, :] for position in range(up_blocks)], axis=1)
        w_down = jnp.concatenate([matrices[:, 4 + up_blocks + position, :] for position in range(up_blocks)], axis=0)

        def first_part(item_pair):
            values, source = item_pair
            normed = low(layer_norm(values, vectors[0], vectors[1]))
            gate_values = jax.nn.sigmoid(jnp.dot(normed, vectors[2], precision=highest))
            return (gate_values, normed[source])
        gate_values, packed = lax.map(jax.checkpoint(first_part), (inputs, sources))
        buffers = reorder(packed)

        def middle(item_pair):
            return attend(item_pair[0], item_pair[1], w_query, w_key, w_value, w_out)
        answers = lax.map(jax.checkpoint(middle), (buffers, segments))
        returned = low_back(reorder(answers))

        def last_part(group_args):
            values, gate_row, slot_row, flag_row, answer_rows = group_args
            weighting = jnp.where(flag_row == 1, gate_row, 0.0)
            picked = answer_rows[jnp.clip(slot_row, 0, M - 1)]
            hidden = values + weighting[:, None] * picked
            normed = low(layer_norm(hidden, vectors[3], vectors[4]))
            pre_active = low_back(jnp.dot(normed, w_up, precision=highest))
            active = low(jax.nn.gelu(pre_active, approximate=False))
            return hidden + jnp.dot(active, w_down, precision=highest)
        return lax.map(jax.checkpoint(last_part), (inputs, gate_values, slot_index, chosen, returned))
    output, pullback = jax.vjp(forward, inputs, blocks, vectors)
    grad_inputs, grad_blocks, grad_vectors = pullback(cotangent.astype(jnp.float32).reshape(devices, token_count, D))
    mixed = output.astype(jnp.bfloat16).reshape(ROWS, S, D)
    grad_tokens = grad_inputs.astype(jnp.bfloat16).reshape(ROWS, S, D)
    left_new = 0.5 * left_stat + 0.5 * jnp.einsum('ibk,jbk->ibj', grad_blocks, grad_blocks, precision=highest)
    right_new = 0.5 * right_stat + 0.5 * jnp.einsum('kbi,kbj->ibj', grad_blocks, grad_blocks, precision=highest)
    lefted = jnp.einsum('ibk,kbj->ibj', left_root, grad_blocks, precision=highest)
    precond = jnp.einsum('ibk,kbj->ibj', lefted, right_root, precision=highest)
    mean_squares = lax.optimization_barrier(jnp.mean(precond * precond, axis=(0, 2)))
    new_blocks = blocks - block_rate * precond * lax.rsqrt(mean_squares + norm_eps)[None, :, None]
    moment_new = 0.5 * moment + 0.5 * grad_vectors
    row_squares = lax.optimization_barrier(jnp.mean(moment_new * moment_new, axis=1, keepdims=True))
    new_vectors = vectors - vector_rate * moment_new * lax.rsqrt(row_squares + norm_eps)
    return (mixed, grad_tokens, grad_blocks, left_new, right_new, new_blocks, grad_vectors, moment_new, new_vectors)
```

```python
import functools
import math

import jax
import jax.numpy as jnp
from jax import lax
from jax.experimental import pallas as pl
from jax.experimental.pallas import tpu as pltpu
from jax.sharding import PartitionSpec as P

HEAD_DIM = 64


norm_eps = 1e-06
block_rate = 0.03
vector_rate = 0.04
highest = lax.Precision.HIGHEST


def layer_norm(values, norm_gain, norm_bias):
    center = values - jnp.mean(values, axis=-1, keepdims=True)
    spread = jnp.mean(center * center, axis=-1, keepdims=True)
    return center * lax.rsqrt(spread + norm_eps) * norm_gain + norm_bias


def gelu_exact(values):
    return jax.nn.gelu(values, approximate=False)


BOTH = ("dp", "own")


def flips(core):
    return (1, 2) if core == 0 else (2, 1)


def swap_pairs():
    return [(i, i ^ 1) for i in range(32)]


def plane_pairs(step):
    pairs = []
    for i in range(32):
        place, core = i // 2, i % 2
        pairs.append((i, (place ^ flips(core)[step]) * 2 + core))
    return pairs


def line_pairs(shift):
    return [(i, (i + 8 * shift) % 32) for i in range(32)]


def send(value, pairs):
    return lax.ppermute(value, BOTH, pairs)


def place_kernel(wide, parts, *refs):
    sources, (out_ref, sems) = refs[: 2 * parts], refs[2 * parts :]
    device = lax.axis_index("dp")
    core = lax.axis_index("own")
    line, place = device // 4, device % 4
    copies = []
    for other in range(2):
        half = core if other == 0 else 1 - core
        first = half + 1
        second = 2 - half
        group = sources[other * parts : (other + 1) * parts]
        views = [(group[shift], shift, 0, 0) for shift in range(4)]
        views += [(group[4].at[shift], shift, 1, 0) for shift in range(4)]
        views += [
            (group[5].at[step, shift], shift, step, 1) for step in range(2) for shift in range(4)
        ]
        for view, shift, flip_one, flip_two in views:
            spot = place
            if flip_one:
                spot = jnp.bitwise_xor(spot, first)
            if flip_two:
                spot = jnp.bitwise_xor(spot, second)
            rows = view.shape[1]
            columns = view.shape[2]
            start = (lax.rem(line - shift + 4, 4) * 4 + spot) * rows
            row_slice = pl.ds(pl.multiple_of(start, rows), rows)
            if wide:
                for number in range(view.shape[0]):
                    offset = number * 2 * columns + half * columns
                    target = out_ref.at[row_slice, pl.ds(pl.multiple_of(offset, columns), columns)]
                    copies.append((view.at[number], target))
            else:
                offset = pl.multiple_of(half * columns, columns)
                copies.append((view, out_ref.at[:, row_slice, pl.ds(offset, columns)]))
    handles = []
    for number, (source, target) in enumerate(copies):
        handle = pltpu.make_async_copy(source, target, sems.at[number])
        handle.start()
        handles.append(handle)
    for handle in handles:
        handle.wait()


def place_parts(mine, theirs, wide):
    parts = len(mine)
    count, rows, columns = mine[0].shape
    full = rows * 16
    if wide:
        shape, copies = (full, count * columns * 2), 32 * count
    else:
        shape, copies = (count, full, columns * 2), 32
    anywhere = pl.BlockSpec(memory_space=pl.ANY)
    return pl.pallas_call(
        functools.partial(place_kernel, wide, parts),
        out_shape=jax.ShapeDtypeStruct(shape, mine[0].dtype),
        in_specs=[anywhere] * (2 * parts),
        out_specs=anywhere,
        scratch_shapes=[pltpu.SemaphoreType.DMA((copies,))],
    )(*mine, *theirs)


def gather_chunk(chunk, wide):
    line = [chunk] + [send(chunk, line_pairs(shift)) for shift in (1, 2, 3)]
    stacked = jnp.stack(line)
    near = send(stacked, plane_pairs(0))
    far = send(jnp.stack([stacked, near]), plane_pairs(1))
    mine = line + [near, far]
    theirs = [send(part, swap_pairs()) for part in mine]
    return place_parts(mine, theirs, wide)


def gather_weights(blocks, up_blocks):
    core = lax.axis_index("own")
    by_block = jnp.transpose(blocks.astype(jnp.bfloat16), (1, 0, 2))
    half = by_block.shape[2] // 2
    low, high = by_block[..., :half], by_block[..., half:]
    keep = jnp.where(core == 0, low, high)
    give = jnp.where(core == 0, high, low)
    got = send(give, swap_pairs())
    every = jnp.where(
        core == 0, jnp.concatenate([keep, got], axis=0), jnp.concatenate([got, keep], axis=0)
    )
    w_attn = gather_chunk(every[:4], False)
    w_up = gather_chunk(every[4 : 4 + up_blocks], True)
    w_down = gather_chunk(every[4 + up_blocks :], False)
    return w_attn, w_up, w_down.reshape(-1, w_down.shape[2])


def shards(
    tokens,
    cotangent,
    selected,
    packing,
    segments,
    blocks,
    left_stat,
    right_stat,
    left_root,
    right_root,
    vectors,
    moment,
):
    model_width = tokens.shape[2]
    token_count = tokens.shape[0] * tokens.shape[1]
    n_data = lax.axis_size("dp")
    n_owner = lax.axis_size("own")
    shard_rows = blocks.shape[0]
    own_blocks = blocks.shape[1]
    up_blocks = (own_blocks * n_owner - 4) // 2
    capacity = packing.shape[1]
    per_peer = capacity // n_data
    head_count = model_width // HEAD_DIM
    score_scale = HEAD_DIM ** (-0.5)
    small = n_data == 16 and n_owner == 2 and up_blocks == 4
    if small:
        w_attn, w_up, w_down = gather_weights(blocks, up_blocks)
        w_query, w_key, w_value, w_out = (w_attn[number] for number in range(4))
    else:
        flat_weights = blocks.astype(jnp.bfloat16).reshape(1, shard_rows * own_blocks * model_width)
        gathered = lax.all_gather(flat_weights, ("dp", "own"), axis=0, tiled=True)
        gathered = gathered.reshape(n_data, n_owner, shard_rows, own_blocks, model_width)

        def matrix(number):
            return gathered[:, number // own_blocks, :, number % own_blocks, :].reshape(
                model_width, model_width
            )

        w_query, w_key, w_value, w_out = (matrix(number) for number in range(4))
        w_up = jnp.concatenate([matrix(4 + position) for position in range(up_blocks)], axis=1)
        w_down = jnp.concatenate(
            [matrix(4 + up_blocks + position) for position in range(up_blocks)], axis=0
        )
    inputs = tokens.reshape(token_count, model_width).astype(jnp.float32)
    chosen = selected.reshape(token_count)
    normed_one, norm_one_back = jax.vjp(layer_norm, inputs, vectors[0], vectors[1])
    first_low = normed_one.astype(jnp.bfloat16)
    first_wide = first_low.astype(jnp.float32)
    gate_values = jax.nn.sigmoid(jnp.dot(first_wide, vectors[2], precision=highest))
    before = jnp.cumsum(chosen) - 1
    slot_index = jnp.where(chosen == 1, packing[0][jnp.clip(before, 0, capacity - 1)], -1)
    placing = (slot_index[None, :] == jnp.arange(capacity, dtype=jnp.int32)[:, None]).astype(
        jnp.bfloat16
    )
    packed = jnp.dot(placing, first_low, preferred_element_type=jnp.float32).astype(jnp.bfloat16)
    buffer = lax.all_to_all(
        packed.reshape(n_data, per_peer, model_width), "dp", split_axis=0, concat_axis=0, tiled=True
    )
    buffer = buffer.reshape(capacity, model_width)

    def project(matrix_in):
        made = jnp.dot(buffer, matrix_in, preferred_element_type=jnp.float32).astype(jnp.bfloat16)
        return made.reshape(capacity, head_count, HEAD_DIM)

    query_rows = project(w_query)
    key_rows = project(w_key)
    value_rows = project(w_value)
    segment = segments[0]
    block_rows = math.gcd(capacity, 512)
    starts = jnp.arange(capacity // block_rows, dtype=jnp.int32) * block_rows

    def masked_scores():
        scores = (
            jnp.einsum("qhd,khd->hqk", query_rows, key_rows, preferred_element_type=jnp.float32)
            * score_scale
        )
        same_segment = segment[:, None] == segment[None, :]
        return (jnp.where(same_segment[None, :, :], scores, -1e30), query_rows)

    def forward_block(first_row):
        scores, unused_block = masked_scores()
        largest = jnp.max(scores, axis=-1, keepdims=True)
        raised = jnp.exp(scores - largest)
        row_total = jnp.sum(raised, axis=-1, keepdims=True)
        shares = (raised / row_total).astype(jnp.bfloat16)
        context_part = jnp.einsum(
            "hqk,khd->qhd", shares, value_rows, preferred_element_type=jnp.float32
        )
        return (context_part.astype(jnp.bfloat16), largest[..., 0] + jnp.log(row_total[..., 0]))

    context_blocks, lse_blocks = lax.map(forward_block, starts)
    context = context_blocks.reshape(capacity, model_width)
    answer = jnp.dot(context, w_out, preferred_element_type=jnp.float32).astype(jnp.bfloat16)
    returned = lax.all_to_all(
        answer.reshape(n_data, per_peer, model_width), "dp", split_axis=0, concat_axis=0, tiled=True
    )
    returned = returned.reshape(capacity, model_width)
    unpacked = jnp.einsum("mt,md->td", placing, returned, preferred_element_type=jnp.float32)
    weighting = jnp.where(chosen == 1, gate_values, 0.0)
    hidden = inputs + weighting[:, None] * unpacked
    normed_two, norm_two_back = jax.vjp(layer_norm, hidden, vectors[3], vectors[4])
    second_low = normed_two.astype(jnp.bfloat16)
    pre_active = jnp.dot(second_low, w_up, preferred_element_type=jnp.float32)
    active_wide, gelu_back = jax.vjp(gelu_exact, pre_active)
    active = active_wide.astype(jnp.bfloat16)
    result = hidden + jnp.dot(active, w_down, preferred_element_type=jnp.float32)
    mixed = result.astype(jnp.bfloat16).reshape(tokens.shape)
    upstream = cotangent.reshape(token_count, model_width)
    grad_down = jnp.einsum("tf,td->fd", active, upstream, preferred_element_type=jnp.float32)
    grad_active = jnp.einsum("td,fd->tf", upstream, w_down, preferred_element_type=jnp.float32)
    grad_inner = gelu_back(grad_active)[0].astype(jnp.bfloat16)
    grad_up = jnp.einsum("td,tf->df", second_low, grad_inner, preferred_element_type=jnp.float32)
    grad_second = jnp.einsum("tf,df->td", grad_inner, w_up, preferred_element_type=jnp.float32)
    grad_hidden_part, grad_gain_two, grad_bias_two = norm_two_back(grad_second)
    grad_hidden = upstream.astype(jnp.float32) + grad_hidden_part
    grad_token_back = (grad_hidden * weighting[:, None]).astype(jnp.bfloat16)
    grad_packed = jnp.dot(placing, grad_token_back, preferred_element_type=jnp.float32).astype(
        jnp.bfloat16
    )
    router_pull = jnp.where(chosen == 1, jnp.sum(grad_hidden * unpacked, axis=-1), 0.0)
    grad_logit = router_pull * gate_values * (1.0 - gate_values)
    grad_answer = lax.all_to_all(
        grad_packed.reshape(n_data, per_peer, model_width),
        "dp",
        split_axis=0,
        concat_axis=0,
        tiled=True,
    )
    grad_answer = grad_answer.reshape(capacity, model_width)
    grad_out = jnp.einsum("md,me->de", context, grad_answer, preferred_element_type=jnp.float32)
    grad_context = jnp.einsum("me,de->md", grad_answer, w_out, preferred_element_type=jnp.float32)
    grad_context = grad_context.astype(jnp.bfloat16).reshape(capacity, head_count, HEAD_DIM)

    def backward_block(running, item_pair):
        first_row, lse_block = item_pair
        scores, query_block = masked_scores()
        shares_wide = jnp.exp(scores - lse_block[..., None])
        grad_shares = jnp.einsum(
            "qhd,khd->hqk", grad_context, value_rows, preferred_element_type=jnp.float32
        )
        inner_sum = jnp.sum(shares_wide * grad_shares, axis=-1, keepdims=True)
        grad_scores = (shares_wide * (grad_shares - inner_sum)).astype(jnp.bfloat16)
        grad_query_block = (
            jnp.einsum("hqk,khd->qhd", grad_scores, key_rows, preferred_element_type=jnp.float32)
            * score_scale
        )
        key_sum = (
            running[0]
            + jnp.einsum(
                "hqk,qhd->khd", grad_scores, query_block, preferred_element_type=jnp.float32
            )
            * score_scale
        )
        value_sum = running[1] + jnp.einsum(
            "hqk,qhd->khd",
            shares_wide.astype(jnp.bfloat16),
            grad_context,
            preferred_element_type=jnp.float32,
        )
        return ((key_sum, value_sum), grad_query_block)

    zeros_init = jnp.zeros((capacity, head_count, HEAD_DIM), jnp.float32)
    (key_total, value_total), query_grads = lax.scan(
        backward_block, (zeros_init, zeros_init), (starts, lse_blocks)
    )
    grad_query = query_grads.reshape(capacity, model_width).astype(jnp.bfloat16)
    grad_key = key_total.reshape(capacity, model_width).astype(jnp.bfloat16)
    grad_value = value_total.reshape(capacity, model_width).astype(jnp.bfloat16)
    grad_w_query = jnp.einsum("md,me->de", buffer, grad_query, preferred_element_type=jnp.float32)
    grad_w_key = jnp.einsum("md,me->de", buffer, grad_key, preferred_element_type=jnp.float32)
    grad_w_value = jnp.einsum("md,me->de", buffer, grad_value, preferred_element_type=jnp.float32)
    grad_buffer = jnp.einsum("me,de->md", grad_query, w_query, preferred_element_type=jnp.float32)
    grad_buffer = grad_buffer + jnp.einsum(
        "me,de->md", grad_key, w_key, preferred_element_type=jnp.float32
    )
    grad_buffer = grad_buffer + jnp.einsum(
        "me,de->md", grad_value, w_value, preferred_element_type=jnp.float32
    )
    grad_buffer = grad_buffer.astype(jnp.bfloat16)
    grad_sent = lax.all_to_all(
        grad_buffer.reshape(n_data, per_peer, model_width),
        "dp",
        split_axis=0,
        concat_axis=0,
        tiled=True,
    )
    grad_sent = grad_sent.reshape(capacity, model_width)
    grad_first = jnp.einsum("mt,md->td", placing, grad_sent, preferred_element_type=jnp.float32)
    grad_first = grad_first + grad_logit[:, None] * vectors[2][None, :]
    grad_router = jnp.sum(grad_logit[:, None] * first_wide, axis=0)
    grad_input_part, grad_gain_one, grad_bias_one = norm_one_back(grad_first)
    grad_tokens = (grad_hidden + grad_input_part).astype(jnp.bfloat16).reshape(tokens.shape)
    pieces = [grad_w_query, grad_w_key, grad_w_value, grad_out]
    pieces = pieces + [
        grad_up[:, position * model_width : (position + 1) * model_width]
        for position in range(up_blocks)
    ]
    pieces = pieces + [
        grad_down[position * model_width : (position + 1) * model_width, :]
        for position in range(up_blocks)
    ]
    local_terms = jnp.stack(pieces, axis=1)
    vector_terms = jnp.stack(
        [grad_gain_one, grad_bias_one, grad_router, grad_gain_two, grad_bias_two]
    )
    if small:
        first_half, second_half = local_terms[:, :own_blocks], local_terms[:, own_blocks:]
        is_first = lax.axis_index("own") == 0
        kept = jnp.where(is_first, first_half, second_half)
        given = jnp.where(is_first, second_half, first_half).astype(jnp.bfloat16)
        both = kept + send(given, swap_pairs()).astype(jnp.float32)
        grad_own = lax.psum_scatter(both, "dp", scatter_dimension=0, tiled=True)
    else:
        partial_value = lax.psum_scatter(local_terms, "dp", scatter_dimension=0, tiled=True)
        grad_own = lax.psum_scatter(
            partial_value.astype(jnp.bfloat16), "own", scatter_dimension=1, tiled=True
        ).astype(jnp.float32)
    vector_grad = lax.psum(vector_terms, ("dp", "own"))
    full_grad = lax.all_gather(grad_own.astype(jnp.bfloat16), "dp", axis=0, tiled=True).astype(
        grad_own.dtype
    )
    row_start = lax.axis_index("dp") * shard_rows
    left_new = 0.5 * left_stat + 0.5 * jnp.einsum(
        "rbk,nbk->rbn", grad_own, full_grad, precision=highest
    )
    column_part = lax.dynamic_slice_in_dim(full_grad, row_start, shard_rows, 2)
    right_new = 0.5 * right_stat + 0.5 * jnp.einsum(
        "nbr,nbk->rbk", column_part, full_grad, precision=highest
    )
    lefted = jnp.einsum("rbn,nbk->rbk", left_root, full_grad, precision=highest)
    precond = jnp.zeros_like(grad_own) + jnp.einsum(
        "rbn,nbk->rbk",
        lefted,
        lax.all_gather(right_root.astype(jnp.bfloat16), "dp", axis=0, tiled=True).astype(
            jnp.float32
        ),
        precision=highest,
    )
    square_sums = lax.psum(jnp.sum(precond * precond, axis=(0, 2)), "dp")
    step_scale = lax.rsqrt(square_sums / (model_width * model_width) + norm_eps)
    new_blocks = blocks - block_rate * precond * step_scale[None, :, None]
    moment_new = 0.5 * moment + 0.5 * vector_grad
    row_squares = jnp.mean(moment_new * moment_new, axis=1, keepdims=True)
    vector_new = vectors - vector_rate * moment_new * lax.rsqrt(row_squares + norm_eps)
    return (
        mixed,
        grad_tokens,
        grad_own,
        left_new,
        right_new,
        new_blocks,
        vector_grad,
        moment_new,
        vector_new,
    )


def solution(mesh):
    placed = (
        P(("dp", "own"), None, None),
        P(("dp", "own"), None, None),
        P(("dp", "own"), None),
        P(("dp", "own"), None),
        P(("dp", "own"), None),
        P("dp", "own", None),
        P("dp", "own", None),
        P("dp", "own", None),
        P("dp", "own", None),
        P("dp", "own", None),
        P(),
        P(),
    )
    return jax.shard_map(
        shards,
        mesh=mesh,
        in_specs=placed,
        out_specs=(
            P(("dp", "own"), None, None),
            P(("dp", "own"), None, None),
            P("dp", "own", None),
            P("dp", "own", None),
            P("dp", "own", None),
            P("dp", "own", None),
            P(),
            P(),
            P(),
        ),
        check_vma=False,
    )
```

```python
import functools
import math

import jax
import jax.numpy as jnp
from jax import lax
from jax.experimental import pallas as pl
from jax.experimental.pallas import tpu as pltpu
from jax.sharding import PartitionSpec as P

HEAD_DIM = 64


norm_eps = 1e-06
block_rate = 0.03
vector_rate = 0.04
highest = lax.Precision.HIGHEST


def layer_norm(values, norm_gain, norm_bias):
    center = values - jnp.mean(values, axis=-1, keepdims=True)
    spread = jnp.mean(center * center, axis=-1, keepdims=True)
    return center * lax.rsqrt(spread + norm_eps) * norm_gain + norm_bias


def gelu_exact(values):
    return jax.nn.gelu(values, approximate=False)


BOTH = ("dp", "own")
low = jnp.bfloat16
wide = jnp.float32


def swap_pairs():
    return [(i, i ^ 1) for i in range(32)]


def plane_pairs(step):
    pairs = []
    for i in range(32):
        place, core = i // 2, i % 2
        flip = (1, 2)[step ^ core]
        pairs.append((i, (place ^ flip) * 2 + core))
    return pairs


def xor_pairs(flip):
    return [(i, ((i // 2) ^ flip) * 2 + i % 2) for i in range(32)]


def line_pairs(shift):
    return [(i, (i + 8 * shift) % 32) for i in range(32)]


def send(value, pairs):
    return lax.ppermute(value, BOTH, pairs)


def pick(value, index, axis):
    return lax.dynamic_index_in_dim(value, index, axis, keepdims=False)


def first_core():
    return lax.axis_index("own") == 0


def halves(value):
    middle = value.shape[-1] // 2
    lower, upper = value[..., :middle], value[..., middle:]
    return jnp.where(first_core(), lower, upper), jnp.where(first_core(), upper, lower)


def in_core_order(mine, theirs, axis):
    return jnp.where(
        first_core(),
        jnp.concatenate([mine, theirs], axis=axis),
        jnp.concatenate([theirs, mine], axis=axis),
    )


def spots(place, half):
    first, second = half + 1, 2 - half
    return [
        place,
        jnp.bitwise_xor(place, first),
        jnp.bitwise_xor(place, second),
        jnp.bitwise_xor(place, 3),
    ]


def gather_plane(value):
    near = send(value, plane_pairs(0))
    far = send(jnp.stack([value, near]), plane_pairs(1))
    return near, far


def here():
    device = lax.axis_index("dp")
    return device // 4, device % 4, lax.axis_index("own")


def weight_kernel(joined, *refs):
    sources, out_ref = refs[:12], refs[12]
    line, place, core = here()
    for other in range(2):
        half = core if other == 0 else 1 - core
        group = sources[other * 6 : other * 6 + 6]
        count, rows, columns = group[0].shape
        for number, spot in enumerate(spots(place, half)):
            for shift in range(4):
                start = (lax.rem(line - shift + 4, 4) * 4 + spot) * rows
                row_slice = pl.ds(pl.multiple_of(start, rows), rows)
                for block in range(count):
                    if number == 0:
                        piece = group[shift][block]
                    elif number == 1:
                        piece = group[4][shift, block]
                    else:
                        piece = group[5][number - 2, shift, block]
                    offset = half * columns
                    if joined:
                        offset = offset + block * 2 * columns
                        column_slice = pl.ds(pl.multiple_of(offset, columns), columns)
                        out_ref[row_slice, column_slice] = piece
                    else:
                        column_slice = pl.ds(pl.multiple_of(offset, columns), columns)
                        out_ref[block, row_slice, column_slice] = piece


def place_weights(mine, theirs, joined):
    count, rows, columns = mine[0].shape
    full = rows * 16
    shape = (full, count * columns * 2) if joined else (count, full, columns * 2)
    return pl.pallas_call(
        functools.partial(weight_kernel, joined),
        out_shape=jax.ShapeDtypeStruct(shape, mine[0].dtype),
        in_specs=[pl.BlockSpec(memory_space=pltpu.VMEM)] * 12,
        out_specs=pl.BlockSpec(memory_space=pltpu.VMEM),
        compiler_params=pltpu.CompilerParams(vmem_limit_bytes=24 * 2**20),
        cost_estimate=pl.CostEstimate(
            flops=0, bytes_accessed=4 * full * count * columns * 2, transcendentals=0
        ),
    )(*mine, *theirs)


def gather_chunk(chunk, joined):
    line = [chunk] + [send(chunk, line_pairs(shift)) for shift in (1, 2, 3)]
    near, far = gather_plane(jnp.stack(line))
    mine = line + [near, far]
    theirs = [send(part, swap_pairs()) for part in mine]
    return place_weights(mine, theirs, joined)


def columns_by_core(value):
    keep, give = halves(jnp.transpose(value.astype(low), (1, 0, 2)))
    return in_core_order(keep, send(give, swap_pairs()), 0)


def gather_weights(blocks, up_blocks):
    every = columns_by_core(blocks)
    w_attn = gather_chunk(every[:4], False)
    w_up = gather_chunk(every[4 : 4 + up_blocks], True)
    w_down = gather_chunk(every[4 + up_blocks :], False)
    return w_attn, w_up, w_down.reshape(-1, w_down.shape[2])


def gather_roots(left_root, right_root):
    line, place, core = here()
    every = columns_by_core(jnp.concatenate([left_root, right_root], axis=2).reshape(
        left_root.shape[0], left_root.shape[1] * 2, left_root.shape[2]
    ))
    rows, columns = every.shape[1:]
    every = every.reshape(3, 4, 2, rows, columns)
    line_parts = [pick(every, line, 1)]
    for shift in (1, 2, 3):
        given = pick(every, lax.rem(line + shift, 4), 1)
        line_parts.append(send(given, line_pairs(shift)))
    stacked = jnp.stack(line_parts)
    left_mine, right_mine = stacked[:, :, 0], stacked[:, :, 1]
    left_theirs = send(left_mine, swap_pairs())
    near, far = gather_plane(right_mine)
    return left_mine, left_theirs, right_mine, near, far


def reduce_chunk(mine, theirs):
    line, place, core = here()
    count, full, columns = mine.shape
    summed = mine + send(theirs, swap_pairs()).astype(wide)
    pieces = summed.reshape(count, 4, 4, full // 16, columns)
    spot = spots(place, core)
    give = jnp.stack([pick(pieces, spot[1], 2), pick(pieces, spot[3], 2)]).astype(low)
    got = send(give, plane_pairs(0)).astype(wide)
    kept = pick(pieces, spot[0], 2) + got[0]
    passed = pick(pieces, spot[2], 2) + got[1]
    kept = kept + send(passed.astype(low), plane_pairs(1)).astype(wide)
    total = pick(kept, line, 0)
    for shift in (1, 2, 3):
        given = pick(kept, lax.rem(line + shift, 4), 0).astype(low)
        total = total + send(given, line_pairs(shift)).astype(wide)
    return total


def step_kernel(
    own_ref,
    near_ref,
    far_ref,
    own_other,
    near_other,
    far_other,
    left_ref,
    left_other,
    right_ref,
    right_near,
    right_far,
    out_ref,
    square_ref,
    grad_ref,
    rows_ref,
    left_rows,
    right_rows,
    cross_ref,
):
    line, place, core = here()
    rows, columns = own_ref.shape[1:]

    def rows_of(row_line, spot):
        return pl.ds(pl.multiple_of((row_line * 4 + spot) * rows, rows), rows)

    def column_half(half):
        return pl.ds(pl.multiple_of(half * columns, columns), columns)

    for other in range(2):
        half = core if other == 0 else 1 - core
        group = (own_other, near_other, far_other) if other else (own_ref, near_ref, far_ref)
        for number, spot in enumerate(spots(place, half)):
            for row_line in range(4):
                if number < 2:
                    piece = group[number][row_line]
                else:
                    piece = group[2][number - 2, row_line]
                grad_ref[rows_of(row_line, spot), column_half(half)] = piece
        for shift in range(4):
            row_line = lax.rem(line - shift + 4, 4)
            target = pl.ds(pl.multiple_of(row_line * rows, rows), rows)
            left_rows[target, column_half(half)] = (left_other if other else left_ref)[shift, 0]
    for number, spot in enumerate(spots(place, core)):
        for shift in range(4):
            row_line = lax.rem(line - shift + 4, 4)
            if number < 2:
                piece = (right_near if number else right_ref)[shift, 0]
            else:
                piece = right_far[number - 2, shift, 0]
            right_rows[rows_of(row_line, spot), :] = piece
    for row_line in range(4):
        rows_ref[row_line * rows : (row_line + 1) * rows, :] = grad_ref[rows_of(row_line, place), :]
    grad = grad_ref[...]
    left = lax.dot_general(
        rows_ref[...],
        grad_ref[column_half(core), :],
        (((1,), (1,)), ((), ())),
        preferred_element_type=wide,
    )
    cross_ref[...] = lax.dot_general(
        grad,
        grad_ref[:, column_half(core)],
        (((0,), (0,)), ((), ())),
        preferred_element_type=wide,
    )
    lefted = jnp.dot(left_rows[...], grad, preferred_element_type=wide).astype(low)
    stepped = jnp.dot(lefted, right_rows[...], preferred_element_type=wide)
    square_ref[...] = jnp.sum(stepped * stepped, axis=0, keepdims=True)
    for row_line in range(4):
        part = slice(row_line * rows, (row_line + 1) * rows)
        out_ref[row_line, 0] = own_ref[row_line]
        out_ref[row_line, 1] = left[part].astype(low)
        out_ref[row_line, 2] = cross_ref[rows_of(row_line, place), :].astype(low)
        out_ref[row_line, 3] = stepped[part].astype(low)


def step_chunk(total, roots, number):
    own = total.astype(low)
    near, far = gather_plane(own)
    parts = [own, near, far]
    parts = parts + [send(part, swap_pairs()) for part in parts]
    lines, rows, columns = own.shape
    full = rows * 16
    whole = pl.BlockSpec(memory_space=pltpu.VMEM)

    def root_spec(root):
        lead = root.ndim - 3
        block = root.shape[:lead] + (1,) + root.shape[lead + 1 :]
        return pl.BlockSpec(block, lambda step: (0,) * lead + (number, 0, 0))

    return pl.pallas_call(
        step_kernel,
        grid=(1,),
        out_shape=(
            jax.ShapeDtypeStruct((lines, 4, rows, columns), low),
            jax.ShapeDtypeStruct((1, columns), wide),
        ),
        in_specs=[whole] * 6 + [root_spec(root) for root in roots],
        out_specs=(whole, whole),
        scratch_shapes=[
            pltpu.VMEM((full, columns * 2), low),
            pltpu.VMEM((lines * rows, columns * 2), low),
            pltpu.VMEM((lines * rows, columns * 2), low),
            pltpu.VMEM((full, columns), low),
            pltpu.VMEM((full, columns), wide),
        ],
        compiler_params=pltpu.CompilerParams(vmem_limit_bytes=24 * 2**20),
        cost_estimate=pl.CostEstimate(
            flops=6 * full * full * columns, bytes_accessed=8 * full * full, transcendentals=0
        ),
    )(*parts, *roots)


def return_chunk(made):
    line, place, core = here()
    parts = [pick(made, line, 0)]
    for shift in (1, 2, 3):
        given = pick(made, lax.rem(line + shift, 4), 0)
        parts.append(send(given, line_pairs(shift)))
    stacked = jnp.stack(parts)
    return jnp.stack([pick(stacked, lax.rem(line - block + 4, 4), 0) for block in range(4)])


def all_sum(value):
    value = value + send(value, swap_pairs())
    for low_flip, high_flip in ((1, 2), (4, 8)):
        near = value + send(value, xor_pairs(low_flip))
        far = send(value, xor_pairs(high_flip)) + send(value, xor_pairs(low_flip + high_flip))
        value = near + far
    return value


def update_small(chunks, roots, blocks, left_stat, right_stat):
    line, place, core = here()
    made, squares = [None] * 3, [None] * 3
    for number in (2, 1, 0):
        total = reduce_chunk(*chunks[number])
        out, square = step_chunk(total, roots, number)
        made[number] = return_chunk(out)
        squares[number] = jnp.sum(square)
    attn, up, down = made
    from_first = [(i, i ^ 1) for i in range(0, 32, 2)]
    from_second = [(i, i ^ 1) for i in range(1, 32, 2)]
    attn_other = send(attn, from_second)
    down_other = send(down, from_first)
    up_mine = jnp.where(first_core(), up[:2], up[2:])
    up_other = send(jnp.where(first_core(), up[2:], up[:2]), swap_pairs())
    mine = jnp.where(
        first_core(), jnp.concatenate([attn, up_mine]), jnp.concatenate([up_mine, down])
    )
    theirs = jnp.where(
        first_core(),
        jnp.concatenate([attn_other, up_other]),
        jnp.concatenate([up_other, down_other]),
    )
    every = in_core_order(mine, theirs, 3).astype(wide)
    every = jnp.transpose(every, (1, 2, 0, 3))
    square = jnp.stack(squares)
    square = square + send(square, swap_pairs())
    square = (square + send(square, xor_pairs(1))) + (
        send(square, xor_pairs(2)) + send(square, xor_pairs(3))
    )
    lines = jnp.stack([square] + [send(square, line_pairs(shift)) for shift in (1, 2, 3)])
    sums = jnp.stack([pick(lines, lax.rem(line - block + 4, 4), 0) for block in range(4)], axis=1)
    sums = sums.reshape(12)
    sums = jnp.where(first_core(), sums[:6], sums[6:])
    size = blocks.shape[2] * blocks.shape[2]
    step_scale = lax.rsqrt(sums / size + norm_eps)
    grad_own, left_part, right_part, precond = (every[kind] for kind in range(4))
    left_new = 0.5 * left_stat + 0.5 * left_part
    right_new = 0.5 * right_stat + 0.5 * right_part
    new_blocks = blocks - block_rate * precond * step_scale[None, :, None]
    return grad_own, left_new, right_new, new_blocks


def shards(
    tokens,
    cotangent,
    selected,
    packing,
    segments,
    blocks,
    left_stat,
    right_stat,
    left_root,
    right_root,
    vectors,
    moment,
):
    model_width = tokens.shape[2]
    token_count = tokens.shape[0] * tokens.shape[1]
    n_data = lax.axis_size("dp")
    n_owner = lax.axis_size("own")
    shard_rows = blocks.shape[0]
    own_blocks = blocks.shape[1]
    up_blocks = (own_blocks * n_owner - 4) // 2
    capacity = packing.shape[1]
    per_peer = capacity // n_data
    head_count = model_width // HEAD_DIM
    score_scale = HEAD_DIM ** (-0.5)
    small = n_data == 16 and n_owner == 2 and own_blocks == 6
    if small:
        w_attn, w_up, w_down = gather_weights(blocks, up_blocks)
        w_query, w_key, w_value, w_out = (w_attn[number] for number in range(4))
        late_left, late_right, w_up = lax.optimization_barrier((left_root, right_root, w_up))
        roots = gather_roots(late_left, late_right)
    else:
        flat_weights = blocks.astype(jnp.bfloat16).reshape(1, shard_rows * own_blocks * model_width)
        gathered = lax.all_gather(flat_weights, ("dp", "own"), axis=0, tiled=True)
        gathered = gathered.reshape(n_data, n_owner, shard_rows, own_blocks, model_width)

        def matrix(number):
            return gathered[:, number // own_blocks, :, number % own_blocks, :].reshape(
                model_width, model_width
            )

        w_query, w_key, w_value, w_out = (matrix(number) for number in range(4))
        w_up = jnp.concatenate([matrix(4 + position) for position in range(up_blocks)], axis=1)
        w_down = jnp.concatenate(
            [matrix(4 + up_blocks + position) for position in range(up_blocks)], axis=0
        )
    inputs = tokens.reshape(token_count, model_width).astype(jnp.float32)
    chosen = selected.reshape(token_count)
    normed_one, norm_one_back = jax.vjp(layer_norm, inputs, vectors[0], vectors[1])
    first_low = normed_one.astype(jnp.bfloat16)
    first_wide = first_low.astype(jnp.float32)
    gate_values = jax.nn.sigmoid(jnp.dot(first_wide, vectors[2], precision=highest))
    before = jnp.cumsum(chosen) - 1
    slot_index = jnp.where(chosen == 1, packing[0][jnp.clip(before, 0, capacity - 1)], -1)
    placing = (slot_index[None, :] == jnp.arange(capacity, dtype=jnp.int32)[:, None]).astype(
        jnp.bfloat16
    )
    packed = jnp.dot(placing, first_low, preferred_element_type=jnp.float32).astype(jnp.bfloat16)
    buffer = lax.all_to_all(
        packed.reshape(n_data, per_peer, model_width), "dp", split_axis=0, concat_axis=0, tiled=True
    )
    buffer = buffer.reshape(capacity, model_width)

    def project(matrix_in):
        made = jnp.dot(buffer, matrix_in, preferred_element_type=jnp.float32).astype(jnp.bfloat16)
        return made.reshape(capacity, head_count, HEAD_DIM)

    query_rows = project(w_query)
    key_rows = project(w_key)
    value_rows = project(w_value)
    segment = segments[0]
    block_rows = math.gcd(capacity, 512)
    starts = jnp.arange(capacity // block_rows, dtype=jnp.int32) * block_rows

    def masked_scores():
        scores = (
            jnp.einsum("qhd,khd->hqk", query_rows, key_rows, preferred_element_type=jnp.float32)
            * score_scale
        )
        same_segment = segment[:, None] == segment[None, :]
        return (jnp.where(same_segment[None, :, :], scores, -1e30), query_rows)

    def forward_block(first_row):
        scores, unused_block = masked_scores()
        largest = jnp.max(scores, axis=-1, keepdims=True)
        raised = jnp.exp(scores - largest)
        row_total = jnp.sum(raised, axis=-1, keepdims=True)
        shares = (raised / row_total).astype(jnp.bfloat16)
        context_part = jnp.einsum(
            "hqk,khd->qhd", shares, value_rows, preferred_element_type=jnp.float32
        )
        return (context_part.astype(jnp.bfloat16), largest[..., 0] + jnp.log(row_total[..., 0]))

    context_blocks, lse_blocks = lax.map(forward_block, starts)
    context = context_blocks.reshape(capacity, model_width)
    answer = jnp.dot(context, w_out, preferred_element_type=jnp.float32).astype(jnp.bfloat16)
    returned = lax.all_to_all(
        answer.reshape(n_data, per_peer, model_width), "dp", split_axis=0, concat_axis=0, tiled=True
    )
    returned = returned.reshape(capacity, model_width)
    unpacked = jnp.einsum("mt,md->td", placing, returned, preferred_element_type=jnp.float32)
    weighting = jnp.where(chosen == 1, gate_values, 0.0)
    hidden = inputs + weighting[:, None] * unpacked
    normed_two, norm_two_back = jax.vjp(layer_norm, hidden, vectors[3], vectors[4])
    second_low = normed_two.astype(jnp.bfloat16)
    pre_active = jnp.dot(second_low, w_up, preferred_element_type=jnp.float32)
    active_wide, gelu_back = jax.vjp(gelu_exact, pre_active)
    active = active_wide.astype(jnp.bfloat16)
    result = hidden + jnp.dot(active, w_down, preferred_element_type=jnp.float32)
    mixed = result.astype(jnp.bfloat16).reshape(tokens.shape)
    upstream = cotangent.reshape(token_count, model_width)
    grad_active = jnp.einsum("td,fd->tf", upstream, w_down, preferred_element_type=jnp.float32)
    grad_inner = gelu_back(grad_active)[0].astype(jnp.bfloat16)
    grad_second = jnp.einsum("tf,df->td", grad_inner, w_up, preferred_element_type=jnp.float32)
    grad_hidden_part, grad_gain_two, grad_bias_two = norm_two_back(grad_second)
    grad_hidden = upstream.astype(jnp.float32) + grad_hidden_part
    grad_token_back = (grad_hidden * weighting[:, None]).astype(jnp.bfloat16)
    grad_packed = jnp.dot(placing, grad_token_back, preferred_element_type=jnp.float32).astype(
        jnp.bfloat16
    )
    router_pull = jnp.where(chosen == 1, jnp.sum(grad_hidden * unpacked, axis=-1), 0.0)
    grad_logit = router_pull * gate_values * (1.0 - gate_values)
    grad_answer = lax.all_to_all(
        grad_packed.reshape(n_data, per_peer, model_width),
        "dp",
        split_axis=0,
        concat_axis=0,
        tiled=True,
    )
    grad_answer = grad_answer.reshape(capacity, model_width)
    grad_context = jnp.einsum("me,de->md", grad_answer, w_out, preferred_element_type=jnp.float32)
    grad_context = grad_context.astype(jnp.bfloat16).reshape(capacity, head_count, HEAD_DIM)

    def backward_block(running, item_pair):
        first_row, lse_block = item_pair
        scores, query_block = masked_scores()
        shares_wide = jnp.exp(scores - lse_block[..., None])
        grad_shares = jnp.einsum(
            "qhd,khd->hqk", grad_context, value_rows, preferred_element_type=jnp.float32
        )
        inner_sum = jnp.sum(shares_wide * grad_shares, axis=-1, keepdims=True)
        grad_scores = (shares_wide * (grad_shares - inner_sum)).astype(jnp.bfloat16)
        grad_query_block = (
            jnp.einsum("hqk,khd->qhd", grad_scores, key_rows, preferred_element_type=jnp.float32)
            * score_scale
        )
        key_sum = (
            running[0]
            + jnp.einsum(
                "hqk,qhd->khd", grad_scores, query_block, preferred_element_type=jnp.float32
            )
            * score_scale
        )
        value_sum = running[1] + jnp.einsum(
            "hqk,qhd->khd",
            shares_wide.astype(jnp.bfloat16),
            grad_context,
            preferred_element_type=jnp.float32,
        )
        return ((key_sum, value_sum), grad_query_block)

    zeros_init = jnp.zeros((capacity, head_count, HEAD_DIM), jnp.float32)
    (key_total, value_total), query_grads = lax.scan(
        backward_block, (zeros_init, zeros_init), (starts, lse_blocks)
    )
    grad_query = query_grads.reshape(capacity, model_width).astype(jnp.bfloat16)
    grad_key = key_total.reshape(capacity, model_width).astype(jnp.bfloat16)
    grad_value = value_total.reshape(capacity, model_width).astype(jnp.bfloat16)
    grad_buffer = jnp.einsum("me,de->md", grad_query, w_query, preferred_element_type=jnp.float32)
    grad_buffer = grad_buffer + jnp.einsum(
        "me,de->md", grad_key, w_key, preferred_element_type=jnp.float32
    )
    grad_buffer = grad_buffer + jnp.einsum(
        "me,de->md", grad_value, w_value, preferred_element_type=jnp.float32
    )
    grad_buffer = grad_buffer.astype(jnp.bfloat16)
    grad_sent = lax.all_to_all(
        grad_buffer.reshape(n_data, per_peer, model_width),
        "dp",
        split_axis=0,
        concat_axis=0,
        tiled=True,
    )
    grad_sent = grad_sent.reshape(capacity, model_width)
    grad_first = jnp.einsum("mt,md->td", placing, grad_sent, preferred_element_type=jnp.float32)
    grad_first = grad_first + grad_logit[:, None] * vectors[2][None, :]
    grad_router = jnp.sum(grad_logit[:, None] * first_wide, axis=0)
    grad_input_part, grad_gain_one, grad_bias_one = norm_one_back(grad_first)
    grad_tokens = (grad_hidden + grad_input_part).astype(jnp.bfloat16).reshape(tokens.shape)
    vector_terms = jnp.stack(
        [grad_gain_one, grad_bias_one, grad_router, grad_gain_two, grad_bias_two]
    )
    if small:

        def outer(left_side, right_side, kind):
            return jnp.einsum("td,te->de", left_side, right_side, preferred_element_type=wide).astype(
                kind
            )

        def two_halves(pairs):
            made = [], []
            for left_side, right_side in pairs:
                for bin_list, half, kind in zip(made, halves(right_side), (wide, low)):
                    bin_list.append(outer(left_side, half, kind))
            return jnp.stack(made[0]), jnp.stack(made[1])

        attn_chunk = two_halves(
            [(buffer, grad_query), (buffer, grad_key), (buffer, grad_value), (context, grad_answer)]
        )
        up_chunk = two_halves(
            [
                (second_low, grad_inner[:, position * model_width : (position + 1) * model_width])
                for position in range(up_blocks)
            ]
        )
        down_chunk = tuple(
            outer(active, half, kind).reshape(up_blocks, model_width, -1)
            for half, kind in zip(halves(upstream), (wide, low))
        )
        grad_own, left_new, right_new, new_blocks = update_small(
            (attn_chunk, up_chunk, down_chunk), roots, blocks, left_stat, right_stat
        )
        vector_grad = all_sum(vector_terms)
    else:
        grad_down = jnp.einsum("tf,td->fd", active, upstream, preferred_element_type=jnp.float32)
        grad_up = jnp.einsum("td,tf->df", second_low, grad_inner, preferred_element_type=jnp.float32)
        grad_out = jnp.einsum("md,me->de", context, grad_answer, preferred_element_type=jnp.float32)
        grad_w_query = jnp.einsum("md,me->de", buffer, grad_query, preferred_element_type=jnp.float32)
        grad_w_key = jnp.einsum("md,me->de", buffer, grad_key, preferred_element_type=jnp.float32)
        grad_w_value = jnp.einsum("md,me->de", buffer, grad_value, preferred_element_type=jnp.float32)
        pieces = [grad_w_query, grad_w_key, grad_w_value, grad_out]
        pieces = pieces + [
            grad_up[:, position * model_width : (position + 1) * model_width]
            for position in range(up_blocks)
        ]
        pieces = pieces + [
            grad_down[position * model_width : (position + 1) * model_width, :]
            for position in range(up_blocks)
        ]
        local_terms = jnp.stack(pieces, axis=1)
        partial_value = lax.psum_scatter(local_terms, "dp", scatter_dimension=0, tiled=True)
        grad_own = lax.psum_scatter(
            partial_value.astype(jnp.bfloat16), "own", scatter_dimension=1, tiled=True
        ).astype(jnp.float32)
        full_grad = lax.all_gather(grad_own.astype(jnp.bfloat16), "dp", axis=0, tiled=True).astype(
            grad_own.dtype
        )
        row_start = lax.axis_index("dp") * shard_rows
        left_new = 0.5 * left_stat + 0.5 * jnp.einsum(
            "rbk,nbk->rbn", grad_own, full_grad, precision=highest
        )
        column_part = lax.dynamic_slice_in_dim(full_grad, row_start, shard_rows, 2)
        right_new = 0.5 * right_stat + 0.5 * jnp.einsum(
            "nbr,nbk->rbk", column_part, full_grad, precision=highest
        )
        lefted = jnp.einsum("rbn,nbk->rbk", left_root, full_grad, precision=highest)
        precond = jnp.zeros_like(grad_own) + jnp.einsum(
            "rbn,nbk->rbk",
            lefted,
            lax.all_gather(right_root.astype(jnp.bfloat16), "dp", axis=0, tiled=True).astype(
                jnp.float32
            ),
            precision=highest,
        )
        square_sums = lax.psum(jnp.sum(precond * precond, axis=(0, 2)), "dp")
        step_scale = lax.rsqrt(square_sums / (model_width * model_width) + norm_eps)
        new_blocks = blocks - block_rate * precond * step_scale[None, :, None]
        vector_grad = lax.psum(vector_terms, ("dp", "own"))
    moment_new = 0.5 * moment + 0.5 * vector_grad
    row_squares = jnp.mean(moment_new * moment_new, axis=1, keepdims=True)
    vector_new = vectors - vector_rate * moment_new * lax.rsqrt(row_squares + norm_eps)
    return (
        mixed,
        grad_tokens,
        grad_own,
        left_new,
        right_new,
        new_blocks,
        vector_grad,
        moment_new,
        vector_new,
    )


def solution(mesh):
    placed = (
        P(("dp", "own"), None, None),
        P(("dp", "own"), None, None),
        P(("dp", "own"), None),
        P(("dp", "own"), None),
        P(("dp", "own"), None),
        P("dp", "own", None),
        P("dp", "own", None),
        P("dp", "own", None),
        P("dp", "own", None),
        P("dp", "own", None),
        P(),
        P(),
    )
    return jax.shard_map(
        shards,
        mesh=mesh,
        in_specs=placed,
        out_specs=(
            P(("dp", "own"), None, None),
            P(("dp", "own"), None, None),
            P("dp", "own", None),
            P("dp", "own", None),
            P("dp", "own", None),
            P("dp", "own", None),
            P(),
            P(),
            P(),
        ),
        check_vma=False,
    )
```

```python
import math

import jax
import jax.numpy as jnp
from jax import lax
from jax.experimental import pallas as pl
from jax.experimental.pallas import tpu as pltpu
from jax.sharding import PartitionSpec as P

HEAD_DIM = 64


norm_eps = 1e-06
block_rate = 0.03
vector_rate = 0.04
highest = lax.Precision.HIGHEST


def layer_norm(values, norm_gain, norm_bias):
    center = values - jnp.mean(values, axis=-1, keepdims=True)
    spread = jnp.mean(center * center, axis=-1, keepdims=True)
    return center * lax.rsqrt(spread + norm_eps) * norm_gain + norm_bias


def gelu_exact(values):
    return jax.nn.gelu(values, approximate=False)


BOTH = ("dp", "own")
low = jnp.bfloat16
wide = jnp.float32
MIB = 2**20


def swap_pairs():
    return [(i, i ^ 1) for i in range(32)]


def plane_pairs(step):
    pairs = []
    for i in range(32):
        place, core = i // 2, i % 2
        flip = (1, 2)[step ^ core]
        pairs.append((i, (place ^ flip) * 2 + core))
    return pairs


def line_pairs(shift):
    return [(i, (i + 8 * shift) % 32) for i in range(32)]


def send(value, pairs):
    return lax.ppermute(value, BOTH, pairs)


def after(value, *others):
    return lax.optimization_barrier((value,) + others)[0]


def pick(value, index, axis):
    return lax.dynamic_index_in_dim(value, index, axis, keepdims=False)


def first_core():
    return lax.axis_index("own") == 0


def halves(value):
    middle = value.shape[-1] // 2
    lower, upper = value[..., :middle], value[..., middle:]
    return jnp.where(first_core(), lower, upper), jnp.where(first_core(), upper, lower)


def in_core_order(mine, theirs, axis):
    return jnp.where(
        first_core(),
        jnp.concatenate([mine, theirs], axis=axis),
        jnp.concatenate([theirs, mine], axis=axis),
    )


def spots(place, half):
    first, second = half + 1, 2 - half
    return [
        place,
        jnp.bitwise_xor(place, first),
        jnp.bitwise_xor(place, second),
        jnp.bitwise_xor(place, 3),
    ]


def gather_plane(value):
    near = send(value, plane_pairs(0))
    far = send(jnp.stack([value, near]), plane_pairs(1))
    return near, far


def here():
    device = lax.axis_index("dp")
    return device // 4, device % 4, lax.axis_index("own")


def dot(left, right, left_axis=1, right_axis=0):
    return lax.dot_general(
        left, right, (((left_axis,), (right_axis,)), ((), ())), preferred_element_type=wide
    )


def on_chip():
    return pl.BlockSpec(memory_space=pltpu.VMEM)


def params(limit):
    return pltpu.CompilerParams(vmem_limit_bytes=limit * MIB)


def cost(flops, moved):
    return pl.CostEstimate(flops=flops, bytes_accessed=moved, transcendentals=0)


def weight_kernel(*refs):
    sources, out_ref = refs[:6], refs[6]
    line, place, core = here()
    for other in range(2):
        half = core if other == 0 else 1 - core
        group = sources[other * 3 : other * 3 + 3]
        count, rows, columns = group[0].shape[1:]
        column_slice = pl.ds(pl.multiple_of(half * columns, columns), columns)
        for number, spot in enumerate(spots(place, half)):
            for shift in range(4):
                start = (lax.rem(line - shift + 4, 4) * 4 + spot) * rows
                row_slice = pl.ds(pl.multiple_of(start, rows), rows)
                for block in range(count):
                    if number < 2:
                        piece = group[number][shift, block]
                    else:
                        piece = group[2][number - 2, shift, block]
                    out_ref[block, row_slice, column_slice] = piece


def place_weights(parts):
    count, rows, columns = parts[0].shape[1:]
    full = rows * 16
    return pl.pallas_call(
        weight_kernel,
        out_shape=jax.ShapeDtypeStruct((count, full, columns * 2), low),
        in_specs=[on_chip()] * 6,
        out_specs=on_chip(),
        compiler_params=params(24),
        cost_estimate=cost(0, 8 * full * count * columns),
    )(*parts)


def columns_by_core(value):
    keep, give = halves(jnp.transpose(value.astype(low), (1, 0, 2)))
    return in_core_order(keep, send(give, swap_pairs()), 0)


def gather_chunk(chunk):
    stacked = jnp.stack([chunk] + [send(chunk, line_pairs(shift)) for shift in (1, 2, 3)])
    near, far = gather_plane(stacked)
    parts = [stacked, near, far]
    return place_weights(parts + [send(part, swap_pairs()) for part in parts]), far


def gather_roots(left_root, right_root):
    line, place, core = here()
    both = jnp.concatenate([left_root, right_root], axis=2)
    every = columns_by_core(
        both.reshape(left_root.shape[0], left_root.shape[1] * 2, left_root.shape[2])
    )
    rows, columns = every.shape[1:]
    every = every.reshape(3, 4, 2, rows, columns)
    line_parts = [pick(every, line, 1)]
    for shift in (1, 2, 3):
        given = pick(every, lax.rem(line + shift, 4), 1)
        line_parts.append(send(given, line_pairs(shift)))
    stacked = jnp.stack(line_parts)
    near, far = gather_plane(stacked)
    parts = [stacked, near, far]
    return parts + [send(part, swap_pairs()) for part in parts]


def reduce_start(mine, theirs):
    line, place, core = here()
    count, full, columns = mine.shape
    summed = mine + send(theirs, swap_pairs()).astype(wide)
    pieces = summed.reshape(count, 4, 4, full // 16, columns)
    spot = spots(place, core)
    give = jnp.stack([pick(pieces, spot[1], 2), pick(pieces, spot[3], 2)]).astype(low)
    return give, pick(pieces, spot[0], 2), pick(pieces, spot[2], 2)


def reduce_rest(give, kept, passed):
    line, place, core = here()
    got = send(give, plane_pairs(0)).astype(wide)
    passed = passed + got[1]
    kept = kept + got[0] + send(passed.astype(low), plane_pairs(1)).astype(wide)
    total = pick(kept, line, 0)
    for shift in (1, 2, 3):
        given = pick(kept, lax.rem(line + shift, 4), 0).astype(low)
        total = total + send(given, line_pairs(shift)).astype(wide)
    return total.astype(low)


def step_kernel(*refs):
    grads, roots = refs[:6], refs[6:12]
    out_ref, grad_ref, rows_ref, left_ref, right_ref, lefted_ref, cross_ref, step_ref = refs[12:]
    line, place, core = here()
    rows, columns = grads[0].shape[1:]

    def rows_of(row_line, spot):
        return pl.ds(pl.multiple_of((row_line * 4 + spot) * rows, rows), rows)

    def column_half(half):
        return pl.ds(pl.multiple_of(half * columns, columns), columns)

    for other in range(2):
        half = core if other == 0 else 1 - core
        group = grads[3 * other : 3 * other + 3]
        root_group = roots[3 * other : 3 * other + 3]
        for number, spot in enumerate(spots(place, half)):
            for step in range(4):
                target = (rows_of(step, spot), column_half(half))
                if number < 2:
                    grad_ref[target] = group[number][step]
                else:
                    grad_ref[target] = group[2][number - 2, step]
                target = (rows_of(lax.rem(line - step + 4, 4), spot), column_half(half))
                for kind, root_ref in enumerate((left_ref, right_ref)):
                    if number < 2:
                        root_ref[target] = root_group[number][step, 0, kind]
                    else:
                        root_ref[target] = root_group[2][number - 2, step, 0, kind]
    for row_line in range(4):
        rows_ref[row_line * rows : (row_line + 1) * rows, :] = grad_ref[rows_of(row_line, place), :]
    left = dot(rows_ref[...], grad_ref[column_half(core), :], 1, 1)
    cross_ref[...] = dot(grad_ref[...], grad_ref[:, column_half(core)], 0, 0)
    lefted_ref[...] = dot(left_ref[...], grad_ref[...]).astype(low)
    stepped = dot(lefted_ref[...], right_ref[...])
    step_ref[...] = stepped
    size = stepped.shape[0] * stepped.shape[1]
    squares = jnp.sum(jnp.sum(stepped * stepped, axis=0, keepdims=True), axis=1, keepdims=True)
    step_scale = lax.rsqrt(squares / size + norm_eps)
    for row_line in range(4):
        part = slice(row_line * rows, (row_line + 1) * rows)
        target = rows_of(row_line, place)
        out_ref[row_line, 0] = grads[0][row_line]
        out_ref[row_line, 1] = left[part].astype(low)
        out_ref[row_line, 2] = cross_ref[target, :].astype(low)
        out_ref[row_line, 3] = (step_ref[target, column_half(core)] * step_scale).astype(low)


def step_chunk(own, roots, number):
    near, far = gather_plane(own)
    parts = [own, near, far]
    parts = parts + [send(part, swap_pairs()) for part in parts]
    lines, rows, columns = own.shape
    full = rows * 16
    square = (full, columns * 2)

    def root_spec(root):
        lead = root.ndim - 4
        block = root.shape[:lead] + (1,) + root.shape[lead + 1 :]
        return pl.BlockSpec(block, lambda step: (0,) * lead + (number, 0, 0, 0))

    return pl.pallas_call(
        step_kernel,
        grid=(1,),
        out_shape=jax.ShapeDtypeStruct((lines, 4, rows, columns), low),
        in_specs=[on_chip()] * 6 + [root_spec(root) for root in roots],
        out_specs=on_chip(),
        scratch_shapes=[
            pltpu.VMEM(square, low),
            pltpu.VMEM((lines * rows, columns * 2), low),
            pltpu.VMEM(square, low),
            pltpu.VMEM(square, low),
            pltpu.VMEM(square, low),
            pltpu.VMEM((full, columns), wide),
            pltpu.VMEM(square, wide),
        ],
        compiler_params=params(32),
        cost_estimate=cost(6 * full**3, 16 * full * full),
    )(*parts, *roots)


def return_chunk(made):
    line, place, core = here()
    parts = [pick(made, line, 0)]
    for shift in (1, 2, 3):
        given = pick(made, lax.rem(line + shift, 4), 0)
        parts.append(send(given, line_pairs(shift)))
    stacked = jnp.stack(parts)
    return jnp.stack([pick(stacked, lax.rem(line - block + 4, 4), 0) for block in range(4)])


def last_kernel(
    attn, attn_other, up, up_other, down, down_other, blocks, left_stat, right_stat, *outs
):
    grad_out, left_out, right_out, block_out = outs
    core = lax.axis_index("own")
    columns = attn.shape[3]

    def update(number, which, mine, mine_index, theirs, theirs_index):
        for source, index, half in ((mine, mine_index, which), (theirs, theirs_index, 1 - which)):
            part = slice(half * columns, (half + 1) * columns)
            pieces = [source[index, kind].astype(wide) for kind in range(4)]
            grad_out[number, :, part] = pieces[0]
            left_out[number, :, part] = 0.5 * left_stat[number, :, part] + 0.5 * pieces[1]
            right_out[number, :, part] = 0.5 * right_stat[number, :, part] + 0.5 * pieces[2]
            block_out[number, :, part] = blocks[number, :, part] - block_rate * pieces[3]

    @pl.when(core == 0)
    def first():
        for number in range(4):
            update(number, 0, attn, number, attn_other, number)
        for number in range(2):
            update(4 + number, 0, up, number, up_other, number)

    @pl.when(core == 1)
    def second():
        for number in range(2):
            update(number, 1, up, 2 + number, up_other, number)
        for number in range(4):
            update(2 + number, 1, down, number, down_other, number)


def update_blocks(made, blocks, left_stat, right_stat):
    attn, up, down = made
    attn_other = send(attn, [(i, i ^ 1) for i in range(1, 32, 2)])
    down_other = send(down, [(i, i ^ 1) for i in range(0, 32, 2)])
    up_other = send(jnp.where(first_core(), up[2:], up[:2]), swap_pairs())
    turned = [jnp.transpose(value, (1, 0, 2)) for value in (blocks, left_stat, right_stat)]
    shape = jax.ShapeDtypeStruct(turned[0].shape, wide)
    outs = pl.pallas_call(
        last_kernel,
        out_shape=(shape,) * 4,
        in_specs=[on_chip()] * 9,
        out_specs=(on_chip(),) * 4,
        compiler_params=params(24),
        cost_estimate=cost(0, 32 * shape.size),
    )(attn, attn_other, up, up_other, down, down_other, *turned)
    return [jnp.transpose(value, (1, 0, 2)) for value in outs]


def head_masks():
    lane = lax.broadcasted_iota(jnp.int32, (1, 2 * HEAD_DIM), 1)
    return [(lane < HEAD_DIM).astype(wide).astype(low), (lane >= HEAD_DIM).astype(wide).astype(low)]


def head_shares(query, key, same):
    scores = dot(query, key, 1, 1) * HEAD_DIM ** (-0.5)
    scores = jnp.where(same, scores, -1e30)
    raised = jnp.exp(scores - jnp.max(scores, axis=-1, keepdims=True))
    return raised / jnp.sum(raised, axis=-1, keepdims=True)


def attend_kernel(buffer, weights, seg_column, seg_row, made_ref, context_ref, answer_ref):
    same = seg_column[...] == seg_row[...]
    for kind in range(3):
        made_ref[kind] = dot(buffer[...], weights[kind]).astype(low)
    width = 2 * HEAD_DIM
    for pair in range(buffer.shape[1] // width):
        part = slice(pair * width, (pair + 1) * width)
        query, key, value = (made_ref[kind, :, part] for kind in range(3))
        context = None
        for mask in head_masks():
            shares = head_shares(query, key * mask, same).astype(low)
            term = dot(shares, value * mask)
            context = term if context is None else context + term
        context_ref[:, part] = context.astype(low)
    answer_ref[...] = dot(context_ref[...], weights[3]).astype(low)


def attend(buffer, weights, segment):
    shape = jax.ShapeDtypeStruct(buffer.shape, low)
    rows, width = buffer.shape
    return pl.pallas_call(
        attend_kernel,
        out_shape=(jax.ShapeDtypeStruct((3,) + buffer.shape, low), shape, shape),
        in_specs=[on_chip()] * 4,
        out_specs=(on_chip(),) * 3,
        compiler_params=params(32),
        cost_estimate=cost(12 * rows * width * width, 12 * width * width),
    )(buffer, weights, segment[:, None], segment[None, :])


def attend_back_kernel(
    buffer,
    weights,
    seg_column,
    seg_row,
    made,
    context,
    grad_answer,
    mine_ref,
    theirs_ref,
    grad_buffer_ref,
    grad_context_ref,
    grads_ref,
):
    same = seg_column[...] == seg_row[...]
    core = lax.axis_index("own")
    grad_context_ref[...] = dot(grad_answer[...], weights[3], 1, 1).astype(low)
    width = 2 * HEAD_DIM
    for pair in range(buffer.shape[1] // width):
        part = slice(pair * width, (pair + 1) * width)
        query, key, value = (made[kind, :, part] for kind in range(3))
        above = grad_context_ref[:, part]
        sums = [None] * 3
        for mask in head_masks():
            key_head = key * mask
            shares = head_shares(query, key_head, same)
            grad_shares = dot(above, value * mask, 1, 1)
            inner = jnp.sum(shares * grad_shares, axis=-1, keepdims=True)
            grad_scores = (shares * (grad_shares - inner)).astype(low)
            terms = (
                dot(grad_scores, key_head),
                dot(grad_scores, query * mask, 0, 0),
                dot(shares.astype(low), above * mask, 0, 0),
            )
            sums = [
                term if total is None else total + term for term, total in zip(terms, sums)
            ]
        for kind, factor in enumerate((HEAD_DIM ** (-0.5), HEAD_DIM ** (-0.5), 1.0)):
            grads_ref[kind, :, part] = (sums[kind] * factor).astype(low)
    columns = mine_ref.shape[2]
    for half, out_ref, kind_of in ((core, mine_ref, wide), (1 - core, theirs_ref, low)):
        part = pl.ds(pl.multiple_of(half * columns, columns), columns)
        for kind in range(3):
            out_ref[kind] = dot(buffer[...], grads_ref[kind, :, part], 0, 0).astype(kind_of)
        out_ref[3] = dot(context[...], grad_answer[:, part], 0, 0).astype(kind_of)
    total = dot(grads_ref[0], weights[0], 1, 1)
    total = total + dot(grads_ref[1], weights[1], 1, 1)
    total = total + dot(grads_ref[2], weights[2], 1, 1)
    grad_buffer_ref[...] = total.astype(low)


def attend_back(buffer, weights, segment, made, context, grad_answer):
    rows, width = buffer.shape
    half = (4, width, width // 2)
    return pl.pallas_call(
        attend_back_kernel,
        out_shape=(
            jax.ShapeDtypeStruct(half, wide),
            jax.ShapeDtypeStruct(half, low),
            jax.ShapeDtypeStruct(buffer.shape, low),
        ),
        in_specs=[on_chip()] * 7,
        out_specs=(on_chip(),) * 3,
        scratch_shapes=[pltpu.VMEM(buffer.shape, low), pltpu.VMEM((3,) + buffer.shape, low)],
        compiler_params=params(40),
        cost_estimate=cost(24 * rows * width * width, 24 * width * width),
    )(buffer, weights, segment[:, None], segment[None, :], made, context, grad_answer)


def normal_parts(values):
    center = values - jnp.mean(values, axis=-1, keepdims=True)
    spread = jnp.mean(center * center, axis=-1, keepdims=True)
    return center, lax.rsqrt(spread + norm_eps)


def token_kernel(
    tokens,
    above,
    placing,
    returned,
    weighting,
    gate_slope,
    vectors,
    w_up,
    w_down,
    mixed_ref,
    packed_ref,
    grad_hidden_ref,
    logit_ref,
    vector_ref,
    second_ref,
    active_ref,
    inner_ref,
    hidden,
    result,
    grad_second,
):
    step = pl.program_id(0)

    @pl.when(step == 0)
    def prepare():
        unpacked = dot(placing[...], returned[...])
        values = tokens[...].astype(wide) + weighting[...] * unpacked
        hidden[...] = values
        center, inverse = normal_parts(values)
        second_ref[...] = (center * inverse * vectors[3:4] + vectors[4:5]).astype(low)
        result[...] = values
        grad_second[...] = jnp.zeros_like(grad_second)

    before = dot(second_ref[...], w_up[0])
    share = 0.5 + 0.5 * lax.erf(before * (0.5**0.5))
    density = jnp.exp(before * before * -0.5) * (0.5 / math.pi) ** 0.5
    active = (before * share).astype(low)
    active_ref[0] = active
    result[...] += dot(active, w_down[0])
    grad_active = dot(above[...], w_down[0], 1, 1)
    grad_inner = (grad_active * (share + before * density)).astype(low)
    inner_ref[0] = grad_inner
    grad_second[...] += dot(grad_inner, w_up[0], 1, 1)

    @pl.when(step == pl.num_programs(0) - 1)
    def finish():
        mixed_ref[...] = result[...].astype(low)
        center, inverse = normal_parts(hidden[...])
        scaled = center * inverse
        grads = grad_second[...]
        vector_ref[0:1] = jnp.sum(grads * scaled, axis=0, keepdims=True)
        vector_ref[1:2] = jnp.sum(grads, axis=0, keepdims=True)
        pulled = grads * vectors[3:4]
        pulled = (
            pulled
            - jnp.mean(pulled, axis=-1, keepdims=True)
            - scaled * jnp.mean(pulled * scaled, axis=-1, keepdims=True)
        )
        grad_hidden = above[...].astype(wide) + inverse * pulled
        grad_hidden_ref[...] = grad_hidden
        weighted = (grad_hidden * weighting[...]).astype(low)
        packed_ref[...] = dot(placing[...], weighted, 0, 0).astype(low)
        unpacked = dot(placing[...], returned[...])
        logit_ref[...] = gate_slope[...] * jnp.sum(grad_hidden * unpacked, axis=-1, keepdims=True)


def token_layer(tokens, above, placing, returned, weighting, gate_slope, vectors, w_up, w_down):
    count, width = tokens.shape
    slots = placing.shape[1]
    blocks = w_up.shape[0]
    block = pl.BlockSpec((1, width, width), lambda step: (step, 0, 0))
    hidden_block = pl.BlockSpec((1, count, width), lambda step: (step, 0, 0))

    def whole(*shape):
        return pl.BlockSpec(shape, lambda step: (0,) * len(shape))

    return pl.pallas_call(
        token_kernel,
        grid=(blocks,),
        out_shape=(
            jax.ShapeDtypeStruct((count, width), low),
            jax.ShapeDtypeStruct((slots, width), low),
            jax.ShapeDtypeStruct((count, width), wide),
            jax.ShapeDtypeStruct((count, 1), wide),
            jax.ShapeDtypeStruct((2, width), wide),
            jax.ShapeDtypeStruct((count, width), low),
            jax.ShapeDtypeStruct((blocks, count, width), low),
            jax.ShapeDtypeStruct((blocks, count, width), low),
        ),
        in_specs=[
            whole(count, width),
            whole(count, width),
            whole(count, slots),
            whole(slots, width),
            whole(count, 1),
            whole(count, 1),
            whole(*vectors.shape),
            block,
            block,
        ],
        out_specs=(
            whole(count, width),
            whole(slots, width),
            whole(count, width),
            whole(count, 1),
            whole(2, width),
            whole(count, width),
            hidden_block,
            hidden_block,
        ),
        scratch_shapes=[pltpu.VMEM((count, width), wide)] * 3,
        compiler_params=params(56),
        cost_estimate=cost(8 * blocks * count * width * width, 8 * blocks * width * width),
    )(tokens, above, placing, returned, weighting, gate_slope, vectors, w_up, w_down)


def outer_kernel(left, right, mine_ref, theirs_ref):
    core = lax.axis_index("own")
    columns = mine_ref.shape[2]
    for half, out_ref, kind_of in ((core, mine_ref, wide), (1 - core, theirs_ref, low)):
        part = pl.ds(pl.multiple_of(half * columns, columns), columns)
        out_ref[0] = dot(left[0], right[0, :, part], 0, 0).astype(kind_of)


def outer_halves(left, right):
    count, width = left.shape[1:]
    blocks = max(left.shape[0], right.shape[0])

    def spec(value):
        if value.shape[0] == 1:
            return pl.BlockSpec((1, count, width), lambda step: (0, 0, 0))
        return pl.BlockSpec((1, count, width), lambda step: (step, 0, 0))

    out_spec = pl.BlockSpec((1, width, width // 2), lambda step: (step, 0, 0))
    shape = (blocks, width, width // 2)
    return pl.pallas_call(
        outer_kernel,
        grid=(blocks,),
        out_shape=(jax.ShapeDtypeStruct(shape, wide), jax.ShapeDtypeStruct(shape, low)),
        in_specs=[spec(left), spec(right)],
        out_specs=(out_spec, out_spec),
        compiler_params=params(32),
        cost_estimate=cost(2 * blocks * count * width * width, 5 * blocks * width * width),
    )(left, right)


def exchange(value, n_data):
    capacity, width = value.shape
    moved = lax.all_to_all(
        value.reshape(n_data, capacity // n_data, width), "dp", split_axis=0, concat_axis=0, tiled=True
    )
    return moved.reshape(capacity, width)


def block_shards(
    tokens,
    cotangent,
    selected,
    packing,
    segments,
    blocks,
    left_stat,
    right_stat,
    left_root,
    right_root,
    vectors,
    moment,
):
    model_width = tokens.shape[2]
    token_count = tokens.shape[0] * tokens.shape[1]
    n_data = lax.axis_size("dp")
    capacity = packing.shape[1]
    every = columns_by_core(blocks)
    w_attn, unused = gather_chunk(every[:4])
    w_up, unused = gather_chunk(every[4:8])
    w_down, arrived = gather_chunk(every[8:])
    roots = gather_roots(after(left_root, arrived), right_root)
    own_tokens = tokens.reshape(token_count, model_width)
    inputs = own_tokens.astype(wide)
    chosen = selected.reshape(token_count)
    normed_one, norm_one_back = jax.vjp(layer_norm, inputs, vectors[0], vectors[1])
    first_low = normed_one.astype(low)
    first_wide = first_low.astype(wide)
    gate_values = jax.nn.sigmoid(jnp.sum(first_wide * vectors[2], axis=-1))
    before = jnp.cumsum(chosen) - 1
    slot_index = jnp.where(chosen == 1, packing[0][jnp.clip(before, 0, capacity - 1)], -1)
    placing = (slot_index[:, None] == jnp.arange(capacity, dtype=jnp.int32)[None, :]).astype(low)
    packed = jnp.einsum("tm,td->md", placing, first_low, preferred_element_type=wide).astype(low)
    buffer = exchange(packed, n_data)
    segment = segments[0]
    made, context, answer = attend(buffer, w_attn, segment)
    returned = exchange(answer, n_data)
    weighting = jnp.where(chosen == 1, gate_values, 0.0)
    gate_slope = weighting * (1.0 - gate_values)
    above = cotangent.reshape(token_count, model_width)
    mixed, grad_packed, grad_hidden, grad_logit, vector_two, second_low, active, grad_inner = (
        token_layer(
            own_tokens,
            above,
            placing,
            returned,
            weighting[:, None],
            gate_slope[:, None],
            vectors,
            w_up,
            w_down,
        )
    )
    grad_answer = exchange(grad_packed, n_data)
    down_start = reduce_start(*outer_halves(active, above[None]))
    up_start = reduce_start(*outer_halves(second_low[None], grad_inner))
    grad_answer = after(grad_answer, down_start[0], up_start[0])
    mine, theirs, grad_buffer = attend_back(buffer, w_attn, segment, made, context, grad_answer)
    attn_start = reduce_start(mine, theirs)
    grad_sent = exchange(grad_buffer, n_data)
    sent = []
    for number, start in ((2, down_start), (1, up_start), (0, attn_start)):
        sent.insert(0, return_chunk(step_chunk(reduce_rest(*start), roots, number)))
    grad_own, left_new, right_new, new_blocks = update_blocks(sent, blocks, left_stat, right_stat)
    grad_first = jnp.einsum("tm,md->td", placing, grad_sent, preferred_element_type=wide)
    grad_first = grad_first + grad_logit * vectors[2][None, :]
    grad_router = jnp.sum(grad_logit * first_wide, axis=0)
    grad_input_part, grad_gain_one, grad_bias_one = norm_one_back(grad_first)
    grad_tokens = (grad_hidden + grad_input_part).astype(low).reshape(tokens.shape)
    vector_terms = jnp.stack(
        [grad_gain_one, grad_bias_one, grad_router, vector_two[0], vector_two[1]]
    )
    vector_grad = jnp.sum(lax.all_gather(vector_terms, BOTH), axis=0)
    moment_new = 0.5 * moment + 0.5 * vector_grad
    row_squares = jnp.mean(moment_new * moment_new, axis=1, keepdims=True)
    vector_new = vectors - vector_rate * moment_new * lax.rsqrt(row_squares + norm_eps)
    return (
        mixed.reshape(tokens.shape),
        grad_tokens,
        grad_own,
        left_new,
        right_new,
        new_blocks,
        vector_grad,
        moment_new,
        vector_new,
    )


def shards(
    tokens,
    cotangent,
    selected,
    packing,
    segments,
    blocks,
    left_stat,
    right_stat,
    left_root,
    right_root,
    vectors,
    moment,
):
    model_width = tokens.shape[2]
    token_count = tokens.shape[0] * tokens.shape[1]
    n_data = lax.axis_size("dp")
    n_owner = lax.axis_size("own")
    shard_rows = blocks.shape[0]
    own_blocks = blocks.shape[1]
    up_blocks = (own_blocks * n_owner - 4) // 2
    capacity = packing.shape[1]
    per_peer = capacity // n_data
    head_count = model_width // HEAD_DIM
    score_scale = HEAD_DIM ** (-0.5)
    flat_weights = blocks.astype(jnp.bfloat16).reshape(1, shard_rows * own_blocks * model_width)
    gathered = lax.all_gather(flat_weights, ("dp", "own"), axis=0, tiled=True)
    gathered = gathered.reshape(n_data, n_owner, shard_rows, own_blocks, model_width)

    def matrix(number):
        return gathered[:, number // own_blocks, :, number % own_blocks, :].reshape(
            model_width, model_width
        )

    w_query = matrix(0)
    w_key = matrix(1)
    w_value = matrix(2)
    w_out = matrix(3)
    w_up = jnp.concatenate([matrix(4 + position) for position in range(up_blocks)], axis=1)
    w_down = jnp.concatenate(
        [matrix(4 + up_blocks + position) for position in range(up_blocks)], axis=0
    )
    inputs = tokens.reshape(token_count, model_width).astype(jnp.float32)
    chosen = selected.reshape(token_count)
    normed_one, norm_one_back = jax.vjp(layer_norm, inputs, vectors[0], vectors[1])
    first_low = normed_one.astype(jnp.bfloat16)
    first_wide = first_low.astype(jnp.float32)
    gate_values = jax.nn.sigmoid(jnp.dot(first_wide, vectors[2], precision=highest))
    before = jnp.cumsum(chosen) - 1
    slot_index = jnp.where(chosen == 1, packing[0][jnp.clip(before, 0, capacity - 1)], -1)
    placing = (slot_index[None, :] == jnp.arange(capacity, dtype=jnp.int32)[:, None]).astype(
        jnp.bfloat16
    )
    packed = jnp.dot(placing, first_low, preferred_element_type=jnp.float32).astype(jnp.bfloat16)
    buffer = lax.all_to_all(
        packed.reshape(n_data, per_peer, model_width), "dp", split_axis=0, concat_axis=0, tiled=True
    )
    buffer = buffer.reshape(capacity, model_width)

    def project(matrix_in):
        made = jnp.dot(buffer, matrix_in, preferred_element_type=jnp.float32).astype(jnp.bfloat16)
        return made.reshape(capacity, head_count, HEAD_DIM)

    query_rows = project(w_query)
    key_rows = project(w_key)
    value_rows = project(w_value)
    segment = segments[0]
    block_rows = math.gcd(capacity, 512)
    starts = jnp.arange(capacity // block_rows, dtype=jnp.int32) * block_rows

    def masked_scores():
        scores = (
            jnp.einsum("qhd,khd->hqk", query_rows, key_rows, preferred_element_type=jnp.float32)
            * score_scale
        )
        same_segment = segment[:, None] == segment[None, :]
        return (jnp.where(same_segment[None, :, :], scores, -1e30), query_rows)

    def forward_block(first_row):
        scores, unused_block = masked_scores()
        largest = jnp.max(scores, axis=-1, keepdims=True)
        raised = jnp.exp(scores - largest)
        row_total = jnp.sum(raised, axis=-1, keepdims=True)
        shares = (raised / row_total).astype(jnp.bfloat16)
        context_part = jnp.einsum(
            "hqk,khd->qhd", shares, value_rows, preferred_element_type=jnp.float32
        )
        return (context_part.astype(jnp.bfloat16), largest[..., 0] + jnp.log(row_total[..., 0]))

    context_blocks, lse_blocks = lax.map(forward_block, starts)
    context = context_blocks.reshape(capacity, model_width)
    answer = jnp.dot(context, w_out, preferred_element_type=jnp.float32).astype(jnp.bfloat16)
    returned = lax.all_to_all(
        answer.reshape(n_data, per_peer, model_width), "dp", split_axis=0, concat_axis=0, tiled=True
    )
    returned = returned.reshape(capacity, model_width)
    unpacked = jnp.einsum("mt,md->td", placing, returned, preferred_element_type=jnp.float32)
    weighting = jnp.where(chosen == 1, gate_values, 0.0)
    hidden = inputs + weighting[:, None] * unpacked
    normed_two, norm_two_back = jax.vjp(layer_norm, hidden, vectors[3], vectors[4])
    second_low = normed_two.astype(jnp.bfloat16)
    pre_active = jnp.dot(second_low, w_up, preferred_element_type=jnp.float32)
    active_wide, gelu_back = jax.vjp(gelu_exact, pre_active)
    active = active_wide.astype(jnp.bfloat16)
    result = hidden + jnp.dot(active, w_down, preferred_element_type=jnp.float32)
    mixed = result.astype(jnp.bfloat16).reshape(tokens.shape)
    upstream = cotangent.reshape(token_count, model_width)
    grad_down = jnp.einsum("tf,td->fd", active, upstream, preferred_element_type=jnp.float32)
    grad_active = jnp.einsum("td,fd->tf", upstream, w_down, preferred_element_type=jnp.float32)
    grad_inner = gelu_back(grad_active)[0].astype(jnp.bfloat16)
    grad_up = jnp.einsum("td,tf->df", second_low, grad_inner, preferred_element_type=jnp.float32)
    grad_second = jnp.einsum("tf,df->td", grad_inner, w_up, preferred_element_type=jnp.float32)
    grad_hidden_part, grad_gain_two, grad_bias_two = norm_two_back(grad_second)
    grad_hidden = upstream.astype(jnp.float32) + grad_hidden_part
    grad_token_back = (grad_hidden * weighting[:, None]).astype(jnp.bfloat16)
    grad_packed = jnp.dot(placing, grad_token_back, preferred_element_type=jnp.float32).astype(
        jnp.bfloat16
    )
    router_pull = jnp.where(chosen == 1, jnp.sum(grad_hidden * unpacked, axis=-1), 0.0)
    grad_logit = router_pull * gate_values * (1.0 - gate_values)
    grad_answer = lax.all_to_all(
        grad_packed.reshape(n_data, per_peer, model_width),
        "dp",
        split_axis=0,
        concat_axis=0,
        tiled=True,
    )
    grad_answer = grad_answer.reshape(capacity, model_width)
    grad_out = jnp.einsum("md,me->de", context, grad_answer, preferred_element_type=jnp.float32)
    grad_context = jnp.einsum("me,de->md", grad_answer, w_out, preferred_element_type=jnp.float32)
    grad_context = grad_context.astype(jnp.bfloat16).reshape(capacity, head_count, HEAD_DIM)

    def backward_block(running, item_pair):
        first_row, lse_block = item_pair
        scores, query_block = masked_scores()
        shares_wide = jnp.exp(scores - lse_block[..., None])
        grad_shares = jnp.einsum(
            "qhd,khd->hqk", grad_context, value_rows, preferred_element_type=jnp.float32
        )
        inner_sum = jnp.sum(shares_wide * grad_shares, axis=-1, keepdims=True)
        grad_scores = (shares_wide * (grad_shares - inner_sum)).astype(jnp.bfloat16)
        grad_query_block = (
            jnp.einsum("hqk,khd->qhd", grad_scores, key_rows, preferred_element_type=jnp.float32)
            * score_scale
        )
        key_sum = (
            running[0]
            + jnp.einsum(
                "hqk,qhd->khd", grad_scores, query_block, preferred_element_type=jnp.float32
            )
            * score_scale
        )
        value_sum = running[1] + jnp.einsum(
            "hqk,qhd->khd",
            shares_wide.astype(jnp.bfloat16),
            grad_context,
            preferred_element_type=jnp.float32,
        )
        return ((key_sum, value_sum), grad_query_block)

    zeros_init = jnp.zeros((capacity, head_count, HEAD_DIM), jnp.float32)
    (key_total, value_total), query_grads = lax.scan(
        backward_block, (zeros_init, zeros_init), (starts, lse_blocks)
    )
    grad_query = query_grads.reshape(capacity, model_width).astype(jnp.bfloat16)
    grad_key = key_total.reshape(capacity, model_width).astype(jnp.bfloat16)
    grad_value = value_total.reshape(capacity, model_width).astype(jnp.bfloat16)
    grad_w_query = jnp.einsum("md,me->de", buffer, grad_query, preferred_element_type=jnp.float32)
    grad_w_key = jnp.einsum("md,me->de", buffer, grad_key, preferred_element_type=jnp.float32)
    grad_w_value = jnp.einsum("md,me->de", buffer, grad_value, preferred_element_type=jnp.float32)
    grad_buffer = jnp.einsum("me,de->md", grad_query, w_query, preferred_element_type=jnp.float32)
    grad_buffer = grad_buffer + jnp.einsum(
        "me,de->md", grad_key, w_key, preferred_element_type=jnp.float32
    )
    grad_buffer = grad_buffer + jnp.einsum(
        "me,de->md", grad_value, w_value, preferred_element_type=jnp.float32
    )
    grad_buffer = grad_buffer.astype(jnp.bfloat16)
    grad_sent = lax.all_to_all(
        grad_buffer.reshape(n_data, per_peer, model_width),
        "dp",
        split_axis=0,
        concat_axis=0,
        tiled=True,
    )
    grad_sent = grad_sent.reshape(capacity, model_width)
    grad_first = jnp.einsum("mt,md->td", placing, grad_sent, preferred_element_type=jnp.float32)
    grad_first = grad_first + grad_logit[:, None] * vectors[2][None, :]
    grad_router = jnp.sum(grad_logit[:, None] * first_wide, axis=0)
    grad_input_part, grad_gain_one, grad_bias_one = norm_one_back(grad_first)
    grad_tokens = (grad_hidden + grad_input_part).astype(jnp.bfloat16).reshape(tokens.shape)
    pieces = [grad_w_query, grad_w_key, grad_w_value, grad_out]
    pieces = pieces + [
        grad_up[:, position * model_width : (position + 1) * model_width]
        for position in range(up_blocks)
    ]
    pieces = pieces + [
        grad_down[position * model_width : (position + 1) * model_width, :]
        for position in range(up_blocks)
    ]
    local_terms = jnp.stack(pieces, axis=1)
    vector_terms = jnp.stack(
        [grad_gain_one, grad_bias_one, grad_router, grad_gain_two, grad_bias_two]
    )
    partial_value = lax.psum_scatter(local_terms, "dp", scatter_dimension=0, tiled=True)
    grad_own = lax.psum_scatter(
        partial_value.astype(jnp.bfloat16), "own", scatter_dimension=1, tiled=True
    ).astype(jnp.float32)
    vector_grad = lax.psum(vector_terms, ("dp", "own"))
    full_grad = lax.all_gather(grad_own.astype(jnp.bfloat16), "dp", axis=0, tiled=True).astype(
        grad_own.dtype
    )
    row_start = lax.axis_index("dp") * shard_rows
    left_new = 0.5 * left_stat + 0.5 * jnp.einsum(
        "rbk,nbk->rbn", grad_own, full_grad, precision=highest
    )
    column_part = lax.dynamic_slice_in_dim(full_grad, row_start, shard_rows, 2)
    right_new = 0.5 * right_stat + 0.5 * jnp.einsum(
        "nbr,nbk->rbk", column_part, full_grad, precision=highest
    )
    lefted = jnp.einsum("rbn,nbk->rbk", left_root, full_grad, precision=highest)
    precond = jnp.zeros_like(grad_own) + jnp.einsum(
        "rbn,nbk->rbk",
        lefted,
        lax.all_gather(right_root.astype(jnp.bfloat16), "dp", axis=0, tiled=True).astype(
            jnp.float32
        ),
        precision=highest,
    )
    square_sums = lax.psum(jnp.sum(precond * precond, axis=(0, 2)), "dp")
    step_scale = lax.rsqrt(square_sums / (model_width * model_width) + norm_eps)
    new_blocks = blocks - block_rate * precond * step_scale[None, :, None]
    moment_new = 0.5 * moment + 0.5 * vector_grad
    row_squares = jnp.mean(moment_new * moment_new, axis=1, keepdims=True)
    vector_new = vectors - vector_rate * moment_new * lax.rsqrt(row_squares + norm_eps)
    return (
        mixed,
        grad_tokens,
        grad_own,
        left_new,
        right_new,
        new_blocks,
        vector_grad,
        moment_new,
        vector_new,
    )


def solution(mesh):
    placed = (
        P(("dp", "own"), None, None),
        P(("dp", "own"), None, None),
        P(("dp", "own"), None),
        P(("dp", "own"), None),
        P(("dp", "own"), None),
        P("dp", "own", None),
        P("dp", "own", None),
        P("dp", "own", None),
        P("dp", "own", None),
        P("dp", "own", None),
        P(),
        P(),
    )
    small = mesh.shape["dp"] == 16 and mesh.shape["own"] == 2
    return jax.shard_map(
        block_shards if small else shards,
        mesh=mesh,
        in_specs=placed,
        out_specs=(
            P(("dp", "own"), None, None),
            P(("dp", "own"), None, None),
            P("dp", "own", None),
            P("dp", "own", None),
            P("dp", "own", None),
            P("dp", "own", None),
            P(),
            P(),
            P(),
        ),
        check_vma=False,
    )
```

```python
import math

import jax
import jax.numpy as jnp
from jax import lax
from jax.experimental import pallas as pl
from jax.experimental.pallas import tpu as pltpu
from jax.sharding import PartitionSpec as P

HEAD_DIM = 64


norm_eps = 1e-06
block_rate = 0.03
vector_rate = 0.04
highest = lax.Precision.HIGHEST


def layer_norm(values, norm_gain, norm_bias):
    center = values - jnp.mean(values, axis=-1, keepdims=True)
    spread = jnp.mean(center * center, axis=-1, keepdims=True)
    return center * lax.rsqrt(spread + norm_eps) * norm_gain + norm_bias


def gelu_exact(values):
    return jax.nn.gelu(values, approximate=False)


BOTH = ("dp", "own")
low = jnp.bfloat16
wide = jnp.float32
MIB = 2**20


def swap_pairs():
    return [(i, i ^ 1) for i in range(32)]


def plane_pairs(step):
    pairs = []
    for i in range(32):
        place, core = i // 2, i % 2
        flip = (1, 2)[step ^ core]
        pairs.append((i, (place ^ flip) * 2 + core))
    return pairs


def line_pairs(shift):
    return [(i, (i + 8 * shift) % 32) for i in range(32)]


def send(value, pairs):
    return lax.ppermute(value, BOTH, pairs)


def after(value, *others):
    return lax.optimization_barrier((value,) + others)[0]


def pick(value, index, axis):
    return lax.dynamic_index_in_dim(value, index, axis, keepdims=False)


def first_core():
    return lax.axis_index("own") == 0


def halves(value):
    middle = value.shape[-1] // 2
    lower, upper = value[..., :middle], value[..., middle:]
    return jnp.where(first_core(), lower, upper), jnp.where(first_core(), upper, lower)


def in_core_order(mine, theirs, axis):
    return jnp.where(
        first_core(),
        jnp.concatenate([mine, theirs], axis=axis),
        jnp.concatenate([theirs, mine], axis=axis),
    )


def spots(place, half):
    first, second = half + 1, 2 - half
    return [
        place,
        jnp.bitwise_xor(place, first),
        jnp.bitwise_xor(place, second),
        jnp.bitwise_xor(place, 3),
    ]


def here():
    device = lax.axis_index("dp")
    return device // 4, device % 4, lax.axis_index("own")


def dot(left, right, left_axis=1, right_axis=0):
    return lax.dot_general(
        left, right, (((left_axis,), (right_axis,)), ((), ())), preferred_element_type=wide
    )


def on_chip():
    return pl.BlockSpec(memory_space=pltpu.VMEM)


def params(limit):
    return pltpu.CompilerParams(vmem_limit_bytes=limit * MIB)


def cost(flops, moved):
    return pl.CostEstimate(flops=flops, bytes_accessed=moved, transcendentals=0)


def weight_kernel(*refs):
    sources, out_ref = refs[:4], refs[4]
    line, place, core = here()
    for other in range(2):
        half = core if other == 0 else 1 - core
        group = sources[other * 2 : other * 2 + 2]
        count, rows, columns = group[0].shape[2:]
        column_slice = pl.ds(pl.multiple_of(half * columns, columns), columns)
        for number, spot in enumerate(spots(place, half)):
            for shift in range(4):
                start = (lax.rem(line - shift + 4, 4) * 4 + spot) * rows
                row_slice = pl.ds(pl.multiple_of(start, rows), rows)
                for block in range(count):
                    piece = group[number // 2][number % 2, shift, block]
                    out_ref[block, row_slice, column_slice] = piece


def place_weights(parts):
    count, rows, columns = parts[0].shape[2:]
    full = rows * 16
    return pl.pallas_call(
        weight_kernel,
        out_shape=jax.ShapeDtypeStruct((count, full, columns * 2), low),
        in_specs=[on_chip()] * 4,
        out_specs=on_chip(),
        compiler_params=params(16),
        cost_estimate=cost(0, 8 * full * count * columns),
    )(*parts)


def columns_by_core(value):
    keep, give = halves(jnp.transpose(value.astype(low), (1, 0, 2)))
    return in_core_order(keep, send(give, swap_pairs()), 0)


def gather_line(chunk):
    return jnp.stack([chunk] + [send(chunk, line_pairs(shift)) for shift in (1, 2, 3)])


def with_other(first, far):
    return [first, far, send(first, swap_pairs()), send(far, swap_pairs())]


def roots_line(left_root, right_root):
    line, place, core = here()
    both = jnp.concatenate([left_root, right_root], axis=2)
    every = columns_by_core(
        both.reshape(left_root.shape[0], left_root.shape[1] * 2, left_root.shape[2])
    )
    rows, columns = every.shape[1:]
    every = every.reshape(3, 4, 2, rows, columns)
    line_parts = [pick(every, line, 1)]
    for shift in (1, 2, 3):
        given = pick(every, lax.rem(line + shift, 4), 1)
        line_parts.append(send(given, line_pairs(shift)))
    return jnp.stack(line_parts)


def reduce_start(mine, theirs):
    line, place, core = here()
    count, full, columns = mine.shape
    summed = mine + send(theirs, swap_pairs()).astype(wide)
    pieces = summed.reshape(count, 4, 4, full // 16, columns)
    spot = spots(place, core)
    give = jnp.stack([pick(pieces, spot[1], 2), pick(pieces, spot[3], 2)]).astype(low)
    return give, pick(pieces, spot[0], 2), pick(pieces, spot[2], 2)


def reduce_rest(starts):
    line, place, core = here()
    kept_list, passed_list = [], []
    for give, kept, passed in starts:
        got = send(give, plane_pairs(0)).astype(wide)
        kept_list.append(kept + got[0])
        passed_list.append((passed + got[1]).astype(low))
    got = send(jnp.stack(passed_list), plane_pairs(1)).astype(wide)
    kept = jnp.stack(kept_list) + got
    total = pick(kept, line, 1)
    for shift in (1, 2, 3):
        given = pick(kept, lax.rem(line + shift, 4), 1).astype(low)
        total = total + send(given, line_pairs(shift)).astype(wide)
    return total.astype(low)


def step_kernel(*refs):
    grads, roots = refs[:2], refs[2:6]
    out_ref, grad_ref, rows_ref, left_ref, right_ref, lefted_ref, cross_ref, step_ref = refs[6:]
    line, place, core = here()
    rows, columns = grads[0].shape[3:]

    def rows_of(row_line, spot):
        return pl.ds(pl.multiple_of((row_line * 4 + spot) * rows, rows), rows)

    def column_half(half):
        return pl.ds(pl.multiple_of(half * columns, columns), columns)

    for other in range(2):
        half = core if other == 0 else 1 - core
        root_group = roots[2 * other : 2 * other + 2]
        for number, spot in enumerate(spots(place, half)):
            for step in range(4):
                grad_ref[rows_of(step, spot), column_half(half)] = grads[other][number, 0, step]
                target = (rows_of(lax.rem(line - step + 4, 4), spot), column_half(half))
                root_piece = root_group[number // 2]
                left_ref[target] = root_piece[number % 2, step, 0, 0]
                right_ref[target] = root_piece[number % 2, step, 0, 1]
    for row_line in range(4):
        rows_ref[row_line * rows : (row_line + 1) * rows, :] = grad_ref[rows_of(row_line, place), :]
    left = dot(rows_ref[...], grad_ref[column_half(core), :], 1, 1)
    cross_ref[...] = dot(grad_ref[...], grad_ref[:, column_half(core)], 0, 0)
    lefted_ref[...] = dot(left_ref[...], grad_ref[...]).astype(low)
    stepped = dot(lefted_ref[...], right_ref[...])
    step_ref[...] = stepped
    size = stepped.shape[0] * stepped.shape[1]
    squares = jnp.sum(jnp.sum(stepped * stepped, axis=0, keepdims=True), axis=1, keepdims=True)
    step_scale = lax.rsqrt(squares / size + norm_eps)
    for row_line in range(4):
        part = slice(row_line * rows, (row_line + 1) * rows)
        target = rows_of(row_line, place)
        out_ref[0, row_line, 0] = grads[0][0, 0, row_line]
        out_ref[0, row_line, 1] = left[part].astype(low)
        out_ref[0, row_line, 2] = cross_ref[target, :].astype(low)
        out_ref[0, row_line, 3] = (step_ref[target, column_half(core)] * step_scale).astype(low)


def step_chunks(own, roots, number):
    near = send(own, plane_pairs(0))
    first = jnp.stack([own, near])
    mine = jnp.concatenate([first, send(first, plane_pairs(1))])
    theirs = send(mine, swap_pairs())
    chunks, lines, rows, columns = own.shape
    full = rows * 16
    square = (full, columns * 2)
    grad_spec = pl.BlockSpec((4, 1, lines, rows, columns), lambda step: (0, step, 0, 0, 0))
    root_spec = pl.BlockSpec(
        (2, lines, 1, 2, rows, columns), lambda step: (0, 0, number + step, 0, 0, 0)
    )
    return pl.pallas_call(
        step_kernel,
        grid=(chunks,),
        out_shape=jax.ShapeDtypeStruct((chunks, lines, 4, rows, columns), low),
        in_specs=[grad_spec] * 2 + [root_spec] * 4,
        out_specs=pl.BlockSpec((1, lines, 4, rows, columns), lambda step: (step, 0, 0, 0, 0)),
        scratch_shapes=[
            pltpu.VMEM(square, low),
            pltpu.VMEM((lines * rows, columns * 2), low),
            pltpu.VMEM(square, low),
            pltpu.VMEM(square, low),
            pltpu.VMEM(square, low),
            pltpu.VMEM((full, columns), wide),
            pltpu.VMEM(square, wide),
        ],
        compiler_params=params(32),
        cost_estimate=cost(6 * chunks * full**3, 16 * chunks * full * full),
    )(mine, theirs, *roots)


def return_chunks(made):
    line, place, core = here()
    parts = [pick(made, line, 1)]
    for shift in (1, 2, 3):
        given = pick(made, lax.rem(line + shift, 4), 1)
        parts.append(send(given, line_pairs(shift)))
    return jnp.stack(parts)


def last_kernel(attn, attn_other, pair, pair_other, blocks, left_stat, right_stat, *outs):
    grad_out, left_out, right_out, block_out = outs
    line, place, core = here()
    columns = attn.shape[4]

    def update(number, which, mine, theirs):
        for (source, index), half in ((mine, which), (theirs, 1 - which)):
            part = slice(half * columns, (half + 1) * columns)
            pieces = [source[index + (kind,)].astype(wide) for kind in range(4)]
            grad_out[number, :, part] = pieces[0]
            left_out[number, :, part] = 0.5 * left_stat[number, :, part] + 0.5 * pieces[1]
            right_out[number, :, part] = 0.5 * right_stat[number, :, part] + 0.5 * pieces[2]
            block_out[number, :, part] = blocks[number, :, part] - block_rate * pieces[3]

    @pl.when(core == 0)
    def first():
        for number in range(4):
            index = (lax.rem(line - number + 4, 4), 0)
            update(number, 0, (attn, index), (attn_other, index))
        for number in range(2):
            update(4 + number, 0, (pair, (number,)), (pair_other, (number,)))

    @pl.when(core == 1)
    def second():
        for number in range(6):
            update(number, 1, (pair, (2 + number,)), (pair_other, (number,)))


def in_block_order(pair):
    line, place, core = here()
    ordered = [pick(pair, lax.rem(line - block + 4, 4), 0) for block in range(4)]
    return jnp.concatenate([jnp.stack([value[kind] for value in ordered]) for kind in range(2)])


def update_blocks(attn, pair, pair_other, blocks, left_stat, right_stat):
    attn_other = send(attn, [(i, i ^ 1) for i in range(1, 32, 2)])
    turned = [jnp.transpose(value, (1, 0, 2)) for value in (blocks, left_stat, right_stat)]
    shape = jax.ShapeDtypeStruct(turned[0].shape, wide)
    outs = pl.pallas_call(
        last_kernel,
        out_shape=(shape,) * 4,
        in_specs=[on_chip()] * 7,
        out_specs=(on_chip(),) * 4,
        compiler_params=params(20),
        cost_estimate=cost(0, 32 * shape.size),
    )(attn, attn_other, pair, pair_other, *turned)
    return [jnp.transpose(value, (1, 0, 2)) for value in outs]


def head_masks():
    lane = lax.broadcasted_iota(jnp.int32, (1, 2 * HEAD_DIM), 1)
    return [(lane < HEAD_DIM).astype(wide).astype(low), (lane >= HEAD_DIM).astype(wide).astype(low)]


def head_shares(query, key, same):
    scores = dot(query, key, 1, 1) * HEAD_DIM ** (-0.5)
    scores = jnp.where(same, scores, -1e30)
    raised = jnp.exp(scores - jnp.max(scores, axis=-1, keepdims=True))
    return raised / jnp.sum(raised, axis=-1, keepdims=True)


def attend_kernel(buffer, weights, seg_column, seg_row, made_ref, context_ref, answer_ref):
    same = seg_column[...] == seg_row[...]
    for kind in range(3):
        made_ref[kind] = dot(buffer[...], weights[kind]).astype(low)
    width = 2 * HEAD_DIM
    for pair in range(buffer.shape[1] // width):
        part = slice(pair * width, (pair + 1) * width)
        query, key, value = (made_ref[kind, :, part] for kind in range(3))
        context = None
        for mask in head_masks():
            shares = head_shares(query, key * mask, same).astype(low)
            term = dot(shares, value * mask)
            context = term if context is None else context + term
        context_ref[:, part] = context.astype(low)
    answer_ref[...] = dot(context_ref[...], weights[3]).astype(low)


def attend(buffer, weights, segment):
    shape = jax.ShapeDtypeStruct(buffer.shape, low)
    rows, width = buffer.shape
    return pl.pallas_call(
        attend_kernel,
        out_shape=(jax.ShapeDtypeStruct((3,) + buffer.shape, low), shape, shape),
        in_specs=[on_chip()] * 4,
        out_specs=(on_chip(),) * 3,
        compiler_params=params(32),
        cost_estimate=cost(12 * rows * width * width, 12 * width * width),
    )(buffer, weights, segment[:, None], segment[None, :])


def attend_back_kernel(
    buffer,
    weights,
    seg_column,
    seg_row,
    made,
    context,
    grad_answer,
    mine_ref,
    theirs_ref,
    grad_buffer_ref,
    grad_context_ref,
    grads_ref,
):
    same = seg_column[...] == seg_row[...]
    core = lax.axis_index("own")
    grad_context_ref[...] = dot(grad_answer[...], weights[3], 1, 1).astype(low)
    width = 2 * HEAD_DIM
    for pair in range(buffer.shape[1] // width):
        part = slice(pair * width, (pair + 1) * width)
        query, key, value = (made[kind, :, part] for kind in range(3))
        above = grad_context_ref[:, part]
        sums = [None] * 3
        for mask in head_masks():
            key_head = key * mask
            shares = head_shares(query, key_head, same)
            grad_shares = dot(above, value * mask, 1, 1)
            inner = jnp.sum(shares * grad_shares, axis=-1, keepdims=True)
            grad_scores = (shares * (grad_shares - inner)).astype(low)
            terms = (
                dot(grad_scores, key_head),
                dot(grad_scores, query * mask, 0, 0),
                dot(shares.astype(low), above * mask, 0, 0),
            )
            sums = [
                term if total is None else total + term for term, total in zip(terms, sums)
            ]
        for kind, factor in enumerate((HEAD_DIM ** (-0.5), HEAD_DIM ** (-0.5), 1.0)):
            grads_ref[kind, :, part] = (sums[kind] * factor).astype(low)
    columns = mine_ref.shape[2]
    for half, out_ref, kind_of in ((core, mine_ref, wide), (1 - core, theirs_ref, low)):
        part = pl.ds(pl.multiple_of(half * columns, columns), columns)
        for kind in range(3):
            out_ref[kind] = dot(buffer[...], grads_ref[kind, :, part], 0, 0).astype(kind_of)
        out_ref[3] = dot(context[...], grad_answer[:, part], 0, 0).astype(kind_of)
    total = dot(grads_ref[0], weights[0], 1, 1)
    total = total + dot(grads_ref[1], weights[1], 1, 1)
    total = total + dot(grads_ref[2], weights[2], 1, 1)
    grad_buffer_ref[...] = total.astype(low)


def attend_back(buffer, weights, segment, made, context, grad_answer):
    rows, width = buffer.shape
    half = (4, width, width // 2)
    return pl.pallas_call(
        attend_back_kernel,
        out_shape=(
            jax.ShapeDtypeStruct(half, wide),
            jax.ShapeDtypeStruct(half, low),
            jax.ShapeDtypeStruct(buffer.shape, low),
        ),
        in_specs=[on_chip()] * 7,
        out_specs=(on_chip(),) * 3,
        scratch_shapes=[pltpu.VMEM(buffer.shape, low), pltpu.VMEM((3,) + buffer.shape, low)],
        compiler_params=params(40),
        cost_estimate=cost(24 * rows * width * width, 24 * width * width),
    )(buffer, weights, segment[:, None], segment[None, :], made, context, grad_answer)


def normal_parts(values):
    center = values - jnp.mean(values, axis=-1, keepdims=True)
    spread = jnp.mean(center * center, axis=-1, keepdims=True)
    return center, lax.rsqrt(spread + norm_eps)


def token_kernel(
    tokens,
    above,
    placing,
    returned,
    weighting,
    gate_slope,
    vectors,
    w_up,
    w_down,
    mixed_ref,
    packed_ref,
    grad_hidden_ref,
    logit_ref,
    vector_ref,
    second_ref,
    active_ref,
    inner_ref,
    hidden,
    result,
    grad_second,
):
    step = pl.program_id(0)

    @pl.when(step == 0)
    def prepare():
        unpacked = dot(placing[...], returned[...])
        values = tokens[...].astype(wide) + weighting[...] * unpacked
        hidden[...] = values
        center, inverse = normal_parts(values)
        second_ref[...] = (center * inverse * vectors[3:4] + vectors[4:5]).astype(low)
        result[...] = values
        grad_second[...] = jnp.zeros_like(grad_second)

    before = dot(second_ref[...], w_up[0])
    share = 0.5 + 0.5 * lax.erf(before * (0.5**0.5))
    density = jnp.exp(before * before * -0.5) * (0.5 / math.pi) ** 0.5
    active = (before * share).astype(low)
    active_ref[0] = active
    result[...] += dot(active, w_down[0])
    grad_active = dot(above[...], w_down[0], 1, 1)
    grad_inner = (grad_active * (share + before * density)).astype(low)
    inner_ref[0] = grad_inner
    grad_second[...] += dot(grad_inner, w_up[0], 1, 1)

    @pl.when(step == pl.num_programs(0) - 1)
    def finish():
        mixed_ref[...] = result[...].astype(low)
        center, inverse = normal_parts(hidden[...])
        scaled = center * inverse
        grads = grad_second[...]
        vector_ref[0:1] = jnp.sum(grads * scaled, axis=0, keepdims=True)
        vector_ref[1:2] = jnp.sum(grads, axis=0, keepdims=True)
        pulled = grads * vectors[3:4]
        pulled = (
            pulled
            - jnp.mean(pulled, axis=-1, keepdims=True)
            - scaled * jnp.mean(pulled * scaled, axis=-1, keepdims=True)
        )
        grad_hidden = above[...].astype(wide) + inverse * pulled
        grad_hidden_ref[...] = grad_hidden
        weighted = (grad_hidden * weighting[...]).astype(low)
        packed_ref[...] = dot(placing[...], weighted, 0, 0).astype(low)
        unpacked = dot(placing[...], returned[...])
        logit_ref[...] = gate_slope[...] * jnp.sum(grad_hidden * unpacked, axis=-1, keepdims=True)


def token_layer(tokens, above, placing, returned, weighting, gate_slope, vectors, w_up, w_down):
    count, width = tokens.shape
    slots = placing.shape[1]
    blocks = w_up.shape[0]
    block = pl.BlockSpec((1, width, width), lambda step: (step, 0, 0))
    hidden_block = pl.BlockSpec((1, count, width), lambda step: (step, 0, 0))

    def whole(*shape):
        return pl.BlockSpec(shape, lambda step: (0,) * len(shape))

    return pl.pallas_call(
        token_kernel,
        grid=(blocks,),
        out_shape=(
            jax.ShapeDtypeStruct((count, width), low),
            jax.ShapeDtypeStruct((slots, width), low),
            jax.ShapeDtypeStruct((count, width), wide),
            jax.ShapeDtypeStruct((count, 1), wide),
            jax.ShapeDtypeStruct((2, width), wide),
            jax.ShapeDtypeStruct((count, width), low),
            jax.ShapeDtypeStruct((blocks, count, width), low),
            jax.ShapeDtypeStruct((blocks, count, width), low),
        ),
        in_specs=[
            whole(count, width),
            whole(count, width),
            whole(count, slots),
            whole(slots, width),
            whole(count, 1),
            whole(count, 1),
            whole(*vectors.shape),
            block,
            block,
        ],
        out_specs=(
            whole(count, width),
            whole(slots, width),
            whole(count, width),
            whole(count, 1),
            whole(2, width),
            whole(count, width),
            hidden_block,
            hidden_block,
        ),
        scratch_shapes=[pltpu.VMEM((count, width), wide)] * 3,
        compiler_params=params(56),
        cost_estimate=cost(8 * blocks * count * width * width, 8 * blocks * width * width),
    )(tokens, above, placing, returned, weighting, gate_slope, vectors, w_up, w_down)


def outer_kernel(left, right, mine_ref, theirs_ref):
    core = lax.axis_index("own")
    columns = mine_ref.shape[2]
    for half, out_ref, kind_of in ((core, mine_ref, wide), (1 - core, theirs_ref, low)):
        part = pl.ds(pl.multiple_of(half * columns, columns), columns)
        out_ref[0] = dot(left[0], right[0, :, part], 0, 0).astype(kind_of)


def outer_halves(left, right):
    count, width = left.shape[1:]
    blocks = max(left.shape[0], right.shape[0])

    def spec(value):
        if value.shape[0] == 1:
            return pl.BlockSpec((1, count, width), lambda step: (0, 0, 0))
        return pl.BlockSpec((1, count, width), lambda step: (step, 0, 0))

    out_spec = pl.BlockSpec((1, width, width // 2), lambda step: (step, 0, 0))
    shape = (blocks, width, width // 2)
    return pl.pallas_call(
        outer_kernel,
        grid=(blocks,),
        out_shape=(jax.ShapeDtypeStruct(shape, wide), jax.ShapeDtypeStruct(shape, low)),
        in_specs=[spec(left), spec(right)],
        out_specs=(out_spec, out_spec),
        compiler_params=params(32),
        cost_estimate=cost(2 * blocks * count * width * width, 5 * blocks * width * width),
    )(left, right)


def column(values):
    return values[:, None]


def pack_kernel(
    tokens, chosen, packing, vectors, first_ref, placing_ref, packed_ref, weight_ref, slope_ref
):
    count = tokens.shape[0]
    capacity = packing.shape[0]
    center, inverse = normal_parts(tokens[...].astype(wide))
    first = (center * inverse * vectors[0:1] + vectors[1:2]).astype(low)
    first_ref[...] = first
    gate = jax.nn.sigmoid(jnp.sum(first.astype(wide) * vectors[2:3], axis=-1, keepdims=True))
    weighting = jnp.where(chosen[...] == 1, gate, 0.0)
    weight_ref[...] = weighting
    slope_ref[...] = weighting * (1.0 - gate)
    above = lax.broadcasted_iota(jnp.int32, (count, count), 0)
    below = lax.broadcasted_iota(jnp.int32, (count, count), 1)
    earlier = (below <= above).astype(wide).astype(low)
    flags = jnp.broadcast_to(chosen[...].astype(wide), (count, capacity))
    rank = dot(earlier, flags.astype(low))
    place_of = lax.broadcasted_iota(jnp.int32, (count, capacity), 1).astype(wide) + 1.0
    ranked = jnp.where(rank == place_of, flags, 0.0).astype(low)
    slots = lax.broadcasted_iota(jnp.int32, (capacity, capacity), 1)
    slot_of = (packing[...] == slots).astype(wide).astype(low)
    placing = dot(ranked, slot_of).astype(low)
    placing_ref[...] = placing
    packed_ref[...] = dot(placing, first, 0, 0).astype(low)


def pack_tokens(tokens, chosen, packing, vectors):
    count, width = tokens.shape
    capacity = packing.shape[0]
    one = jax.ShapeDtypeStruct((count, 1), wide)
    return pl.pallas_call(
        pack_kernel,
        out_shape=(
            jax.ShapeDtypeStruct((count, width), low),
            jax.ShapeDtypeStruct((count, capacity), low),
            jax.ShapeDtypeStruct((capacity, width), low),
            one,
            one,
        ),
        in_specs=[on_chip()] * 4,
        out_specs=(on_chip(),) * 5,
        compiler_params=params(24),
        cost_estimate=cost(4 * count * capacity * width, 8 * count * width),
    )(tokens, column(chosen), column(packing), vectors)


def token_back_kernel(
    tokens, first, placing, grad_sent, grad_hidden, grad_logit, vectors, out_ref, vector_ref
):
    grad_first = dot(placing[...], grad_sent[...]) + grad_logit[...] * vectors[2:3]
    center, inverse = normal_parts(tokens[...].astype(wide))
    scaled = center * inverse
    vector_ref[0:1] = jnp.sum(grad_first * scaled, axis=0, keepdims=True)
    vector_ref[1:2] = jnp.sum(grad_first, axis=0, keepdims=True)
    vector_ref[2:3] = jnp.sum(grad_logit[...] * first[...].astype(wide), axis=0, keepdims=True)
    pulled = grad_first * vectors[0:1]
    pulled = (
        pulled
        - jnp.mean(pulled, axis=-1, keepdims=True)
        - scaled * jnp.mean(pulled * scaled, axis=-1, keepdims=True)
    )
    out_ref[...] = (grad_hidden[...] + inverse * pulled).astype(low)


def token_back(tokens, first, placing, grad_sent, grad_hidden, grad_logit, vectors):
    count, width = tokens.shape
    return pl.pallas_call(
        token_back_kernel,
        out_shape=(
            jax.ShapeDtypeStruct((count, width), low),
            jax.ShapeDtypeStruct((3, width), wide),
        ),
        in_specs=[on_chip()] * 7,
        out_specs=(on_chip(),) * 2,
        compiler_params=params(24),
        cost_estimate=cost(2 * count * width * placing.shape[1], 12 * count * width),
    )(tokens, first, placing, grad_sent, grad_hidden, grad_logit, vectors)


def all_sum(value):
    value = value + send(value, swap_pairs())
    for flip in (2, 4, 8, 16):
        value = value + send(value, [(i, i ^ flip) for i in range(32)])
    return value


def exchange(value, n_data):
    capacity, width = value.shape
    moved = lax.all_to_all(
        value.reshape(n_data, capacity // n_data, width), "dp", split_axis=0, concat_axis=0, tiled=True
    )
    return moved.reshape(capacity, width)


def block_shards(
    tokens,
    cotangent,
    selected,
    packing,
    segments,
    blocks,
    left_stat,
    right_stat,
    left_root,
    right_root,
    vectors,
    moment,
):
    model_width = tokens.shape[2]
    token_count = tokens.shape[0] * tokens.shape[1]
    n_data = lax.axis_size("dp")
    capacity = packing.shape[1]
    own_tokens = tokens.reshape(token_count, model_width)
    every = columns_by_core(blocks)
    first_low, placing, packed, weighting, gate_slope = pack_tokens(
        own_tokens, selected.reshape(token_count), packing[0], vectors
    )
    buffer = exchange(packed, n_data)
    line_attn = after(gather_line(every[:4]), packed)
    line_up = gather_line(after(every[4:8], line_attn))
    line_down = gather_line(after(every[8:], line_up))
    near_attn = send(line_attn, plane_pairs(0))
    first_attn = jnp.stack([line_attn, near_attn])
    far_attn = send(first_attn, plane_pairs(1))
    near_up = send(after(line_up, buffer), plane_pairs(0))
    first_up = jnp.stack([line_up, near_up])
    far_up = send(first_up, plane_pairs(1))
    near_down = send(line_down, plane_pairs(0))
    w_attn = place_weights(with_other(first_attn, far_attn))
    segment = segments[0]
    made, context, answer = attend(buffer, w_attn, segment)
    first_down = after(jnp.stack([line_down, near_down]), answer)
    far_down = send(first_down, plane_pairs(1))
    w_up = place_weights(with_other(first_up, far_up))
    root_line = roots_line(after(left_root, line_down), right_root)
    near_root = send(root_line, plane_pairs(0))
    first_root = jnp.stack([root_line, near_root])
    far_root = send(first_root, plane_pairs(1))
    w_down = place_weights(with_other(first_down, far_down))
    returned = exchange(answer, n_data)
    above = cotangent.reshape(token_count, model_width)
    mixed, grad_packed, grad_hidden, grad_logit, vector_two, second_low, active, grad_inner = (
        token_layer(
            own_tokens,
            above,
            placing,
            returned,
            weighting,
            gate_slope,
            vectors,
            w_up,
            after(w_down, first_root),
        )
    )
    grad_answer = exchange(grad_packed, n_data)
    roots = with_other(first_root, far_root)
    down_start = reduce_start(*outer_halves(after(active, far_root), above[None]))
    up_start = reduce_start(*outer_halves(second_low[None], grad_inner))
    grad_answer = after(grad_answer, down_start[0], up_start[0])
    mine, theirs, grad_buffer = attend_back(buffer, w_attn, segment, made, context, grad_answer)
    attn_start = reduce_start(mine, theirs)
    grad_sent = exchange(grad_buffer, n_data)
    pair = in_block_order(
        return_chunks(step_chunks(reduce_rest([up_start, down_start]), roots, 1))
    )
    pair_given = jnp.where(
        first_core(), pair[2:], jnp.concatenate([pair[:2], pair[4:]])
    )
    pair_other = send(pair_given, swap_pairs())
    attn = return_chunks(step_chunks(reduce_rest([attn_start]), roots, 0))
    grad_own, left_new, right_new, new_blocks = update_blocks(
        attn, pair, pair_other, blocks, left_stat, right_stat
    )
    grad_tokens, vector_one = token_back(
        own_tokens, first_low, placing, grad_sent, grad_hidden, grad_logit, vectors
    )
    vector_grad = all_sum(jnp.concatenate([vector_one, vector_two]))
    moment_new = 0.5 * moment + 0.5 * vector_grad
    row_squares = jnp.mean(moment_new * moment_new, axis=1, keepdims=True)
    vector_new = vectors - vector_rate * moment_new * lax.rsqrt(row_squares + norm_eps)
    return (
        mixed.reshape(tokens.shape),
        grad_tokens.reshape(tokens.shape),
        grad_own,
        left_new,
        right_new,
        new_blocks,
        vector_grad,
        moment_new,
        vector_new,
    )


def shards(
    tokens,
    cotangent,
    selected,
    packing,
    segments,
    blocks,
    left_stat,
    right_stat,
    left_root,
    right_root,
    vectors,
    moment,
):
    model_width = tokens.shape[2]
    token_count = tokens.shape[0] * tokens.shape[1]
    n_data = lax.axis_size("dp")
    n_owner = lax.axis_size("own")
    shard_rows = blocks.shape[0]
    own_blocks = blocks.shape[1]
    up_blocks = (own_blocks * n_owner - 4) // 2
    capacity = packing.shape[1]
    per_peer = capacity // n_data
    head_count = model_width // HEAD_DIM
    score_scale = HEAD_DIM ** (-0.5)
    flat_weights = blocks.astype(jnp.bfloat16).reshape(1, shard_rows * own_blocks * model_width)
    gathered = lax.all_gather(flat_weights, ("dp", "own"), axis=0, tiled=True)
    gathered = gathered.reshape(n_data, n_owner, shard_rows, own_blocks, model_width)

    def matrix(number):
        return gathered[:, number // own_blocks, :, number % own_blocks, :].reshape(
            model_width, model_width
        )

    w_query = matrix(0)
    w_key = matrix(1)
    w_value = matrix(2)
    w_out = matrix(3)
    w_up = jnp.concatenate([matrix(4 + position) for position in range(up_blocks)], axis=1)
    w_down = jnp.concatenate(
        [matrix(4 + up_blocks + position) for position in range(up_blocks)], axis=0
    )
    inputs = tokens.reshape(token_count, model_width).astype(jnp.float32)
    chosen = selected.reshape(token_count)
    normed_one, norm_one_back = jax.vjp(layer_norm, inputs, vectors[0], vectors[1])
    first_low = normed_one.astype(jnp.bfloat16)
    first_wide = first_low.astype(jnp.float32)
    gate_values = jax.nn.sigmoid(jnp.dot(first_wide, vectors[2], precision=highest))
    before = jnp.cumsum(chosen) - 1
    slot_index = jnp.where(chosen == 1, packing[0][jnp.clip(before, 0, capacity - 1)], -1)
    placing = (slot_index[None, :] == jnp.arange(capacity, dtype=jnp.int32)[:, None]).astype(
        jnp.bfloat16
    )
    packed = jnp.dot(placing, first_low, preferred_element_type=jnp.float32).astype(jnp.bfloat16)
    buffer = lax.all_to_all(
        packed.reshape(n_data, per_peer, model_width), "dp", split_axis=0, concat_axis=0, tiled=True
    )
    buffer = buffer.reshape(capacity, model_width)

    def project(matrix_in):
        made = jnp.dot(buffer, matrix_in, preferred_element_type=jnp.float32).astype(jnp.bfloat16)
        return made.reshape(capacity, head_count, HEAD_DIM)

    query_rows = project(w_query)
    key_rows = project(w_key)
    value_rows = project(w_value)
    segment = segments[0]
    block_rows = math.gcd(capacity, 512)
    starts = jnp.arange(capacity // block_rows, dtype=jnp.int32) * block_rows

    def masked_scores():
        scores = (
            jnp.einsum("qhd,khd->hqk", query_rows, key_rows, preferred_element_type=jnp.float32)
            * score_scale
        )
        same_segment = segment[:, None] == segment[None, :]
        return (jnp.where(same_segment[None, :, :], scores, -1e30), query_rows)

    def forward_block(first_row):
        scores, unused_block = masked_scores()
        largest = jnp.max(scores, axis=-1, keepdims=True)
        raised = jnp.exp(scores - largest)
        row_total = jnp.sum(raised, axis=-1, keepdims=True)
        shares = (raised / row_total).astype(jnp.bfloat16)
        context_part = jnp.einsum(
            "hqk,khd->qhd", shares, value_rows, preferred_element_type=jnp.float32
        )
        return (context_part.astype(jnp.bfloat16), largest[..., 0] + jnp.log(row_total[..., 0]))

    context_blocks, lse_blocks = lax.map(forward_block, starts)
    context = context_blocks.reshape(capacity, model_width)
    answer = jnp.dot(context, w_out, preferred_element_type=jnp.float32).astype(jnp.bfloat16)
    returned = lax.all_to_all(
        answer.reshape(n_data, per_peer, model_width), "dp", split_axis=0, concat_axis=0, tiled=True
    )
    returned = returned.reshape(capacity, model_width)
    unpacked = jnp.einsum("mt,md->td", placing, returned, preferred_element_type=jnp.float32)
    weighting = jnp.where(chosen == 1, gate_values, 0.0)
    hidden = inputs + weighting[:, None] * unpacked
    normed_two, norm_two_back = jax.vjp(layer_norm, hidden, vectors[3], vectors[4])
    second_low = normed_two.astype(jnp.bfloat16)
    pre_active = jnp.dot(second_low, w_up, preferred_element_type=jnp.float32)
    active_wide, gelu_back = jax.vjp(gelu_exact, pre_active)
    active = active_wide.astype(jnp.bfloat16)
    result = hidden + jnp.dot(active, w_down, preferred_element_type=jnp.float32)
    mixed = result.astype(jnp.bfloat16).reshape(tokens.shape)
    upstream = cotangent.reshape(token_count, model_width)
    grad_down = jnp.einsum("tf,td->fd", active, upstream, preferred_element_type=jnp.float32)
    grad_active = jnp.einsum("td,fd->tf", upstream, w_down, preferred_element_type=jnp.float32)
    grad_inner = gelu_back(grad_active)[0].astype(jnp.bfloat16)
    grad_up = jnp.einsum("td,tf->df", second_low, grad_inner, preferred_element_type=jnp.float32)
    grad_second = jnp.einsum("tf,df->td", grad_inner, w_up, preferred_element_type=jnp.float32)
    grad_hidden_part, grad_gain_two, grad_bias_two = norm_two_back(grad_second)
    grad_hidden = upstream.astype(jnp.float32) + grad_hidden_part
    grad_token_back = (grad_hidden * weighting[:, None]).astype(jnp.bfloat16)
    grad_packed = jnp.dot(placing, grad_token_back, preferred_element_type=jnp.float32).astype(
        jnp.bfloat16
    )
    router_pull = jnp.where(chosen == 1, jnp.sum(grad_hidden * unpacked, axis=-1), 0.0)
    grad_logit = router_pull * gate_values * (1.0 - gate_values)
    grad_answer = lax.all_to_all(
        grad_packed.reshape(n_data, per_peer, model_width),
        "dp",
        split_axis=0,
        concat_axis=0,
        tiled=True,
    )
    grad_answer = grad_answer.reshape(capacity, model_width)
    grad_out = jnp.einsum("md,me->de", context, grad_answer, preferred_element_type=jnp.float32)
    grad_context = jnp.einsum("me,de->md", grad_answer, w_out, preferred_element_type=jnp.float32)
    grad_context = grad_context.astype(jnp.bfloat16).reshape(capacity, head_count, HEAD_DIM)

    def backward_block(running, item_pair):
        first_row, lse_block = item_pair
        scores, query_block = masked_scores()
        shares_wide = jnp.exp(scores - lse_block[..., None])
        grad_shares = jnp.einsum(
            "qhd,khd->hqk", grad_context, value_rows, preferred_element_type=jnp.float32
        )
        inner_sum = jnp.sum(shares_wide * grad_shares, axis=-1, keepdims=True)
        grad_scores = (shares_wide * (grad_shares - inner_sum)).astype(jnp.bfloat16)
        grad_query_block = (
            jnp.einsum("hqk,khd->qhd", grad_scores, key_rows, preferred_element_type=jnp.float32)
            * score_scale
        )
        key_sum = (
            running[0]
            + jnp.einsum(
                "hqk,qhd->khd", grad_scores, query_block, preferred_element_type=jnp.float32
            )
            * score_scale
        )
        value_sum = running[1] + jnp.einsum(
            "hqk,qhd->khd",
            shares_wide.astype(jnp.bfloat16),
            grad_context,
            preferred_element_type=jnp.float32,
        )
        return ((key_sum, value_sum), grad_query_block)

    zeros_init = jnp.zeros((capacity, head_count, HEAD_DIM), jnp.float32)
    (key_total, value_total), query_grads = lax.scan(
        backward_block, (zeros_init, zeros_init), (starts, lse_blocks)
    )
    grad_query = query_grads.reshape(capacity, model_width).astype(jnp.bfloat16)
    grad_key = key_total.reshape(capacity, model_width).astype(jnp.bfloat16)
    grad_value = value_total.reshape(capacity, model_width).astype(jnp.bfloat16)
    grad_w_query = jnp.einsum("md,me->de", buffer, grad_query, preferred_element_type=jnp.float32)
    grad_w_key = jnp.einsum("md,me->de", buffer, grad_key, preferred_element_type=jnp.float32)
    grad_w_value = jnp.einsum("md,me->de", buffer, grad_value, preferred_element_type=jnp.float32)
    grad_buffer = jnp.einsum("me,de->md", grad_query, w_query, preferred_element_type=jnp.float32)
    grad_buffer = grad_buffer + jnp.einsum(
        "me,de->md", grad_key, w_key, preferred_element_type=jnp.float32
    )
    grad_buffer = grad_buffer + jnp.einsum(
        "me,de->md", grad_value, w_value, preferred_element_type=jnp.float32
    )
    grad_buffer = grad_buffer.astype(jnp.bfloat16)
    grad_sent = lax.all_to_all(
        grad_buffer.reshape(n_data, per_peer, model_width),
        "dp",
        split_axis=0,
        concat_axis=0,
        tiled=True,
    )
    grad_sent = grad_sent.reshape(capacity, model_width)
    grad_first = jnp.einsum("mt,md->td", placing, grad_sent, preferred_element_type=jnp.float32)
    grad_first = grad_first + grad_logit[:, None] * vectors[2][None, :]
    grad_router = jnp.sum(grad_logit[:, None] * first_wide, axis=0)
    grad_input_part, grad_gain_one, grad_bias_one = norm_one_back(grad_first)
    grad_tokens = (grad_hidden + grad_input_part).astype(jnp.bfloat16).reshape(tokens.shape)
    pieces = [grad_w_query, grad_w_key, grad_w_value, grad_out]
    pieces = pieces + [
        grad_up[:, position * model_width : (position + 1) * model_width]
        for position in range(up_blocks)
    ]
    pieces = pieces + [
        grad_down[position * model_width : (position + 1) * model_width, :]
        for position in range(up_blocks)
    ]
    local_terms = jnp.stack(pieces, axis=1)
    vector_terms = jnp.stack(
        [grad_gain_one, grad_bias_one, grad_router, grad_gain_two, grad_bias_two]
    )
    partial_value = lax.psum_scatter(local_terms, "dp", scatter_dimension=0, tiled=True)
    grad_own = lax.psum_scatter(
        partial_value.astype(jnp.bfloat16), "own", scatter_dimension=1, tiled=True
    ).astype(jnp.float32)
    vector_grad = lax.psum(vector_terms, ("dp", "own"))
    full_grad = lax.all_gather(grad_own.astype(jnp.bfloat16), "dp", axis=0, tiled=True).astype(
        grad_own.dtype
    )
    row_start = lax.axis_index("dp") * shard_rows
    left_new = 0.5 * left_stat + 0.5 * jnp.einsum(
        "rbk,nbk->rbn", grad_own, full_grad, precision=highest
    )
    column_part = lax.dynamic_slice_in_dim(full_grad, row_start, shard_rows, 2)
    right_new = 0.5 * right_stat + 0.5 * jnp.einsum(
        "nbr,nbk->rbk", column_part, full_grad, precision=highest
    )
    lefted = jnp.einsum("rbn,nbk->rbk", left_root, full_grad, precision=highest)
    precond = jnp.zeros_like(grad_own) + jnp.einsum(
        "rbn,nbk->rbk",
        lefted,
        lax.all_gather(right_root.astype(jnp.bfloat16), "dp", axis=0, tiled=True).astype(
            jnp.float32
        ),
        precision=highest,
    )
    square_sums = lax.psum(jnp.sum(precond * precond, axis=(0, 2)), "dp")
    step_scale = lax.rsqrt(square_sums / (model_width * model_width) + norm_eps)
    new_blocks = blocks - block_rate * precond * step_scale[None, :, None]
    moment_new = 0.5 * moment + 0.5 * vector_grad
    row_squares = jnp.mean(moment_new * moment_new, axis=1, keepdims=True)
    vector_new = vectors - vector_rate * moment_new * lax.rsqrt(row_squares + norm_eps)
    return (
        mixed,
        grad_tokens,
        grad_own,
        left_new,
        right_new,
        new_blocks,
        vector_grad,
        moment_new,
        vector_new,
    )


def solution(mesh):
    placed = (
        P(("dp", "own"), None, None),
        P(("dp", "own"), None, None),
        P(("dp", "own"), None),
        P(("dp", "own"), None),
        P(("dp", "own"), None),
        P("dp", "own", None),
        P("dp", "own", None),
        P("dp", "own", None),
        P("dp", "own", None),
        P("dp", "own", None),
        P(),
        P(),
    )
    small = mesh.shape["dp"] == 16 and mesh.shape["own"] == 2
    return jax.shard_map(
        block_shards if small else shards,
        mesh=mesh,
        in_specs=placed,
        out_specs=(
            P(("dp", "own"), None, None),
            P(("dp", "own"), None, None),
            P("dp", "own", None),
            P("dp", "own", None),
            P("dp", "own", None),
            P("dp", "own", None),
            P(),
            P(),
            P(),
        ),
        check_vma=False,
    )
```

```python
import math

import jax
import jax.numpy as jnp
from jax import lax
from jax.experimental import pallas as pl
from jax.experimental.pallas import tpu as pltpu
from jax.sharding import PartitionSpec as P

HEAD_DIM = 64


norm_eps = 1e-06
block_rate = 0.03
vector_rate = 0.04
highest = lax.Precision.HIGHEST


def layer_norm(values, norm_gain, norm_bias):
    center = values - jnp.mean(values, axis=-1, keepdims=True)
    spread = jnp.mean(center * center, axis=-1, keepdims=True)
    return center * lax.rsqrt(spread + norm_eps) * norm_gain + norm_bias


def gelu_exact(values):
    return jax.nn.gelu(values, approximate=False)


BOTH = ("dp", "own")
low = jnp.bfloat16
wide = jnp.float32
MIB = 2**20


def swap_pairs():
    return [(i, i ^ 1) for i in range(32)]


def plane_pairs(step):
    pairs = []
    for i in range(32):
        place, core = i // 2, i % 2
        flip = (1, 2)[step ^ core]
        pairs.append((i, (place ^ flip) * 2 + core))
    return pairs


def line_pairs(flip):
    return [(i, i ^ (8 * flip)) for i in range(32)]


def send(value, pairs):
    return lax.ppermute(value, BOTH, pairs)


def after(value, *others):
    return lax.optimization_barrier((value,) + others)[0]


def pick(value, index, axis):
    return lax.dynamic_index_in_dim(value, index, axis, keepdims=False)


def first_core():
    return lax.axis_index("own") == 0


def halves(value):
    middle = value.shape[-1] // 2
    lower, upper = value[..., :middle], value[..., middle:]
    return jnp.where(first_core(), lower, upper), jnp.where(first_core(), upper, lower)


def in_core_order(mine, theirs, axis):
    return jnp.where(
        first_core(),
        jnp.concatenate([mine, theirs], axis=axis),
        jnp.concatenate([theirs, mine], axis=axis),
    )


LINE_FLIPS = (0, 2, 1, 3)


def flipped(index, flip):
    return jnp.bitwise_xor(index, flip)


def spots(place, half):
    first, second = half + 1, 2 - half
    return [
        place,
        flipped(place, first),
        flipped(place, second),
        flipped(place, 3),
    ]


def here():
    device = lax.axis_index("dp")
    return device // 4, device % 4, lax.axis_index("own")


def dot(left, right, left_axis=1, right_axis=0):
    return lax.dot_general(
        left, right, (((left_axis,), (right_axis,)), ((), ())), preferred_element_type=wide
    )


def on_chip():
    return pl.BlockSpec(memory_space=pltpu.VMEM)


def params(limit):
    return pltpu.CompilerParams(vmem_limit_bytes=limit * MIB)


def cost(flops, moved):
    return pl.CostEstimate(flops=flops, bytes_accessed=moved, transcendentals=0)


def weight_kernel(*refs):
    sources, out_ref = refs[:4], refs[4]
    line, place, core = here()
    for other in range(2):
        half = core if other == 0 else 1 - core
        group = sources[other * 2 : other * 2 + 2]
        count, rows, columns = group[0].shape[2:]
        column_slice = pl.ds(pl.multiple_of(half * columns, columns), columns)
        for number, spot in enumerate(spots(place, half)):
            for shift, flip in enumerate(LINE_FLIPS):
                start = (flipped(line, flip) * 4 + spot) * rows
                row_slice = pl.ds(pl.multiple_of(start, rows), rows)
                for block in range(count):
                    piece = group[number // 2][number % 2, shift, block]
                    out_ref[block, row_slice, column_slice] = piece


def place_weights(parts):
    count, rows, columns = parts[0].shape[2:]
    full = rows * 16
    return pl.pallas_call(
        weight_kernel,
        out_shape=jax.ShapeDtypeStruct((count, full, columns * 2), low),
        in_specs=[on_chip()] * 4,
        out_specs=on_chip(),
        compiler_params=params(8),
        cost_estimate=cost(0, 8 * full * count * columns),
    )(*parts)


def columns_by_core(value):
    keep, give = halves(jnp.transpose(value.astype(low), (1, 0, 2)))
    return in_core_order(keep, send(give, swap_pairs()), 0)


def gather_line(chunk):
    pair = jnp.stack([chunk, send(chunk, line_pairs(2))])
    return jnp.concatenate([pair, send(pair, line_pairs(1))])


def with_other(first, far):
    return [first, far, send(first, swap_pairs()), send(far, swap_pairs())]


def roots_line(left_root, right_root):
    line, place, core = here()
    both = jnp.concatenate([left_root, right_root], axis=2)
    every = columns_by_core(
        both.reshape(left_root.shape[0], left_root.shape[1] * 2, left_root.shape[2])
    )
    rows, columns = every.shape[1:]
    every = every.reshape(3, 4, 2, rows, columns)
    line_parts = [pick(every, line, 1)]
    for flip in (1, 2, 3):
        given = pick(every, flipped(line, flip), 1)
        line_parts.append(send(given, line_pairs(flip)))
    return jnp.stack(line_parts)


def reduce_start(mine, theirs):
    line, place, core = here()
    count, full, columns = mine.shape
    summed = mine + send(theirs, swap_pairs()).astype(wide)
    pieces = summed.reshape(count, 4, 4, full // 16, columns)
    spot = spots(place, core)
    give = jnp.stack([pick(pieces, spot[1], 2), pick(pieces, spot[3], 2)]).astype(low)
    return give, pick(pieces, spot[0], 2), pick(pieces, spot[2], 2)


def add_first(got, kept, passed):
    return kept + got[0].astype(wide), (passed + got[1].astype(wide)).astype(low)


def add_second(kept, got):
    line, place, core = here()
    kept = kept + got.astype(wide)
    given = jnp.stack([pick(kept, flipped(line, flip), 0) for flip in (1, 3)]).astype(low)
    return pick(kept, line, 0), pick(kept, flipped(line, 2), 0), given


def gathered_parts(first, far):
    return jnp.concatenate([first, far])


def step_kernel(*refs):
    grads, roots = refs[:2], refs[2:6]
    out_ref, grad_ref, rows_ref, left_ref, right_ref, lefted_ref, cross_ref, step_ref = refs[6:]
    line, place, core = here()
    rows, columns = grads[0].shape[2:]

    def rows_of(row_line, spot):
        return pl.ds(pl.multiple_of((row_line * 4 + spot) * rows, rows), rows)

    def column_half(half):
        return pl.ds(pl.multiple_of(half * columns, columns), columns)

    for other in range(2):
        half = core if other == 0 else 1 - core
        root_group = roots[2 * other : 2 * other + 2]
        for number, spot in enumerate(spots(place, half)):
            for step in range(4):
                grad_ref[rows_of(step, spot), column_half(half)] = grads[other][number, step]
                target = (rows_of(flipped(line, step), spot), column_half(half))
                root_piece = root_group[number // 2]
                left_ref[target] = root_piece[number % 2, step, 0, 0]
                right_ref[target] = root_piece[number % 2, step, 0, 1]
    for row_line in range(4):
        rows_ref[row_line * rows : (row_line + 1) * rows, :] = grad_ref[rows_of(row_line, place), :]
    left = dot(rows_ref[...], grad_ref[column_half(core), :], 1, 1)
    cross_ref[...] = dot(grad_ref[...], grad_ref[:, column_half(core)], 0, 0)
    lefted_ref[...] = dot(left_ref[...], grad_ref[...]).astype(low)
    stepped = dot(lefted_ref[...], right_ref[...])
    step_ref[...] = stepped
    size = stepped.shape[0] * stepped.shape[1]
    squares = jnp.sum(jnp.sum(stepped * stepped, axis=0, keepdims=True), axis=1, keepdims=True)
    step_scale = lax.rsqrt(squares / size + norm_eps)
    for row_line in range(4):
        part = slice(row_line * rows, (row_line + 1) * rows)
        target = rows_of(row_line, place)
        out_ref[row_line, 0] = grads[0][0, row_line]
        out_ref[row_line, 1] = left[part].astype(low)
        out_ref[row_line, 2] = cross_ref[target, :].astype(low)
        out_ref[row_line, 3] = (step_ref[target, column_half(core)] * step_scale).astype(low)


def step_chunk(mine, theirs, roots, number):
    lines, rows, columns = mine.shape[1:]
    full = rows * 16
    square = (full, columns * 2)
    root_spec = pl.BlockSpec((2, lines, 1, 2, rows, columns), lambda step: (0, 0, number, 0, 0, 0))
    return pl.pallas_call(
        step_kernel,
        grid=(1,),
        out_shape=jax.ShapeDtypeStruct((lines, 4, rows, columns), low),
        in_specs=[on_chip()] * 2 + [root_spec] * 4,
        out_specs=on_chip(),
        scratch_shapes=[
            pltpu.VMEM(square, low),
            pltpu.VMEM((lines * rows, columns * 2), low),
            pltpu.VMEM(square, low),
            pltpu.VMEM(square, low),
            pltpu.VMEM(square, low),
            pltpu.VMEM((full, columns), wide),
            pltpu.VMEM(square, wide),
        ],
        compiler_params=params(28),
        cost_estimate=cost(6 * full**3, 16 * full * full),
    )(mine, theirs, *roots)


def return_chunk(made):
    line, place, core = here()
    parts = [pick(made, line, 0)]
    for flip in (1, 2, 3):
        parts.append(send(pick(made, flipped(line, flip), 0), line_pairs(flip)))
    return jnp.stack(parts)


def last_kernel(attn, attn_other, pair, pair_other, blocks, left_stat, right_stat, *outs):
    grad_out, left_out, right_out, block_out = outs
    line, place, core = here()
    columns = attn.shape[3]

    def update(number, which, mine, theirs):
        for (source, index), half in ((mine, which), (theirs, 1 - which)):
            part = slice(half * columns, (half + 1) * columns)
            pieces = [source[index + (kind,)].astype(wide) for kind in range(4)]
            grad_out[number, :, part] = pieces[0]
            left_out[number, :, part] = 0.5 * left_stat[number, :, part] + 0.5 * pieces[1]
            right_out[number, :, part] = 0.5 * right_stat[number, :, part] + 0.5 * pieces[2]
            block_out[number, :, part] = blocks[number, :, part] - block_rate * pieces[3]

    @pl.when(core == 0)
    def first():
        for number in range(4):
            index = (flipped(line, number),)
            update(number, 0, (attn, index), (attn_other, index))
        for number in range(2):
            update(4 + number, 0, (pair, (number,)), (pair_other, (number,)))

    @pl.when(core == 1)
    def second():
        for number in range(6):
            update(number, 1, (pair, (2 + number,)), (pair_other, (number,)))


def in_block_order(chunk):
    line, place, core = here()
    return [pick(chunk, flipped(line, block), 0) for block in range(4)]


def update_blocks(attn, pair, pair_other, blocks, left_stat, right_stat):
    attn_other = send(attn, [(i, i ^ 1) for i in range(1, 32, 2)])
    turned = [jnp.transpose(value, (1, 0, 2)) for value in (blocks, left_stat, right_stat)]
    shape = jax.ShapeDtypeStruct(turned[0].shape, wide)
    outs = pl.pallas_call(
        last_kernel,
        out_shape=(shape,) * 4,
        in_specs=[on_chip()] * 7,
        out_specs=(on_chip(),) * 4,
        compiler_params=params(8),
        cost_estimate=cost(0, 32 * shape.size),
    )(attn, attn_other, pair, pair_other, *turned)
    return [jnp.transpose(value, (1, 0, 2)) for value in outs]


def head_masks():
    lane = lax.broadcasted_iota(jnp.int32, (1, 2 * HEAD_DIM), 1)
    return [(lane < HEAD_DIM).astype(wide).astype(low), (lane >= HEAD_DIM).astype(wide).astype(low)]


def head_shares(query, key, same):
    scores = dot(query, key, 1, 1) * HEAD_DIM ** (-0.5)
    scores = jnp.where(same, scores, -1e30)
    raised = jnp.exp(scores - jnp.max(scores, axis=-1, keepdims=True))
    return raised / jnp.sum(raised, axis=-1, keepdims=True)


def attend_kernel(buffer, weights, seg_column, seg_row, made_ref, context_ref, answer_ref):
    same = seg_column[...] == seg_row[...]
    for kind in range(3):
        made_ref[kind] = dot(buffer[...], weights[kind]).astype(low)
    width = 2 * HEAD_DIM
    for pair in range(buffer.shape[1] // width):
        part = slice(pair * width, (pair + 1) * width)
        query, key, value = (made_ref[kind, :, part] for kind in range(3))
        context = None
        for mask in head_masks():
            shares = head_shares(query, key * mask, same).astype(low)
            term = dot(shares, value * mask)
            context = term if context is None else context + term
        context_ref[:, part] = context.astype(low)
    answer_ref[...] = dot(context_ref[...], weights[3]).astype(low)


def attend(buffer, weights, segment):
    shape = jax.ShapeDtypeStruct(buffer.shape, low)
    rows, width = buffer.shape
    return pl.pallas_call(
        attend_kernel,
        out_shape=(jax.ShapeDtypeStruct((3,) + buffer.shape, low), shape, shape),
        in_specs=[on_chip()] * 4,
        out_specs=(on_chip(),) * 3,
        compiler_params=params(10),
        cost_estimate=cost(12 * rows * width * width, 12 * width * width),
    )(buffer, weights, segment[:, None], segment[None, :])


def attend_back_kernel(
    buffer,
    weights,
    seg_column,
    seg_row,
    made,
    context,
    grad_answer,
    mine_ref,
    theirs_ref,
    grad_buffer_ref,
    grad_context_ref,
    grads_ref,
):
    same = seg_column[...] == seg_row[...]
    core = lax.axis_index("own")
    grad_context_ref[...] = dot(grad_answer[...], weights[3], 1, 1).astype(low)
    width = 2 * HEAD_DIM
    for pair in range(buffer.shape[1] // width):
        part = slice(pair * width, (pair + 1) * width)
        query, key, value = (made[kind, :, part] for kind in range(3))
        above = grad_context_ref[:, part]
        sums = [None] * 3
        for mask in head_masks():
            key_head = key * mask
            shares = head_shares(query, key_head, same)
            grad_shares = dot(above, value * mask, 1, 1)
            inner = jnp.sum(shares * grad_shares, axis=-1, keepdims=True)
            grad_scores = (shares * (grad_shares - inner)).astype(low)
            terms = (
                dot(grad_scores, key_head),
                dot(grad_scores, query * mask, 0, 0),
                dot(shares.astype(low), above * mask, 0, 0),
            )
            sums = [
                term if total is None else total + term for term, total in zip(terms, sums)
            ]
        for kind, factor in enumerate((HEAD_DIM ** (-0.5), HEAD_DIM ** (-0.5), 1.0)):
            grads_ref[kind, :, part] = (sums[kind] * factor).astype(low)
    columns = mine_ref.shape[2]
    for half, out_ref, kind_of in ((core, mine_ref, wide), (1 - core, theirs_ref, low)):
        part = pl.ds(pl.multiple_of(half * columns, columns), columns)
        for kind in range(3):
            out_ref[kind] = dot(buffer[...], grads_ref[kind, :, part], 0, 0).astype(kind_of)
        out_ref[3] = dot(context[...], grad_answer[:, part], 0, 0).astype(kind_of)
    total = dot(grads_ref[0], weights[0], 1, 1)
    total = total + dot(grads_ref[1], weights[1], 1, 1)
    total = total + dot(grads_ref[2], weights[2], 1, 1)
    grad_buffer_ref[...] = total.astype(low)


def attend_back(buffer, weights, segment, made, context, grad_answer):
    rows, width = buffer.shape
    half = (4, width, width // 2)
    return pl.pallas_call(
        attend_back_kernel,
        out_shape=(
            jax.ShapeDtypeStruct(half, wide),
            jax.ShapeDtypeStruct(half, low),
            jax.ShapeDtypeStruct(buffer.shape, low),
        ),
        in_specs=[on_chip()] * 7,
        out_specs=(on_chip(),) * 3,
        scratch_shapes=[pltpu.VMEM(buffer.shape, low), pltpu.VMEM((3,) + buffer.shape, low)],
        compiler_params=params(14),
        cost_estimate=cost(24 * rows * width * width, 24 * width * width),
    )(buffer, weights, segment[:, None], segment[None, :], made, context, grad_answer)


def normal_parts(values):
    center = values - jnp.mean(values, axis=-1, keepdims=True)
    spread = jnp.mean(center * center, axis=-1, keepdims=True)
    return center, lax.rsqrt(spread + norm_eps)


def forward_kernel(
    tokens,
    placing,
    returned,
    weighting,
    vectors,
    w_up,
    hidden_ref,
    second_ref,
    active_ref,
    slope_ref,
):
    step = pl.program_id(0)

    @pl.when(step == 0)
    def prepare():
        values = tokens[...].astype(wide) + weighting[...] * dot(placing[...], returned[...])
        hidden_ref[...] = values
        center, inverse = normal_parts(values)
        second_ref[...] = (center * inverse * vectors[3:4] + vectors[4:5]).astype(low)

    before = dot(second_ref[...], w_up[step])
    share = 0.5 + 0.5 * lax.erf(before * (0.5**0.5))
    density = jnp.exp(before * before * -0.5) * (0.5 / math.pi) ** 0.5
    active_ref[step] = (before * share).astype(low)
    slope_ref[step] = (share + before * density).astype(low)


def token_forward(tokens, placing, returned, weighting, vectors, w_up):
    count, width = tokens.shape
    blocks = w_up.shape[0]
    by_block = jax.ShapeDtypeStruct((blocks, count, width), low)
    return pl.pallas_call(
        forward_kernel,
        grid=(blocks,),
        out_shape=(
            jax.ShapeDtypeStruct((count, width), wide),
            jax.ShapeDtypeStruct((count, width), low),
            by_block,
            by_block,
        ),
        in_specs=[on_chip()] * 6,
        out_specs=(on_chip(),) * 4,
        compiler_params=params(20),
        cost_estimate=cost(8 * blocks * count * width * width, 8 * blocks * width * width),
    )(tokens, placing, returned, weighting, vectors, w_up)


def backward_kernel(
    above,
    hidden,
    active,
    slope,
    placing,
    returned,
    weighting,
    gate_slope,
    vectors,
    w_up,
    w_down,
    mixed_ref,
    packed_ref,
    grad_hidden_ref,
    logit_ref,
    vector_ref,
    inner_ref,
    result,
    grad_second,
):
    step = pl.program_id(0)

    @pl.when(step == 0)
    def prepare():
        result[...] = hidden[...]
        grad_second[...] = jnp.zeros_like(grad_second)

    grad_active = dot(above[...], w_down[step], 1, 1)
    grad_inner = (grad_active * slope[step].astype(wide)).astype(low)
    inner_ref[step] = grad_inner
    result[...] += dot(active[step], w_down[step])
    grad_second[...] += dot(grad_inner, w_up[step], 1, 1)

    @pl.when(step == pl.num_programs(0) - 1)
    def finish():
        mixed_ref[...] = result[...].astype(low)
        center, inverse = normal_parts(hidden[...])
        scaled = center * inverse
        grads = grad_second[...]
        vector_ref[0:1] = jnp.sum(grads * scaled, axis=0, keepdims=True)
        vector_ref[1:2] = jnp.sum(grads, axis=0, keepdims=True)
        pulled = grads * vectors[3:4]
        pulled = (
            pulled
            - jnp.mean(pulled, axis=-1, keepdims=True)
            - scaled * jnp.mean(pulled * scaled, axis=-1, keepdims=True)
        )
        grad_hidden = above[...].astype(wide) + inverse * pulled
        grad_hidden_ref[...] = grad_hidden
        weighted = (grad_hidden * weighting[...]).astype(low)
        packed_ref[...] = dot(placing[...], weighted, 0, 0).astype(low)
        unpacked = dot(placing[...], returned[...])
        logit_ref[...] = gate_slope[...] * jnp.sum(grad_hidden * unpacked, axis=-1, keepdims=True)


def token_backward(above, hidden, active, slope, placing, returned, weighting, gate_slope, vectors, w_up, w_down):
    count, width = above.shape
    slots = placing.shape[1]
    blocks = w_up.shape[0]
    return pl.pallas_call(
        backward_kernel,
        grid=(blocks,),
        out_shape=(
            jax.ShapeDtypeStruct((count, width), low),
            jax.ShapeDtypeStruct((slots, width), low),
            jax.ShapeDtypeStruct((count, width), wide),
            jax.ShapeDtypeStruct((count, 1), wide),
            jax.ShapeDtypeStruct((2, width), wide),
            jax.ShapeDtypeStruct((blocks, count, width), low),
        ),
        in_specs=[on_chip()] * 11,
        out_specs=(on_chip(),) * 6,
        scratch_shapes=[pltpu.VMEM((count, width), wide)] * 2,
        compiler_params=params(20),
        cost_estimate=cost(8 * blocks * count * width * width, 8 * blocks * width * width),
    )(
        above,
        hidden,
        active,
        slope,
        placing,
        returned,
        weighting,
        gate_slope,
        vectors,
        w_up,
        w_down,
    )


def outer_kernel(left, right, mine_ref, theirs_ref):
    core = lax.axis_index("own")
    step = pl.program_id(0)
    columns = mine_ref.shape[2]
    left_step = step if left.shape[0] > 1 else 0
    right_step = step if right.shape[0] > 1 else 0
    for half, out_ref, kind_of in ((core, mine_ref, wide), (1 - core, theirs_ref, low)):
        part = pl.ds(pl.multiple_of(half * columns, columns), columns)
        out_ref[step] = dot(left[left_step], right[right_step, :, part], 0, 0).astype(kind_of)


def outer_halves(left, right):
    count, width = left.shape[1:]
    blocks = max(left.shape[0], right.shape[0])
    shape = (blocks, width, width // 2)
    return pl.pallas_call(
        outer_kernel,
        grid=(blocks,),
        out_shape=(jax.ShapeDtypeStruct(shape, wide), jax.ShapeDtypeStruct(shape, low)),
        in_specs=[on_chip()] * 2,
        out_specs=(on_chip(),) * 2,
        compiler_params=params(8),
        cost_estimate=cost(2 * blocks * count * width * width, 5 * blocks * width * width),
    )(left, right)


def column(values):
    return values[:, None]


def pack_kernel(
    tokens, chosen, packing, vectors, first_ref, placing_ref, packed_ref, weight_ref, slope_ref
):
    count = tokens.shape[0]
    capacity = packing.shape[0]
    center, inverse = normal_parts(tokens[...].astype(wide))
    first = (center * inverse * vectors[0:1] + vectors[1:2]).astype(low)
    first_ref[...] = first
    gate = jax.nn.sigmoid(jnp.sum(first.astype(wide) * vectors[2:3], axis=-1, keepdims=True))
    weighting = jnp.where(chosen[...] == 1, gate, 0.0)
    weight_ref[...] = weighting
    slope_ref[...] = weighting * (1.0 - gate)
    above = lax.broadcasted_iota(jnp.int32, (count, count), 0)
    below = lax.broadcasted_iota(jnp.int32, (count, count), 1)
    earlier = (below <= above).astype(wide).astype(low)
    flags = jnp.broadcast_to(chosen[...].astype(wide), (count, capacity))
    rank = dot(earlier, flags.astype(low))
    place_of = lax.broadcasted_iota(jnp.int32, (count, capacity), 1).astype(wide) + 1.0
    ranked = jnp.where(rank == place_of, flags, 0.0).astype(low)
    slots = lax.broadcasted_iota(jnp.int32, (capacity, capacity), 1)
    slot_of = (packing[...] == slots).astype(wide).astype(low)
    placing = dot(ranked, slot_of).astype(low)
    placing_ref[...] = placing
    packed_ref[...] = dot(placing, first, 0, 0).astype(low)


def pack_tokens(tokens, chosen, packing, vectors):
    count, width = tokens.shape
    capacity = packing.shape[0]
    one = jax.ShapeDtypeStruct((count, 1), wide)
    return pl.pallas_call(
        pack_kernel,
        out_shape=(
            jax.ShapeDtypeStruct((count, width), low),
            jax.ShapeDtypeStruct((count, capacity), low),
            jax.ShapeDtypeStruct((capacity, width), low),
            one,
            one,
        ),
        in_specs=[on_chip()] * 4,
        out_specs=(on_chip(),) * 5,
        compiler_params=params(12),
        cost_estimate=cost(4 * count * capacity * width, 8 * count * width),
    )(tokens, column(chosen), column(packing), vectors)


def token_back_kernel(
    tokens, first, placing, grad_sent, grad_hidden, grad_logit, vectors, out_ref, vector_ref
):
    grad_first = dot(placing[...], grad_sent[...]) + grad_logit[...] * vectors[2:3]
    center, inverse = normal_parts(tokens[...].astype(wide))
    scaled = center * inverse
    vector_ref[0:1] = jnp.sum(grad_first * scaled, axis=0, keepdims=True)
    vector_ref[1:2] = jnp.sum(grad_first, axis=0, keepdims=True)
    vector_ref[2:3] = jnp.sum(grad_logit[...] * first[...].astype(wide), axis=0, keepdims=True)
    pulled = grad_first * vectors[0:1]
    pulled = (
        pulled
        - jnp.mean(pulled, axis=-1, keepdims=True)
        - scaled * jnp.mean(pulled * scaled, axis=-1, keepdims=True)
    )
    out_ref[...] = (grad_hidden[...] + inverse * pulled).astype(low)


def token_back(tokens, first, placing, grad_sent, grad_hidden, grad_logit, vectors):
    count, width = tokens.shape
    return pl.pallas_call(
        token_back_kernel,
        out_shape=(
            jax.ShapeDtypeStruct((count, width), low),
            jax.ShapeDtypeStruct((3, width), wide),
        ),
        in_specs=[on_chip()] * 7,
        out_specs=(on_chip(),) * 2,
        compiler_params=params(12),
        cost_estimate=cost(2 * count * width * placing.shape[1], 12 * count * width),
    )(tokens, first, placing, grad_sent, grad_hidden, grad_logit, vectors)


def all_sum(value):
    value = value + send(value, swap_pairs())
    for flip in (2, 4, 8, 16):
        value = value + send(value, [(i, i ^ flip) for i in range(32)])
    return value


def exchange(value, n_data):
    capacity, width = value.shape
    moved = lax.all_to_all(
        value.reshape(n_data, capacity // n_data, width), "dp", split_axis=0, concat_axis=0, tiled=True
    )
    return moved.reshape(capacity, width)


def block_shards(
    tokens,
    cotangent,
    selected,
    packing,
    segments,
    blocks,
    left_stat,
    right_stat,
    left_root,
    right_root,
    vectors,
    moment,
):
    model_width = tokens.shape[2]
    token_count = tokens.shape[0] * tokens.shape[1]
    n_data = lax.axis_size("dp")
    capacity = packing.shape[1]
    own_tokens = tokens.reshape(token_count, model_width)
    every = columns_by_core(blocks)
    first_low, placing, packed, weighting, gate_slope = pack_tokens(
        own_tokens, selected.reshape(token_count), packing[0], vectors
    )
    buffer = exchange(packed, n_data)
    line_attn = after(gather_line(every[:4]), packed)
    near_attn = send(line_attn, plane_pairs(0))
    line_up = gather_line(after(every[4:8], line_attn))
    first_attn = after(jnp.stack([line_attn, near_attn]), line_up)
    far_attn = send(first_attn, plane_pairs(1))
    near_up = send(after(line_up, buffer), plane_pairs(0))
    line_down = gather_line(after(every[8:], line_up))
    first_up = after(jnp.stack([line_up, near_up]), line_down)
    far_up = send(first_up, plane_pairs(1))
    near_down = send(line_down, plane_pairs(0))
    w_attn = place_weights(with_other(first_attn, far_attn))
    segment = segments[0]
    made, context, answer = attend(buffer, w_attn, segment)
    first_down = after(jnp.stack([line_down, near_down]), answer)
    far_down = send(first_down, plane_pairs(1))
    w_up = place_weights(with_other(first_up, far_up))
    root_line = roots_line(after(left_root, line_down), right_root)
    near_root = send(root_line, plane_pairs(0))
    first_root = jnp.stack([root_line, near_root])
    far_root = send(first_root, plane_pairs(1))
    returned = exchange(answer, n_data)
    above = cotangent.reshape(token_count, model_width)
    hidden, second_low, active, slope = token_forward(
        own_tokens, placing, returned, weighting, vectors, w_up
    )
    down_mine, down_theirs = outer_halves(active, above[None])
    w_down = place_weights(with_other(first_down, after(far_down, active)))
    mixed, grad_packed, grad_hidden, grad_logit, vector_two, grad_inner = token_backward(
        above,
        hidden,
        active,
        slope,
        placing,
        returned,
        weighting,
        gate_slope,
        vectors,
        w_up,
        after(w_down, down_theirs, near_root),
    )
    grad_answer = exchange(grad_packed, n_data)
    down_give, *down_kept = reduce_start(down_mine, after(down_theirs, grad_packed))
    down_got = send(down_give, plane_pairs(0))
    up_mine, up_theirs = outer_halves(after(second_low, down_give)[None], grad_inner)
    up_give, *up_kept = reduce_start(up_mine, up_theirs)
    up_got = send(up_give, plane_pairs(0))
    grad_answer = after(grad_answer, up_give, far_root)
    roots = with_other(first_root, far_root)
    mine, theirs, grad_buffer = attend_back(
        buffer, w_attn, segment, made, context, after(grad_answer, down_got)
    )
    grad_sent = exchange(grad_buffer, n_data)

    down_kept, down_give = add_first(down_got, *down_kept)
    down_got = send(down_give, plane_pairs(1))
    attn_give, *attn_kept = reduce_start(mine, after(theirs, up_got))

    down_own, down_two, down_give = add_second(down_kept, down_got)
    up_kept, up_give = add_first(up_got, *up_kept)
    down_got = send(down_give, line_pairs(1))
    up_got = send(up_give, plane_pairs(1))
    attn_got = send(attn_give, plane_pairs(0))

    down_give = (down_two + down_got[1].astype(wide)).astype(low)
    down_own = down_own + down_got[0].astype(wide)
    up_own, up_two, up_give = add_second(up_kept, up_got)
    down_got = send(down_give, line_pairs(2))
    up_got = send(up_give, line_pairs(1))

    down_own = (down_own + down_got.astype(wide)).astype(low)
    down_near = send(down_own, plane_pairs(0))
    up_give = (up_two + up_got[1].astype(wide)).astype(low)
    up_own = up_own + up_got[0].astype(wide)
    attn_kept, attn_give = add_first(after(attn_got, down_own, up_give), *attn_kept)
    attn_got = send(attn_give, plane_pairs(1))
    up_got = send(up_give, line_pairs(2))

    down_first = jnp.stack([down_own, down_near])
    down_far = send(down_first, plane_pairs(1))
    up_own = (up_own + up_got.astype(wide)).astype(low)
    attn_own, attn_two, attn_give = add_second(
        attn_kept, after(attn_got, down_first, up_own)
    )
    attn_got = send(attn_give, line_pairs(1))
    up_near = send(up_own, plane_pairs(0))
    down_mine = jnp.concatenate([down_first, down_far])
    down_theirs = send(down_mine, swap_pairs())

    attn_got = after(attn_got, down_theirs, up_near)
    attn_give = (attn_two + attn_got[1].astype(wide)).astype(low)
    attn_own = attn_own + attn_got[0].astype(wide)
    attn_got = send(attn_give, line_pairs(2))
    up_first = jnp.stack([up_own, up_near])
    up_far = send(up_first, plane_pairs(1))
    down_made = step_chunk(down_mine, down_theirs, roots, 2)

    attn_own = (attn_own + after(attn_got, up_far, down_made).astype(wide)).astype(low)
    attn_near = send(attn_own, plane_pairs(0))
    up_mine = jnp.concatenate([up_first, up_far])
    up_theirs = send(up_mine, swap_pairs())
    down = return_chunk(down_made)

    attn_first = jnp.stack([attn_own, after(attn_near, up_theirs)])
    attn_far = send(attn_first, plane_pairs(1))
    up_made = step_chunk(up_mine, up_theirs, roots, 1)
    grad_tokens, vector_one = token_back(
        own_tokens, first_low, placing, grad_sent, grad_hidden, grad_logit, vectors
    )

    attn_mine = jnp.concatenate([attn_first, after(attn_far, up_made, down)])
    attn_theirs = send(attn_mine, swap_pairs())
    up = return_chunk(up_made)
    attn = return_chunk(after(step_chunk(attn_mine, attn_theirs, roots, 0), up))
    up_blocks, down_blocks = in_block_order(up), in_block_order(down)
    pair = jnp.stack(up_blocks + down_blocks)
    pair_given = jnp.where(
        first_core(), jnp.stack(up_blocks[2:] + down_blocks), jnp.stack(up_blocks[:2] + down_blocks)
    )
    pair_other = send(pair_given, swap_pairs())
    grad_own, left_new, right_new, new_blocks = update_blocks(
        attn, pair, pair_other, blocks, left_stat, right_stat
    )
    vector_grad = all_sum(jnp.concatenate([vector_one, vector_two]))
    moment_new = 0.5 * moment + 0.5 * vector_grad
    row_squares = jnp.mean(moment_new * moment_new, axis=1, keepdims=True)
    vector_new = vectors - vector_rate * moment_new * lax.rsqrt(row_squares + norm_eps)
    return (
        mixed.reshape(tokens.shape),
        grad_tokens.reshape(tokens.shape),
        grad_own,
        left_new,
        right_new,
        new_blocks,
        vector_grad,
        moment_new,
        vector_new,
    )


def shards(
    tokens,
    cotangent,
    selected,
    packing,
    segments,
    blocks,
    left_stat,
    right_stat,
    left_root,
    right_root,
    vectors,
    moment,
):
    model_width = tokens.shape[2]
    token_count = tokens.shape[0] * tokens.shape[1]
    n_data = lax.axis_size("dp")
    n_owner = lax.axis_size("own")
    shard_rows = blocks.shape[0]
    own_blocks = blocks.shape[1]
    up_blocks = (own_blocks * n_owner - 4) // 2
    capacity = packing.shape[1]
    per_peer = capacity // n_data
    head_count = model_width // HEAD_DIM
    score_scale = HEAD_DIM ** (-0.5)
    flat_weights = blocks.astype(jnp.bfloat16).reshape(1, shard_rows * own_blocks * model_width)
    gathered = lax.all_gather(flat_weights, ("dp", "own"), axis=0, tiled=True)
    gathered = gathered.reshape(n_data, n_owner, shard_rows, own_blocks, model_width)

    def matrix(number):
        return gathered[:, number // own_blocks, :, number % own_blocks, :].reshape(
            model_width, model_width
        )

    w_query = matrix(0)
    w_key = matrix(1)
    w_value = matrix(2)
    w_out = matrix(3)
    w_up = jnp.concatenate([matrix(4 + position) for position in range(up_blocks)], axis=1)
    w_down = jnp.concatenate(
        [matrix(4 + up_blocks + position) for position in range(up_blocks)], axis=0
    )
    inputs = tokens.reshape(token_count, model_width).astype(jnp.float32)
    chosen = selected.reshape(token_count)
    normed_one, norm_one_back = jax.vjp(layer_norm, inputs, vectors[0], vectors[1])
    first_low = normed_one.astype(jnp.bfloat16)
    first_wide = first_low.astype(jnp.float32)
    gate_values = jax.nn.sigmoid(jnp.dot(first_wide, vectors[2], precision=highest))
    before = jnp.cumsum(chosen) - 1
    slot_index = jnp.where(chosen == 1, packing[0][jnp.clip(before, 0, capacity - 1)], -1)
    placing = (slot_index[None, :] == jnp.arange(capacity, dtype=jnp.int32)[:, None]).astype(
        jnp.bfloat16
    )
    packed = jnp.dot(placing, first_low, preferred_element_type=jnp.float32).astype(jnp.bfloat16)
    buffer = lax.all_to_all(
        packed.reshape(n_data, per_peer, model_width), "dp", split_axis=0, concat_axis=0, tiled=True
    )
    buffer = buffer.reshape(capacity, model_width)

    def project(matrix_in):
        made = jnp.dot(buffer, matrix_in, preferred_element_type=jnp.float32).astype(jnp.bfloat16)
        return made.reshape(capacity, head_count, HEAD_DIM)

    query_rows = project(w_query)
    key_rows = project(w_key)
    value_rows = project(w_value)
    segment = segments[0]
    block_rows = math.gcd(capacity, 512)
    starts = jnp.arange(capacity // block_rows, dtype=jnp.int32) * block_rows

    def masked_scores():
        scores = (
            jnp.einsum("qhd,khd->hqk", query_rows, key_rows, preferred_element_type=jnp.float32)
            * score_scale
        )
        same_segment = segment[:, None] == segment[None, :]
        return (jnp.where(same_segment[None, :, :], scores, -1e30), query_rows)

    def forward_block(first_row):
        scores, unused_block = masked_scores()
        largest = jnp.max(scores, axis=-1, keepdims=True)
        raised = jnp.exp(scores - largest)
        row_total = jnp.sum(raised, axis=-1, keepdims=True)
        shares = (raised / row_total).astype(jnp.bfloat16)
        context_part = jnp.einsum(
            "hqk,khd->qhd", shares, value_rows, preferred_element_type=jnp.float32
        )
        return (context_part.astype(jnp.bfloat16), largest[..., 0] + jnp.log(row_total[..., 0]))

    context_blocks, lse_blocks = lax.map(forward_block, starts)
    context = context_blocks.reshape(capacity, model_width)
    answer = jnp.dot(context, w_out, preferred_element_type=jnp.float32).astype(jnp.bfloat16)
    returned = lax.all_to_all(
        answer.reshape(n_data, per_peer, model_width), "dp", split_axis=0, concat_axis=0, tiled=True
    )
    returned = returned.reshape(capacity, model_width)
    unpacked = jnp.einsum("mt,md->td", placing, returned, preferred_element_type=jnp.float32)
    weighting = jnp.where(chosen == 1, gate_values, 0.0)
    hidden = inputs + weighting[:, None] * unpacked
    normed_two, norm_two_back = jax.vjp(layer_norm, hidden, vectors[3], vectors[4])
    second_low = normed_two.astype(jnp.bfloat16)
    pre_active = jnp.dot(second_low, w_up, preferred_element_type=jnp.float32)
    active_wide, gelu_back = jax.vjp(gelu_exact, pre_active)
    active = active_wide.astype(jnp.bfloat16)
    result = hidden + jnp.dot(active, w_down, preferred_element_type=jnp.float32)
    mixed = result.astype(jnp.bfloat16).reshape(tokens.shape)
    upstream = cotangent.reshape(token_count, model_width)
    grad_down = jnp.einsum("tf,td->fd", active, upstream, preferred_element_type=jnp.float32)
    grad_active = jnp.einsum("td,fd->tf", upstream, w_down, preferred_element_type=jnp.float32)
    grad_inner = gelu_back(grad_active)[0].astype(jnp.bfloat16)
    grad_up = jnp.einsum("td,tf->df", second_low, grad_inner, preferred_element_type=jnp.float32)
    grad_second = jnp.einsum("tf,df->td", grad_inner, w_up, preferred_element_type=jnp.float32)
    grad_hidden_part, grad_gain_two, grad_bias_two = norm_two_back(grad_second)
    grad_hidden = upstream.astype(jnp.float32) + grad_hidden_part
    grad_token_back = (grad_hidden * weighting[:, None]).astype(jnp.bfloat16)
    grad_packed = jnp.dot(placing, grad_token_back, preferred_element_type=jnp.float32).astype(
        jnp.bfloat16
    )
    router_pull = jnp.where(chosen == 1, jnp.sum(grad_hidden * unpacked, axis=-1), 0.0)
    grad_logit = router_pull * gate_values * (1.0 - gate_values)
    grad_answer = lax.all_to_all(
        grad_packed.reshape(n_data, per_peer, model_width),
        "dp",
        split_axis=0,
        concat_axis=0,
        tiled=True,
    )
    grad_answer = grad_answer.reshape(capacity, model_width)
    grad_out = jnp.einsum("md,me->de", context, grad_answer, preferred_element_type=jnp.float32)
    grad_context = jnp.einsum("me,de->md", grad_answer, w_out, preferred_element_type=jnp.float32)
    grad_context = grad_context.astype(jnp.bfloat16).reshape(capacity, head_count, HEAD_DIM)

    def backward_block(running, item_pair):
        first_row, lse_block = item_pair
        scores, query_block = masked_scores()
        shares_wide = jnp.exp(scores - lse_block[..., None])
        grad_shares = jnp.einsum(
            "qhd,khd->hqk", grad_context, value_rows, preferred_element_type=jnp.float32
        )
        inner_sum = jnp.sum(shares_wide * grad_shares, axis=-1, keepdims=True)
        grad_scores = (shares_wide * (grad_shares - inner_sum)).astype(jnp.bfloat16)
        grad_query_block = (
            jnp.einsum("hqk,khd->qhd", grad_scores, key_rows, preferred_element_type=jnp.float32)
            * score_scale
        )
        key_sum = (
            running[0]
            + jnp.einsum(
                "hqk,qhd->khd", grad_scores, query_block, preferred_element_type=jnp.float32
            )
            * score_scale
        )
        value_sum = running[1] + jnp.einsum(
            "hqk,qhd->khd",
            shares_wide.astype(jnp.bfloat16),
            grad_context,
            preferred_element_type=jnp.float32,
        )
        return ((key_sum, value_sum), grad_query_block)

    zeros_init = jnp.zeros((capacity, head_count, HEAD_DIM), jnp.float32)
    (key_total, value_total), query_grads = lax.scan(
        backward_block, (zeros_init, zeros_init), (starts, lse_blocks)
    )
    grad_query = query_grads.reshape(capacity, model_width).astype(jnp.bfloat16)
    grad_key = key_total.reshape(capacity, model_width).astype(jnp.bfloat16)
    grad_value = value_total.reshape(capacity, model_width).astype(jnp.bfloat16)
    grad_w_query = jnp.einsum("md,me->de", buffer, grad_query, preferred_element_type=jnp.float32)
    grad_w_key = jnp.einsum("md,me->de", buffer, grad_key, preferred_element_type=jnp.float32)
    grad_w_value = jnp.einsum("md,me->de", buffer, grad_value, preferred_element_type=jnp.float32)
    grad_buffer = jnp.einsum("me,de->md", grad_query, w_query, preferred_element_type=jnp.float32)
    grad_buffer = grad_buffer + jnp.einsum(
        "me,de->md", grad_key, w_key, preferred_element_type=jnp.float32
    )
    grad_buffer = grad_buffer + jnp.einsum(
        "me,de->md", grad_value, w_value, preferred_element_type=jnp.float32
    )
    grad_buffer = grad_buffer.astype(jnp.bfloat16)
    grad_sent = lax.all_to_all(
        grad_buffer.reshape(n_data, per_peer, model_width),
        "dp",
        split_axis=0,
        concat_axis=0,
        tiled=True,
    )
    grad_sent = grad_sent.reshape(capacity, model_width)
    grad_first = jnp.einsum("mt,md->td", placing, grad_sent, preferred_element_type=jnp.float32)
    grad_first = grad_first + grad_logit[:, None] * vectors[2][None, :]
    grad_router = jnp.sum(grad_logit[:, None] * first_wide, axis=0)
    grad_input_part, grad_gain_one, grad_bias_one = norm_one_back(grad_first)
    grad_tokens = (grad_hidden + grad_input_part).astype(jnp.bfloat16).reshape(tokens.shape)
    pieces = [grad_w_query, grad_w_key, grad_w_value, grad_out]
    pieces = pieces + [
        grad_up[:, position * model_width : (position + 1) * model_width]
        for position in range(up_blocks)
    ]
    pieces = pieces + [
        grad_down[position * model_width : (position + 1) * model_width, :]
        for position in range(up_blocks)
    ]
    local_terms = jnp.stack(pieces, axis=1)
    vector_terms = jnp.stack(
        [grad_gain_one, grad_bias_one, grad_router, grad_gain_two, grad_bias_two]
    )
    partial_value = lax.psum_scatter(local_terms, "dp", scatter_dimension=0, tiled=True)
    grad_own = lax.psum_scatter(
        partial_value.astype(jnp.bfloat16), "own", scatter_dimension=1, tiled=True
    ).astype(jnp.float32)
    vector_grad = lax.psum(vector_terms, ("dp", "own"))
    full_grad = lax.all_gather(grad_own.astype(jnp.bfloat16), "dp", axis=0, tiled=True).astype(
        grad_own.dtype
    )
    row_start = lax.axis_index("dp") * shard_rows
    left_new = 0.5 * left_stat + 0.5 * jnp.einsum(
        "rbk,nbk->rbn", grad_own, full_grad, precision=highest
    )
    column_part = lax.dynamic_slice_in_dim(full_grad, row_start, shard_rows, 2)
    right_new = 0.5 * right_stat + 0.5 * jnp.einsum(
        "nbr,nbk->rbk", column_part, full_grad, precision=highest
    )
    lefted = jnp.einsum("rbn,nbk->rbk", left_root, full_grad, precision=highest)
    precond = jnp.zeros_like(grad_own) + jnp.einsum(
        "rbn,nbk->rbk",
        lefted,
        lax.all_gather(right_root.astype(jnp.bfloat16), "dp", axis=0, tiled=True).astype(
            jnp.float32
        ),
        precision=highest,
    )
    square_sums = lax.psum(jnp.sum(precond * precond, axis=(0, 2)), "dp")
    step_scale = lax.rsqrt(square_sums / (model_width * model_width) + norm_eps)
    new_blocks = blocks - block_rate * precond * step_scale[None, :, None]
    moment_new = 0.5 * moment + 0.5 * vector_grad
    row_squares = jnp.mean(moment_new * moment_new, axis=1, keepdims=True)
    vector_new = vectors - vector_rate * moment_new * lax.rsqrt(row_squares + norm_eps)
    return (
        mixed,
        grad_tokens,
        grad_own,
        left_new,
        right_new,
        new_blocks,
        vector_grad,
        moment_new,
        vector_new,
    )


def solution(mesh):
    placed = (
        P(("dp", "own"), None, None),
        P(("dp", "own"), None, None),
        P(("dp", "own"), None),
        P(("dp", "own"), None),
        P(("dp", "own"), None),
        P("dp", "own", None),
        P("dp", "own", None),
        P("dp", "own", None),
        P("dp", "own", None),
        P("dp", "own", None),
        P(),
        P(),
    )
    small = mesh.shape["dp"] == 16 and mesh.shape["own"] == 2
    return jax.shard_map(
        block_shards if small else shards,
        mesh=mesh,
        in_specs=placed,
        out_specs=(
            P(("dp", "own"), None, None),
            P(("dp", "own"), None, None),
            P("dp", "own", None),
            P("dp", "own", None),
            P("dp", "own", None),
            P("dp", "own", None),
            P(),
            P(),
            P(),
        ),
        check_vma=False,
    )
```

```python
import functools
import math

import jax
import jax.numpy as jnp
from jax import lax
from jax.experimental import pallas as pl
from jax.experimental.pallas import tpu as pltpu
from jax.sharding import PartitionSpec as P

HEAD_DIM = 64


norm_eps = 1e-06
block_rate = 0.03
vector_rate = 0.04
highest = lax.Precision.HIGHEST


def layer_norm(values, norm_gain, norm_bias):
    center = values - jnp.mean(values, axis=-1, keepdims=True)
    spread = jnp.mean(center * center, axis=-1, keepdims=True)
    return center * lax.rsqrt(spread + norm_eps) * norm_gain + norm_bias


def gelu_exact(values):
    return jax.nn.gelu(values, approximate=False)


BOTH = ("dp", "own")
low = jnp.bfloat16
wide = jnp.float32
MIB = 2**20


def swap_pairs():
    return [(i, i ^ 1) for i in range(32)]


def plane_pairs(step):
    pairs = []
    for i in range(32):
        place, core = i // 2, i % 2
        flip = (1, 2)[step ^ core]
        pairs.append((i, (place ^ flip) * 2 + core))
    return pairs


def line_pairs(flip):
    return [(i, i ^ (8 * flip)) for i in range(32)]


def send(value, pairs):
    return lax.ppermute(value, BOTH, pairs)


def after(value, *others):
    return lax.optimization_barrier((value,) + others)[0]


def pick(value, index, axis):
    return lax.dynamic_index_in_dim(value, index, axis, keepdims=False)


def first_core():
    return lax.axis_index("own") == 0


def halves(value):
    middle = value.shape[-1] // 2
    lower, upper = value[..., :middle], value[..., middle:]
    return jnp.where(first_core(), lower, upper), jnp.where(first_core(), upper, lower)


def in_core_order(mine, theirs, axis):
    return jnp.where(
        first_core(),
        jnp.concatenate([mine, theirs], axis=axis),
        jnp.concatenate([theirs, mine], axis=axis),
    )


LINE_FLIPS = (0, 2, 1, 3)


def flipped(index, flip):
    return jnp.bitwise_xor(index, flip)


def spots(place, half):
    first, second = half + 1, 2 - half
    return [
        place,
        flipped(place, first),
        flipped(place, second),
        flipped(place, 3),
    ]


def here():
    device = lax.axis_index("dp")
    return device // 4, device % 4, lax.axis_index("own")


def dot(left, right, left_axis=1, right_axis=0):
    return lax.dot_general(
        left, right, (((left_axis,), (right_axis,)), ((), ())), preferred_element_type=wide
    )


def on_chip():
    return pl.BlockSpec(memory_space=pltpu.VMEM)


def params(limit):
    return pltpu.CompilerParams(vmem_limit_bytes=limit * MIB)


def cost(flops, moved):
    return pl.CostEstimate(flops=flops, bytes_accessed=moved, transcendentals=0)


def weight_kernel(*refs):
    sources, out_ref = refs[:4], refs[4]
    line, place, core = here()
    for other in range(2):
        half = core if other == 0 else 1 - core
        group = sources[other * 2 : other * 2 + 2]
        count, rows, columns = group[0].shape[2:]
        column_slice = pl.ds(pl.multiple_of(half * columns, columns), columns)
        for number, spot in enumerate(spots(place, half)):
            for shift, flip in enumerate(LINE_FLIPS):
                start = (flipped(line, flip) * 4 + spot) * rows
                row_slice = pl.ds(pl.multiple_of(start, rows), rows)
                for block in range(count):
                    piece = group[number // 2][number % 2, shift, block]
                    out_ref[block, row_slice, column_slice] = piece


def place_weights(parts):
    count, rows, columns = parts[0].shape[2:]
    full = rows * 16
    return pl.pallas_call(
        weight_kernel,
        out_shape=jax.ShapeDtypeStruct((count, full, columns * 2), low),
        in_specs=[on_chip()] * 4,
        out_specs=on_chip(),
        compiler_params=params(8),
        cost_estimate=cost(0, 8 * full * count * columns),
    )(*parts)


def columns_by_core(value):
    keep, give = halves(value)
    return in_core_order(keep, send(give, swap_pairs()), 0)


def gather_far(pair):
    return jnp.concatenate([pair, send(pair, line_pairs(1))])


def with_other(first, far):
    return [first, far, send(first, swap_pairs()), send(far, swap_pairs())]


def roots_line(left_root, right_root):
    line, place, core = here()
    both = [jnp.transpose(root, (1, 0, 2)).astype(low) for root in (left_root, right_root)]
    every = columns_by_core(jnp.stack(both, axis=1))
    every = every.reshape((3, 4) + every.shape[1:])
    parts = [pick(every, line, 1)]
    for flip in (1, 2, 3):
        parts.append(send(pick(every, flipped(line, flip), 1), line_pairs(flip)))
    return parts


def sum_kernel(left_of, left, right, got, give_ref, kept_ref, passed_ref, total):
    line, place, core = here()
    step = pl.program_id(0)
    columns = got.shape[2]
    rows = kept_ref.shape[2]
    part = pl.ds(pl.multiple_of(core * columns, columns), columns)
    right_step = step if right.shape[0] > 1 else 0
    made = dot(left[left_of(step)], right[right_step, :, part], 0, 0)
    total[...] = made + got[step].astype(wide)
    own, first, second, both = spots(place, core)
    for row_line in range(4):

        def piece(spot):
            return total[pl.ds(pl.multiple_of((row_line * 4 + spot) * rows, rows), rows), :]

        give_ref[0, step, row_line] = piece(first).astype(low)
        give_ref[1, step, row_line] = piece(both).astype(low)
        kept_ref[step, row_line] = piece(own)
        passed_ref[step, row_line] = piece(second)


def sum_start(left_of, left, right, got):
    count, width = left.shape[1:]
    blocks, full, columns = got.shape
    shape = (blocks, 4, full // 16, columns)
    return pl.pallas_call(
        functools.partial(sum_kernel, left_of),
        grid=(blocks,),
        out_shape=(
            jax.ShapeDtypeStruct((2,) + shape, low),
            jax.ShapeDtypeStruct(shape, wide),
            jax.ShapeDtypeStruct(shape, wide),
        ),
        in_specs=[on_chip()] * 3,
        out_specs=(on_chip(),) * 3,
        scratch_shapes=[pltpu.VMEM((full, columns), wide)],
        compiler_params=params(10),
        cost_estimate=cost(blocks * count * width * width, 5 * blocks * width * width),
    )(left, right, got)


def add_first(got, kept, passed):
    return kept + got[0].astype(wide), (passed + got[1].astype(wide)).astype(low)


def cut_line(kept):
    line, place, core = here()
    given = jnp.stack([pick(kept, flipped(line, flip), 1) for flip in (1, 3)]).astype(low)
    return pick(kept, line, 1), pick(kept, flipped(line, 2), 1), given


def add_line(own, two, got):
    return own + got[0].astype(wide), (two + got[1].astype(wide)).astype(low)


def step_kernel(
    mine,
    theirs,
    left_mine,
    left_theirs,
    right_first,
    right_far,
    out_ref,
    square_ref,
    grad_ref,
    rows_ref,
    left_ref,
    right_ref,
    cross_ref,
):
    line, place, core = here()
    rows, columns = mine.shape[3:]

    def rows_of(row_line, spot):
        return pl.ds(pl.multiple_of((row_line * 4 + spot) * rows, rows), rows)

    def column_half(half):
        return pl.ds(pl.multiple_of(half * columns, columns), columns)

    for half, group, left in ((core, mine, left_mine), (1 - core, theirs, left_theirs)):
        for number, spot in enumerate(spots(place, half)):
            for step in range(4):
                grad_ref[rows_of(step, spot), column_half(half)] = group[number, 0, step]
        for flip in range(4):
            target = pl.ds(pl.multiple_of(flipped(line, flip) * rows, rows), rows)
            left_ref[target, column_half(half)] = left[flip, 0]
    for number, spot in enumerate(spots(place, core)):
        source = right_far if number > 1 else right_first
        for flip in range(4):
            right_ref[rows_of(flipped(line, flip), spot), :] = source[number % 2, flip, 0]
    for row_line in range(4):
        rows_ref[row_line * rows : (row_line + 1) * rows, :] = grad_ref[rows_of(row_line, place), :]
    left = dot(rows_ref[...], grad_ref[column_half(core), :], 1, 1)
    cross_ref[...] = dot(grad_ref[...], grad_ref[:, column_half(core)], 0, 0)
    lefted = dot(left_ref[...], grad_ref[...]).astype(low)
    stepped = dot(lefted, right_ref[...])
    square_ref[0] = jnp.sum(stepped * stepped, axis=0, keepdims=True)
    for row_line in range(4):
        part = slice(row_line * rows, (row_line + 1) * rows)
        out_ref[0, row_line, 0] = mine[0, 0, row_line]
        out_ref[0, row_line, 1] = left[part].astype(low)
        out_ref[0, row_line, 2] = cross_ref[rows_of(row_line, place), :].astype(low)
        out_ref[0, row_line, 3] = stepped[part].astype(low)


def step_chunks(mine, theirs, roots, number):
    chunks, lines, rows, columns = mine.shape[1:]
    full = rows * 16
    grad_spec = pl.BlockSpec((4, 1, lines, rows, columns), lambda step: (0, step, 0, 0, 0))
    left_spec = pl.BlockSpec((lines, 1, rows, columns), lambda step: (0, number + step, 0, 0))
    right_spec = pl.BlockSpec(
        (2, lines, 1, rows, columns), lambda step: (0, 0, number + step, 0, 0)
    )
    return pl.pallas_call(
        step_kernel,
        grid=(chunks,),
        out_shape=(
            jax.ShapeDtypeStruct((chunks, lines, 4, rows, columns), low),
            jax.ShapeDtypeStruct((chunks, 1, columns), wide),
        ),
        in_specs=[grad_spec] * 2 + [left_spec] * 2 + [right_spec] * 2,
        out_specs=(
            pl.BlockSpec((1, lines, 4, rows, columns), lambda step: (step, 0, 0, 0, 0)),
            pl.BlockSpec((1, 1, columns), lambda step: (step, 0, 0)),
        ),
        scratch_shapes=[
            pltpu.VMEM((full, columns * 2), low),
            pltpu.VMEM((lines * rows, columns * 2), low),
            pltpu.VMEM((lines * rows, columns * 2), low),
            pltpu.VMEM((full, columns), low),
            pltpu.VMEM((full, columns), wide),
        ],
        compiler_params=params(20),
        cost_estimate=cost(3 * chunks * full**3, 16 * chunks * full * full),
    )(mine, theirs, *roots)


def return_chunks(made):
    line, place, core = here()
    parts = [pick(made, line, 1)]
    for flip in (1, 2, 3):
        parts.append(send(pick(made, flipped(line, flip), 1), line_pairs(flip)))
    return jnp.stack(parts)


def last_kernel(
    attn, attn_other, pair, pair_other, blocks, left_stat, right_stat, scales, *outs
):
    grad_out, left_out, right_out, block_out = outs
    line, place, core = here()
    columns = attn.shape[4]

    def update(number, which, mine, theirs):
        for (source, index), half in ((mine, which), (theirs, 1 - which)):
            part = slice(half * columns, (half + 1) * columns)
            pieces = [source[index + (kind,)].astype(wide) for kind in range(4)]
            grad_out[number, :, part] = pieces[0]
            left_out[number, :, part] = 0.5 * left_stat[number, :, part] + 0.5 * pieces[1]
            right_out[number, :, part] = 0.5 * right_stat[number, :, part] + 0.5 * pieces[2]
            step = pieces[3] * scales[6 * which + number]
            block_out[number, :, part] = blocks[number, :, part] - step

    @pl.when(core == 0)
    def first():
        for number in range(6):
            source, other = (attn, attn_other) if number < 4 else (pair, pair_other)
            index = (flipped(line, number % 4), 0)
            update(number, 0, (source, index), (other, index))

    @pl.when(core == 1)
    def second():
        for number in range(6):
            block = number + 2
            index = (flipped(line, block % 4), block // 4)
            update(number, 1, (pair, index), (pair_other, index))


def update_blocks(attn, attn_other, pair, pair_other, blocks, left_stat, right_stat, scales):
    turned = [jnp.transpose(value, (1, 0, 2)) for value in (blocks, left_stat, right_stat)]
    shape = jax.ShapeDtypeStruct(turned[0].shape, wide)
    outs = pl.pallas_call(
        last_kernel,
        out_shape=(shape,) * 4,
        in_specs=[on_chip()] * 7 + [pl.BlockSpec(memory_space=pltpu.SMEM)],
        out_specs=(on_chip(),) * 4,
        compiler_params=params(8),
        cost_estimate=cost(0, 32 * shape.size),
    )(attn, attn_other, pair, pair_other, *turned, scales)
    return [jnp.transpose(value, (1, 0, 2)) for value in outs]


def head_masks():
    lane = lax.broadcasted_iota(jnp.int32, (1, 2 * HEAD_DIM), 1)
    return [(lane < HEAD_DIM).astype(wide).astype(low), (lane >= HEAD_DIM).astype(wide).astype(low)]


def head_shares(query, key, same):
    scores = dot(query, key, 1, 1) * HEAD_DIM ** (-0.5)
    scores = jnp.where(same, scores, -1e30)
    raised = jnp.exp(scores - jnp.max(scores, axis=-1, keepdims=True))
    return raised / jnp.sum(raised, axis=-1, keepdims=True)


def attend_kernel(buffer, weights, seg_column, seg_row, made_ref, sides_ref, answer_ref):
    same = seg_column[...] == seg_row[...]
    for kind in range(3):
        made_ref[kind] = dot(buffer[...], weights[kind]).astype(low)
    width = 2 * HEAD_DIM
    for pair in range(buffer.shape[1] // width):
        part = slice(pair * width, (pair + 1) * width)
        query, key, value = (made_ref[kind, :, part] for kind in range(3))
        context = None
        for mask in head_masks():
            shares = head_shares(query, key * mask, same).astype(low)
            term = dot(shares, value * mask)
            context = term if context is None else context + term
        sides_ref[1, :, part] = context.astype(low)
    sides_ref[0] = buffer[...]
    answer_ref[...] = dot(sides_ref[1], weights[3]).astype(low)


def attend(buffer, weights, segment):
    shape = jax.ShapeDtypeStruct(buffer.shape, low)
    rows, width = buffer.shape
    return pl.pallas_call(
        attend_kernel,
        out_shape=(
            jax.ShapeDtypeStruct((3,) + buffer.shape, low),
            jax.ShapeDtypeStruct((2,) + buffer.shape, low),
            shape,
        ),
        in_specs=[on_chip()] * 4,
        out_specs=(on_chip(),) * 3,
        compiler_params=params(10),
        cost_estimate=cost(12 * rows * width * width, 12 * width * width),
    )(buffer, weights, segment[:, None], segment[None, :])


def attend_back_kernel(
    sides,
    weights,
    seg_column,
    seg_row,
    made,
    grad_answer,
    theirs_ref,
    grads_ref,
    grad_buffer_ref,
    grad_context_ref,
):
    same = seg_column[...] == seg_row[...]
    core = lax.axis_index("own")
    grad_context_ref[...] = dot(grad_answer[...], weights[3], 1, 1).astype(low)
    grads_ref[3] = grad_answer[...]
    width = 2 * HEAD_DIM
    for pair in range(sides.shape[2] // width):
        part = slice(pair * width, (pair + 1) * width)
        query, key, value = (made[kind, :, part] for kind in range(3))
        above = grad_context_ref[:, part]
        sums = [None] * 3
        for mask in head_masks():
            key_head = key * mask
            shares = head_shares(query, key_head, same)
            grad_shares = dot(above, value * mask, 1, 1)
            inner = jnp.sum(shares * grad_shares, axis=-1, keepdims=True)
            grad_scores = (shares * (grad_shares - inner)).astype(low)
            terms = (
                dot(grad_scores, key_head),
                dot(grad_scores, query * mask, 0, 0),
                dot(shares.astype(low), above * mask, 0, 0),
            )
            sums = [
                term if total is None else total + term for term, total in zip(terms, sums)
            ]
        for kind, factor in enumerate((HEAD_DIM ** (-0.5), HEAD_DIM ** (-0.5), 1.0)):
            grads_ref[kind, :, part] = (sums[kind] * factor).astype(low)
    columns = theirs_ref.shape[2]
    part = pl.ds(pl.multiple_of((1 - core) * columns, columns), columns)
    for kind in range(4):
        theirs_ref[kind] = dot(sides[kind // 3], grads_ref[kind, :, part], 0, 0).astype(low)
    total = dot(grads_ref[0], weights[0], 1, 1)
    total = total + dot(grads_ref[1], weights[1], 1, 1)
    total = total + dot(grads_ref[2], weights[2], 1, 1)
    grad_buffer_ref[...] = total.astype(low)


def attend_back(sides, weights, segment, made, grad_answer):
    rows, width = grad_answer.shape
    return pl.pallas_call(
        attend_back_kernel,
        out_shape=(
            jax.ShapeDtypeStruct((4, width, width // 2), low),
            jax.ShapeDtypeStruct((4, rows, width), low),
            jax.ShapeDtypeStruct((rows, width), low),
        ),
        in_specs=[on_chip()] * 6,
        out_specs=(on_chip(),) * 3,
        scratch_shapes=[pltpu.VMEM((rows, width), low)],
        compiler_params=params(14),
        cost_estimate=cost(20 * rows * width * width, 16 * width * width),
    )(sides, weights, segment[:, None], segment[None, :], made, grad_answer)


def normal_parts(values):
    center = values - jnp.mean(values, axis=-1, keepdims=True)
    spread = jnp.mean(center * center, axis=-1, keepdims=True)
    return center, lax.rsqrt(spread + norm_eps)


def forward_kernel(
    tokens,
    placing,
    returned,
    gates,
    vectors,
    w_up,
    hidden_ref,
    second_ref,
    active_ref,
    slope_ref,
):
    step = pl.program_id(0)

    @pl.when(step == 0)
    def prepare():
        values = tokens[...].astype(wide) + gates[:, 0:1] * dot(placing[...], returned[...])
        hidden_ref[...] = values
        center, inverse = normal_parts(values)
        second_ref[...] = (center * inverse * vectors[3:4] + vectors[4:5]).astype(low)

    before = dot(second_ref[...], w_up[step])
    share = 0.5 + 0.5 * lax.erf(before * (0.5**0.5))
    density = jnp.exp(before * before * -0.5) * (0.5 / math.pi) ** 0.5
    active_ref[step] = (before * share).astype(low)
    slope_ref[step] = (share + before * density).astype(low)


def token_forward(tokens, placing, returned, gates, vectors, w_up):
    count, width = tokens.shape
    blocks = w_up.shape[0]
    by_block = jax.ShapeDtypeStruct((blocks, count, width), low)
    return pl.pallas_call(
        forward_kernel,
        grid=(blocks,),
        out_shape=(
            jax.ShapeDtypeStruct((count, width), wide),
            jax.ShapeDtypeStruct((count, width), low),
            by_block,
            by_block,
        ),
        in_specs=[on_chip()] * 6,
        out_specs=(on_chip(),) * 4,
        compiler_params=params(20),
        cost_estimate=cost(8 * blocks * count * width * width, 8 * blocks * width * width),
    )(tokens, placing, returned, gates, vectors, w_up)


def backward_kernel(
    above,
    hidden,
    active,
    slope,
    placing,
    returned,
    gates,
    vectors,
    w_up,
    w_down,
    mixed_ref,
    packed_ref,
    grad_hidden_ref,
    logit_ref,
    vector_ref,
    inner_ref,
    result,
    grad_second,
):
    step = pl.program_id(0)

    @pl.when(step == 0)
    def prepare():
        result[...] = hidden[...]
        grad_second[...] = jnp.zeros_like(grad_second)

    grad_active = dot(above[...], w_down[step], 1, 1)
    grad_inner = (grad_active * slope[step].astype(wide)).astype(low)
    inner_ref[step] = grad_inner
    result[...] += dot(active[step], w_down[step])
    grad_second[...] += dot(grad_inner, w_up[step], 1, 1)

    @pl.when(step == pl.num_programs(0) - 1)
    def finish():
        mixed_ref[...] = result[...].astype(low)
        center, inverse = normal_parts(hidden[...])
        scaled = center * inverse
        grads = grad_second[...]
        vector_ref[0:1] = jnp.sum(grads * scaled, axis=0, keepdims=True)
        vector_ref[1:2] = jnp.sum(grads, axis=0, keepdims=True)
        pulled = grads * vectors[3:4]
        pulled = (
            pulled
            - jnp.mean(pulled, axis=-1, keepdims=True)
            - scaled * jnp.mean(pulled * scaled, axis=-1, keepdims=True)
        )
        grad_hidden = above[...].astype(wide) + inverse * pulled
        grad_hidden_ref[...] = grad_hidden
        weighted = (grad_hidden * gates[:, 0:1]).astype(low)
        packed_ref[...] = dot(placing[...], weighted, 0, 0).astype(low)
        unpacked = dot(placing[...], returned[...])
        logit_ref[...] = gates[:, 1:2] * jnp.sum(grad_hidden * unpacked, axis=-1, keepdims=True)


def token_backward(above, hidden, active, slope, placing, returned, gates, vectors, w_up, w_down):
    count, width = above.shape
    slots = placing.shape[1]
    blocks = w_up.shape[0]
    return pl.pallas_call(
        backward_kernel,
        grid=(blocks,),
        out_shape=(
            jax.ShapeDtypeStruct((count, width), low),
            jax.ShapeDtypeStruct((slots, width), low),
            jax.ShapeDtypeStruct((count, width), wide),
            jax.ShapeDtypeStruct((count, 1), wide),
            jax.ShapeDtypeStruct((2, width), wide),
            jax.ShapeDtypeStruct((blocks, count, width), low),
        ),
        in_specs=[on_chip()] * 10,
        out_specs=(on_chip(),) * 6,
        scratch_shapes=[pltpu.VMEM((count, width), wide)] * 2,
        compiler_params=params(20),
        cost_estimate=cost(8 * blocks * count * width * width, 8 * blocks * width * width),
    )(
        above,
        hidden,
        active,
        slope,
        placing,
        returned,
        gates,
        vectors,
        w_up,
        w_down,
    )


def outer_kernel(left, right, theirs_ref):
    core = lax.axis_index("own")
    step = pl.program_id(0)
    columns = theirs_ref.shape[2]
    left_step = step if left.shape[0] > 1 else 0
    right_step = step if right.shape[0] > 1 else 0
    part = pl.ds(pl.multiple_of((1 - core) * columns, columns), columns)
    theirs_ref[step] = dot(left[left_step], right[right_step, :, part], 0, 0).astype(low)


def outer_theirs(left, right):
    count, width = left.shape[1:]
    blocks = max(left.shape[0], right.shape[0])
    return pl.pallas_call(
        outer_kernel,
        grid=(blocks,),
        out_shape=jax.ShapeDtypeStruct((blocks, width, width // 2), low),
        in_specs=[on_chip()] * 2,
        out_specs=on_chip(),
        compiler_params=params(8),
        cost_estimate=cost(blocks * count * width * width, 3 * blocks * width * width),
    )(left, right)


def column(values):
    return values[:, None]


def pack_kernel(
    tokens, chosen, packing, vectors, placing_ref, packed_ref, gates_ref
):
    count = tokens.shape[0]
    capacity = packing.shape[0]
    center, inverse = normal_parts(tokens[...].astype(wide))
    first = (center * inverse * vectors[0:1] + vectors[1:2]).astype(low)
    gate = jax.nn.sigmoid(jnp.sum(first.astype(wide) * vectors[2:3], axis=-1, keepdims=True))
    weighting = jnp.where(chosen[...] == 1, gate, 0.0)
    gates_ref[:, 0:1] = weighting
    gates_ref[:, 1:2] = weighting * (1.0 - gate)
    above = lax.broadcasted_iota(jnp.int32, (count, count), 0)
    below = lax.broadcasted_iota(jnp.int32, (count, count), 1)
    earlier = (below <= above).astype(wide).astype(low)
    flags = jnp.broadcast_to(chosen[...].astype(wide), (count, capacity))
    rank = dot(earlier, flags.astype(low))
    place_of = lax.broadcasted_iota(jnp.int32, (count, capacity), 1).astype(wide) + 1.0
    ranked = jnp.where(rank == place_of, flags, 0.0).astype(low)
    slots = lax.broadcasted_iota(jnp.int32, (capacity, capacity), 1)
    slot_of = (packing[...] == slots).astype(wide).astype(low)
    placing = dot(ranked, slot_of).astype(low)
    placing_ref[...] = placing
    packed_ref[...] = dot(placing, first, 0, 0).astype(low)


def pack_tokens(tokens, chosen, packing, vectors):
    count, width = tokens.shape
    capacity = packing.shape[0]
    return pl.pallas_call(
        pack_kernel,
        out_shape=(
            jax.ShapeDtypeStruct((count, capacity), low),
            jax.ShapeDtypeStruct((capacity, width), low),
            jax.ShapeDtypeStruct((count, 2), wide),
        ),
        in_specs=[on_chip()] * 4,
        out_specs=(on_chip(),) * 3,
        compiler_params=params(12),
        cost_estimate=cost(4 * count * capacity * width, 8 * count * width),
    )(tokens, column(chosen), column(packing), vectors)


def token_back_kernel(
    tokens, placing, grad_sent, grad_hidden, grad_logit, vectors, out_ref, vector_ref
):
    grad_first = dot(placing[...], grad_sent[...]) + grad_logit[...] * vectors[2:3]
    center, inverse = normal_parts(tokens[...].astype(wide))
    scaled = center * inverse
    vector_ref[0:1] = jnp.sum(grad_first * scaled, axis=0, keepdims=True)
    vector_ref[1:2] = jnp.sum(grad_first, axis=0, keepdims=True)
    first = (scaled * vectors[0:1] + vectors[1:2]).astype(low).astype(wide)
    vector_ref[2:3] = jnp.sum(grad_logit[...] * first, axis=0, keepdims=True)
    pulled = grad_first * vectors[0:1]
    pulled = (
        pulled
        - jnp.mean(pulled, axis=-1, keepdims=True)
        - scaled * jnp.mean(pulled * scaled, axis=-1, keepdims=True)
    )
    out_ref[...] = (grad_hidden[...] + inverse * pulled).astype(low)


def token_back(tokens, placing, grad_sent, grad_hidden, grad_logit, vectors):
    count, width = tokens.shape
    return pl.pallas_call(
        token_back_kernel,
        out_shape=(
            jax.ShapeDtypeStruct((count, width), low),
            jax.ShapeDtypeStruct((3, width), wide),
        ),
        in_specs=[on_chip()] * 6,
        out_specs=(on_chip(),) * 2,
        compiler_params=params(12),
        cost_estimate=cost(2 * count * width * placing.shape[1], 12 * count * width),
    )(tokens, placing, grad_sent, grad_hidden, grad_logit, vectors)


def all_sum(value):
    value = value + send(value, swap_pairs())
    for flip in (2, 4, 8, 16):
        value = value + send(value, [(i, i ^ flip) for i in range(32)])
    return value


def exchange(value, n_data):
    capacity, width = value.shape
    moved = lax.all_to_all(
        value.reshape(n_data, capacity // n_data, width), "dp", split_axis=0, concat_axis=0, tiled=True
    )
    return moved.reshape(capacity, width)


def block_shards(
    tokens,
    cotangent,
    selected,
    packing,
    segments,
    blocks,
    left_stat,
    right_stat,
    left_root,
    right_root,
    vectors,
    moment,
):
    model_width = tokens.shape[2]
    token_count = tokens.shape[0] * tokens.shape[1]
    n_data = lax.axis_size("dp")
    capacity = packing.shape[1]
    line, place, core = here()
    own_tokens = tokens.reshape(token_count, model_width)
    above = cotangent.reshape(token_count, model_width)
    segment = segments[0]

    every = columns_by_core(jnp.transpose(blocks, (1, 0, 2)).astype(low))
    placing, packed, gates = pack_tokens(
        own_tokens, selected.reshape(token_count), packing[0], vectors
    )
    buffer = exchange(packed, n_data)
    attn_two = send(every[:4], line_pairs(2))
    ffn_two = jnp.stack([every[4:], send(after(every[4:], attn_two), line_pairs(2))])
    line_attn = after(gather_far(jnp.stack([every[:4], attn_two])), packed)
    near_attn = send(line_attn, plane_pairs(0))
    first_attn = after(jnp.stack([line_attn, near_attn]), ffn_two)
    line_ffn = gather_far(ffn_two)
    far_attn = after(send(first_attn, plane_pairs(1)), line_ffn, buffer)
    near_ffn = send(line_ffn, plane_pairs(0))
    w_attn = place_weights(with_other(first_attn, far_attn))
    made, sides, answer = attend(buffer, w_attn, segment)
    root_parts = roots_line(after(left_root, line_ffn), right_root)
    root_parts = lax.optimization_barrier((answer, *root_parts))[1:]
    left_line, right_line = (jnp.stack([part[:, kind] for part in root_parts]) for kind in range(2))
    first_up = jnp.stack([line_ffn[:, :4], after(near_ffn, answer, right_line)[:, :4]])
    far_up = send(first_up, plane_pairs(1))
    first_down = after(jnp.stack([line_ffn[:, 4:], near_ffn[:, 4:]]), far_up)
    far_down = send(first_down, plane_pairs(1))
    w_up = place_weights(with_other(first_up, far_up))
    returned = exchange(answer, n_data)

    hidden, second_low, active, slope = token_forward(
        own_tokens, placing, returned, gates, vectors, w_up
    )
    down_theirs = outer_theirs(active, above[None])
    w_down = place_weights(with_other(first_down, after(far_down, active)))
    near_right = send(after(right_line, w_down), plane_pairs(0))
    mixed, grad_packed, grad_hidden, grad_logit, vector_two, grad_inner = token_backward(
        above,
        hidden,
        active,
        slope,
        placing,
        returned,
        gates,
        vectors,
        w_up,
        after(w_down, down_theirs),
    )
    grad_answer = exchange(grad_packed, n_data)
    up_theirs = outer_theirs(after(second_low, near_right)[None], grad_inner)
    first_right = jnp.stack([right_line, near_right])
    far_right = send(first_right, plane_pairs(1))
    roots = (left_line, send(left_line, swap_pairs()), first_right, far_right)
    down_got = send(down_theirs, swap_pairs())
    down_give, *down_kept = sum_start(lambda step: step, active, above[None], down_got)
    down_got = send(after(down_give, grad_answer, far_right), plane_pairs(0))
    up_got = send(up_theirs, swap_pairs())
    up_give, *up_kept = sum_start(lambda step: 0, second_low[None], grad_inner, up_got)
    up_got = send(after(up_give, grad_answer), plane_pairs(0))

    attn_theirs, grads, grad_buffer = attend_back(
        sides, w_attn, segment, made, after(grad_answer, up_give)
    )
    grad_sent = exchange(grad_buffer, n_data)
    attn_got = send(after(attn_theirs, down_got), swap_pairs())
    attn_give, *attn_kept = sum_start(lambda step: step // 3, sides, grads, attn_got)

    up_kept, up_give = add_first(up_got, *up_kept)
    down_kept, down_give = add_first(down_got, *down_kept)
    pair_got = send(jnp.stack([up_give, down_give]), plane_pairs(1))
    pair_kept = jnp.stack([up_kept, down_kept]) + pair_got.astype(wide)
    pair_own, pair_two, pair_give = cut_line(pair_kept)
    pair_got = send(after(pair_give, attn_give, grad_sent), line_pairs(1))
    attn_got = send(attn_give, plane_pairs(0))
    pair_own, pair_give = add_line(pair_own, pair_two, pair_got)

    grad_tokens, vector_one = token_back(
        own_tokens, placing, grad_sent, grad_hidden, grad_logit, vectors
    )
    pair_got = send(after(pair_give, attn_got, vector_one), line_pairs(2))
    attn_kept, attn_give = add_first(attn_got, *attn_kept)
    attn_got = send(attn_give, plane_pairs(1))
    pair_own = (pair_own + pair_got.astype(wide)).astype(low)

    pair_near = send(after(pair_own, attn_got), plane_pairs(0))
    attn_own, attn_two, attn_give = cut_line((attn_kept + attn_got.astype(wide))[None])
    attn_got = send(attn_give, line_pairs(1))
    pair_first = jnp.stack([pair_own, pair_near])
    attn_own, attn_give = add_line(attn_own, attn_two, attn_got)

    pair_far = send(after(pair_first, attn_give), plane_pairs(1))
    attn_got = send(attn_give, line_pairs(2))
    pair_mine = jnp.concatenate([pair_first, pair_far])
    attn_own = (attn_own + attn_got.astype(wide)).astype(low)

    pair_theirs = send(after(pair_mine, attn_own), swap_pairs())
    attn_near = send(attn_own, plane_pairs(0))
    attn_first = jnp.stack([attn_own, attn_near])

    pair_made, pair_square = step_chunks(
        pair_mine, after(pair_theirs, attn_first), roots, 1
    )
    attn_far = send(attn_first, plane_pairs(1))
    attn_mine = jnp.concatenate([attn_first, attn_far])

    pair = return_chunks(after(pair_made, attn_far))
    attn_theirs = send(after(attn_mine, pair_made), swap_pairs())
    attn_made, attn_square = step_chunks(attn_mine, attn_theirs, roots, 0)
    attn = return_chunks(after(attn_made, pair))
    squares = jnp.concatenate([jnp.sum(attn_square, axis=2), jnp.sum(pair_square, axis=2)])
    lane = lax.broadcasted_iota(jnp.int32, (1, model_width), 1)
    square_row = sum(
        jnp.where(lane == 4 * chunk + line, squares[chunk], 0.0) for chunk in range(3)
    )
    sums = all_sum(jnp.concatenate([vector_one, vector_two, square_row]))
    vector_grad = sums[:5]
    pair_other = send(pair, swap_pairs())
    attn_other = send(attn, [(i, i ^ 1) for i in range(1, 32, 2)])
    size = model_width * model_width
    scales = block_rate * lax.rsqrt(sums[5, :12] / size + norm_eps)
    grad_own, left_new, right_new, new_blocks = update_blocks(
        attn, attn_other, pair, pair_other, blocks, left_stat, right_stat, scales
    )
    moment_new = 0.5 * moment + 0.5 * vector_grad
    row_squares = jnp.mean(moment_new * moment_new, axis=1, keepdims=True)
    vector_new = vectors - vector_rate * moment_new * lax.rsqrt(row_squares + norm_eps)
    return (
        mixed.reshape(tokens.shape),
        grad_tokens.reshape(tokens.shape),
        grad_own,
        left_new,
        right_new,
        new_blocks,
        vector_grad,
        moment_new,
        vector_new,
    )


def shards(
    tokens,
    cotangent,
    selected,
    packing,
    segments,
    blocks,
    left_stat,
    right_stat,
    left_root,
    right_root,
    vectors,
    moment,
):
    model_width = tokens.shape[2]
    token_count = tokens.shape[0] * tokens.shape[1]
    n_data = lax.axis_size("dp")
    n_owner = lax.axis_size("own")
    shard_rows = blocks.shape[0]
    own_blocks = blocks.shape[1]
    up_blocks = (own_blocks * n_owner - 4) // 2
    capacity = packing.shape[1]
    per_peer = capacity // n_data
    head_count = model_width // HEAD_DIM
    score_scale = HEAD_DIM ** (-0.5)
    flat_weights = blocks.astype(jnp.bfloat16).reshape(1, shard_rows * own_blocks * model_width)
    gathered = lax.all_gather(flat_weights, ("dp", "own"), axis=0, tiled=True)
    gathered = gathered.reshape(n_data, n_owner, shard_rows, own_blocks, model_width)

    def matrix(number):
        return gathered[:, number // own_blocks, :, number % own_blocks, :].reshape(
            model_width, model_width
        )

    w_query = matrix(0)
    w_key = matrix(1)
    w_value = matrix(2)
    w_out = matrix(3)
    w_up = jnp.concatenate([matrix(4 + position) for position in range(up_blocks)], axis=1)
    w_down = jnp.concatenate(
        [matrix(4 + up_blocks + position) for position in range(up_blocks)], axis=0
    )
    inputs = tokens.reshape(token_count, model_width).astype(jnp.float32)
    chosen = selected.reshape(token_count)
    normed_one, norm_one_back = jax.vjp(layer_norm, inputs, vectors[0], vectors[1])
    first_low = normed_one.astype(jnp.bfloat16)
    first_wide = first_low.astype(jnp.float32)
    gate_values = jax.nn.sigmoid(jnp.dot(first_wide, vectors[2], precision=highest))
    before = jnp.cumsum(chosen) - 1
    slot_index = jnp.where(chosen == 1, packing[0][jnp.clip(before, 0, capacity - 1)], -1)
    placing = (slot_index[None, :] == jnp.arange(capacity, dtype=jnp.int32)[:, None]).astype(
        jnp.bfloat16
    )
    packed = jnp.dot(placing, first_low, preferred_element_type=jnp.float32).astype(jnp.bfloat16)
    buffer = lax.all_to_all(
        packed.reshape(n_data, per_peer, model_width), "dp", split_axis=0, concat_axis=0, tiled=True
    )
    buffer = buffer.reshape(capacity, model_width)

    def project(matrix_in):
        made = jnp.dot(buffer, matrix_in, preferred_element_type=jnp.float32).astype(jnp.bfloat16)
        return made.reshape(capacity, head_count, HEAD_DIM)

    query_rows = project(w_query)
    key_rows = project(w_key)
    value_rows = project(w_value)
    segment = segments[0]
    block_rows = math.gcd(capacity, 512)
    starts = jnp.arange(capacity // block_rows, dtype=jnp.int32) * block_rows

    def masked_scores():
        scores = (
            jnp.einsum("qhd,khd->hqk", query_rows, key_rows, preferred_element_type=jnp.float32)
            * score_scale
        )
        same_segment = segment[:, None] == segment[None, :]
        return (jnp.where(same_segment[None, :, :], scores, -1e30), query_rows)

    def forward_block(first_row):
        scores, unused_block = masked_scores()
        largest = jnp.max(scores, axis=-1, keepdims=True)
        raised = jnp.exp(scores - largest)
        row_total = jnp.sum(raised, axis=-1, keepdims=True)
        shares = (raised / row_total).astype(jnp.bfloat16)
        context_part = jnp.einsum(
            "hqk,khd->qhd", shares, value_rows, preferred_element_type=jnp.float32
        )
        return (context_part.astype(jnp.bfloat16), largest[..., 0] + jnp.log(row_total[..., 0]))

    context_blocks, lse_blocks = lax.map(forward_block, starts)
    context = context_blocks.reshape(capacity, model_width)
    answer = jnp.dot(context, w_out, preferred_element_type=jnp.float32).astype(jnp.bfloat16)
    returned = lax.all_to_all(
        answer.reshape(n_data, per_peer, model_width), "dp", split_axis=0, concat_axis=0, tiled=True
    )
    returned = returned.reshape(capacity, model_width)
    unpacked = jnp.einsum("mt,md->td", placing, returned, preferred_element_type=jnp.float32)
    weighting = jnp.where(chosen == 1, gate_values, 0.0)
    hidden = inputs + weighting[:, None] * unpacked
    normed_two, norm_two_back = jax.vjp(layer_norm, hidden, vectors[3], vectors[4])
    second_low = normed_two.astype(jnp.bfloat16)
    pre_active = jnp.dot(second_low, w_up, preferred_element_type=jnp.float32)
    active_wide, gelu_back = jax.vjp(gelu_exact, pre_active)
    active = active_wide.astype(jnp.bfloat16)
    result = hidden + jnp.dot(active, w_down, preferred_element_type=jnp.float32)
    mixed = result.astype(jnp.bfloat16).reshape(tokens.shape)
    upstream = cotangent.reshape(token_count, model_width)
    grad_down = jnp.einsum("tf,td->fd", active, upstream, preferred_element_type=jnp.float32)
    grad_active = jnp.einsum("td,fd->tf", upstream, w_down, preferred_element_type=jnp.float32)
    grad_inner = gelu_back(grad_active)[0].astype(jnp.bfloat16)
    grad_up = jnp.einsum("td,tf->df", second_low, grad_inner, preferred_element_type=jnp.float32)
    grad_second = jnp.einsum("tf,df->td", grad_inner, w_up, preferred_element_type=jnp.float32)
    grad_hidden_part, grad_gain_two, grad_bias_two = norm_two_back(grad_second)
    grad_hidden = upstream.astype(jnp.float32) + grad_hidden_part
    grad_token_back = (grad_hidden * weighting[:, None]).astype(jnp.bfloat16)
    grad_packed = jnp.dot(placing, grad_token_back, preferred_element_type=jnp.float32).astype(
        jnp.bfloat16
    )
    router_pull = jnp.where(chosen == 1, jnp.sum(grad_hidden * unpacked, axis=-1), 0.0)
    grad_logit = router_pull * gate_values * (1.0 - gate_values)
    grad_answer = lax.all_to_all(
        grad_packed.reshape(n_data, per_peer, model_width),
        "dp",
        split_axis=0,
        concat_axis=0,
        tiled=True,
    )
    grad_answer = grad_answer.reshape(capacity, model_width)
    grad_out = jnp.einsum("md,me->de", context, grad_answer, preferred_element_type=jnp.float32)
    grad_context = jnp.einsum("me,de->md", grad_answer, w_out, preferred_element_type=jnp.float32)
    grad_context = grad_context.astype(jnp.bfloat16).reshape(capacity, head_count, HEAD_DIM)

    def backward_block(running, item_pair):
        first_row, lse_block = item_pair
        scores, query_block = masked_scores()
        shares_wide = jnp.exp(scores - lse_block[..., None])
        grad_shares = jnp.einsum(
            "qhd,khd->hqk", grad_context, value_rows, preferred_element_type=jnp.float32
        )
        inner_sum = jnp.sum(shares_wide * grad_shares, axis=-1, keepdims=True)
        grad_scores = (shares_wide * (grad_shares - inner_sum)).astype(jnp.bfloat16)
        grad_query_block = (
            jnp.einsum("hqk,khd->qhd", grad_scores, key_rows, preferred_element_type=jnp.float32)
            * score_scale
        )
        key_sum = (
            running[0]
            + jnp.einsum(
                "hqk,qhd->khd", grad_scores, query_block, preferred_element_type=jnp.float32
            )
            * score_scale
        )
        value_sum = running[1] + jnp.einsum(
            "hqk,qhd->khd",
            shares_wide.astype(jnp.bfloat16),
            grad_context,
            preferred_element_type=jnp.float32,
        )
        return ((key_sum, value_sum), grad_query_block)

    zeros_init = jnp.zeros((capacity, head_count, HEAD_DIM), jnp.float32)
    (key_total, value_total), query_grads = lax.scan(
        backward_block, (zeros_init, zeros_init), (starts, lse_blocks)
    )
    grad_query = query_grads.reshape(capacity, model_width).astype(jnp.bfloat16)
    grad_key = key_total.reshape(capacity, model_width).astype(jnp.bfloat16)
    grad_value = value_total.reshape(capacity, model_width).astype(jnp.bfloat16)
    grad_w_query = jnp.einsum("md,me->de", buffer, grad_query, preferred_element_type=jnp.float32)
    grad_w_key = jnp.einsum("md,me->de", buffer, grad_key, preferred_element_type=jnp.float32)
    grad_w_value = jnp.einsum("md,me->de", buffer, grad_value, preferred_element_type=jnp.float32)
    grad_buffer = jnp.einsum("me,de->md", grad_query, w_query, preferred_element_type=jnp.float32)
    grad_buffer = grad_buffer + jnp.einsum(
        "me,de->md", grad_key, w_key, preferred_element_type=jnp.float32
    )
    grad_buffer = grad_buffer + jnp.einsum(
        "me,de->md", grad_value, w_value, preferred_element_type=jnp.float32
    )
    grad_buffer = grad_buffer.astype(jnp.bfloat16)
    grad_sent = lax.all_to_all(
        grad_buffer.reshape(n_data, per_peer, model_width),
        "dp",
        split_axis=0,
        concat_axis=0,
        tiled=True,
    )
    grad_sent = grad_sent.reshape(capacity, model_width)
    grad_first = jnp.einsum("mt,md->td", placing, grad_sent, preferred_element_type=jnp.float32)
    grad_first = grad_first + grad_logit[:, None] * vectors[2][None, :]
    grad_router = jnp.sum(grad_logit[:, None] * first_wide, axis=0)
    grad_input_part, grad_gain_one, grad_bias_one = norm_one_back(grad_first)
    grad_tokens = (grad_hidden + grad_input_part).astype(jnp.bfloat16).reshape(tokens.shape)
    pieces = [grad_w_query, grad_w_key, grad_w_value, grad_out]
    pieces = pieces + [
        grad_up[:, position * model_width : (position + 1) * model_width]
        for position in range(up_blocks)
    ]
    pieces = pieces + [
        grad_down[position * model_width : (position + 1) * model_width, :]
        for position in range(up_blocks)
    ]
    local_terms = jnp.stack(pieces, axis=1)
    vector_terms = jnp.stack(
        [grad_gain_one, grad_bias_one, grad_router, grad_gain_two, grad_bias_two]
    )
    partial_value = lax.psum_scatter(local_terms, "dp", scatter_dimension=0, tiled=True)
    grad_own = lax.psum_scatter(
        partial_value.astype(jnp.bfloat16), "own", scatter_dimension=1, tiled=True
    ).astype(jnp.float32)
    vector_grad = lax.psum(vector_terms, ("dp", "own"))
    full_grad = lax.all_gather(grad_own.astype(jnp.bfloat16), "dp", axis=0, tiled=True).astype(
        grad_own.dtype
    )
    row_start = lax.axis_index("dp") * shard_rows
    left_new = 0.5 * left_stat + 0.5 * jnp.einsum(
        "rbk,nbk->rbn", grad_own, full_grad, precision=highest
    )
    column_part = lax.dynamic_slice_in_dim(full_grad, row_start, shard_rows, 2)
    right_new = 0.5 * right_stat + 0.5 * jnp.einsum(
        "nbr,nbk->rbk", column_part, full_grad, precision=highest
    )
    lefted = jnp.einsum("rbn,nbk->rbk", left_root, full_grad, precision=highest)
    precond = jnp.zeros_like(grad_own) + jnp.einsum(
        "rbn,nbk->rbk",
        lefted,
        lax.all_gather(right_root.astype(jnp.bfloat16), "dp", axis=0, tiled=True).astype(
            jnp.float32
        ),
        precision=highest,
    )
    square_sums = lax.psum(jnp.sum(precond * precond, axis=(0, 2)), "dp")
    step_scale = lax.rsqrt(square_sums / (model_width * model_width) + norm_eps)
    new_blocks = blocks - block_rate * precond * step_scale[None, :, None]
    moment_new = 0.5 * moment + 0.5 * vector_grad
    row_squares = jnp.mean(moment_new * moment_new, axis=1, keepdims=True)
    vector_new = vectors - vector_rate * moment_new * lax.rsqrt(row_squares + norm_eps)
    return (
        mixed,
        grad_tokens,
        grad_own,
        left_new,
        right_new,
        new_blocks,
        vector_grad,
        moment_new,
        vector_new,
    )


def solution(mesh):
    placed = (
        P(("dp", "own"), None, None),
        P(("dp", "own"), None, None),
        P(("dp", "own"), None),
        P(("dp", "own"), None),
        P(("dp", "own"), None),
        P("dp", "own", None),
        P("dp", "own", None),
        P("dp", "own", None),
        P("dp", "own", None),
        P("dp", "own", None),
        P(),
        P(),
    )
    small = mesh.shape["dp"] == 16 and mesh.shape["own"] == 2
    return jax.shard_map(
        block_shards if small else shards,
        mesh=mesh,
        in_specs=placed,
        out_specs=(
            P(("dp", "own"), None, None),
            P(("dp", "own"), None, None),
            P("dp", "own", None),
            P("dp", "own", None),
            P("dp", "own", None),
            P("dp", "own", None),
            P(),
            P(),
            P(),
        ),
        check_vma=False,
    )
```

```python
import functools
import math

import jax
import jax.numpy as jnp
from jax import lax
from jax.experimental import pallas as pl
from jax.experimental.pallas import tpu as pltpu
from jax.sharding import PartitionSpec as P

HEAD_DIM = 64


norm_eps = 1e-06
block_rate = 0.03
vector_rate = 0.04
highest = lax.Precision.HIGHEST


def layer_norm(values, norm_gain, norm_bias):
    center = values - jnp.mean(values, axis=-1, keepdims=True)
    spread = jnp.mean(center * center, axis=-1, keepdims=True)
    return center * lax.rsqrt(spread + norm_eps) * norm_gain + norm_bias


def gelu_exact(values):
    return jax.nn.gelu(values, approximate=False)


BOTH = ("dp", "own")
low = jnp.bfloat16
wide = jnp.float32
MIB = 2**20


def swap_pairs():
    return [(i, i ^ 1) for i in range(32)]


def plane_pairs(step):
    pairs = []
    for i in range(32):
        place, core = i // 2, i % 2
        flip = (1, 2)[step ^ core]
        pairs.append((i, (place ^ flip) * 2 + core))
    return pairs


def line_pairs(flip):
    return [(i, i ^ (8 * flip)) for i in range(32)]


def send(value, pairs):
    return lax.ppermute(value, BOTH, pairs)


def after(value, *others):
    return lax.optimization_barrier((value,) + others)[0]


def pick(value, index, axis):
    return lax.dynamic_index_in_dim(value, index, axis, keepdims=False)


def first_core():
    return lax.axis_index("own") == 0


def halves(value):
    middle = value.shape[-1] // 2
    lower, upper = value[..., :middle], value[..., middle:]
    return jnp.where(first_core(), lower, upper), jnp.where(first_core(), upper, lower)


def in_core_order(mine, theirs, axis):
    return jnp.where(
        first_core(),
        jnp.concatenate([mine, theirs], axis=axis),
        jnp.concatenate([theirs, mine], axis=axis),
    )


LINE_FLIPS = (0, 2, 1, 3)


def flipped(index, flip):
    return jnp.bitwise_xor(index, flip)


def spots(place, half):
    first, second = half + 1, 2 - half
    return [
        place,
        flipped(place, first),
        flipped(place, second),
        flipped(place, 3),
    ]


def here():
    device = lax.axis_index("dp")
    return device // 4, device % 4, lax.axis_index("own")


def dot(left, right, left_axis=1, right_axis=0):
    return lax.dot_general(
        left, right, (((left_axis,), (right_axis,)), ((), ())), preferred_element_type=wide
    )


def on_chip():
    return pl.BlockSpec(memory_space=pltpu.VMEM)


def whole(value):
    return pl.BlockSpec(value.shape, lambda *steps: (0,) * value.ndim)


def params(limit):
    return pltpu.CompilerParams(vmem_limit_bytes=limit * MIB)


def cost(flops, moved):
    return pl.CostEstimate(flops=flops, bytes_accessed=moved, transcendentals=0)


def place_block(parts, block, target):
    line, place, core = here()
    rows, columns = parts[0].shape[3:]
    for other in range(2):
        half = core if other == 0 else 1 - core
        column_slice = pl.ds(pl.multiple_of(half * columns, columns), columns)
        for number, spot in enumerate(spots(place, half)):
            for index, flip in enumerate(LINE_FLIPS):
                start = (flipped(line, flip) * 4 + spot) * rows
                row_slice = pl.ds(pl.multiple_of(start, rows), rows)
                piece = parts[2 * other + number // 2][number % 2, index, block]
                target[row_slice, column_slice] = piece


def columns_by_core(value):
    keep, give = halves(value)
    return in_core_order(keep, send(give, swap_pairs()), 0)


def gather_far(pair):
    return jnp.concatenate([pair, send(pair, line_pairs(1))])


def with_other(first, far):
    return [first, far, send(first, swap_pairs()), send(far, swap_pairs())]


def roots_by_core(left_root, right_root):
    both = [jnp.transpose(root, (1, 0, 2)).astype(low) for root in (left_root, right_root)]
    every = columns_by_core(jnp.stack(both, axis=1))
    return every.reshape((3, 4) + every.shape[1:])


def roots_line(every):
    line, place, core = here()
    parts = [pick(every, line, 1)]
    for flip in (1, 2, 3):
        parts.append(send(pick(every, flipped(line, flip), 1), line_pairs(flip)))
    return parts


def sum_kernel(left_of, left, right, got, give_ref, kept_ref, passed_ref, total):
    line, place, core = here()
    step = pl.program_id(0)
    columns = got.shape[2]
    rows = kept_ref.shape[2]
    part = pl.ds(pl.multiple_of(core * columns, columns), columns)
    right_step = step if right.shape[0] > 1 else 0
    made = dot(left[left_of(step)], right[right_step, :, part], 0, 0)
    total[...] = made + got[step].astype(wide)
    own, first, second, both = spots(place, core)
    for row_line in range(4):

        def piece(spot):
            return total[pl.ds(pl.multiple_of((row_line * 4 + spot) * rows, rows), rows), :]

        give_ref[0, step, row_line] = piece(first).astype(low)
        give_ref[1, step, row_line] = piece(both).astype(low)
        kept_ref[step, row_line] = piece(own)
        passed_ref[step, row_line] = piece(second)


def sum_start(left_of, left, right, got):
    count, width = left.shape[1:]
    blocks, full, columns = got.shape
    shape = (blocks, 4, full // 16, columns)
    return pl.pallas_call(
        functools.partial(sum_kernel, left_of),
        grid=(blocks,),
        out_shape=(
            jax.ShapeDtypeStruct((2,) + shape, low),
            jax.ShapeDtypeStruct(shape, wide),
            jax.ShapeDtypeStruct(shape, wide),
        ),
        in_specs=[on_chip()] * 3,
        out_specs=(on_chip(),) * 3,
        scratch_shapes=[pltpu.VMEM((full, columns), wide)],
        compiler_params=params(10),
        cost_estimate=cost(blocks * count * width * width, 5 * blocks * width * width),
    )(left, right, got)


def add_first(got, kept, passed):
    return kept + got[0].astype(wide), (passed + got[1].astype(wide)).astype(low)


def cut_line(kept):
    line, place, core = here()
    given = jnp.stack([pick(kept, flipped(line, flip), 1) for flip in (1, 3)]).astype(low)
    return pick(kept, line, 1), pick(kept, flipped(line, 2), 1), given


def add_line(own, two, got):
    return own + got[0].astype(wide), (two + got[1].astype(wide)).astype(low)


def step_kernel(
    mine,
    theirs,
    left_mine,
    left_theirs,
    right_first,
    right_far,
    out_ref,
    square_ref,
    grad_ref,
    rows_ref,
    left_ref,
    right_ref,
    cross_ref,
):
    line, place, core = here()
    rows, columns = mine.shape[3:]

    def rows_of(row_line, spot):
        return pl.ds(pl.multiple_of((row_line * 4 + spot) * rows, rows), rows)

    def column_half(half):
        return pl.ds(pl.multiple_of(half * columns, columns), columns)

    for half, group, left in ((core, mine, left_mine), (1 - core, theirs, left_theirs)):
        for number, spot in enumerate(spots(place, half)):
            for step in range(4):
                grad_ref[rows_of(step, spot), column_half(half)] = group[number, 0, step]
        for flip in range(4):
            target = pl.ds(pl.multiple_of(flipped(line, flip) * rows, rows), rows)
            left_ref[target, column_half(half)] = left[flip, 0]
    for number, spot in enumerate(spots(place, core)):
        source = right_far if number > 1 else right_first
        for flip in range(4):
            right_ref[rows_of(flipped(line, flip), spot), :] = source[number % 2, flip, 0]
    for row_line in range(4):
        rows_ref[row_line * rows : (row_line + 1) * rows, :] = grad_ref[rows_of(row_line, place), :]
    left = dot(rows_ref[...], grad_ref[column_half(core), :], 1, 1)
    cross_ref[...] = dot(grad_ref[...], grad_ref[:, column_half(core)], 0, 0)
    lefted = dot(left_ref[...], grad_ref[...]).astype(low)
    stepped = dot(lefted, right_ref[...])
    square_ref[0] = jnp.sum(stepped * stepped, axis=0, keepdims=True)
    for row_line in range(4):
        part = slice(row_line * rows, (row_line + 1) * rows)
        out_ref[0, row_line, 0] = left[part].astype(low)
        out_ref[0, row_line, 1] = cross_ref[rows_of(row_line, place), :].astype(low)
        out_ref[0, row_line, 2] = stepped[part].astype(low)


def step_chunks(mine, theirs, roots, number):
    chunks, lines, rows, columns = mine.shape[1:]
    full = rows * 16
    grad_spec = pl.BlockSpec((4, 1, lines, rows, columns), lambda step: (0, step, 0, 0, 0))
    left_spec = pl.BlockSpec((lines, 1, rows, columns), lambda step: (0, number + step, 0, 0))
    right_spec = pl.BlockSpec(
        (2, lines, 1, rows, columns), lambda step: (0, 0, number + step, 0, 0)
    )
    return pl.pallas_call(
        step_kernel,
        grid=(chunks,),
        out_shape=(
            jax.ShapeDtypeStruct((chunks, lines, 3, rows, columns), low),
            jax.ShapeDtypeStruct((chunks, 1, columns), wide),
        ),
        in_specs=[grad_spec] * 2 + [left_spec] * 2 + [right_spec] * 2,
        out_specs=(
            pl.BlockSpec((1, lines, 3, rows, columns), lambda step: (step, 0, 0, 0, 0)),
            pl.BlockSpec((1, 1, columns), lambda step: (step, 0, 0)),
        ),
        scratch_shapes=[
            pltpu.VMEM((full, columns * 2), low),
            pltpu.VMEM((lines * rows, columns * 2), low),
            pltpu.VMEM((lines * rows, columns * 2), low),
            pltpu.VMEM((full, columns), low),
            pltpu.VMEM((full, columns), wide),
        ],
        compiler_params=params(20),
        cost_estimate=cost(3 * chunks * full**3, 16 * chunks * full * full),
    )(mine, theirs, *roots)


def return_chunks(made):
    line, place, core = here()
    parts = [pick(made, line, 1)]
    for flip in (1, 2, 3):
        parts.append(send(pick(made, flipped(line, flip), 1), line_pairs(flip)))
    return parts


def joined(rows, rest):
    return jnp.stack(
        [jnp.concatenate([row[:, None], more], axis=1) for row, more in zip(rows, rest)]
    )


def last_kernel(
    attn, attn_other, pair, pair_other, blocks, left_stat, right_stat, scales, *outs
):
    grad_out, left_out, right_out, block_out = outs
    line, place, core = here()
    columns = attn.shape[4]

    def update(number, which, mine, theirs):
        for (source, index), half in ((mine, which), (theirs, 1 - which)):
            part = slice(half * columns, (half + 1) * columns)
            pieces = [source[index + (kind,)].astype(wide) for kind in range(4)]
            grad_out[number, :, part] = pieces[0]
            left_out[number, :, part] = 0.5 * left_stat[number, :, part] + 0.5 * pieces[1]
            right_out[number, :, part] = 0.5 * right_stat[number, :, part] + 0.5 * pieces[2]
            step = pieces[3] * scales[6 * which + number]
            block_out[number, :, part] = blocks[number, :, part] - step

    @pl.when(core == 0)
    def first():
        for number in range(6):
            source, other = (attn, attn_other) if number < 4 else (pair, pair_other)
            index = (flipped(line, number % 4), 0)
            update(number, 0, (source, index), (other, index))

    @pl.when(core == 1)
    def second():
        for number in range(6):
            block = number + 2
            index = (flipped(line, block % 4), block // 4)
            update(number, 1, (pair, index), (pair_other, index))


def update_blocks(attn, attn_other, pair, pair_other, blocks, left_stat, right_stat, scales):
    turned = [jnp.transpose(value, (1, 0, 2)) for value in (blocks, left_stat, right_stat)]
    shape = jax.ShapeDtypeStruct(turned[0].shape, wide)
    outs = pl.pallas_call(
        last_kernel,
        out_shape=(shape,) * 4,
        in_specs=[on_chip()] * 7 + [pl.BlockSpec(memory_space=pltpu.SMEM)],
        out_specs=(on_chip(),) * 4,
        compiler_params=params(8),
        cost_estimate=cost(0, 32 * shape.size),
    )(attn, attn_other, pair, pair_other, *turned, scales)
    return [jnp.transpose(value, (1, 0, 2)) for value in outs]


def head_masks():
    lane = lax.broadcasted_iota(jnp.int32, (1, 2 * HEAD_DIM), 1)
    return [(lane < HEAD_DIM).astype(wide).astype(low), (lane >= HEAD_DIM).astype(wide).astype(low)]


def head_shares(query, key, same):
    scores = dot(query, key, 1, 1) * HEAD_DIM ** (-0.5)
    scores = jnp.where(same, scores, -1e30)
    raised = jnp.exp(scores - jnp.max(scores, axis=-1, keepdims=True))
    return raised / jnp.sum(raised, axis=-1, keepdims=True)


def attend_kernel(
    buffer, one, two, three, four, seg_column, seg_row, made_ref, sides_ref, answer_ref, weights
):
    for block in range(4):
        place_block((one, two, three, four), block, weights.at[block])
    same = seg_column[...] == seg_row[...]
    for kind in range(3):
        made_ref[kind] = dot(buffer[...], weights[kind]).astype(low)
    width = 2 * HEAD_DIM
    for pair in range(buffer.shape[1] // width):
        part = slice(pair * width, (pair + 1) * width)
        query, key, value = (made_ref[kind, :, part] for kind in range(3))
        context = None
        for mask in head_masks():
            shares = head_shares(query, key * mask, same).astype(low)
            term = dot(shares, value * mask)
            context = term if context is None else context + term
        sides_ref[1, :, part] = context.astype(low)
    sides_ref[0] = buffer[...]
    answer_ref[...] = dot(sides_ref[1], weights[3]).astype(low)


def attend(buffer, parts, segment):
    shape = jax.ShapeDtypeStruct(buffer.shape, low)
    rows, width = buffer.shape
    return pl.pallas_call(
        attend_kernel,
        out_shape=(
            jax.ShapeDtypeStruct((3,) + buffer.shape, low),
            jax.ShapeDtypeStruct((2,) + buffer.shape, low),
            shape,
            jax.ShapeDtypeStruct((4, width, width), low),
        ),
        in_specs=[on_chip()] * 7,
        out_specs=(on_chip(),) * 4,
        compiler_params=params(14),
        cost_estimate=cost(12 * rows * width * width, 12 * width * width),
    )(buffer, *parts, segment[:, None], segment[None, :])


def attend_back_kernel(
    sides,
    weights,
    seg_column,
    seg_row,
    made,
    grad_answer,
    theirs_ref,
    grads_ref,
    grad_buffer_ref,
    grad_context_ref,
):
    same = seg_column[...] == seg_row[...]
    core = lax.axis_index("own")
    grad_context_ref[...] = dot(grad_answer[...], weights[3], 1, 1).astype(low)
    grads_ref[3] = grad_answer[...]
    width = 2 * HEAD_DIM
    for pair in range(sides.shape[2] // width):
        part = slice(pair * width, (pair + 1) * width)
        query, key, value = (made[kind, :, part] for kind in range(3))
        above = grad_context_ref[:, part]
        sums = [None] * 3
        for mask in head_masks():
            key_head = key * mask
            shares = head_shares(query, key_head, same)
            grad_shares = dot(above, value * mask, 1, 1)
            inner = jnp.sum(shares * grad_shares, axis=-1, keepdims=True)
            grad_scores = (shares * (grad_shares - inner)).astype(low)
            terms = (
                dot(grad_scores, key_head),
                dot(grad_scores, query * mask, 0, 0),
                dot(shares.astype(low), above * mask, 0, 0),
            )
            sums = [
                term if total is None else total + term for term, total in zip(terms, sums)
            ]
        for kind, factor in enumerate((HEAD_DIM ** (-0.5), HEAD_DIM ** (-0.5), 1.0)):
            grads_ref[kind, :, part] = (sums[kind] * factor).astype(low)
    columns = theirs_ref.shape[2]
    part = pl.ds(pl.multiple_of((1 - core) * columns, columns), columns)
    for kind in range(4):
        theirs_ref[kind] = dot(sides[kind // 3], grads_ref[kind, :, part], 0, 0).astype(low)
    total = dot(grads_ref[0], weights[0], 1, 1)
    total = total + dot(grads_ref[1], weights[1], 1, 1)
    total = total + dot(grads_ref[2], weights[2], 1, 1)
    grad_buffer_ref[...] = total.astype(low)


def attend_back(sides, weights, segment, made, grad_answer):
    rows, width = grad_answer.shape
    return pl.pallas_call(
        attend_back_kernel,
        out_shape=(
            jax.ShapeDtypeStruct((4, width, width // 2), low),
            jax.ShapeDtypeStruct((4, rows, width), low),
            jax.ShapeDtypeStruct((rows, width), low),
        ),
        in_specs=[on_chip()] * 6,
        out_specs=(on_chip(),) * 3,
        scratch_shapes=[pltpu.VMEM((rows, width), low)],
        compiler_params=params(14),
        cost_estimate=cost(20 * rows * width * width, 16 * width * width),
    )(sides, weights, segment[:, None], segment[None, :], made, grad_answer)


def normal_parts(values):
    center = values - jnp.mean(values, axis=-1, keepdims=True)
    spread = jnp.mean(center * center, axis=-1, keepdims=True)
    return center, lax.rsqrt(spread + norm_eps)


def forward_kernel(
    tokens,
    placing,
    returned,
    gates,
    vectors,
    one,
    two,
    three,
    four,
    hidden_ref,
    second_ref,
    active_ref,
    slope_ref,
    w_up,
):
    step = pl.program_id(0)
    place_block((one, two, three, four), step, w_up.at[step])

    @pl.when(step == 0)
    def prepare():
        values = tokens[...].astype(wide) + gates[:, 0:1] * dot(placing[...], returned[...])
        hidden_ref[...] = values
        center, inverse = normal_parts(values)
        second_ref[...] = (center * inverse * vectors[3:4] + vectors[4:5]).astype(low)

    before = dot(second_ref[...], w_up[step])
    share = 0.5 + 0.5 * lax.erf(before * (0.5**0.5))
    density = jnp.exp(before * before * -0.5) * (0.5 / math.pi) ** 0.5
    active_ref[step] = (before * share).astype(low)
    slope_ref[step] = (share + before * density).astype(low)


def token_forward(tokens, placing, returned, gates, vectors, parts):
    count, width = tokens.shape
    blocks = parts[0].shape[2]
    by_block = jax.ShapeDtypeStruct((blocks, count, width), low)
    fetched = (tokens, placing, returned, gates, vectors)
    return pl.pallas_call(
        forward_kernel,
        grid=(blocks,),
        out_shape=(
            jax.ShapeDtypeStruct((count, width), wide),
            jax.ShapeDtypeStruct((count, width), low),
            by_block,
            by_block,
            jax.ShapeDtypeStruct((blocks, width, width), low),
        ),
        in_specs=[whole(value) for value in fetched] + [on_chip()] * 4,
        out_specs=(on_chip(),) * 5,
        compiler_params=params(24),
        cost_estimate=cost(8 * blocks * count * width * width, 8 * blocks * width * width),
    )(*fetched, *parts)


def backward_kernel(
    above,
    hidden,
    active,
    slope,
    placing,
    returned,
    gates,
    vectors,
    w_up,
    one,
    two,
    three,
    four,
    mixed_ref,
    packed_ref,
    grad_hidden_ref,
    logit_ref,
    vector_ref,
    inner_ref,
    result,
    grad_second,
    w_down,
):
    step = pl.program_id(0)
    place_block((one, two, three, four), step, w_down)

    @pl.when(step == 0)
    def prepare():
        result[...] = hidden[...]
        grad_second[...] = jnp.zeros_like(grad_second)

    grad_active = dot(above[...], w_down[...], 1, 1)
    grad_inner = (grad_active * slope[step].astype(wide)).astype(low)
    inner_ref[step] = grad_inner
    result[...] += dot(active[step], w_down[...])
    grad_second[...] += dot(grad_inner, w_up[step], 1, 1)

    @pl.when(step == pl.num_programs(0) - 1)
    def finish():
        mixed_ref[...] = result[...].astype(low)
        center, inverse = normal_parts(hidden[...])
        scaled = center * inverse
        grads = grad_second[...]
        vector_ref[0:1] = jnp.sum(grads * scaled, axis=0, keepdims=True)
        vector_ref[1:2] = jnp.sum(grads, axis=0, keepdims=True)
        pulled = grads * vectors[3:4]
        pulled = (
            pulled
            - jnp.mean(pulled, axis=-1, keepdims=True)
            - scaled * jnp.mean(pulled * scaled, axis=-1, keepdims=True)
        )
        grad_hidden = above[...].astype(wide) + inverse * pulled
        grad_hidden_ref[...] = grad_hidden
        weighted = (grad_hidden * gates[:, 0:1]).astype(low)
        packed_ref[...] = dot(placing[...], weighted, 0, 0).astype(low)
        unpacked = dot(placing[...], returned[...])
        logit_ref[...] = gates[:, 1:2] * jnp.sum(grad_hidden * unpacked, axis=-1, keepdims=True)


def token_backward(above, hidden, active, slope, placing, returned, gates, vectors, w_up, parts):
    count, width = above.shape
    slots = placing.shape[1]
    blocks = w_up.shape[0]
    return pl.pallas_call(
        backward_kernel,
        grid=(blocks,),
        out_shape=(
            jax.ShapeDtypeStruct((count, width), low),
            jax.ShapeDtypeStruct((slots, width), low),
            jax.ShapeDtypeStruct((count, width), wide),
            jax.ShapeDtypeStruct((count, 1), wide),
            jax.ShapeDtypeStruct((2, width), wide),
            jax.ShapeDtypeStruct((blocks, count, width), low),
        ),
        in_specs=[whole(above)]
        + [on_chip()] * 3
        + [whole(value) for value in (placing, returned, gates, vectors)]
        + [on_chip()] * 5,
        out_specs=(on_chip(),) * 6,
        scratch_shapes=[
            pltpu.VMEM((count, width), wide),
            pltpu.VMEM((count, width), wide),
            pltpu.VMEM((width, width), low),
        ],
        compiler_params=params(26),
        cost_estimate=cost(8 * blocks * count * width * width, 8 * blocks * width * width),
    )(above, hidden, active, slope, placing, returned, gates, vectors, w_up, *parts)


def outer_kernel(left, right, theirs_ref):
    core = lax.axis_index("own")
    step = pl.program_id(0)
    columns = theirs_ref.shape[2]
    left_step = step if left.shape[0] > 1 else 0
    right_step = step if right.shape[0] > 1 else 0
    part = pl.ds(pl.multiple_of((1 - core) * columns, columns), columns)
    theirs_ref[step] = dot(left[left_step], right[right_step, :, part], 0, 0).astype(low)


def outer_theirs(left, right):
    count, width = left.shape[1:]
    blocks = max(left.shape[0], right.shape[0])
    return pl.pallas_call(
        outer_kernel,
        grid=(blocks,),
        out_shape=jax.ShapeDtypeStruct((blocks, width, width // 2), low),
        in_specs=[on_chip()] * 2,
        out_specs=on_chip(),
        compiler_params=params(8),
        cost_estimate=cost(blocks * count * width * width, 3 * blocks * width * width),
    )(left, right)


def column(values):
    return values[:, None]


def pack_kernel(
    tokens, chosen, packing, vectors, placing_ref, packed_ref, gates_ref
):
    count = tokens.shape[0]
    capacity = packing.shape[0]
    center, inverse = normal_parts(tokens[...].astype(wide))
    first = (center * inverse * vectors[0:1] + vectors[1:2]).astype(low)
    gate = jax.nn.sigmoid(jnp.sum(first.astype(wide) * vectors[2:3], axis=-1, keepdims=True))
    weighting = jnp.where(chosen[...] == 1, gate, 0.0)
    gates_ref[:, 0:1] = weighting
    gates_ref[:, 1:2] = weighting * (1.0 - gate)
    above = lax.broadcasted_iota(jnp.int32, (count, count), 0)
    below = lax.broadcasted_iota(jnp.int32, (count, count), 1)
    earlier = (below <= above).astype(wide).astype(low)
    flags = jnp.broadcast_to(chosen[...].astype(wide), (count, capacity))
    rank = dot(earlier, flags.astype(low))
    place_of = lax.broadcasted_iota(jnp.int32, (count, capacity), 1).astype(wide) + 1.0
    ranked = jnp.where(rank == place_of, flags, 0.0).astype(low)
    slots = lax.broadcasted_iota(jnp.int32, (capacity, capacity), 1)
    slot_of = (packing[...] == slots).astype(wide).astype(low)
    placing = dot(ranked, slot_of).astype(low)
    placing_ref[...] = placing
    packed_ref[...] = dot(placing, first, 0, 0).astype(low)


def pack_tokens(tokens, chosen, packing, vectors):
    count, width = tokens.shape
    capacity = packing.shape[0]
    return pl.pallas_call(
        pack_kernel,
        out_shape=(
            jax.ShapeDtypeStruct((count, capacity), low),
            jax.ShapeDtypeStruct((capacity, width), low),
            jax.ShapeDtypeStruct((count, 2), wide),
        ),
        in_specs=[on_chip()] * 4,
        out_specs=(on_chip(),) * 3,
        compiler_params=params(12),
        cost_estimate=cost(4 * count * capacity * width, 8 * count * width),
    )(tokens, column(chosen), column(packing), vectors)


def token_back_kernel(
    tokens, placing, grad_sent, grad_hidden, grad_logit, vectors, out_ref, vector_ref
):
    grad_first = dot(placing[...], grad_sent[...]) + grad_logit[...] * vectors[2:3]
    center, inverse = normal_parts(tokens[...].astype(wide))
    scaled = center * inverse
    vector_ref[0:1] = jnp.sum(grad_first * scaled, axis=0, keepdims=True)
    vector_ref[1:2] = jnp.sum(grad_first, axis=0, keepdims=True)
    first = (scaled * vectors[0:1] + vectors[1:2]).astype(low).astype(wide)
    vector_ref[2:3] = jnp.sum(grad_logit[...] * first, axis=0, keepdims=True)
    pulled = grad_first * vectors[0:1]
    pulled = (
        pulled
        - jnp.mean(pulled, axis=-1, keepdims=True)
        - scaled * jnp.mean(pulled * scaled, axis=-1, keepdims=True)
    )
    out_ref[...] = (grad_hidden[...] + inverse * pulled).astype(low)


def token_back(tokens, placing, grad_sent, grad_hidden, grad_logit, vectors):
    count, width = tokens.shape
    return pl.pallas_call(
        token_back_kernel,
        out_shape=(
            jax.ShapeDtypeStruct((count, width), low),
            jax.ShapeDtypeStruct((3, width), wide),
        ),
        grid=(1,),
        in_specs=[
            whole(value) for value in (tokens, placing, grad_sent, grad_hidden, grad_logit, vectors)
        ],
        out_specs=(on_chip(),) * 2,
        compiler_params=params(22),
        cost_estimate=cost(2 * count * width * placing.shape[1], 12 * count * width),
    )(tokens, placing, grad_sent, grad_hidden, grad_logit, vectors)


def all_sum(value, flips):
    for flip in flips:
        value = value + send(value, [(i, i ^ flip) for i in range(32)])
    return value


def exchange(value, n_data):
    capacity, width = value.shape
    moved = lax.all_to_all(
        value.reshape(n_data, capacity // n_data, width), "dp", split_axis=0, concat_axis=0, tiled=True
    )
    return moved.reshape(capacity, width)


def block_shards(
    tokens,
    cotangent,
    selected,
    packing,
    segments,
    blocks,
    left_stat,
    right_stat,
    left_root,
    right_root,
    vectors,
    moment,
):
    model_width = tokens.shape[2]
    token_count = tokens.shape[0] * tokens.shape[1]
    n_data = lax.axis_size("dp")
    capacity = packing.shape[1]
    line, place, core = here()
    own_tokens = tokens.reshape(token_count, model_width)
    above = cotangent.reshape(token_count, model_width)
    segment = segments[0]

    every = columns_by_core(jnp.transpose(blocks, (1, 0, 2)).astype(low))
    placing, packed, gates = pack_tokens(
        own_tokens, selected.reshape(token_count), packing[0], vectors
    )
    buffer = exchange(packed, n_data)
    attn_two = send(every[:4], line_pairs(2))
    ffn_two = jnp.stack([every[4:], send(after(every[4:], attn_two), line_pairs(2))])
    line_attn = after(gather_far(jnp.stack([every[:4], attn_two])), packed, ffn_two)
    near_attn = send(line_attn, plane_pairs(0))
    every_root = roots_by_core(after(left_root, ffn_two), right_root)
    first_attn = after(jnp.stack([line_attn, near_attn]), every_root, buffer)
    far_attn = send(first_attn, plane_pairs(1))
    line_ffn = gather_far(ffn_two)
    near_ffn = send(line_ffn, plane_pairs(0))
    w_parts = with_other(first_attn, far_attn)
    made, sides, answer, w_attn = attend(buffer, w_parts, segment)
    root_parts = roots_line(after(every_root, line_ffn, buffer))
    first_up = jnp.stack([line_ffn[:, :4], near_ffn[:, :4]])
    far_up = send(first_up, plane_pairs(1))
    left_line, right_line = (jnp.stack([part[:, kind] for part in root_parts]) for kind in range(2))
    first_down = after(jnp.stack([line_ffn[:, 4:], near_ffn[:, 4:]]), far_up)
    far_down = send(first_down, plane_pairs(1))
    up_parts = with_other(first_up, far_up)
    returned = exchange(answer, n_data)

    hidden, second_low, active, slope, w_up = token_forward(
        own_tokens, placing, returned, gates, vectors, up_parts
    )
    down_theirs = outer_theirs(after(active, far_down, *root_parts[1:]), above[None])
    down_parts = with_other(first_down, far_down)
    down_got = send(down_theirs, swap_pairs())
    down_give, *down_kept = sum_start(lambda step: step, active, above[None], down_got)
    down_got = send(down_give, plane_pairs(0))
    mixed, grad_packed, grad_hidden, grad_logit, vector_two, grad_inner = token_backward(
        above,
        hidden,
        active,
        slope,
        placing,
        returned,
        gates,
        vectors,
        after(w_up, down_give),
        down_parts,
    )
    grad_answer = exchange(grad_packed, n_data)
    up_theirs = outer_theirs(after(second_low, down_got)[None], grad_inner)
    up_got = send(up_theirs, swap_pairs())
    up_give, *up_kept = sum_start(lambda step: 0, second_low[None], grad_inner, up_got)
    up_got = send(after(up_give, grad_answer), plane_pairs(0))

    attn_theirs, grads, grad_buffer = attend_back(
        sides, w_attn, segment, made, after(grad_answer, up_give)
    )
    grad_sent = exchange(after(grad_buffer, up_got), n_data)
    attn_got = send(after(attn_theirs, up_got), swap_pairs())
    attn_give, *attn_kept = sum_start(lambda step: step // 3, sides, grads, attn_got)

    up_kept, up_give = add_first(up_got, *up_kept)
    down_kept, down_give = add_first(down_got, *down_kept)
    pair_got = send(jnp.stack([up_give, down_give]), plane_pairs(1))
    attn_got = send(attn_give, plane_pairs(0))
    pair_kept = jnp.stack([up_kept, down_kept]) + after(pair_got, attn_give).astype(wide)
    pair_own, pair_two, pair_give = cut_line(pair_kept)

    near_right = send(after(right_line, pair_got), plane_pairs(0))
    pair_got = send(after(pair_give, attn_got, grad_sent), line_pairs(1))
    attn_kept, attn_give = add_first(attn_got, *attn_kept)
    attn_got = send(attn_give, plane_pairs(1))
    pair_own, pair_give = add_line(pair_own, pair_two, pair_got)
    first_right = jnp.stack([right_line, near_right])
    far_right = send(after(first_right, pair_got), plane_pairs(1))
    roots = (left_line, send(left_line, swap_pairs()), first_right, far_right)
    grad_tokens, vector_one = token_back(
        own_tokens, placing, grad_sent, grad_hidden, grad_logit, vectors
    )

    pair_got = send(after(pair_give, attn_got, vector_one, near_right), line_pairs(2))
    attn_own, attn_two, attn_give = cut_line((attn_kept + attn_got.astype(wide))[None])
    attn_got = send(attn_give, line_pairs(1))
    pair_own = (pair_own + pair_got.astype(wide)).astype(low)
    attn_own, attn_give = add_line(attn_own, attn_two, attn_got)

    pair_near = send(after(pair_own, attn_give, far_right), plane_pairs(0))
    attn_got = send(attn_give, line_pairs(2))
    attn_own = (attn_own + attn_got.astype(wide)).astype(low)
    pair_first = jnp.stack([pair_own, pair_near])

    pair_far = send(after(pair_first, attn_own), plane_pairs(1))
    attn_near = send(attn_own, plane_pairs(0))
    pair_rows = return_chunks(pair_own)
    pair_mine = jnp.concatenate([pair_first, pair_far])
    attn_first = jnp.stack([attn_own, attn_near])

    pair_theirs = send(after(pair_mine, attn_first, *pair_rows[1:]), swap_pairs())
    attn_far = send(attn_first, plane_pairs(1))
    attn_rows = return_chunks(attn_own)
    attn_mine = jnp.concatenate([attn_first, attn_far])

    pair_made, pair_square = step_chunks(
        pair_mine, after(pair_theirs, attn_mine, *attn_rows[1:]), roots, 1
    )
    attn_theirs = send(attn_mine, swap_pairs())
    attn_made, attn_square = step_chunks(
        attn_mine, after(attn_theirs, pair_made), roots, 0
    )
    pair = return_chunks(pair_made)
    attn = return_chunks(attn_made)
    squares = jnp.concatenate([jnp.sum(attn_square, axis=2), jnp.sum(pair_square, axis=2)])
    lane = lax.broadcasted_iota(jnp.int32, (1, model_width), 1)
    square_row = sum(
        jnp.where(lane == 4 * chunk + line, squares[chunk], 0.0) for chunk in range(3)
    )
    sums = all_sum(jnp.concatenate([vector_one, vector_two, square_row]), (1, 2, 4, 8))
    sums = all_sum(after(sums, *pair[1:], *attn[1:]), (16,))
    pair = joined(pair_rows, pair)
    pair_other = send(pair, swap_pairs())
    attn = joined(attn_rows, attn)
    attn_other = send(attn, [(i, i ^ 1) for i in range(1, 32, 2)])
    vector_grad = sums[:5]
    size = model_width * model_width
    scales = block_rate * lax.rsqrt(sums[5, :12] / size + norm_eps)
    grad_own, left_new, right_new, new_blocks = update_blocks(
        attn, attn_other, pair, pair_other, blocks, left_stat, right_stat, scales
    )
    moment_new = 0.5 * moment + 0.5 * vector_grad
    row_squares = jnp.mean(moment_new * moment_new, axis=1, keepdims=True)
    vector_new = vectors - vector_rate * moment_new * lax.rsqrt(row_squares + norm_eps)
    return (
        mixed.reshape(tokens.shape),
        grad_tokens.reshape(tokens.shape),
        grad_own,
        left_new,
        right_new,
        new_blocks,
        vector_grad,
        moment_new,
        vector_new,
    )


def shards(
    tokens,
    cotangent,
    selected,
    packing,
    segments,
    blocks,
    left_stat,
    right_stat,
    left_root,
    right_root,
    vectors,
    moment,
):
    model_width = tokens.shape[2]
    token_count = tokens.shape[0] * tokens.shape[1]
    n_data = lax.axis_size("dp")
    n_owner = lax.axis_size("own")
    shard_rows = blocks.shape[0]
    own_blocks = blocks.shape[1]
    up_blocks = (own_blocks * n_owner - 4) // 2
    capacity = packing.shape[1]
    per_peer = capacity // n_data
    head_count = model_width // HEAD_DIM
    score_scale = HEAD_DIM ** (-0.5)
    flat_weights = blocks.astype(jnp.bfloat16).reshape(1, shard_rows * own_blocks * model_width)
    gathered = lax.all_gather(flat_weights, ("dp", "own"), axis=0, tiled=True)
    gathered = gathered.reshape(n_data, n_owner, shard_rows, own_blocks, model_width)

    def matrix(number):
        return gathered[:, number // own_blocks, :, number % own_blocks, :].reshape(
            model_width, model_width
        )

    w_query = matrix(0)
    w_key = matrix(1)
    w_value = matrix(2)
    w_out = matrix(3)
    w_up = jnp.concatenate([matrix(4 + position) for position in range(up_blocks)], axis=1)
    w_down = jnp.concatenate(
        [matrix(4 + up_blocks + position) for position in range(up_blocks)], axis=0
    )
    inputs = tokens.reshape(token_count, model_width).astype(jnp.float32)
    chosen = selected.reshape(token_count)
    normed_one, norm_one_back = jax.vjp(layer_norm, inputs, vectors[0], vectors[1])
    first_low = normed_one.astype(jnp.bfloat16)
    first_wide = first_low.astype(jnp.float32)
    gate_values = jax.nn.sigmoid(jnp.dot(first_wide, vectors[2], precision=highest))
    before = jnp.cumsum(chosen) - 1
    slot_index = jnp.where(chosen == 1, packing[0][jnp.clip(before, 0, capacity - 1)], -1)
    placing = (slot_index[None, :] == jnp.arange(capacity, dtype=jnp.int32)[:, None]).astype(
        jnp.bfloat16
    )
    packed = jnp.dot(placing, first_low, preferred_element_type=jnp.float32).astype(jnp.bfloat16)
    buffer = lax.all_to_all(
        packed.reshape(n_data, per_peer, model_width), "dp", split_axis=0, concat_axis=0, tiled=True
    )
    buffer = buffer.reshape(capacity, model_width)

    def project(matrix_in):
        made = jnp.dot(buffer, matrix_in, preferred_element_type=jnp.float32).astype(jnp.bfloat16)
        return made.reshape(capacity, head_count, HEAD_DIM)

    query_rows = project(w_query)
    key_rows = project(w_key)
    value_rows = project(w_value)
    segment = segments[0]
    block_rows = math.gcd(capacity, 512)
    starts = jnp.arange(capacity // block_rows, dtype=jnp.int32) * block_rows

    def masked_scores():
        scores = (
            jnp.einsum("qhd,khd->hqk", query_rows, key_rows, preferred_element_type=jnp.float32)
            * score_scale
        )
        same_segment = segment[:, None] == segment[None, :]
        return (jnp.where(same_segment[None, :, :], scores, -1e30), query_rows)

    def forward_block(first_row):
        scores, unused_block = masked_scores()
        largest = jnp.max(scores, axis=-1, keepdims=True)
        raised = jnp.exp(scores - largest)
        row_total = jnp.sum(raised, axis=-1, keepdims=True)
        shares = (raised / row_total).astype(jnp.bfloat16)
        context_part = jnp.einsum(
            "hqk,khd->qhd", shares, value_rows, preferred_element_type=jnp.float32
        )
        return (context_part.astype(jnp.bfloat16), largest[..., 0] + jnp.log(row_total[..., 0]))

    context_blocks, lse_blocks = lax.map(forward_block, starts)
    context = context_blocks.reshape(capacity, model_width)
    answer = jnp.dot(context, w_out, preferred_element_type=jnp.float32).astype(jnp.bfloat16)
    returned = lax.all_to_all(
        answer.reshape(n_data, per_peer, model_width), "dp", split_axis=0, concat_axis=0, tiled=True
    )
    returned = returned.reshape(capacity, model_width)
    unpacked = jnp.einsum("mt,md->td", placing, returned, preferred_element_type=jnp.float32)
    weighting = jnp.where(chosen == 1, gate_values, 0.0)
    hidden = inputs + weighting[:, None] * unpacked
    normed_two, norm_two_back = jax.vjp(layer_norm, hidden, vectors[3], vectors[4])
    second_low = normed_two.astype(jnp.bfloat16)
    pre_active = jnp.dot(second_low, w_up, preferred_element_type=jnp.float32)
    active_wide, gelu_back = jax.vjp(gelu_exact, pre_active)
    active = active_wide.astype(jnp.bfloat16)
    result = hidden + jnp.dot(active, w_down, preferred_element_type=jnp.float32)
    mixed = result.astype(jnp.bfloat16).reshape(tokens.shape)
    upstream = cotangent.reshape(token_count, model_width)
    grad_down = jnp.einsum("tf,td->fd", active, upstream, preferred_element_type=jnp.float32)
    grad_active = jnp.einsum("td,fd->tf", upstream, w_down, preferred_element_type=jnp.float32)
    grad_inner = gelu_back(grad_active)[0].astype(jnp.bfloat16)
    grad_up = jnp.einsum("td,tf->df", second_low, grad_inner, preferred_element_type=jnp.float32)
    grad_second = jnp.einsum("tf,df->td", grad_inner, w_up, preferred_element_type=jnp.float32)
    grad_hidden_part, grad_gain_two, grad_bias_two = norm_two_back(grad_second)
    grad_hidden = upstream.astype(jnp.float32) + grad_hidden_part
    grad_token_back = (grad_hidden * weighting[:, None]).astype(jnp.bfloat16)
    grad_packed = jnp.dot(placing, grad_token_back, preferred_element_type=jnp.float32).astype(
        jnp.bfloat16
    )
    router_pull = jnp.where(chosen == 1, jnp.sum(grad_hidden * unpacked, axis=-1), 0.0)
    grad_logit = router_pull * gate_values * (1.0 - gate_values)
    grad_answer = lax.all_to_all(
        grad_packed.reshape(n_data, per_peer, model_width),
        "dp",
        split_axis=0,
        concat_axis=0,
        tiled=True,
    )
    grad_answer = grad_answer.reshape(capacity, model_width)
    grad_out = jnp.einsum("md,me->de", context, grad_answer, preferred_element_type=jnp.float32)
    grad_context = jnp.einsum("me,de->md", grad_answer, w_out, preferred_element_type=jnp.float32)
    grad_context = grad_context.astype(jnp.bfloat16).reshape(capacity, head_count, HEAD_DIM)

    def backward_block(running, item_pair):
        first_row, lse_block = item_pair
        scores, query_block = masked_scores()
        shares_wide = jnp.exp(scores - lse_block[..., None])
        grad_shares = jnp.einsum(
            "qhd,khd->hqk", grad_context, value_rows, preferred_element_type=jnp.float32
        )
        inner_sum = jnp.sum(shares_wide * grad_shares, axis=-1, keepdims=True)
        grad_scores = (shares_wide * (grad_shares - inner_sum)).astype(jnp.bfloat16)
        grad_query_block = (
            jnp.einsum("hqk,khd->qhd", grad_scores, key_rows, preferred_element_type=jnp.float32)
            * score_scale
        )
        key_sum = (
            running[0]
            + jnp.einsum(
                "hqk,qhd->khd", grad_scores, query_block, preferred_element_type=jnp.float32
            )
            * score_scale
        )
        value_sum = running[1] + jnp.einsum(
            "hqk,qhd->khd",
            shares_wide.astype(jnp.bfloat16),
            grad_context,
            preferred_element_type=jnp.float32,
        )
        return ((key_sum, value_sum), grad_query_block)

    zeros_init = jnp.zeros((capacity, head_count, HEAD_DIM), jnp.float32)
    (key_total, value_total), query_grads = lax.scan(
        backward_block, (zeros_init, zeros_init), (starts, lse_blocks)
    )
    grad_query = query_grads.reshape(capacity, model_width).astype(jnp.bfloat16)
    grad_key = key_total.reshape(capacity, model_width).astype(jnp.bfloat16)
    grad_value = value_total.reshape(capacity, model_width).astype(jnp.bfloat16)
    grad_w_query = jnp.einsum("md,me->de", buffer, grad_query, preferred_element_type=jnp.float32)
    grad_w_key = jnp.einsum("md,me->de", buffer, grad_key, preferred_element_type=jnp.float32)
    grad_w_value = jnp.einsum("md,me->de", buffer, grad_value, preferred_element_type=jnp.float32)
    grad_buffer = jnp.einsum("me,de->md", grad_query, w_query, preferred_element_type=jnp.float32)
    grad_buffer = grad_buffer + jnp.einsum(
        "me,de->md", grad_key, w_key, preferred_element_type=jnp.float32
    )
    grad_buffer = grad_buffer + jnp.einsum(
        "me,de->md", grad_value, w_value, preferred_element_type=jnp.float32
    )
    grad_buffer = grad_buffer.astype(jnp.bfloat16)
    grad_sent = lax.all_to_all(
        grad_buffer.reshape(n_data, per_peer, model_width),
        "dp",
        split_axis=0,
        concat_axis=0,
        tiled=True,
    )
    grad_sent = grad_sent.reshape(capacity, model_width)
    grad_first = jnp.einsum("mt,md->td", placing, grad_sent, preferred_element_type=jnp.float32)
    grad_first = grad_first + grad_logit[:, None] * vectors[2][None, :]
    grad_router = jnp.sum(grad_logit[:, None] * first_wide, axis=0)
    grad_input_part, grad_gain_one, grad_bias_one = norm_one_back(grad_first)
    grad_tokens = (grad_hidden + grad_input_part).astype(jnp.bfloat16).reshape(tokens.shape)
    pieces = [grad_w_query, grad_w_key, grad_w_value, grad_out]
    pieces = pieces + [
        grad_up[:, position * model_width : (position + 1) * model_width]
        for position in range(up_blocks)
    ]
    pieces = pieces + [
        grad_down[position * model_width : (position + 1) * model_width, :]
        for position in range(up_blocks)
    ]
    local_terms = jnp.stack(pieces, axis=1)
    vector_terms = jnp.stack(
        [grad_gain_one, grad_bias_one, grad_router, grad_gain_two, grad_bias_two]
    )
    partial_value = lax.psum_scatter(local_terms, "dp", scatter_dimension=0, tiled=True)
    grad_own = lax.psum_scatter(
        partial_value.astype(jnp.bfloat16), "own", scatter_dimension=1, tiled=True
    ).astype(jnp.float32)
    vector_grad = lax.psum(vector_terms, ("dp", "own"))
    full_grad = lax.all_gather(grad_own.astype(jnp.bfloat16), "dp", axis=0, tiled=True).astype(
        grad_own.dtype
    )
    row_start = lax.axis_index("dp") * shard_rows
    left_new = 0.5 * left_stat + 0.5 * jnp.einsum(
        "rbk,nbk->rbn", grad_own, full_grad, precision=highest
    )
    column_part = lax.dynamic_slice_in_dim(full_grad, row_start, shard_rows, 2)
    right_new = 0.5 * right_stat + 0.5 * jnp.einsum(
        "nbr,nbk->rbk", column_part, full_grad, precision=highest
    )
    lefted = jnp.einsum("rbn,nbk->rbk", left_root, full_grad, precision=highest)
    precond = jnp.zeros_like(grad_own) + jnp.einsum(
        "rbn,nbk->rbk",
        lefted,
        lax.all_gather(right_root.astype(jnp.bfloat16), "dp", axis=0, tiled=True).astype(
            jnp.float32
        ),
        precision=highest,
    )
    square_sums = lax.psum(jnp.sum(precond * precond, axis=(0, 2)), "dp")
    step_scale = lax.rsqrt(square_sums / (model_width * model_width) + norm_eps)
    new_blocks = blocks - block_rate * precond * step_scale[None, :, None]
    moment_new = 0.5 * moment + 0.5 * vector_grad
    row_squares = jnp.mean(moment_new * moment_new, axis=1, keepdims=True)
    vector_new = vectors - vector_rate * moment_new * lax.rsqrt(row_squares + norm_eps)
    return (
        mixed,
        grad_tokens,
        grad_own,
        left_new,
        right_new,
        new_blocks,
        vector_grad,
        moment_new,
        vector_new,
    )


def solution(mesh):
    placed = (
        P(("dp", "own"), None, None),
        P(("dp", "own"), None, None),
        P(("dp", "own"), None),
        P(("dp", "own"), None),
        P(("dp", "own"), None),
        P("dp", "own", None),
        P("dp", "own", None),
        P("dp", "own", None),
        P("dp", "own", None),
        P("dp", "own", None),
        P(),
        P(),
    )
    small = mesh.shape["dp"] == 16 and mesh.shape["own"] == 2
    return jax.shard_map(
        block_shards if small else shards,
        mesh=mesh,
        in_specs=placed,
        out_specs=(
            P(("dp", "own"), None, None),
            P(("dp", "own"), None, None),
            P("dp", "own", None),
            P("dp", "own", None),
            P("dp", "own", None),
            P("dp", "own", None),
            P(),
            P(),
            P(),
        ),
        check_vma=False,
    )
```

```python
import functools
import math

import jax
import jax.numpy as jnp
from jax import lax
from jax.experimental import pallas as pl
from jax.experimental.pallas import tpu as pltpu
from jax.sharding import PartitionSpec as P

HEAD_DIM = 64


norm_eps = 1e-06
block_rate = 0.03
vector_rate = 0.04
highest = lax.Precision.HIGHEST


def layer_norm(values, norm_gain, norm_bias):
    center = values - jnp.mean(values, axis=-1, keepdims=True)
    spread = jnp.mean(center * center, axis=-1, keepdims=True)
    return center * lax.rsqrt(spread + norm_eps) * norm_gain + norm_bias


def gelu_exact(values):
    return jax.nn.gelu(values, approximate=False)


BOTH = ("dp", "own")
low = jnp.bfloat16
wide = jnp.float32
MIB = 2**20


def swap_pairs():
    return [(i, i ^ 1) for i in range(32)]


def plane_pairs(step):
    pairs = []
    for i in range(32):
        place, core = i // 2, i % 2
        flip = (1, 2)[step ^ core]
        pairs.append((i, (place ^ flip) * 2 + core))
    return pairs


def line_pairs(flip):
    return [(i, i ^ (8 * flip)) for i in range(32)]


def send(value, pairs):
    return lax.ppermute(value, BOTH, pairs)


def after(value, *others):
    return lax.optimization_barrier((value,) + others)[0]


def pick(value, index, axis):
    return lax.dynamic_index_in_dim(value, index, axis, keepdims=False)


def first_core():
    return lax.axis_index("own") == 0


def halves(value):
    middle = value.shape[-1] // 2
    lower, upper = value[..., :middle], value[..., middle:]
    return jnp.where(first_core(), lower, upper), jnp.where(first_core(), upper, lower)


def in_core_order(mine, theirs, axis):
    return jnp.where(
        first_core(),
        jnp.concatenate([mine, theirs], axis=axis),
        jnp.concatenate([theirs, mine], axis=axis),
    )


LINE_FLIPS = (0, 2, 1, 3)


def flipped(index, flip):
    return jnp.bitwise_xor(index, flip)


def spots(place, half):
    first, second = half + 1, 2 - half
    return [
        place,
        flipped(place, first),
        flipped(place, second),
        flipped(place, 3),
    ]


def here():
    device = lax.axis_index("dp")
    return device // 4, device % 4, lax.axis_index("own")


def dot(left, right, left_axis=1, right_axis=0):
    return lax.dot_general(
        left, right, (((left_axis,), (right_axis,)), ((), ())), preferred_element_type=wide
    )


def on_chip():
    return pl.BlockSpec(memory_space=pltpu.VMEM)


def whole(value):
    return pl.BlockSpec(value.shape, lambda *steps: (0,) * value.ndim)


def in_hbm():
    return pl.BlockSpec(memory_space=pltpu.HBM)


def fetch_scratch(values):
    return [pltpu.VMEM(value.shape, value.dtype) for value in values] + [
        pltpu.SemaphoreType.DMA((len(values),))
    ]


def fetch(sources, targets, sems):
    copies = [
        pltpu.make_async_copy(source, target, sems.at[number])
        for number, (source, target) in enumerate(zip(sources, targets))
    ]
    for copy in copies:
        copy.start()
    return copies


def finish(copies):
    for copy in copies:
        copy.wait()


def params(limit):
    return pltpu.CompilerParams(vmem_limit_bytes=limit * MIB)


def cost(flops, moved):
    return pl.CostEstimate(flops=flops, bytes_accessed=moved, transcendentals=0)


def place_block(parts, block, target):
    line, place, core = here()
    rows, columns = parts[0].shape[3:]
    for other in range(2):
        half = core if other == 0 else 1 - core
        column_slice = pl.ds(pl.multiple_of(half * columns, columns), columns)
        for number, spot in enumerate(spots(place, half)):
            for index, flip in enumerate(LINE_FLIPS):
                start = (flipped(line, flip) * 4 + spot) * rows
                row_slice = pl.ds(pl.multiple_of(start, rows), rows)
                piece = parts[2 * other + number // 2][number % 2, index, block]
                target[row_slice, column_slice] = piece


def columns_by_core(value):
    keep, give = halves(value)
    return in_core_order(keep, send(give, swap_pairs()), 0)


def gather_far(pair):
    return jnp.concatenate([pair, send(pair, line_pairs(1))])


def with_other(first, far):
    return [first, far, send(first, swap_pairs()), send(far, swap_pairs())]


def roots_by_core(left_root, right_root):
    both = [jnp.transpose(root, (1, 0, 2)).astype(low) for root in (left_root, right_root)]
    every = columns_by_core(jnp.stack(both, axis=1))
    return every.reshape((3, 4) + every.shape[1:])


def roots_given(every):
    line, place, core = here()
    return [pick(every, flipped(line, flip), 1) for flip in range(4)]


def sum_kernel(left_of, left, right, got, give_ref, kept_ref, passed_ref, total):
    line, place, core = here()
    step = pl.program_id(0)
    columns = got.shape[2]
    rows = kept_ref.shape[2]
    part = pl.ds(pl.multiple_of(core * columns, columns), columns)
    right_step = step if right.shape[0] > 1 else 0
    made = dot(left[left_of(step)], right[right_step, :, part], 0, 0)
    total[...] = made + got[step].astype(wide)
    own, first, second, both = spots(place, core)
    for row_line in range(4):

        def piece(spot):
            return total[pl.ds(pl.multiple_of((row_line * 4 + spot) * rows, rows), rows), :]

        give_ref[0, step, row_line] = piece(first).astype(low)
        give_ref[1, step, row_line] = piece(both).astype(low)
        kept_ref[step, row_line] = piece(own).astype(low)
        passed_ref[step, row_line] = piece(second).astype(low)


def sum_start(left_of, left, right, got):
    count, width = left.shape[1:]
    blocks, full, columns = got.shape
    shape = (blocks, 4, full // 16, columns)
    return pl.pallas_call(
        functools.partial(sum_kernel, left_of),
        grid=(blocks,),
        out_shape=(
            jax.ShapeDtypeStruct((2,) + shape, low),
            jax.ShapeDtypeStruct(shape, low),
            jax.ShapeDtypeStruct(shape, low),
        ),
        in_specs=[on_chip()] * 3,
        out_specs=(on_chip(),) * 3,
        scratch_shapes=[pltpu.VMEM((full, columns), wide)],
        compiler_params=params(12),
        cost_estimate=cost(blocks * count * width * width, 5 * blocks * width * width),
    )(left, right, got)


def add_first(got, kept, passed):
    kept = kept.astype(wide) + got[0].astype(wide)
    return kept, (passed.astype(wide) + got[1].astype(wide)).astype(low)


def cut_line(kept):
    line, place, core = here()
    given = jnp.stack([pick(kept, flipped(line, flip), 1) for flip in (1, 3)]).astype(low)
    return pick(kept, line, 1), pick(kept, flipped(line, 2), 1), given


def add_line(own, two, got):
    return own + got[0].astype(wide), (two + got[1].astype(wide)).astype(low)


def step_kernel(
    number,
    mine,
    theirs,
    left_mine_from,
    left_theirs_from,
    right_first_from,
    right_far_from,
    out_ref,
    square_ref,
    grad_ref,
    rows_ref,
    left_ref,
    right_ref,
    cross_ref,
    left_mine,
    left_theirs,
    right_first,
    right_far,
    sems,
):
    chunk = number + pl.program_id(0)
    copies = fetch(
        [
            left_mine_from.at[:, chunk],
            left_theirs_from.at[:, chunk],
            right_first_from.at[:, :, chunk],
            right_far_from.at[:, :, chunk],
        ],
        [left_mine, left_theirs, right_first, right_far],
        sems,
    )
    line, place, core = here()
    rows, columns = mine.shape[3:]

    def rows_of(row_line, spot):
        return pl.ds(pl.multiple_of((row_line * 4 + spot) * rows, rows), rows)

    def column_half(half):
        return pl.ds(pl.multiple_of(half * columns, columns), columns)

    for half, group in ((core, mine), (1 - core, theirs)):
        for number, spot in enumerate(spots(place, half)):
            for step in range(4):
                grad_ref[rows_of(step, spot), column_half(half)] = group[number, 0, step]
    finish(copies)
    for half, left in ((core, left_mine), (1 - core, left_theirs)):
        for flip in range(4):
            target = pl.ds(pl.multiple_of(flipped(line, flip) * rows, rows), rows)
            left_ref[target, column_half(half)] = left[flip]
    for number, spot in enumerate(spots(place, core)):
        source = right_far if number > 1 else right_first
        for flip in range(4):
            right_ref[rows_of(flipped(line, flip), spot), :] = source[number % 2, flip]
    for row_line in range(4):
        rows_ref[row_line * rows : (row_line + 1) * rows, :] = grad_ref[rows_of(row_line, place), :]
    left = dot(rows_ref[...], grad_ref[column_half(core), :], 1, 1)
    cross_ref[...] = dot(grad_ref[...], grad_ref[:, column_half(core)], 0, 0)
    lefted = dot(left_ref[...], grad_ref[...]).astype(low)
    stepped = dot(lefted, right_ref[...])
    square_ref[0] = jnp.sum(stepped * stepped, axis=0, keepdims=True)
    for row_line in range(4):
        part = slice(row_line * rows, (row_line + 1) * rows)
        out_ref[0, row_line, 0] = mine[0, 0, row_line]
        out_ref[0, row_line, 1] = left[part].astype(low)
        out_ref[0, row_line, 2] = cross_ref[rows_of(row_line, place), :].astype(low)
        out_ref[0, row_line, 3] = stepped[part].astype(low)


def step_chunks(mine, theirs, roots, number):
    chunks, lines, rows, columns = mine.shape[1:]
    full = rows * 16
    grad_spec = pl.BlockSpec((4, 1, lines, rows, columns), lambda step: (0, step, 0, 0, 0))
    return pl.pallas_call(
        functools.partial(step_kernel, number),
        grid=(chunks,),
        out_shape=(
            jax.ShapeDtypeStruct((chunks, lines, 4, rows, columns), low),
            jax.ShapeDtypeStruct((chunks, 1, columns), wide),
        ),
        in_specs=[grad_spec] * 2 + [in_hbm()] * 4,
        out_specs=(
            pl.BlockSpec((1, lines, 4, rows, columns), lambda step: (step, 0, 0, 0, 0)),
            pl.BlockSpec((1, 1, columns), lambda step: (step, 0, 0)),
        ),
        scratch_shapes=[
            pltpu.VMEM((full, columns * 2), low),
            pltpu.VMEM((lines * rows, columns * 2), low),
            pltpu.VMEM((lines * rows, columns * 2), low),
            pltpu.VMEM((full, columns), low),
            pltpu.VMEM((full, columns), wide),
            pltpu.VMEM((lines, rows, columns), low),
            pltpu.VMEM((lines, rows, columns), low),
            pltpu.VMEM((2, lines, rows, columns), low),
            pltpu.VMEM((2, lines, rows, columns), low),
            pltpu.SemaphoreType.DMA((4,)),
        ],
        compiler_params=params(15),
        cost_estimate=cost(3 * chunks * full**3, 16 * chunks * full * full),
    )(mine, theirs, *roots)


def return_chunks(made):
    line, place, core = here()
    parts = [pick(made, line, 1)]
    for flip in (1, 2, 3):
        parts.append(send(pick(made, flipped(line, flip), 1), line_pairs(flip)))
    return parts


def last_kernel(
    attn, attn_other, pair, pair_other, blocks, left_stat, right_stat, scales, *outs
):
    grad_out, left_out, right_out, block_out = outs
    line, place, core = here()
    columns = attn.shape[4]

    def update(number, which, mine, theirs):
        for (source, index), half in ((mine, which), (theirs, 1 - which)):
            part = slice(half * columns, (half + 1) * columns)
            pieces = [source[index + (kind,)].astype(wide) for kind in range(4)]
            grad_out[number, :, part] = pieces[0]
            left_out[number, :, part] = 0.5 * left_stat[number, :, part] + 0.5 * pieces[1]
            right_out[number, :, part] = 0.5 * right_stat[number, :, part] + 0.5 * pieces[2]
            step = pieces[3] * scales[6 * which + number]
            block_out[number, :, part] = blocks[number, :, part] - step

    @pl.when(core == 0)
    def first():
        for number in range(6):
            source, other = (attn, attn_other) if number < 4 else (pair, pair_other)
            index = (flipped(line, number % 4), 0)
            update(number, 0, (source, index), (other, index))

    @pl.when(core == 1)
    def second():
        for number in range(6):
            block = number + 2
            index = (flipped(line, block % 4), block // 4)
            update(number, 1, (pair, index), (pair_other, index))


def update_blocks(attn, attn_other, pair, pair_other, blocks, left_stat, right_stat, scales):
    turned = [jnp.transpose(value, (1, 0, 2)) for value in (blocks, left_stat, right_stat)]
    shape = jax.ShapeDtypeStruct(turned[0].shape, wide)
    outs = pl.pallas_call(
        last_kernel,
        out_shape=(shape,) * 4,
        in_specs=[on_chip()] * 7 + [pl.BlockSpec(memory_space=pltpu.SMEM)],
        out_specs=(on_chip(),) * 4,
        compiler_params=params(10),
        cost_estimate=cost(0, 32 * shape.size),
    )(attn, attn_other, pair, pair_other, *turned, scales)
    return [jnp.transpose(value, (1, 0, 2)) for value in outs]


def head_masks():
    lane = lax.broadcasted_iota(jnp.int32, (1, 2 * HEAD_DIM), 1)
    return [(lane < HEAD_DIM).astype(wide).astype(low), (lane >= HEAD_DIM).astype(wide).astype(low)]


def head_shares(query, key, same):
    scores = dot(query, key, 1, 1) * HEAD_DIM ** (-0.5)
    scores = jnp.where(same, scores, -1e30)
    raised = jnp.exp(scores - jnp.max(scores, axis=-1, keepdims=True))
    return raised / jnp.sum(raised, axis=-1, keepdims=True)


STORE_ROWS = 32768


def store_views(store, rows, width):
    weights = [store.at[pl.ds(block * width, width)] for block in range(4)]
    made = [store.at[pl.ds(4 * width + kind * rows, rows)] for kind in range(3)]
    sides = [store.at[pl.ds(4 * width + (3 + side) * rows, rows)] for side in range(2)]
    return weights, made, sides


def attend_kernel(
    buffer, one, two, three, four, seg_column, seg_row, answer_ref, store, weights, made, sides, sems
):
    rows, width = buffer.shape
    weights_out, made_out, sides_out = store_views(store, rows, width)
    for block in range(4):
        place_block((one, two, three, four), block, weights.at[block])
    copies = fetch([weights.at[block] for block in range(4)], weights_out, sems)
    same = seg_column[...] == seg_row[...]
    for kind in range(3):
        made[kind] = dot(buffer[...], weights[kind]).astype(low)
    copies += fetch([made.at[kind] for kind in range(3)], made_out, sems.at[pl.ds(4, 3)])
    pair_width = 2 * HEAD_DIM
    for pair in range(width // pair_width):
        part = slice(pair * pair_width, (pair + 1) * pair_width)
        query, key, value = (made[kind, :, part] for kind in range(3))
        context = None
        for mask in head_masks():
            shares = head_shares(query, key * mask, same).astype(low)
            term = dot(shares, value * mask)
            context = term if context is None else context + term
        sides[1, :, part] = context.astype(low)
    sides[0] = buffer[...]
    copies += fetch([sides.at[side] for side in range(2)], sides_out, sems.at[pl.ds(7, 2)])
    answer_ref[...] = dot(sides[1], weights[3]).astype(low)
    finish(copies)


def attend_scratch(rows, width):
    return [
        pltpu.VMEM((4, width, width), low),
        pltpu.VMEM((3, rows, width), low),
        pltpu.VMEM((2, rows, width), low),
        pltpu.SemaphoreType.DMA((9,)),
    ]


def attend(buffer, parts, segment):
    rows, width = buffer.shape
    return pl.pallas_call(
        attend_kernel,
        out_shape=(
            jax.ShapeDtypeStruct((rows, width), low),
            jax.ShapeDtypeStruct((STORE_ROWS, width), low),
        ),
        in_specs=[on_chip()] * 7,
        out_specs=(on_chip(), in_hbm()),
        scratch_shapes=attend_scratch(rows, width),
        compiler_params=params(20),
        cost_estimate=cost(12 * rows * width * width, 12 * width * width),
    )(buffer, *parts, segment[:, None], segment[None, :])


def attend_back_kernel(
    store,
    seg_column,
    seg_row,
    grad_answer,
    theirs_ref,
    grads_ref,
    grad_buffer_ref,
    sides,
    grad_context_ref,
    weights,
    made,
    sems,
):
    rows, width = grad_answer.shape
    weights_from, made_from, sides_from = store_views(store, rows, width)
    out_copy, *copies = fetch(
        [weights_from[3]] + made_from + sides_from + weights_from[:3],
        [weights.at[3]]
        + [made.at[kind] for kind in range(3)]
        + [sides.at[side] for side in range(2)]
        + [weights.at[block] for block in range(3)],
        sems,
    )
    same = seg_column[...] == seg_row[...]
    core = lax.axis_index("own")
    out_copy.wait()
    grad_context_ref[...] = dot(grad_answer[...], weights[3], 1, 1).astype(low)
    finish(copies[:3])
    grads_ref[3] = grad_answer[...]
    pair_width = 2 * HEAD_DIM
    for pair in range(width // pair_width):
        part = slice(pair * pair_width, (pair + 1) * pair_width)
        query, key, value = (made[kind, :, part] for kind in range(3))
        above = grad_context_ref[:, part]
        sums = [None] * 3
        for mask in head_masks():
            key_head = key * mask
            shares = head_shares(query, key_head, same)
            grad_shares = dot(above, value * mask, 1, 1)
            inner = jnp.sum(shares * grad_shares, axis=-1, keepdims=True)
            grad_scores = (shares * (grad_shares - inner)).astype(low)
            terms = (
                dot(grad_scores, key_head),
                dot(grad_scores, query * mask, 0, 0),
                dot(shares.astype(low), above * mask, 0, 0),
            )
            sums = [
                term if total is None else total + term for term, total in zip(terms, sums)
            ]
        for kind, factor in enumerate((HEAD_DIM ** (-0.5), HEAD_DIM ** (-0.5), 1.0)):
            grads_ref[kind, :, part] = (sums[kind] * factor).astype(low)
    finish(copies[3:5])
    columns = theirs_ref.shape[2]
    part = pl.ds(pl.multiple_of((1 - core) * columns, columns), columns)
    for kind in range(4):
        theirs_ref[kind] = dot(sides[kind // 3], grads_ref[kind, :, part], 0, 0).astype(low)
    finish(copies[5:])
    total = dot(grads_ref[0], weights[0], 1, 1)
    total = total + dot(grads_ref[1], weights[1], 1, 1)
    total = total + dot(grads_ref[2], weights[2], 1, 1)
    grad_buffer_ref[...] = total.astype(low)


def attend_back(store, segment, grad_answer):
    rows, width = grad_answer.shape
    weights, made, sides, sems = attend_scratch(rows, width)
    return pl.pallas_call(
        attend_back_kernel,
        out_shape=(
            jax.ShapeDtypeStruct((4, width, width // 2), low),
            jax.ShapeDtypeStruct((4, rows, width), low),
            jax.ShapeDtypeStruct((rows, width), low),
            jax.ShapeDtypeStruct((2, rows, width), low),
        ),
        in_specs=[in_hbm()] + [on_chip()] * 3,
        out_specs=(on_chip(),) * 4,
        scratch_shapes=[pltpu.VMEM((rows, width), low), weights, made, sems],
        compiler_params=params(18),
        cost_estimate=cost(20 * rows * width * width, 16 * width * width),
    )(store, segment[:, None], segment[None, :], grad_answer)


def normal_parts(values):
    center = values - jnp.mean(values, axis=-1, keepdims=True)
    spread = jnp.mean(center * center, axis=-1, keepdims=True)
    return center, lax.rsqrt(spread + norm_eps)


def forward_kernel(*refs):
    sources, parts = refs[:5], refs[5:9]
    hidden_ref, second_ref, active_ref, slope_ref, w_up = refs[9:14]
    fetched, sems = refs[14:19], refs[19]
    tokens, placing, returned, gates, vectors = fetched
    step = pl.program_id(0)

    @pl.when(step == 0)
    def prepare():
        finish(fetch(sources, fetched, sems))
        values = tokens[...].astype(wide) + gates[:, 0:1] * dot(placing[...], returned[...])
        hidden_ref[...] = values
        center, inverse = normal_parts(values)
        second_ref[...] = (center * inverse * vectors[3:4] + vectors[4:5]).astype(low)

    place_block(parts, step, w_up.at[step])
    before = dot(second_ref[...], w_up[step])
    share = 0.5 + 0.5 * lax.erf(before * (0.5**0.5))
    density = jnp.exp(before * before * -0.5) * (0.5 / math.pi) ** 0.5
    active_ref[step] = (before * share).astype(low)
    slope_ref[step] = (share + before * density).astype(low)


def token_forward(tokens, placing, returned, gates, vectors, parts):
    count, width = tokens.shape
    blocks = parts[0].shape[2] // 2
    by_block = jax.ShapeDtypeStruct((blocks, count, width), low)
    fetched = (tokens, placing, returned, gates, vectors)
    return pl.pallas_call(
        forward_kernel,
        grid=(blocks,),
        out_shape=(
            jax.ShapeDtypeStruct((count, width), wide),
            jax.ShapeDtypeStruct((count, width), low),
            by_block,
            by_block,
            jax.ShapeDtypeStruct((blocks, width, width), low),
        ),
        in_specs=[in_hbm()] * 5 + [on_chip()] * 4,
        out_specs=(on_chip(),) * 5,
        scratch_shapes=fetch_scratch(fetched),
        compiler_params=params(18),
        cost_estimate=cost(8 * blocks * count * width * width, 8 * blocks * width * width),
    )(*fetched, *parts)


def backward_kernel(*refs):
    sources, (hidden, active, slope, w_up), parts = refs[:5], refs[5:9], refs[9:13]
    mixed_ref, packed_ref, grad_hidden_ref, logit_ref, vector_ref, inner_ref = refs[13:19]
    result, grad_second, w_down = refs[19:22]
    fetched, sems = refs[22:27], refs[27]
    above, placing, returned, gates, vectors = fetched
    step = pl.program_id(0)
    place_block(parts, 4 + step, w_down)

    @pl.when(step == 0)
    def prepare():
        copies = fetch(sources, fetched, sems)
        result[...] = hidden[...]
        grad_second[...] = jnp.zeros_like(grad_second)
        finish(copies)

    grad_active = dot(above[...], w_down[...], 1, 1)
    grad_inner = (grad_active * slope[step].astype(wide)).astype(low)
    inner_ref[step] = grad_inner
    result[...] += dot(active[step], w_down[...])
    grad_second[...] += dot(grad_inner, w_up[step], 1, 1)

    @pl.when(step == pl.num_programs(0) - 1)
    def complete():
        mixed_ref[...] = result[...].astype(low)
        center, inverse = normal_parts(hidden[...])
        scaled = center * inverse
        grads = grad_second[...]
        vector_ref[0:1] = jnp.sum(grads * scaled, axis=0, keepdims=True)
        vector_ref[1:2] = jnp.sum(grads, axis=0, keepdims=True)
        pulled = grads * vectors[3:4]
        pulled = (
            pulled
            - jnp.mean(pulled, axis=-1, keepdims=True)
            - scaled * jnp.mean(pulled * scaled, axis=-1, keepdims=True)
        )
        grad_hidden = above[...].astype(wide) + inverse * pulled
        grad_hidden_ref[...] = grad_hidden
        weighted = (grad_hidden * gates[:, 0:1]).astype(low)
        packed_ref[...] = dot(placing[...], weighted, 0, 0).astype(low)
        unpacked = dot(placing[...], returned[...])
        logit_ref[...] = gates[:, 1:2] * jnp.sum(grad_hidden * unpacked, axis=-1, keepdims=True)


def token_backward(above, hidden, active, slope, placing, returned, gates, vectors, w_up, parts):
    count, width = above.shape
    slots = placing.shape[1]
    blocks = w_up.shape[0]
    fetched = (above, placing, returned, gates, vectors)
    return pl.pallas_call(
        backward_kernel,
        grid=(blocks,),
        out_shape=(
            jax.ShapeDtypeStruct((count, width), low),
            jax.ShapeDtypeStruct((slots, width), low),
            jax.ShapeDtypeStruct((count, width), wide),
            jax.ShapeDtypeStruct((count, 1), wide),
            jax.ShapeDtypeStruct((2, width), wide),
            jax.ShapeDtypeStruct((blocks, count, width), low),
        ),
        in_specs=[in_hbm()] * 5 + [on_chip()] * 8,
        out_specs=(on_chip(),) * 6,
        scratch_shapes=[
            pltpu.VMEM((count, width), wide),
            pltpu.VMEM((count, width), wide),
            pltpu.VMEM((width, width), low),
        ]
        + fetch_scratch(fetched),
        compiler_params=params(30),
        cost_estimate=cost(8 * blocks * count * width * width, 8 * blocks * width * width),
    )(*fetched, hidden, active, slope, w_up, *parts)


def outer_kernel(left, right, theirs_ref):
    core = lax.axis_index("own")
    step = pl.program_id(0)
    columns = theirs_ref.shape[2]
    left_step = step if left.shape[0] > 1 else 0
    right_step = step if right.shape[0] > 1 else 0
    part = pl.ds(pl.multiple_of((1 - core) * columns, columns), columns)
    theirs_ref[step] = dot(left[left_step], right[right_step, :, part], 0, 0).astype(low)


def outer_theirs(left, right):
    count, width = left.shape[1:]
    blocks = max(left.shape[0], right.shape[0])
    return pl.pallas_call(
        outer_kernel,
        grid=(blocks,),
        out_shape=jax.ShapeDtypeStruct((blocks, width, width // 2), low),
        in_specs=[on_chip()] * 2,
        out_specs=on_chip(),
        compiler_params=params(8),
        cost_estimate=cost(blocks * count * width * width, 3 * blocks * width * width),
    )(left, right)


def column(values):
    return values[:, None]


def pack_kernel(
    tokens, chosen, packing, vectors, placing_ref, packed_ref, gates_ref
):
    count = tokens.shape[0]
    capacity = packing.shape[0]
    center, inverse = normal_parts(tokens[...].astype(wide))
    first = (center * inverse * vectors[0:1] + vectors[1:2]).astype(low)
    gate = jax.nn.sigmoid(jnp.sum(first.astype(wide) * vectors[2:3], axis=-1, keepdims=True))
    weighting = jnp.where(chosen[...] == 1, gate, 0.0)
    gates_ref[:, 0:1] = weighting
    gates_ref[:, 1:2] = weighting * (1.0 - gate)
    above = lax.broadcasted_iota(jnp.int32, (count, count), 0)
    below = lax.broadcasted_iota(jnp.int32, (count, count), 1)
    earlier = (below <= above).astype(wide).astype(low)
    flags = jnp.broadcast_to(chosen[...].astype(wide), (count, capacity))
    rank = dot(earlier, flags.astype(low))
    place_of = lax.broadcasted_iota(jnp.int32, (count, capacity), 1).astype(wide) + 1.0
    ranked = jnp.where(rank == place_of, flags, 0.0).astype(low)
    slots = lax.broadcasted_iota(jnp.int32, (capacity, capacity), 1)
    slot_of = (packing[...] == slots).astype(wide).astype(low)
    placing = dot(ranked, slot_of).astype(low)
    placing_ref[...] = placing
    packed_ref[...] = dot(placing, first, 0, 0).astype(low)


def pack_tokens(tokens, chosen, packing, vectors):
    count, width = tokens.shape
    capacity = packing.shape[0]
    return pl.pallas_call(
        pack_kernel,
        out_shape=(
            jax.ShapeDtypeStruct((count, capacity), low),
            jax.ShapeDtypeStruct((capacity, width), low),
            jax.ShapeDtypeStruct((count, 2), wide),
        ),
        in_specs=[on_chip()] * 4,
        out_specs=(on_chip(),) * 3,
        compiler_params=params(10),
        cost_estimate=cost(4 * count * capacity * width, 8 * count * width),
    )(tokens, column(chosen), column(packing), vectors)


def token_back_kernel(*refs):
    sources, (out_ref, vector_ref), fetched, sems = refs[:6], refs[6:8], refs[8:14], refs[14]
    finish(fetch(sources, fetched, sems))
    tokens, placing, grad_sent, grad_hidden, grad_logit, vectors = fetched
    grad_first = dot(placing[...], grad_sent[...]) + grad_logit[...] * vectors[2:3]
    center, inverse = normal_parts(tokens[...].astype(wide))
    scaled = center * inverse
    vector_ref[0:1] = jnp.sum(grad_first * scaled, axis=0, keepdims=True)
    vector_ref[1:2] = jnp.sum(grad_first, axis=0, keepdims=True)
    first = (scaled * vectors[0:1] + vectors[1:2]).astype(low).astype(wide)
    vector_ref[2:3] = jnp.sum(grad_logit[...] * first, axis=0, keepdims=True)
    pulled = grad_first * vectors[0:1]
    pulled = (
        pulled
        - jnp.mean(pulled, axis=-1, keepdims=True)
        - scaled * jnp.mean(pulled * scaled, axis=-1, keepdims=True)
    )
    out_ref[...] = (grad_hidden[...] + inverse * pulled).astype(low)


def token_back(tokens, placing, grad_sent, grad_hidden, grad_logit, vectors):
    count, width = tokens.shape
    return pl.pallas_call(
        token_back_kernel,
        out_shape=(
            jax.ShapeDtypeStruct((count, width), low),
            jax.ShapeDtypeStruct((3, width), wide),
        ),
        in_specs=[in_hbm()] * 6,
        out_specs=(on_chip(),) * 2,
        scratch_shapes=fetch_scratch(
            (tokens, placing, grad_sent, grad_hidden, grad_logit, vectors)
        ),
        compiler_params=params(17),
        cost_estimate=cost(2 * count * width * placing.shape[1], 12 * count * width),
    )(tokens, placing, grad_sent, grad_hidden, grad_logit, vectors)


def all_sum(value, flips):
    for flip in flips:
        value = value + send(value, [(i, i ^ flip) for i in range(32)])
    return value


def exchange(value, n_data):
    capacity, width = value.shape
    moved = lax.all_to_all(
        value.reshape(n_data, capacity // n_data, width), "dp", split_axis=0, concat_axis=0, tiled=True
    )
    return moved.reshape(capacity, width)


def block_shards(
    tokens,
    cotangent,
    selected,
    packing,
    segments,
    blocks,
    left_stat,
    right_stat,
    left_root,
    right_root,
    vectors,
    moment,
):
    model_width = tokens.shape[2]
    token_count = tokens.shape[0] * tokens.shape[1]
    n_data = lax.axis_size("dp")
    capacity = packing.shape[1]
    line, place, core = here()
    own_tokens = tokens.reshape(token_count, model_width)
    above = cotangent.reshape(token_count, model_width)
    segment = segments[0]

    every = columns_by_core(jnp.transpose(blocks, (1, 0, 2)).astype(low))
    placing, packed, gates = pack_tokens(
        own_tokens, selected.reshape(token_count), packing[0], vectors
    )
    buffer = exchange(packed, n_data)
    attn_two = send(every[:4], line_pairs(2))
    ffn_got = send(after(every[4:], attn_two), line_pairs(2))
    attn_pair = jnp.stack([every[:4], attn_two])
    attn_got = send(attn_pair, line_pairs(1))
    line_attn = after(jnp.concatenate([attn_pair, attn_got]), packed, ffn_got)
    ffn_two = jnp.stack([every[4:], after(ffn_got, attn_got)])
    near_attn = send(line_attn, plane_pairs(0))
    every_root = roots_by_core(after(left_root, ffn_two), right_root)
    first_attn = after(jnp.stack([line_attn, near_attn]), every_root, buffer)
    far_attn = send(first_attn, plane_pairs(1))
    line_ffn = gather_far(ffn_two)
    near_ffn = send(after(line_ffn, near_attn), plane_pairs(0))
    w_parts = with_other(first_attn, far_attn)
    answer, store = attend(buffer, w_parts, segment)
    root_given = lax.optimization_barrier((*roots_given(every_root), buffer, line_ffn))[:4]
    root_parts = [root_given[0]]
    for flip in (1, 2, 3):
        root_parts.append(send(root_given[flip], line_pairs(flip)))
    first_ffn = jnp.stack([line_ffn, near_ffn])
    far_ffn = after(send(after(first_ffn, far_attn), plane_pairs(1)), answer)
    left_line, right_line = (jnp.stack([part[:, kind] for part in root_parts]) for kind in range(2))
    ffn_parts = with_other(first_ffn, far_ffn)
    returned = exchange(answer, n_data)

    hidden, second_low, active, slope, w_up = token_forward(
        own_tokens, placing, after(returned, *root_given), gates, vectors, ffn_parts
    )
    down_theirs = outer_theirs(active, above[None])
    down_got = send(down_theirs, swap_pairs())
    down_give, *down_kept = sum_start(lambda step: step, active, above[None], down_got)
    down_got = send(down_give, plane_pairs(0))
    mixed, grad_packed, grad_hidden, grad_logit, vector_two, grad_inner = token_backward(
        above,
        hidden,
        active,
        slope,
        placing,
        returned,
        gates,
        vectors,
        after(w_up, down_give),
        ffn_parts,
    )
    grad_answer = exchange(grad_packed, n_data)
    up_theirs = outer_theirs(after(second_low, down_got, *root_parts[1:])[None], grad_inner)
    up_got = send(up_theirs, swap_pairs())
    up_give, *up_kept = sum_start(lambda step: 0, second_low[None], grad_inner, up_got)
    up_got = send(after(up_give, grad_answer), plane_pairs(0))

    attn_theirs, grads, grad_buffer, sides = attend_back(
        store, segment, after(grad_answer, up_give)
    )
    grad_sent = exchange(after(grad_buffer, up_got), n_data)
    attn_got = send(after(attn_theirs, up_got), swap_pairs())
    attn_give, *attn_kept = sum_start(lambda step: step // 3, sides, grads, attn_got)

    up_kept, up_give = add_first(up_got, *up_kept)
    down_kept, down_give = add_first(down_got, *down_kept)
    pair_got = send(jnp.stack([up_give, down_give]), plane_pairs(1))
    attn_got = send(attn_give, plane_pairs(0))
    pair_kept = jnp.stack([up_kept, down_kept]) + after(pair_got, attn_give).astype(wide)
    pair_own, pair_two, pair_give = cut_line(pair_kept)

    near_right = send(after(right_line, pair_got), plane_pairs(0))
    pair_got = send(after(pair_give, attn_got, grad_sent), line_pairs(1))
    attn_kept, attn_give = add_first(attn_got, *attn_kept)
    attn_got = send(attn_give, plane_pairs(1))
    pair_own, pair_give = add_line(pair_own, pair_two, pair_got)
    first_right = jnp.stack([right_line, near_right])
    far_right = send(after(first_right, pair_got), plane_pairs(1))
    roots = (left_line, send(left_line, swap_pairs()), first_right, far_right)
    grad_tokens, vector_one = token_back(
        own_tokens, placing, grad_sent, grad_hidden, grad_logit, vectors
    )

    pair_got = send(after(pair_give, attn_got, vector_one, near_right), line_pairs(2))
    attn_own, attn_two, attn_give = cut_line((attn_kept + attn_got.astype(wide))[None])
    attn_got = send(attn_give, line_pairs(1))
    pair_own = (pair_own + pair_got.astype(wide)).astype(low)
    attn_own, attn_give = add_line(attn_own, attn_two, attn_got)

    pair_near = send(after(pair_own, attn_give, far_right), plane_pairs(0))
    attn_got = send(attn_give, line_pairs(2))
    attn_own = (attn_own + attn_got.astype(wide)).astype(low)
    pair_first = jnp.stack([pair_own, pair_near])

    pair_far = send(after(pair_first, attn_own), plane_pairs(1))
    attn_near = send(attn_own, plane_pairs(0))
    pair_mine = jnp.concatenate([pair_first, pair_far])
    attn_first = jnp.stack([attn_own, attn_near])

    pair_theirs = send(pair_mine, swap_pairs())
    attn_far = send(attn_first, plane_pairs(1))
    attn_mine = jnp.concatenate([attn_first, attn_far])

    pair_made, pair_square = step_chunks(pair_mine, after(pair_theirs, attn_first), roots, 1)
    pair = return_chunks(pair_made)
    attn_theirs = send(attn_mine, swap_pairs())
    attn_made, attn_square = step_chunks(attn_mine, after(attn_theirs, pair[1]), roots, 0)
    attn = return_chunks(attn_made)
    squares = jnp.concatenate([jnp.sum(attn_square, axis=2), jnp.sum(pair_square, axis=2)])
    lane = lax.broadcasted_iota(jnp.int32, (1, model_width), 1)
    square_row = sum(
        jnp.where(lane == 4 * chunk + line, squares[chunk], 0.0) for chunk in range(3)
    )
    sums = jnp.concatenate([vector_one, vector_two, square_row])
    sums = all_sum(after(sums, *pair[2:]), (1, 2, 4, 8))
    sums = all_sum(after(sums, *attn[1:]), (16,))
    pair = jnp.stack(pair)
    pair_other = send(pair, swap_pairs())
    attn = jnp.stack(attn)
    attn_other = send(attn, [(i, i ^ 1) for i in range(1, 32, 2)])
    vector_grad = sums[:5]
    size = model_width * model_width
    scales = block_rate * lax.rsqrt(sums[5, :12] / size + norm_eps)
    grad_own, left_new, right_new, new_blocks = update_blocks(
        attn, attn_other, pair, pair_other, blocks, left_stat, right_stat, scales
    )
    moment_new = 0.5 * moment + 0.5 * vector_grad
    row_squares = jnp.mean(moment_new * moment_new, axis=1, keepdims=True)
    vector_new = vectors - vector_rate * moment_new * lax.rsqrt(row_squares + norm_eps)
    return (
        mixed.reshape(tokens.shape),
        grad_tokens.reshape(tokens.shape),
        grad_own,
        left_new,
        right_new,
        new_blocks,
        vector_grad,
        moment_new,
        vector_new,
    )


def shards(
    tokens,
    cotangent,
    selected,
    packing,
    segments,
    blocks,
    left_stat,
    right_stat,
    left_root,
    right_root,
    vectors,
    moment,
):
    model_width = tokens.shape[2]
    token_count = tokens.shape[0] * tokens.shape[1]
    n_data = lax.axis_size("dp")
    n_owner = lax.axis_size("own")
    shard_rows = blocks.shape[0]
    own_blocks = blocks.shape[1]
    up_blocks = (own_blocks * n_owner - 4) // 2
    capacity = packing.shape[1]
    per_peer = capacity // n_data
    head_count = model_width // HEAD_DIM
    score_scale = HEAD_DIM ** (-0.5)
    flat_weights = blocks.astype(jnp.bfloat16).reshape(1, shard_rows * own_blocks * model_width)
    gathered = lax.all_gather(flat_weights, ("dp", "own"), axis=0, tiled=True)
    gathered = gathered.reshape(n_data, n_owner, shard_rows, own_blocks, model_width)

    def matrix(number):
        return gathered[:, number // own_blocks, :, number % own_blocks, :].reshape(
            model_width, model_width
        )

    w_query = matrix(0)
    w_key = matrix(1)
    w_value = matrix(2)
    w_out = matrix(3)
    w_up = jnp.concatenate([matrix(4 + position) for position in range(up_blocks)], axis=1)
    w_down = jnp.concatenate(
        [matrix(4 + up_blocks + position) for position in range(up_blocks)], axis=0
    )
    inputs = tokens.reshape(token_count, model_width).astype(jnp.float32)
    chosen = selected.reshape(token_count)
    normed_one, norm_one_back = jax.vjp(layer_norm, inputs, vectors[0], vectors[1])
    first_low = normed_one.astype(jnp.bfloat16)
    first_wide = first_low.astype(jnp.float32)
    gate_values = jax.nn.sigmoid(jnp.dot(first_wide, vectors[2], precision=highest))
    before = jnp.cumsum(chosen) - 1
    slot_index = jnp.where(chosen == 1, packing[0][jnp.clip(before, 0, capacity - 1)], -1)
    placing = (slot_index[None, :] == jnp.arange(capacity, dtype=jnp.int32)[:, None]).astype(
        jnp.bfloat16
    )
    packed = jnp.dot(placing, first_low, preferred_element_type=jnp.float32).astype(jnp.bfloat16)
    buffer = lax.all_to_all(
        packed.reshape(n_data, per_peer, model_width), "dp", split_axis=0, concat_axis=0, tiled=True
    )
    buffer = buffer.reshape(capacity, model_width)

    def project(matrix_in):
        made = jnp.dot(buffer, matrix_in, preferred_element_type=jnp.float32).astype(jnp.bfloat16)
        return made.reshape(capacity, head_count, HEAD_DIM)

    query_rows = project(w_query)
    key_rows = project(w_key)
    value_rows = project(w_value)
    segment = segments[0]
    block_rows = math.gcd(capacity, 512)
    starts = jnp.arange(capacity // block_rows, dtype=jnp.int32) * block_rows

    def masked_scores():
        scores = (
            jnp.einsum("qhd,khd->hqk", query_rows, key_rows, preferred_element_type=jnp.float32)
            * score_scale
        )
        same_segment = segment[:, None] == segment[None, :]
        return (jnp.where(same_segment[None, :, :], scores, -1e30), query_rows)

    def forward_block(first_row):
        scores, unused_block = masked_scores()
        largest = jnp.max(scores, axis=-1, keepdims=True)
        raised = jnp.exp(scores - largest)
        row_total = jnp.sum(raised, axis=-1, keepdims=True)
        shares = (raised / row_total).astype(jnp.bfloat16)
        context_part = jnp.einsum(
            "hqk,khd->qhd", shares, value_rows, preferred_element_type=jnp.float32
        )
        return (context_part.astype(jnp.bfloat16), largest[..., 0] + jnp.log(row_total[..., 0]))

    context_blocks, lse_blocks = lax.map(forward_block, starts)
    context = context_blocks.reshape(capacity, model_width)
    answer = jnp.dot(context, w_out, preferred_element_type=jnp.float32).astype(jnp.bfloat16)
    returned = lax.all_to_all(
        answer.reshape(n_data, per_peer, model_width), "dp", split_axis=0, concat_axis=0, tiled=True
    )
    returned = returned.reshape(capacity, model_width)
    unpacked = jnp.einsum("mt,md->td", placing, returned, preferred_element_type=jnp.float32)
    weighting = jnp.where(chosen == 1, gate_values, 0.0)
    hidden = inputs + weighting[:, None] * unpacked
    normed_two, norm_two_back = jax.vjp(layer_norm, hidden, vectors[3], vectors[4])
    second_low = normed_two.astype(jnp.bfloat16)
    pre_active = jnp.dot(second_low, w_up, preferred_element_type=jnp.float32)
    active_wide, gelu_back = jax.vjp(gelu_exact, pre_active)
    active = active_wide.astype(jnp.bfloat16)
    result = hidden + jnp.dot(active, w_down, preferred_element_type=jnp.float32)
    mixed = result.astype(jnp.bfloat16).reshape(tokens.shape)
    upstream = cotangent.reshape(token_count, model_width)
    grad_down = jnp.einsum("tf,td->fd", active, upstream, preferred_element_type=jnp.float32)
    grad_active = jnp.einsum("td,fd->tf", upstream, w_down, preferred_element_type=jnp.float32)
    grad_inner = gelu_back(grad_active)[0].astype(jnp.bfloat16)
    grad_up = jnp.einsum("td,tf->df", second_low, grad_inner, preferred_element_type=jnp.float32)
    grad_second = jnp.einsum("tf,df->td", grad_inner, w_up, preferred_element_type=jnp.float32)
    grad_hidden_part, grad_gain_two, grad_bias_two = norm_two_back(grad_second)
    grad_hidden = upstream.astype(jnp.float32) + grad_hidden_part
    grad_token_back = (grad_hidden * weighting[:, None]).astype(jnp.bfloat16)
    grad_packed = jnp.dot(placing, grad_token_back, preferred_element_type=jnp.float32).astype(
        jnp.bfloat16
    )
    router_pull = jnp.where(chosen == 1, jnp.sum(grad_hidden * unpacked, axis=-1), 0.0)
    grad_logit = router_pull * gate_values * (1.0 - gate_values)
    grad_answer = lax.all_to_all(
        grad_packed.reshape(n_data, per_peer, model_width),
        "dp",
        split_axis=0,
        concat_axis=0,
        tiled=True,
    )
    grad_answer = grad_answer.reshape(capacity, model_width)
    grad_out = jnp.einsum("md,me->de", context, grad_answer, preferred_element_type=jnp.float32)
    grad_context = jnp.einsum("me,de->md", grad_answer, w_out, preferred_element_type=jnp.float32)
    grad_context = grad_context.astype(jnp.bfloat16).reshape(capacity, head_count, HEAD_DIM)

    def backward_block(running, item_pair):
        first_row, lse_block = item_pair
        scores, query_block = masked_scores()
        shares_wide = jnp.exp(scores - lse_block[..., None])
        grad_shares = jnp.einsum(
            "qhd,khd->hqk", grad_context, value_rows, preferred_element_type=jnp.float32
        )
        inner_sum = jnp.sum(shares_wide * grad_shares, axis=-1, keepdims=True)
        grad_scores = (shares_wide * (grad_shares - inner_sum)).astype(jnp.bfloat16)
        grad_query_block = (
            jnp.einsum("hqk,khd->qhd", grad_scores, key_rows, preferred_element_type=jnp.float32)
            * score_scale
        )
        key_sum = (
            running[0]
            + jnp.einsum(
                "hqk,qhd->khd", grad_scores, query_block, preferred_element_type=jnp.float32
            )
            * score_scale
        )
        value_sum = running[1] + jnp.einsum(
            "hqk,qhd->khd",
            shares_wide.astype(jnp.bfloat16),
            grad_context,
            preferred_element_type=jnp.float32,
        )
        return ((key_sum, value_sum), grad_query_block)

    zeros_init = jnp.zeros((capacity, head_count, HEAD_DIM), jnp.float32)
    (key_total, value_total), query_grads = lax.scan(
        backward_block, (zeros_init, zeros_init), (starts, lse_blocks)
    )
    grad_query = query_grads.reshape(capacity, model_width).astype(jnp.bfloat16)
    grad_key = key_total.reshape(capacity, model_width).astype(jnp.bfloat16)
    grad_value = value_total.reshape(capacity, model_width).astype(jnp.bfloat16)
    grad_w_query = jnp.einsum("md,me->de", buffer, grad_query, preferred_element_type=jnp.float32)
    grad_w_key = jnp.einsum("md,me->de", buffer, grad_key, preferred_element_type=jnp.float32)
    grad_w_value = jnp.einsum("md,me->de", buffer, grad_value, preferred_element_type=jnp.float32)
    grad_buffer = jnp.einsum("me,de->md", grad_query, w_query, preferred_element_type=jnp.float32)
    grad_buffer = grad_buffer + jnp.einsum(
        "me,de->md", grad_key, w_key, preferred_element_type=jnp.float32
    )
    grad_buffer = grad_buffer + jnp.einsum(
        "me,de->md", grad_value, w_value, preferred_element_type=jnp.float32
    )
    grad_buffer = grad_buffer.astype(jnp.bfloat16)
    grad_sent = lax.all_to_all(
        grad_buffer.reshape(n_data, per_peer, model_width),
        "dp",
        split_axis=0,
        concat_axis=0,
        tiled=True,
    )
    grad_sent = grad_sent.reshape(capacity, model_width)
    grad_first = jnp.einsum("mt,md->td", placing, grad_sent, preferred_element_type=jnp.float32)
    grad_first = grad_first + grad_logit[:, None] * vectors[2][None, :]
    grad_router = jnp.sum(grad_logit[:, None] * first_wide, axis=0)
    grad_input_part, grad_gain_one, grad_bias_one = norm_one_back(grad_first)
    grad_tokens = (grad_hidden + grad_input_part).astype(jnp.bfloat16).reshape(tokens.shape)
    pieces = [grad_w_query, grad_w_key, grad_w_value, grad_out]
    pieces = pieces + [
        grad_up[:, position * model_width : (position + 1) * model_width]
        for position in range(up_blocks)
    ]
    pieces = pieces + [
        grad_down[position * model_width : (position + 1) * model_width, :]
        for position in range(up_blocks)
    ]
    local_terms = jnp.stack(pieces, axis=1)
    vector_terms = jnp.stack(
        [grad_gain_one, grad_bias_one, grad_router, grad_gain_two, grad_bias_two]
    )
    partial_value = lax.psum_scatter(local_terms, "dp", scatter_dimension=0, tiled=True)
    grad_own = lax.psum_scatter(
        partial_value.astype(jnp.bfloat16), "own", scatter_dimension=1, tiled=True
    ).astype(jnp.float32)
    vector_grad = lax.psum(vector_terms, ("dp", "own"))
    full_grad = lax.all_gather(grad_own.astype(jnp.bfloat16), "dp", axis=0, tiled=True).astype(
        grad_own.dtype
    )
    row_start = lax.axis_index("dp") * shard_rows
    left_new = 0.5 * left_stat + 0.5 * jnp.einsum(
        "rbk,nbk->rbn", grad_own, full_grad, precision=highest
    )
    column_part = lax.dynamic_slice_in_dim(full_grad, row_start, shard_rows, 2)
    right_new = 0.5 * right_stat + 0.5 * jnp.einsum(
        "nbr,nbk->rbk", column_part, full_grad, precision=highest
    )
    lefted = jnp.einsum("rbn,nbk->rbk", left_root, full_grad, precision=highest)
    precond = jnp.zeros_like(grad_own) + jnp.einsum(
        "rbn,nbk->rbk",
        lefted,
        lax.all_gather(right_root.astype(jnp.bfloat16), "dp", axis=0, tiled=True).astype(
            jnp.float32
        ),
        precision=highest,
    )
    square_sums = lax.psum(jnp.sum(precond * precond, axis=(0, 2)), "dp")
    step_scale = lax.rsqrt(square_sums / (model_width * model_width) + norm_eps)
    new_blocks = blocks - block_rate * precond * step_scale[None, :, None]
    moment_new = 0.5 * moment + 0.5 * vector_grad
    row_squares = jnp.mean(moment_new * moment_new, axis=1, keepdims=True)
    vector_new = vectors - vector_rate * moment_new * lax.rsqrt(row_squares + norm_eps)
    return (
        mixed,
        grad_tokens,
        grad_own,
        left_new,
        right_new,
        new_blocks,
        vector_grad,
        moment_new,
        vector_new,
    )


def solution(mesh):
    placed = (
        P(("dp", "own"), None, None),
        P(("dp", "own"), None, None),
        P(("dp", "own"), None),
        P(("dp", "own"), None),
        P(("dp", "own"), None),
        P("dp", "own", None),
        P("dp", "own", None),
        P("dp", "own", None),
        P("dp", "own", None),
        P("dp", "own", None),
        P(),
        P(),
    )
    small = mesh.shape["dp"] == 16 and mesh.shape["own"] == 2
    return jax.shard_map(
        block_shards if small else shards,
        mesh=mesh,
        in_specs=placed,
        out_specs=(
            P(("dp", "own"), None, None),
            P(("dp", "own"), None, None),
            P("dp", "own", None),
            P("dp", "own", None),
            P("dp", "own", None),
            P("dp", "own", None),
            P(),
            P(),
            P(),
        ),
        check_vma=False,
    )
```

```python
import functools
import math

import jax
import jax.numpy as jnp
from jax import lax
from jax.experimental import pallas as pl
from jax.experimental.pallas import tpu as pltpu
from jax.sharding import PartitionSpec as P

HEAD_DIM = 64


norm_eps = 1e-06
block_rate = 0.03
vector_rate = 0.04
highest = lax.Precision.HIGHEST


def layer_norm(values, norm_gain, norm_bias):
    center = values - jnp.mean(values, axis=-1, keepdims=True)
    spread = jnp.mean(center * center, axis=-1, keepdims=True)
    return center * lax.rsqrt(spread + norm_eps) * norm_gain + norm_bias


def gelu_exact(values):
    return jax.nn.gelu(values, approximate=False)


BOTH = ("dp", "own")
low = jnp.bfloat16
wide = jnp.float32
MIB = 2**20


def swap_pairs():
    return [(i, i ^ 1) for i in range(32)]


def plane_pairs(step):
    pairs = []
    for i in range(32):
        place, core = i // 2, i % 2
        flip = (1, 2)[step ^ core]
        pairs.append((i, (place ^ flip) * 2 + core))
    return pairs


def line_pairs(flip):
    return [(i, i ^ (8 * flip)) for i in range(32)]


def send(value, pairs):
    return lax.ppermute(value, BOTH, pairs)


def after(value, *others):
    return lax.optimization_barrier((value,) + others)[0]


def pick(value, index, axis):
    return lax.dynamic_index_in_dim(value, index, axis, keepdims=False)


def first_core():
    return lax.axis_index("own") == 0


def halves(value):
    middle = value.shape[-1] // 2
    lower, upper = value[..., :middle], value[..., middle:]
    return jnp.where(first_core(), lower, upper), jnp.where(first_core(), upper, lower)


def in_core_order(mine, theirs, axis):
    return jnp.where(
        first_core(),
        jnp.concatenate([mine, theirs], axis=axis),
        jnp.concatenate([theirs, mine], axis=axis),
    )


LINE_FLIPS = (0, 2, 1, 3)


def flipped(index, flip):
    return jnp.bitwise_xor(index, flip)


def spots(place, half):
    first, second = half + 1, 2 - half
    return [
        place,
        flipped(place, first),
        flipped(place, second),
        flipped(place, 3),
    ]


def here():
    device = lax.axis_index("dp")
    return device // 4, device % 4, lax.axis_index("own")


def dot(left, right, left_axis=1, right_axis=0):
    return lax.dot_general(
        left, right, (((left_axis,), (right_axis,)), ((), ())), preferred_element_type=wide
    )


def on_chip():
    return pl.BlockSpec(memory_space=pltpu.VMEM)


def whole(value):
    return pl.BlockSpec(value.shape, lambda *steps: (0,) * value.ndim)


def in_hbm():
    return pl.BlockSpec(memory_space=pltpu.HBM)


def fetch_scratch(values):
    return [pltpu.VMEM(value.shape, value.dtype) for value in values] + [
        pltpu.SemaphoreType.DMA((len(values),))
    ]


def fetch(sources, targets, sems):
    copies = [
        pltpu.make_async_copy(source, target, sems.at[number])
        for number, (source, target) in enumerate(zip(sources, targets))
    ]
    for copy in copies:
        copy.start()
    return copies


def finish(copies):
    for copy in copies:
        copy.wait()


def params(limit):
    return pltpu.CompilerParams(vmem_limit_bytes=limit * MIB)


def cost(flops, moved):
    return pl.CostEstimate(flops=flops, bytes_accessed=moved, transcendentals=0)


def place_block(parts, block, target):
    line, place, core = here()
    rows, columns = parts[0].shape[3:]
    for other in range(2):
        half = core if other == 0 else 1 - core
        column_slice = pl.ds(pl.multiple_of(half * columns, columns), columns)
        for number, spot in enumerate(spots(place, half)):
            for index, flip in enumerate(LINE_FLIPS):
                start = (flipped(line, flip) * 4 + spot) * rows
                row_slice = pl.ds(pl.multiple_of(start, rows), rows)
                piece = parts[2 * other + number // 2][number % 2, index, block]
                target[row_slice, column_slice] = piece


def columns_by_core(value):
    keep, give = halves(value)
    return in_core_order(keep, send(give, swap_pairs()), 0)


def gather_far(pair):
    return jnp.concatenate([pair, send(pair, line_pairs(1))])


def with_other(first, far):
    return [first, far, send(first, swap_pairs()), send(far, swap_pairs())]


def roots_by_core(left_root, right_root):
    both = [jnp.transpose(root, (1, 0, 2)).astype(low) for root in (left_root, right_root)]
    every = columns_by_core(jnp.stack(both, axis=1))
    return every.reshape((3, 4) + every.shape[1:])


def roots_given(every):
    line, place, core = here()
    return [pick(every, flipped(line, flip), 1) for flip in range(4)]


def sum_kernel(left_of, left, right, got, give_ref, kept_ref, passed_ref, total):
    line, place, core = here()
    step = pl.program_id(0)
    columns = got.shape[2]
    rows = kept_ref.shape[2]
    part = pl.ds(pl.multiple_of(core * columns, columns), columns)
    right_step = step if right.shape[0] > 1 else 0
    made = dot(left[left_of(step)], right[right_step, :, part], 0, 0)
    total[...] = made + got[step].astype(wide)
    own, first, second, both = spots(place, core)
    for row_line in range(4):

        def piece(spot):
            return total[pl.ds(pl.multiple_of((row_line * 4 + spot) * rows, rows), rows), :]

        give_ref[0, step, row_line] = piece(first).astype(low)
        give_ref[1, step, row_line] = piece(both).astype(low)
        kept_ref[step, row_line] = piece(own).astype(low)
        passed_ref[step, row_line] = piece(second).astype(low)


def sum_start(left_of, left, right, got):
    count, width = left.shape[1:]
    blocks, full, columns = got.shape
    shape = (blocks, 4, full // 16, columns)
    return pl.pallas_call(
        functools.partial(sum_kernel, left_of),
        grid=(blocks,),
        out_shape=(
            jax.ShapeDtypeStruct((2,) + shape, low),
            jax.ShapeDtypeStruct(shape, low),
            jax.ShapeDtypeStruct(shape, low),
        ),
        in_specs=[on_chip()] * 3,
        out_specs=(on_chip(),) * 3,
        scratch_shapes=[pltpu.VMEM((full, columns), wide)],
        compiler_params=params(12),
        cost_estimate=cost(blocks * count * width * width, 5 * blocks * width * width),
    )(left, right, got)


def add_first(got, kept, passed):
    kept = kept.astype(wide) + got[0].astype(wide)
    return kept, (passed.astype(wide) + got[1].astype(wide)).astype(low)


def cut_line(kept):
    line, place, core = here()
    given = jnp.stack([pick(kept, flipped(line, flip), 1) for flip in (1, 3)]).astype(low)
    return pick(kept, line, 1), pick(kept, flipped(line, 2), 1), given


def add_line(own, two, got):
    return own + got[0].astype(wide), (two + got[1].astype(wide)).astype(low)


def step_kernel(
    number,
    mine,
    theirs,
    left_mine_from,
    left_theirs_from,
    right_first_from,
    right_far_from,
    out_ref,
    square_ref,
    grad_ref,
    rows_ref,
    left_ref,
    right_ref,
    cross_ref,
    left_mine,
    left_theirs,
    right_first,
    right_far,
    sems,
):
    chunk = number + pl.program_id(0)
    copies = fetch(
        [
            left_mine_from.at[:, chunk],
            left_theirs_from.at[:, chunk],
            right_first_from.at[:, :, chunk],
            right_far_from.at[:, :, chunk],
        ],
        [left_mine, left_theirs, right_first, right_far],
        sems,
    )
    line, place, core = here()
    rows, columns = mine.shape[3:]

    def rows_of(row_line, spot):
        return pl.ds(pl.multiple_of((row_line * 4 + spot) * rows, rows), rows)

    def column_half(half):
        return pl.ds(pl.multiple_of(half * columns, columns), columns)

    for half, group in ((core, mine), (1 - core, theirs)):
        for number, spot in enumerate(spots(place, half)):
            for step in range(4):
                grad_ref[rows_of(step, spot), column_half(half)] = group[number, 0, step]
    finish(copies)
    for half, left in ((core, left_mine), (1 - core, left_theirs)):
        for flip in range(4):
            target = pl.ds(pl.multiple_of(flipped(line, flip) * rows, rows), rows)
            left_ref[target, column_half(half)] = left[flip]
    for number, spot in enumerate(spots(place, core)):
        source = right_far if number > 1 else right_first
        for flip in range(4):
            right_ref[rows_of(flipped(line, flip), spot), :] = source[number % 2, flip]
    for row_line in range(4):
        rows_ref[row_line * rows : (row_line + 1) * rows, :] = grad_ref[rows_of(row_line, place), :]
    left = dot(rows_ref[...], grad_ref[column_half(core), :], 1, 1)
    cross_ref[...] = dot(grad_ref[...], grad_ref[:, column_half(core)], 0, 0)
    lefted = dot(left_ref[...], grad_ref[...]).astype(low)
    stepped = dot(lefted, right_ref[...])
    square_ref[0] = jnp.sum(stepped * stepped, axis=0, keepdims=True)
    for row_line in range(4):
        part = slice(row_line * rows, (row_line + 1) * rows)
        out_ref[0, row_line, 0] = mine[0, 0, row_line]
        out_ref[0, row_line, 1] = left[part].astype(low)
        out_ref[0, row_line, 2] = cross_ref[rows_of(row_line, place), :].astype(low)
        out_ref[0, row_line, 3] = stepped[part].astype(low)


def step_chunks(mine, theirs, roots, number):
    chunks, lines, rows, columns = mine.shape[1:]
    full = rows * 16
    grad_spec = pl.BlockSpec((4, 1, lines, rows, columns), lambda step: (0, step, 0, 0, 0))
    return pl.pallas_call(
        functools.partial(step_kernel, number),
        grid=(chunks,),
        out_shape=(
            jax.ShapeDtypeStruct((chunks, lines, 4, rows, columns), low),
            jax.ShapeDtypeStruct((chunks, 1, columns), wide),
        ),
        in_specs=[grad_spec] * 2 + [in_hbm()] * 4,
        out_specs=(
            pl.BlockSpec((1, lines, 4, rows, columns), lambda step: (step, 0, 0, 0, 0)),
            pl.BlockSpec((1, 1, columns), lambda step: (step, 0, 0)),
        ),
        scratch_shapes=[
            pltpu.VMEM((full, columns * 2), low),
            pltpu.VMEM((lines * rows, columns * 2), low),
            pltpu.VMEM((lines * rows, columns * 2), low),
            pltpu.VMEM((full, columns), low),
            pltpu.VMEM((full, columns), wide),
            pltpu.VMEM((lines, rows, columns), low),
            pltpu.VMEM((lines, rows, columns), low),
            pltpu.VMEM((2, lines, rows, columns), low),
            pltpu.VMEM((2, lines, rows, columns), low),
            pltpu.SemaphoreType.DMA((4,)),
        ],
        compiler_params=params(15),
        cost_estimate=cost(3 * chunks * full**3, 16 * chunks * full * full),
    )(mine, theirs, *roots)


def return_chunks(made):
    line, place, core = here()
    parts = [pick(made, line, 1)]
    for flip in (1, 2, 3):
        parts.append(send(pick(made, flipped(line, flip), 1), line_pairs(flip)))
    return parts


def last_kernel(
    pair, pair_other, down, down_other, blocks, left_stat, right_stat, scales, *outs
):
    grad_out, left_out, right_out, block_out = outs
    line, place, core = here()
    columns = pair.shape[4]

    def update(number, which, mine, theirs):
        for (source, index), half in ((mine, which), (theirs, 1 - which)):
            part = slice(half * columns, (half + 1) * columns)
            pieces = [source[index + (kind,)].astype(wide) for kind in range(4)]
            grad_out[number, :, part] = pieces[0]
            left_out[number, :, part] = 0.5 * left_stat[number, :, part] + 0.5 * pieces[1]
            right_out[number, :, part] = 0.5 * right_stat[number, :, part] + 0.5 * pieces[2]
            step = pieces[3] * scales[6 * which + number]
            block_out[number, :, part] = blocks[number, :, part] - step

    @pl.when(core == 0)
    def first():
        for number in range(6):
            index = (flipped(line, number % 4), number // 4)
            update(number, 0, (pair, index), (pair_other, index))

    @pl.when(core == 1)
    def second():
        for number in range(6):
            source, other = (pair, pair_other) if number < 2 else (down, down_other)
            index = (flipped(line, (number + 2) % 4), 1 if number < 2 else 0)
            update(number, 1, (source, index), (other, index))


def update_blocks(pair, pair_other, down, down_other, blocks, left_stat, right_stat, scales):
    turned = [jnp.transpose(value, (1, 0, 2)) for value in (blocks, left_stat, right_stat)]
    shape = jax.ShapeDtypeStruct(turned[0].shape, wide)
    outs = pl.pallas_call(
        last_kernel,
        out_shape=(shape,) * 4,
        in_specs=[on_chip()] * 7 + [pl.BlockSpec(memory_space=pltpu.SMEM)],
        out_specs=(on_chip(),) * 4,
        compiler_params=params(10),
        cost_estimate=cost(0, 32 * shape.size),
    )(pair, pair_other, down, down_other, *turned, scales)
    return [jnp.transpose(value, (1, 0, 2)) for value in outs]


def head_masks():
    lane = lax.broadcasted_iota(jnp.int32, (1, 2 * HEAD_DIM), 1)
    return [(lane < HEAD_DIM).astype(wide).astype(low), (lane >= HEAD_DIM).astype(wide).astype(low)]


def head_shares(query, key, same):
    scores = dot(query, key, 1, 1) * HEAD_DIM ** (-0.5)
    scores = jnp.where(same, scores, -1e30)
    raised = jnp.exp(scores - jnp.max(scores, axis=-1, keepdims=True))
    return raised / jnp.sum(raised, axis=-1, keepdims=True)


STORE_ROWS = 32768


def store_views(store, rows, width):
    weights = [store.at[pl.ds(block * width, width)] for block in range(4)]
    made = [store.at[pl.ds(4 * width + kind * rows, rows)] for kind in range(3)]
    sides = [store.at[pl.ds(4 * width + (3 + side) * rows, rows)] for side in range(2)]
    return weights, made, sides


def attend_kernel(
    buffer, one, two, three, four, seg_column, seg_row, answer_ref, store, weights, made, sides, sems
):
    rows, width = buffer.shape
    weights_out, made_out, sides_out = store_views(store, rows, width)
    for block in range(4):
        place_block((one, two, three, four), block, weights.at[block])
    copies = fetch([weights.at[block] for block in range(4)], weights_out, sems)
    same = seg_column[...] == seg_row[...]
    for kind in range(3):
        made[kind] = dot(buffer[...], weights[kind]).astype(low)
    copies += fetch([made.at[kind] for kind in range(3)], made_out, sems.at[pl.ds(4, 3)])
    pair_width = 2 * HEAD_DIM
    for pair in range(width // pair_width):
        part = slice(pair * pair_width, (pair + 1) * pair_width)
        query, key, value = (made[kind, :, part] for kind in range(3))
        context = None
        for mask in head_masks():
            shares = head_shares(query, key * mask, same).astype(low)
            term = dot(shares, value * mask)
            context = term if context is None else context + term
        sides[1, :, part] = context.astype(low)
    sides[0] = buffer[...]
    copies += fetch([sides.at[side] for side in range(2)], sides_out, sems.at[pl.ds(7, 2)])
    answer_ref[...] = dot(sides[1], weights[3]).astype(low)
    finish(copies)


def attend_scratch(rows, width):
    return [
        pltpu.VMEM((4, width, width), low),
        pltpu.VMEM((3, rows, width), low),
        pltpu.VMEM((2, rows, width), low),
        pltpu.SemaphoreType.DMA((9,)),
    ]


def attend(buffer, parts, segment):
    rows, width = buffer.shape
    return pl.pallas_call(
        attend_kernel,
        out_shape=(
            jax.ShapeDtypeStruct((rows, width), low),
            jax.ShapeDtypeStruct((STORE_ROWS, width), low),
        ),
        in_specs=[on_chip()] * 7,
        out_specs=(on_chip(), in_hbm()),
        scratch_shapes=attend_scratch(rows, width),
        compiler_params=params(20),
        cost_estimate=cost(12 * rows * width * width, 12 * width * width),
    )(buffer, *parts, segment[:, None], segment[None, :])


def attend_back_kernel(
    store,
    seg_column,
    seg_row,
    grad_answer,
    theirs_ref,
    grads_ref,
    grad_buffer_ref,
    sides,
    grad_context_ref,
    weights,
    made,
    sems,
):
    rows, width = grad_answer.shape
    weights_from, made_from, sides_from = store_views(store, rows, width)
    out_copy, *copies = fetch(
        [weights_from[3]] + made_from + sides_from + weights_from[:3],
        [weights.at[3]]
        + [made.at[kind] for kind in range(3)]
        + [sides.at[side] for side in range(2)]
        + [weights.at[block] for block in range(3)],
        sems,
    )
    same = seg_column[...] == seg_row[...]
    core = lax.axis_index("own")
    out_copy.wait()
    grad_context_ref[...] = dot(grad_answer[...], weights[3], 1, 1).astype(low)
    finish(copies[:3])
    grads_ref[3] = grad_answer[...]
    pair_width = 2 * HEAD_DIM
    for pair in range(width // pair_width):
        part = slice(pair * pair_width, (pair + 1) * pair_width)
        query, key, value = (made[kind, :, part] for kind in range(3))
        above = grad_context_ref[:, part]
        sums = [None] * 3
        for mask in head_masks():
            key_head = key * mask
            shares = head_shares(query, key_head, same)
            grad_shares = dot(above, value * mask, 1, 1)
            inner = jnp.sum(shares * grad_shares, axis=-1, keepdims=True)
            grad_scores = (shares * (grad_shares - inner)).astype(low)
            terms = (
                dot(grad_scores, key_head),
                dot(grad_scores, query * mask, 0, 0),
                dot(shares.astype(low), above * mask, 0, 0),
            )
            sums = [
                term if total is None else total + term for term, total in zip(terms, sums)
            ]
        for kind, factor in enumerate((HEAD_DIM ** (-0.5), HEAD_DIM ** (-0.5), 1.0)):
            grads_ref[kind, :, part] = (sums[kind] * factor).astype(low)
    finish(copies[3:5])
    columns = theirs_ref.shape[2]
    part = pl.ds(pl.multiple_of((1 - core) * columns, columns), columns)
    for kind in range(4):
        theirs_ref[kind] = dot(sides[kind // 3], grads_ref[kind, :, part], 0, 0).astype(low)
    finish(copies[5:])
    total = dot(grads_ref[0], weights[0], 1, 1)
    total = total + dot(grads_ref[1], weights[1], 1, 1)
    total = total + dot(grads_ref[2], weights[2], 1, 1)
    grad_buffer_ref[...] = total.astype(low)


def attend_back(store, segment, grad_answer):
    rows, width = grad_answer.shape
    weights, made, sides, sems = attend_scratch(rows, width)
    return pl.pallas_call(
        attend_back_kernel,
        out_shape=(
            jax.ShapeDtypeStruct((4, width, width // 2), low),
            jax.ShapeDtypeStruct((4, rows, width), low),
            jax.ShapeDtypeStruct((rows, width), low),
            jax.ShapeDtypeStruct((2, rows, width), low),
        ),
        in_specs=[in_hbm()] + [on_chip()] * 3,
        out_specs=(on_chip(),) * 4,
        scratch_shapes=[pltpu.VMEM((rows, width), low), weights, made, sems],
        compiler_params=params(18),
        cost_estimate=cost(20 * rows * width * width, 16 * width * width),
    )(store, segment[:, None], segment[None, :], grad_answer)


def normal_parts(values):
    center = values - jnp.mean(values, axis=-1, keepdims=True)
    spread = jnp.mean(center * center, axis=-1, keepdims=True)
    return center, lax.rsqrt(spread + norm_eps)


def forward_kernel(*refs):
    tokens, placing, returned, gates, vectors = refs[:5]
    parts = refs[5:9]
    hidden_ref, second_ref, active_ref, slope_ref, w_up = refs[9:14]
    step = pl.program_id(0)

    @pl.when(step == 0)
    def prepare():
        values = tokens[...].astype(wide) + gates[:, 0:1] * dot(placing[...], returned[...])
        hidden_ref[...] = values
        center, inverse = normal_parts(values)
        second_ref[...] = (center * inverse * vectors[3:4] + vectors[4:5]).astype(low)

    place_block(parts, step, w_up.at[step])
    before = dot(second_ref[...], w_up[step])
    share = 0.5 + 0.5 * lax.erf(before * (0.5**0.5))
    density = jnp.exp(before * before * -0.5) * (0.5 / math.pi) ** 0.5
    active_ref[step] = (before * share).astype(low)
    slope_ref[step] = (share + before * density).astype(low)


def token_forward(tokens, placing, returned, gates, vectors, parts):
    count, width = tokens.shape
    blocks = parts[0].shape[2] // 2
    by_block = jax.ShapeDtypeStruct((blocks, count, width), low)
    fetched = (tokens, placing, returned, gates, vectors)
    return pl.pallas_call(
        forward_kernel,
        grid=(blocks,),
        out_shape=(
            jax.ShapeDtypeStruct((count, width), wide),
            jax.ShapeDtypeStruct((count, width), low),
            by_block,
            by_block,
            jax.ShapeDtypeStruct((blocks, width, width), low),
        ),
        in_specs=[whole(value) for value in fetched] + [on_chip()] * 4,
        out_specs=(on_chip(),) * 5,
        compiler_params=params(18),
        cost_estimate=cost(8 * blocks * count * width * width, 8 * blocks * width * width),
    )(*fetched, *parts)


def backward_kernel(*refs):
    above, placing, returned, gates, vectors = refs[:5]
    (hidden, active, slope, w_up), parts = refs[5:9], refs[9:13]
    mixed_ref, packed_ref, grad_hidden_ref, logit_ref, vector_ref, inner_ref = refs[13:19]
    result, grad_second, w_down = refs[19:22]
    step = pl.program_id(0)
    place_block(parts, 4 + step, w_down)

    @pl.when(step == 0)
    def prepare():
        result[...] = hidden[...]
        grad_second[...] = jnp.zeros_like(grad_second)

    grad_active = dot(above[...], w_down[...], 1, 1)
    grad_inner = (grad_active * slope[step].astype(wide)).astype(low)
    inner_ref[step] = grad_inner
    result[...] += dot(active[step], w_down[...])
    grad_second[...] += dot(grad_inner, w_up[step], 1, 1)

    @pl.when(step == pl.num_programs(0) - 1)
    def complete():
        mixed_ref[...] = result[...].astype(low)
        center, inverse = normal_parts(hidden[...])
        scaled = center * inverse
        grads = grad_second[...]
        vector_ref[0:1] = jnp.sum(grads * scaled, axis=0, keepdims=True)
        vector_ref[1:2] = jnp.sum(grads, axis=0, keepdims=True)
        pulled = grads * vectors[3:4]
        pulled = (
            pulled
            - jnp.mean(pulled, axis=-1, keepdims=True)
            - scaled * jnp.mean(pulled * scaled, axis=-1, keepdims=True)
        )
        grad_hidden = above[...].astype(wide) + inverse * pulled
        grad_hidden_ref[...] = grad_hidden
        weighted = (grad_hidden * gates[:, 0:1]).astype(low)
        packed_ref[...] = dot(placing[...], weighted, 0, 0).astype(low)
        unpacked = dot(placing[...], returned[...])
        logit_ref[...] = gates[:, 1:2] * jnp.sum(grad_hidden * unpacked, axis=-1, keepdims=True)


def token_backward(above, hidden, active, slope, placing, returned, gates, vectors, w_up, parts):
    count, width = above.shape
    slots = placing.shape[1]
    blocks = w_up.shape[0]
    fetched = (above, placing, returned, gates, vectors)
    return pl.pallas_call(
        backward_kernel,
        grid=(blocks,),
        out_shape=(
            jax.ShapeDtypeStruct((count, width), low),
            jax.ShapeDtypeStruct((slots, width), low),
            jax.ShapeDtypeStruct((count, width), wide),
            jax.ShapeDtypeStruct((count, 1), wide),
            jax.ShapeDtypeStruct((2, width), wide),
            jax.ShapeDtypeStruct((blocks, count, width), low),
        ),
        in_specs=[whole(value) for value in fetched] + [on_chip()] * 8,
        out_specs=(on_chip(),) * 6,
        scratch_shapes=[
            pltpu.VMEM((count, width), wide),
            pltpu.VMEM((count, width), wide),
            pltpu.VMEM((width, width), low),
        ],
        compiler_params=params(30),
        cost_estimate=cost(8 * blocks * count * width * width, 8 * blocks * width * width),
    )(*fetched, hidden, active, slope, w_up, *parts)


def outer_kernel(left, right, theirs_ref):
    core = lax.axis_index("own")
    step = pl.program_id(0)
    columns = theirs_ref.shape[2]
    left_step = step if left.shape[0] > 1 else 0
    right_step = step if right.shape[0] > 1 else 0
    part = pl.ds(pl.multiple_of((1 - core) * columns, columns), columns)
    theirs_ref[step] = dot(left[left_step], right[right_step, :, part], 0, 0).astype(low)


def outer_theirs(left, right):
    count, width = left.shape[1:]
    blocks = max(left.shape[0], right.shape[0])
    return pl.pallas_call(
        outer_kernel,
        grid=(blocks,),
        out_shape=jax.ShapeDtypeStruct((blocks, width, width // 2), low),
        in_specs=[on_chip()] * 2,
        out_specs=on_chip(),
        compiler_params=params(8),
        cost_estimate=cost(blocks * count * width * width, 3 * blocks * width * width),
    )(left, right)


def column(values):
    return values[:, None]


def pack_kernel(
    tokens, chosen, packing, vectors, placing_ref, packed_ref, gates_ref
):
    count = tokens.shape[0]
    capacity = packing.shape[0]
    center, inverse = normal_parts(tokens[...].astype(wide))
    first = (center * inverse * vectors[0:1] + vectors[1:2]).astype(low)
    gate = jax.nn.sigmoid(jnp.sum(first.astype(wide) * vectors[2:3], axis=-1, keepdims=True))
    weighting = jnp.where(chosen[...] == 1, gate, 0.0)
    gates_ref[:, 0:1] = weighting
    gates_ref[:, 1:2] = weighting * (1.0 - gate)
    above = lax.broadcasted_iota(jnp.int32, (count, count), 0)
    below = lax.broadcasted_iota(jnp.int32, (count, count), 1)
    earlier = (below <= above).astype(wide).astype(low)
    flags = jnp.broadcast_to(chosen[...].astype(wide), (count, capacity))
    rank = dot(earlier, flags.astype(low))
    place_of = lax.broadcasted_iota(jnp.int32, (count, capacity), 1).astype(wide) + 1.0
    ranked = jnp.where(rank == place_of, flags, 0.0).astype(low)
    slots = lax.broadcasted_iota(jnp.int32, (capacity, capacity), 1)
    slot_of = (packing[...] == slots).astype(wide).astype(low)
    placing = dot(ranked, slot_of).astype(low)
    placing_ref[...] = placing
    packed_ref[...] = dot(placing, first, 0, 0).astype(low)


def pack_tokens(tokens, chosen, packing, vectors):
    count, width = tokens.shape
    capacity = packing.shape[0]
    return pl.pallas_call(
        pack_kernel,
        out_shape=(
            jax.ShapeDtypeStruct((count, capacity), low),
            jax.ShapeDtypeStruct((capacity, width), low),
            jax.ShapeDtypeStruct((count, 2), wide),
        ),
        in_specs=[on_chip()] * 4,
        out_specs=(on_chip(),) * 3,
        compiler_params=params(10),
        cost_estimate=cost(4 * count * capacity * width, 8 * count * width),
    )(tokens, column(chosen), column(packing), vectors)


def token_back_kernel(*refs):
    sources, (out_ref, vector_ref), fetched, sems = refs[:6], refs[6:8], refs[8:14], refs[14]
    finish(fetch(sources, fetched, sems))
    tokens, placing, grad_sent, grad_hidden, grad_logit, vectors = fetched
    grad_first = dot(placing[...], grad_sent[...]) + grad_logit[...] * vectors[2:3]
    center, inverse = normal_parts(tokens[...].astype(wide))
    scaled = center * inverse
    vector_ref[0:1] = jnp.sum(grad_first * scaled, axis=0, keepdims=True)
    vector_ref[1:2] = jnp.sum(grad_first, axis=0, keepdims=True)
    first = (scaled * vectors[0:1] + vectors[1:2]).astype(low).astype(wide)
    vector_ref[2:3] = jnp.sum(grad_logit[...] * first, axis=0, keepdims=True)
    pulled = grad_first * vectors[0:1]
    pulled = (
        pulled
        - jnp.mean(pulled, axis=-1, keepdims=True)
        - scaled * jnp.mean(pulled * scaled, axis=-1, keepdims=True)
    )
    out_ref[...] = (grad_hidden[...] + inverse * pulled).astype(low)


def token_back(tokens, placing, grad_sent, grad_hidden, grad_logit, vectors):
    count, width = tokens.shape
    return pl.pallas_call(
        token_back_kernel,
        out_shape=(
            jax.ShapeDtypeStruct((count, width), low),
            jax.ShapeDtypeStruct((3, width), wide),
        ),
        in_specs=[in_hbm()] * 6,
        out_specs=(on_chip(),) * 2,
        scratch_shapes=fetch_scratch(
            (tokens, placing, grad_sent, grad_hidden, grad_logit, vectors)
        ),
        compiler_params=params(17),
        cost_estimate=cost(2 * count * width * placing.shape[1], 12 * count * width),
    )(tokens, placing, grad_sent, grad_hidden, grad_logit, vectors)


def flip_pairs(flip):
    return [(i, i ^ flip) for i in range(32)]


def all_sum(value):
    value = value + send(value, swap_pairs())
    for one, two in ((2, 4), (8, 16)):
        near = value + send(value, flip_pairs(one))
        far = send(value, flip_pairs(two)) + send(value, flip_pairs(one + two))
        value = near + far
    return value


def exchange(value, n_data):
    capacity, width = value.shape
    moved = lax.all_to_all(
        value.reshape(n_data, capacity // n_data, width), "dp", split_axis=0, concat_axis=0, tiled=True
    )
    return moved.reshape(capacity, width)


def block_shards(
    tokens,
    cotangent,
    selected,
    packing,
    segments,
    blocks,
    left_stat,
    right_stat,
    left_root,
    right_root,
    vectors,
    moment,
):
    model_width = tokens.shape[2]
    token_count = tokens.shape[0] * tokens.shape[1]
    n_data = lax.axis_size("dp")
    capacity = packing.shape[1]
    line, place, core = here()
    own_tokens = tokens.reshape(token_count, model_width)
    above = cotangent.reshape(token_count, model_width)
    segment = segments[0]

    every = columns_by_core(jnp.transpose(blocks, (1, 0, 2)).astype(low))
    placing, packed, gates = pack_tokens(
        own_tokens, selected.reshape(token_count), packing[0], vectors
    )
    buffer = exchange(packed, n_data)
    attn_two = send(every[:4], line_pairs(2))
    ffn_got = send(after(every[4:], attn_two), line_pairs(2))
    attn_pair = jnp.stack([every[:4], attn_two])
    attn_got = send(attn_pair, line_pairs(1))
    line_attn = after(jnp.concatenate([attn_pair, attn_got]), packed, ffn_got)
    ffn_two = jnp.stack([every[4:], after(ffn_got, attn_got)])
    near_attn = send(line_attn, plane_pairs(0))
    every_root = roots_by_core(after(left_root, ffn_two), right_root)
    first_attn = after(jnp.stack([line_attn, near_attn]), every_root, buffer)
    far_attn = send(first_attn, plane_pairs(1))
    line_ffn = gather_far(ffn_two)
    near_ffn = send(after(line_ffn, near_attn), plane_pairs(0))
    w_parts = with_other(first_attn, far_attn)
    answer, store = attend(buffer, w_parts, segment)
    root_given = lax.optimization_barrier((*roots_given(every_root), buffer, line_ffn))[:4]
    root_parts = [root_given[0]]
    for flip in (1, 2, 3):
        root_parts.append(send(root_given[flip], line_pairs(flip)))
    first_ffn = jnp.stack([line_ffn, near_ffn])
    returned = exchange(answer, n_data)
    far_ffn = after(send(after(first_ffn, far_attn), plane_pairs(1)), returned)
    left_line, right_line = (jnp.stack([part[:, kind] for part in root_parts]) for kind in range(2))
    ffn_parts = with_other(first_ffn, far_ffn)

    hidden, second_low, active, slope, w_up = token_forward(
        own_tokens, placing, after(returned, *root_given), gates, vectors, ffn_parts
    )
    down_theirs = outer_theirs(active, above[None])
    down_got = send(down_theirs, swap_pairs())
    down_give, *down_kept = sum_start(lambda step: step, active, above[None], down_got)
    down_got = send(down_give, plane_pairs(0))
    mixed, grad_packed, grad_hidden, grad_logit, vector_two, grad_inner = token_backward(
        above,
        hidden,
        active,
        slope,
        placing,
        returned,
        gates,
        vectors,
        after(w_up, down_give),
        ffn_parts,
    )
    grad_answer = exchange(grad_packed, n_data)
    up_theirs = outer_theirs(after(second_low, down_got, *root_parts[1:])[None], grad_inner)

    down_kept, down_give = add_first(down_got, *down_kept)
    down_got = send(down_give, plane_pairs(1))
    near_right = send(right_line, plane_pairs(0))
    up_got = send(up_theirs, swap_pairs())
    up_give, *up_kept = sum_start(
        lambda step: 0, second_low[None], grad_inner, after(up_got, down_got, near_right)
    )
    down_own, down_two, down_give = cut_line((down_kept + down_got.astype(wide))[None])
    down_got = send(down_give, line_pairs(1))
    first_right = jnp.stack([right_line, near_right])
    far_right = send(first_right, plane_pairs(1))
    up_got = send(after(up_give, grad_answer), plane_pairs(0))
    attn_theirs, grads, grad_buffer, sides = attend_back(
        store, segment, after(grad_answer, up_give, down_got, far_right)
    )
    down_own, down_give = add_line(down_own, down_two, down_got)
    down_got = send(down_give, line_pairs(2))
    roots = (left_line, send(left_line, swap_pairs()), first_right, far_right)
    attn_got = send(after(attn_theirs, up_got, down_got), swap_pairs())
    grad_sent = exchange(after(grad_buffer, up_got), n_data)
    down_own = (down_own + down_got.astype(wide)).astype(low)
    down_near = send(down_own, plane_pairs(0))
    attn_give, *attn_kept = sum_start(
        lambda step: step // 3, sides, grads, after(attn_got, down_near)
    )
    attn_got = send(attn_give, plane_pairs(0))
    down_first = jnp.stack([down_own, down_near])
    down_far = send(down_first, plane_pairs(1))
    down_mine = jnp.concatenate([down_first, down_far])
    down_theirs = send(down_mine, swap_pairs())

    up_kept, up_give = add_first(up_got, *up_kept)
    attn_kept, attn_give = add_first(after(attn_got, down_far), *attn_kept)
    pair_got = send(jnp.stack([attn_give, up_give]), plane_pairs(1))
    down_made, down_square = step_chunks(down_mine, down_theirs, roots, 2)
    down = return_chunks(down_made)
    pair_got = after(pair_got, down_made, grad_sent)
    pair_kept = jnp.stack([attn_kept, up_kept]) + pair_got.astype(wide)
    pair_own, pair_two, pair_give = cut_line(pair_kept)
    pair_got = send(after(pair_give, *down[1:]), line_pairs(1))
    grad_tokens, vector_one = token_back(
        own_tokens, placing, grad_sent, grad_hidden, grad_logit, vectors
    )
    pair_own, pair_give = add_line(pair_own, pair_two, pair_got)
    pair_got = send(after(pair_give, vector_one), line_pairs(2))
    down = jnp.stack(down)
    down_other = send(down, [(i, i ^ 1) for i in range(0, 32, 2)])
    pair_own = (pair_own + after(pair_got, down_other).astype(wide)).astype(low)
    pair_near = send(pair_own, plane_pairs(0))
    pair_first = jnp.stack([pair_own, pair_near])
    pair_far = send(pair_first, plane_pairs(1))
    pair_mine = jnp.concatenate([pair_first, pair_far])
    pair_theirs = send(pair_mine, swap_pairs())
    pair_made, pair_square = step_chunks(pair_mine, pair_theirs, roots, 0)
    pair = jnp.stack(return_chunks(pair_made))
    pair_other = send(pair, swap_pairs())
    squares = jnp.concatenate([jnp.sum(pair_square, axis=2), jnp.sum(down_square, axis=2)])
    lane = lax.broadcasted_iota(jnp.int32, (1, model_width), 1)
    square_row = sum(
        jnp.where(lane == 4 * chunk + line, squares[chunk], 0.0) for chunk in range(3)
    )
    sums = all_sum(jnp.concatenate([vector_one, vector_two, square_row]))
    vector_grad = sums[:5]
    size = model_width * model_width
    scales = block_rate * lax.rsqrt(sums[5, :12] / size + norm_eps)
    grad_own, left_new, right_new, new_blocks = update_blocks(
        pair, pair_other, down, down_other, blocks, left_stat, right_stat, scales
    )
    moment_new = 0.5 * moment + 0.5 * vector_grad
    row_squares = jnp.mean(moment_new * moment_new, axis=1, keepdims=True)
    vector_new = vectors - vector_rate * moment_new * lax.rsqrt(row_squares + norm_eps)
    return (
        mixed.reshape(tokens.shape),
        grad_tokens.reshape(tokens.shape),
        grad_own,
        left_new,
        right_new,
        new_blocks,
        vector_grad,
        moment_new,
        vector_new,
    )


def shards(
    tokens,
    cotangent,
    selected,
    packing,
    segments,
    blocks,
    left_stat,
    right_stat,
    left_root,
    right_root,
    vectors,
    moment,
):
    model_width = tokens.shape[2]
    token_count = tokens.shape[0] * tokens.shape[1]
    n_data = lax.axis_size("dp")
    n_owner = lax.axis_size("own")
    shard_rows = blocks.shape[0]
    own_blocks = blocks.shape[1]
    up_blocks = (own_blocks * n_owner - 4) // 2
    capacity = packing.shape[1]
    per_peer = capacity // n_data
    head_count = model_width // HEAD_DIM
    score_scale = HEAD_DIM ** (-0.5)
    flat_weights = blocks.astype(jnp.bfloat16).reshape(1, shard_rows * own_blocks * model_width)
    gathered = lax.all_gather(flat_weights, ("dp", "own"), axis=0, tiled=True)
    gathered = gathered.reshape(n_data, n_owner, shard_rows, own_blocks, model_width)

    def matrix(number):
        return gathered[:, number // own_blocks, :, number % own_blocks, :].reshape(
            model_width, model_width
        )

    w_query = matrix(0)
    w_key = matrix(1)
    w_value = matrix(2)
    w_out = matrix(3)
    w_up = jnp.concatenate([matrix(4 + position) for position in range(up_blocks)], axis=1)
    w_down = jnp.concatenate(
        [matrix(4 + up_blocks + position) for position in range(up_blocks)], axis=0
    )
    inputs = tokens.reshape(token_count, model_width).astype(jnp.float32)
    chosen = selected.reshape(token_count)
    normed_one, norm_one_back = jax.vjp(layer_norm, inputs, vectors[0], vectors[1])
    first_low = normed_one.astype(jnp.bfloat16)
    first_wide = first_low.astype(jnp.float32)
    gate_values = jax.nn.sigmoid(jnp.dot(first_wide, vectors[2], precision=highest))
    before = jnp.cumsum(chosen) - 1
    slot_index = jnp.where(chosen == 1, packing[0][jnp.clip(before, 0, capacity - 1)], -1)
    placing = (slot_index[None, :] == jnp.arange(capacity, dtype=jnp.int32)[:, None]).astype(
        jnp.bfloat16
    )
    packed = jnp.dot(placing, first_low, preferred_element_type=jnp.float32).astype(jnp.bfloat16)
    buffer = lax.all_to_all(
        packed.reshape(n_data, per_peer, model_width), "dp", split_axis=0, concat_axis=0, tiled=True
    )
    buffer = buffer.reshape(capacity, model_width)

    def project(matrix_in):
        made = jnp.dot(buffer, matrix_in, preferred_element_type=jnp.float32).astype(jnp.bfloat16)
        return made.reshape(capacity, head_count, HEAD_DIM)

    query_rows = project(w_query)
    key_rows = project(w_key)
    value_rows = project(w_value)
    segment = segments[0]
    block_rows = math.gcd(capacity, 512)
    starts = jnp.arange(capacity // block_rows, dtype=jnp.int32) * block_rows

    def masked_scores():
        scores = (
            jnp.einsum("qhd,khd->hqk", query_rows, key_rows, preferred_element_type=jnp.float32)
            * score_scale
        )
        same_segment = segment[:, None] == segment[None, :]
        return (jnp.where(same_segment[None, :, :], scores, -1e30), query_rows)

    def forward_block(first_row):
        scores, unused_block = masked_scores()
        largest = jnp.max(scores, axis=-1, keepdims=True)
        raised = jnp.exp(scores - largest)
        row_total = jnp.sum(raised, axis=-1, keepdims=True)
        shares = (raised / row_total).astype(jnp.bfloat16)
        context_part = jnp.einsum(
            "hqk,khd->qhd", shares, value_rows, preferred_element_type=jnp.float32
        )
        return (context_part.astype(jnp.bfloat16), largest[..., 0] + jnp.log(row_total[..., 0]))

    context_blocks, lse_blocks = lax.map(forward_block, starts)
    context = context_blocks.reshape(capacity, model_width)
    answer = jnp.dot(context, w_out, preferred_element_type=jnp.float32).astype(jnp.bfloat16)
    returned = lax.all_to_all(
        answer.reshape(n_data, per_peer, model_width), "dp", split_axis=0, concat_axis=0, tiled=True
    )
    returned = returned.reshape(capacity, model_width)
    unpacked = jnp.einsum("mt,md->td", placing, returned, preferred_element_type=jnp.float32)
    weighting = jnp.where(chosen == 1, gate_values, 0.0)
    hidden = inputs + weighting[:, None] * unpacked
    normed_two, norm_two_back = jax.vjp(layer_norm, hidden, vectors[3], vectors[4])
    second_low = normed_two.astype(jnp.bfloat16)
    pre_active = jnp.dot(second_low, w_up, preferred_element_type=jnp.float32)
    active_wide, gelu_back = jax.vjp(gelu_exact, pre_active)
    active = active_wide.astype(jnp.bfloat16)
    result = hidden + jnp.dot(active, w_down, preferred_element_type=jnp.float32)
    mixed = result.astype(jnp.bfloat16).reshape(tokens.shape)
    upstream = cotangent.reshape(token_count, model_width)
    grad_down = jnp.einsum("tf,td->fd", active, upstream, preferred_element_type=jnp.float32)
    grad_active = jnp.einsum("td,fd->tf", upstream, w_down, preferred_element_type=jnp.float32)
    grad_inner = gelu_back(grad_active)[0].astype(jnp.bfloat16)
    grad_up = jnp.einsum("td,tf->df", second_low, grad_inner, preferred_element_type=jnp.float32)
    grad_second = jnp.einsum("tf,df->td", grad_inner, w_up, preferred_element_type=jnp.float32)
    grad_hidden_part, grad_gain_two, grad_bias_two = norm_two_back(grad_second)
    grad_hidden = upstream.astype(jnp.float32) + grad_hidden_part
    grad_token_back = (grad_hidden * weighting[:, None]).astype(jnp.bfloat16)
    grad_packed = jnp.dot(placing, grad_token_back, preferred_element_type=jnp.float32).astype(
        jnp.bfloat16
    )
    router_pull = jnp.where(chosen == 1, jnp.sum(grad_hidden * unpacked, axis=-1), 0.0)
    grad_logit = router_pull * gate_values * (1.0 - gate_values)
    grad_answer = lax.all_to_all(
        grad_packed.reshape(n_data, per_peer, model_width),
        "dp",
        split_axis=0,
        concat_axis=0,
        tiled=True,
    )
    grad_answer = grad_answer.reshape(capacity, model_width)
    grad_out = jnp.einsum("md,me->de", context, grad_answer, preferred_element_type=jnp.float32)
    grad_context = jnp.einsum("me,de->md", grad_answer, w_out, preferred_element_type=jnp.float32)
    grad_context = grad_context.astype(jnp.bfloat16).reshape(capacity, head_count, HEAD_DIM)

    def backward_block(running, item_pair):
        first_row, lse_block = item_pair
        scores, query_block = masked_scores()
        shares_wide = jnp.exp(scores - lse_block[..., None])
        grad_shares = jnp.einsum(
            "qhd,khd->hqk", grad_context, value_rows, preferred_element_type=jnp.float32
        )
        inner_sum = jnp.sum(shares_wide * grad_shares, axis=-1, keepdims=True)
        grad_scores = (shares_wide * (grad_shares - inner_sum)).astype(jnp.bfloat16)
        grad_query_block = (
            jnp.einsum("hqk,khd->qhd", grad_scores, key_rows, preferred_element_type=jnp.float32)
            * score_scale
        )
        key_sum = (
            running[0]
            + jnp.einsum(
                "hqk,qhd->khd", grad_scores, query_block, preferred_element_type=jnp.float32
            )
            * score_scale
        )
        value_sum = running[1] + jnp.einsum(
            "hqk,qhd->khd",
            shares_wide.astype(jnp.bfloat16),
            grad_context,
            preferred_element_type=jnp.float32,
        )
        return ((key_sum, value_sum), grad_query_block)

    zeros_init = jnp.zeros((capacity, head_count, HEAD_DIM), jnp.float32)
    (key_total, value_total), query_grads = lax.scan(
        backward_block, (zeros_init, zeros_init), (starts, lse_blocks)
    )
    grad_query = query_grads.reshape(capacity, model_width).astype(jnp.bfloat16)
    grad_key = key_total.reshape(capacity, model_width).astype(jnp.bfloat16)
    grad_value = value_total.reshape(capacity, model_width).astype(jnp.bfloat16)
    grad_w_query = jnp.einsum("md,me->de", buffer, grad_query, preferred_element_type=jnp.float32)
    grad_w_key = jnp.einsum("md,me->de", buffer, grad_key, preferred_element_type=jnp.float32)
    grad_w_value = jnp.einsum("md,me->de", buffer, grad_value, preferred_element_type=jnp.float32)
    grad_buffer = jnp.einsum("me,de->md", grad_query, w_query, preferred_element_type=jnp.float32)
    grad_buffer = grad_buffer + jnp.einsum(
        "me,de->md", grad_key, w_key, preferred_element_type=jnp.float32
    )
    grad_buffer = grad_buffer + jnp.einsum(
        "me,de->md", grad_value, w_value, preferred_element_type=jnp.float32
    )
    grad_buffer = grad_buffer.astype(jnp.bfloat16)
    grad_sent = lax.all_to_all(
        grad_buffer.reshape(n_data, per_peer, model_width),
        "dp",
        split_axis=0,
        concat_axis=0,
        tiled=True,
    )
    grad_sent = grad_sent.reshape(capacity, model_width)
    grad_first = jnp.einsum("mt,md->td", placing, grad_sent, preferred_element_type=jnp.float32)
    grad_first = grad_first + grad_logit[:, None] * vectors[2][None, :]
    grad_router = jnp.sum(grad_logit[:, None] * first_wide, axis=0)
    grad_input_part, grad_gain_one, grad_bias_one = norm_one_back(grad_first)
    grad_tokens = (grad_hidden + grad_input_part).astype(jnp.bfloat16).reshape(tokens.shape)
    pieces = [grad_w_query, grad_w_key, grad_w_value, grad_out]
    pieces = pieces + [
        grad_up[:, position * model_width : (position + 1) * model_width]
        for position in range(up_blocks)
    ]
    pieces = pieces + [
        grad_down[position * model_width : (position + 1) * model_width, :]
        for position in range(up_blocks)
    ]
    local_terms = jnp.stack(pieces, axis=1)
    vector_terms = jnp.stack(
        [grad_gain_one, grad_bias_one, grad_router, grad_gain_two, grad_bias_two]
    )
    partial_value = lax.psum_scatter(local_terms, "dp", scatter_dimension=0, tiled=True)
    grad_own = lax.psum_scatter(
        partial_value.astype(jnp.bfloat16), "own", scatter_dimension=1, tiled=True
    ).astype(jnp.float32)
    vector_grad = lax.psum(vector_terms, ("dp", "own"))
    full_grad = lax.all_gather(grad_own.astype(jnp.bfloat16), "dp", axis=0, tiled=True).astype(
        grad_own.dtype
    )
    row_start = lax.axis_index("dp") * shard_rows
    left_new = 0.5 * left_stat + 0.5 * jnp.einsum(
        "rbk,nbk->rbn", grad_own, full_grad, precision=highest
    )
    column_part = lax.dynamic_slice_in_dim(full_grad, row_start, shard_rows, 2)
    right_new = 0.5 * right_stat + 0.5 * jnp.einsum(
        "nbr,nbk->rbk", column_part, full_grad, precision=highest
    )
    lefted = jnp.einsum("rbn,nbk->rbk", left_root, full_grad, precision=highest)
    precond = jnp.zeros_like(grad_own) + jnp.einsum(
        "rbn,nbk->rbk",
        lefted,
        lax.all_gather(right_root.astype(jnp.bfloat16), "dp", axis=0, tiled=True).astype(
            jnp.float32
        ),
        precision=highest,
    )
    square_sums = lax.psum(jnp.sum(precond * precond, axis=(0, 2)), "dp")
    step_scale = lax.rsqrt(square_sums / (model_width * model_width) + norm_eps)
    new_blocks = blocks - block_rate * precond * step_scale[None, :, None]
    moment_new = 0.5 * moment + 0.5 * vector_grad
    row_squares = jnp.mean(moment_new * moment_new, axis=1, keepdims=True)
    vector_new = vectors - vector_rate * moment_new * lax.rsqrt(row_squares + norm_eps)
    return (
        mixed,
        grad_tokens,
        grad_own,
        left_new,
        right_new,
        new_blocks,
        vector_grad,
        moment_new,
        vector_new,
    )


def solution(mesh):
    placed = (
        P(("dp", "own"), None, None),
        P(("dp", "own"), None, None),
        P(("dp", "own"), None),
        P(("dp", "own"), None),
        P(("dp", "own"), None),
        P("dp", "own", None),
        P("dp", "own", None),
        P("dp", "own", None),
        P("dp", "own", None),
        P("dp", "own", None),
        P(),
        P(),
    )
    small = mesh.shape["dp"] == 16 and mesh.shape["own"] == 2
    return jax.shard_map(
        block_shards if small else shards,
        mesh=mesh,
        in_specs=placed,
        out_specs=(
            P(("dp", "own"), None, None),
            P(("dp", "own"), None, None),
            P("dp", "own", None),
            P("dp", "own", None),
            P("dp", "own", None),
            P("dp", "own", None),
            P(),
            P(),
            P(),
        ),
        check_vma=False,
    )
```

```python
import functools
import math

import jax
import jax.numpy as jnp
from jax import lax
from jax.experimental import pallas as pl
from jax.experimental.pallas import tpu as pltpu
from jax.sharding import PartitionSpec as P

HEAD_DIM = 64


norm_eps = 1e-06
block_rate = 0.03
vector_rate = 0.04
highest = lax.Precision.HIGHEST


def layer_norm(values, norm_gain, norm_bias):
    center = values - jnp.mean(values, axis=-1, keepdims=True)
    spread = jnp.mean(center * center, axis=-1, keepdims=True)
    return center * lax.rsqrt(spread + norm_eps) * norm_gain + norm_bias


def gelu_exact(values):
    return jax.nn.gelu(values, approximate=False)


BOTH = ("dp", "own")
low = jnp.bfloat16
wide = jnp.float32
MIB = 2**20


def swap_pairs():
    return [(i, i ^ 1) for i in range(32)]


def plane_pairs(step):
    pairs = []
    for i in range(32):
        place, core = i // 2, i % 2
        flip = (1, 2)[step ^ core]
        pairs.append((i, (place ^ flip) * 2 + core))
    return pairs


def line_pairs(flip):
    return [(i, i ^ (8 * flip)) for i in range(32)]


def send(value, pairs):
    return lax.ppermute(value, BOTH, pairs)


def after(value, *others):
    return lax.optimization_barrier((value,) + others)[0]


def pick(value, index, axis):
    return lax.dynamic_index_in_dim(value, index, axis, keepdims=False)


def first_core():
    return lax.axis_index("own") == 0


def halves(value):
    middle = value.shape[-1] // 2
    lower, upper = value[..., :middle], value[..., middle:]
    return jnp.where(first_core(), lower, upper), jnp.where(first_core(), upper, lower)


def in_core_order(mine, theirs, axis):
    return jnp.where(
        first_core(),
        jnp.concatenate([mine, theirs], axis=axis),
        jnp.concatenate([theirs, mine], axis=axis),
    )


LINE_FLIPS = (0, 2, 1, 3)


def flipped(index, flip):
    return jnp.bitwise_xor(index, flip)


def spots(place, half):
    first, second = half + 1, 2 - half
    return [
        place,
        flipped(place, first),
        flipped(place, second),
        flipped(place, 3),
    ]


def here():
    device = lax.axis_index("dp")
    return device // 4, device % 4, lax.axis_index("own")


def dot(left, right, left_axis=1, right_axis=0):
    return lax.dot_general(
        left, right, (((left_axis,), (right_axis,)), ((), ())), preferred_element_type=wide
    )


def on_chip():
    return pl.BlockSpec(memory_space=pltpu.VMEM)


def whole(value):
    return pl.BlockSpec(value.shape, lambda *steps: (0,) * value.ndim)


def in_hbm():
    return pl.BlockSpec(memory_space=pltpu.HBM)


def fetch_scratch(values):
    return [pltpu.VMEM(value.shape, value.dtype) for value in values] + [
        pltpu.SemaphoreType.DMA((len(values),))
    ]


def fetch(sources, targets, sems):
    copies = [
        pltpu.make_async_copy(source, target, sems.at[number])
        for number, (source, target) in enumerate(zip(sources, targets))
    ]
    for copy in copies:
        copy.start()
    return copies


def finish(copies):
    for copy in copies:
        copy.wait()


def params(limit):
    return pltpu.CompilerParams(vmem_limit_bytes=limit * MIB)


def cost(flops, moved):
    return pl.CostEstimate(flops=flops, bytes_accessed=moved, transcendentals=0)


def place_block(parts, block, target):
    line, place, core = here()
    rows, columns = parts[0].shape[3:]
    for other in range(2):
        half = core if other == 0 else 1 - core
        column_slice = pl.ds(pl.multiple_of(half * columns, columns), columns)
        for number, spot in enumerate(spots(place, half)):
            for index, flip in enumerate(LINE_FLIPS):
                start = (flipped(line, flip) * 4 + spot) * rows
                row_slice = pl.ds(pl.multiple_of(start, rows), rows)
                piece = parts[2 * other + number // 2][number % 2, index, block]
                target[row_slice, column_slice] = piece


def columns_by_core(value):
    keep, give = halves(value)
    return in_core_order(keep, send(give, swap_pairs()), 0)


def gather_far(pair):
    return jnp.concatenate([pair, send(pair, line_pairs(1))])


def with_other(first, far):
    return [first, far, send(first, swap_pairs()), send(far, swap_pairs())]


def roots_by_core(left_root, right_root):
    both = [jnp.transpose(root, (1, 0, 2)).astype(low) for root in (left_root, right_root)]
    every = columns_by_core(jnp.stack(both, axis=1))
    return every.reshape((3, 4) + every.shape[1:])


def roots_given(every):
    line, place, core = here()
    return [pick(every, flipped(line, flip), 1) for flip in range(4)]


def sum_kernel(left_of, left, right, got, give_ref, kept_ref, passed_ref, total):
    line, place, core = here()
    step = pl.program_id(0)
    columns = got.shape[2]
    rows = kept_ref.shape[2]
    part = pl.ds(pl.multiple_of(core * columns, columns), columns)
    right_step = step if right.shape[0] > 1 else 0
    made = dot(left[left_of(step)], right[right_step, :, part], 0, 0)
    total[...] = made + got[step].astype(wide)
    own, first, second, both = spots(place, core)
    for row_line in range(4):

        def piece(spot):
            return total[pl.ds(pl.multiple_of((row_line * 4 + spot) * rows, rows), rows), :]

        give_ref[0, step, row_line] = piece(first).astype(low)
        give_ref[1, step, row_line] = piece(both).astype(low)
        kept_ref[step, row_line] = piece(own).astype(low)
        passed_ref[step, row_line] = piece(second).astype(low)


def sum_start(left_of, left, right, got):
    count, width = left.shape[1:]
    blocks, full, columns = got.shape
    shape = (blocks, 4, full // 16, columns)
    return pl.pallas_call(
        functools.partial(sum_kernel, left_of),
        grid=(blocks,),
        out_shape=(
            jax.ShapeDtypeStruct((2,) + shape, low),
            jax.ShapeDtypeStruct(shape, low),
            jax.ShapeDtypeStruct(shape, low),
        ),
        in_specs=[on_chip()] * 3,
        out_specs=(on_chip(),) * 3,
        scratch_shapes=[pltpu.VMEM((full, columns), wide)],
        compiler_params=params(12),
        cost_estimate=cost(blocks * count * width * width, 5 * blocks * width * width),
    )(left, right, got)


def add_first(got, kept, passed):
    kept = kept.astype(wide) + got[0].astype(wide)
    return kept, (passed.astype(wide) + got[1].astype(wide)).astype(low)


def cut_line(kept):
    line, place, core = here()
    given = jnp.stack([pick(kept, flipped(line, flip), 1) for flip in (1, 3)]).astype(low)
    return pick(kept, line, 1), pick(kept, flipped(line, 2), 1), given


def add_line(own, two, got):
    return own + got[0].astype(wide), (two + got[1].astype(wide)).astype(low)


def step_kernel(
    number,
    mine,
    theirs,
    left_mine_from,
    left_theirs_from,
    right_first_from,
    right_far_from,
    out_ref,
    square_ref,
    grad_ref,
    rows_ref,
    left_ref,
    right_ref,
    cross_ref,
    left_mine,
    left_theirs,
    right_first,
    right_far,
    sems,
):
    chunk = number + pl.program_id(0)
    copies = fetch(
        [
            left_mine_from.at[:, chunk],
            left_theirs_from.at[:, chunk],
            right_first_from.at[:, :, chunk],
            right_far_from.at[:, :, chunk],
        ],
        [left_mine, left_theirs, right_first, right_far],
        sems,
    )
    line, place, core = here()
    rows, columns = mine.shape[3:]

    def rows_of(row_line, spot):
        return pl.ds(pl.multiple_of((row_line * 4 + spot) * rows, rows), rows)

    def column_half(half):
        return pl.ds(pl.multiple_of(half * columns, columns), columns)

    for half, group in ((core, mine), (1 - core, theirs)):
        for number, spot in enumerate(spots(place, half)):
            for step in range(4):
                grad_ref[rows_of(step, spot), column_half(half)] = group[number, 0, step]
    finish(copies)
    for half, left in ((core, left_mine), (1 - core, left_theirs)):
        for flip in range(4):
            target = pl.ds(pl.multiple_of(flipped(line, flip) * rows, rows), rows)
            left_ref[target, column_half(half)] = left[flip]
    for number, spot in enumerate(spots(place, core)):
        source = right_far if number > 1 else right_first
        for flip in range(4):
            right_ref[rows_of(flipped(line, flip), spot), :] = source[number % 2, flip]
    for row_line in range(4):
        rows_ref[row_line * rows : (row_line + 1) * rows, :] = grad_ref[rows_of(row_line, place), :]
    left = dot(rows_ref[...], grad_ref[column_half(core), :], 1, 1)
    cross_ref[...] = dot(grad_ref[...], grad_ref[:, column_half(core)], 0, 0)
    lefted = dot(left_ref[...], grad_ref[...]).astype(low)
    stepped = dot(lefted, right_ref[...])
    square_ref[0] = jnp.sum(stepped * stepped, axis=0, keepdims=True)
    for row_line in range(4):
        part = slice(row_line * rows, (row_line + 1) * rows)
        out_ref[0, row_line, 0] = mine[0, 0, row_line]
        out_ref[0, row_line, 1] = left[part].astype(low)
        out_ref[0, row_line, 2] = cross_ref[rows_of(row_line, place), :].astype(low)
        out_ref[0, row_line, 3] = stepped[part].astype(low)


def step_chunks(mine, theirs, roots, number):
    chunks, lines, rows, columns = mine.shape[1:]
    full = rows * 16
    grad_spec = pl.BlockSpec((4, 1, lines, rows, columns), lambda step: (0, step, 0, 0, 0))
    return pl.pallas_call(
        functools.partial(step_kernel, number),
        grid=(chunks,),
        out_shape=(
            jax.ShapeDtypeStruct((chunks, lines, 4, rows, columns), low),
            jax.ShapeDtypeStruct((chunks, 1, columns), wide),
        ),
        in_specs=[grad_spec] * 2 + [in_hbm()] * 4,
        out_specs=(
            pl.BlockSpec((1, lines, 4, rows, columns), lambda step: (step, 0, 0, 0, 0)),
            pl.BlockSpec((1, 1, columns), lambda step: (step, 0, 0)),
        ),
        scratch_shapes=[
            pltpu.VMEM((full, columns * 2), low),
            pltpu.VMEM((lines * rows, columns * 2), low),
            pltpu.VMEM((lines * rows, columns * 2), low),
            pltpu.VMEM((full, columns), low),
            pltpu.VMEM((full, columns), wide),
            pltpu.VMEM((lines, rows, columns), low),
            pltpu.VMEM((lines, rows, columns), low),
            pltpu.VMEM((2, lines, rows, columns), low),
            pltpu.VMEM((2, lines, rows, columns), low),
            pltpu.SemaphoreType.DMA((4,)),
        ],
        compiler_params=params(15),
        cost_estimate=cost(3 * chunks * full**3, 16 * chunks * full * full),
    )(mine, theirs, *roots)


def return_chunks(made):
    line, place, core = here()
    parts = [pick(made, line, 1)]
    for flip in (1, 2, 3):
        parts.append(send(pick(made, flipped(line, flip), 1), line_pairs(flip)))
    return parts


def last_kernel(
    pair, pair_other, down, down_other, blocks, left_stat, right_stat, scales, *outs
):
    grad_out, left_out, right_out, block_out = outs
    line, place, core = here()
    columns = pair.shape[4]

    def update(number, which, mine, theirs):
        for (source, index), half in ((mine, which), (theirs, 1 - which)):
            part = slice(half * columns, (half + 1) * columns)
            pieces = [source[index + (kind,)].astype(wide) for kind in range(4)]
            grad_out[number, :, part] = pieces[0]
            left_out[number, :, part] = 0.5 * left_stat[number, :, part] + 0.5 * pieces[1]
            right_out[number, :, part] = 0.5 * right_stat[number, :, part] + 0.5 * pieces[2]
            step = pieces[3] * scales[6 * which + number]
            block_out[number, :, part] = blocks[number, :, part] - step

    @pl.when(core == 0)
    def first():
        for number in range(6):
            index = (flipped(line, number % 4), number // 4)
            update(number, 0, (pair, index), (pair_other, index))

    @pl.when(core == 1)
    def second():
        for number in range(6):
            source, other = (pair, pair_other) if number < 2 else (down, down_other)
            index = (flipped(line, (number + 2) % 4), 1 if number < 2 else 0)
            update(number, 1, (source, index), (other, index))


def update_blocks(pair, pair_other, down, down_other, blocks, left_stat, right_stat, scales):
    turned = [jnp.transpose(value, (1, 0, 2)) for value in (blocks, left_stat, right_stat)]
    shape = jax.ShapeDtypeStruct(turned[0].shape, wide)
    outs = pl.pallas_call(
        last_kernel,
        out_shape=(shape,) * 4,
        in_specs=[on_chip()] * 7 + [pl.BlockSpec(memory_space=pltpu.SMEM)],
        out_specs=(on_chip(),) * 4,
        compiler_params=params(10),
        cost_estimate=cost(0, 32 * shape.size),
    )(pair, pair_other, down, down_other, *turned, scales)
    return [jnp.transpose(value, (1, 0, 2)) for value in outs]


def head_masks():
    lane = lax.broadcasted_iota(jnp.int32, (1, 2 * HEAD_DIM), 1)
    return [(lane < HEAD_DIM).astype(wide).astype(low), (lane >= HEAD_DIM).astype(wide).astype(low)]


def head_shares(query, key, same):
    scores = dot(query, key, 1, 1) * HEAD_DIM ** (-0.5)
    scores = jnp.where(same, scores, -1e30)
    raised = jnp.exp(scores - jnp.max(scores, axis=-1, keepdims=True))
    return raised / jnp.sum(raised, axis=-1, keepdims=True)


STORE_ROWS = 32768


def store_views(store, rows, width):
    weights = [store.at[pl.ds(block * width, width)] for block in range(4)]
    made = [store.at[pl.ds(4 * width + kind * rows, rows)] for kind in range(3)]
    sides = [store.at[pl.ds(4 * width + (3 + side) * rows, rows)] for side in range(2)]
    return weights, made, sides


def attend_kernel(
    buffer, one, two, three, four, seg_column, seg_row, answer_ref, store, weights, made, sides, sems
):
    rows, width = buffer.shape
    weights_out, made_out, sides_out = store_views(store, rows, width)
    for block in range(4):
        place_block((one, two, three, four), block, weights.at[block])
    copies = fetch([weights.at[block] for block in range(4)], weights_out, sems)
    same = seg_column[...] == seg_row[...]
    for kind in range(3):
        made[kind] = dot(buffer[...], weights[kind]).astype(low)
    copies += fetch([made.at[kind] for kind in range(3)], made_out, sems.at[pl.ds(4, 3)])
    pair_width = 2 * HEAD_DIM
    for pair in range(width // pair_width):
        part = slice(pair * pair_width, (pair + 1) * pair_width)
        query, key, value = (made[kind, :, part] for kind in range(3))
        context = None
        for mask in head_masks():
            shares = head_shares(query, key * mask, same).astype(low)
            term = dot(shares, value * mask)
            context = term if context is None else context + term
        sides[1, :, part] = context.astype(low)
    sides[0] = buffer[...]
    copies += fetch([sides.at[side] for side in range(2)], sides_out, sems.at[pl.ds(7, 2)])
    answer_ref[...] = dot(sides[1], weights[3]).astype(low)
    finish(copies)


def attend_scratch(rows, width):
    return [
        pltpu.VMEM((4, width, width), low),
        pltpu.VMEM((3, rows, width), low),
        pltpu.VMEM((2, rows, width), low),
        pltpu.SemaphoreType.DMA((9,)),
    ]


def attend(buffer, parts, segment):
    rows, width = buffer.shape
    return pl.pallas_call(
        attend_kernel,
        out_shape=(
            jax.ShapeDtypeStruct((rows, width), low),
            jax.ShapeDtypeStruct((STORE_ROWS, width), low),
        ),
        in_specs=[on_chip()] * 7,
        out_specs=(on_chip(), in_hbm()),
        scratch_shapes=attend_scratch(rows, width),
        compiler_params=params(20),
        cost_estimate=cost(12 * rows * width * width, 12 * width * width),
    )(buffer, *parts, segment[:, None], segment[None, :])


def attend_back_kernel(
    store,
    seg_column,
    seg_row,
    grad_answer,
    theirs_ref,
    grads_ref,
    grad_buffer_ref,
    sides,
    grad_context_ref,
    weights,
    made,
    sems,
):
    rows, width = grad_answer.shape
    weights_from, made_from, sides_from = store_views(store, rows, width)
    out_copy, *copies = fetch(
        [weights_from[3]] + made_from + sides_from + weights_from[:3],
        [weights.at[3]]
        + [made.at[kind] for kind in range(3)]
        + [sides.at[side] for side in range(2)]
        + [weights.at[block] for block in range(3)],
        sems,
    )
    same = seg_column[...] == seg_row[...]
    core = lax.axis_index("own")
    out_copy.wait()
    grad_context_ref[...] = dot(grad_answer[...], weights[3], 1, 1).astype(low)
    finish(copies[:3])
    grads_ref[3] = grad_answer[...]
    pair_width = 2 * HEAD_DIM
    for pair in range(width // pair_width):
        part = slice(pair * pair_width, (pair + 1) * pair_width)
        query, key, value = (made[kind, :, part] for kind in range(3))
        above = grad_context_ref[:, part]
        sums = [None] * 3
        for mask in head_masks():
            key_head = key * mask
            shares = head_shares(query, key_head, same)
            grad_shares = dot(above, value * mask, 1, 1)
            inner = jnp.sum(shares * grad_shares, axis=-1, keepdims=True)
            grad_scores = (shares * (grad_shares - inner)).astype(low)
            terms = (
                dot(grad_scores, key_head),
                dot(grad_scores, query * mask, 0, 0),
                dot(shares.astype(low), above * mask, 0, 0),
            )
            sums = [
                term if total is None else total + term for term, total in zip(terms, sums)
            ]
        for kind, factor in enumerate((HEAD_DIM ** (-0.5), HEAD_DIM ** (-0.5), 1.0)):
            grads_ref[kind, :, part] = (sums[kind] * factor).astype(low)
    finish(copies[3:5])
    columns = theirs_ref.shape[2]
    part = pl.ds(pl.multiple_of((1 - core) * columns, columns), columns)
    for kind in range(4):
        theirs_ref[kind] = dot(sides[kind // 3], grads_ref[kind, :, part], 0, 0).astype(low)
    finish(copies[5:])
    total = dot(grads_ref[0], weights[0], 1, 1)
    total = total + dot(grads_ref[1], weights[1], 1, 1)
    total = total + dot(grads_ref[2], weights[2], 1, 1)
    grad_buffer_ref[...] = total.astype(low)


def attend_back(store, segment, grad_answer):
    rows, width = grad_answer.shape
    weights, made, sides, sems = attend_scratch(rows, width)
    return pl.pallas_call(
        attend_back_kernel,
        out_shape=(
            jax.ShapeDtypeStruct((4, width, width // 2), low),
            jax.ShapeDtypeStruct((4, rows, width), low),
            jax.ShapeDtypeStruct((rows, width), low),
            jax.ShapeDtypeStruct((2, rows, width), low),
        ),
        in_specs=[in_hbm()] + [on_chip()] * 3,
        out_specs=(on_chip(),) * 4,
        scratch_shapes=[pltpu.VMEM((rows, width), low), weights, made, sems],
        compiler_params=params(18),
        cost_estimate=cost(20 * rows * width * width, 16 * width * width),
    )(store, segment[:, None], segment[None, :], grad_answer)


def normal_parts(values):
    center = values - jnp.mean(values, axis=-1, keepdims=True)
    spread = jnp.mean(center * center, axis=-1, keepdims=True)
    return center, lax.rsqrt(spread + norm_eps)


def forward_kernel(*refs):
    tokens, placing, returned, gates, vectors = refs[:5]
    parts = refs[5:9]
    hidden_ref, second_ref, active_ref, slope_ref, w_up = refs[9:14]
    step = pl.program_id(0)

    @pl.when(step == 0)
    def prepare():
        values = tokens[...].astype(wide) + gates[:, 0:1] * dot(placing[...], returned[...])
        hidden_ref[...] = values
        center, inverse = normal_parts(values)
        second_ref[...] = (center * inverse * vectors[3:4] + vectors[4:5]).astype(low)

    place_block(parts, step, w_up.at[step])
    before = dot(second_ref[...], w_up[step])
    share = 0.5 + 0.5 * lax.erf(before * (0.5**0.5))
    density = jnp.exp(before * before * -0.5) * (0.5 / math.pi) ** 0.5
    active_ref[step] = (before * share).astype(low)
    slope_ref[step] = (share + before * density).astype(low)


def token_forward(tokens, placing, returned, gates, vectors, parts):
    count, width = tokens.shape
    blocks = parts[0].shape[2] // 2
    by_block = jax.ShapeDtypeStruct((blocks, count, width), low)
    fetched = (tokens, placing, returned, gates, vectors)
    return pl.pallas_call(
        forward_kernel,
        grid=(blocks,),
        out_shape=(
            jax.ShapeDtypeStruct((count, width), wide),
            jax.ShapeDtypeStruct((count, width), low),
            by_block,
            by_block,
            jax.ShapeDtypeStruct((blocks, width, width), low),
        ),
        in_specs=[whole(value) for value in fetched] + [on_chip()] * 4,
        out_specs=(on_chip(),) * 5,
        compiler_params=params(18),
        cost_estimate=cost(8 * blocks * count * width * width, 8 * blocks * width * width),
    )(*fetched, *parts)


def backward_kernel(*refs):
    above, placing, returned, gates, vectors = refs[:5]
    (hidden, active, slope, w_up), parts = refs[5:9], refs[9:13]
    mixed_ref, packed_ref, grad_hidden_ref, logit_ref, vector_ref, inner_ref = refs[13:19]
    result, grad_second, w_down = refs[19:22]
    step = pl.program_id(0)
    place_block(parts, 4 + step, w_down)

    @pl.when(step == 0)
    def prepare():
        result[...] = hidden[...]
        grad_second[...] = jnp.zeros_like(grad_second)

    grad_active = dot(above[...], w_down[...], 1, 1)
    grad_inner = (grad_active * slope[step].astype(wide)).astype(low)
    inner_ref[step] = grad_inner
    result[...] += dot(active[step], w_down[...])
    grad_second[...] += dot(grad_inner, w_up[step], 1, 1)

    @pl.when(step == pl.num_programs(0) - 1)
    def complete():
        mixed_ref[...] = result[...].astype(low)
        center, inverse = normal_parts(hidden[...])
        scaled = center * inverse
        grads = grad_second[...]
        vector_ref[0:1] = jnp.sum(grads * scaled, axis=0, keepdims=True)
        vector_ref[1:2] = jnp.sum(grads, axis=0, keepdims=True)
        pulled = grads * vectors[3:4]
        pulled = (
            pulled
            - jnp.mean(pulled, axis=-1, keepdims=True)
            - scaled * jnp.mean(pulled * scaled, axis=-1, keepdims=True)
        )
        grad_hidden = above[...].astype(wide) + inverse * pulled
        grad_hidden_ref[...] = grad_hidden
        weighted = (grad_hidden * gates[:, 0:1]).astype(low)
        packed_ref[...] = dot(placing[...], weighted, 0, 0).astype(low)
        unpacked = dot(placing[...], returned[...])
        logit_ref[...] = gates[:, 1:2] * jnp.sum(grad_hidden * unpacked, axis=-1, keepdims=True)


def token_backward(above, hidden, active, slope, placing, returned, gates, vectors, w_up, parts):
    count, width = above.shape
    slots = placing.shape[1]
    blocks = w_up.shape[0]
    fetched = (above, placing, returned, gates, vectors)
    return pl.pallas_call(
        backward_kernel,
        grid=(blocks,),
        out_shape=(
            jax.ShapeDtypeStruct((count, width), low),
            jax.ShapeDtypeStruct((slots, width), low),
            jax.ShapeDtypeStruct((count, width), wide),
            jax.ShapeDtypeStruct((count, 1), wide),
            jax.ShapeDtypeStruct((2, width), wide),
            jax.ShapeDtypeStruct((blocks, count, width), low),
        ),
        in_specs=[whole(value) for value in fetched] + [on_chip()] * 8,
        out_specs=(on_chip(),) * 6,
        scratch_shapes=[
            pltpu.VMEM((count, width), wide),
            pltpu.VMEM((count, width), wide),
            pltpu.VMEM((width, width), low),
        ],
        compiler_params=params(30),
        cost_estimate=cost(8 * blocks * count * width * width, 8 * blocks * width * width),
    )(*fetched, hidden, active, slope, w_up, *parts)


def outer_kernel(left, right, theirs_ref):
    core = lax.axis_index("own")
    step = pl.program_id(0)
    columns = theirs_ref.shape[2]
    left_step = step if left.shape[0] > 1 else 0
    right_step = step if right.shape[0] > 1 else 0
    part = pl.ds(pl.multiple_of((1 - core) * columns, columns), columns)
    theirs_ref[step] = dot(left[left_step], right[right_step, :, part], 0, 0).astype(low)


def outer_theirs(left, right):
    count, width = left.shape[1:]
    blocks = max(left.shape[0], right.shape[0])
    return pl.pallas_call(
        outer_kernel,
        grid=(blocks,),
        out_shape=jax.ShapeDtypeStruct((blocks, width, width // 2), low),
        in_specs=[on_chip()] * 2,
        out_specs=on_chip(),
        compiler_params=params(8),
        cost_estimate=cost(blocks * count * width * width, 3 * blocks * width * width),
    )(left, right)


def column(values):
    return values[:, None]


def pack_kernel(
    tokens, chosen, packing, vectors, placing_ref, packed_ref, gates_ref
):
    count = tokens.shape[0]
    capacity = packing.shape[0]
    center, inverse = normal_parts(tokens[...].astype(wide))
    first = (center * inverse * vectors[0:1] + vectors[1:2]).astype(low)
    gate = jax.nn.sigmoid(jnp.sum(first.astype(wide) * vectors[2:3], axis=-1, keepdims=True))
    weighting = jnp.where(chosen[...] == 1, gate, 0.0)
    gates_ref[:, 0:1] = weighting
    gates_ref[:, 1:2] = weighting * (1.0 - gate)
    above = lax.broadcasted_iota(jnp.int32, (count, count), 0)
    below = lax.broadcasted_iota(jnp.int32, (count, count), 1)
    earlier = (below <= above).astype(wide).astype(low)
    flags = jnp.broadcast_to(chosen[...].astype(wide), (count, capacity))
    rank = dot(earlier, flags.astype(low))
    place_of = lax.broadcasted_iota(jnp.int32, (count, capacity), 1).astype(wide) + 1.0
    ranked = jnp.where(rank == place_of, flags, 0.0).astype(low)
    slots = lax.broadcasted_iota(jnp.int32, (capacity, capacity), 1)
    slot_of = (packing[...] == slots).astype(wide).astype(low)
    placing = dot(ranked, slot_of).astype(low)
    placing_ref[...] = placing
    packed_ref[...] = dot(placing, first, 0, 0).astype(low)


def pack_tokens(tokens, chosen, packing, vectors):
    count, width = tokens.shape
    capacity = packing.shape[0]
    return pl.pallas_call(
        pack_kernel,
        out_shape=(
            jax.ShapeDtypeStruct((count, capacity), low),
            jax.ShapeDtypeStruct((capacity, width), low),
            jax.ShapeDtypeStruct((count, 2), wide),
        ),
        in_specs=[on_chip()] * 4,
        out_specs=(on_chip(),) * 3,
        compiler_params=params(10),
        cost_estimate=cost(4 * count * capacity * width, 8 * count * width),
    )(tokens, column(chosen), column(packing), vectors)


def token_back_kernel(*refs):
    sources, (out_ref, vector_ref), fetched, sems = refs[:6], refs[6:8], refs[8:14], refs[14]
    finish(fetch(sources, fetched, sems))
    tokens, placing, grad_sent, grad_hidden, grad_logit, vectors = fetched
    grad_first = dot(placing[...], grad_sent[...]) + grad_logit[...] * vectors[2:3]
    center, inverse = normal_parts(tokens[...].astype(wide))
    scaled = center * inverse
    vector_ref[0:1] = jnp.sum(grad_first * scaled, axis=0, keepdims=True)
    vector_ref[1:2] = jnp.sum(grad_first, axis=0, keepdims=True)
    first = (scaled * vectors[0:1] + vectors[1:2]).astype(low).astype(wide)
    vector_ref[2:3] = jnp.sum(grad_logit[...] * first, axis=0, keepdims=True)
    pulled = grad_first * vectors[0:1]
    pulled = (
        pulled
        - jnp.mean(pulled, axis=-1, keepdims=True)
        - scaled * jnp.mean(pulled * scaled, axis=-1, keepdims=True)
    )
    out_ref[...] = (grad_hidden[...] + inverse * pulled).astype(low)


def token_back(tokens, placing, grad_sent, grad_hidden, grad_logit, vectors):
    count, width = tokens.shape
    return pl.pallas_call(
        token_back_kernel,
        out_shape=(
            jax.ShapeDtypeStruct((count, width), low),
            jax.ShapeDtypeStruct((3, width), wide),
        ),
        in_specs=[in_hbm()] * 6,
        out_specs=(on_chip(),) * 2,
        scratch_shapes=fetch_scratch(
            (tokens, placing, grad_sent, grad_hidden, grad_logit, vectors)
        ),
        compiler_params=params(17),
        cost_estimate=cost(2 * count * width * placing.shape[1], 12 * count * width),
    )(tokens, placing, grad_sent, grad_hidden, grad_logit, vectors)


def flip_pairs(flip):
    return [(i, i ^ flip) for i in range(32)]


def all_sum(value):
    value = value + send(value, swap_pairs())
    for one, two in ((2, 4), (8, 16)):
        near = value + send(value, flip_pairs(one))
        far = send(value, flip_pairs(two)) + send(value, flip_pairs(one + two))
        value = near + far
    return value


def exchange(value, n_data):
    capacity, width = value.shape
    moved = lax.all_to_all(
        value.reshape(n_data, capacity // n_data, width), "dp", split_axis=0, concat_axis=0, tiled=True
    )
    return moved.reshape(capacity, width)


def block_shards(
    tokens,
    cotangent,
    selected,
    packing,
    segments,
    blocks,
    left_stat,
    right_stat,
    left_root,
    right_root,
    vectors,
    moment,
):
    model_width = tokens.shape[2]
    token_count = tokens.shape[0] * tokens.shape[1]
    n_data = lax.axis_size("dp")
    capacity = packing.shape[1]
    line, place, core = here()
    own_tokens = tokens.reshape(token_count, model_width)
    above = cotangent.reshape(token_count, model_width)
    segment = segments[0]

    every = columns_by_core(jnp.transpose(blocks, (1, 0, 2)).astype(low))
    placing, packed, gates = pack_tokens(
        own_tokens, selected.reshape(token_count), packing[0], vectors
    )
    buffer = exchange(packed, n_data)
    attn_two = send(every[:4], line_pairs(2))
    ffn_got = send(after(every[4:], attn_two), line_pairs(2))
    attn_pair = jnp.stack([every[:4], attn_two])
    attn_got = send(attn_pair, line_pairs(1))
    line_attn = after(jnp.concatenate([attn_pair, attn_got]), packed)
    ffn_two = jnp.stack([every[4:], after(ffn_got, attn_got)])
    near_attn = send(line_attn, plane_pairs(0))
    every_root = roots_by_core(after(left_root, ffn_two), right_root)
    first_attn = after(jnp.stack([line_attn, near_attn]), every_root, buffer)
    far_attn = send(first_attn, plane_pairs(1))
    line_ffn = gather_far(ffn_two)
    near_ffn = send(after(line_ffn, near_attn), plane_pairs(0))
    w_parts = with_other(first_attn, far_attn)
    answer, store = attend(buffer, w_parts, segment)
    root_given = lax.optimization_barrier((*roots_given(every_root), buffer, line_ffn))[:4]
    root_parts = [root_given[0]]
    for flip in (1, 2, 3):
        root_parts.append(send(root_given[flip], line_pairs(flip)))
    first_ffn = jnp.stack([line_ffn, near_ffn])
    returned = exchange(answer, n_data)
    far_ffn = after(send(after(first_ffn, far_attn), plane_pairs(1)), returned, *root_parts[1:])
    left_line, right_line = (jnp.stack([part[:, kind] for part in root_parts]) for kind in range(2))
    ffn_parts = with_other(first_ffn, far_ffn)

    near_right = send(after(right_line, far_ffn), plane_pairs(0))
    first_right = jnp.stack([right_line, near_right])
    hidden, second_low, active, slope, w_up = token_forward(
        own_tokens, placing, returned, gates, vectors, ffn_parts
    )
    down_theirs = outer_theirs(after(active, near_right), above[None])
    far_right = send(first_right, plane_pairs(1))
    roots = (left_line, send(left_line, swap_pairs()), first_right, far_right)
    down_got = send(down_theirs, swap_pairs())
    down_give, *down_kept = sum_start(lambda step: step, active, above[None], down_got)
    down_got = send(down_give, plane_pairs(0))
    mixed, grad_packed, grad_hidden, grad_logit, vector_two, grad_inner = token_backward(
        above,
        hidden,
        active,
        slope,
        placing,
        returned,
        gates,
        vectors,
        after(w_up, down_give, far_right),
        ffn_parts,
    )
    grad_answer = exchange(grad_packed, n_data)
    up_theirs = outer_theirs(after(second_low, down_got)[None], grad_inner)

    down_kept, down_give = add_first(down_got, *down_kept)
    down_got = send(down_give, plane_pairs(1))
    up_got = send(after(up_theirs, grad_answer), swap_pairs())
    attn_theirs, grads, grad_buffer, sides = attend_back(store, segment, grad_answer)
    attn_got = send(after(attn_theirs, down_got), swap_pairs())
    up_give, *up_kept = sum_start(
        lambda step: 0, second_low[None], grad_inner, after(up_got, attn_theirs)
    )
    up_got = send(up_give, plane_pairs(0))
    down_own, down_two, down_give = cut_line((down_kept + down_got.astype(wide))[None])
    down_got = send(down_give, line_pairs(1))
    attn_give, *attn_kept = sum_start(
        lambda step: step // 3, sides, grads, after(attn_got, up_give)
    )
    attn_got = send(attn_give, plane_pairs(0))
    grad_sent = exchange(after(grad_buffer, attn_give), n_data)
    down_own, down_give = add_line(down_own, down_two, down_got)
    down_got = send(down_give, line_pairs(2))
    down_own = (down_own + down_got.astype(wide)).astype(low)
    down_near = send(down_own, plane_pairs(0))
    down_first = jnp.stack([down_own, down_near])
    down_far = send(down_first, plane_pairs(1))
    down_mine = jnp.concatenate([down_first, down_far])
    down_theirs = send(down_mine, swap_pairs())

    up_kept, up_give = add_first(up_got, *up_kept)
    attn_kept, attn_give = add_first(after(attn_got, down_far), *attn_kept)
    pair_got = send(jnp.stack([attn_give, up_give]), plane_pairs(1))
    down_made, down_square = step_chunks(down_mine, down_theirs, roots, 2)
    down_parts = return_chunks(down_made)
    pair_got = after(pair_got, down_made, grad_sent)
    pair_kept = jnp.stack([attn_kept, up_kept]) + pair_got.astype(wide)
    pair_own, pair_two, pair_give = cut_line(pair_kept)
    pair_got = send(pair_give, line_pairs(1))
    grad_tokens, vector_one = token_back(
        own_tokens, placing, grad_sent, grad_hidden, grad_logit, vectors
    )
    pair_own, pair_give = add_line(pair_own, pair_two, pair_got)
    pair_got = send(after(pair_give, vector_one), line_pairs(2))
    down = jnp.stack(down_parts)
    down_other = send(down, [(i, i ^ 1) for i in range(0, 32, 2)])
    pair_own = (pair_own + pair_got.astype(wide)).astype(low)
    pair_near = send(pair_own, plane_pairs(0))
    pair_first = jnp.stack([pair_own, pair_near])
    pair_far = send(pair_first, plane_pairs(1))
    pair_mine = jnp.concatenate([pair_first, pair_far])
    pair_theirs = send(after(pair_mine, *down_parts[1:]), swap_pairs())
    pair_made, pair_square = step_chunks(pair_mine, pair_theirs, roots, 0)
    pair = jnp.stack(return_chunks(pair_made))
    pair_other = send(pair, swap_pairs())
    squares = jnp.concatenate([jnp.sum(pair_square, axis=2), jnp.sum(down_square, axis=2)])
    lane = lax.broadcasted_iota(jnp.int32, (1, model_width), 1)
    square_row = sum(
        jnp.where(lane == 4 * chunk + line, squares[chunk], 0.0) for chunk in range(3)
    )
    sums = all_sum(jnp.concatenate([vector_one, vector_two, square_row]))
    vector_grad = sums[:5]
    size = model_width * model_width
    scales = block_rate * lax.rsqrt(sums[5, :12] / size + norm_eps)
    grad_own, left_new, right_new, new_blocks = update_blocks(
        pair, pair_other, down, down_other, blocks, left_stat, right_stat, scales
    )
    moment_new = 0.5 * moment + 0.5 * vector_grad
    row_squares = jnp.mean(moment_new * moment_new, axis=1, keepdims=True)
    vector_new = vectors - vector_rate * moment_new * lax.rsqrt(row_squares + norm_eps)
    return (
        mixed.reshape(tokens.shape),
        grad_tokens.reshape(tokens.shape),
        grad_own,
        left_new,
        right_new,
        new_blocks,
        vector_grad,
        moment_new,
        vector_new,
    )


def shards(
    tokens,
    cotangent,
    selected,
    packing,
    segments,
    blocks,
    left_stat,
    right_stat,
    left_root,
    right_root,
    vectors,
    moment,
):
    model_width = tokens.shape[2]
    token_count = tokens.shape[0] * tokens.shape[1]
    n_data = lax.axis_size("dp")
    n_owner = lax.axis_size("own")
    shard_rows = blocks.shape[0]
    own_blocks = blocks.shape[1]
    up_blocks = (own_blocks * n_owner - 4) // 2
    capacity = packing.shape[1]
    per_peer = capacity // n_data
    head_count = model_width // HEAD_DIM
    score_scale = HEAD_DIM ** (-0.5)
    flat_weights = blocks.astype(jnp.bfloat16).reshape(1, shard_rows * own_blocks * model_width)
    gathered = lax.all_gather(flat_weights, ("dp", "own"), axis=0, tiled=True)
    gathered = gathered.reshape(n_data, n_owner, shard_rows, own_blocks, model_width)

    def matrix(number):
        return gathered[:, number // own_blocks, :, number % own_blocks, :].reshape(
            model_width, model_width
        )

    w_query = matrix(0)
    w_key = matrix(1)
    w_value = matrix(2)
    w_out = matrix(3)
    w_up = jnp.concatenate([matrix(4 + position) for position in range(up_blocks)], axis=1)
    w_down = jnp.concatenate(
        [matrix(4 + up_blocks + position) for position in range(up_blocks)], axis=0
    )
    inputs = tokens.reshape(token_count, model_width).astype(jnp.float32)
    chosen = selected.reshape(token_count)
    normed_one, norm_one_back = jax.vjp(layer_norm, inputs, vectors[0], vectors[1])
    first_low = normed_one.astype(jnp.bfloat16)
    first_wide = first_low.astype(jnp.float32)
    gate_values = jax.nn.sigmoid(jnp.dot(first_wide, vectors[2], precision=highest))
    before = jnp.cumsum(chosen) - 1
    slot_index = jnp.where(chosen == 1, packing[0][jnp.clip(before, 0, capacity - 1)], -1)
    placing = (slot_index[None, :] == jnp.arange(capacity, dtype=jnp.int32)[:, None]).astype(
        jnp.bfloat16
    )
    packed = jnp.dot(placing, first_low, preferred_element_type=jnp.float32).astype(jnp.bfloat16)
    buffer = lax.all_to_all(
        packed.reshape(n_data, per_peer, model_width), "dp", split_axis=0, concat_axis=0, tiled=True
    )
    buffer = buffer.reshape(capacity, model_width)

    def project(matrix_in):
        made = jnp.dot(buffer, matrix_in, preferred_element_type=jnp.float32).astype(jnp.bfloat16)
        return made.reshape(capacity, head_count, HEAD_DIM)

    query_rows = project(w_query)
    key_rows = project(w_key)
    value_rows = project(w_value)
    segment = segments[0]
    block_rows = math.gcd(capacity, 512)
    starts = jnp.arange(capacity // block_rows, dtype=jnp.int32) * block_rows

    def masked_scores():
        scores = (
            jnp.einsum("qhd,khd->hqk", query_rows, key_rows, preferred_element_type=jnp.float32)
            * score_scale
        )
        same_segment = segment[:, None] == segment[None, :]
        return (jnp.where(same_segment[None, :, :], scores, -1e30), query_rows)

    def forward_block(first_row):
        scores, unused_block = masked_scores()
        largest = jnp.max(scores, axis=-1, keepdims=True)
        raised = jnp.exp(scores - largest)
        row_total = jnp.sum(raised, axis=-1, keepdims=True)
        shares = (raised / row_total).astype(jnp.bfloat16)
        context_part = jnp.einsum(
            "hqk,khd->qhd", shares, value_rows, preferred_element_type=jnp.float32
        )
        return (context_part.astype(jnp.bfloat16), largest[..., 0] + jnp.log(row_total[..., 0]))

    context_blocks, lse_blocks = lax.map(forward_block, starts)
    context = context_blocks.reshape(capacity, model_width)
    answer = jnp.dot(context, w_out, preferred_element_type=jnp.float32).astype(jnp.bfloat16)
    returned = lax.all_to_all(
        answer.reshape(n_data, per_peer, model_width), "dp", split_axis=0, concat_axis=0, tiled=True
    )
    returned = returned.reshape(capacity, model_width)
    unpacked = jnp.einsum("mt,md->td", placing, returned, preferred_element_type=jnp.float32)
    weighting = jnp.where(chosen == 1, gate_values, 0.0)
    hidden = inputs + weighting[:, None] * unpacked
    normed_two, norm_two_back = jax.vjp(layer_norm, hidden, vectors[3], vectors[4])
    second_low = normed_two.astype(jnp.bfloat16)
    pre_active = jnp.dot(second_low, w_up, preferred_element_type=jnp.float32)
    active_wide, gelu_back = jax.vjp(gelu_exact, pre_active)
    active = active_wide.astype(jnp.bfloat16)
    result = hidden + jnp.dot(active, w_down, preferred_element_type=jnp.float32)
    mixed = result.astype(jnp.bfloat16).reshape(tokens.shape)
    upstream = cotangent.reshape(token_count, model_width)
    grad_down = jnp.einsum("tf,td->fd", active, upstream, preferred_element_type=jnp.float32)
    grad_active = jnp.einsum("td,fd->tf", upstream, w_down, preferred_element_type=jnp.float32)
    grad_inner = gelu_back(grad_active)[0].astype(jnp.bfloat16)
    grad_up = jnp.einsum("td,tf->df", second_low, grad_inner, preferred_element_type=jnp.float32)
    grad_second = jnp.einsum("tf,df->td", grad_inner, w_up, preferred_element_type=jnp.float32)
    grad_hidden_part, grad_gain_two, grad_bias_two = norm_two_back(grad_second)
    grad_hidden = upstream.astype(jnp.float32) + grad_hidden_part
    grad_token_back = (grad_hidden * weighting[:, None]).astype(jnp.bfloat16)
    grad_packed = jnp.dot(placing, grad_token_back, preferred_element_type=jnp.float32).astype(
        jnp.bfloat16
    )
    router_pull = jnp.where(chosen == 1, jnp.sum(grad_hidden * unpacked, axis=-1), 0.0)
    grad_logit = router_pull * gate_values * (1.0 - gate_values)
    grad_answer = lax.all_to_all(
        grad_packed.reshape(n_data, per_peer, model_width),
        "dp",
        split_axis=0,
        concat_axis=0,
        tiled=True,
    )
    grad_answer = grad_answer.reshape(capacity, model_width)
    grad_out = jnp.einsum("md,me->de", context, grad_answer, preferred_element_type=jnp.float32)
    grad_context = jnp.einsum("me,de->md", grad_answer, w_out, preferred_element_type=jnp.float32)
    grad_context = grad_context.astype(jnp.bfloat16).reshape(capacity, head_count, HEAD_DIM)

    def backward_block(running, item_pair):
        first_row, lse_block = item_pair
        scores, query_block = masked_scores()
        shares_wide = jnp.exp(scores - lse_block[..., None])
        grad_shares = jnp.einsum(
            "qhd,khd->hqk", grad_context, value_rows, preferred_element_type=jnp.float32
        )
        inner_sum = jnp.sum(shares_wide * grad_shares, axis=-1, keepdims=True)
        grad_scores = (shares_wide * (grad_shares - inner_sum)).astype(jnp.bfloat16)
        grad_query_block = (
            jnp.einsum("hqk,khd->qhd", grad_scores, key_rows, preferred_element_type=jnp.float32)
            * score_scale
        )
        key_sum = (
            running[0]
            + jnp.einsum(
                "hqk,qhd->khd", grad_scores, query_block, preferred_element_type=jnp.float32
            )
            * score_scale
        )
        value_sum = running[1] + jnp.einsum(
            "hqk,qhd->khd",
            shares_wide.astype(jnp.bfloat16),
            grad_context,
            preferred_element_type=jnp.float32,
        )
        return ((key_sum, value_sum), grad_query_block)

    zeros_init = jnp.zeros((capacity, head_count, HEAD_DIM), jnp.float32)
    (key_total, value_total), query_grads = lax.scan(
        backward_block, (zeros_init, zeros_init), (starts, lse_blocks)
    )
    grad_query = query_grads.reshape(capacity, model_width).astype(jnp.bfloat16)
    grad_key = key_total.reshape(capacity, model_width).astype(jnp.bfloat16)
    grad_value = value_total.reshape(capacity, model_width).astype(jnp.bfloat16)
    grad_w_query = jnp.einsum("md,me->de", buffer, grad_query, preferred_element_type=jnp.float32)
    grad_w_key = jnp.einsum("md,me->de", buffer, grad_key, preferred_element_type=jnp.float32)
    grad_w_value = jnp.einsum("md,me->de", buffer, grad_value, preferred_element_type=jnp.float32)
    grad_buffer = jnp.einsum("me,de->md", grad_query, w_query, preferred_element_type=jnp.float32)
    grad_buffer = grad_buffer + jnp.einsum(
        "me,de->md", grad_key, w_key, preferred_element_type=jnp.float32
    )
    grad_buffer = grad_buffer + jnp.einsum(
        "me,de->md", grad_value, w_value, preferred_element_type=jnp.float32
    )
    grad_buffer = grad_buffer.astype(jnp.bfloat16)
    grad_sent = lax.all_to_all(
        grad_buffer.reshape(n_data, per_peer, model_width),
        "dp",
        split_axis=0,
        concat_axis=0,
        tiled=True,
    )
    grad_sent = grad_sent.reshape(capacity, model_width)
    grad_first = jnp.einsum("mt,md->td", placing, grad_sent, preferred_element_type=jnp.float32)
    grad_first = grad_first + grad_logit[:, None] * vectors[2][None, :]
    grad_router = jnp.sum(grad_logit[:, None] * first_wide, axis=0)
    grad_input_part, grad_gain_one, grad_bias_one = norm_one_back(grad_first)
    grad_tokens = (grad_hidden + grad_input_part).astype(jnp.bfloat16).reshape(tokens.shape)
    pieces = [grad_w_query, grad_w_key, grad_w_value, grad_out]
    pieces = pieces + [
        grad_up[:, position * model_width : (position + 1) * model_width]
        for position in range(up_blocks)
    ]
    pieces = pieces + [
        grad_down[position * model_width : (position + 1) * model_width, :]
        for position in range(up_blocks)
    ]
    local_terms = jnp.stack(pieces, axis=1)
    vector_terms = jnp.stack(
        [grad_gain_one, grad_bias_one, grad_router, grad_gain_two, grad_bias_two]
    )
    partial_value = lax.psum_scatter(local_terms, "dp", scatter_dimension=0, tiled=True)
    grad_own = lax.psum_scatter(
        partial_value.astype(jnp.bfloat16), "own", scatter_dimension=1, tiled=True
    ).astype(jnp.float32)
    vector_grad = lax.psum(vector_terms, ("dp", "own"))
    full_grad = lax.all_gather(grad_own.astype(jnp.bfloat16), "dp", axis=0, tiled=True).astype(
        grad_own.dtype
    )
    row_start = lax.axis_index("dp") * shard_rows
    left_new = 0.5 * left_stat + 0.5 * jnp.einsum(
        "rbk,nbk->rbn", grad_own, full_grad, precision=highest
    )
    column_part = lax.dynamic_slice_in_dim(full_grad, row_start, shard_rows, 2)
    right_new = 0.5 * right_stat + 0.5 * jnp.einsum(
        "nbr,nbk->rbk", column_part, full_grad, precision=highest
    )
    lefted = jnp.einsum("rbn,nbk->rbk", left_root, full_grad, precision=highest)
    precond = jnp.zeros_like(grad_own) + jnp.einsum(
        "rbn,nbk->rbk",
        lefted,
        lax.all_gather(right_root.astype(jnp.bfloat16), "dp", axis=0, tiled=True).astype(
            jnp.float32
        ),
        precision=highest,
    )
    square_sums = lax.psum(jnp.sum(precond * precond, axis=(0, 2)), "dp")
    step_scale = lax.rsqrt(square_sums / (model_width * model_width) + norm_eps)
    new_blocks = blocks - block_rate * precond * step_scale[None, :, None]
    moment_new = 0.5 * moment + 0.5 * vector_grad
    row_squares = jnp.mean(moment_new * moment_new, axis=1, keepdims=True)
    vector_new = vectors - vector_rate * moment_new * lax.rsqrt(row_squares + norm_eps)
    return (
        mixed,
        grad_tokens,
        grad_own,
        left_new,
        right_new,
        new_blocks,
        vector_grad,
        moment_new,
        vector_new,
    )


def solution(mesh):
    placed = (
        P(("dp", "own"), None, None),
        P(("dp", "own"), None, None),
        P(("dp", "own"), None),
        P(("dp", "own"), None),
        P(("dp", "own"), None),
        P("dp", "own", None),
        P("dp", "own", None),
        P("dp", "own", None),
        P("dp", "own", None),
        P("dp", "own", None),
        P(),
        P(),
    )
    small = mesh.shape["dp"] == 16 and mesh.shape["own"] == 2
    return jax.shard_map(
        block_shards if small else shards,
        mesh=mesh,
        in_specs=placed,
        out_specs=(
            P(("dp", "own"), None, None),
            P(("dp", "own"), None, None),
            P("dp", "own", None),
            P("dp", "own", None),
            P("dp", "own", None),
            P("dp", "own", None),
            P(),
            P(),
            P(),
        ),
        check_vma=False,
    )
```

```python
import functools
import math

import jax
import jax.numpy as jnp
from jax import lax
from jax.experimental import pallas as pl
from jax.experimental.pallas import tpu as pltpu
from jax.sharding import PartitionSpec as P

HEAD_DIM = 64


norm_eps = 1e-06
block_rate = 0.03
vector_rate = 0.04
highest = lax.Precision.HIGHEST


def layer_norm(values, norm_gain, norm_bias):
    center = values - jnp.mean(values, axis=-1, keepdims=True)
    spread = jnp.mean(center * center, axis=-1, keepdims=True)
    return center * lax.rsqrt(spread + norm_eps) * norm_gain + norm_bias


def gelu_exact(values):
    return jax.nn.gelu(values, approximate=False)


BOTH = ("dp", "own")
low = jnp.bfloat16
wide = jnp.float32
MIB = 2**20


def swap_pairs():
    return [(i, i ^ 1) for i in range(32)]


def plane_pairs(step):
    pairs = []
    for i in range(32):
        place, core = i // 2, i % 2
        flip = (1, 2)[step ^ core]
        pairs.append((i, (place ^ flip) * 2 + core))
    return pairs


def line_pairs(flip):
    return [(i, i ^ (8 * flip)) for i in range(32)]


def send(value, pairs):
    return lax.ppermute(value, BOTH, pairs)


def after(value, *others):
    return lax.optimization_barrier((value,) + others)[0]


def pick(value, index, axis):
    return lax.dynamic_index_in_dim(value, index, axis, keepdims=False)


def first_core():
    return lax.axis_index("own") == 0


def halves(value):
    middle = value.shape[-1] // 2
    lower, upper = value[..., :middle], value[..., middle:]
    return jnp.where(first_core(), lower, upper), jnp.where(first_core(), upper, lower)


def in_core_order(mine, theirs, axis):
    return jnp.where(
        first_core(),
        jnp.concatenate([mine, theirs], axis=axis),
        jnp.concatenate([theirs, mine], axis=axis),
    )


LINE_FLIPS = (0, 2, 1, 3)


def flipped(index, flip):
    return jnp.bitwise_xor(index, flip)


def spots(place, half):
    first, second = half + 1, 2 - half
    return [
        place,
        flipped(place, first),
        flipped(place, second),
        flipped(place, 3),
    ]


def here():
    device = lax.axis_index("dp")
    return device // 4, device % 4, lax.axis_index("own")


def dot(left, right, left_axis=1, right_axis=0):
    return lax.dot_general(
        left, right, (((left_axis,), (right_axis,)), ((), ())), preferred_element_type=wide
    )


def on_chip():
    return pl.BlockSpec(memory_space=pltpu.VMEM)


def whole(value):
    return pl.BlockSpec(value.shape, lambda *steps: (0,) * value.ndim)


def in_hbm():
    return pl.BlockSpec(memory_space=pltpu.HBM)


def fetch_scratch(values):
    return [pltpu.VMEM(value.shape, value.dtype) for value in values] + [
        pltpu.SemaphoreType.DMA((len(values),))
    ]


def fetch(sources, targets, sems):
    copies = [
        pltpu.make_async_copy(source, target, sems.at[number])
        for number, (source, target) in enumerate(zip(sources, targets))
    ]
    for copy in copies:
        copy.start()
    return copies


def finish(copies):
    for copy in copies:
        copy.wait()


def params(limit):
    return pltpu.CompilerParams(vmem_limit_bytes=limit * MIB)


def cost(flops, moved):
    return pl.CostEstimate(flops=flops, bytes_accessed=moved, transcendentals=0)


def place_block(parts, block, target):
    line, place, core = here()
    rows, columns = parts[0].shape[3:]
    for other in range(2):
        half = core if other == 0 else 1 - core
        column_slice = pl.ds(pl.multiple_of(half * columns, columns), columns)
        for number, spot in enumerate(spots(place, half)):
            for index, flip in enumerate(LINE_FLIPS):
                start = (flipped(line, flip) * 4 + spot) * rows
                row_slice = pl.ds(pl.multiple_of(start, rows), rows)
                piece = parts[2 * other + number // 2][number % 2, index, block]
                target[row_slice, column_slice] = piece


def columns_by_core(value):
    keep, give = halves(value)
    return in_core_order(keep, send(give, swap_pairs()), 0)


def gather_far(pair):
    return jnp.concatenate([pair, send(pair, line_pairs(1))])


def with_other(first, far):
    return [first, far, send(first, swap_pairs()), send(far, swap_pairs())]


def roots_by_core(left_root, right_root):
    both = [jnp.transpose(root, (1, 0, 2)).astype(low) for root in (left_root, right_root)]
    every = columns_by_core(jnp.stack(both, axis=1))
    return every.reshape((3, 4) + every.shape[1:])


def roots_given(every):
    line, place, core = here()
    return [pick(every, flipped(line, flip), 1) for flip in range(4)]


def sum_kernel(left_of, left, right, got, give_ref, kept_ref, passed_ref, total):
    line, place, core = here()
    step = pl.program_id(0)
    columns = got.shape[2]
    rows = kept_ref.shape[2]
    part = pl.ds(pl.multiple_of(core * columns, columns), columns)
    right_step = step if right.shape[0] > 1 else 0
    made = dot(left[left_of(step)], right[right_step, :, part], 0, 0)
    total[...] = made + got[step].astype(wide)
    own, first, second, both = spots(place, core)
    for row_line in range(4):

        def piece(spot):
            return total[pl.ds(pl.multiple_of((row_line * 4 + spot) * rows, rows), rows), :]

        give_ref[0, step, row_line] = piece(first).astype(low)
        give_ref[1, step, row_line] = piece(both).astype(low)
        kept_ref[step, row_line] = piece(own).astype(low)
        passed_ref[step, row_line] = piece(second).astype(low)


def sum_start(left_of, left, right, got):
    count, width = left.shape[1:]
    blocks, full, columns = got.shape
    shape = (blocks, 4, full // 16, columns)
    return pl.pallas_call(
        functools.partial(sum_kernel, left_of),
        grid=(blocks,),
        out_shape=(
            jax.ShapeDtypeStruct((2,) + shape, low),
            jax.ShapeDtypeStruct(shape, low),
            jax.ShapeDtypeStruct(shape, low),
        ),
        in_specs=[on_chip()] * 3,
        out_specs=(on_chip(),) * 3,
        scratch_shapes=[pltpu.VMEM((full, columns), wide)],
        compiler_params=params(12),
        cost_estimate=cost(blocks * count * width * width, 5 * blocks * width * width),
    )(left, right, got)


def add_first(got, kept, passed):
    kept = kept.astype(wide) + got[0].astype(wide)
    return kept, (passed.astype(wide) + got[1].astype(wide)).astype(low)


def cut_line(kept):
    line, place, core = here()
    given = jnp.stack([pick(kept, flipped(line, flip), 1) for flip in (1, 3)]).astype(low)
    return pick(kept, line, 1), pick(kept, flipped(line, 2), 1), given


def add_line(own, two, got):
    return own + got[0].astype(wide), (two + got[1].astype(wide)).astype(low)


def step_kernel(
    number,
    mine,
    theirs,
    left_mine_from,
    left_theirs_from,
    right_first_from,
    right_far_from,
    out_ref,
    square_ref,
    grad_ref,
    rows_ref,
    left_ref,
    right_ref,
    cross_ref,
    left_mine,
    left_theirs,
    right_first,
    right_far,
    sems,
):
    chunk = number + pl.program_id(0)
    copies = fetch(
        [
            left_mine_from.at[:, chunk],
            left_theirs_from.at[:, chunk],
            right_first_from.at[:, :, chunk],
            right_far_from.at[:, :, chunk],
        ],
        [left_mine, left_theirs, right_first, right_far],
        sems,
    )
    line, place, core = here()
    rows, columns = mine.shape[3:]

    def rows_of(row_line, spot):
        return pl.ds(pl.multiple_of((row_line * 4 + spot) * rows, rows), rows)

    def column_half(half):
        return pl.ds(pl.multiple_of(half * columns, columns), columns)

    for half, group in ((core, mine), (1 - core, theirs)):
        for number, spot in enumerate(spots(place, half)):
            for step in range(4):
                grad_ref[rows_of(step, spot), column_half(half)] = group[number, 0, step]
    finish(copies)
    for half, left in ((core, left_mine), (1 - core, left_theirs)):
        for flip in range(4):
            target = pl.ds(pl.multiple_of(flipped(line, flip) * rows, rows), rows)
            left_ref[target, column_half(half)] = left[flip]
    for number, spot in enumerate(spots(place, core)):
        source = right_far if number > 1 else right_first
        for flip in range(4):
            right_ref[rows_of(flipped(line, flip), spot), :] = source[number % 2, flip]
    for row_line in range(4):
        rows_ref[row_line * rows : (row_line + 1) * rows, :] = grad_ref[rows_of(row_line, place), :]
    left = dot(rows_ref[...], grad_ref[column_half(core), :], 1, 1)
    cross_ref[...] = dot(grad_ref[...], grad_ref[:, column_half(core)], 0, 0)
    lefted = dot(left_ref[...], grad_ref[...]).astype(low)
    stepped = dot(lefted, right_ref[...])
    square_ref[0] = jnp.sum(stepped * stepped, axis=0, keepdims=True)
    for row_line in range(4):
        part = slice(row_line * rows, (row_line + 1) * rows)
        out_ref[0, row_line, 0] = mine[0, 0, row_line]
        out_ref[0, row_line, 1] = left[part].astype(low)
        out_ref[0, row_line, 2] = cross_ref[rows_of(row_line, place), :].astype(low)
        out_ref[0, row_line, 3] = stepped[part].astype(low)


def step_chunks(mine, theirs, roots, number):
    chunks, lines, rows, columns = mine.shape[1:]
    full = rows * 16
    grad_spec = pl.BlockSpec((4, 1, lines, rows, columns), lambda step: (0, step, 0, 0, 0))
    return pl.pallas_call(
        functools.partial(step_kernel, number),
        grid=(chunks,),
        out_shape=(
            jax.ShapeDtypeStruct((chunks, lines, 4, rows, columns), low),
            jax.ShapeDtypeStruct((chunks, 1, columns), wide),
        ),
        in_specs=[grad_spec] * 2 + [in_hbm()] * 4,
        out_specs=(
            pl.BlockSpec((1, lines, 4, rows, columns), lambda step: (step, 0, 0, 0, 0)),
            pl.BlockSpec((1, 1, columns), lambda step: (step, 0, 0)),
        ),
        scratch_shapes=[
            pltpu.VMEM((full, columns * 2), low),
            pltpu.VMEM((lines * rows, columns * 2), low),
            pltpu.VMEM((lines * rows, columns * 2), low),
            pltpu.VMEM((full, columns), low),
            pltpu.VMEM((full, columns), wide),
            pltpu.VMEM((lines, rows, columns), low),
            pltpu.VMEM((lines, rows, columns), low),
            pltpu.VMEM((2, lines, rows, columns), low),
            pltpu.VMEM((2, lines, rows, columns), low),
            pltpu.SemaphoreType.DMA((4,)),
        ],
        compiler_params=params(15),
        cost_estimate=cost(3 * chunks * full**3, 16 * chunks * full * full),
    )(mine, theirs, *roots)


def return_chunks(made):
    line, place, core = here()
    parts = [pick(made, line, 1)]
    for flip in (1, 2, 3):
        parts.append(send(pick(made, flipped(line, flip), 1), line_pairs(flip)))
    return parts


def last_kernel(
    pair, pair_other, down, down_other, blocks, left_stat, right_stat, scales, *outs
):
    grad_out, left_out, right_out, block_out = outs
    line, place, core = here()
    columns = pair.shape[4]

    def update(number, which, mine, theirs):
        for (source, index), half in ((mine, which), (theirs, 1 - which)):
            part = slice(half * columns, (half + 1) * columns)
            pieces = [source[index + (kind,)].astype(wide) for kind in range(4)]
            grad_out[number, :, part] = pieces[0]
            left_out[number, :, part] = 0.5 * left_stat[number, :, part] + 0.5 * pieces[1]
            right_out[number, :, part] = 0.5 * right_stat[number, :, part] + 0.5 * pieces[2]
            step = pieces[3] * scales[6 * which + number]
            block_out[number, :, part] = blocks[number, :, part] - step

    @pl.when(core == 0)
    def first():
        for number in range(6):
            index = (flipped(line, number % 4), number // 4)
            update(number, 0, (pair, index), (pair_other, index))

    @pl.when(core == 1)
    def second():
        for number in range(6):
            source, other = (pair, pair_other) if number < 2 else (down, down_other)
            index = (flipped(line, (number + 2) % 4), 1 if number < 2 else 0)
            update(number, 1, (source, index), (other, index))


def update_blocks(pair, pair_other, down, down_other, blocks, left_stat, right_stat, scales):
    turned = [jnp.transpose(value, (1, 0, 2)) for value in (blocks, left_stat, right_stat)]
    shape = jax.ShapeDtypeStruct(turned[0].shape, wide)
    outs = pl.pallas_call(
        last_kernel,
        out_shape=(shape,) * 4,
        in_specs=[on_chip()] * 7 + [pl.BlockSpec(memory_space=pltpu.SMEM)],
        out_specs=(on_chip(),) * 4,
        compiler_params=params(10),
        cost_estimate=cost(0, 32 * shape.size),
    )(pair, pair_other, down, down_other, *turned, scales)
    return [jnp.transpose(value, (1, 0, 2)) for value in outs]


def head_masks():
    lane = lax.broadcasted_iota(jnp.int32, (1, 2 * HEAD_DIM), 1)
    return [(lane < HEAD_DIM).astype(wide).astype(low), (lane >= HEAD_DIM).astype(wide).astype(low)]


def head_shares(query, key, same):
    scores = dot(query, key, 1, 1) * HEAD_DIM ** (-0.5)
    scores = jnp.where(same, scores, -1e30)
    raised = jnp.exp(scores - jnp.max(scores, axis=-1, keepdims=True))
    return raised / jnp.sum(raised, axis=-1, keepdims=True)


STORE_ROWS = 32768


def store_views(store, rows, width):
    weights = [store.at[pl.ds(block * width, width)] for block in range(4)]
    made = [store.at[pl.ds(4 * width + kind * rows, rows)] for kind in range(3)]
    sides = [store.at[pl.ds(4 * width + (3 + side) * rows, rows)] for side in range(2)]
    return weights, made, sides


def attend_kernel(
    buffer, one, two, three, four, seg_column, seg_row, answer_ref, store, weights, made, sides, sems
):
    rows, width = buffer.shape
    weights_out, made_out, sides_out = store_views(store, rows, width)
    for block in range(4):
        place_block((one, two, three, four), block, weights.at[block])
    copies = fetch([weights.at[block] for block in range(4)], weights_out, sems)
    same = seg_column[...] == seg_row[...]
    for kind in range(3):
        made[kind] = dot(buffer[...], weights[kind]).astype(low)
    copies += fetch([made.at[kind] for kind in range(3)], made_out, sems.at[pl.ds(4, 3)])
    pair_width = 2 * HEAD_DIM
    for pair in range(width // pair_width):
        part = slice(pair * pair_width, (pair + 1) * pair_width)
        query, key, value = (made[kind, :, part] for kind in range(3))
        context = None
        for mask in head_masks():
            shares = head_shares(query, key * mask, same).astype(low)
            term = dot(shares, value * mask)
            context = term if context is None else context + term
        sides[1, :, part] = context.astype(low)
    sides[0] = buffer[...]
    copies += fetch([sides.at[side] for side in range(2)], sides_out, sems.at[pl.ds(7, 2)])
    answer_ref[...] = dot(sides[1], weights[3]).astype(low)
    finish(copies)


def attend_scratch(rows, width):
    return [
        pltpu.VMEM((4, width, width), low),
        pltpu.VMEM((3, rows, width), low),
        pltpu.VMEM((2, rows, width), low),
        pltpu.SemaphoreType.DMA((9,)),
    ]


def attend(buffer, parts, segment):
    rows, width = buffer.shape
    return pl.pallas_call(
        attend_kernel,
        out_shape=(
            jax.ShapeDtypeStruct((rows, width), low),
            jax.ShapeDtypeStruct((STORE_ROWS, width), low),
        ),
        in_specs=[on_chip()] * 7,
        out_specs=(on_chip(), in_hbm()),
        scratch_shapes=attend_scratch(rows, width),
        compiler_params=params(20),
        cost_estimate=cost(12 * rows * width * width, 12 * width * width),
    )(buffer, *parts, segment[:, None], segment[None, :])


def attend_back_kernel(
    store,
    seg_column,
    seg_row,
    grad_answer,
    theirs_ref,
    grads_ref,
    grad_buffer_ref,
    sides,
    grad_context_ref,
    weights,
    made,
    sems,
):
    rows, width = grad_answer.shape
    weights_from, made_from, sides_from = store_views(store, rows, width)
    out_copy, *copies = fetch(
        [weights_from[3]] + made_from + sides_from + weights_from[:3],
        [weights.at[3]]
        + [made.at[kind] for kind in range(3)]
        + [sides.at[side] for side in range(2)]
        + [weights.at[block] for block in range(3)],
        sems,
    )
    same = seg_column[...] == seg_row[...]
    core = lax.axis_index("own")
    out_copy.wait()
    grad_context_ref[...] = dot(grad_answer[...], weights[3], 1, 1).astype(low)
    finish(copies[:3])
    grads_ref[3] = grad_answer[...]
    pair_width = 2 * HEAD_DIM
    for pair in range(width // pair_width):
        part = slice(pair * pair_width, (pair + 1) * pair_width)
        query, key, value = (made[kind, :, part] for kind in range(3))
        above = grad_context_ref[:, part]
        sums = [None] * 3
        for mask in head_masks():
            key_head = key * mask
            shares = head_shares(query, key_head, same)
            grad_shares = dot(above, value * mask, 1, 1)
            inner = jnp.sum(shares * grad_shares, axis=-1, keepdims=True)
            grad_scores = (shares * (grad_shares - inner)).astype(low)
            terms = (
                dot(grad_scores, key_head),
                dot(grad_scores, query * mask, 0, 0),
                dot(shares.astype(low), above * mask, 0, 0),
            )
            sums = [
                term if total is None else total + term for term, total in zip(terms, sums)
            ]
        for kind, factor in enumerate((HEAD_DIM ** (-0.5), HEAD_DIM ** (-0.5), 1.0)):
            grads_ref[kind, :, part] = (sums[kind] * factor).astype(low)
    finish(copies[3:5])
    columns = theirs_ref.shape[2]
    part = pl.ds(pl.multiple_of((1 - core) * columns, columns), columns)
    for kind in range(4):
        theirs_ref[kind] = dot(sides[kind // 3], grads_ref[kind, :, part], 0, 0).astype(low)
    finish(copies[5:])
    total = dot(grads_ref[0], weights[0], 1, 1)
    total = total + dot(grads_ref[1], weights[1], 1, 1)
    total = total + dot(grads_ref[2], weights[2], 1, 1)
    grad_buffer_ref[...] = total.astype(low)


def attend_back(store, segment, grad_answer):
    rows, width = grad_answer.shape
    weights, made, sides, sems = attend_scratch(rows, width)
    return pl.pallas_call(
        attend_back_kernel,
        out_shape=(
            jax.ShapeDtypeStruct((4, width, width // 2), low),
            jax.ShapeDtypeStruct((4, rows, width), low),
            jax.ShapeDtypeStruct((rows, width), low),
            jax.ShapeDtypeStruct((2, rows, width), low),
        ),
        in_specs=[in_hbm()] + [on_chip()] * 3,
        out_specs=(on_chip(),) * 4,
        scratch_shapes=[pltpu.VMEM((rows, width), low), weights, made, sems],
        compiler_params=params(18),
        cost_estimate=cost(20 * rows * width * width, 16 * width * width),
    )(store, segment[:, None], segment[None, :], grad_answer)


def normal_parts(values):
    center = values - jnp.mean(values, axis=-1, keepdims=True)
    spread = jnp.mean(center * center, axis=-1, keepdims=True)
    return center, lax.rsqrt(spread + norm_eps)


def forward_kernel(*refs):
    tokens, placing, returned, gates, vectors = refs[:5]
    parts = refs[5:9]
    hidden_ref, second_ref, active_ref, slope_ref, w_up = refs[9:14]
    step = pl.program_id(0)

    @pl.when(step == 0)
    def prepare():
        values = tokens[...].astype(wide) + gates[:, 0:1] * dot(placing[...], returned[...])
        hidden_ref[...] = values
        center, inverse = normal_parts(values)
        second_ref[...] = (center * inverse * vectors[3:4] + vectors[4:5]).astype(low)

    place_block(parts, step, w_up.at[step])
    before = dot(second_ref[...], w_up[step])
    share = 0.5 + 0.5 * lax.erf(before * (0.5**0.5))
    density = jnp.exp(before * before * -0.5) * (0.5 / math.pi) ** 0.5
    active_ref[step] = (before * share).astype(low)
    slope_ref[step] = (share + before * density).astype(low)


def token_forward(tokens, placing, returned, gates, vectors, parts):
    count, width = tokens.shape
    blocks = parts[0].shape[2] // 2
    by_block = jax.ShapeDtypeStruct((blocks, count, width), low)
    fetched = (tokens, placing, returned, gates, vectors)
    return pl.pallas_call(
        forward_kernel,
        grid=(blocks,),
        out_shape=(
            jax.ShapeDtypeStruct((count, width), wide),
            jax.ShapeDtypeStruct((count, width), low),
            by_block,
            by_block,
            jax.ShapeDtypeStruct((blocks, width, width), low),
        ),
        in_specs=[whole(value) for value in fetched] + [on_chip()] * 4,
        out_specs=(on_chip(),) * 5,
        compiler_params=params(18),
        cost_estimate=cost(8 * blocks * count * width * width, 8 * blocks * width * width),
    )(*fetched, *parts)


def backward_kernel(*refs):
    above, placing, returned, gates, vectors = refs[:5]
    (hidden, active, slope, w_up), parts = refs[5:9], refs[9:13]
    mixed_ref, packed_ref, grad_hidden_ref, logit_ref, vector_ref, inner_ref = refs[13:19]
    result, grad_second, w_down = refs[19:22]
    step = pl.program_id(0)
    place_block(parts, 4 + step, w_down)

    @pl.when(step == 0)
    def prepare():
        result[...] = hidden[...]
        grad_second[...] = jnp.zeros_like(grad_second)

    grad_active = dot(above[...], w_down[...], 1, 1)
    grad_inner = (grad_active * slope[step].astype(wide)).astype(low)
    inner_ref[step] = grad_inner
    result[...] += dot(active[step], w_down[...])
    grad_second[...] += dot(grad_inner, w_up[step], 1, 1)

    @pl.when(step == pl.num_programs(0) - 1)
    def complete():
        mixed_ref[...] = result[...].astype(low)
        center, inverse = normal_parts(hidden[...])
        scaled = center * inverse
        grads = grad_second[...]
        vector_ref[0:1] = jnp.sum(grads * scaled, axis=0, keepdims=True)
        vector_ref[1:2] = jnp.sum(grads, axis=0, keepdims=True)
        pulled = grads * vectors[3:4]
        pulled = (
            pulled
            - jnp.mean(pulled, axis=-1, keepdims=True)
            - scaled * jnp.mean(pulled * scaled, axis=-1, keepdims=True)
        )
        grad_hidden = above[...].astype(wide) + inverse * pulled
        grad_hidden_ref[...] = grad_hidden
        weighted = (grad_hidden * gates[:, 0:1]).astype(low)
        packed_ref[...] = dot(placing[...], weighted, 0, 0).astype(low)
        unpacked = dot(placing[...], returned[...])
        logit_ref[...] = gates[:, 1:2] * jnp.sum(grad_hidden * unpacked, axis=-1, keepdims=True)


def token_backward(above, hidden, active, slope, placing, returned, gates, vectors, w_up, parts):
    count, width = above.shape
    slots = placing.shape[1]
    blocks = w_up.shape[0]
    fetched = (above, placing, returned, gates, vectors)
    return pl.pallas_call(
        backward_kernel,
        grid=(blocks,),
        out_shape=(
            jax.ShapeDtypeStruct((count, width), low),
            jax.ShapeDtypeStruct((slots, width), low),
            jax.ShapeDtypeStruct((count, width), wide),
            jax.ShapeDtypeStruct((count, 1), wide),
            jax.ShapeDtypeStruct((2, width), wide),
            jax.ShapeDtypeStruct((blocks, count, width), low),
        ),
        in_specs=[whole(value) for value in fetched] + [on_chip()] * 8,
        out_specs=(on_chip(),) * 6,
        scratch_shapes=[
            pltpu.VMEM((count, width), wide),
            pltpu.VMEM((count, width), wide),
            pltpu.VMEM((width, width), low),
        ],
        compiler_params=params(30),
        cost_estimate=cost(8 * blocks * count * width * width, 8 * blocks * width * width),
    )(*fetched, hidden, active, slope, w_up, *parts)


def outer_kernel(left, right, theirs_ref):
    core = lax.axis_index("own")
    step = pl.program_id(0)
    columns = theirs_ref.shape[2]
    left_step = step if left.shape[0] > 1 else 0
    right_step = step if right.shape[0] > 1 else 0
    part = pl.ds(pl.multiple_of((1 - core) * columns, columns), columns)
    theirs_ref[step] = dot(left[left_step], right[right_step, :, part], 0, 0).astype(low)


def outer_theirs(left, right):
    count, width = left.shape[1:]
    blocks = max(left.shape[0], right.shape[0])
    return pl.pallas_call(
        outer_kernel,
        grid=(blocks,),
        out_shape=jax.ShapeDtypeStruct((blocks, width, width // 2), low),
        in_specs=[on_chip()] * 2,
        out_specs=on_chip(),
        compiler_params=params(8),
        cost_estimate=cost(blocks * count * width * width, 3 * blocks * width * width),
    )(left, right)


def column(values):
    return values[:, None]


def pack_kernel(
    tokens, chosen, packing, vectors, placing_ref, packed_ref, gates_ref
):
    count = tokens.shape[0]
    capacity = packing.shape[0]
    center, inverse = normal_parts(tokens[...].astype(wide))
    first = (center * inverse * vectors[0:1] + vectors[1:2]).astype(low)
    gate = jax.nn.sigmoid(jnp.sum(first.astype(wide) * vectors[2:3], axis=-1, keepdims=True))
    weighting = jnp.where(chosen[...] == 1, gate, 0.0)
    gates_ref[:, 0:1] = weighting
    gates_ref[:, 1:2] = weighting * (1.0 - gate)
    above = lax.broadcasted_iota(jnp.int32, (count, count), 0)
    below = lax.broadcasted_iota(jnp.int32, (count, count), 1)
    earlier = (below <= above).astype(wide).astype(low)
    flags = jnp.broadcast_to(chosen[...].astype(wide), (count, capacity))
    rank = dot(earlier, flags.astype(low))
    place_of = lax.broadcasted_iota(jnp.int32, (count, capacity), 1).astype(wide) + 1.0
    ranked = jnp.where(rank == place_of, flags, 0.0).astype(low)
    slots = lax.broadcasted_iota(jnp.int32, (capacity, capacity), 1)
    slot_of = (packing[...] == slots).astype(wide).astype(low)
    placing = dot(ranked, slot_of).astype(low)
    placing_ref[...] = placing
    packed_ref[...] = dot(placing, first, 0, 0).astype(low)


def pack_tokens(tokens, chosen, packing, vectors):
    count, width = tokens.shape
    capacity = packing.shape[0]
    return pl.pallas_call(
        pack_kernel,
        out_shape=(
            jax.ShapeDtypeStruct((count, capacity), low),
            jax.ShapeDtypeStruct((capacity, width), low),
            jax.ShapeDtypeStruct((count, 2), wide),
        ),
        in_specs=[on_chip()] * 4,
        out_specs=(on_chip(),) * 3,
        compiler_params=params(10),
        cost_estimate=cost(4 * count * capacity * width, 8 * count * width),
    )(tokens, column(chosen), column(packing), vectors)


def token_back_kernel(*refs):
    sources, (out_ref, vector_ref), fetched, sems = refs[:6], refs[6:8], refs[8:14], refs[14]
    finish(fetch(sources, fetched, sems))
    tokens, placing, grad_sent, grad_hidden, grad_logit, vectors = fetched
    grad_first = dot(placing[...], grad_sent[...]) + grad_logit[...] * vectors[2:3]
    center, inverse = normal_parts(tokens[...].astype(wide))
    scaled = center * inverse
    vector_ref[0:1] = jnp.sum(grad_first * scaled, axis=0, keepdims=True)
    vector_ref[1:2] = jnp.sum(grad_first, axis=0, keepdims=True)
    first = (scaled * vectors[0:1] + vectors[1:2]).astype(low).astype(wide)
    vector_ref[2:3] = jnp.sum(grad_logit[...] * first, axis=0, keepdims=True)
    pulled = grad_first * vectors[0:1]
    pulled = (
        pulled
        - jnp.mean(pulled, axis=-1, keepdims=True)
        - scaled * jnp.mean(pulled * scaled, axis=-1, keepdims=True)
    )
    out_ref[...] = (grad_hidden[...] + inverse * pulled).astype(low)


def token_back(tokens, placing, grad_sent, grad_hidden, grad_logit, vectors):
    count, width = tokens.shape
    return pl.pallas_call(
        token_back_kernel,
        out_shape=(
            jax.ShapeDtypeStruct((count, width), low),
            jax.ShapeDtypeStruct((3, width), wide),
        ),
        in_specs=[in_hbm()] * 6,
        out_specs=(on_chip(),) * 2,
        scratch_shapes=fetch_scratch(
            (tokens, placing, grad_sent, grad_hidden, grad_logit, vectors)
        ),
        compiler_params=params(17),
        cost_estimate=cost(2 * count * width * placing.shape[1], 12 * count * width),
    )(tokens, placing, grad_sent, grad_hidden, grad_logit, vectors)


def flip_pairs(flip):
    return [(i, i ^ flip) for i in range(32)]


def all_sum(value):
    value = value + send(value, swap_pairs())
    for one, two in ((2, 4), (8, 16)):
        near = value + send(value, flip_pairs(one))
        far = send(value, flip_pairs(two)) + send(value, flip_pairs(one + two))
        value = near + far
    return value


def exchange(value, n_data):
    capacity, width = value.shape
    moved = lax.all_to_all(
        value.reshape(n_data, capacity // n_data, width), "dp", split_axis=0, concat_axis=0, tiled=True
    )
    return moved.reshape(capacity, width)


def block_shards(
    tokens,
    cotangent,
    selected,
    packing,
    segments,
    blocks,
    left_stat,
    right_stat,
    left_root,
    right_root,
    vectors,
    moment,
):
    model_width = tokens.shape[2]
    token_count = tokens.shape[0] * tokens.shape[1]
    n_data = lax.axis_size("dp")
    capacity = packing.shape[1]
    line, place, core = here()
    own_tokens = tokens.reshape(token_count, model_width)
    above = cotangent.reshape(token_count, model_width)
    segment = segments[0]

    every = columns_by_core(jnp.transpose(blocks, (1, 0, 2)).astype(low))
    placing, packed, gates = pack_tokens(
        own_tokens, selected.reshape(token_count), packing[0], vectors
    )
    buffer = exchange(packed, n_data)
    attn_two = send(every[:4], line_pairs(2))
    ffn_got = send(after(every[4:], attn_two), line_pairs(2))
    attn_pair = jnp.stack([every[:4], attn_two])
    attn_got = send(attn_pair, line_pairs(1))
    line_attn = after(jnp.concatenate([attn_pair, attn_got]), packed)
    ffn_two = jnp.stack([every[4:], after(ffn_got, attn_got)])
    near_attn = send(line_attn, plane_pairs(0))
    every_root = roots_by_core(after(left_root, ffn_two), right_root)
    first_attn = after(jnp.stack([line_attn, near_attn]), every_root, buffer)
    far_attn = send(first_attn, plane_pairs(1))
    line_ffn = gather_far(ffn_two)
    near_ffn = send(after(line_ffn, near_attn), plane_pairs(0))
    root_given = lax.optimization_barrier((*roots_given(every_root), buffer, line_ffn))[:4]
    root_parts = [root_given[0]]
    for flip in (1, 2, 3):
        root_parts.append(send(root_given[flip], line_pairs(flip)))
    w_parts = with_other(first_attn, far_attn)
    answer, store = attend(buffer, w_parts, segment)
    first_ffn = jnp.stack([line_ffn, near_ffn])
    returned = exchange(answer, n_data)
    far_ffn = after(send(after(first_ffn, far_attn, *root_parts[1:]), plane_pairs(1)), returned)
    left_line, right_line = (jnp.stack([part[:, kind] for part in root_parts]) for kind in range(2))
    ffn_parts = with_other(first_ffn, far_ffn)

    near_right = send(after(right_line, far_ffn), plane_pairs(0))
    first_right = jnp.stack([right_line, near_right])
    hidden, second_low, active, slope, w_up = token_forward(
        own_tokens, placing, returned, gates, vectors, ffn_parts
    )
    down_theirs = outer_theirs(after(active, near_right), above[None])
    far_right = send(first_right, plane_pairs(1))
    roots = (left_line, send(left_line, swap_pairs()), first_right, far_right)
    down_got = send(down_theirs, swap_pairs())
    down_give, *down_kept = sum_start(lambda step: step, active, above[None], down_got)
    down_got = send(down_give, plane_pairs(0))
    mixed, grad_packed, grad_hidden, grad_logit, vector_two, grad_inner = token_backward(
        above,
        hidden,
        active,
        slope,
        placing,
        returned,
        gates,
        vectors,
        after(w_up, down_give, far_right),
        ffn_parts,
    )
    grad_answer = exchange(grad_packed, n_data)
    up_theirs = outer_theirs(after(second_low, down_got)[None], grad_inner)

    down_kept, down_give = add_first(down_got, *down_kept)
    down_got = send(down_give, plane_pairs(1))
    up_got = send(after(up_theirs, grad_answer), swap_pairs())
    attn_theirs, grads, grad_buffer, sides = attend_back(store, segment, grad_answer)
    attn_got = send(after(attn_theirs, down_got), swap_pairs())
    up_give, *up_kept = sum_start(
        lambda step: 0, second_low[None], grad_inner, after(up_got, attn_theirs)
    )
    up_got = send(up_give, plane_pairs(0))
    down_own, down_two, down_give = cut_line((down_kept + down_got.astype(wide))[None])
    down_got = send(down_give, line_pairs(1))
    attn_give, *attn_kept = sum_start(
        lambda step: step // 3, sides, grads, after(attn_got, up_give)
    )
    attn_got = send(attn_give, plane_pairs(0))
    grad_sent = exchange(after(grad_buffer, attn_give), n_data)
    down_own, down_give = add_line(down_own, down_two, down_got)
    down_got = send(down_give, line_pairs(2))
    down_own = (down_own + down_got.astype(wide)).astype(low)
    down_near = send(down_own, plane_pairs(0))
    down_first = jnp.stack([down_own, down_near])
    down_far = send(down_first, plane_pairs(1))
    down_mine = jnp.concatenate([down_first, down_far])
    down_theirs = send(down_mine, swap_pairs())

    up_kept, up_give = add_first(up_got, *up_kept)
    attn_kept, attn_give = add_first(after(attn_got, down_far), *attn_kept)
    pair_got = send(jnp.stack([attn_give, up_give]), plane_pairs(1))
    down_made, down_square = step_chunks(down_mine, down_theirs, roots, 2)
    down_parts = return_chunks(down_made)
    pair_got = after(pair_got, down_made, grad_sent)
    pair_kept = jnp.stack([attn_kept, up_kept]) + pair_got.astype(wide)
    pair_own, pair_two, pair_give = cut_line(pair_kept)
    pair_got = send(pair_give, line_pairs(1))
    grad_tokens, vector_one = token_back(
        own_tokens, placing, grad_sent, grad_hidden, grad_logit, vectors
    )
    pair_own, pair_give = add_line(pair_own, pair_two, pair_got)
    pair_got = send(after(pair_give, vector_one), line_pairs(2))
    down = jnp.stack(down_parts)
    down_other = send(down, [(i, i ^ 1) for i in range(0, 32, 2)])
    pair_own = (pair_own + pair_got.astype(wide)).astype(low)
    pair_near = send(pair_own, plane_pairs(0))
    pair_first = jnp.stack([pair_own, pair_near])
    pair_far = send(pair_first, plane_pairs(1))
    pair_mine = jnp.concatenate([pair_first, pair_far])
    pair_theirs = send(after(pair_mine, *down_parts[1:]), swap_pairs())
    pair_made, pair_square = step_chunks(pair_mine, pair_theirs, roots, 0)
    pair = jnp.stack(return_chunks(pair_made))
    pair_other = send(pair, swap_pairs())
    squares = jnp.concatenate([jnp.sum(pair_square, axis=2), jnp.sum(down_square, axis=2)])
    lane = lax.broadcasted_iota(jnp.int32, (1, model_width), 1)
    square_row = sum(
        jnp.where(lane == 4 * chunk + line, squares[chunk], 0.0) for chunk in range(3)
    )
    sums = all_sum(jnp.concatenate([vector_one, vector_two, square_row]))
    vector_grad = sums[:5]
    size = model_width * model_width
    scales = block_rate * lax.rsqrt(sums[5, :12] / size + norm_eps)
    grad_own, left_new, right_new, new_blocks = update_blocks(
        pair, pair_other, down, down_other, blocks, left_stat, right_stat, scales
    )
    moment_new = 0.5 * moment + 0.5 * vector_grad
    row_squares = jnp.mean(moment_new * moment_new, axis=1, keepdims=True)
    vector_new = vectors - vector_rate * moment_new * lax.rsqrt(row_squares + norm_eps)
    return (
        mixed.reshape(tokens.shape),
        grad_tokens.reshape(tokens.shape),
        grad_own,
        left_new,
        right_new,
        new_blocks,
        vector_grad,
        moment_new,
        vector_new,
    )


def shards(
    tokens,
    cotangent,
    selected,
    packing,
    segments,
    blocks,
    left_stat,
    right_stat,
    left_root,
    right_root,
    vectors,
    moment,
):
    model_width = tokens.shape[2]
    token_count = tokens.shape[0] * tokens.shape[1]
    n_data = lax.axis_size("dp")
    n_owner = lax.axis_size("own")
    shard_rows = blocks.shape[0]
    own_blocks = blocks.shape[1]
    up_blocks = (own_blocks * n_owner - 4) // 2
    capacity = packing.shape[1]
    per_peer = capacity // n_data
    head_count = model_width // HEAD_DIM
    score_scale = HEAD_DIM ** (-0.5)
    flat_weights = blocks.astype(jnp.bfloat16).reshape(1, shard_rows * own_blocks * model_width)
    gathered = lax.all_gather(flat_weights, ("dp", "own"), axis=0, tiled=True)
    gathered = gathered.reshape(n_data, n_owner, shard_rows, own_blocks, model_width)

    def matrix(number):
        return gathered[:, number // own_blocks, :, number % own_blocks, :].reshape(
            model_width, model_width
        )

    w_query = matrix(0)
    w_key = matrix(1)
    w_value = matrix(2)
    w_out = matrix(3)
    w_up = jnp.concatenate([matrix(4 + position) for position in range(up_blocks)], axis=1)
    w_down = jnp.concatenate(
        [matrix(4 + up_blocks + position) for position in range(up_blocks)], axis=0
    )
    inputs = tokens.reshape(token_count, model_width).astype(jnp.float32)
    chosen = selected.reshape(token_count)
    normed_one, norm_one_back = jax.vjp(layer_norm, inputs, vectors[0], vectors[1])
    first_low = normed_one.astype(jnp.bfloat16)
    first_wide = first_low.astype(jnp.float32)
    gate_values = jax.nn.sigmoid(jnp.dot(first_wide, vectors[2], precision=highest))
    before = jnp.cumsum(chosen) - 1
    slot_index = jnp.where(chosen == 1, packing[0][jnp.clip(before, 0, capacity - 1)], -1)
    placing = (slot_index[None, :] == jnp.arange(capacity, dtype=jnp.int32)[:, None]).astype(
        jnp.bfloat16
    )
    packed = jnp.dot(placing, first_low, preferred_element_type=jnp.float32).astype(jnp.bfloat16)
    buffer = lax.all_to_all(
        packed.reshape(n_data, per_peer, model_width), "dp", split_axis=0, concat_axis=0, tiled=True
    )
    buffer = buffer.reshape(capacity, model_width)

    def project(matrix_in):
        made = jnp.dot(buffer, matrix_in, preferred_element_type=jnp.float32).astype(jnp.bfloat16)
        return made.reshape(capacity, head_count, HEAD_DIM)

    query_rows = project(w_query)
    key_rows = project(w_key)
    value_rows = project(w_value)
    segment = segments[0]
    block_rows = math.gcd(capacity, 512)
    starts = jnp.arange(capacity // block_rows, dtype=jnp.int32) * block_rows

    def masked_scores():
        scores = (
            jnp.einsum("qhd,khd->hqk", query_rows, key_rows, preferred_element_type=jnp.float32)
            * score_scale
        )
        same_segment = segment[:, None] == segment[None, :]
        return (jnp.where(same_segment[None, :, :], scores, -1e30), query_rows)

    def forward_block(first_row):
        scores, unused_block = masked_scores()
        largest = jnp.max(scores, axis=-1, keepdims=True)
        raised = jnp.exp(scores - largest)
        row_total = jnp.sum(raised, axis=-1, keepdims=True)
        shares = (raised / row_total).astype(jnp.bfloat16)
        context_part = jnp.einsum(
            "hqk,khd->qhd", shares, value_rows, preferred_element_type=jnp.float32
        )
        return (context_part.astype(jnp.bfloat16), largest[..., 0] + jnp.log(row_total[..., 0]))

    context_blocks, lse_blocks = lax.map(forward_block, starts)
    context = context_blocks.reshape(capacity, model_width)
    answer = jnp.dot(context, w_out, preferred_element_type=jnp.float32).astype(jnp.bfloat16)
    returned = lax.all_to_all(
        answer.reshape(n_data, per_peer, model_width), "dp", split_axis=0, concat_axis=0, tiled=True
    )
    returned = returned.reshape(capacity, model_width)
    unpacked = jnp.einsum("mt,md->td", placing, returned, preferred_element_type=jnp.float32)
    weighting = jnp.where(chosen == 1, gate_values, 0.0)
    hidden = inputs + weighting[:, None] * unpacked
    normed_two, norm_two_back = jax.vjp(layer_norm, hidden, vectors[3], vectors[4])
    second_low = normed_two.astype(jnp.bfloat16)
    pre_active = jnp.dot(second_low, w_up, preferred_element_type=jnp.float32)
    active_wide, gelu_back = jax.vjp(gelu_exact, pre_active)
    active = active_wide.astype(jnp.bfloat16)
    result = hidden + jnp.dot(active, w_down, preferred_element_type=jnp.float32)
    mixed = result.astype(jnp.bfloat16).reshape(tokens.shape)
    upstream = cotangent.reshape(token_count, model_width)
    grad_down = jnp.einsum("tf,td->fd", active, upstream, preferred_element_type=jnp.float32)
    grad_active = jnp.einsum("td,fd->tf", upstream, w_down, preferred_element_type=jnp.float32)
    grad_inner = gelu_back(grad_active)[0].astype(jnp.bfloat16)
    grad_up = jnp.einsum("td,tf->df", second_low, grad_inner, preferred_element_type=jnp.float32)
    grad_second = jnp.einsum("tf,df->td", grad_inner, w_up, preferred_element_type=jnp.float32)
    grad_hidden_part, grad_gain_two, grad_bias_two = norm_two_back(grad_second)
    grad_hidden = upstream.astype(jnp.float32) + grad_hidden_part
    grad_token_back = (grad_hidden * weighting[:, None]).astype(jnp.bfloat16)
    grad_packed = jnp.dot(placing, grad_token_back, preferred_element_type=jnp.float32).astype(
        jnp.bfloat16
    )
    router_pull = jnp.where(chosen == 1, jnp.sum(grad_hidden * unpacked, axis=-1), 0.0)
    grad_logit = router_pull * gate_values * (1.0 - gate_values)
    grad_answer = lax.all_to_all(
        grad_packed.reshape(n_data, per_peer, model_width),
        "dp",
        split_axis=0,
        concat_axis=0,
        tiled=True,
    )
    grad_answer = grad_answer.reshape(capacity, model_width)
    grad_out = jnp.einsum("md,me->de", context, grad_answer, preferred_element_type=jnp.float32)
    grad_context = jnp.einsum("me,de->md", grad_answer, w_out, preferred_element_type=jnp.float32)
    grad_context = grad_context.astype(jnp.bfloat16).reshape(capacity, head_count, HEAD_DIM)

    def backward_block(running, item_pair):
        first_row, lse_block = item_pair
        scores, query_block = masked_scores()
        shares_wide = jnp.exp(scores - lse_block[..., None])
        grad_shares = jnp.einsum(
            "qhd,khd->hqk", grad_context, value_rows, preferred_element_type=jnp.float32
        )
        inner_sum = jnp.sum(shares_wide * grad_shares, axis=-1, keepdims=True)
        grad_scores = (shares_wide * (grad_shares - inner_sum)).astype(jnp.bfloat16)
        grad_query_block = (
            jnp.einsum("hqk,khd->qhd", grad_scores, key_rows, preferred_element_type=jnp.float32)
            * score_scale
        )
        key_sum = (
            running[0]
            + jnp.einsum(
                "hqk,qhd->khd", grad_scores, query_block, preferred_element_type=jnp.float32
            )
            * score_scale
        )
        value_sum = running[1] + jnp.einsum(
            "hqk,qhd->khd",
            shares_wide.astype(jnp.bfloat16),
            grad_context,
            preferred_element_type=jnp.float32,
        )
        return ((key_sum, value_sum), grad_query_block)

    zeros_init = jnp.zeros((capacity, head_count, HEAD_DIM), jnp.float32)
    (key_total, value_total), query_grads = lax.scan(
        backward_block, (zeros_init, zeros_init), (starts, lse_blocks)
    )
    grad_query = query_grads.reshape(capacity, model_width).astype(jnp.bfloat16)
    grad_key = key_total.reshape(capacity, model_width).astype(jnp.bfloat16)
    grad_value = value_total.reshape(capacity, model_width).astype(jnp.bfloat16)
    grad_w_query = jnp.einsum("md,me->de", buffer, grad_query, preferred_element_type=jnp.float32)
    grad_w_key = jnp.einsum("md,me->de", buffer, grad_key, preferred_element_type=jnp.float32)
    grad_w_value = jnp.einsum("md,me->de", buffer, grad_value, preferred_element_type=jnp.float32)
    grad_buffer = jnp.einsum("me,de->md", grad_query, w_query, preferred_element_type=jnp.float32)
    grad_buffer = grad_buffer + jnp.einsum(
        "me,de->md", grad_key, w_key, preferred_element_type=jnp.float32
    )
    grad_buffer = grad_buffer + jnp.einsum(
        "me,de->md", grad_value, w_value, preferred_element_type=jnp.float32
    )
    grad_buffer = grad_buffer.astype(jnp.bfloat16)
    grad_sent = lax.all_to_all(
        grad_buffer.reshape(n_data, per_peer, model_width),
        "dp",
        split_axis=0,
        concat_axis=0,
        tiled=True,
    )
    grad_sent = grad_sent.reshape(capacity, model_width)
    grad_first = jnp.einsum("mt,md->td", placing, grad_sent, preferred_element_type=jnp.float32)
    grad_first = grad_first + grad_logit[:, None] * vectors[2][None, :]
    grad_router = jnp.sum(grad_logit[:, None] * first_wide, axis=0)
    grad_input_part, grad_gain_one, grad_bias_one = norm_one_back(grad_first)
    grad_tokens = (grad_hidden + grad_input_part).astype(jnp.bfloat16).reshape(tokens.shape)
    pieces = [grad_w_query, grad_w_key, grad_w_value, grad_out]
    pieces = pieces + [
        grad_up[:, position * model_width : (position + 1) * model_width]
        for position in range(up_blocks)
    ]
    pieces = pieces + [
        grad_down[position * model_width : (position + 1) * model_width, :]
        for position in range(up_blocks)
    ]
    local_terms = jnp.stack(pieces, axis=1)
    vector_terms = jnp.stack(
        [grad_gain_one, grad_bias_one, grad_router, grad_gain_two, grad_bias_two]
    )
    partial_value = lax.psum_scatter(local_terms, "dp", scatter_dimension=0, tiled=True)
    grad_own = lax.psum_scatter(
        partial_value.astype(jnp.bfloat16), "own", scatter_dimension=1, tiled=True
    ).astype(jnp.float32)
    vector_grad = lax.psum(vector_terms, ("dp", "own"))
    full_grad = lax.all_gather(grad_own.astype(jnp.bfloat16), "dp", axis=0, tiled=True).astype(
        grad_own.dtype
    )
    row_start = lax.axis_index("dp") * shard_rows
    left_new = 0.5 * left_stat + 0.5 * jnp.einsum(
        "rbk,nbk->rbn", grad_own, full_grad, precision=highest
    )
    column_part = lax.dynamic_slice_in_dim(full_grad, row_start, shard_rows, 2)
    right_new = 0.5 * right_stat + 0.5 * jnp.einsum(
        "nbr,nbk->rbk", column_part, full_grad, precision=highest
    )
    lefted = jnp.einsum("rbn,nbk->rbk", left_root, full_grad, precision=highest)
    precond = jnp.zeros_like(grad_own) + jnp.einsum(
        "rbn,nbk->rbk",
        lefted,
        lax.all_gather(right_root.astype(jnp.bfloat16), "dp", axis=0, tiled=True).astype(
            jnp.float32
        ),
        precision=highest,
    )
    square_sums = lax.psum(jnp.sum(precond * precond, axis=(0, 2)), "dp")
    step_scale = lax.rsqrt(square_sums / (model_width * model_width) + norm_eps)
    new_blocks = blocks - block_rate * precond * step_scale[None, :, None]
    moment_new = 0.5 * moment + 0.5 * vector_grad
    row_squares = jnp.mean(moment_new * moment_new, axis=1, keepdims=True)
    vector_new = vectors - vector_rate * moment_new * lax.rsqrt(row_squares + norm_eps)
    return (
        mixed,
        grad_tokens,
        grad_own,
        left_new,
        right_new,
        new_blocks,
        vector_grad,
        moment_new,
        vector_new,
    )


def solution(mesh):
    placed = (
        P(("dp", "own"), None, None),
        P(("dp", "own"), None, None),
        P(("dp", "own"), None),
        P(("dp", "own"), None),
        P(("dp", "own"), None),
        P("dp", "own", None),
        P("dp", "own", None),
        P("dp", "own", None),
        P("dp", "own", None),
        P("dp", "own", None),
        P(),
        P(),
    )
    small = mesh.shape["dp"] == 16 and mesh.shape["own"] == 2
    return jax.shard_map(
        block_shards if small else shards,
        mesh=mesh,
        in_specs=placed,
        out_specs=(
            P(("dp", "own"), None, None),
            P(("dp", "own"), None, None),
            P("dp", "own", None),
            P("dp", "own", None),
            P("dp", "own", None),
            P("dp", "own", None),
            P(),
            P(),
            P(),
        ),
        check_vma=False,
    )
```

```python
import functools
import math

import jax
import jax.numpy as jnp
from jax import lax
from jax.experimental import pallas as pl
from jax.experimental.pallas import tpu as pltpu
from jax.sharding import PartitionSpec as P

HEAD_DIM = 64


norm_eps = 1e-06
block_rate = 0.03
vector_rate = 0.04
highest = lax.Precision.HIGHEST


def layer_norm(values, norm_gain, norm_bias):
    center = values - jnp.mean(values, axis=-1, keepdims=True)
    spread = jnp.mean(center * center, axis=-1, keepdims=True)
    return center * lax.rsqrt(spread + norm_eps) * norm_gain + norm_bias


def gelu_exact(values):
    return jax.nn.gelu(values, approximate=False)


BOTH = ("dp", "own")
low = jnp.bfloat16
wide = jnp.float32
MIB = 2**20


def swap_pairs():
    return [(i, i ^ 1) for i in range(32)]


def plane_pairs(step):
    pairs = []
    for i in range(32):
        place, core = i // 2, i % 2
        flip = (1, 2)[step ^ core]
        pairs.append((i, (place ^ flip) * 2 + core))
    return pairs


def line_pairs(flip):
    return [(i, i ^ (8 * flip)) for i in range(32)]


def send(value, pairs):
    return lax.ppermute(value, BOTH, pairs)


def after(value, *others):
    return lax.optimization_barrier((value,) + others)[0]


def pick(value, index, axis):
    return lax.dynamic_index_in_dim(value, index, axis, keepdims=False)


def first_core():
    return lax.axis_index("own") == 0


def halves(value):
    middle = value.shape[-1] // 2
    lower, upper = value[..., :middle], value[..., middle:]
    return jnp.where(first_core(), lower, upper), jnp.where(first_core(), upper, lower)


def in_core_order(mine, theirs, axis):
    return jnp.where(
        first_core(),
        jnp.concatenate([mine, theirs], axis=axis),
        jnp.concatenate([theirs, mine], axis=axis),
    )


LINE_FLIPS = (0, 2, 1, 3)


def flipped(index, flip):
    return jnp.bitwise_xor(index, flip)


def spots(place, half):
    first, second = half + 1, 2 - half
    return [
        place,
        flipped(place, first),
        flipped(place, second),
        flipped(place, 3),
    ]


def here():
    device = lax.axis_index("dp")
    return device // 4, device % 4, lax.axis_index("own")


def dot(left, right, left_axis=1, right_axis=0):
    return lax.dot_general(
        left, right, (((left_axis,), (right_axis,)), ((), ())), preferred_element_type=wide
    )


def on_chip():
    return pl.BlockSpec(memory_space=pltpu.VMEM)


def whole(value):
    return pl.BlockSpec(value.shape, lambda *steps: (0,) * value.ndim)


def in_hbm():
    return pl.BlockSpec(memory_space=pltpu.HBM)


def fetch_scratch(values):
    return [pltpu.VMEM(value.shape, value.dtype) for value in values] + [
        pltpu.SemaphoreType.DMA((len(values),))
    ]


def fetch(sources, targets, sems):
    copies = [
        pltpu.make_async_copy(source, target, sems.at[number])
        for number, (source, target) in enumerate(zip(sources, targets))
    ]
    for copy in copies:
        copy.start()
    return copies


def finish(copies):
    for copy in copies:
        copy.wait()


def params(limit):
    return pltpu.CompilerParams(vmem_limit_bytes=limit * MIB)


def cost(flops, moved):
    return pl.CostEstimate(flops=flops, bytes_accessed=moved, transcendentals=0)


def place_block(parts, block, target):
    line, place, core = here()
    rows, columns = parts[0].shape[3:]
    for other in range(2):
        half = core if other == 0 else 1 - core
        column_slice = pl.ds(pl.multiple_of(half * columns, columns), columns)
        for number, spot in enumerate(spots(place, half)):
            for index, flip in enumerate(LINE_FLIPS):
                start = (flipped(line, flip) * 4 + spot) * rows
                row_slice = pl.ds(pl.multiple_of(start, rows), rows)
                piece = parts[2 * other + number // 2][number % 2, index, block]
                target[row_slice, column_slice] = piece


def columns_by_core(value):
    keep, give = halves(value)
    return in_core_order(keep, send(give, swap_pairs()), 0)


def gather_far(pair):
    return jnp.concatenate([pair, send(pair, line_pairs(1))])


def with_other(first, far):
    return [first, far, send(first, swap_pairs()), send(far, swap_pairs())]


def roots_by_core(left_root, right_root):
    both = [jnp.transpose(root, (1, 0, 2)).astype(low) for root in (left_root, right_root)]
    every = columns_by_core(jnp.stack(both, axis=1))
    return every.reshape((3, 4) + every.shape[1:])


def roots_given(every):
    line, place, core = here()
    return [pick(every, flipped(line, flip), 1) for flip in range(4)]


def sum_kernel(left_of, left, right, got, give_ref, kept_ref, passed_ref, total):
    line, place, core = here()
    step = pl.program_id(0)
    columns = got.shape[2]
    rows = kept_ref.shape[2]
    part = pl.ds(pl.multiple_of(core * columns, columns), columns)
    right_step = step if right.shape[0] > 1 else 0
    made = dot(left[left_of(step)], right[right_step, :, part], 0, 0)
    total[...] = made + got[step].astype(wide)
    own, first, second, both = spots(place, core)
    for row_line in range(4):

        def piece(spot):
            return total[pl.ds(pl.multiple_of((row_line * 4 + spot) * rows, rows), rows), :]

        give_ref[0, step, row_line] = piece(first).astype(low)
        give_ref[1, step, row_line] = piece(both).astype(low)
        kept_ref[step, row_line] = piece(own).astype(low)
        passed_ref[step, row_line] = piece(second).astype(low)


def sum_start(left_of, left, right, got):
    count, width = left.shape[1:]
    blocks, full, columns = got.shape
    shape = (blocks, 4, full // 16, columns)
    return pl.pallas_call(
        functools.partial(sum_kernel, left_of),
        grid=(blocks,),
        out_shape=(
            jax.ShapeDtypeStruct((2,) + shape, low),
            jax.ShapeDtypeStruct(shape, low),
            jax.ShapeDtypeStruct(shape, low),
        ),
        in_specs=[on_chip()] * 3,
        out_specs=(on_chip(),) * 3,
        scratch_shapes=[pltpu.VMEM((full, columns), wide)],
        compiler_params=params(12),
        cost_estimate=cost(blocks * count * width * width, 5 * blocks * width * width),
    )(left, right, got)


def add_first(got, kept, passed):
    kept = kept.astype(wide) + got[0].astype(wide)
    return kept, (passed.astype(wide) + got[1].astype(wide)).astype(low)


def cut_line(kept):
    line, place, core = here()
    given = jnp.stack([pick(kept, flipped(line, flip), 1) for flip in (1, 3)]).astype(low)
    return pick(kept, line, 1), pick(kept, flipped(line, 2), 1), given


def add_line(own, two, got):
    return own + got[0].astype(wide), (two + got[1].astype(wide)).astype(low)


def step_kernel(
    number,
    mine,
    theirs,
    left_mine_from,
    left_theirs_from,
    right_first_from,
    right_far_from,
    out_ref,
    square_ref,
    grad_ref,
    rows_ref,
    left_ref,
    right_ref,
    cross_ref,
    left_mine,
    left_theirs,
    right_first,
    right_far,
    sems,
):
    chunk = number + pl.program_id(0)
    copies = fetch(
        [
            left_mine_from.at[:, chunk],
            left_theirs_from.at[:, chunk],
            right_first_from.at[:, :, chunk],
            right_far_from.at[:, :, chunk],
        ],
        [left_mine, left_theirs, right_first, right_far],
        sems,
    )
    line, place, core = here()
    rows, columns = mine.shape[3:]

    def rows_of(row_line, spot):
        return pl.ds(pl.multiple_of((row_line * 4 + spot) * rows, rows), rows)

    def column_half(half):
        return pl.ds(pl.multiple_of(half * columns, columns), columns)

    for half, group in ((core, mine), (1 - core, theirs)):
        for number, spot in enumerate(spots(place, half)):
            for step in range(4):
                grad_ref[rows_of(step, spot), column_half(half)] = group[number, 0, step]
    finish(copies)
    for half, left in ((core, left_mine), (1 - core, left_theirs)):
        for flip in range(4):
            target = pl.ds(pl.multiple_of(flipped(line, flip) * rows, rows), rows)
            left_ref[target, column_half(half)] = left[flip]
    for number, spot in enumerate(spots(place, core)):
        source = right_far if number > 1 else right_first
        for flip in range(4):
            right_ref[rows_of(flipped(line, flip), spot), :] = source[number % 2, flip]
    for row_line in range(4):
        rows_ref[row_line * rows : (row_line + 1) * rows, :] = grad_ref[rows_of(row_line, place), :]
    left = dot(rows_ref[...], grad_ref[column_half(core), :], 1, 1)
    cross_ref[...] = dot(grad_ref[...], grad_ref[:, column_half(core)], 0, 0)
    lefted = dot(left_ref[...], grad_ref[...]).astype(low)
    stepped = dot(lefted, right_ref[...])
    square_ref[0] = jnp.sum(stepped * stepped, axis=0, keepdims=True)
    for row_line in range(4):
        part = slice(row_line * rows, (row_line + 1) * rows)
        out_ref[0, row_line, 0] = mine[0, 0, row_line]
        out_ref[0, row_line, 1] = left[part].astype(low)
        out_ref[0, row_line, 2] = cross_ref[rows_of(row_line, place), :].astype(low)
        out_ref[0, row_line, 3] = stepped[part].astype(low)


def step_chunks(mine, theirs, roots, number):
    chunks, lines, rows, columns = mine.shape[1:]
    full = rows * 16
    grad_spec = pl.BlockSpec((4, 1, lines, rows, columns), lambda step: (0, step, 0, 0, 0))
    return pl.pallas_call(
        functools.partial(step_kernel, number),
        grid=(chunks,),
        out_shape=(
            jax.ShapeDtypeStruct((chunks, lines, 4, rows, columns), low),
            jax.ShapeDtypeStruct((chunks, 1, columns), wide),
        ),
        in_specs=[grad_spec] * 2 + [in_hbm()] * 4,
        out_specs=(
            pl.BlockSpec((1, lines, 4, rows, columns), lambda step: (step, 0, 0, 0, 0)),
            pl.BlockSpec((1, 1, columns), lambda step: (step, 0, 0)),
        ),
        scratch_shapes=[
            pltpu.VMEM((full, columns * 2), low),
            pltpu.VMEM((lines * rows, columns * 2), low),
            pltpu.VMEM((lines * rows, columns * 2), low),
            pltpu.VMEM((full, columns), low),
            pltpu.VMEM((full, columns), wide),
            pltpu.VMEM((lines, rows, columns), low),
            pltpu.VMEM((lines, rows, columns), low),
            pltpu.VMEM((2, lines, rows, columns), low),
            pltpu.VMEM((2, lines, rows, columns), low),
            pltpu.SemaphoreType.DMA((4,)),
        ],
        compiler_params=params(56),
        cost_estimate=cost(3 * chunks * full**3, 16 * chunks * full * full),
    )(mine, theirs, *roots)


def return_chunks(made):
    line, place, core = here()
    parts = [pick(made, line, 1)]
    for flip in (1, 2, 3):
        parts.append(send(pick(made, flipped(line, flip), 1), line_pairs(flip)))
    return parts


def last_kernel(
    pair, pair_other, down, down_other, blocks, left_stat, right_stat, scales, *outs
):
    grad_out, left_out, right_out, block_out = outs
    line, place, core = here()
    columns = pair.shape[4]

    def update(number, which, mine, theirs):
        for (source, index), half in ((mine, which), (theirs, 1 - which)):
            part = slice(half * columns, (half + 1) * columns)
            pieces = [source[index + (kind,)].astype(wide) for kind in range(4)]
            grad_out[number, :, part] = pieces[0]
            left_out[number, :, part] = 0.5 * left_stat[number, :, part] + 0.5 * pieces[1]
            right_out[number, :, part] = 0.5 * right_stat[number, :, part] + 0.5 * pieces[2]
            step = pieces[3] * scales[6 * which + number]
            block_out[number, :, part] = blocks[number, :, part] - step

    @pl.when(core == 0)
    def first():
        for number in range(6):
            index = (flipped(line, number % 4), number // 4)
            update(number, 0, (pair, index), (pair_other, index))

    @pl.when(core == 1)
    def second():
        for number in range(6):
            source, other = (pair, pair_other) if number < 2 else (down, down_other)
            index = (flipped(line, (number + 2) % 4), 1 if number < 2 else 0)
            update(number, 1, (source, index), (other, index))


def update_blocks(pair, pair_other, down, down_other, blocks, left_stat, right_stat, scales):
    turned = [jnp.transpose(value, (1, 0, 2)) for value in (blocks, left_stat, right_stat)]
    shape = jax.ShapeDtypeStruct(turned[0].shape, wide)
    outs = pl.pallas_call(
        last_kernel,
        out_shape=(shape,) * 4,
        in_specs=[on_chip()] * 7 + [pl.BlockSpec(memory_space=pltpu.SMEM)],
        out_specs=(on_chip(),) * 4,
        compiler_params=params(10),
        cost_estimate=cost(0, 32 * shape.size),
    )(pair, pair_other, down, down_other, *turned, scales)
    return [jnp.transpose(value, (1, 0, 2)) for value in outs]


def head_masks():
    lane = lax.broadcasted_iota(jnp.int32, (1, 2 * HEAD_DIM), 1)
    return [(lane < HEAD_DIM).astype(wide).astype(low), (lane >= HEAD_DIM).astype(wide).astype(low)]


def head_shares(query, key, same):
    scores = dot(query, key, 1, 1) * HEAD_DIM ** (-0.5)
    scores = jnp.where(same, scores, -1e30)
    raised = jnp.exp(scores - jnp.max(scores, axis=-1, keepdims=True))
    return raised / jnp.sum(raised, axis=-1, keepdims=True)


STORE_ROWS = 32768


def store_views(store, rows, width):
    weights = [store.at[pl.ds(block * width, width)] for block in range(4)]
    made = [store.at[pl.ds(4 * width + kind * rows, rows)] for kind in range(3)]
    sides = [store.at[pl.ds(4 * width + (3 + side) * rows, rows)] for side in range(2)]
    return weights, made, sides


def attend_kernel(
    buffer, one, two, three, four, seg_column, seg_row, answer_ref, store, weights, made, sides, sems
):
    rows, width = buffer.shape
    weights_out, made_out, sides_out = store_views(store, rows, width)
    for block in range(4):
        place_block((one, two, three, four), block, weights.at[block])
    copies = fetch([weights.at[block] for block in range(4)], weights_out, sems)
    same = seg_column[...] == seg_row[...]
    for kind in range(3):
        made[kind] = dot(buffer[...], weights[kind]).astype(low)
    copies += fetch([made.at[kind] for kind in range(3)], made_out, sems.at[pl.ds(4, 3)])
    pair_width = 2 * HEAD_DIM
    for pair in range(width // pair_width):
        part = slice(pair * pair_width, (pair + 1) * pair_width)
        query, key, value = (made[kind, :, part] for kind in range(3))
        context = None
        for mask in head_masks():
            shares = head_shares(query, key * mask, same).astype(low)
            term = dot(shares, value * mask)
            context = term if context is None else context + term
        sides[1, :, part] = context.astype(low)
    sides[0] = buffer[...]
    copies += fetch([sides.at[side] for side in range(2)], sides_out, sems.at[pl.ds(7, 2)])
    answer_ref[...] = dot(sides[1], weights[3]).astype(low)
    finish(copies)


def attend_scratch(rows, width):
    return [
        pltpu.VMEM((4, width, width), low),
        pltpu.VMEM((3, rows, width), low),
        pltpu.VMEM((2, rows, width), low),
        pltpu.SemaphoreType.DMA((9,)),
    ]


def attend(buffer, parts, segment):
    rows, width = buffer.shape
    return pl.pallas_call(
        attend_kernel,
        out_shape=(
            jax.ShapeDtypeStruct((rows, width), low),
            jax.ShapeDtypeStruct((STORE_ROWS, width), low),
        ),
        in_specs=[on_chip()] * 7,
        out_specs=(on_chip(), in_hbm()),
        scratch_shapes=attend_scratch(rows, width),
        compiler_params=params(20),
        cost_estimate=cost(12 * rows * width * width, 12 * width * width),
    )(buffer, *parts, segment[:, None], segment[None, :])


def attend_back_kernel(
    store,
    seg_column,
    seg_row,
    grad_answer,
    theirs_ref,
    grads_ref,
    grad_buffer_ref,
    sides,
    grad_context_ref,
    weights,
    made,
    sems,
):
    rows, width = grad_answer.shape
    weights_from, made_from, sides_from = store_views(store, rows, width)
    out_copy, *copies = fetch(
        [weights_from[3]] + made_from + sides_from + weights_from[:3],
        [weights.at[3]]
        + [made.at[kind] for kind in range(3)]
        + [sides.at[side] for side in range(2)]
        + [weights.at[block] for block in range(3)],
        sems,
    )
    same = seg_column[...] == seg_row[...]
    core = lax.axis_index("own")
    out_copy.wait()
    grad_context_ref[...] = dot(grad_answer[...], weights[3], 1, 1).astype(low)
    finish(copies[:3])
    grads_ref[3] = grad_answer[...]
    pair_width = 2 * HEAD_DIM
    for pair in range(width // pair_width):
        part = slice(pair * pair_width, (pair + 1) * pair_width)
        query, key, value = (made[kind, :, part] for kind in range(3))
        above = grad_context_ref[:, part]
        sums = [None] * 3
        for mask in head_masks():
            key_head = key * mask
            shares = head_shares(query, key_head, same)
            grad_shares = dot(above, value * mask, 1, 1)
            inner = jnp.sum(shares * grad_shares, axis=-1, keepdims=True)
            grad_scores = (shares * (grad_shares - inner)).astype(low)
            terms = (
                dot(grad_scores, key_head),
                dot(grad_scores, query * mask, 0, 0),
                dot(shares.astype(low), above * mask, 0, 0),
            )
            sums = [
                term if total is None else total + term for term, total in zip(terms, sums)
            ]
        for kind, factor in enumerate((HEAD_DIM ** (-0.5), HEAD_DIM ** (-0.5), 1.0)):
            grads_ref[kind, :, part] = (sums[kind] * factor).astype(low)
    finish(copies[3:5])
    columns = theirs_ref.shape[2]
    part = pl.ds(pl.multiple_of((1 - core) * columns, columns), columns)
    for kind in range(4):
        theirs_ref[kind] = dot(sides[kind // 3], grads_ref[kind, :, part], 0, 0).astype(low)
    finish(copies[5:])
    total = dot(grads_ref[0], weights[0], 1, 1)
    total = total + dot(grads_ref[1], weights[1], 1, 1)
    total = total + dot(grads_ref[2], weights[2], 1, 1)
    grad_buffer_ref[...] = total.astype(low)


def attend_back(store, segment, grad_answer):
    rows, width = grad_answer.shape
    weights, made, sides, sems = attend_scratch(rows, width)
    return pl.pallas_call(
        attend_back_kernel,
        out_shape=(
            jax.ShapeDtypeStruct((4, width, width // 2), low),
            jax.ShapeDtypeStruct((4, rows, width), low),
            jax.ShapeDtypeStruct((rows, width), low),
            jax.ShapeDtypeStruct((2, rows, width), low),
        ),
        in_specs=[in_hbm()] + [on_chip()] * 3,
        out_specs=(on_chip(),) * 4,
        scratch_shapes=[pltpu.VMEM((rows, width), low), weights, made, sems],
        compiler_params=params(18),
        cost_estimate=cost(20 * rows * width * width, 16 * width * width),
    )(store, segment[:, None], segment[None, :], grad_answer)


def normal_parts(values):
    center = values - jnp.mean(values, axis=-1, keepdims=True)
    spread = jnp.mean(center * center, axis=-1, keepdims=True)
    return center, lax.rsqrt(spread + norm_eps)


def forward_kernel(*refs):
    tokens, placing, returned, gates, vectors = refs[:5]
    parts = refs[5:9]
    hidden_ref, second_ref, active_ref, slope_ref, w_up = refs[9:14]
    step = pl.program_id(0)

    @pl.when(step == 0)
    def prepare():
        values = tokens[...].astype(wide) + gates[:, 0:1] * dot(placing[...], returned[...])
        hidden_ref[...] = values
        center, inverse = normal_parts(values)
        second_ref[...] = (center * inverse * vectors[3:4] + vectors[4:5]).astype(low)

    place_block(parts, step, w_up.at[step])
    before = dot(second_ref[...], w_up[step])
    share = 0.5 + 0.5 * lax.erf(before * (0.5**0.5))
    density = jnp.exp(before * before * -0.5) * (0.5 / math.pi) ** 0.5
    active_ref[step] = (before * share).astype(low)
    slope_ref[step] = (share + before * density).astype(low)


def token_forward(tokens, placing, returned, gates, vectors, parts):
    count, width = tokens.shape
    blocks = parts[0].shape[2] // 2
    by_block = jax.ShapeDtypeStruct((blocks, count, width), low)
    fetched = (tokens, placing, returned, gates, vectors)
    return pl.pallas_call(
        forward_kernel,
        grid=(blocks,),
        out_shape=(
            jax.ShapeDtypeStruct((count, width), wide),
            jax.ShapeDtypeStruct((count, width), low),
            by_block,
            by_block,
            jax.ShapeDtypeStruct((blocks, width, width), low),
        ),
        in_specs=[whole(value) for value in fetched] + [on_chip()] * 4,
        out_specs=(on_chip(),) * 5,
        compiler_params=params(18),
        cost_estimate=cost(8 * blocks * count * width * width, 8 * blocks * width * width),
    )(*fetched, *parts)


def backward_kernel(*refs):
    above, placing, returned, gates, vectors = refs[:5]
    (hidden, active, slope, w_up), parts = refs[5:9], refs[9:13]
    mixed_ref, packed_ref, grad_hidden_ref, logit_ref, vector_ref, inner_ref = refs[13:19]
    result, grad_second, w_down = refs[19:22]
    step = pl.program_id(0)
    place_block(parts, 4 + step, w_down)

    @pl.when(step == 0)
    def prepare():
        result[...] = hidden[...]
        grad_second[...] = jnp.zeros_like(grad_second)

    grad_active = dot(above[...], w_down[...], 1, 1)
    grad_inner = (grad_active * slope[step].astype(wide)).astype(low)
    inner_ref[step] = grad_inner
    result[...] += dot(active[step], w_down[...])
    grad_second[...] += dot(grad_inner, w_up[step], 1, 1)

    @pl.when(step == pl.num_programs(0) - 1)
    def complete():
        mixed_ref[...] = result[...].astype(low)
        center, inverse = normal_parts(hidden[...])
        scaled = center * inverse
        grads = grad_second[...]
        vector_ref[0:1] = jnp.sum(grads * scaled, axis=0, keepdims=True)
        vector_ref[1:2] = jnp.sum(grads, axis=0, keepdims=True)
        pulled = grads * vectors[3:4]
        pulled = (
            pulled
            - jnp.mean(pulled, axis=-1, keepdims=True)
            - scaled * jnp.mean(pulled * scaled, axis=-1, keepdims=True)
        )
        grad_hidden = above[...].astype(wide) + inverse * pulled
        grad_hidden_ref[...] = grad_hidden
        weighted = (grad_hidden * gates[:, 0:1]).astype(low)
        packed_ref[...] = dot(placing[...], weighted, 0, 0).astype(low)
        unpacked = dot(placing[...], returned[...])
        logit_ref[...] = gates[:, 1:2] * jnp.sum(grad_hidden * unpacked, axis=-1, keepdims=True)


def token_backward(above, hidden, active, slope, placing, returned, gates, vectors, w_up, parts):
    count, width = above.shape
    slots = placing.shape[1]
    blocks = w_up.shape[0]
    fetched = (above, placing, returned, gates, vectors)
    return pl.pallas_call(
        backward_kernel,
        grid=(blocks,),
        out_shape=(
            jax.ShapeDtypeStruct((count, width), low),
            jax.ShapeDtypeStruct((slots, width), low),
            jax.ShapeDtypeStruct((count, width), wide),
            jax.ShapeDtypeStruct((count, 1), wide),
            jax.ShapeDtypeStruct((2, width), wide),
            jax.ShapeDtypeStruct((blocks, count, width), low),
        ),
        in_specs=[whole(value) for value in fetched] + [on_chip()] * 8,
        out_specs=(on_chip(),) * 6,
        scratch_shapes=[
            pltpu.VMEM((count, width), wide),
            pltpu.VMEM((count, width), wide),
            pltpu.VMEM((width, width), low),
        ],
        compiler_params=params(30),
        cost_estimate=cost(8 * blocks * count * width * width, 8 * blocks * width * width),
    )(*fetched, hidden, active, slope, w_up, *parts)


def outer_kernel(left, right, theirs_ref):
    core = lax.axis_index("own")
    step = pl.program_id(0)
    columns = theirs_ref.shape[2]
    left_step = step if left.shape[0] > 1 else 0
    right_step = step if right.shape[0] > 1 else 0
    part = pl.ds(pl.multiple_of((1 - core) * columns, columns), columns)
    theirs_ref[step] = dot(left[left_step], right[right_step, :, part], 0, 0).astype(low)


def outer_theirs(left, right):
    count, width = left.shape[1:]
    blocks = max(left.shape[0], right.shape[0])
    return pl.pallas_call(
        outer_kernel,
        grid=(blocks,),
        out_shape=jax.ShapeDtypeStruct((blocks, width, width // 2), low),
        in_specs=[on_chip()] * 2,
        out_specs=on_chip(),
        compiler_params=params(8),
        cost_estimate=cost(blocks * count * width * width, 3 * blocks * width * width),
    )(left, right)


def column(values):
    return values[:, None]


def pack_kernel(
    tokens, chosen, packing, vectors, placing_ref, packed_ref, gates_ref
):
    count = tokens.shape[0]
    capacity = packing.shape[0]
    center, inverse = normal_parts(tokens[...].astype(wide))
    first = (center * inverse * vectors[0:1] + vectors[1:2]).astype(low)
    gate = jax.nn.sigmoid(jnp.sum(first.astype(wide) * vectors[2:3], axis=-1, keepdims=True))
    weighting = jnp.where(chosen[...] == 1, gate, 0.0)
    gates_ref[:, 0:1] = weighting
    gates_ref[:, 1:2] = weighting * (1.0 - gate)
    above = lax.broadcasted_iota(jnp.int32, (count, count), 0)
    below = lax.broadcasted_iota(jnp.int32, (count, count), 1)
    earlier = (below <= above).astype(wide).astype(low)
    flags = jnp.broadcast_to(chosen[...].astype(wide), (count, capacity))
    rank = dot(earlier, flags.astype(low))
    place_of = lax.broadcasted_iota(jnp.int32, (count, capacity), 1).astype(wide) + 1.0
    ranked = jnp.where(rank == place_of, flags, 0.0).astype(low)
    slots = lax.broadcasted_iota(jnp.int32, (capacity, capacity), 1)
    slot_of = (packing[...] == slots).astype(wide).astype(low)
    placing = dot(ranked, slot_of).astype(low)
    placing_ref[...] = placing
    packed_ref[...] = dot(placing, first, 0, 0).astype(low)


def pack_tokens(tokens, chosen, packing, vectors):
    count, width = tokens.shape
    capacity = packing.shape[0]
    return pl.pallas_call(
        pack_kernel,
        out_shape=(
            jax.ShapeDtypeStruct((count, capacity), low),
            jax.ShapeDtypeStruct((capacity, width), low),
            jax.ShapeDtypeStruct((count, 2), wide),
        ),
        in_specs=[on_chip()] * 4,
        out_specs=(on_chip(),) * 3,
        compiler_params=params(10),
        cost_estimate=cost(4 * count * capacity * width, 8 * count * width),
    )(tokens, column(chosen), column(packing), vectors)


def token_back_kernel(*refs):
    sources, (out_ref, vector_ref), fetched, sems = refs[:6], refs[6:8], refs[8:14], refs[14]
    finish(fetch(sources, fetched, sems))
    tokens, placing, grad_sent, grad_hidden, grad_logit, vectors = fetched
    grad_first = dot(placing[...], grad_sent[...]) + grad_logit[...] * vectors[2:3]
    center, inverse = normal_parts(tokens[...].astype(wide))
    scaled = center * inverse
    vector_ref[0:1] = jnp.sum(grad_first * scaled, axis=0, keepdims=True)
    vector_ref[1:2] = jnp.sum(grad_first, axis=0, keepdims=True)
    first = (scaled * vectors[0:1] + vectors[1:2]).astype(low).astype(wide)
    vector_ref[2:3] = jnp.sum(grad_logit[...] * first, axis=0, keepdims=True)
    pulled = grad_first * vectors[0:1]
    pulled = (
        pulled
        - jnp.mean(pulled, axis=-1, keepdims=True)
        - scaled * jnp.mean(pulled * scaled, axis=-1, keepdims=True)
    )
    out_ref[...] = (grad_hidden[...] + inverse * pulled).astype(low)


def token_back(tokens, placing, grad_sent, grad_hidden, grad_logit, vectors):
    count, width = tokens.shape
    return pl.pallas_call(
        token_back_kernel,
        out_shape=(
            jax.ShapeDtypeStruct((count, width), low),
            jax.ShapeDtypeStruct((3, width), wide),
        ),
        in_specs=[in_hbm()] * 6,
        out_specs=(on_chip(),) * 2,
        scratch_shapes=fetch_scratch(
            (tokens, placing, grad_sent, grad_hidden, grad_logit, vectors)
        ),
        compiler_params=params(17),
        cost_estimate=cost(2 * count * width * placing.shape[1], 12 * count * width),
    )(tokens, placing, grad_sent, grad_hidden, grad_logit, vectors)


def flip_pairs(flip):
    return [(i, i ^ flip) for i in range(32)]


def all_sum(value):
    value = value + send(value, swap_pairs())
    for one, two in ((2, 4), (8, 16)):
        near = value + send(value, flip_pairs(one))
        far = send(value, flip_pairs(two)) + send(value, flip_pairs(one + two))
        value = near + far
    return value


def exchange(value, n_data):
    capacity, width = value.shape
    moved = lax.all_to_all(
        value.reshape(n_data, capacity // n_data, width), "dp", split_axis=0, concat_axis=0, tiled=True
    )
    return moved.reshape(capacity, width)


def block_shards(
    tokens,
    cotangent,
    selected,
    packing,
    segments,
    blocks,
    left_stat,
    right_stat,
    left_root,
    right_root,
    vectors,
    moment,
):
    model_width = tokens.shape[2]
    token_count = tokens.shape[0] * tokens.shape[1]
    n_data = lax.axis_size("dp")
    capacity = packing.shape[1]
    line, place, core = here()
    own_tokens = tokens.reshape(token_count, model_width)
    above = cotangent.reshape(token_count, model_width)
    segment = segments[0]

    every = columns_by_core(jnp.transpose(blocks, (1, 0, 2)).astype(low))
    placing, packed, gates = pack_tokens(
        own_tokens, selected.reshape(token_count), packing[0], vectors
    )
    buffer = exchange(packed, n_data)
    attn_two = send(every[:4], line_pairs(2))
    ffn_got = send(after(every[4:], attn_two), line_pairs(2))
    attn_pair = jnp.stack([every[:4], attn_two])
    attn_got = send(attn_pair, line_pairs(1))
    line_attn = after(jnp.concatenate([attn_pair, attn_got]), packed)
    ffn_two = jnp.stack([every[4:], after(ffn_got, attn_got)])
    near_attn = send(line_attn, plane_pairs(0))
    every_root = roots_by_core(after(left_root, near_attn), right_root)
    first_attn = after(jnp.stack([line_attn, near_attn]), buffer, ffn_got)
    far_attn = send(first_attn, plane_pairs(1))
    line_ffn = gather_far(ffn_two)
    near_ffn = send(after(line_ffn, far_attn), plane_pairs(0))
    root_given = lax.optimization_barrier((*roots_given(every_root), buffer, line_ffn))[:4]
    root_parts = [root_given[0]]
    for flip in (1, 2, 3):
        root_parts.append(send(root_given[flip], line_pairs(flip)))
    w_parts = with_other(first_attn, far_attn)
    answer, store = attend(buffer, w_parts, segment)
    left_line, right_line = (jnp.stack([part[:, kind] for part in root_parts]) for kind in range(2))
    first_ffn = jnp.stack([line_ffn, after(near_ffn, answer)])
    returned = exchange(answer, n_data)
    far_ffn = after(send(first_ffn, plane_pairs(1)), returned, right_line, left_line)
    ffn_parts = with_other(first_ffn, far_ffn)

    near_right = send(after(right_line, far_ffn), plane_pairs(0))
    first_right = jnp.stack([right_line, near_right])
    hidden, second_low, active, slope, w_up = token_forward(
        own_tokens, placing, returned, gates, vectors, ffn_parts
    )
    down_theirs = outer_theirs(after(active, near_right), above[None])
    far_right = send(first_right, plane_pairs(1))
    roots = (left_line, send(left_line, swap_pairs()), first_right, far_right)
    down_got = send(down_theirs, swap_pairs())
    down_give, *down_kept = sum_start(lambda step: step, active, above[None], down_got)
    down_got = send(down_give, plane_pairs(0))
    mixed, grad_packed, grad_hidden, grad_logit, vector_two, grad_inner = token_backward(
        above,
        hidden,
        active,
        slope,
        placing,
        returned,
        gates,
        vectors,
        after(w_up, down_give),
        ffn_parts,
    )
    grad_answer = exchange(grad_packed, n_data)
    up_theirs = outer_theirs(after(second_low, down_got, far_right)[None], grad_inner)

    down_kept, down_give = add_first(down_got, *down_kept)
    down_got = send(down_give, plane_pairs(1))
    up_got = send(after(up_theirs, grad_answer), swap_pairs())
    attn_theirs, grads, grad_buffer, sides = attend_back(store, segment, grad_answer)
    attn_got = send(after(attn_theirs, down_got), swap_pairs())
    up_give, *up_kept = sum_start(
        lambda step: 0, second_low[None], grad_inner, after(up_got, attn_theirs)
    )
    up_got = send(up_give, plane_pairs(0))
    down_own, down_two, down_give = cut_line((down_kept + down_got.astype(wide))[None])
    down_got = send(down_give, line_pairs(1))
    attn_give, *attn_kept = sum_start(
        lambda step: step // 3, sides, grads, after(attn_got, up_give)
    )
    attn_got = send(attn_give, plane_pairs(0))
    grad_sent = exchange(after(grad_buffer, attn_give), n_data)
    down_own, down_give = add_line(down_own, down_two, down_got)
    down_got = send(down_give, line_pairs(2))
    down_own = (down_own + down_got.astype(wide)).astype(low)
    down_near = send(down_own, plane_pairs(0))
    down_first = jnp.stack([down_own, down_near])
    down_far = send(down_first, plane_pairs(1))
    down_mine = jnp.concatenate([down_first, down_far])
    down_theirs = send(down_mine, swap_pairs())

    up_kept, up_give = add_first(up_got, *up_kept)
    attn_kept, attn_give = add_first(after(attn_got, down_far), *attn_kept)
    pair_got = send(jnp.stack([attn_give, up_give]), plane_pairs(1))
    down_made, down_square = step_chunks(down_mine, down_theirs, roots, 2)
    down_parts = return_chunks(down_made)
    pair_got = after(pair_got, down_made)
    pair_kept = jnp.stack([attn_kept, up_kept]) + pair_got.astype(wide)
    pair_own, pair_two, pair_give = cut_line(pair_kept)
    pair_got = send(pair_give, line_pairs(1))
    grad_tokens, vector_one = token_back(
        own_tokens, placing, grad_sent, grad_hidden, grad_logit, vectors
    )
    pair_own, pair_give = add_line(pair_own, pair_two, pair_got)
    pair_got = send(after(pair_give, vector_one), line_pairs(2))
    down = jnp.stack(down_parts)
    down_other = send(down, [(i, i ^ 1) for i in range(0, 32, 2)])
    pair_own = (pair_own + pair_got.astype(wide)).astype(low)
    pair_near = send(pair_own, plane_pairs(0))
    pair_first = jnp.stack([pair_own, pair_near])
    pair_far = send(pair_first, plane_pairs(1))
    pair_mine = jnp.concatenate([pair_first, pair_far])
    pair_theirs = after(send(pair_mine, swap_pairs()), *down_parts[1:])
    pair_made, pair_square = step_chunks(pair_mine, pair_theirs, roots, 0)
    pair = jnp.stack(return_chunks(pair_made))
    pair_other = send(pair, swap_pairs())
    squares = jnp.concatenate([jnp.sum(pair_square, axis=2), jnp.sum(down_square, axis=2)])
    lane = lax.broadcasted_iota(jnp.int32, (1, model_width), 1)
    square_row = sum(
        jnp.where(lane == 4 * chunk + line, squares[chunk], 0.0) for chunk in range(3)
    )
    sums = all_sum(jnp.concatenate([vector_one, vector_two, square_row]))
    vector_grad = sums[:5]
    size = model_width * model_width
    scales = block_rate * lax.rsqrt(sums[5, :12] / size + norm_eps)
    grad_own, left_new, right_new, new_blocks = update_blocks(
        pair, pair_other, down, down_other, blocks, left_stat, right_stat, scales
    )
    moment_new = 0.5 * moment + 0.5 * vector_grad
    row_squares = jnp.mean(moment_new * moment_new, axis=1, keepdims=True)
    vector_new = vectors - vector_rate * moment_new * lax.rsqrt(row_squares + norm_eps)
    return (
        mixed.reshape(tokens.shape),
        grad_tokens.reshape(tokens.shape),
        grad_own,
        left_new,
        right_new,
        new_blocks,
        vector_grad,
        moment_new,
        vector_new,
    )


def shards(
    tokens,
    cotangent,
    selected,
    packing,
    segments,
    blocks,
    left_stat,
    right_stat,
    left_root,
    right_root,
    vectors,
    moment,
):
    model_width = tokens.shape[2]
    token_count = tokens.shape[0] * tokens.shape[1]
    n_data = lax.axis_size("dp")
    n_owner = lax.axis_size("own")
    shard_rows = blocks.shape[0]
    own_blocks = blocks.shape[1]
    up_blocks = (own_blocks * n_owner - 4) // 2
    capacity = packing.shape[1]
    per_peer = capacity // n_data
    head_count = model_width // HEAD_DIM
    score_scale = HEAD_DIM ** (-0.5)
    flat_weights = blocks.astype(jnp.bfloat16).reshape(1, shard_rows * own_blocks * model_width)
    gathered = lax.all_gather(flat_weights, ("dp", "own"), axis=0, tiled=True)
    gathered = gathered.reshape(n_data, n_owner, shard_rows, own_blocks, model_width)

    def matrix(number):
        return gathered[:, number // own_blocks, :, number % own_blocks, :].reshape(
            model_width, model_width
        )

    w_query = matrix(0)
    w_key = matrix(1)
    w_value = matrix(2)
    w_out = matrix(3)
    w_up = jnp.concatenate([matrix(4 + position) for position in range(up_blocks)], axis=1)
    w_down = jnp.concatenate(
        [matrix(4 + up_blocks + position) for position in range(up_blocks)], axis=0
    )
    inputs = tokens.reshape(token_count, model_width).astype(jnp.float32)
    chosen = selected.reshape(token_count)
    normed_one, norm_one_back = jax.vjp(layer_norm, inputs, vectors[0], vectors[1])
    first_low = normed_one.astype(jnp.bfloat16)
    first_wide = first_low.astype(jnp.float32)
    gate_values = jax.nn.sigmoid(jnp.dot(first_wide, vectors[2], precision=highest))
    before = jnp.cumsum(chosen) - 1
    slot_index = jnp.where(chosen == 1, packing[0][jnp.clip(before, 0, capacity - 1)], -1)
    placing = (slot_index[None, :] == jnp.arange(capacity, dtype=jnp.int32)[:, None]).astype(
        jnp.bfloat16
    )
    packed = jnp.dot(placing, first_low, preferred_element_type=jnp.float32).astype(jnp.bfloat16)
    buffer = lax.all_to_all(
        packed.reshape(n_data, per_peer, model_width), "dp", split_axis=0, concat_axis=0, tiled=True
    )
    buffer = buffer.reshape(capacity, model_width)

    def project(matrix_in):
        made = jnp.dot(buffer, matrix_in, preferred_element_type=jnp.float32).astype(jnp.bfloat16)
        return made.reshape(capacity, head_count, HEAD_DIM)

    query_rows = project(w_query)
    key_rows = project(w_key)
    value_rows = project(w_value)
    segment = segments[0]
    block_rows = math.gcd(capacity, 512)
    starts = jnp.arange(capacity // block_rows, dtype=jnp.int32) * block_rows

    def masked_scores():
        scores = (
            jnp.einsum("qhd,khd->hqk", query_rows, key_rows, preferred_element_type=jnp.float32)
            * score_scale
        )
        same_segment = segment[:, None] == segment[None, :]
        return (jnp.where(same_segment[None, :, :], scores, -1e30), query_rows)

    def forward_block(first_row):
        scores, unused_block = masked_scores()
        largest = jnp.max(scores, axis=-1, keepdims=True)
        raised = jnp.exp(scores - largest)
        row_total = jnp.sum(raised, axis=-1, keepdims=True)
        shares = (raised / row_total).astype(jnp.bfloat16)
        context_part = jnp.einsum(
            "hqk,khd->qhd", shares, value_rows, preferred_element_type=jnp.float32
        )
        return (context_part.astype(jnp.bfloat16), largest[..., 0] + jnp.log(row_total[..., 0]))

    context_blocks, lse_blocks = lax.map(forward_block, starts)
    context = context_blocks.reshape(capacity, model_width)
    answer = jnp.dot(context, w_out, preferred_element_type=jnp.float32).astype(jnp.bfloat16)
    returned = lax.all_to_all(
        answer.reshape(n_data, per_peer, model_width), "dp", split_axis=0, concat_axis=0, tiled=True
    )
    returned = returned.reshape(capacity, model_width)
    unpacked = jnp.einsum("mt,md->td", placing, returned, preferred_element_type=jnp.float32)
    weighting = jnp.where(chosen == 1, gate_values, 0.0)
    hidden = inputs + weighting[:, None] * unpacked
    normed_two, norm_two_back = jax.vjp(layer_norm, hidden, vectors[3], vectors[4])
    second_low = normed_two.astype(jnp.bfloat16)
    pre_active = jnp.dot(second_low, w_up, preferred_element_type=jnp.float32)
    active_wide, gelu_back = jax.vjp(gelu_exact, pre_active)
    active = active_wide.astype(jnp.bfloat16)
    result = hidden + jnp.dot(active, w_down, preferred_element_type=jnp.float32)
    mixed = result.astype(jnp.bfloat16).reshape(tokens.shape)
    upstream = cotangent.reshape(token_count, model_width)
    grad_down = jnp.einsum("tf,td->fd", active, upstream, preferred_element_type=jnp.float32)
    grad_active = jnp.einsum("td,fd->tf", upstream, w_down, preferred_element_type=jnp.float32)
    grad_inner = gelu_back(grad_active)[0].astype(jnp.bfloat16)
    grad_up = jnp.einsum("td,tf->df", second_low, grad_inner, preferred_element_type=jnp.float32)
    grad_second = jnp.einsum("tf,df->td", grad_inner, w_up, preferred_element_type=jnp.float32)
    grad_hidden_part, grad_gain_two, grad_bias_two = norm_two_back(grad_second)
    grad_hidden = upstream.astype(jnp.float32) + grad_hidden_part
    grad_token_back = (grad_hidden * weighting[:, None]).astype(jnp.bfloat16)
    grad_packed = jnp.dot(placing, grad_token_back, preferred_element_type=jnp.float32).astype(
        jnp.bfloat16
    )
    router_pull = jnp.where(chosen == 1, jnp.sum(grad_hidden * unpacked, axis=-1), 0.0)
    grad_logit = router_pull * gate_values * (1.0 - gate_values)
    grad_answer = lax.all_to_all(
        grad_packed.reshape(n_data, per_peer, model_width),
        "dp",
        split_axis=0,
        concat_axis=0,
        tiled=True,
    )
    grad_answer = grad_answer.reshape(capacity, model_width)
    grad_out = jnp.einsum("md,me->de", context, grad_answer, preferred_element_type=jnp.float32)
    grad_context = jnp.einsum("me,de->md", grad_answer, w_out, preferred_element_type=jnp.float32)
    grad_context = grad_context.astype(jnp.bfloat16).reshape(capacity, head_count, HEAD_DIM)

    def backward_block(running, item_pair):
        first_row, lse_block = item_pair
        scores, query_block = masked_scores()
        shares_wide = jnp.exp(scores - lse_block[..., None])
        grad_shares = jnp.einsum(
            "qhd,khd->hqk", grad_context, value_rows, preferred_element_type=jnp.float32
        )
        inner_sum = jnp.sum(shares_wide * grad_shares, axis=-1, keepdims=True)
        grad_scores = (shares_wide * (grad_shares - inner_sum)).astype(jnp.bfloat16)
        grad_query_block = (
            jnp.einsum("hqk,khd->qhd", grad_scores, key_rows, preferred_element_type=jnp.float32)
            * score_scale
        )
        key_sum = (
            running[0]
            + jnp.einsum(
                "hqk,qhd->khd", grad_scores, query_block, preferred_element_type=jnp.float32
            )
            * score_scale
        )
        value_sum = running[1] + jnp.einsum(
            "hqk,qhd->khd",
            shares_wide.astype(jnp.bfloat16),
            grad_context,
            preferred_element_type=jnp.float32,
        )
        return ((key_sum, value_sum), grad_query_block)

    zeros_init = jnp.zeros((capacity, head_count, HEAD_DIM), jnp.float32)
    (key_total, value_total), query_grads = lax.scan(
        backward_block, (zeros_init, zeros_init), (starts, lse_blocks)
    )
    grad_query = query_grads.reshape(capacity, model_width).astype(jnp.bfloat16)
    grad_key = key_total.reshape(capacity, model_width).astype(jnp.bfloat16)
    grad_value = value_total.reshape(capacity, model_width).astype(jnp.bfloat16)
    grad_w_query = jnp.einsum("md,me->de", buffer, grad_query, preferred_element_type=jnp.float32)
    grad_w_key = jnp.einsum("md,me->de", buffer, grad_key, preferred_element_type=jnp.float32)
    grad_w_value = jnp.einsum("md,me->de", buffer, grad_value, preferred_element_type=jnp.float32)
    grad_buffer = jnp.einsum("me,de->md", grad_query, w_query, preferred_element_type=jnp.float32)
    grad_buffer = grad_buffer + jnp.einsum(
        "me,de->md", grad_key, w_key, preferred_element_type=jnp.float32
    )
    grad_buffer = grad_buffer + jnp.einsum(
        "me,de->md", grad_value, w_value, preferred_element_type=jnp.float32
    )
    grad_buffer = grad_buffer.astype(jnp.bfloat16)
    grad_sent = lax.all_to_all(
        grad_buffer.reshape(n_data, per_peer, model_width),
        "dp",
        split_axis=0,
        concat_axis=0,
        tiled=True,
    )
    grad_sent = grad_sent.reshape(capacity, model_width)
    grad_first = jnp.einsum("mt,md->td", placing, grad_sent, preferred_element_type=jnp.float32)
    grad_first = grad_first + grad_logit[:, None] * vectors[2][None, :]
    grad_router = jnp.sum(grad_logit[:, None] * first_wide, axis=0)
    grad_input_part, grad_gain_one, grad_bias_one = norm_one_back(grad_first)
    grad_tokens = (grad_hidden + grad_input_part).astype(jnp.bfloat16).reshape(tokens.shape)
    pieces = [grad_w_query, grad_w_key, grad_w_value, grad_out]
    pieces = pieces + [
        grad_up[:, position * model_width : (position + 1) * model_width]
        for position in range(up_blocks)
    ]
    pieces = pieces + [
        grad_down[position * model_width : (position + 1) * model_width, :]
        for position in range(up_blocks)
    ]
    local_terms = jnp.stack(pieces, axis=1)
    vector_terms = jnp.stack(
        [grad_gain_one, grad_bias_one, grad_router, grad_gain_two, grad_bias_two]
    )
    partial_value = lax.psum_scatter(local_terms, "dp", scatter_dimension=0, tiled=True)
    grad_own = lax.psum_scatter(
        partial_value.astype(jnp.bfloat16), "own", scatter_dimension=1, tiled=True
    ).astype(jnp.float32)
    vector_grad = lax.psum(vector_terms, ("dp", "own"))
    full_grad = lax.all_gather(grad_own.astype(jnp.bfloat16), "dp", axis=0, tiled=True).astype(
        grad_own.dtype
    )
    row_start = lax.axis_index("dp") * shard_rows
    left_new = 0.5 * left_stat + 0.5 * jnp.einsum(
        "rbk,nbk->rbn", grad_own, full_grad, precision=highest
    )
    column_part = lax.dynamic_slice_in_dim(full_grad, row_start, shard_rows, 2)
    right_new = 0.5 * right_stat + 0.5 * jnp.einsum(
        "nbr,nbk->rbk", column_part, full_grad, precision=highest
    )
    lefted = jnp.einsum("rbn,nbk->rbk", left_root, full_grad, precision=highest)
    precond = jnp.zeros_like(grad_own) + jnp.einsum(
        "rbn,nbk->rbk",
        lefted,
        lax.all_gather(right_root.astype(jnp.bfloat16), "dp", axis=0, tiled=True).astype(
            jnp.float32
        ),
        precision=highest,
    )
    square_sums = lax.psum(jnp.sum(precond * precond, axis=(0, 2)), "dp")
    step_scale = lax.rsqrt(square_sums / (model_width * model_width) + norm_eps)
    new_blocks = blocks - block_rate * precond * step_scale[None, :, None]
    moment_new = 0.5 * moment + 0.5 * vector_grad
    row_squares = jnp.mean(moment_new * moment_new, axis=1, keepdims=True)
    vector_new = vectors - vector_rate * moment_new * lax.rsqrt(row_squares + norm_eps)
    return (
        mixed,
        grad_tokens,
        grad_own,
        left_new,
        right_new,
        new_blocks,
        vector_grad,
        moment_new,
        vector_new,
    )


def solution(mesh):
    placed = (
        P(("dp", "own"), None, None),
        P(("dp", "own"), None, None),
        P(("dp", "own"), None),
        P(("dp", "own"), None),
        P(("dp", "own"), None),
        P("dp", "own", None),
        P("dp", "own", None),
        P("dp", "own", None),
        P("dp", "own", None),
        P("dp", "own", None),
        P(),
        P(),
    )
    small = mesh.shape["dp"] == 16 and mesh.shape["own"] == 2
    return jax.shard_map(
        block_shards if small else shards,
        mesh=mesh,
        in_specs=placed,
        out_specs=(
            P(("dp", "own"), None, None),
            P(("dp", "own"), None, None),
            P("dp", "own", None),
            P("dp", "own", None),
            P("dp", "own", None),
            P("dp", "own", None),
            P(),
            P(),
            P(),
        ),
        check_vma=False,
    )
```

```python
import functools
import math

import jax
import jax.numpy as jnp
from jax import lax
from jax.experimental import pallas as pl
from jax.experimental.pallas import tpu as pltpu
from jax.sharding import PartitionSpec as P

HEAD_DIM = 64


norm_eps = 1e-06
block_rate = 0.03
vector_rate = 0.04
highest = lax.Precision.HIGHEST


def layer_norm(values, norm_gain, norm_bias):
    center = values - jnp.mean(values, axis=-1, keepdims=True)
    spread = jnp.mean(center * center, axis=-1, keepdims=True)
    return center * lax.rsqrt(spread + norm_eps) * norm_gain + norm_bias


def gelu_exact(values):
    return jax.nn.gelu(values, approximate=False)


BOTH = ("dp", "own")
low = jnp.bfloat16
wide = jnp.float32
MIB = 2**20


def swap_pairs():
    return [(i, i ^ 1) for i in range(32)]


def plane_pairs(step):
    pairs = []
    for i in range(32):
        place, core = i // 2, i % 2
        flip = (1, 2)[step ^ core]
        pairs.append((i, (place ^ flip) * 2 + core))
    return pairs


def line_pairs(flip):
    return [(i, i ^ (8 * flip)) for i in range(32)]


def send(value, pairs):
    return lax.ppermute(value, BOTH, pairs)


def after(value, *others):
    return lax.optimization_barrier((value,) + others)[0]


def pick(value, index, axis):
    return lax.dynamic_index_in_dim(value, index, axis, keepdims=False)


def first_core():
    return lax.axis_index("own") == 0


def halves(value):
    middle = value.shape[-1] // 2
    lower, upper = value[..., :middle], value[..., middle:]
    return jnp.where(first_core(), lower, upper), jnp.where(first_core(), upper, lower)


def in_core_order(mine, theirs, axis):
    return jnp.where(
        first_core(),
        jnp.concatenate([mine, theirs], axis=axis),
        jnp.concatenate([theirs, mine], axis=axis),
    )


LINE_FLIPS = (0, 2, 1, 3)


def flipped(index, flip):
    return jnp.bitwise_xor(index, flip)


def spots(place, half):
    first, second = half + 1, 2 - half
    return [
        place,
        flipped(place, first),
        flipped(place, second),
        flipped(place, 3),
    ]


def here():
    device = lax.axis_index("dp")
    return device // 4, device % 4, lax.axis_index("own")


def dot(left, right, left_axis=1, right_axis=0):
    return lax.dot_general(
        left, right, (((left_axis,), (right_axis,)), ((), ())), preferred_element_type=wide
    )


def on_chip():
    return pl.BlockSpec(memory_space=pltpu.VMEM)


def whole(value):
    return pl.BlockSpec(value.shape, lambda *steps: (0,) * value.ndim)


def in_hbm():
    return pl.BlockSpec(memory_space=pltpu.HBM)


def fetch_scratch(values):
    return [pltpu.VMEM(value.shape, value.dtype) for value in values] + [
        pltpu.SemaphoreType.DMA((len(values),))
    ]


def fetch(sources, targets, sems):
    copies = [
        pltpu.make_async_copy(source, target, sems.at[number])
        for number, (source, target) in enumerate(zip(sources, targets))
    ]
    for copy in copies:
        copy.start()
    return copies


def finish(copies):
    for copy in copies:
        copy.wait()


def params(limit):
    return pltpu.CompilerParams(vmem_limit_bytes=limit * MIB)


def cost(flops, moved):
    return pl.CostEstimate(flops=flops, bytes_accessed=moved, transcendentals=0)


def place_block(parts, block, target):
    line, place, core = here()
    rows, columns = parts[0].shape[3:]
    for other in range(2):
        half = core if other == 0 else 1 - core
        column_slice = pl.ds(pl.multiple_of(half * columns, columns), columns)
        for number, spot in enumerate(spots(place, half)):
            for index, flip in enumerate(LINE_FLIPS):
                start = (flipped(line, flip) * 4 + spot) * rows
                row_slice = pl.ds(pl.multiple_of(start, rows), rows)
                piece = parts[2 * other + number // 2][number % 2, index, block]
                target[row_slice, column_slice] = piece


def columns_by_core(value):
    keep, give = halves(value)
    return in_core_order(keep, send(give, swap_pairs()), 0)


def gather_far(pair):
    return jnp.concatenate([pair, send(pair, line_pairs(1))])


def with_other(first, far):
    return [first, far, send(first, swap_pairs()), send(far, swap_pairs())]


def roots_by_core(left_root, right_root):
    both = [jnp.transpose(root, (1, 0, 2)).astype(low) for root in (left_root, right_root)]
    every = columns_by_core(jnp.stack(both, axis=1))
    return every.reshape((3, 4) + every.shape[1:])


def roots_given(every):
    line, place, core = here()
    return [pick(every, flipped(line, flip), 1) for flip in range(4)]


def sum_kernel(left_of, left, right, got, give_ref, kept_ref, passed_ref, total):
    line, place, core = here()
    step = pl.program_id(0)
    columns = got.shape[2]
    rows = kept_ref.shape[2]
    part = pl.ds(pl.multiple_of(core * columns, columns), columns)
    right_step = step if right.shape[0] > 1 else 0
    made = dot(left[left_of(step)], right[right_step, :, part], 0, 0)
    total[...] = made + got[step].astype(wide)
    own, first, second, both = spots(place, core)
    for row_line in range(4):

        def piece(spot):
            return total[pl.ds(pl.multiple_of((row_line * 4 + spot) * rows, rows), rows), :]

        give_ref[0, step, row_line] = piece(first).astype(low)
        give_ref[1, step, row_line] = piece(both).astype(low)
        kept_ref[step, row_line] = piece(own).astype(low)
        passed_ref[step, row_line] = piece(second).astype(low)


def sum_start(left_of, left, right, got):
    count, width = left.shape[1:]
    blocks, full, columns = got.shape
    shape = (blocks, 4, full // 16, columns)
    return pl.pallas_call(
        functools.partial(sum_kernel, left_of),
        grid=(blocks,),
        out_shape=(
            jax.ShapeDtypeStruct((2,) + shape, low),
            jax.ShapeDtypeStruct(shape, low),
            jax.ShapeDtypeStruct(shape, low),
        ),
        in_specs=[on_chip()] * 3,
        out_specs=(on_chip(),) * 3,
        scratch_shapes=[pltpu.VMEM((full, columns), wide)],
        compiler_params=params(12),
        cost_estimate=cost(blocks * count * width * width, 5 * blocks * width * width),
    )(left, right, got)


def add_first(got, kept, passed):
    kept = kept.astype(wide) + got[0].astype(wide)
    return kept, (passed.astype(wide) + got[1].astype(wide)).astype(low)


def cut_line(kept):
    line, place, core = here()
    given = jnp.stack([pick(kept, flipped(line, flip), 1) for flip in (1, 3)]).astype(low)
    return pick(kept, line, 1), pick(kept, flipped(line, 2), 1), given


def add_line(own, two, got):
    return own + got[0].astype(wide), (two + got[1].astype(wide)).astype(low)


def step_kernel(
    number,
    mine,
    theirs,
    left_mine_from,
    left_theirs_from,
    right_first_from,
    right_far_from,
    out_ref,
    square_ref,
    grad_ref,
    rows_ref,
    left_ref,
    right_ref,
    cross_ref,
    left_mine,
    left_theirs,
    right_first,
    right_far,
    sems,
):
    chunk = number + pl.program_id(0)
    copies = fetch(
        [
            left_mine_from.at[:, chunk],
            left_theirs_from.at[:, chunk],
            right_first_from.at[:, :, chunk],
            right_far_from.at[:, :, chunk],
        ],
        [left_mine, left_theirs, right_first, right_far],
        sems,
    )
    line, place, core = here()
    rows, columns = mine.shape[3:]

    def rows_of(row_line, spot):
        return pl.ds(pl.multiple_of((row_line * 4 + spot) * rows, rows), rows)

    def column_half(half):
        return pl.ds(pl.multiple_of(half * columns, columns), columns)

    for half, group in ((core, mine), (1 - core, theirs)):
        for number, spot in enumerate(spots(place, half)):
            for step in range(4):
                grad_ref[rows_of(step, spot), column_half(half)] = group[number, 0, step]
    finish(copies)
    for half, left in ((core, left_mine), (1 - core, left_theirs)):
        for flip in range(4):
            target = pl.ds(pl.multiple_of(flipped(line, flip) * rows, rows), rows)
            left_ref[target, column_half(half)] = left[flip]
    for number, spot in enumerate(spots(place, core)):
        source = right_far if number > 1 else right_first
        for flip in range(4):
            right_ref[rows_of(flipped(line, flip), spot), :] = source[number % 2, flip]
    for row_line in range(4):
        rows_ref[row_line * rows : (row_line + 1) * rows, :] = grad_ref[rows_of(row_line, place), :]
    left = dot(rows_ref[...], grad_ref[column_half(core), :], 1, 1)
    cross_ref[...] = dot(grad_ref[...], grad_ref[:, column_half(core)], 0, 0)
    lefted = dot(left_ref[...], grad_ref[...]).astype(low)
    stepped = dot(lefted, right_ref[...])
    square_ref[0] = jnp.sum(stepped * stepped, axis=0, keepdims=True)
    for row_line in range(4):
        part = slice(row_line * rows, (row_line + 1) * rows)
        out_ref[0, row_line, 0] = mine[0, 0, row_line]
        out_ref[0, row_line, 1] = left[part].astype(low)
        out_ref[0, row_line, 2] = cross_ref[rows_of(row_line, place), :].astype(low)
        out_ref[0, row_line, 3] = stepped[part].astype(low)


def step_chunks(mine, theirs, roots, number):
    chunks, lines, rows, columns = mine.shape[1:]
    full = rows * 16
    grad_spec = pl.BlockSpec((4, 1, lines, rows, columns), lambda step: (0, step, 0, 0, 0))
    return pl.pallas_call(
        functools.partial(step_kernel, number),
        grid=(chunks,),
        out_shape=(
            jax.ShapeDtypeStruct((chunks, lines, 4, rows, columns), low),
            jax.ShapeDtypeStruct((chunks, 1, columns), wide),
        ),
        in_specs=[grad_spec] * 2 + [in_hbm()] * 4,
        out_specs=(
            pl.BlockSpec((1, lines, 4, rows, columns), lambda step: (step, 0, 0, 0, 0)),
            pl.BlockSpec((1, 1, columns), lambda step: (step, 0, 0)),
        ),
        scratch_shapes=[
            pltpu.VMEM((full, columns * 2), low),
            pltpu.VMEM((lines * rows, columns * 2), low),
            pltpu.VMEM((lines * rows, columns * 2), low),
            pltpu.VMEM((full, columns), low),
            pltpu.VMEM((full, columns), wide),
            pltpu.VMEM((lines, rows, columns), low),
            pltpu.VMEM((lines, rows, columns), low),
            pltpu.VMEM((2, lines, rows, columns), low),
            pltpu.VMEM((2, lines, rows, columns), low),
            pltpu.SemaphoreType.DMA((4,)),
        ],
        compiler_params=params(15),
        cost_estimate=cost(3 * chunks * full**3, 16 * chunks * full * full),
    )(mine, theirs, *roots)


def return_chunks(made):
    line, place, core = here()
    parts = [pick(made, line, 1)]
    for flip in (1, 2, 3):
        parts.append(send(pick(made, flipped(line, flip), 1), line_pairs(flip)))
    return parts


def last_kernel(
    pair, pair_other, down, down_other, blocks, left_stat, right_stat, scales, *outs
):
    grad_out, left_out, right_out, block_out = outs
    line, place, core = here()
    columns = pair.shape[4]

    def update(number, which, mine, theirs):
        for (source, index), half in ((mine, which), (theirs, 1 - which)):
            part = slice(half * columns, (half + 1) * columns)
            pieces = [source[index + (kind,)].astype(wide) for kind in range(4)]
            grad_out[number, :, part] = pieces[0]
            left_out[number, :, part] = 0.5 * left_stat[number, :, part] + 0.5 * pieces[1]
            right_out[number, :, part] = 0.5 * right_stat[number, :, part] + 0.5 * pieces[2]
            step = pieces[3] * scales[6 * which + number]
            block_out[number, :, part] = blocks[number, :, part] - step

    @pl.when(core == 0)
    def first():
        for number in range(6):
            index = (flipped(line, number % 4), number // 4)
            update(number, 0, (pair, index), (pair_other, index))

    @pl.when(core == 1)
    def second():
        for number in range(6):
            source, other = (pair, pair_other) if number < 2 else (down, down_other)
            index = (flipped(line, (number + 2) % 4), 1 if number < 2 else 0)
            update(number, 1, (source, index), (other, index))


def update_blocks(pair, pair_other, down, down_other, blocks, left_stat, right_stat, scales):
    turned = [jnp.transpose(value, (1, 0, 2)) for value in (blocks, left_stat, right_stat)]
    shape = jax.ShapeDtypeStruct(turned[0].shape, wide)
    outs = pl.pallas_call(
        last_kernel,
        out_shape=(shape,) * 4,
        in_specs=[on_chip()] * 7 + [pl.BlockSpec(memory_space=pltpu.SMEM)],
        out_specs=(on_chip(),) * 4,
        compiler_params=params(10),
        cost_estimate=cost(0, 32 * shape.size),
    )(pair, pair_other, down, down_other, *turned, scales)
    return [jnp.transpose(value, (1, 0, 2)) for value in outs]


def head_masks():
    lane = lax.broadcasted_iota(jnp.int32, (1, 2 * HEAD_DIM), 1)
    return [(lane < HEAD_DIM).astype(wide).astype(low), (lane >= HEAD_DIM).astype(wide).astype(low)]


def head_shares(query, key, same):
    scores = dot(query, key, 1, 1) * HEAD_DIM ** (-0.5)
    scores = jnp.where(same, scores, -1e30)
    raised = jnp.exp(scores - jnp.max(scores, axis=-1, keepdims=True))
    return raised / jnp.sum(raised, axis=-1, keepdims=True)


STORE_ROWS = 32768


def store_views(store, rows, width):
    weights = [store.at[pl.ds(block * width, width)] for block in range(4)]
    made = [store.at[pl.ds(4 * width + kind * rows, rows)] for kind in range(3)]
    sides = [store.at[pl.ds(4 * width + (3 + side) * rows, rows)] for side in range(2)]
    return weights, made, sides


def attend_kernel(
    buffer, one, two, three, four, seg_column, seg_row, answer_ref, store, weights, made, sides, sems
):
    rows, width = buffer.shape
    weights_out, made_out, sides_out = store_views(store, rows, width)
    for block in range(4):
        place_block((one, two, three, four), block, weights.at[block])
    copies = fetch([weights.at[block] for block in range(4)], weights_out, sems)
    same = seg_column[...] == seg_row[...]
    for kind in range(3):
        made[kind] = dot(buffer[...], weights[kind]).astype(low)
    copies += fetch([made.at[kind] for kind in range(3)], made_out, sems.at[pl.ds(4, 3)])
    pair_width = 2 * HEAD_DIM
    for pair in range(width // pair_width):
        part = slice(pair * pair_width, (pair + 1) * pair_width)
        query, key, value = (made[kind, :, part] for kind in range(3))
        context = None
        for mask in head_masks():
            shares = head_shares(query, key * mask, same).astype(low)
            term = dot(shares, value * mask)
            context = term if context is None else context + term
        sides[1, :, part] = context.astype(low)
    sides[0] = buffer[...]
    copies += fetch([sides.at[side] for side in range(2)], sides_out, sems.at[pl.ds(7, 2)])
    answer_ref[...] = dot(sides[1], weights[3]).astype(low)
    finish(copies)


def attend_scratch(rows, width):
    return [
        pltpu.VMEM((4, width, width), low),
        pltpu.VMEM((3, rows, width), low),
        pltpu.VMEM((2, rows, width), low),
        pltpu.SemaphoreType.DMA((9,)),
    ]


def attend(buffer, parts, segment):
    rows, width = buffer.shape
    return pl.pallas_call(
        attend_kernel,
        out_shape=(
            jax.ShapeDtypeStruct((rows, width), low),
            jax.ShapeDtypeStruct((STORE_ROWS, width), low),
        ),
        in_specs=[on_chip()] * 7,
        out_specs=(on_chip(), in_hbm()),
        scratch_shapes=attend_scratch(rows, width),
        compiler_params=params(20),
        cost_estimate=cost(12 * rows * width * width, 12 * width * width),
    )(buffer, *parts, segment[:, None], segment[None, :])


def attend_back_kernel(
    store,
    seg_column,
    seg_row,
    grad_answer,
    theirs_ref,
    grads_ref,
    grad_buffer_ref,
    sides,
    grad_context_ref,
    weights,
    made,
    sems,
):
    rows, width = grad_answer.shape
    weights_from, made_from, sides_from = store_views(store, rows, width)
    out_copy, *copies = fetch(
        [weights_from[3]] + made_from + sides_from + weights_from[:3],
        [weights.at[3]]
        + [made.at[kind] for kind in range(3)]
        + [sides.at[side] for side in range(2)]
        + [weights.at[block] for block in range(3)],
        sems,
    )
    same = seg_column[...] == seg_row[...]
    core = lax.axis_index("own")
    out_copy.wait()
    grad_context_ref[...] = dot(grad_answer[...], weights[3], 1, 1).astype(low)
    finish(copies[:3])
    grads_ref[3] = grad_answer[...]
    pair_width = 2 * HEAD_DIM
    for pair in range(width // pair_width):
        part = slice(pair * pair_width, (pair + 1) * pair_width)
        query, key, value = (made[kind, :, part] for kind in range(3))
        above = grad_context_ref[:, part]
        sums = [None] * 3
        for mask in head_masks():
            key_head = key * mask
            shares = head_shares(query, key_head, same)
            grad_shares = dot(above, value * mask, 1, 1)
            inner = jnp.sum(shares * grad_shares, axis=-1, keepdims=True)
            grad_scores = (shares * (grad_shares - inner)).astype(low)
            terms = (
                dot(grad_scores, key_head),
                dot(grad_scores, query * mask, 0, 0),
                dot(shares.astype(low), above * mask, 0, 0),
            )
            sums = [
                term if total is None else total + term for term, total in zip(terms, sums)
            ]
        for kind, factor in enumerate((HEAD_DIM ** (-0.5), HEAD_DIM ** (-0.5), 1.0)):
            grads_ref[kind, :, part] = (sums[kind] * factor).astype(low)
    finish(copies[3:5])
    columns = theirs_ref.shape[2]
    part = pl.ds(pl.multiple_of((1 - core) * columns, columns), columns)
    for kind in range(4):
        theirs_ref[kind] = dot(sides[kind // 3], grads_ref[kind, :, part], 0, 0).astype(low)
    finish(copies[5:])
    total = dot(grads_ref[0], weights[0], 1, 1)
    total = total + dot(grads_ref[1], weights[1], 1, 1)
    total = total + dot(grads_ref[2], weights[2], 1, 1)
    grad_buffer_ref[...] = total.astype(low)


def attend_back(store, segment, grad_answer):
    rows, width = grad_answer.shape
    weights, made, sides, sems = attend_scratch(rows, width)
    return pl.pallas_call(
        attend_back_kernel,
        out_shape=(
            jax.ShapeDtypeStruct((4, width, width // 2), low),
            jax.ShapeDtypeStruct((4, rows, width), low),
            jax.ShapeDtypeStruct((rows, width), low),
            jax.ShapeDtypeStruct((2, rows, width), low),
        ),
        in_specs=[in_hbm()] + [on_chip()] * 3,
        out_specs=(on_chip(),) * 4,
        scratch_shapes=[pltpu.VMEM((rows, width), low), weights, made, sems],
        compiler_params=params(18),
        cost_estimate=cost(20 * rows * width * width, 16 * width * width),
    )(store, segment[:, None], segment[None, :], grad_answer)


def normal_parts(values):
    center = values - jnp.mean(values, axis=-1, keepdims=True)
    spread = jnp.mean(center * center, axis=-1, keepdims=True)
    return center, lax.rsqrt(spread + norm_eps)


def forward_kernel(*refs):
    tokens, placing, returned, gates, vectors = refs[:5]
    parts = refs[5:9]
    hidden_ref, second_ref, active_ref, slope_ref, w_up = refs[9:14]
    step = pl.program_id(0)

    @pl.when(step == 0)
    def prepare():
        values = tokens[...].astype(wide) + gates[:, 0:1] * dot(placing[...], returned[...])
        hidden_ref[...] = values
        center, inverse = normal_parts(values)
        second_ref[...] = (center * inverse * vectors[3:4] + vectors[4:5]).astype(low)

    place_block(parts, step, w_up.at[step])
    before = dot(second_ref[...], w_up[step])
    share = 0.5 + 0.5 * lax.erf(before * (0.5**0.5))
    density = jnp.exp(before * before * -0.5) * (0.5 / math.pi) ** 0.5
    active_ref[step] = (before * share).astype(low)
    slope_ref[step] = (share + before * density).astype(low)


def token_forward(tokens, placing, returned, gates, vectors, parts):
    count, width = tokens.shape
    blocks = parts[0].shape[2] // 2
    by_block = jax.ShapeDtypeStruct((blocks, count, width), low)
    fetched = (tokens, placing, returned, gates, vectors)
    return pl.pallas_call(
        forward_kernel,
        grid=(blocks,),
        out_shape=(
            jax.ShapeDtypeStruct((count, width), wide),
            jax.ShapeDtypeStruct((count, width), low),
            by_block,
            by_block,
            jax.ShapeDtypeStruct((blocks, width, width), low),
        ),
        in_specs=[whole(value) for value in fetched] + [on_chip()] * 4,
        out_specs=(on_chip(),) * 5,
        compiler_params=params(18),
        cost_estimate=cost(8 * blocks * count * width * width, 8 * blocks * width * width),
    )(*fetched, *parts)


def backward_kernel(*refs):
    above, placing, returned, gates, vectors = refs[:5]
    (hidden, active, slope, w_up), parts = refs[5:9], refs[9:13]
    mixed_ref, packed_ref, grad_hidden_ref, logit_ref, vector_ref, inner_ref = refs[13:19]
    result, grad_second, w_down = refs[19:22]
    step = pl.program_id(0)
    place_block(parts, 4 + step, w_down)

    @pl.when(step == 0)
    def prepare():
        result[...] = hidden[...]
        grad_second[...] = jnp.zeros_like(grad_second)

    grad_active = dot(above[...], w_down[...], 1, 1)
    grad_inner = (grad_active * slope[step].astype(wide)).astype(low)
    inner_ref[step] = grad_inner
    result[...] += dot(active[step], w_down[...])
    grad_second[...] += dot(grad_inner, w_up[step], 1, 1)

    @pl.when(step == pl.num_programs(0) - 1)
    def complete():
        mixed_ref[...] = result[...].astype(low)
        center, inverse = normal_parts(hidden[...])
        scaled = center * inverse
        grads = grad_second[...]
        vector_ref[0:1] = jnp.sum(grads * scaled, axis=0, keepdims=True)
        vector_ref[1:2] = jnp.sum(grads, axis=0, keepdims=True)
        pulled = grads * vectors[3:4]
        pulled = (
            pulled
            - jnp.mean(pulled, axis=-1, keepdims=True)
            - scaled * jnp.mean(pulled * scaled, axis=-1, keepdims=True)
        )
        grad_hidden = above[...].astype(wide) + inverse * pulled
        grad_hidden_ref[...] = grad_hidden
        weighted = (grad_hidden * gates[:, 0:1]).astype(low)
        packed_ref[...] = dot(placing[...], weighted, 0, 0).astype(low)
        unpacked = dot(placing[...], returned[...])
        logit_ref[...] = gates[:, 1:2] * jnp.sum(grad_hidden * unpacked, axis=-1, keepdims=True)


def token_backward(above, hidden, active, slope, placing, returned, gates, vectors, w_up, parts):
    count, width = above.shape
    slots = placing.shape[1]
    blocks = w_up.shape[0]
    fetched = (above, placing, returned, gates, vectors)
    return pl.pallas_call(
        backward_kernel,
        grid=(blocks,),
        out_shape=(
            jax.ShapeDtypeStruct((count, width), low),
            jax.ShapeDtypeStruct((slots, width), low),
            jax.ShapeDtypeStruct((count, width), wide),
            jax.ShapeDtypeStruct((count, 1), wide),
            jax.ShapeDtypeStruct((2, width), wide),
            jax.ShapeDtypeStruct((blocks, count, width), low),
        ),
        in_specs=[whole(value) for value in fetched] + [on_chip()] * 8,
        out_specs=(on_chip(),) * 6,
        scratch_shapes=[
            pltpu.VMEM((count, width), wide),
            pltpu.VMEM((count, width), wide),
            pltpu.VMEM((width, width), low),
        ],
        compiler_params=params(30),
        cost_estimate=cost(8 * blocks * count * width * width, 8 * blocks * width * width),
    )(*fetched, hidden, active, slope, w_up, *parts)


def outer_kernel(left, right, theirs_ref):
    core = lax.axis_index("own")
    step = pl.program_id(0)
    columns = theirs_ref.shape[2]
    left_step = step if left.shape[0] > 1 else 0
    right_step = step if right.shape[0] > 1 else 0
    part = pl.ds(pl.multiple_of((1 - core) * columns, columns), columns)
    theirs_ref[step] = dot(left[left_step], right[right_step, :, part], 0, 0).astype(low)


def outer_theirs(left, right):
    count, width = left.shape[1:]
    blocks = max(left.shape[0], right.shape[0])
    return pl.pallas_call(
        outer_kernel,
        grid=(blocks,),
        out_shape=jax.ShapeDtypeStruct((blocks, width, width // 2), low),
        in_specs=[on_chip()] * 2,
        out_specs=on_chip(),
        compiler_params=params(8),
        cost_estimate=cost(blocks * count * width * width, 3 * blocks * width * width),
    )(left, right)


def column(values):
    return values[:, None]


def pack_kernel(
    tokens, chosen, packing, vectors, placing_ref, packed_ref, gates_ref
):
    count = tokens.shape[0]
    capacity = packing.shape[0]
    center, inverse = normal_parts(tokens[...].astype(wide))
    first = (center * inverse * vectors[0:1] + vectors[1:2]).astype(low)
    gate = jax.nn.sigmoid(jnp.sum(first.astype(wide) * vectors[2:3], axis=-1, keepdims=True))
    weighting = jnp.where(chosen[...] == 1, gate, 0.0)
    gates_ref[:, 0:1] = weighting
    gates_ref[:, 1:2] = weighting * (1.0 - gate)
    above = lax.broadcasted_iota(jnp.int32, (count, count), 0)
    below = lax.broadcasted_iota(jnp.int32, (count, count), 1)
    earlier = (below <= above).astype(wide).astype(low)
    flags = jnp.broadcast_to(chosen[...].astype(wide), (count, capacity))
    rank = dot(earlier, flags.astype(low))
    place_of = lax.broadcasted_iota(jnp.int32, (count, capacity), 1).astype(wide) + 1.0
    ranked = jnp.where(rank == place_of, flags, 0.0).astype(low)
    slots = lax.broadcasted_iota(jnp.int32, (capacity, capacity), 1)
    slot_of = (packing[...] == slots).astype(wide).astype(low)
    placing = dot(ranked, slot_of).astype(low)
    placing_ref[...] = placing
    packed_ref[...] = dot(placing, first, 0, 0).astype(low)


def pack_tokens(tokens, chosen, packing, vectors):
    count, width = tokens.shape
    capacity = packing.shape[0]
    return pl.pallas_call(
        pack_kernel,
        out_shape=(
            jax.ShapeDtypeStruct((count, capacity), low),
            jax.ShapeDtypeStruct((capacity, width), low),
            jax.ShapeDtypeStruct((count, 2), wide),
        ),
        in_specs=[on_chip()] * 4,
        out_specs=(on_chip(),) * 3,
        compiler_params=params(10),
        cost_estimate=cost(4 * count * capacity * width, 8 * count * width),
    )(tokens, column(chosen), column(packing), vectors)


def token_back_kernel(*refs):
    sources, (out_ref, vector_ref), fetched, sems = refs[:6], refs[6:8], refs[8:14], refs[14]
    finish(fetch(sources, fetched, sems))
    tokens, placing, grad_sent, grad_hidden, grad_logit, vectors = fetched
    grad_first = dot(placing[...], grad_sent[...]) + grad_logit[...] * vectors[2:3]
    center, inverse = normal_parts(tokens[...].astype(wide))
    scaled = center * inverse
    vector_ref[0:1] = jnp.sum(grad_first * scaled, axis=0, keepdims=True)
    vector_ref[1:2] = jnp.sum(grad_first, axis=0, keepdims=True)
    first = (scaled * vectors[0:1] + vectors[1:2]).astype(low).astype(wide)
    vector_ref[2:3] = jnp.sum(grad_logit[...] * first, axis=0, keepdims=True)
    pulled = grad_first * vectors[0:1]
    pulled = (
        pulled
        - jnp.mean(pulled, axis=-1, keepdims=True)
        - scaled * jnp.mean(pulled * scaled, axis=-1, keepdims=True)
    )
    out_ref[...] = (grad_hidden[...] + inverse * pulled).astype(low)


def token_back(tokens, placing, grad_sent, grad_hidden, grad_logit, vectors):
    count, width = tokens.shape
    return pl.pallas_call(
        token_back_kernel,
        out_shape=(
            jax.ShapeDtypeStruct((count, width), low),
            jax.ShapeDtypeStruct((3, width), wide),
        ),
        in_specs=[in_hbm()] * 6,
        out_specs=(on_chip(),) * 2,
        scratch_shapes=fetch_scratch(
            (tokens, placing, grad_sent, grad_hidden, grad_logit, vectors)
        ),
        compiler_params=params(17),
        cost_estimate=cost(2 * count * width * placing.shape[1], 12 * count * width),
    )(tokens, placing, grad_sent, grad_hidden, grad_logit, vectors)


def flip_pairs(flip):
    return [(i, i ^ flip) for i in range(32)]


def all_sum(value):
    value = value + send(value, swap_pairs())
    for one, two in ((2, 4), (8, 16)):
        near = value + send(value, flip_pairs(one))
        far = send(value, flip_pairs(two)) + send(value, flip_pairs(one + two))
        value = near + far
    return value


def exchange(value, n_data):
    capacity, width = value.shape
    moved = lax.all_to_all(
        value.reshape(n_data, capacity // n_data, width), "dp", split_axis=0, concat_axis=0, tiled=True
    )
    return moved.reshape(capacity, width)


def block_shards(
    tokens,
    cotangent,
    selected,
    packing,
    segments,
    blocks,
    left_stat,
    right_stat,
    left_root,
    right_root,
    vectors,
    moment,
):
    model_width = tokens.shape[2]
    token_count = tokens.shape[0] * tokens.shape[1]
    n_data = lax.axis_size("dp")
    capacity = packing.shape[1]
    line, place, core = here()
    own_tokens = tokens.reshape(token_count, model_width)
    above = cotangent.reshape(token_count, model_width)
    segment = segments[0]

    every = columns_by_core(jnp.transpose(blocks, (1, 0, 2)).astype(low))
    placing, packed, gates = pack_tokens(
        own_tokens, selected.reshape(token_count), packing[0], vectors
    )
    buffer = exchange(packed, n_data)
    attn_two = send(every[:4], line_pairs(2))
    ffn_got = send(after(every[4:], attn_two), line_pairs(2))
    attn_pair = jnp.stack([every[:4], attn_two])
    attn_got = send(attn_pair, line_pairs(1))
    line_attn = after(jnp.concatenate([attn_pair, attn_got]), packed)
    ffn_two = jnp.stack([every[4:], after(ffn_got, attn_got)])
    near_attn = send(line_attn, plane_pairs(0))
    every_root = roots_by_core(after(left_root, ffn_two), right_root)
    first_attn = after(jnp.stack([line_attn, near_attn]), every_root, buffer)
    far_attn = send(first_attn, plane_pairs(1))
    line_ffn = gather_far(ffn_two)
    near_ffn = send(after(line_ffn, near_attn), plane_pairs(0))
    root_given = lax.optimization_barrier((*roots_given(every_root), buffer, line_ffn))[:4]
    root_parts = [root_given[0]]
    for flip in (1, 2, 3):
        root_parts.append(send(root_given[flip], line_pairs(flip)))
    w_parts = with_other(first_attn, far_attn)
    answer, store = attend(buffer, w_parts, segment)
    first_ffn = jnp.stack([line_ffn, near_ffn])
    left_line, right_line = (jnp.stack([part[:, kind] for part in root_parts]) for kind in range(2))
    returned = exchange(answer, n_data)
    far_ffn = after(send(after(first_ffn, far_attn, *root_parts[1:]), plane_pairs(1)), returned, right_line, left_line)
    ffn_parts = with_other(first_ffn, far_ffn)

    near_right = send(after(right_line, far_ffn), plane_pairs(0))
    first_right = jnp.stack([right_line, near_right])
    hidden, second_low, active, slope, w_up = token_forward(
        own_tokens, placing, returned, gates, vectors, ffn_parts
    )
    down_theirs = outer_theirs(after(active, near_right), above[None])
    far_right = send(first_right, plane_pairs(1))
    roots = (left_line, send(left_line, swap_pairs()), first_right, far_right)
    down_got = send(down_theirs, swap_pairs())
    down_give, *down_kept = sum_start(lambda step: step, active, above[None], down_got)
    down_got = send(down_give, plane_pairs(0))
    mixed, grad_packed, grad_hidden, grad_logit, vector_two, grad_inner = token_backward(
        above,
        hidden,
        active,
        slope,
        placing,
        returned,
        gates,
        vectors,
        after(w_up, down_give),
        ffn_parts,
    )
    grad_answer = exchange(grad_packed, n_data)
    up_theirs = outer_theirs(after(second_low, down_got, far_right)[None], grad_inner)

    down_kept, down_give = add_first(down_got, *down_kept)
    down_got = send(down_give, plane_pairs(1))
    up_got = send(after(up_theirs, grad_answer), swap_pairs())
    attn_theirs, grads, grad_buffer, sides = attend_back(store, segment, grad_answer)
    attn_got = send(after(attn_theirs, down_got), swap_pairs())
    up_give, *up_kept = sum_start(
        lambda step: 0, second_low[None], grad_inner, after(up_got, attn_theirs)
    )
    up_got = send(up_give, plane_pairs(0))
    down_own, down_two, down_give = cut_line((down_kept + down_got.astype(wide))[None])
    down_got = send(down_give, line_pairs(1))
    attn_give, *attn_kept = sum_start(
        lambda step: step // 3, sides, grads, after(attn_got, up_give)
    )
    attn_got = send(attn_give, plane_pairs(0))
    grad_sent = exchange(after(grad_buffer, attn_give), n_data)
    down_own, down_give = add_line(down_own, down_two, down_got)
    down_got = send(down_give, line_pairs(2))
    down_own = (down_own + down_got.astype(wide)).astype(low)
    down_near = send(down_own, plane_pairs(0))
    down_first = jnp.stack([down_own, down_near])
    down_far = send(down_first, plane_pairs(1))
    down_mine = jnp.concatenate([down_first, down_far])
    down_theirs = send(down_mine, swap_pairs())

    up_kept, up_give = add_first(up_got, *up_kept)
    attn_kept, attn_give = add_first(after(attn_got, down_far), *attn_kept)
    pair_got = send(jnp.stack([attn_give, up_give]), plane_pairs(1))
    down_made, down_square = step_chunks(down_mine, down_theirs, roots, 2)
    down_parts = return_chunks(down_made)
    pair_got = after(pair_got, down_made)
    pair_kept = jnp.stack([attn_kept, up_kept]) + pair_got.astype(wide)
    pair_own, pair_two, pair_give = cut_line(pair_kept)
    pair_got = send(pair_give, line_pairs(1))
    grad_tokens, vector_one = token_back(
        own_tokens, placing, grad_sent, grad_hidden, grad_logit, vectors
    )
    pair_own, pair_give = add_line(pair_own, pair_two, pair_got)
    pair_got = send(after(pair_give, vector_one), line_pairs(2))
    down = jnp.stack(down_parts)
    down_other = send(down, [(i, i ^ 1) for i in range(0, 32, 2)])
    pair_own = (pair_own + pair_got.astype(wide)).astype(low)
    pair_near = send(pair_own, plane_pairs(0))
    pair_first = jnp.stack([pair_own, pair_near])
    pair_far = send(pair_first, plane_pairs(1))
    pair_mine = jnp.concatenate([pair_first, pair_far])
    pair_theirs = send(after(pair_mine, *down_parts[1:]), swap_pairs())
    pair_made, pair_square = step_chunks(pair_mine, pair_theirs, roots, 0)
    pair = jnp.stack(return_chunks(pair_made))
    pair_other = send(pair, swap_pairs())
    squares = jnp.concatenate([jnp.sum(pair_square, axis=2), jnp.sum(down_square, axis=2)])
    lane = lax.broadcasted_iota(jnp.int32, (1, model_width), 1)
    square_row = sum(
        jnp.where(lane == 4 * chunk + line, squares[chunk], 0.0) for chunk in range(3)
    )
    sums = all_sum(jnp.concatenate([vector_one, vector_two, square_row]))
    vector_grad = sums[:5]
    size = model_width * model_width
    scales = block_rate * lax.rsqrt(sums[5, :12] / size + norm_eps)
    grad_own, left_new, right_new, new_blocks = update_blocks(
        pair, pair_other, down, down_other, blocks, left_stat, right_stat, scales
    )
    moment_new = 0.5 * moment + 0.5 * vector_grad
    row_squares = jnp.mean(moment_new * moment_new, axis=1, keepdims=True)
    vector_new = vectors - vector_rate * moment_new * lax.rsqrt(row_squares + norm_eps)
    return (
        mixed.reshape(tokens.shape),
        grad_tokens.reshape(tokens.shape),
        grad_own,
        left_new,
        right_new,
        new_blocks,
        vector_grad,
        moment_new,
        vector_new,
    )


def shards(
    tokens,
    cotangent,
    selected,
    packing,
    segments,
    blocks,
    left_stat,
    right_stat,
    left_root,
    right_root,
    vectors,
    moment,
):
    model_width = tokens.shape[2]
    token_count = tokens.shape[0] * tokens.shape[1]
    n_data = lax.axis_size("dp")
    n_owner = lax.axis_size("own")
    shard_rows = blocks.shape[0]
    own_blocks = blocks.shape[1]
    up_blocks = (own_blocks * n_owner - 4) // 2
    capacity = packing.shape[1]
    per_peer = capacity // n_data
    head_count = model_width // HEAD_DIM
    score_scale = HEAD_DIM ** (-0.5)
    flat_weights = blocks.astype(jnp.bfloat16).reshape(1, shard_rows * own_blocks * model_width)
    gathered = lax.all_gather(flat_weights, ("dp", "own"), axis=0, tiled=True)
    gathered = gathered.reshape(n_data, n_owner, shard_rows, own_blocks, model_width)

    def matrix(number):
        return gathered[:, number // own_blocks, :, number % own_blocks, :].reshape(
            model_width, model_width
        )

    w_query = matrix(0)
    w_key = matrix(1)
    w_value = matrix(2)
    w_out = matrix(3)
    w_up = jnp.concatenate([matrix(4 + position) for position in range(up_blocks)], axis=1)
    w_down = jnp.concatenate(
        [matrix(4 + up_blocks + position) for position in range(up_blocks)], axis=0
    )
    inputs = tokens.reshape(token_count, model_width).astype(jnp.float32)
    chosen = selected.reshape(token_count)
    normed_one, norm_one_back = jax.vjp(layer_norm, inputs, vectors[0], vectors[1])
    first_low = normed_one.astype(jnp.bfloat16)
    first_wide = first_low.astype(jnp.float32)
    gate_values = jax.nn.sigmoid(jnp.dot(first_wide, vectors[2], precision=highest))
    before = jnp.cumsum(chosen) - 1
    slot_index = jnp.where(chosen == 1, packing[0][jnp.clip(before, 0, capacity - 1)], -1)
    placing = (slot_index[None, :] == jnp.arange(capacity, dtype=jnp.int32)[:, None]).astype(
        jnp.bfloat16
    )
    packed = jnp.dot(placing, first_low, preferred_element_type=jnp.float32).astype(jnp.bfloat16)
    buffer = lax.all_to_all(
        packed.reshape(n_data, per_peer, model_width), "dp", split_axis=0, concat_axis=0, tiled=True
    )
    buffer = buffer.reshape(capacity, model_width)

    def project(matrix_in):
        made = jnp.dot(buffer, matrix_in, preferred_element_type=jnp.float32).astype(jnp.bfloat16)
        return made.reshape(capacity, head_count, HEAD_DIM)

    query_rows = project(w_query)
    key_rows = project(w_key)
    value_rows = project(w_value)
    segment = segments[0]
    block_rows = math.gcd(capacity, 512)
    starts = jnp.arange(capacity // block_rows, dtype=jnp.int32) * block_rows

    def masked_scores():
        scores = (
            jnp.einsum("qhd,khd->hqk", query_rows, key_rows, preferred_element_type=jnp.float32)
            * score_scale
        )
        same_segment = segment[:, None] == segment[None, :]
        return (jnp.where(same_segment[None, :, :], scores, -1e30), query_rows)

    def forward_block(first_row):
        scores, unused_block = masked_scores()
        largest = jnp.max(scores, axis=-1, keepdims=True)
        raised = jnp.exp(scores - largest)
        row_total = jnp.sum(raised, axis=-1, keepdims=True)
        shares = (raised / row_total).astype(jnp.bfloat16)
        context_part = jnp.einsum(
            "hqk,khd->qhd", shares, value_rows, preferred_element_type=jnp.float32
        )
        return (context_part.astype(jnp.bfloat16), largest[..., 0] + jnp.log(row_total[..., 0]))

    context_blocks, lse_blocks = lax.map(forward_block, starts)
    context = context_blocks.reshape(capacity, model_width)
    answer = jnp.dot(context, w_out, preferred_element_type=jnp.float32).astype(jnp.bfloat16)
    returned = lax.all_to_all(
        answer.reshape(n_data, per_peer, model_width), "dp", split_axis=0, concat_axis=0, tiled=True
    )
    returned = returned.reshape(capacity, model_width)
    unpacked = jnp.einsum("mt,md->td", placing, returned, preferred_element_type=jnp.float32)
    weighting = jnp.where(chosen == 1, gate_values, 0.0)
    hidden = inputs + weighting[:, None] * unpacked
    normed_two, norm_two_back = jax.vjp(layer_norm, hidden, vectors[3], vectors[4])
    second_low = normed_two.astype(jnp.bfloat16)
    pre_active = jnp.dot(second_low, w_up, preferred_element_type=jnp.float32)
    active_wide, gelu_back = jax.vjp(gelu_exact, pre_active)
    active = active_wide.astype(jnp.bfloat16)
    result = hidden + jnp.dot(active, w_down, preferred_element_type=jnp.float32)
    mixed = result.astype(jnp.bfloat16).reshape(tokens.shape)
    upstream = cotangent.reshape(token_count, model_width)
    grad_down = jnp.einsum("tf,td->fd", active, upstream, preferred_element_type=jnp.float32)
    grad_active = jnp.einsum("td,fd->tf", upstream, w_down, preferred_element_type=jnp.float32)
    grad_inner = gelu_back(grad_active)[0].astype(jnp.bfloat16)
    grad_up = jnp.einsum("td,tf->df", second_low, grad_inner, preferred_element_type=jnp.float32)
    grad_second = jnp.einsum("tf,df->td", grad_inner, w_up, preferred_element_type=jnp.float32)
    grad_hidden_part, grad_gain_two, grad_bias_two = norm_two_back(grad_second)
    grad_hidden = upstream.astype(jnp.float32) + grad_hidden_part
    grad_token_back = (grad_hidden * weighting[:, None]).astype(jnp.bfloat16)
    grad_packed = jnp.dot(placing, grad_token_back, preferred_element_type=jnp.float32).astype(
        jnp.bfloat16
    )
    router_pull = jnp.where(chosen == 1, jnp.sum(grad_hidden * unpacked, axis=-1), 0.0)
    grad_logit = router_pull * gate_values * (1.0 - gate_values)
    grad_answer = lax.all_to_all(
        grad_packed.reshape(n_data, per_peer, model_width),
        "dp",
        split_axis=0,
        concat_axis=0,
        tiled=True,
    )
    grad_answer = grad_answer.reshape(capacity, model_width)
    grad_out = jnp.einsum("md,me->de", context, grad_answer, preferred_element_type=jnp.float32)
    grad_context = jnp.einsum("me,de->md", grad_answer, w_out, preferred_element_type=jnp.float32)
    grad_context = grad_context.astype(jnp.bfloat16).reshape(capacity, head_count, HEAD_DIM)

    def backward_block(running, item_pair):
        first_row, lse_block = item_pair
        scores, query_block = masked_scores()
        shares_wide = jnp.exp(scores - lse_block[..., None])
        grad_shares = jnp.einsum(
            "qhd,khd->hqk", grad_context, value_rows, preferred_element_type=jnp.float32
        )
        inner_sum = jnp.sum(shares_wide * grad_shares, axis=-1, keepdims=True)
        grad_scores = (shares_wide * (grad_shares - inner_sum)).astype(jnp.bfloat16)
        grad_query_block = (
            jnp.einsum("hqk,khd->qhd", grad_scores, key_rows, preferred_element_type=jnp.float32)
            * score_scale
        )
        key_sum = (
            running[0]
            + jnp.einsum(
                "hqk,qhd->khd", grad_scores, query_block, preferred_element_type=jnp.float32
            )
            * score_scale
        )
        value_sum = running[1] + jnp.einsum(
            "hqk,qhd->khd",
            shares_wide.astype(jnp.bfloat16),
            grad_context,
            preferred_element_type=jnp.float32,
        )
        return ((key_sum, value_sum), grad_query_block)

    zeros_init = jnp.zeros((capacity, head_count, HEAD_DIM), jnp.float32)
    (key_total, value_total), query_grads = lax.scan(
        backward_block, (zeros_init, zeros_init), (starts, lse_blocks)
    )
    grad_query = query_grads.reshape(capacity, model_width).astype(jnp.bfloat16)
    grad_key = key_total.reshape(capacity, model_width).astype(jnp.bfloat16)
    grad_value = value_total.reshape(capacity, model_width).astype(jnp.bfloat16)
    grad_w_query = jnp.einsum("md,me->de", buffer, grad_query, preferred_element_type=jnp.float32)
    grad_w_key = jnp.einsum("md,me->de", buffer, grad_key, preferred_element_type=jnp.float32)
    grad_w_value = jnp.einsum("md,me->de", buffer, grad_value, preferred_element_type=jnp.float32)
    grad_buffer = jnp.einsum("me,de->md", grad_query, w_query, preferred_element_type=jnp.float32)
    grad_buffer = grad_buffer + jnp.einsum(
        "me,de->md", grad_key, w_key, preferred_element_type=jnp.float32
    )
    grad_buffer = grad_buffer + jnp.einsum(
        "me,de->md", grad_value, w_value, preferred_element_type=jnp.float32
    )
    grad_buffer = grad_buffer.astype(jnp.bfloat16)
    grad_sent = lax.all_to_all(
        grad_buffer.reshape(n_data, per_peer, model_width),
        "dp",
        split_axis=0,
        concat_axis=0,
        tiled=True,
    )
    grad_sent = grad_sent.reshape(capacity, model_width)
    grad_first = jnp.einsum("mt,md->td", placing, grad_sent, preferred_element_type=jnp.float32)
    grad_first = grad_first + grad_logit[:, None] * vectors[2][None, :]
    grad_router = jnp.sum(grad_logit[:, None] * first_wide, axis=0)
    grad_input_part, grad_gain_one, grad_bias_one = norm_one_back(grad_first)
    grad_tokens = (grad_hidden + grad_input_part).astype(jnp.bfloat16).reshape(tokens.shape)
    pieces = [grad_w_query, grad_w_key, grad_w_value, grad_out]
    pieces = pieces + [
        grad_up[:, position * model_width : (position + 1) * model_width]
        for position in range(up_blocks)
    ]
    pieces = pieces + [
        grad_down[position * model_width : (position + 1) * model_width, :]
        for position in range(up_blocks)
    ]
    local_terms = jnp.stack(pieces, axis=1)
    vector_terms = jnp.stack(
        [grad_gain_one, grad_bias_one, grad_router, grad_gain_two, grad_bias_two]
    )
    partial_value = lax.psum_scatter(local_terms, "dp", scatter_dimension=0, tiled=True)
    grad_own = lax.psum_scatter(
        partial_value.astype(jnp.bfloat16), "own", scatter_dimension=1, tiled=True
    ).astype(jnp.float32)
    vector_grad = lax.psum(vector_terms, ("dp", "own"))
    full_grad = lax.all_gather(grad_own.astype(jnp.bfloat16), "dp", axis=0, tiled=True).astype(
        grad_own.dtype
    )
    row_start = lax.axis_index("dp") * shard_rows
    left_new = 0.5 * left_stat + 0.5 * jnp.einsum(
        "rbk,nbk->rbn", grad_own, full_grad, precision=highest
    )
    column_part = lax.dynamic_slice_in_dim(full_grad, row_start, shard_rows, 2)
    right_new = 0.5 * right_stat + 0.5 * jnp.einsum(
        "nbr,nbk->rbk", column_part, full_grad, precision=highest
    )
    lefted = jnp.einsum("rbn,nbk->rbk", left_root, full_grad, precision=highest)
    precond = jnp.zeros_like(grad_own) + jnp.einsum(
        "rbn,nbk->rbk",
        lefted,
        lax.all_gather(right_root.astype(jnp.bfloat16), "dp", axis=0, tiled=True).astype(
            jnp.float32
        ),
        precision=highest,
    )
    square_sums = lax.psum(jnp.sum(precond * precond, axis=(0, 2)), "dp")
    step_scale = lax.rsqrt(square_sums / (model_width * model_width) + norm_eps)
    new_blocks = blocks - block_rate * precond * step_scale[None, :, None]
    moment_new = 0.5 * moment + 0.5 * vector_grad
    row_squares = jnp.mean(moment_new * moment_new, axis=1, keepdims=True)
    vector_new = vectors - vector_rate * moment_new * lax.rsqrt(row_squares + norm_eps)
    return (
        mixed,
        grad_tokens,
        grad_own,
        left_new,
        right_new,
        new_blocks,
        vector_grad,
        moment_new,
        vector_new,
    )


def solution(mesh):
    placed = (
        P(("dp", "own"), None, None),
        P(("dp", "own"), None, None),
        P(("dp", "own"), None),
        P(("dp", "own"), None),
        P(("dp", "own"), None),
        P("dp", "own", None),
        P("dp", "own", None),
        P("dp", "own", None),
        P("dp", "own", None),
        P("dp", "own", None),
        P(),
        P(),
    )
    small = mesh.shape["dp"] == 16 and mesh.shape["own"] == 2
    return jax.shard_map(
        block_shards if small else shards,
        mesh=mesh,
        in_specs=placed,
        out_specs=(
            P(("dp", "own"), None, None),
            P(("dp", "own"), None, None),
            P("dp", "own", None),
            P("dp", "own", None),
            P("dp", "own", None),
            P("dp", "own", None),
            P(),
            P(),
            P(),
        ),
        check_vma=False,
    )
```

```python
import functools
import math

import jax
import jax.numpy as jnp
from jax import lax
from jax.experimental import pallas as pl
from jax.experimental.pallas import tpu as pltpu
from jax.sharding import PartitionSpec as P

HEAD_DIM = 64


norm_eps = 1e-06
block_rate = 0.03
vector_rate = 0.04
highest = lax.Precision.HIGHEST


def layer_norm(values, norm_gain, norm_bias):
    center = values - jnp.mean(values, axis=-1, keepdims=True)
    spread = jnp.mean(center * center, axis=-1, keepdims=True)
    return center * lax.rsqrt(spread + norm_eps) * norm_gain + norm_bias


def gelu_exact(values):
    return jax.nn.gelu(values, approximate=False)


BOTH = ("dp", "own")
low = jnp.bfloat16
wide = jnp.float32
MIB = 2**20


def swap_pairs():
    return [(i, i ^ 1) for i in range(32)]


def plane_pairs(step):
    pairs = []
    for i in range(32):
        place, core = i // 2, i % 2
        flip = (1, 2)[step ^ core]
        pairs.append((i, (place ^ flip) * 2 + core))
    return pairs


def line_pairs(flip):
    return [(i, i ^ (8 * flip)) for i in range(32)]


def send(value, pairs):
    return lax.ppermute(value, BOTH, pairs)


def after(value, *others):
    return lax.optimization_barrier((value,) + others)[0]


def pick(value, index, axis):
    return lax.dynamic_index_in_dim(value, index, axis, keepdims=False)


def first_core():
    return lax.axis_index("own") == 0


def halves(value):
    middle = value.shape[-1] // 2
    lower, upper = value[..., :middle], value[..., middle:]
    return jnp.where(first_core(), lower, upper), jnp.where(first_core(), upper, lower)


def in_core_order(mine, theirs, axis):
    return jnp.where(
        first_core(),
        jnp.concatenate([mine, theirs], axis=axis),
        jnp.concatenate([theirs, mine], axis=axis),
    )


LINE_FLIPS = (0, 2, 1, 3)


def flipped(index, flip):
    return jnp.bitwise_xor(index, flip)


def spots(place, half):
    first, second = half + 1, 2 - half
    return [
        place,
        flipped(place, first),
        flipped(place, second),
        flipped(place, 3),
    ]


def here():
    device = lax.axis_index("dp")
    return device // 4, device % 4, lax.axis_index("own")


def dot(left, right, left_axis=1, right_axis=0):
    return lax.dot_general(
        left, right, (((left_axis,), (right_axis,)), ((), ())), preferred_element_type=wide
    )


def on_chip():
    return pl.BlockSpec(memory_space=pltpu.VMEM)


def whole(value):
    return pl.BlockSpec(value.shape, lambda *steps: (0,) * value.ndim)


def in_hbm():
    return pl.BlockSpec(memory_space=pltpu.HBM)


def fetch_scratch(values):
    return [pltpu.VMEM(value.shape, value.dtype) for value in values] + [
        pltpu.SemaphoreType.DMA((len(values),))
    ]


def fetch(sources, targets, sems):
    copies = [
        pltpu.make_async_copy(source, target, sems.at[number])
        for number, (source, target) in enumerate(zip(sources, targets))
    ]
    for copy in copies:
        copy.start()
    return copies


def finish(copies):
    for copy in copies:
        copy.wait()


def params(limit):
    return pltpu.CompilerParams(vmem_limit_bytes=limit * MIB)


def cost(flops, moved):
    return pl.CostEstimate(flops=flops, bytes_accessed=moved, transcendentals=0)


def place_block(parts, block, target, line_first=False):
    line, place, core = here()
    rows, columns = parts[0].shape[3:]
    for other in range(2):
        half = core if other == 0 else 1 - core
        column_slice = pl.ds(pl.multiple_of(half * columns, columns), columns)
        for number, spot in enumerate(spots(place, half)):
            for index, flip in enumerate(LINE_FLIPS):
                start = (flipped(line, flip) * 4 + spot) * rows
                row_slice = pl.ds(pl.multiple_of(start, rows), rows)
                place_index = (index, number % 2) if line_first else (number % 2, index)
                piece = parts[2 * other + number // 2][place_index + (block,)]
                target[row_slice, column_slice] = piece


def columns_by_core(value):
    keep, give = halves(value)
    return in_core_order(keep, send(give, swap_pairs()), 0)


def gather_far(pair):
    return jnp.concatenate([pair, send(pair, line_pairs(1))])


def with_other(first, far):
    return [first, far, send(first, swap_pairs()), send(far, swap_pairs())]


def roots_by_core(left_root, right_root):
    both = [jnp.transpose(root, (1, 0, 2)).astype(low) for root in (left_root, right_root)]
    every = columns_by_core(jnp.stack(both, axis=1))
    return every.reshape((3, 4) + every.shape[1:])


def roots_given(every):
    line, place, core = here()
    return [pick(every, flipped(line, flip), 1) for flip in range(4)]


def sum_kernel(left_of, left, right, got, give_ref, kept_ref, passed_ref, total):
    line, place, core = here()
    step = pl.program_id(0)
    columns = got.shape[2]
    rows = kept_ref.shape[2]
    part = pl.ds(pl.multiple_of(core * columns, columns), columns)
    right_step = step if right.shape[0] > 1 else 0
    made = dot(left[left_of(step)], right[right_step, :, part], 0, 0)
    total[...] = made + got[step].astype(wide)
    own, first, second, both = spots(place, core)
    for row_line in range(4):

        def piece(spot):
            return total[pl.ds(pl.multiple_of((row_line * 4 + spot) * rows, rows), rows), :]

        give_ref[0, step, row_line] = piece(first).astype(low)
        give_ref[1, step, row_line] = piece(both).astype(low)
        kept_ref[step, row_line] = piece(own).astype(low)
        passed_ref[step, row_line] = piece(second).astype(low)


def sum_start(left_of, left, right, got):
    count, width = left.shape[1:]
    blocks, full, columns = got.shape
    shape = (blocks, 4, full // 16, columns)
    return pl.pallas_call(
        functools.partial(sum_kernel, left_of),
        grid=(blocks,),
        out_shape=(
            jax.ShapeDtypeStruct((2,) + shape, low),
            jax.ShapeDtypeStruct(shape, low),
            jax.ShapeDtypeStruct(shape, low),
        ),
        in_specs=[on_chip()] * 3,
        out_specs=(on_chip(),) * 3,
        scratch_shapes=[pltpu.VMEM((full, columns), wide)],
        compiler_params=params(12),
        cost_estimate=cost(blocks * count * width * width, 5 * blocks * width * width),
    )(left, right, got)


def add_first(got, kept, passed):
    kept = kept.astype(wide) + got[0].astype(wide)
    return kept, (passed.astype(wide) + got[1].astype(wide)).astype(low)


def cut_line(kept):
    line, place, core = here()
    given = jnp.stack([pick(kept, flipped(line, flip), 1) for flip in (1, 3)]).astype(low)
    return pick(kept, line, 1), pick(kept, flipped(line, 2), 1), given


def add_line(own, two, got):
    return own + got[0].astype(wide), (two + got[1].astype(wide)).astype(low)


def step_kernel(
    number,
    mine,
    theirs,
    left_mine_from,
    left_theirs_from,
    right_first_from,
    right_far_from,
    out_ref,
    square_ref,
    grad_ref,
    rows_ref,
    left_ref,
    right_ref,
    cross_ref,
    left_mine,
    left_theirs,
    right_first,
    right_far,
    sems,
):
    chunk = number + pl.program_id(0)
    copies = fetch(
        [
            left_mine_from.at[:, chunk],
            left_theirs_from.at[:, chunk],
            right_first_from.at[:, :, chunk],
            right_far_from.at[:, :, chunk],
        ],
        [left_mine, left_theirs, right_first, right_far],
        sems,
    )
    line, place, core = here()
    rows, columns = mine.shape[3:]

    def rows_of(row_line, spot):
        return pl.ds(pl.multiple_of((row_line * 4 + spot) * rows, rows), rows)

    def column_half(half):
        return pl.ds(pl.multiple_of(half * columns, columns), columns)

    for half, group in ((core, mine), (1 - core, theirs)):
        for number, spot in enumerate(spots(place, half)):
            for step in range(4):
                grad_ref[rows_of(step, spot), column_half(half)] = group[number, 0, step]
    finish(copies)
    for half, left in ((core, left_mine), (1 - core, left_theirs)):
        for flip in range(4):
            target = pl.ds(pl.multiple_of(flipped(line, flip) * rows, rows), rows)
            left_ref[target, column_half(half)] = left[flip]
    for number, spot in enumerate(spots(place, core)):
        source = right_far if number > 1 else right_first
        for flip in range(4):
            right_ref[rows_of(flipped(line, flip), spot), :] = source[number % 2, flip]
    for row_line in range(4):
        rows_ref[row_line * rows : (row_line + 1) * rows, :] = grad_ref[rows_of(row_line, place), :]
    left = dot(rows_ref[...], grad_ref[column_half(core), :], 1, 1)
    cross_ref[...] = dot(grad_ref[...], grad_ref[:, column_half(core)], 0, 0)
    lefted = dot(left_ref[...], grad_ref[...]).astype(low)
    stepped = dot(lefted, right_ref[...])
    square_ref[0] = jnp.sum(stepped * stepped, axis=0, keepdims=True)
    for row_line in range(4):
        part = slice(row_line * rows, (row_line + 1) * rows)
        out_ref[0, row_line, 0] = mine[0, 0, row_line]
        out_ref[0, row_line, 1] = left[part].astype(low)
        out_ref[0, row_line, 2] = cross_ref[rows_of(row_line, place), :].astype(low)
        out_ref[0, row_line, 3] = stepped[part].astype(low)


def step_chunks(mine, theirs, roots, number):
    chunks, lines, rows, columns = mine.shape[1:]
    full = rows * 16
    grad_spec = pl.BlockSpec((4, 1, lines, rows, columns), lambda step: (0, step, 0, 0, 0))
    return pl.pallas_call(
        functools.partial(step_kernel, number),
        grid=(chunks,),
        out_shape=(
            jax.ShapeDtypeStruct((chunks, lines, 4, rows, columns), low),
            jax.ShapeDtypeStruct((chunks, 1, columns), wide),
        ),
        in_specs=[grad_spec] * 2 + [in_hbm()] * 4,
        out_specs=(
            pl.BlockSpec((1, lines, 4, rows, columns), lambda step: (step, 0, 0, 0, 0)),
            pl.BlockSpec((1, 1, columns), lambda step: (step, 0, 0)),
        ),
        scratch_shapes=[
            pltpu.VMEM((full, columns * 2), low),
            pltpu.VMEM((lines * rows, columns * 2), low),
            pltpu.VMEM((lines * rows, columns * 2), low),
            pltpu.VMEM((full, columns), low),
            pltpu.VMEM((full, columns), wide),
            pltpu.VMEM((lines, rows, columns), low),
            pltpu.VMEM((lines, rows, columns), low),
            pltpu.VMEM((2, lines, rows, columns), low),
            pltpu.VMEM((2, lines, rows, columns), low),
            pltpu.SemaphoreType.DMA((4,)),
        ],
        compiler_params=params(15),
        cost_estimate=cost(3 * chunks * full**3, 16 * chunks * full * full),
    )(mine, theirs, *roots)


def return_chunks(made):
    line, place, core = here()
    parts = [pick(made, line, 1)]
    for flip in (1, 2, 3):
        parts.append(send(pick(made, flipped(line, flip), 1), line_pairs(flip)))
    return parts


def last_kernel(
    pair, pair_other, down, down_other, blocks, left_stat, right_stat, scales, *outs
):
    grad_out, left_out, right_out, block_out = outs
    line, place, core = here()
    columns = pair.shape[4]

    def update(number, which, mine, theirs):
        for (source, index), half in ((mine, which), (theirs, 1 - which)):
            part = slice(half * columns, (half + 1) * columns)
            pieces = [source[index + (kind,)].astype(wide) for kind in range(4)]
            grad_out[number, :, part] = pieces[0]
            left_out[number, :, part] = 0.5 * left_stat[number, :, part] + 0.5 * pieces[1]
            right_out[number, :, part] = 0.5 * right_stat[number, :, part] + 0.5 * pieces[2]
            step = pieces[3] * scales[6 * which + number]
            block_out[number, :, part] = blocks[number, :, part] - step

    @pl.when(core == 0)
    def first():
        for number in range(6):
            index = (flipped(line, number % 4), number // 4)
            update(number, 0, (pair, index), (pair_other, index))

    @pl.when(core == 1)
    def second():
        for number in range(6):
            source, other = (pair, pair_other) if number < 2 else (down, down_other)
            index = (flipped(line, (number + 2) % 4), 1 if number < 2 else 0)
            update(number, 1, (source, index), (other, index))


def update_blocks(pair, pair_other, down, down_other, blocks, left_stat, right_stat, scales):
    turned = [jnp.transpose(value, (1, 0, 2)) for value in (blocks, left_stat, right_stat)]
    shape = jax.ShapeDtypeStruct(turned[0].shape, wide)
    outs = pl.pallas_call(
        last_kernel,
        out_shape=(shape,) * 4,
        in_specs=[on_chip()] * 7 + [pl.BlockSpec(memory_space=pltpu.SMEM)],
        out_specs=(on_chip(),) * 4,
        compiler_params=params(10),
        cost_estimate=cost(0, 32 * shape.size),
    )(pair, pair_other, down, down_other, *turned, scales)
    return [jnp.transpose(value, (1, 0, 2)) for value in outs]


def head_masks():
    lane = lax.broadcasted_iota(jnp.int32, (1, 2 * HEAD_DIM), 1)
    return [(lane < HEAD_DIM).astype(wide).astype(low), (lane >= HEAD_DIM).astype(wide).astype(low)]


def head_shares(query, key, same):
    scores = dot(query, key, 1, 1) * HEAD_DIM ** (-0.5)
    scores = jnp.where(same, scores, -1e30)
    raised = jnp.exp(scores - jnp.max(scores, axis=-1, keepdims=True))
    return raised / jnp.sum(raised, axis=-1, keepdims=True)


STORE_ROWS = 32768


def store_views(store, rows, width):
    weights = [store.at[pl.ds(block * width, width)] for block in range(4)]
    made = [store.at[pl.ds(4 * width + kind * rows, rows)] for kind in range(3)]
    sides = [store.at[pl.ds(4 * width + (3 + side) * rows, rows)] for side in range(2)]
    return weights, made, sides


def attend_kernel(
    buffer, one, two, three, four, seg_column, seg_row, answer_ref, store, weights, made, sides, sems
):
    rows, width = buffer.shape
    weights_out, made_out, sides_out = store_views(store, rows, width)
    for block in range(4):
        place_block((one, two, three, four), block, weights.at[block])
    copies = fetch([weights.at[block] for block in range(4)], weights_out, sems)
    same = seg_column[...] == seg_row[...]
    for kind in range(3):
        made[kind] = dot(buffer[...], weights[kind]).astype(low)
    copies += fetch([made.at[kind] for kind in range(3)], made_out, sems.at[pl.ds(4, 3)])
    pair_width = 2 * HEAD_DIM
    for pair in range(width // pair_width):
        part = slice(pair * pair_width, (pair + 1) * pair_width)
        query, key, value = (made[kind, :, part] for kind in range(3))
        context = None
        for mask in head_masks():
            shares = head_shares(query, key * mask, same).astype(low)
            term = dot(shares, value * mask)
            context = term if context is None else context + term
        sides[1, :, part] = context.astype(low)
    sides[0] = buffer[...]
    copies += fetch([sides.at[side] for side in range(2)], sides_out, sems.at[pl.ds(7, 2)])
    answer_ref[...] = dot(sides[1], weights[3]).astype(low)
    finish(copies)


def attend_scratch(rows, width):
    return [
        pltpu.VMEM((4, width, width), low),
        pltpu.VMEM((3, rows, width), low),
        pltpu.VMEM((2, rows, width), low),
        pltpu.SemaphoreType.DMA((9,)),
    ]


def attend(buffer, parts, segment):
    rows, width = buffer.shape
    return pl.pallas_call(
        attend_kernel,
        out_shape=(
            jax.ShapeDtypeStruct((rows, width), low),
            jax.ShapeDtypeStruct((STORE_ROWS, width), low),
        ),
        in_specs=[on_chip()] * 7,
        out_specs=(on_chip(), in_hbm()),
        scratch_shapes=attend_scratch(rows, width),
        compiler_params=params(20),
        cost_estimate=cost(12 * rows * width * width, 12 * width * width),
    )(buffer, *parts, segment[:, None], segment[None, :])


def attend_back_kernel(
    store,
    seg_column,
    seg_row,
    grad_answer,
    theirs_ref,
    grads_ref,
    grad_buffer_ref,
    sides,
    grad_context_ref,
    weights,
    made,
    sems,
):
    rows, width = grad_answer.shape
    weights_from, made_from, sides_from = store_views(store, rows, width)
    out_copy, *copies = fetch(
        [weights_from[3]] + made_from + sides_from + weights_from[:3],
        [weights.at[3]]
        + [made.at[kind] for kind in range(3)]
        + [sides.at[side] for side in range(2)]
        + [weights.at[block] for block in range(3)],
        sems,
    )
    same = seg_column[...] == seg_row[...]
    core = lax.axis_index("own")
    out_copy.wait()
    grad_context_ref[...] = dot(grad_answer[...], weights[3], 1, 1).astype(low)
    finish(copies[:3])
    grads_ref[3] = grad_answer[...]
    pair_width = 2 * HEAD_DIM
    for pair in range(width // pair_width):
        part = slice(pair * pair_width, (pair + 1) * pair_width)
        query, key, value = (made[kind, :, part] for kind in range(3))
        above = grad_context_ref[:, part]
        sums = [None] * 3
        for mask in head_masks():
            key_head = key * mask
            shares = head_shares(query, key_head, same)
            grad_shares = dot(above, value * mask, 1, 1)
            inner = jnp.sum(shares * grad_shares, axis=-1, keepdims=True)
            grad_scores = (shares * (grad_shares - inner)).astype(low)
            terms = (
                dot(grad_scores, key_head),
                dot(grad_scores, query * mask, 0, 0),
                dot(shares.astype(low), above * mask, 0, 0),
            )
            sums = [
                term if total is None else total + term for term, total in zip(terms, sums)
            ]
        for kind, factor in enumerate((HEAD_DIM ** (-0.5), HEAD_DIM ** (-0.5), 1.0)):
            grads_ref[kind, :, part] = (sums[kind] * factor).astype(low)
    finish(copies[3:5])
    columns = theirs_ref.shape[2]
    part = pl.ds(pl.multiple_of((1 - core) * columns, columns), columns)
    for kind in range(4):
        theirs_ref[kind] = dot(sides[kind // 3], grads_ref[kind, :, part], 0, 0).astype(low)
    finish(copies[5:])
    total = dot(grads_ref[0], weights[0], 1, 1)
    total = total + dot(grads_ref[1], weights[1], 1, 1)
    total = total + dot(grads_ref[2], weights[2], 1, 1)
    grad_buffer_ref[...] = total.astype(low)


def attend_back(store, segment, grad_answer):
    rows, width = grad_answer.shape
    weights, made, sides, sems = attend_scratch(rows, width)
    return pl.pallas_call(
        attend_back_kernel,
        out_shape=(
            jax.ShapeDtypeStruct((4, width, width // 2), low),
            jax.ShapeDtypeStruct((4, rows, width), low),
            jax.ShapeDtypeStruct((rows, width), low),
            jax.ShapeDtypeStruct((2, rows, width), low),
        ),
        in_specs=[in_hbm()] + [on_chip()] * 3,
        out_specs=(on_chip(),) * 4,
        scratch_shapes=[pltpu.VMEM((rows, width), low), weights, made, sems],
        compiler_params=params(18),
        cost_estimate=cost(20 * rows * width * width, 16 * width * width),
    )(store, segment[:, None], segment[None, :], grad_answer)


def normal_parts(values):
    center = values - jnp.mean(values, axis=-1, keepdims=True)
    spread = jnp.mean(center * center, axis=-1, keepdims=True)
    return center, lax.rsqrt(spread + norm_eps)


def forward_kernel(*refs):
    tokens, placing, returned, gates, vectors = refs[:5]
    parts = refs[5:9]
    hidden_ref, second_ref, active_ref, slope_ref, w_up = refs[9:14]
    step = pl.program_id(0)

    @pl.when(step == 0)
    def prepare():
        values = tokens[...].astype(wide) + gates[:, 0:1] * dot(placing[...], returned[...])
        hidden_ref[...] = values
        center, inverse = normal_parts(values)
        second_ref[...] = (center * inverse * vectors[3:4] + vectors[4:5]).astype(low)

    place_block(parts, step, w_up.at[step], True)
    before = dot(second_ref[...], w_up[step])
    share = 0.5 + 0.5 * lax.erf(before * (0.5**0.5))
    density = jnp.exp(before * before * -0.5) * (0.5 / math.pi) ** 0.5
    active_ref[step] = (before * share).astype(low)
    slope_ref[step] = (share + before * density).astype(low)


def token_forward(tokens, placing, returned, gates, vectors, parts):
    count, width = tokens.shape
    blocks = parts[0].shape[2] // 2
    by_block = jax.ShapeDtypeStruct((blocks, count, width), low)
    fetched = (tokens, placing, returned, gates, vectors)
    return pl.pallas_call(
        forward_kernel,
        grid=(blocks,),
        out_shape=(
            jax.ShapeDtypeStruct((count, width), wide),
            jax.ShapeDtypeStruct((count, width), low),
            by_block,
            by_block,
            jax.ShapeDtypeStruct((blocks, width, width), low),
        ),
        in_specs=[whole(value) for value in fetched] + [on_chip()] * 4,
        out_specs=(on_chip(),) * 5,
        compiler_params=params(18),
        cost_estimate=cost(8 * blocks * count * width * width, 8 * blocks * width * width),
    )(*fetched, *parts)


def backward_kernel(*refs):
    above, placing, returned, gates, vectors = refs[:5]
    (hidden, active, slope, w_up), parts = refs[5:9], refs[9:13]
    mixed_ref, packed_ref, grad_hidden_ref, logit_ref, vector_ref, inner_ref = refs[13:19]
    result, grad_second, w_down = refs[19:22]
    step = pl.program_id(0)
    place_block(parts, 4 + step, w_down, True)

    @pl.when(step == 0)
    def prepare():
        result[...] = hidden[...]
        grad_second[...] = jnp.zeros_like(grad_second)

    grad_active = dot(above[...], w_down[...], 1, 1)
    grad_inner = (grad_active * slope[step].astype(wide)).astype(low)
    inner_ref[step] = grad_inner
    result[...] += dot(active[step], w_down[...])
    grad_second[...] += dot(grad_inner, w_up[step], 1, 1)

    @pl.when(step == pl.num_programs(0) - 1)
    def complete():
        mixed_ref[...] = result[...].astype(low)
        center, inverse = normal_parts(hidden[...])
        scaled = center * inverse
        grads = grad_second[...]
        vector_ref[0:1] = jnp.sum(grads * scaled, axis=0, keepdims=True)
        vector_ref[1:2] = jnp.sum(grads, axis=0, keepdims=True)
        pulled = grads * vectors[3:4]
        pulled = (
            pulled
            - jnp.mean(pulled, axis=-1, keepdims=True)
            - scaled * jnp.mean(pulled * scaled, axis=-1, keepdims=True)
        )
        grad_hidden = above[...].astype(wide) + inverse * pulled
        grad_hidden_ref[...] = grad_hidden
        weighted = (grad_hidden * gates[:, 0:1]).astype(low)
        packed_ref[...] = dot(placing[...], weighted, 0, 0).astype(low)
        unpacked = dot(placing[...], returned[...])
        logit_ref[...] = gates[:, 1:2] * jnp.sum(grad_hidden * unpacked, axis=-1, keepdims=True)


def token_backward(above, hidden, active, slope, placing, returned, gates, vectors, w_up, parts):
    count, width = above.shape
    slots = placing.shape[1]
    blocks = w_up.shape[0]
    fetched = (above, placing, returned, gates, vectors)
    return pl.pallas_call(
        backward_kernel,
        grid=(blocks,),
        out_shape=(
            jax.ShapeDtypeStruct((count, width), low),
            jax.ShapeDtypeStruct((slots, width), low),
            jax.ShapeDtypeStruct((count, width), wide),
            jax.ShapeDtypeStruct((count, 1), wide),
            jax.ShapeDtypeStruct((2, width), wide),
            jax.ShapeDtypeStruct((blocks, count, width), low),
        ),
        in_specs=[whole(value) for value in fetched] + [on_chip()] * 8,
        out_specs=(on_chip(),) * 6,
        scratch_shapes=[
            pltpu.VMEM((count, width), wide),
            pltpu.VMEM((count, width), wide),
            pltpu.VMEM((width, width), low),
        ],
        compiler_params=params(30),
        cost_estimate=cost(8 * blocks * count * width * width, 8 * blocks * width * width),
    )(*fetched, hidden, active, slope, w_up, *parts)


def outer_kernel(left, right, theirs_ref):
    core = lax.axis_index("own")
    step = pl.program_id(0)
    columns = theirs_ref.shape[2]
    left_step = step if left.shape[0] > 1 else 0
    right_step = step if right.shape[0] > 1 else 0
    part = pl.ds(pl.multiple_of((1 - core) * columns, columns), columns)
    theirs_ref[step] = dot(left[left_step], right[right_step, :, part], 0, 0).astype(low)


def outer_theirs(left, right):
    count, width = left.shape[1:]
    blocks = max(left.shape[0], right.shape[0])
    return pl.pallas_call(
        outer_kernel,
        grid=(blocks,),
        out_shape=jax.ShapeDtypeStruct((blocks, width, width // 2), low),
        in_specs=[on_chip()] * 2,
        out_specs=on_chip(),
        compiler_params=params(8),
        cost_estimate=cost(blocks * count * width * width, 3 * blocks * width * width),
    )(left, right)


def column(values):
    return values[:, None]


def pack_kernel(
    tokens, chosen, packing, vectors, placing_ref, packed_ref, gates_ref
):
    count = tokens.shape[0]
    capacity = packing.shape[0]
    center, inverse = normal_parts(tokens[...].astype(wide))
    first = (center * inverse * vectors[0:1] + vectors[1:2]).astype(low)
    gate = jax.nn.sigmoid(jnp.sum(first.astype(wide) * vectors[2:3], axis=-1, keepdims=True))
    weighting = jnp.where(chosen[...] == 1, gate, 0.0)
    gates_ref[:, 0:1] = weighting
    gates_ref[:, 1:2] = weighting * (1.0 - gate)
    above = lax.broadcasted_iota(jnp.int32, (count, count), 0)
    below = lax.broadcasted_iota(jnp.int32, (count, count), 1)
    earlier = (below <= above).astype(wide).astype(low)
    flags = jnp.broadcast_to(chosen[...].astype(wide), (count, capacity))
    rank = dot(earlier, flags.astype(low))
    place_of = lax.broadcasted_iota(jnp.int32, (count, capacity), 1).astype(wide) + 1.0
    ranked = jnp.where(rank == place_of, flags, 0.0).astype(low)
    slots = lax.broadcasted_iota(jnp.int32, (capacity, capacity), 1)
    slot_of = (packing[...] == slots).astype(wide).astype(low)
    placing = dot(ranked, slot_of).astype(low)
    placing_ref[...] = placing
    packed_ref[...] = dot(placing, first, 0, 0).astype(low)


def pack_tokens(tokens, chosen, packing, vectors):
    count, width = tokens.shape
    capacity = packing.shape[0]
    return pl.pallas_call(
        pack_kernel,
        out_shape=(
            jax.ShapeDtypeStruct((count, capacity), low),
            jax.ShapeDtypeStruct((capacity, width), low),
            jax.ShapeDtypeStruct((count, 2), wide),
        ),
        in_specs=[on_chip()] * 4,
        out_specs=(on_chip(),) * 3,
        compiler_params=params(10),
        cost_estimate=cost(4 * count * capacity * width, 8 * count * width),
    )(tokens, column(chosen), column(packing), vectors)


def token_back_kernel(*refs):
    sources, (out_ref, vector_ref), fetched, sems = refs[:6], refs[6:8], refs[8:14], refs[14]
    finish(fetch(sources, fetched, sems))
    tokens, placing, grad_sent, grad_hidden, grad_logit, vectors = fetched
    grad_first = dot(placing[...], grad_sent[...]) + grad_logit[...] * vectors[2:3]
    center, inverse = normal_parts(tokens[...].astype(wide))
    scaled = center * inverse
    vector_ref[0:1] = jnp.sum(grad_first * scaled, axis=0, keepdims=True)
    vector_ref[1:2] = jnp.sum(grad_first, axis=0, keepdims=True)
    first = (scaled * vectors[0:1] + vectors[1:2]).astype(low).astype(wide)
    vector_ref[2:3] = jnp.sum(grad_logit[...] * first, axis=0, keepdims=True)
    pulled = grad_first * vectors[0:1]
    pulled = (
        pulled
        - jnp.mean(pulled, axis=-1, keepdims=True)
        - scaled * jnp.mean(pulled * scaled, axis=-1, keepdims=True)
    )
    out_ref[...] = (grad_hidden[...] + inverse * pulled).astype(low)


def token_back(tokens, placing, grad_sent, grad_hidden, grad_logit, vectors):
    count, width = tokens.shape
    return pl.pallas_call(
        token_back_kernel,
        out_shape=(
            jax.ShapeDtypeStruct((count, width), low),
            jax.ShapeDtypeStruct((3, width), wide),
        ),
        in_specs=[in_hbm()] * 6,
        out_specs=(on_chip(),) * 2,
        scratch_shapes=fetch_scratch(
            (tokens, placing, grad_sent, grad_hidden, grad_logit, vectors)
        ),
        compiler_params=params(17),
        cost_estimate=cost(2 * count * width * placing.shape[1], 12 * count * width),
    )(tokens, placing, grad_sent, grad_hidden, grad_logit, vectors)


def flip_pairs(flip):
    return [(i, i ^ flip) for i in range(32)]


def all_sum(value):
    value = value + send(value, swap_pairs())
    for one, two in ((2, 4), (8, 16)):
        near = value + send(value, flip_pairs(one))
        far = send(value, flip_pairs(two)) + send(value, flip_pairs(one + two))
        value = near + far
    return value


def exchange(value, n_data):
    capacity, width = value.shape
    moved = lax.all_to_all(
        value.reshape(n_data, capacity // n_data, width), "dp", split_axis=0, concat_axis=0, tiled=True
    )
    return moved.reshape(capacity, width)


def block_shards(
    tokens,
    cotangent,
    selected,
    packing,
    segments,
    blocks,
    left_stat,
    right_stat,
    left_root,
    right_root,
    vectors,
    moment,
):
    model_width = tokens.shape[2]
    token_count = tokens.shape[0] * tokens.shape[1]
    n_data = lax.axis_size("dp")
    capacity = packing.shape[1]
    line, place, core = here()
    own_tokens = tokens.reshape(token_count, model_width)
    above = cotangent.reshape(token_count, model_width)
    segment = segments[0]

    every = columns_by_core(jnp.transpose(blocks, (1, 0, 2)).astype(low))
    placing, packed, gates = pack_tokens(
        own_tokens, selected.reshape(token_count), packing[0], vectors
    )
    buffer = exchange(packed, n_data)
    near_ffn = send(every[4:], plane_pairs(0))
    attn_two = send(every[:4], line_pairs(2))
    ffn_pair = jnp.stack([every[4:], near_ffn])
    ffn_got = send(after(ffn_pair, attn_two), line_pairs(2))
    attn_pair = jnp.stack([every[:4], after(attn_two, near_ffn)])
    attn_got = send(attn_pair, line_pairs(1))
    line_attn = after(jnp.concatenate([attn_pair, attn_got]), packed, ffn_got)
    every_root = roots_by_core(after(left_root, ffn_got), right_root)
    ffn_two = jnp.stack([ffn_pair, after(ffn_got, attn_got)])
    near_attn = send(line_attn, plane_pairs(0))
    first_attn = after(jnp.stack([line_attn, near_attn]), buffer, every_root)
    far_attn = send(first_attn, plane_pairs(1))
    first_ffn = gather_far(ffn_two)
    w_parts = with_other(first_attn, far_attn)
    answer, store = attend(buffer, w_parts, segment)
    root_given = lax.optimization_barrier((*roots_given(every_root), buffer, first_ffn))[:4]
    root_parts = [root_given[0]]
    for flip in (1, 2, 3):
        root_parts.append(send(root_given[flip], line_pairs(flip)))
    left_line, right_line = (jnp.stack([part[:, kind] for part in root_parts]) for kind in range(2))
    returned = exchange(answer, n_data)
    far_ffn = send(after(first_ffn, answer), plane_pairs(1))
    far_ffn = after(far_ffn, returned, right_line, left_line)
    ffn_parts = with_other(first_ffn, far_ffn)

    near_right = send(after(right_line, far_ffn), plane_pairs(0))
    first_right = jnp.stack([right_line, near_right])
    hidden, second_low, active, slope, w_up = token_forward(
        own_tokens, placing, returned, gates, vectors, ffn_parts
    )
    down_theirs = outer_theirs(after(active, near_right), above[None])
    far_right = send(first_right, plane_pairs(1))
    roots = (left_line, send(left_line, swap_pairs()), first_right, far_right)
    down_got = send(down_theirs, swap_pairs())
    down_give, *down_kept = sum_start(lambda step: step, active, above[None], down_got)
    down_got = send(down_give, plane_pairs(0))
    mixed, grad_packed, grad_hidden, grad_logit, vector_two, grad_inner = token_backward(
        above,
        hidden,
        active,
        slope,
        placing,
        returned,
        gates,
        vectors,
        after(w_up, down_give),
        ffn_parts,
    )
    grad_answer = exchange(grad_packed, n_data)
    up_theirs = outer_theirs(after(second_low, down_got, far_right)[None], grad_inner)

    down_kept, down_give = add_first(down_got, *down_kept)
    down_got = send(down_give, plane_pairs(1))
    up_got = send(after(up_theirs, grad_answer), swap_pairs())
    attn_theirs, grads, grad_buffer, sides = attend_back(store, segment, grad_answer)
    attn_got = send(after(attn_theirs, down_got), swap_pairs())
    up_give, *up_kept = sum_start(
        lambda step: 0, second_low[None], grad_inner, after(up_got, attn_theirs)
    )
    up_got = send(up_give, plane_pairs(0))
    down_own, down_two, down_give = cut_line((down_kept + down_got.astype(wide))[None])
    down_got = send(down_give, line_pairs(1))
    attn_give, *attn_kept = sum_start(
        lambda step: step // 3, sides, grads, after(attn_got, up_give)
    )
    attn_got = send(attn_give, plane_pairs(0))
    grad_sent = exchange(after(grad_buffer, attn_give), n_data)
    down_own, down_give = add_line(down_own, down_two, down_got)
    down_got = send(down_give, line_pairs(2))
    down_own = (down_own + down_got.astype(wide)).astype(low)
    down_near = send(down_own, plane_pairs(0))
    down_first = jnp.stack([down_own, down_near])
    down_far = send(down_first, plane_pairs(1))
    down_mine = jnp.concatenate([down_first, down_far])
    down_theirs = send(down_mine, swap_pairs())

    up_kept, up_give = add_first(up_got, *up_kept)
    attn_kept, attn_give = add_first(after(attn_got, down_far), *attn_kept)
    pair_got = send(jnp.stack([attn_give, up_give]), plane_pairs(1))
    down_made, down_square = step_chunks(down_mine, down_theirs, roots, 2)
    down_parts = return_chunks(down_made)
    pair_got = after(pair_got, down_made)
    pair_kept = jnp.stack([attn_kept, up_kept]) + pair_got.astype(wide)
    pair_own, pair_two, pair_give = cut_line(pair_kept)
    pair_got = send(pair_give, line_pairs(1))
    grad_tokens, vector_one = token_back(
        own_tokens, placing, grad_sent, grad_hidden, grad_logit, vectors
    )
    pair_own, pair_give = add_line(pair_own, pair_two, pair_got)
    pair_got = send(after(pair_give, vector_one), line_pairs(2))
    down = jnp.stack(down_parts)
    down_other = send(down, [(i, i ^ 1) for i in range(0, 32, 2)])
    pair_own = (pair_own + pair_got.astype(wide)).astype(low)
    pair_near = send(pair_own, plane_pairs(0))
    pair_first = jnp.stack([pair_own, pair_near])
    pair_far = send(pair_first, plane_pairs(1))
    pair_mine = jnp.concatenate([pair_first, pair_far])
    pair_theirs = send(after(pair_mine, *down_parts[1:]), swap_pairs())
    pair_made, pair_square = step_chunks(pair_mine, pair_theirs, roots, 0)
    pair = jnp.stack(return_chunks(pair_made))
    pair_other = send(pair, swap_pairs())
    squares = jnp.concatenate([jnp.sum(pair_square, axis=2), jnp.sum(down_square, axis=2)])
    lane = lax.broadcasted_iota(jnp.int32, (1, model_width), 1)
    square_row = sum(
        jnp.where(lane == 4 * chunk + line, squares[chunk], 0.0) for chunk in range(3)
    )
    sums = all_sum(jnp.concatenate([vector_one, vector_two, square_row]))
    vector_grad = sums[:5]
    size = model_width * model_width
    scales = block_rate * lax.rsqrt(sums[5, :12] / size + norm_eps)
    grad_own, left_new, right_new, new_blocks = update_blocks(
        pair, pair_other, down, down_other, blocks, left_stat, right_stat, scales
    )
    moment_new = 0.5 * moment + 0.5 * vector_grad
    row_squares = jnp.mean(moment_new * moment_new, axis=1, keepdims=True)
    vector_new = vectors - vector_rate * moment_new * lax.rsqrt(row_squares + norm_eps)
    return (
        mixed.reshape(tokens.shape),
        grad_tokens.reshape(tokens.shape),
        grad_own,
        left_new,
        right_new,
        new_blocks,
        vector_grad,
        moment_new,
        vector_new,
    )


def shards(
    tokens,
    cotangent,
    selected,
    packing,
    segments,
    blocks,
    left_stat,
    right_stat,
    left_root,
    right_root,
    vectors,
    moment,
):
    model_width = tokens.shape[2]
    token_count = tokens.shape[0] * tokens.shape[1]
    n_data = lax.axis_size("dp")
    n_owner = lax.axis_size("own")
    shard_rows = blocks.shape[0]
    own_blocks = blocks.shape[1]
    up_blocks = (own_blocks * n_owner - 4) // 2
    capacity = packing.shape[1]
    per_peer = capacity // n_data
    head_count = model_width // HEAD_DIM
    score_scale = HEAD_DIM ** (-0.5)
    flat_weights = blocks.astype(jnp.bfloat16).reshape(1, shard_rows * own_blocks * model_width)
    gathered = lax.all_gather(flat_weights, ("dp", "own"), axis=0, tiled=True)
    gathered = gathered.reshape(n_data, n_owner, shard_rows, own_blocks, model_width)

    def matrix(number):
        return gathered[:, number // own_blocks, :, number % own_blocks, :].reshape(
            model_width, model_width
        )

    w_query = matrix(0)
    w_key = matrix(1)
    w_value = matrix(2)
    w_out = matrix(3)
    w_up = jnp.concatenate([matrix(4 + position) for position in range(up_blocks)], axis=1)
    w_down = jnp.concatenate(
        [matrix(4 + up_blocks + position) for position in range(up_blocks)], axis=0
    )
    inputs = tokens.reshape(token_count, model_width).astype(jnp.float32)
    chosen = selected.reshape(token_count)
    normed_one, norm_one_back = jax.vjp(layer_norm, inputs, vectors[0], vectors[1])
    first_low = normed_one.astype(jnp.bfloat16)
    first_wide = first_low.astype(jnp.float32)
    gate_values = jax.nn.sigmoid(jnp.dot(first_wide, vectors[2], precision=highest))
    before = jnp.cumsum(chosen) - 1
    slot_index = jnp.where(chosen == 1, packing[0][jnp.clip(before, 0, capacity - 1)], -1)
    placing = (slot_index[None, :] == jnp.arange(capacity, dtype=jnp.int32)[:, None]).astype(
        jnp.bfloat16
    )
    packed = jnp.dot(placing, first_low, preferred_element_type=jnp.float32).astype(jnp.bfloat16)
    buffer = lax.all_to_all(
        packed.reshape(n_data, per_peer, model_width), "dp", split_axis=0, concat_axis=0, tiled=True
    )
    buffer = buffer.reshape(capacity, model_width)

    def project(matrix_in):
        made = jnp.dot(buffer, matrix_in, preferred_element_type=jnp.float32).astype(jnp.bfloat16)
        return made.reshape(capacity, head_count, HEAD_DIM)

    query_rows = project(w_query)
    key_rows = project(w_key)
    value_rows = project(w_value)
    segment = segments[0]
    block_rows = math.gcd(capacity, 512)
    starts = jnp.arange(capacity // block_rows, dtype=jnp.int32) * block_rows

    def masked_scores():
        scores = (
            jnp.einsum("qhd,khd->hqk", query_rows, key_rows, preferred_element_type=jnp.float32)
            * score_scale
        )
        same_segment = segment[:, None] == segment[None, :]
        return (jnp.where(same_segment[None, :, :], scores, -1e30), query_rows)

    def forward_block(first_row):
        scores, unused_block = masked_scores()
        largest = jnp.max(scores, axis=-1, keepdims=True)
        raised = jnp.exp(scores - largest)
        row_total = jnp.sum(raised, axis=-1, keepdims=True)
        shares = (raised / row_total).astype(jnp.bfloat16)
        context_part = jnp.einsum(
            "hqk,khd->qhd", shares, value_rows, preferred_element_type=jnp.float32
        )
        return (context_part.astype(jnp.bfloat16), largest[..., 0] + jnp.log(row_total[..., 0]))

    context_blocks, lse_blocks = lax.map(forward_block, starts)
    context = context_blocks.reshape(capacity, model_width)
    answer = jnp.dot(context, w_out, preferred_element_type=jnp.float32).astype(jnp.bfloat16)
    returned = lax.all_to_all(
        answer.reshape(n_data, per_peer, model_width), "dp", split_axis=0, concat_axis=0, tiled=True
    )
    returned = returned.reshape(capacity, model_width)
    unpacked = jnp.einsum("mt,md->td", placing, returned, preferred_element_type=jnp.float32)
    weighting = jnp.where(chosen == 1, gate_values, 0.0)
    hidden = inputs + weighting[:, None] * unpacked
    normed_two, norm_two_back = jax.vjp(layer_norm, hidden, vectors[3], vectors[4])
    second_low = normed_two.astype(jnp.bfloat16)
    pre_active = jnp.dot(second_low, w_up, preferred_element_type=jnp.float32)
    active_wide, gelu_back = jax.vjp(gelu_exact, pre_active)
    active = active_wide.astype(jnp.bfloat16)
    result = hidden + jnp.dot(active, w_down, preferred_element_type=jnp.float32)
    mixed = result.astype(jnp.bfloat16).reshape(tokens.shape)
    upstream = cotangent.reshape(token_count, model_width)
    grad_down = jnp.einsum("tf,td->fd", active, upstream, preferred_element_type=jnp.float32)
    grad_active = jnp.einsum("td,fd->tf", upstream, w_down, preferred_element_type=jnp.float32)
    grad_inner = gelu_back(grad_active)[0].astype(jnp.bfloat16)
    grad_up = jnp.einsum("td,tf->df", second_low, grad_inner, preferred_element_type=jnp.float32)
    grad_second = jnp.einsum("tf,df->td", grad_inner, w_up, preferred_element_type=jnp.float32)
    grad_hidden_part, grad_gain_two, grad_bias_two = norm_two_back(grad_second)
    grad_hidden = upstream.astype(jnp.float32) + grad_hidden_part
    grad_token_back = (grad_hidden * weighting[:, None]).astype(jnp.bfloat16)
    grad_packed = jnp.dot(placing, grad_token_back, preferred_element_type=jnp.float32).astype(
        jnp.bfloat16
    )
    router_pull = jnp.where(chosen == 1, jnp.sum(grad_hidden * unpacked, axis=-1), 0.0)
    grad_logit = router_pull * gate_values * (1.0 - gate_values)
    grad_answer = lax.all_to_all(
        grad_packed.reshape(n_data, per_peer, model_width),
        "dp",
        split_axis=0,
        concat_axis=0,
        tiled=True,
    )
    grad_answer = grad_answer.reshape(capacity, model_width)
    grad_out = jnp.einsum("md,me->de", context, grad_answer, preferred_element_type=jnp.float32)
    grad_context = jnp.einsum("me,de->md", grad_answer, w_out, preferred_element_type=jnp.float32)
    grad_context = grad_context.astype(jnp.bfloat16).reshape(capacity, head_count, HEAD_DIM)

    def backward_block(running, item_pair):
        first_row, lse_block = item_pair
        scores, query_block = masked_scores()
        shares_wide = jnp.exp(scores - lse_block[..., None])
        grad_shares = jnp.einsum(
            "qhd,khd->hqk", grad_context, value_rows, preferred_element_type=jnp.float32
        )
        inner_sum = jnp.sum(shares_wide * grad_shares, axis=-1, keepdims=True)
        grad_scores = (shares_wide * (grad_shares - inner_sum)).astype(jnp.bfloat16)
        grad_query_block = (
            jnp.einsum("hqk,khd->qhd", grad_scores, key_rows, preferred_element_type=jnp.float32)
            * score_scale
        )
        key_sum = (
            running[0]
            + jnp.einsum(
                "hqk,qhd->khd", grad_scores, query_block, preferred_element_type=jnp.float32
            )
            * score_scale
        )
        value_sum = running[1] + jnp.einsum(
            "hqk,qhd->khd",
            shares_wide.astype(jnp.bfloat16),
            grad_context,
            preferred_element_type=jnp.float32,
        )
        return ((key_sum, value_sum), grad_query_block)

    zeros_init = jnp.zeros((capacity, head_count, HEAD_DIM), jnp.float32)
    (key_total, value_total), query_grads = lax.scan(
        backward_block, (zeros_init, zeros_init), (starts, lse_blocks)
    )
    grad_query = query_grads.reshape(capacity, model_width).astype(jnp.bfloat16)
    grad_key = key_total.reshape(capacity, model_width).astype(jnp.bfloat16)
    grad_value = value_total.reshape(capacity, model_width).astype(jnp.bfloat16)
    grad_w_query = jnp.einsum("md,me->de", buffer, grad_query, preferred_element_type=jnp.float32)
    grad_w_key = jnp.einsum("md,me->de", buffer, grad_key, preferred_element_type=jnp.float32)
    grad_w_value = jnp.einsum("md,me->de", buffer, grad_value, preferred_element_type=jnp.float32)
    grad_buffer = jnp.einsum("me,de->md", grad_query, w_query, preferred_element_type=jnp.float32)
    grad_buffer = grad_buffer + jnp.einsum(
        "me,de->md", grad_key, w_key, preferred_element_type=jnp.float32
    )
    grad_buffer = grad_buffer + jnp.einsum(
        "me,de->md", grad_value, w_value, preferred_element_type=jnp.float32
    )
    grad_buffer = grad_buffer.astype(jnp.bfloat16)
    grad_sent = lax.all_to_all(
        grad_buffer.reshape(n_data, per_peer, model_width),
        "dp",
        split_axis=0,
        concat_axis=0,
        tiled=True,
    )
    grad_sent = grad_sent.reshape(capacity, model_width)
    grad_first = jnp.einsum("mt,md->td", placing, grad_sent, preferred_element_type=jnp.float32)
    grad_first = grad_first + grad_logit[:, None] * vectors[2][None, :]
    grad_router = jnp.sum(grad_logit[:, None] * first_wide, axis=0)
    grad_input_part, grad_gain_one, grad_bias_one = norm_one_back(grad_first)
    grad_tokens = (grad_hidden + grad_input_part).astype(jnp.bfloat16).reshape(tokens.shape)
    pieces = [grad_w_query, grad_w_key, grad_w_value, grad_out]
    pieces = pieces + [
        grad_up[:, position * model_width : (position + 1) * model_width]
        for position in range(up_blocks)
    ]
    pieces = pieces + [
        grad_down[position * model_width : (position + 1) * model_width, :]
        for position in range(up_blocks)
    ]
    local_terms = jnp.stack(pieces, axis=1)
    vector_terms = jnp.stack(
        [grad_gain_one, grad_bias_one, grad_router, grad_gain_two, grad_bias_two]
    )
    partial_value = lax.psum_scatter(local_terms, "dp", scatter_dimension=0, tiled=True)
    grad_own = lax.psum_scatter(
        partial_value.astype(jnp.bfloat16), "own", scatter_dimension=1, tiled=True
    ).astype(jnp.float32)
    vector_grad = lax.psum(vector_terms, ("dp", "own"))
    full_grad = lax.all_gather(grad_own.astype(jnp.bfloat16), "dp", axis=0, tiled=True).astype(
        grad_own.dtype
    )
    row_start = lax.axis_index("dp") * shard_rows
    left_new = 0.5 * left_stat + 0.5 * jnp.einsum(
        "rbk,nbk->rbn", grad_own, full_grad, precision=highest
    )
    column_part = lax.dynamic_slice_in_dim(full_grad, row_start, shard_rows, 2)
    right_new = 0.5 * right_stat + 0.5 * jnp.einsum(
        "nbr,nbk->rbk", column_part, full_grad, precision=highest
    )
    lefted = jnp.einsum("rbn,nbk->rbk", left_root, full_grad, precision=highest)
    precond = jnp.zeros_like(grad_own) + jnp.einsum(
        "rbn,nbk->rbk",
        lefted,
        lax.all_gather(right_root.astype(jnp.bfloat16), "dp", axis=0, tiled=True).astype(
            jnp.float32
        ),
        precision=highest,
    )
    square_sums = lax.psum(jnp.sum(precond * precond, axis=(0, 2)), "dp")
    step_scale = lax.rsqrt(square_sums / (model_width * model_width) + norm_eps)
    new_blocks = blocks - block_rate * precond * step_scale[None, :, None]
    moment_new = 0.5 * moment + 0.5 * vector_grad
    row_squares = jnp.mean(moment_new * moment_new, axis=1, keepdims=True)
    vector_new = vectors - vector_rate * moment_new * lax.rsqrt(row_squares + norm_eps)
    return (
        mixed,
        grad_tokens,
        grad_own,
        left_new,
        right_new,
        new_blocks,
        vector_grad,
        moment_new,
        vector_new,
    )


def solution(mesh):
    placed = (
        P(("dp", "own"), None, None),
        P(("dp", "own"), None, None),
        P(("dp", "own"), None),
        P(("dp", "own"), None),
        P(("dp", "own"), None),
        P("dp", "own", None),
        P("dp", "own", None),
        P("dp", "own", None),
        P("dp", "own", None),
        P("dp", "own", None),
        P(),
        P(),
    )
    small = mesh.shape["dp"] == 16 and mesh.shape["own"] == 2
    return jax.shard_map(
        block_shards if small else shards,
        mesh=mesh,
        in_specs=placed,
        out_specs=(
            P(("dp", "own"), None, None),
            P(("dp", "own"), None, None),
            P("dp", "own", None),
            P("dp", "own", None),
            P("dp", "own", None),
            P("dp", "own", None),
            P(),
            P(),
            P(),
        ),
        check_vma=False,
    )
```

```python
import functools
import math

import jax
import jax.numpy as jnp
from jax import lax
from jax.experimental import pallas as pl
from jax.experimental.pallas import tpu as pltpu
from jax.sharding import PartitionSpec as P

HEAD_DIM = 64


norm_eps = 1e-06
block_rate = 0.03
vector_rate = 0.04
highest = lax.Precision.HIGHEST


def layer_norm(values, norm_gain, norm_bias):
    center = values - jnp.mean(values, axis=-1, keepdims=True)
    spread = jnp.mean(center * center, axis=-1, keepdims=True)
    return center * lax.rsqrt(spread + norm_eps) * norm_gain + norm_bias


def gelu_exact(values):
    return jax.nn.gelu(values, approximate=False)


BOTH = ("dp", "own")
low = jnp.bfloat16
wide = jnp.float32
MIB = 2**20


def swap_pairs():
    return [(i, i ^ 1) for i in range(32)]


def plane_pairs(step):
    pairs = []
    for i in range(32):
        place, core = i // 2, i % 2
        flip = (1, 2)[step ^ core]
        pairs.append((i, (place ^ flip) * 2 + core))
    return pairs


def line_pairs(flip):
    return [(i, i ^ (8 * flip)) for i in range(32)]


def send(value, pairs):
    return lax.ppermute(value, BOTH, pairs)


def after(value, *others):
    return lax.optimization_barrier((value,) + others)[0]


def pick(value, index, axis):
    return lax.dynamic_index_in_dim(value, index, axis, keepdims=False)


def first_core():
    return lax.axis_index("own") == 0


def halves(value):
    middle = value.shape[-1] // 2
    lower, upper = value[..., :middle], value[..., middle:]
    return jnp.where(first_core(), lower, upper), jnp.where(first_core(), upper, lower)


def in_core_order(mine, theirs, axis):
    return jnp.where(
        first_core(),
        jnp.concatenate([mine, theirs], axis=axis),
        jnp.concatenate([theirs, mine], axis=axis),
    )


LINE_FLIPS = (0, 2, 1, 3)


def flipped(index, flip):
    return jnp.bitwise_xor(index, flip)


def spots(place, half):
    first, second = half + 1, 2 - half
    return [
        place,
        flipped(place, first),
        flipped(place, second),
        flipped(place, 3),
    ]


def here():
    device = lax.axis_index("dp")
    return device // 4, device % 4, lax.axis_index("own")


def dot(left, right, left_axis=1, right_axis=0):
    return lax.dot_general(
        left, right, (((left_axis,), (right_axis,)), ((), ())), preferred_element_type=wide
    )


def on_chip():
    return pl.BlockSpec(memory_space=pltpu.VMEM)


def whole(value):
    return pl.BlockSpec(value.shape, lambda *steps: (0,) * value.ndim)


def in_hbm():
    return pl.BlockSpec(memory_space=pltpu.HBM)


def fetch_scratch(values):
    return [pltpu.VMEM(value.shape, value.dtype) for value in values] + [
        pltpu.SemaphoreType.DMA((len(values),))
    ]


def fetch(sources, targets, sems):
    copies = [
        pltpu.make_async_copy(source, target, sems.at[number])
        for number, (source, target) in enumerate(zip(sources, targets))
    ]
    for copy in copies:
        copy.start()
    return copies


def finish(copies):
    for copy in copies:
        copy.wait()


def params(limit):
    return pltpu.CompilerParams(vmem_limit_bytes=limit * MIB)


def cost(flops, moved):
    return pl.CostEstimate(flops=flops, bytes_accessed=moved, transcendentals=0)


def place_block(parts, block, target):
    line, place, core = here()
    rows, columns = parts[0].shape[3:]
    for other in range(2):
        half = core if other == 0 else 1 - core
        column_slice = pl.ds(pl.multiple_of(half * columns, columns), columns)
        for number, spot in enumerate(spots(place, half)):
            for index, flip in enumerate(LINE_FLIPS):
                start = (flipped(line, flip) * 4 + spot) * rows
                row_slice = pl.ds(pl.multiple_of(start, rows), rows)
                piece = parts[2 * other + number // 2][number % 2, index, block]
                target[row_slice, column_slice] = piece


def weight_kernel(first_block, one, two, three, four, out_ref):
    for block in range(out_ref.shape[0]):
        place_block((one, two, three, four), first_block + block, out_ref.at[block])


def place_weights(parts, first_block, blocks):
    rows, columns = parts[0].shape[3:]
    full = rows * 16
    return pl.pallas_call(
        functools.partial(weight_kernel, first_block),
        out_shape=jax.ShapeDtypeStruct((blocks, full, 2 * columns), low),
        in_specs=[on_chip()] * 4,
        out_specs=on_chip(),
        compiler_params=params(10),
        cost_estimate=cost(0, 8 * blocks * full * columns),
    )(*parts)


def columns_by_core(value):
    keep, give = halves(value)
    return in_core_order(keep, send(give, swap_pairs()), 0)


def gather_far(pair):
    return jnp.concatenate([pair, send(pair, line_pairs(1))])


def with_other(first, far):
    return [first, far, send(first, swap_pairs()), send(far, swap_pairs())]


def roots_by_core(left_root, right_root):
    both = [jnp.transpose(root, (1, 0, 2)).astype(low) for root in (left_root, right_root)]
    every = columns_by_core(jnp.stack(both, axis=1))
    return every.reshape((3, 4) + every.shape[1:])


def roots_given(every):
    line, place, core = here()
    return [pick(every, flipped(line, flip), 1) for flip in range(4)]


def sum_kernel(left_of, left, right, got, give_ref, kept_ref, passed_ref, total):
    line, place, core = here()
    step = pl.program_id(0)
    columns = got.shape[2]
    rows = kept_ref.shape[2]
    part = pl.ds(pl.multiple_of(core * columns, columns), columns)
    right_step = step if right.shape[0] > 1 else 0
    made = dot(left[left_of(step)], right[right_step, :, part], 0, 0)
    total[...] = made + got[step].astype(wide)
    own, first, second, both = spots(place, core)
    for row_line in range(4):

        def piece(spot):
            return total[pl.ds(pl.multiple_of((row_line * 4 + spot) * rows, rows), rows), :]

        give_ref[0, step, row_line] = piece(first).astype(low)
        give_ref[1, step, row_line] = piece(both).astype(low)
        kept_ref[step, row_line] = piece(own).astype(low)
        passed_ref[step, row_line] = piece(second).astype(low)


def sum_start(left_of, left, right, got):
    count, width = left.shape[1:]
    blocks, full, columns = got.shape
    shape = (blocks, 4, full // 16, columns)
    return pl.pallas_call(
        functools.partial(sum_kernel, left_of),
        grid=(blocks,),
        out_shape=(
            jax.ShapeDtypeStruct((2,) + shape, low),
            jax.ShapeDtypeStruct(shape, low),
            jax.ShapeDtypeStruct(shape, low),
        ),
        in_specs=[on_chip()] * 3,
        out_specs=(on_chip(),) * 3,
        scratch_shapes=[pltpu.VMEM((full, columns), wide)],
        compiler_params=params(12),
        cost_estimate=cost(blocks * count * width * width, 5 * blocks * width * width),
    )(left, right, got)


def add_first(got, kept, passed):
    kept = kept.astype(wide) + got[0].astype(wide)
    return kept, (passed.astype(wide) + got[1].astype(wide)).astype(low)


def cut_line(kept):
    line, place, core = here()
    given = jnp.stack([pick(kept, flipped(line, flip), 1) for flip in (1, 3)]).astype(low)
    return pick(kept, line, 1), pick(kept, flipped(line, 2), 1), given


def add_line(own, two, got):
    return own + got[0].astype(wide), (two + got[1].astype(wide)).astype(low)


def step_kernel(
    number,
    mine,
    theirs,
    left_mine_from,
    left_theirs_from,
    right_first_from,
    right_far_from,
    out_ref,
    square_ref,
    grad_ref,
    rows_ref,
    left_ref,
    right_ref,
    cross_ref,
    left_mine,
    left_theirs,
    right_first,
    right_far,
    sems,
):
    chunk = number + pl.program_id(0)
    copies = fetch(
        [
            left_mine_from.at[:, chunk],
            left_theirs_from.at[:, chunk],
            right_first_from.at[:, :, chunk],
            right_far_from.at[:, :, chunk],
        ],
        [left_mine, left_theirs, right_first, right_far],
        sems,
    )
    line, place, core = here()
    rows, columns = mine.shape[3:]

    def rows_of(row_line, spot):
        return pl.ds(pl.multiple_of((row_line * 4 + spot) * rows, rows), rows)

    def column_half(half):
        return pl.ds(pl.multiple_of(half * columns, columns), columns)

    for half, group in ((core, mine), (1 - core, theirs)):
        for number, spot in enumerate(spots(place, half)):
            for step in range(4):
                grad_ref[rows_of(step, spot), column_half(half)] = group[number, 0, step]
    finish(copies)
    for half, left in ((core, left_mine), (1 - core, left_theirs)):
        for flip in range(4):
            target = pl.ds(pl.multiple_of(flipped(line, flip) * rows, rows), rows)
            left_ref[target, column_half(half)] = left[flip]
    for number, spot in enumerate(spots(place, core)):
        source = right_far if number > 1 else right_first
        for flip in range(4):
            right_ref[rows_of(flipped(line, flip), spot), :] = source[number % 2, flip]
    for row_line in range(4):
        rows_ref[row_line * rows : (row_line + 1) * rows, :] = grad_ref[rows_of(row_line, place), :]
    left = dot(rows_ref[...], grad_ref[column_half(core), :], 1, 1)
    cross_ref[...] = dot(grad_ref[...], grad_ref[:, column_half(core)], 0, 0)
    lefted = dot(left_ref[...], grad_ref[...]).astype(low)
    stepped = dot(lefted, right_ref[...])
    square_ref[0] = jnp.sum(stepped * stepped, axis=0, keepdims=True)
    for row_line in range(4):
        part = slice(row_line * rows, (row_line + 1) * rows)
        out_ref[0, row_line, 0] = mine[0, 0, row_line]
        out_ref[0, row_line, 1] = left[part].astype(low)
        out_ref[0, row_line, 2] = cross_ref[rows_of(row_line, place), :].astype(low)
        out_ref[0, row_line, 3] = stepped[part].astype(low)


def step_chunks(mine, theirs, roots, number):
    chunks, lines, rows, columns = mine.shape[1:]
    full = rows * 16
    grad_spec = pl.BlockSpec((4, 1, lines, rows, columns), lambda step: (0, step, 0, 0, 0))
    return pl.pallas_call(
        functools.partial(step_kernel, number),
        grid=(chunks,),
        out_shape=(
            jax.ShapeDtypeStruct((chunks, lines, 4, rows, columns), low),
            jax.ShapeDtypeStruct((chunks, 1, columns), wide),
        ),
        in_specs=[grad_spec] * 2 + [in_hbm()] * 4,
        out_specs=(
            pl.BlockSpec((1, lines, 4, rows, columns), lambda step: (step, 0, 0, 0, 0)),
            pl.BlockSpec((1, 1, columns), lambda step: (step, 0, 0)),
        ),
        scratch_shapes=[
            pltpu.VMEM((full, columns * 2), low),
            pltpu.VMEM((lines * rows, columns * 2), low),
            pltpu.VMEM((lines * rows, columns * 2), low),
            pltpu.VMEM((full, columns), low),
            pltpu.VMEM((full, columns), wide),
            pltpu.VMEM((lines, rows, columns), low),
            pltpu.VMEM((lines, rows, columns), low),
            pltpu.VMEM((2, lines, rows, columns), low),
            pltpu.VMEM((2, lines, rows, columns), low),
            pltpu.SemaphoreType.DMA((4,)),
        ],
        compiler_params=params(15),
        cost_estimate=cost(3 * chunks * full**3, 16 * chunks * full * full),
    )(mine, theirs, *roots)


def return_chunks(made):
    line, place, core = here()
    parts = [pick(made, line, 1)]
    for flip in (1, 2, 3):
        parts.append(send(pick(made, flipped(line, flip), 1), line_pairs(flip)))
    return parts


def last_kernel(
    pair, pair_other, down, down_other, blocks, left_stat, right_stat, scales, *outs
):
    grad_out, left_out, right_out, block_out = outs
    line, place, core = here()
    columns = pair.shape[4]

    def update(number, which, mine, theirs):
        for (source, index), half in ((mine, which), (theirs, 1 - which)):
            part = slice(half * columns, (half + 1) * columns)
            pieces = [source[index + (kind,)].astype(wide) for kind in range(4)]
            grad_out[number, :, part] = pieces[0]
            left_out[number, :, part] = 0.5 * left_stat[number, :, part] + 0.5 * pieces[1]
            right_out[number, :, part] = 0.5 * right_stat[number, :, part] + 0.5 * pieces[2]
            step = pieces[3] * scales[6 * which + number]
            block_out[number, :, part] = blocks[number, :, part] - step

    @pl.when(core == 0)
    def first():
        for number in range(6):
            index = (flipped(line, number % 4), number // 4)
            update(number, 0, (pair, index), (pair_other, index))

    @pl.when(core == 1)
    def second():
        for number in range(6):
            source, other = (pair, pair_other) if number < 2 else (down, down_other)
            index = (flipped(line, (number + 2) % 4), 1 if number < 2 else 0)
            update(number, 1, (source, index), (other, index))


def update_blocks(pair, pair_other, down, down_other, blocks, left_stat, right_stat, scales):
    turned = [jnp.transpose(value, (1, 0, 2)) for value in (blocks, left_stat, right_stat)]
    shape = jax.ShapeDtypeStruct(turned[0].shape, wide)
    outs = pl.pallas_call(
        last_kernel,
        out_shape=(shape,) * 4,
        in_specs=[on_chip()] * 7 + [pl.BlockSpec(memory_space=pltpu.SMEM)],
        out_specs=(on_chip(),) * 4,
        compiler_params=params(10),
        cost_estimate=cost(0, 32 * shape.size),
    )(pair, pair_other, down, down_other, *turned, scales)
    return [jnp.transpose(value, (1, 0, 2)) for value in outs]


def head_masks():
    lane = lax.broadcasted_iota(jnp.int32, (1, 2 * HEAD_DIM), 1)
    return [(lane < HEAD_DIM).astype(wide).astype(low), (lane >= HEAD_DIM).astype(wide).astype(low)]


def head_shares(query, key, same):
    scores = dot(query, key, 1, 1) * HEAD_DIM ** (-0.5)
    scores = jnp.where(same, scores, -1e30)
    raised = jnp.exp(scores - jnp.max(scores, axis=-1, keepdims=True))
    return raised / jnp.sum(raised, axis=-1, keepdims=True)


STORE_ROWS = 32768


def store_views(store, rows, width):
    weights = [store.at[pl.ds(block * width, width)] for block in range(4)]
    made = [store.at[pl.ds(4 * width + kind * rows, rows)] for kind in range(3)]
    sides = [store.at[pl.ds(4 * width + (3 + side) * rows, rows)] for side in range(2)]
    return weights, made, sides


def attend_kernel(
    buffer, one, two, three, four, seg_column, seg_row, answer_ref, store, weights, made, sides, sems
):
    rows, width = buffer.shape
    weights_out, made_out, sides_out = store_views(store, rows, width)
    for block in range(4):
        place_block((one, two, three, four), block, weights.at[block])
    copies = fetch([weights.at[block] for block in range(4)], weights_out, sems)
    same = seg_column[...] == seg_row[...]
    for kind in range(3):
        made[kind] = dot(buffer[...], weights[kind]).astype(low)
    copies += fetch([made.at[kind] for kind in range(3)], made_out, sems.at[pl.ds(4, 3)])
    pair_width = 2 * HEAD_DIM
    for pair in range(width // pair_width):
        part = slice(pair * pair_width, (pair + 1) * pair_width)
        query, key, value = (made[kind, :, part] for kind in range(3))
        context = None
        for mask in head_masks():
            shares = head_shares(query, key * mask, same).astype(low)
            term = dot(shares, value * mask)
            context = term if context is None else context + term
        sides[1, :, part] = context.astype(low)
    sides[0] = buffer[...]
    copies += fetch([sides.at[side] for side in range(2)], sides_out, sems.at[pl.ds(7, 2)])
    answer_ref[...] = dot(sides[1], weights[3]).astype(low)
    finish(copies)


def attend_scratch(rows, width):
    return [
        pltpu.VMEM((4, width, width), low),
        pltpu.VMEM((3, rows, width), low),
        pltpu.VMEM((2, rows, width), low),
        pltpu.SemaphoreType.DMA((9,)),
    ]


def attend(buffer, parts, segment):
    rows, width = buffer.shape
    return pl.pallas_call(
        attend_kernel,
        out_shape=(
            jax.ShapeDtypeStruct((rows, width), low),
            jax.ShapeDtypeStruct((STORE_ROWS, width), low),
        ),
        in_specs=[on_chip()] * 7,
        out_specs=(on_chip(), in_hbm()),
        scratch_shapes=attend_scratch(rows, width),
        compiler_params=params(20),
        cost_estimate=cost(12 * rows * width * width, 12 * width * width),
    )(buffer, *parts, segment[:, None], segment[None, :])


def attend_back_kernel(
    store,
    seg_column,
    seg_row,
    grad_answer,
    theirs_ref,
    grads_ref,
    grad_buffer_ref,
    sides,
    grad_context_ref,
    weights,
    made,
    sems,
):
    rows, width = grad_answer.shape
    weights_from, made_from, sides_from = store_views(store, rows, width)
    out_copy, *copies = fetch(
        [weights_from[3]] + made_from + sides_from + weights_from[:3],
        [weights.at[3]]
        + [made.at[kind] for kind in range(3)]
        + [sides.at[side] for side in range(2)]
        + [weights.at[block] for block in range(3)],
        sems,
    )
    same = seg_column[...] == seg_row[...]
    core = lax.axis_index("own")
    out_copy.wait()
    grad_context_ref[...] = dot(grad_answer[...], weights[3], 1, 1).astype(low)
    finish(copies[:3])
    grads_ref[3] = grad_answer[...]
    pair_width = 2 * HEAD_DIM
    for pair in range(width // pair_width):
        part = slice(pair * pair_width, (pair + 1) * pair_width)
        query, key, value = (made[kind, :, part] for kind in range(3))
        above = grad_context_ref[:, part]
        sums = [None] * 3
        for mask in head_masks():
            key_head = key * mask
            shares = head_shares(query, key_head, same)
            grad_shares = dot(above, value * mask, 1, 1)
            inner = jnp.sum(shares * grad_shares, axis=-1, keepdims=True)
            grad_scores = (shares * (grad_shares - inner)).astype(low)
            terms = (
                dot(grad_scores, key_head),
                dot(grad_scores, query * mask, 0, 0),
                dot(shares.astype(low), above * mask, 0, 0),
            )
            sums = [
                term if total is None else total + term for term, total in zip(terms, sums)
            ]
        for kind, factor in enumerate((HEAD_DIM ** (-0.5), HEAD_DIM ** (-0.5), 1.0)):
            grads_ref[kind, :, part] = (sums[kind] * factor).astype(low)
    finish(copies[3:5])
    columns = theirs_ref.shape[2]
    part = pl.ds(pl.multiple_of((1 - core) * columns, columns), columns)
    for kind in range(4):
        theirs_ref[kind] = dot(sides[kind // 3], grads_ref[kind, :, part], 0, 0).astype(low)
    finish(copies[5:])
    total = dot(grads_ref[0], weights[0], 1, 1)
    total = total + dot(grads_ref[1], weights[1], 1, 1)
    total = total + dot(grads_ref[2], weights[2], 1, 1)
    grad_buffer_ref[...] = total.astype(low)


def attend_back(store, segment, grad_answer):
    rows, width = grad_answer.shape
    weights, made, sides, sems = attend_scratch(rows, width)
    return pl.pallas_call(
        attend_back_kernel,
        out_shape=(
            jax.ShapeDtypeStruct((4, width, width // 2), low),
            jax.ShapeDtypeStruct((4, rows, width), low),
            jax.ShapeDtypeStruct((rows, width), low),
            jax.ShapeDtypeStruct((2, rows, width), low),
        ),
        in_specs=[in_hbm()] + [on_chip()] * 3,
        out_specs=(on_chip(),) * 4,
        scratch_shapes=[pltpu.VMEM((rows, width), low), weights, made, sems],
        compiler_params=params(18),
        cost_estimate=cost(20 * rows * width * width, 16 * width * width),
    )(store, segment[:, None], segment[None, :], grad_answer)


def normal_parts(values):
    center = values - jnp.mean(values, axis=-1, keepdims=True)
    spread = jnp.mean(center * center, axis=-1, keepdims=True)
    return center, lax.rsqrt(spread + norm_eps)


def forward_kernel(*refs):
    tokens, placing, returned, gates, vectors = refs[:5]
    parts = refs[5:9]
    hidden_ref, second_ref, active_ref, slope_ref, w_up = refs[9:14]
    step = pl.program_id(0)

    @pl.when(step == 0)
    def prepare():
        values = tokens[...].astype(wide) + gates[:, 0:1] * dot(placing[...], returned[...])
        hidden_ref[...] = values
        center, inverse = normal_parts(values)
        second_ref[...] = (center * inverse * vectors[3:4] + vectors[4:5]).astype(low)

    place_block(parts, step, w_up.at[step])
    before = dot(second_ref[...], w_up[step])
    share = 0.5 + 0.5 * lax.erf(before * (0.5**0.5))
    density = jnp.exp(before * before * -0.5) * (0.5 / math.pi) ** 0.5
    active_ref[step] = (before * share).astype(low)
    slope_ref[step] = (share + before * density).astype(low)


def token_forward(tokens, placing, returned, gates, vectors, parts):
    count, width = tokens.shape
    blocks = parts[0].shape[2] // 2
    by_block = jax.ShapeDtypeStruct((blocks, count, width), low)
    fetched = (tokens, placing, returned, gates, vectors)
    return pl.pallas_call(
        forward_kernel,
        grid=(blocks,),
        out_shape=(
            jax.ShapeDtypeStruct((count, width), wide),
            jax.ShapeDtypeStruct((count, width), low),
            by_block,
            by_block,
            jax.ShapeDtypeStruct((blocks, width, width), low),
        ),
        in_specs=[whole(value) for value in fetched] + [on_chip()] * 4,
        out_specs=(on_chip(),) * 5,
        compiler_params=params(18),
        cost_estimate=cost(8 * blocks * count * width * width, 8 * blocks * width * width),
    )(*fetched, *parts)


def backward_kernel(*refs):
    above, placing, returned, gates, vectors = refs[:5]
    hidden, active, slope, w_up, w_down = refs[5:10]
    mixed_ref, packed_ref, grad_hidden_ref, logit_ref, vector_ref, inner_ref = refs[10:16]
    result, grad_second = refs[16:]
    step = pl.program_id(0)

    @pl.when(step == 0)
    def prepare():
        result[...] = hidden[...]
        grad_second[...] = jnp.zeros_like(grad_second)

    grad_active = dot(above[...], w_down[step], 1, 1)
    grad_inner = (grad_active * slope[step].astype(wide)).astype(low)
    inner_ref[step] = grad_inner
    result[...] += dot(active[step], w_down[step])
    grad_second[...] += dot(grad_inner, w_up[step], 1, 1)

    @pl.when(step == pl.num_programs(0) - 1)
    def complete():
        mixed_ref[...] = result[...].astype(low)
        center, inverse = normal_parts(hidden[...])
        scaled = center * inverse
        grads = grad_second[...]
        vector_ref[0:1] = jnp.sum(grads * scaled, axis=0, keepdims=True)
        vector_ref[1:2] = jnp.sum(grads, axis=0, keepdims=True)
        pulled = grads * vectors[3:4]
        pulled = (
            pulled
            - jnp.mean(pulled, axis=-1, keepdims=True)
            - scaled * jnp.mean(pulled * scaled, axis=-1, keepdims=True)
        )
        grad_hidden = above[...].astype(wide) + inverse * pulled
        grad_hidden_ref[...] = grad_hidden
        weighted = (grad_hidden * gates[:, 0:1]).astype(low)
        packed_ref[...] = dot(placing[...], weighted, 0, 0).astype(low)
        unpacked = dot(placing[...], returned[...])
        logit_ref[...] = gates[:, 1:2] * jnp.sum(grad_hidden * unpacked, axis=-1, keepdims=True)


def token_backward(above, hidden, active, slope, placing, returned, gates, vectors, w_up, w_down):
    count, width = above.shape
    slots = placing.shape[1]
    blocks = w_up.shape[0]
    fetched = (above, placing, returned, gates, vectors)
    return pl.pallas_call(
        backward_kernel,
        grid=(blocks,),
        out_shape=(
            jax.ShapeDtypeStruct((count, width), low),
            jax.ShapeDtypeStruct((slots, width), low),
            jax.ShapeDtypeStruct((count, width), wide),
            jax.ShapeDtypeStruct((count, 1), wide),
            jax.ShapeDtypeStruct((2, width), wide),
            jax.ShapeDtypeStruct((blocks, count, width), low),
        ),
        in_specs=[whole(value) for value in fetched] + [on_chip()] * 5,
        out_specs=(on_chip(),) * 6,
        scratch_shapes=[
            pltpu.VMEM((count, width), wide),
            pltpu.VMEM((count, width), wide),
        ],
        compiler_params=params(30),
        cost_estimate=cost(8 * blocks * count * width * width, 8 * blocks * width * width),
    )(*fetched, hidden, active, slope, w_up, w_down)


def outer_kernel(left, right, theirs_ref):
    core = lax.axis_index("own")
    step = pl.program_id(0)
    columns = theirs_ref.shape[2]
    left_step = step if left.shape[0] > 1 else 0
    right_step = step if right.shape[0] > 1 else 0
    part = pl.ds(pl.multiple_of((1 - core) * columns, columns), columns)
    theirs_ref[step] = dot(left[left_step], right[right_step, :, part], 0, 0).astype(low)


def outer_theirs(left, right):
    count, width = left.shape[1:]
    blocks = max(left.shape[0], right.shape[0])
    return pl.pallas_call(
        outer_kernel,
        grid=(blocks,),
        out_shape=jax.ShapeDtypeStruct((blocks, width, width // 2), low),
        in_specs=[on_chip()] * 2,
        out_specs=on_chip(),
        compiler_params=params(8),
        cost_estimate=cost(blocks * count * width * width, 3 * blocks * width * width),
    )(left, right)


def column(values):
    return values[:, None]


def pack_kernel(
    tokens, chosen, packing, vectors, placing_ref, packed_ref, gates_ref
):
    count = tokens.shape[0]
    capacity = packing.shape[0]
    center, inverse = normal_parts(tokens[...].astype(wide))
    first = (center * inverse * vectors[0:1] + vectors[1:2]).astype(low)
    gate = jax.nn.sigmoid(jnp.sum(first.astype(wide) * vectors[2:3], axis=-1, keepdims=True))
    weighting = jnp.where(chosen[...] == 1, gate, 0.0)
    gates_ref[:, 0:1] = weighting
    gates_ref[:, 1:2] = weighting * (1.0 - gate)
    above = lax.broadcasted_iota(jnp.int32, (count, count), 0)
    below = lax.broadcasted_iota(jnp.int32, (count, count), 1)
    earlier = (below <= above).astype(wide).astype(low)
    flags = jnp.broadcast_to(chosen[...].astype(wide), (count, capacity))
    rank = dot(earlier, flags.astype(low))
    place_of = lax.broadcasted_iota(jnp.int32, (count, capacity), 1).astype(wide) + 1.0
    ranked = jnp.where(rank == place_of, flags, 0.0).astype(low)
    slots = lax.broadcasted_iota(jnp.int32, (capacity, capacity), 1)
    slot_of = (packing[...] == slots).astype(wide).astype(low)
    placing = dot(ranked, slot_of).astype(low)
    placing_ref[...] = placing
    packed_ref[...] = dot(placing, first, 0, 0).astype(low)


def pack_tokens(tokens, chosen, packing, vectors):
    count, width = tokens.shape
    capacity = packing.shape[0]
    return pl.pallas_call(
        pack_kernel,
        out_shape=(
            jax.ShapeDtypeStruct((count, capacity), low),
            jax.ShapeDtypeStruct((capacity, width), low),
            jax.ShapeDtypeStruct((count, 2), wide),
        ),
        in_specs=[on_chip()] * 4,
        out_specs=(on_chip(),) * 3,
        compiler_params=params(10),
        cost_estimate=cost(4 * count * capacity * width, 8 * count * width),
    )(tokens, column(chosen), column(packing), vectors)


def token_back_kernel(*refs):
    sources, (out_ref, vector_ref), fetched, sems = refs[:6], refs[6:8], refs[8:14], refs[14]
    finish(fetch(sources, fetched, sems))
    tokens, placing, grad_sent, grad_hidden, grad_logit, vectors = fetched
    grad_first = dot(placing[...], grad_sent[...]) + grad_logit[...] * vectors[2:3]
    center, inverse = normal_parts(tokens[...].astype(wide))
    scaled = center * inverse
    vector_ref[0:1] = jnp.sum(grad_first * scaled, axis=0, keepdims=True)
    vector_ref[1:2] = jnp.sum(grad_first, axis=0, keepdims=True)
    first = (scaled * vectors[0:1] + vectors[1:2]).astype(low).astype(wide)
    vector_ref[2:3] = jnp.sum(grad_logit[...] * first, axis=0, keepdims=True)
    pulled = grad_first * vectors[0:1]
    pulled = (
        pulled
        - jnp.mean(pulled, axis=-1, keepdims=True)
        - scaled * jnp.mean(pulled * scaled, axis=-1, keepdims=True)
    )
    out_ref[...] = (grad_hidden[...] + inverse * pulled).astype(low)


def token_back(tokens, placing, grad_sent, grad_hidden, grad_logit, vectors):
    count, width = tokens.shape
    return pl.pallas_call(
        token_back_kernel,
        out_shape=(
            jax.ShapeDtypeStruct((count, width), low),
            jax.ShapeDtypeStruct((3, width), wide),
        ),
        in_specs=[in_hbm()] * 6,
        out_specs=(on_chip(),) * 2,
        scratch_shapes=fetch_scratch(
            (tokens, placing, grad_sent, grad_hidden, grad_logit, vectors)
        ),
        compiler_params=params(17),
        cost_estimate=cost(2 * count * width * placing.shape[1], 12 * count * width),
    )(tokens, placing, grad_sent, grad_hidden, grad_logit, vectors)


def flip_pairs(flip):
    return [(i, i ^ flip) for i in range(32)]


def all_sum(value):
    value = value + send(value, swap_pairs())
    for one, two in ((2, 4), (8, 16)):
        near = value + send(value, flip_pairs(one))
        far = send(value, flip_pairs(two)) + send(value, flip_pairs(one + two))
        value = near + far
    return value


def exchange(value, n_data):
    capacity, width = value.shape
    moved = lax.all_to_all(
        value.reshape(n_data, capacity // n_data, width), "dp", split_axis=0, concat_axis=0, tiled=True
    )
    return moved.reshape(capacity, width)


def block_shards(
    tokens,
    cotangent,
    selected,
    packing,
    segments,
    blocks,
    left_stat,
    right_stat,
    left_root,
    right_root,
    vectors,
    moment,
):
    model_width = tokens.shape[2]
    token_count = tokens.shape[0] * tokens.shape[1]
    n_data = lax.axis_size("dp")
    capacity = packing.shape[1]
    line, place, core = here()
    own_tokens = tokens.reshape(token_count, model_width)
    above = cotangent.reshape(token_count, model_width)
    segment = segments[0]

    every = columns_by_core(jnp.transpose(blocks, (1, 0, 2)).astype(low))
    placing, packed, gates = pack_tokens(
        own_tokens, selected.reshape(token_count), packing[0], vectors
    )
    buffer = exchange(packed, n_data)
    attn_two = send(every[:4], line_pairs(2))
    ffn_got = send(after(every[4:], attn_two), line_pairs(2))
    attn_pair = jnp.stack([every[:4], attn_two])
    attn_got = send(attn_pair, line_pairs(1))
    line_attn = after(jnp.concatenate([attn_pair, attn_got]), packed)
    ffn_two = jnp.stack([every[4:], after(ffn_got, attn_got)])
    near_attn = send(line_attn, plane_pairs(0))
    every_root = roots_by_core(after(left_root, ffn_two), right_root)
    first_attn = after(jnp.stack([line_attn, near_attn]), every_root, buffer)
    far_attn = send(first_attn, plane_pairs(1))
    line_ffn = gather_far(ffn_two)
    near_ffn = send(after(line_ffn, far_attn), plane_pairs(0))
    root_given = lax.optimization_barrier((*roots_given(every_root), buffer, line_ffn))[:4]
    root_parts = [root_given[0]]
    for flip in (1, 2, 3):
        root_parts.append(send(root_given[flip], line_pairs(flip)))
    w_parts = with_other(first_attn, far_attn)
    answer, store = attend(buffer, w_parts, segment)
    first_ffn = jnp.stack([line_ffn, near_ffn])
    left_line, right_line = (jnp.stack([part[:, kind] for part in root_parts]) for kind in range(2))
    returned = exchange(answer, n_data)
    far_ffn = after(send(after(first_ffn, *root_parts[1:]), plane_pairs(1)), returned, right_line, left_line)
    ffn_parts = with_other(first_ffn, far_ffn)

    near_right = send(after(right_line, far_ffn), plane_pairs(0))
    first_right = jnp.stack([right_line, near_right])
    hidden, second_low, active, slope, w_up = token_forward(
        own_tokens, placing, returned, gates, vectors, ffn_parts
    )
    down_theirs = outer_theirs(after(active, near_right), above[None])
    far_right = send(first_right, plane_pairs(1))
    roots = (left_line, send(left_line, swap_pairs()), first_right, far_right)
    w_down = place_weights(ffn_parts, 4, 4)
    down_got = send(down_theirs, swap_pairs())
    down_give, *down_kept = sum_start(
        lambda step: step, active, above[None], after(down_got, w_down)
    )
    down_got = send(down_give, plane_pairs(0))
    mixed, grad_packed, grad_hidden, grad_logit, vector_two, grad_inner = token_backward(
        above,
        hidden,
        active,
        slope,
        placing,
        returned,
        gates,
        vectors,
        w_up,
        after(w_down, down_give),
    )
    grad_answer = exchange(grad_packed, n_data)
    up_theirs = outer_theirs(after(second_low, down_got, far_right)[None], grad_inner)

    down_kept, down_give = add_first(down_got, *down_kept)
    down_got = send(down_give, plane_pairs(1))
    up_got = send(after(up_theirs, grad_answer), swap_pairs())
    attn_theirs, grads, grad_buffer, sides = attend_back(store, segment, grad_answer)
    attn_got = send(after(attn_theirs, down_got), swap_pairs())
    up_give, *up_kept = sum_start(
        lambda step: 0, second_low[None], grad_inner, after(up_got, attn_theirs)
    )
    up_got = send(up_give, plane_pairs(0))
    down_own, down_two, down_give = cut_line((down_kept + down_got.astype(wide))[None])
    down_got = send(down_give, line_pairs(1))
    attn_give, *attn_kept = sum_start(
        lambda step: step // 3, sides, grads, after(attn_got, up_give)
    )
    attn_got = send(attn_give, plane_pairs(0))
    grad_sent = exchange(after(grad_buffer, attn_give), n_data)
    down_own, down_give = add_line(down_own, down_two, down_got)
    down_got = send(down_give, line_pairs(2))
    down_own = (down_own + down_got.astype(wide)).astype(low)
    down_near = send(down_own, plane_pairs(0))
    down_first = jnp.stack([down_own, down_near])
    down_far = send(down_first, plane_pairs(1))
    down_mine = jnp.concatenate([down_first, down_far])
    down_theirs = send(down_mine, swap_pairs())

    up_kept, up_give = add_first(up_got, *up_kept)
    attn_kept, attn_give = add_first(after(attn_got, down_far), *attn_kept)
    pair_got = send(jnp.stack([attn_give, up_give]), plane_pairs(1))
    down_made, down_square = step_chunks(down_mine, down_theirs, roots, 2)
    down_parts = return_chunks(down_made)
    pair_got = after(pair_got, down_made)
    pair_kept = jnp.stack([attn_kept, up_kept]) + pair_got.astype(wide)
    pair_own, pair_two, pair_give = cut_line(pair_kept)
    pair_got = send(pair_give, line_pairs(1))
    grad_tokens, vector_one = token_back(
        own_tokens, placing, grad_sent, grad_hidden, grad_logit, vectors
    )
    pair_own, pair_give = add_line(pair_own, pair_two, pair_got)
    pair_got = send(after(pair_give, vector_one), line_pairs(2))
    down = jnp.stack(down_parts)
    down_other = send(down, [(i, i ^ 1) for i in range(0, 32, 2)])
    pair_own = (pair_own + pair_got.astype(wide)).astype(low)
    pair_near = send(pair_own, plane_pairs(0))
    pair_first = jnp.stack([pair_own, pair_near])
    pair_far = send(pair_first, plane_pairs(1))
    pair_mine = jnp.concatenate([pair_first, pair_far])
    pair_theirs = send(after(pair_mine, *down_parts[1:]), swap_pairs())
    pair_made, pair_square = step_chunks(pair_mine, pair_theirs, roots, 0)
    pair = jnp.stack(return_chunks(pair_made))
    pair_other = send(pair, swap_pairs())
    squares = jnp.concatenate([jnp.sum(pair_square, axis=2), jnp.sum(down_square, axis=2)])
    lane = lax.broadcasted_iota(jnp.int32, (1, model_width), 1)
    square_row = sum(
        jnp.where(lane == 4 * chunk + line, squares[chunk], 0.0) for chunk in range(3)
    )
    sums = all_sum(jnp.concatenate([vector_one, vector_two, square_row]))
    vector_grad = sums[:5]
    size = model_width * model_width
    scales = block_rate * lax.rsqrt(sums[5, :12] / size + norm_eps)
    grad_own, left_new, right_new, new_blocks = update_blocks(
        pair, pair_other, down, down_other, blocks, left_stat, right_stat, scales
    )
    moment_new = 0.5 * moment + 0.5 * vector_grad
    row_squares = jnp.mean(moment_new * moment_new, axis=1, keepdims=True)
    vector_new = vectors - vector_rate * moment_new * lax.rsqrt(row_squares + norm_eps)
    return (
        mixed.reshape(tokens.shape),
        grad_tokens.reshape(tokens.shape),
        grad_own,
        left_new,
        right_new,
        new_blocks,
        vector_grad,
        moment_new,
        vector_new,
    )


def shards(
    tokens,
    cotangent,
    selected,
    packing,
    segments,
    blocks,
    left_stat,
    right_stat,
    left_root,
    right_root,
    vectors,
    moment,
):
    model_width = tokens.shape[2]
    token_count = tokens.shape[0] * tokens.shape[1]
    n_data = lax.axis_size("dp")
    n_owner = lax.axis_size("own")
    shard_rows = blocks.shape[0]
    own_blocks = blocks.shape[1]
    up_blocks = (own_blocks * n_owner - 4) // 2
    capacity = packing.shape[1]
    per_peer = capacity // n_data
    head_count = model_width // HEAD_DIM
    score_scale = HEAD_DIM ** (-0.5)
    flat_weights = blocks.astype(jnp.bfloat16).reshape(1, shard_rows * own_blocks * model_width)
    gathered = lax.all_gather(flat_weights, ("dp", "own"), axis=0, tiled=True)
    gathered = gathered.reshape(n_data, n_owner, shard_rows, own_blocks, model_width)

    def matrix(number):
        return gathered[:, number // own_blocks, :, number % own_blocks, :].reshape(
            model_width, model_width
        )

    w_query = matrix(0)
    w_key = matrix(1)
    w_value = matrix(2)
    w_out = matrix(3)
    w_up = jnp.concatenate([matrix(4 + position) for position in range(up_blocks)], axis=1)
    w_down = jnp.concatenate(
        [matrix(4 + up_blocks + position) for position in range(up_blocks)], axis=0
    )
    inputs = tokens.reshape(token_count, model_width).astype(jnp.float32)
    chosen = selected.reshape(token_count)
    normed_one, norm_one_back = jax.vjp(layer_norm, inputs, vectors[0], vectors[1])
    first_low = normed_one.astype(jnp.bfloat16)
    first_wide = first_low.astype(jnp.float32)
    gate_values = jax.nn.sigmoid(jnp.dot(first_wide, vectors[2], precision=highest))
    before = jnp.cumsum(chosen) - 1
    slot_index = jnp.where(chosen == 1, packing[0][jnp.clip(before, 0, capacity - 1)], -1)
    placing = (slot_index[None, :] == jnp.arange(capacity, dtype=jnp.int32)[:, None]).astype(
        jnp.bfloat16
    )
    packed = jnp.dot(placing, first_low, preferred_element_type=jnp.float32).astype(jnp.bfloat16)
    buffer = lax.all_to_all(
        packed.reshape(n_data, per_peer, model_width), "dp", split_axis=0, concat_axis=0, tiled=True
    )
    buffer = buffer.reshape(capacity, model_width)

    def project(matrix_in):
        made = jnp.dot(buffer, matrix_in, preferred_element_type=jnp.float32).astype(jnp.bfloat16)
        return made.reshape(capacity, head_count, HEAD_DIM)

    query_rows = project(w_query)
    key_rows = project(w_key)
    value_rows = project(w_value)
    segment = segments[0]
    block_rows = math.gcd(capacity, 512)
    starts = jnp.arange(capacity // block_rows, dtype=jnp.int32) * block_rows

    def masked_scores():
        scores = (
            jnp.einsum("qhd,khd->hqk", query_rows, key_rows, preferred_element_type=jnp.float32)
            * score_scale
        )
        same_segment = segment[:, None] == segment[None, :]
        return (jnp.where(same_segment[None, :, :], scores, -1e30), query_rows)

    def forward_block(first_row):
        scores, unused_block = masked_scores()
        largest = jnp.max(scores, axis=-1, keepdims=True)
        raised = jnp.exp(scores - largest)
        row_total = jnp.sum(raised, axis=-1, keepdims=True)
        shares = (raised / row_total).astype(jnp.bfloat16)
        context_part = jnp.einsum(
            "hqk,khd->qhd", shares, value_rows, preferred_element_type=jnp.float32
        )
        return (context_part.astype(jnp.bfloat16), largest[..., 0] + jnp.log(row_total[..., 0]))

    context_blocks, lse_blocks = lax.map(forward_block, starts)
    context = context_blocks.reshape(capacity, model_width)
    answer = jnp.dot(context, w_out, preferred_element_type=jnp.float32).astype(jnp.bfloat16)
    returned = lax.all_to_all(
        answer.reshape(n_data, per_peer, model_width), "dp", split_axis=0, concat_axis=0, tiled=True
    )
    returned = returned.reshape(capacity, model_width)
    unpacked = jnp.einsum("mt,md->td", placing, returned, preferred_element_type=jnp.float32)
    weighting = jnp.where(chosen == 1, gate_values, 0.0)
    hidden = inputs + weighting[:, None] * unpacked
    normed_two, norm_two_back = jax.vjp(layer_norm, hidden, vectors[3], vectors[4])
    second_low = normed_two.astype(jnp.bfloat16)
    pre_active = jnp.dot(second_low, w_up, preferred_element_type=jnp.float32)
    active_wide, gelu_back = jax.vjp(gelu_exact, pre_active)
    active = active_wide.astype(jnp.bfloat16)
    result = hidden + jnp.dot(active, w_down, preferred_element_type=jnp.float32)
    mixed = result.astype(jnp.bfloat16).reshape(tokens.shape)
    upstream = cotangent.reshape(token_count, model_width)
    grad_down = jnp.einsum("tf,td->fd", active, upstream, preferred_element_type=jnp.float32)
    grad_active = jnp.einsum("td,fd->tf", upstream, w_down, preferred_element_type=jnp.float32)
    grad_inner = gelu_back(grad_active)[0].astype(jnp.bfloat16)
    grad_up = jnp.einsum("td,tf->df", second_low, grad_inner, preferred_element_type=jnp.float32)
    grad_second = jnp.einsum("tf,df->td", grad_inner, w_up, preferred_element_type=jnp.float32)
    grad_hidden_part, grad_gain_two, grad_bias_two = norm_two_back(grad_second)
    grad_hidden = upstream.astype(jnp.float32) + grad_hidden_part
    grad_token_back = (grad_hidden * weighting[:, None]).astype(jnp.bfloat16)
    grad_packed = jnp.dot(placing, grad_token_back, preferred_element_type=jnp.float32).astype(
        jnp.bfloat16
    )
    router_pull = jnp.where(chosen == 1, jnp.sum(grad_hidden * unpacked, axis=-1), 0.0)
    grad_logit = router_pull * gate_values * (1.0 - gate_values)
    grad_answer = lax.all_to_all(
        grad_packed.reshape(n_data, per_peer, model_width),
        "dp",
        split_axis=0,
        concat_axis=0,
        tiled=True,
    )
    grad_answer = grad_answer.reshape(capacity, model_width)
    grad_out = jnp.einsum("md,me->de", context, grad_answer, preferred_element_type=jnp.float32)
    grad_context = jnp.einsum("me,de->md", grad_answer, w_out, preferred_element_type=jnp.float32)
    grad_context = grad_context.astype(jnp.bfloat16).reshape(capacity, head_count, HEAD_DIM)

    def backward_block(running, item_pair):
        first_row, lse_block = item_pair
        scores, query_block = masked_scores()
        shares_wide = jnp.exp(scores - lse_block[..., None])
        grad_shares = jnp.einsum(
            "qhd,khd->hqk", grad_context, value_rows, preferred_element_type=jnp.float32
        )
        inner_sum = jnp.sum(shares_wide * grad_shares, axis=-1, keepdims=True)
        grad_scores = (shares_wide * (grad_shares - inner_sum)).astype(jnp.bfloat16)
        grad_query_block = (
            jnp.einsum("hqk,khd->qhd", grad_scores, key_rows, preferred_element_type=jnp.float32)
            * score_scale
        )
        key_sum = (
            running[0]
            + jnp.einsum(
                "hqk,qhd->khd", grad_scores, query_block, preferred_element_type=jnp.float32
            )
            * score_scale
        )
        value_sum = running[1] + jnp.einsum(
            "hqk,qhd->khd",
            shares_wide.astype(jnp.bfloat16),
            grad_context,
            preferred_element_type=jnp.float32,
        )
        return ((key_sum, value_sum), grad_query_block)

    zeros_init = jnp.zeros((capacity, head_count, HEAD_DIM), jnp.float32)
    (key_total, value_total), query_grads = lax.scan(
        backward_block, (zeros_init, zeros_init), (starts, lse_blocks)
    )
    grad_query = query_grads.reshape(capacity, model_width).astype(jnp.bfloat16)
    grad_key = key_total.reshape(capacity, model_width).astype(jnp.bfloat16)
    grad_value = value_total.reshape(capacity, model_width).astype(jnp.bfloat16)
    grad_w_query = jnp.einsum("md,me->de", buffer, grad_query, preferred_element_type=jnp.float32)
    grad_w_key = jnp.einsum("md,me->de", buffer, grad_key, preferred_element_type=jnp.float32)
    grad_w_value = jnp.einsum("md,me->de", buffer, grad_value, preferred_element_type=jnp.float32)
    grad_buffer = jnp.einsum("me,de->md", grad_query, w_query, preferred_element_type=jnp.float32)
    grad_buffer = grad_buffer + jnp.einsum(
        "me,de->md", grad_key, w_key, preferred_element_type=jnp.float32
    )
    grad_buffer = grad_buffer + jnp.einsum(
        "me,de->md", grad_value, w_value, preferred_element_type=jnp.float32
    )
    grad_buffer = grad_buffer.astype(jnp.bfloat16)
    grad_sent = lax.all_to_all(
        grad_buffer.reshape(n_data, per_peer, model_width),
        "dp",
        split_axis=0,
        concat_axis=0,
        tiled=True,
    )
    grad_sent = grad_sent.reshape(capacity, model_width)
    grad_first = jnp.einsum("mt,md->td", placing, grad_sent, preferred_element_type=jnp.float32)
    grad_first = grad_first + grad_logit[:, None] * vectors[2][None, :]
    grad_router = jnp.sum(grad_logit[:, None] * first_wide, axis=0)
    grad_input_part, grad_gain_one, grad_bias_one = norm_one_back(grad_first)
    grad_tokens = (grad_hidden + grad_input_part).astype(jnp.bfloat16).reshape(tokens.shape)
    pieces = [grad_w_query, grad_w_key, grad_w_value, grad_out]
    pieces = pieces + [
        grad_up[:, position * model_width : (position + 1) * model_width]
        for position in range(up_blocks)
    ]
    pieces = pieces + [
        grad_down[position * model_width : (position + 1) * model_width, :]
        for position in range(up_blocks)
    ]
    local_terms = jnp.stack(pieces, axis=1)
    vector_terms = jnp.stack(
        [grad_gain_one, grad_bias_one, grad_router, grad_gain_two, grad_bias_two]
    )
    partial_value = lax.psum_scatter(local_terms, "dp", scatter_dimension=0, tiled=True)
    grad_own = lax.psum_scatter(
        partial_value.astype(jnp.bfloat16), "own", scatter_dimension=1, tiled=True
    ).astype(jnp.float32)
    vector_grad = lax.psum(vector_terms, ("dp", "own"))
    full_grad = lax.all_gather(grad_own.astype(jnp.bfloat16), "dp", axis=0, tiled=True).astype(
        grad_own.dtype
    )
    row_start = lax.axis_index("dp") * shard_rows
    left_new = 0.5 * left_stat + 0.5 * jnp.einsum(
        "rbk,nbk->rbn", grad_own, full_grad, precision=highest
    )
    column_part = lax.dynamic_slice_in_dim(full_grad, row_start, shard_rows, 2)
    right_new = 0.5 * right_stat + 0.5 * jnp.einsum(
        "nbr,nbk->rbk", column_part, full_grad, precision=highest
    )
    lefted = jnp.einsum("rbn,nbk->rbk", left_root, full_grad, precision=highest)
    precond = jnp.zeros_like(grad_own) + jnp.einsum(
        "rbn,nbk->rbk",
        lefted,
        lax.all_gather(right_root.astype(jnp.bfloat16), "dp", axis=0, tiled=True).astype(
            jnp.float32
        ),
        precision=highest,
    )
    square_sums = lax.psum(jnp.sum(precond * precond, axis=(0, 2)), "dp")
    step_scale = lax.rsqrt(square_sums / (model_width * model_width) + norm_eps)
    new_blocks = blocks - block_rate * precond * step_scale[None, :, None]
    moment_new = 0.5 * moment + 0.5 * vector_grad
    row_squares = jnp.mean(moment_new * moment_new, axis=1, keepdims=True)
    vector_new = vectors - vector_rate * moment_new * lax.rsqrt(row_squares + norm_eps)
    return (
        mixed,
        grad_tokens,
        grad_own,
        left_new,
        right_new,
        new_blocks,
        vector_grad,
        moment_new,
        vector_new,
    )


def solution(mesh):
    placed = (
        P(("dp", "own"), None, None),
        P(("dp", "own"), None, None),
        P(("dp", "own"), None),
        P(("dp", "own"), None),
        P(("dp", "own"), None),
        P("dp", "own", None),
        P("dp", "own", None),
        P("dp", "own", None),
        P("dp", "own", None),
        P("dp", "own", None),
        P(),
        P(),
    )
    small = mesh.shape["dp"] == 16 and mesh.shape["own"] == 2
    return jax.shard_map(
        block_shards if small else shards,
        mesh=mesh,
        in_specs=placed,
        out_specs=(
            P(("dp", "own"), None, None),
            P(("dp", "own"), None, None),
            P("dp", "own", None),
            P("dp", "own", None),
            P("dp", "own", None),
            P("dp", "own", None),
            P(),
            P(),
            P(),
        ),
        check_vma=False,
    )
```

```python
import functools
import math

import jax
import jax.numpy as jnp
from jax import lax
from jax.experimental import pallas as pl
from jax.experimental.pallas import tpu as pltpu
from jax.sharding import PartitionSpec as P

HEAD_DIM = 64


norm_eps = 1e-06
block_rate = 0.03
vector_rate = 0.04
highest = lax.Precision.HIGHEST


def layer_norm(values, norm_gain, norm_bias):
    center = values - jnp.mean(values, axis=-1, keepdims=True)
    spread = jnp.mean(center * center, axis=-1, keepdims=True)
    return center * lax.rsqrt(spread + norm_eps) * norm_gain + norm_bias


def gelu_exact(values):
    return jax.nn.gelu(values, approximate=False)


BOTH = ("dp", "own")
low = jnp.bfloat16
wide = jnp.float32
MIB = 2**20


def swap_pairs():
    return [(i, i ^ 1) for i in range(32)]


def plane_pairs(step):
    pairs = []
    for i in range(32):
        place, core = i // 2, i % 2
        flip = (1, 2)[step ^ core]
        pairs.append((i, (place ^ flip) * 2 + core))
    return pairs


def line_pairs(flip):
    return [(i, i ^ (8 * flip)) for i in range(32)]


def send(value, pairs):
    return lax.ppermute(value, BOTH, pairs)


def after(value, *others):
    return lax.optimization_barrier((value,) + others)[0]


def pick(value, index, axis):
    return lax.dynamic_index_in_dim(value, index, axis, keepdims=False)


def first_core():
    return lax.axis_index("own") == 0


def halves(value):
    middle = value.shape[-1] // 2
    lower, upper = value[..., :middle], value[..., middle:]
    return jnp.where(first_core(), lower, upper), jnp.where(first_core(), upper, lower)


def in_core_order(mine, theirs, axis):
    return jnp.where(
        first_core(),
        jnp.concatenate([mine, theirs], axis=axis),
        jnp.concatenate([theirs, mine], axis=axis),
    )


LINE_FLIPS = (0, 2, 1, 3)


def flipped(index, flip):
    return jnp.bitwise_xor(index, flip)


def spots(place, half):
    first, second = half + 1, 2 - half
    return [
        place,
        flipped(place, first),
        flipped(place, second),
        flipped(place, 3),
    ]


def here():
    device = lax.axis_index("dp")
    return device // 4, device % 4, lax.axis_index("own")


def dot(left, right, left_axis=1, right_axis=0):
    return lax.dot_general(
        left, right, (((left_axis,), (right_axis,)), ((), ())), preferred_element_type=wide
    )


def on_chip():
    return pl.BlockSpec(memory_space=pltpu.VMEM)


def whole(value):
    return pl.BlockSpec(value.shape, lambda *steps: (0,) * value.ndim)


def in_hbm():
    return pl.BlockSpec(memory_space=pltpu.HBM)


def fetch_scratch(values):
    return [pltpu.VMEM(value.shape, value.dtype) for value in values] + [
        pltpu.SemaphoreType.DMA((len(values),))
    ]


def fetch(sources, targets, sems):
    copies = [
        pltpu.make_async_copy(source, target, sems.at[number])
        for number, (source, target) in enumerate(zip(sources, targets))
    ]
    for copy in copies:
        copy.start()
    return copies


def finish(copies):
    for copy in copies:
        copy.wait()


def params(limit):
    return pltpu.CompilerParams(vmem_limit_bytes=limit * MIB)


def cost(flops, moved):
    return pl.CostEstimate(flops=flops, bytes_accessed=moved, transcendentals=0)


def place_block(parts, block, target):
    line, place, core = here()
    rows, columns = parts[0].shape[3:]
    for other in range(2):
        half = core if other == 0 else 1 - core
        column_slice = pl.ds(pl.multiple_of(half * columns, columns), columns)
        for number, spot in enumerate(spots(place, half)):
            for index, flip in enumerate(LINE_FLIPS):
                start = (flipped(line, flip) * 4 + spot) * rows
                row_slice = pl.ds(pl.multiple_of(start, rows), rows)
                piece = parts[2 * other + number // 2][number % 2, index, block]
                target[row_slice, column_slice] = piece


def weight_kernel(first_block, one, two, three, four, out_ref):
    for block in range(out_ref.shape[0]):
        place_block((one, two, three, four), first_block + block, out_ref.at[block])


def place_weights(parts, first_block, blocks):
    rows, columns = parts[0].shape[3:]
    full = rows * 16
    return pl.pallas_call(
        functools.partial(weight_kernel, first_block),
        out_shape=jax.ShapeDtypeStruct((blocks, full, 2 * columns), low),
        in_specs=[on_chip()] * 4,
        out_specs=on_chip(),
        compiler_params=params(10),
        cost_estimate=cost(0, 8 * blocks * full * columns),
    )(*parts)


def columns_by_core(value):
    keep, give = halves(value)
    return in_core_order(keep, send(give, swap_pairs()), 0)


def gather_far(pair):
    return jnp.concatenate([pair, send(pair, line_pairs(1))])


def with_other(first, far):
    return [first, far, send(first, swap_pairs()), send(far, swap_pairs())]


def roots_by_core(left_root, right_root):
    both = [jnp.transpose(root, (1, 0, 2)).astype(low) for root in (left_root, right_root)]
    every = columns_by_core(jnp.stack(both, axis=1))
    return every.reshape((3, 4) + every.shape[1:])


def roots_given(every):
    line, place, core = here()
    return [pick(every, flipped(line, flip), 1) for flip in range(4)]


def sum_kernel(left_of, left, right, got, give_ref, kept_ref, passed_ref, total):
    line, place, core = here()
    step = pl.program_id(0)
    columns = got.shape[2]
    rows = kept_ref.shape[2]
    part = pl.ds(pl.multiple_of(core * columns, columns), columns)
    right_step = step if right.shape[0] > 1 else 0
    made = dot(left[left_of(step)], right[right_step, :, part], 0, 0)
    total[...] = made + got[step].astype(wide)
    own, first, second, both = spots(place, core)
    for row_line in range(4):

        def piece(spot):
            return total[pl.ds(pl.multiple_of((row_line * 4 + spot) * rows, rows), rows), :]

        give_ref[0, step, row_line] = piece(first).astype(low)
        give_ref[1, step, row_line] = piece(both).astype(low)
        kept_ref[step, row_line] = piece(own).astype(low)
        passed_ref[step, row_line] = piece(second).astype(low)


def sum_start(left_of, left, right, got):
    count, width = left.shape[1:]
    blocks, full, columns = got.shape
    shape = (blocks, 4, full // 16, columns)
    return pl.pallas_call(
        functools.partial(sum_kernel, left_of),
        grid=(blocks,),
        out_shape=(
            jax.ShapeDtypeStruct((2,) + shape, low),
            jax.ShapeDtypeStruct(shape, low),
            jax.ShapeDtypeStruct(shape, low),
        ),
        in_specs=[on_chip()] * 3,
        out_specs=(on_chip(),) * 3,
        scratch_shapes=[pltpu.VMEM((full, columns), wide)],
        compiler_params=params(12),
        cost_estimate=cost(blocks * count * width * width, 5 * blocks * width * width),
    )(left, right, got)


def add_first(got, kept, passed):
    kept = kept.astype(wide) + got[0].astype(wide)
    return kept, (passed.astype(wide) + got[1].astype(wide)).astype(low)


def cut_line(kept):
    line, place, core = here()
    given = jnp.stack([pick(kept, flipped(line, flip), 1) for flip in (1, 3)]).astype(low)
    return pick(kept, line, 1), pick(kept, flipped(line, 2), 1), given


def add_line(own, two, got):
    return own + got[0].astype(wide), (two + got[1].astype(wide)).astype(low)


def step_kernel(
    number,
    mine,
    theirs,
    left_mine_from,
    left_theirs_from,
    right_first_from,
    right_far_from,
    out_ref,
    square_ref,
    grad_ref,
    rows_ref,
    left_ref,
    right_ref,
    cross_ref,
    left_mine,
    left_theirs,
    right_first,
    right_far,
    sems,
):
    chunk = number + pl.program_id(0)
    copies = fetch(
        [
            left_mine_from.at[:, chunk],
            left_theirs_from.at[:, chunk],
            right_first_from.at[:, :, chunk],
            right_far_from.at[:, :, chunk],
        ],
        [left_mine, left_theirs, right_first, right_far],
        sems,
    )
    line, place, core = here()
    rows, columns = mine.shape[3:]

    def rows_of(row_line, spot):
        return pl.ds(pl.multiple_of((row_line * 4 + spot) * rows, rows), rows)

    def column_half(half):
        return pl.ds(pl.multiple_of(half * columns, columns), columns)

    for half, group in ((core, mine), (1 - core, theirs)):
        for number, spot in enumerate(spots(place, half)):
            for step in range(4):
                grad_ref[rows_of(step, spot), column_half(half)] = group[number, 0, step]
    finish(copies)
    for half, left in ((core, left_mine), (1 - core, left_theirs)):
        for flip in range(4):
            target = pl.ds(pl.multiple_of(flipped(line, flip) * rows, rows), rows)
            left_ref[target, column_half(half)] = left[flip]
    for number, spot in enumerate(spots(place, core)):
        source = right_far if number > 1 else right_first
        for flip in range(4):
            right_ref[rows_of(flipped(line, flip), spot), :] = source[number % 2, flip]
    for row_line in range(4):
        rows_ref[row_line * rows : (row_line + 1) * rows, :] = grad_ref[rows_of(row_line, place), :]
    left = dot(rows_ref[...], grad_ref[column_half(core), :], 1, 1)
    cross_ref[...] = dot(grad_ref[...], grad_ref[:, column_half(core)], 0, 0)
    lefted = dot(left_ref[...], grad_ref[...]).astype(low)
    stepped = dot(lefted, right_ref[...])
    square_ref[0] = jnp.sum(stepped * stepped, axis=0, keepdims=True)
    for row_line in range(4):
        part = slice(row_line * rows, (row_line + 1) * rows)
        out_ref[0, row_line, 0] = mine[0, 0, row_line]
        out_ref[0, row_line, 1] = left[part].astype(low)
        out_ref[0, row_line, 2] = cross_ref[rows_of(row_line, place), :].astype(low)
        out_ref[0, row_line, 3] = stepped[part].astype(low)


def step_chunks(mine, theirs, roots, number):
    chunks, lines, rows, columns = mine.shape[1:]
    full = rows * 16
    grad_spec = pl.BlockSpec((4, 1, lines, rows, columns), lambda step: (0, step, 0, 0, 0))
    return pl.pallas_call(
        functools.partial(step_kernel, number),
        grid=(chunks,),
        out_shape=(
            jax.ShapeDtypeStruct((chunks, lines, 4, rows, columns), low),
            jax.ShapeDtypeStruct((chunks, 1, columns), wide),
        ),
        in_specs=[grad_spec] * 2 + [in_hbm()] * 4,
        out_specs=(
            pl.BlockSpec((1, lines, 4, rows, columns), lambda step: (step, 0, 0, 0, 0)),
            pl.BlockSpec((1, 1, columns), lambda step: (step, 0, 0)),
        ),
        scratch_shapes=[
            pltpu.VMEM((full, columns * 2), low),
            pltpu.VMEM((lines * rows, columns * 2), low),
            pltpu.VMEM((lines * rows, columns * 2), low),
            pltpu.VMEM((full, columns), low),
            pltpu.VMEM((full, columns), wide),
            pltpu.VMEM((lines, rows, columns), low),
            pltpu.VMEM((lines, rows, columns), low),
            pltpu.VMEM((2, lines, rows, columns), low),
            pltpu.VMEM((2, lines, rows, columns), low),
            pltpu.SemaphoreType.DMA((4,)),
        ],
        compiler_params=params(15),
        cost_estimate=cost(3 * chunks * full**3, 16 * chunks * full * full),
    )(mine, theirs, *roots)


def return_chunks(made):
    line, place, core = here()
    parts = [pick(made, line, 1)]
    for flip in (1, 2, 3):
        parts.append(send(pick(made, flipped(line, flip), 1), line_pairs(flip)))
    return parts


def last_kernel(
    pair, pair_other, down, down_other, blocks, left_stat, right_stat, scales, *outs
):
    grad_out, left_out, right_out, block_out = outs
    line, place, core = here()
    columns = pair.shape[4]

    def update(number, which, mine, theirs):
        for (source, index), half in ((mine, which), (theirs, 1 - which)):
            part = slice(half * columns, (half + 1) * columns)
            pieces = [source[index + (kind,)].astype(wide) for kind in range(4)]
            grad_out[number, :, part] = pieces[0]
            left_out[number, :, part] = 0.5 * left_stat[number, :, part] + 0.5 * pieces[1]
            right_out[number, :, part] = 0.5 * right_stat[number, :, part] + 0.5 * pieces[2]
            step = pieces[3] * scales[6 * which + number]
            block_out[number, :, part] = blocks[number, :, part] - step

    @pl.when(core == 0)
    def first():
        for number in range(6):
            index = (flipped(line, number % 4), number // 4)
            update(number, 0, (pair, index), (pair_other, index))

    @pl.when(core == 1)
    def second():
        for number in range(6):
            source, other = (pair, pair_other) if number < 2 else (down, down_other)
            index = (flipped(line, (number + 2) % 4), 1 if number < 2 else 0)
            update(number, 1, (source, index), (other, index))


def update_blocks(pair, pair_other, down, down_other, blocks, left_stat, right_stat, scales):
    turned = [jnp.transpose(value, (1, 0, 2)) for value in (blocks, left_stat, right_stat)]
    shape = jax.ShapeDtypeStruct(turned[0].shape, wide)
    outs = pl.pallas_call(
        last_kernel,
        out_shape=(shape,) * 4,
        in_specs=[on_chip()] * 7 + [pl.BlockSpec(memory_space=pltpu.SMEM)],
        out_specs=(on_chip(),) * 4,
        compiler_params=params(10),
        cost_estimate=cost(0, 32 * shape.size),
    )(pair, pair_other, down, down_other, *turned, scales)
    return [jnp.transpose(value, (1, 0, 2)) for value in outs]


def head_masks():
    lane = lax.broadcasted_iota(jnp.int32, (1, 2 * HEAD_DIM), 1)
    return [(lane < HEAD_DIM).astype(wide).astype(low), (lane >= HEAD_DIM).astype(wide).astype(low)]


def head_shares(query, key, same):
    scores = dot(query, key, 1, 1) * HEAD_DIM ** (-0.5)
    scores = jnp.where(same, scores, -1e30)
    raised = jnp.exp(scores - jnp.max(scores, axis=-1, keepdims=True))
    return raised / jnp.sum(raised, axis=-1, keepdims=True)


STORE_ROWS = 32768


def store_views(store, rows, width):
    weights = [store.at[pl.ds(block * width, width)] for block in range(4)]
    made = [store.at[pl.ds(4 * width + kind * rows, rows)] for kind in range(3)]
    sides = [store.at[pl.ds(4 * width + (3 + side) * rows, rows)] for side in range(2)]
    return weights, made, sides


def attend_kernel(
    buffer, one, two, three, four, seg_column, seg_row, answer_ref, store, weights, made, sides, sems
):
    rows, width = buffer.shape
    weights_out, made_out, sides_out = store_views(store, rows, width)
    for block in range(4):
        place_block((one, two, three, four), block, weights.at[block])
    copies = fetch([weights.at[block] for block in range(4)], weights_out, sems)
    same = seg_column[...] == seg_row[...]
    for kind in range(3):
        made[kind] = dot(buffer[...], weights[kind]).astype(low)
    copies += fetch([made.at[kind] for kind in range(3)], made_out, sems.at[pl.ds(4, 3)])
    pair_width = 2 * HEAD_DIM
    for pair in range(width // pair_width):
        part = slice(pair * pair_width, (pair + 1) * pair_width)
        query, key, value = (made[kind, :, part] for kind in range(3))
        context = None
        for mask in head_masks():
            shares = head_shares(query, key * mask, same).astype(low)
            term = dot(shares, value * mask)
            context = term if context is None else context + term
        sides[1, :, part] = context.astype(low)
    sides[0] = buffer[...]
    copies += fetch([sides.at[side] for side in range(2)], sides_out, sems.at[pl.ds(7, 2)])
    answer_ref[...] = dot(sides[1], weights[3]).astype(low)
    finish(copies)


def attend_scratch(rows, width):
    return [
        pltpu.VMEM((4, width, width), low),
        pltpu.VMEM((3, rows, width), low),
        pltpu.VMEM((2, rows, width), low),
        pltpu.SemaphoreType.DMA((9,)),
    ]


def attend(buffer, parts, segment):
    rows, width = buffer.shape
    return pl.pallas_call(
        attend_kernel,
        out_shape=(
            jax.ShapeDtypeStruct((rows, width), low),
            jax.ShapeDtypeStruct((STORE_ROWS, width), low),
        ),
        in_specs=[on_chip()] * 7,
        out_specs=(on_chip(), in_hbm()),
        scratch_shapes=attend_scratch(rows, width),
        compiler_params=params(20),
        cost_estimate=cost(12 * rows * width * width, 12 * width * width),
    )(buffer, *parts, segment[:, None], segment[None, :])


def attend_back_kernel(
    store,
    seg_column,
    seg_row,
    grad_answer,
    theirs_ref,
    grads_ref,
    grad_buffer_ref,
    sides,
    grad_context_ref,
    weights,
    made,
    sems,
):
    rows, width = grad_answer.shape
    weights_from, made_from, sides_from = store_views(store, rows, width)
    out_copy, *copies = fetch(
        [weights_from[3]] + made_from + sides_from + weights_from[:3],
        [weights.at[3]]
        + [made.at[kind] for kind in range(3)]
        + [sides.at[side] for side in range(2)]
        + [weights.at[block] for block in range(3)],
        sems,
    )
    same = seg_column[...] == seg_row[...]
    core = lax.axis_index("own")
    out_copy.wait()
    grad_context_ref[...] = dot(grad_answer[...], weights[3], 1, 1).astype(low)
    finish(copies[:3])
    grads_ref[3] = grad_answer[...]
    pair_width = 2 * HEAD_DIM
    for pair in range(width // pair_width):
        part = slice(pair * pair_width, (pair + 1) * pair_width)
        query, key, value = (made[kind, :, part] for kind in range(3))
        above = grad_context_ref[:, part]
        sums = [None] * 3
        for mask in head_masks():
            key_head = key * mask
            shares = head_shares(query, key_head, same)
            grad_shares = dot(above, value * mask, 1, 1)
            inner = jnp.sum(shares * grad_shares, axis=-1, keepdims=True)
            grad_scores = (shares * (grad_shares - inner)).astype(low)
            terms = (
                dot(grad_scores, key_head),
                dot(grad_scores, query * mask, 0, 0),
                dot(shares.astype(low), above * mask, 0, 0),
            )
            sums = [
                term if total is None else total + term for term, total in zip(terms, sums)
            ]
        for kind, factor in enumerate((HEAD_DIM ** (-0.5), HEAD_DIM ** (-0.5), 1.0)):
            grads_ref[kind, :, part] = (sums[kind] * factor).astype(low)
    finish(copies[3:5])
    columns = theirs_ref.shape[2]
    part = pl.ds(pl.multiple_of((1 - core) * columns, columns), columns)
    for kind in range(4):
        theirs_ref[kind] = dot(sides[kind // 3], grads_ref[kind, :, part], 0, 0).astype(low)
    finish(copies[5:])
    total = dot(grads_ref[0], weights[0], 1, 1)
    total = total + dot(grads_ref[1], weights[1], 1, 1)
    total = total + dot(grads_ref[2], weights[2], 1, 1)
    grad_buffer_ref[...] = total.astype(low)


def attend_back(store, segment, grad_answer):
    rows, width = grad_answer.shape
    weights, made, sides, sems = attend_scratch(rows, width)
    return pl.pallas_call(
        attend_back_kernel,
        out_shape=(
            jax.ShapeDtypeStruct((4, width, width // 2), low),
            jax.ShapeDtypeStruct((4, rows, width), low),
            jax.ShapeDtypeStruct((rows, width), low),
            jax.ShapeDtypeStruct((2, rows, width), low),
        ),
        in_specs=[in_hbm()] + [on_chip()] * 3,
        out_specs=(on_chip(),) * 4,
        scratch_shapes=[pltpu.VMEM((rows, width), low), weights, made, sems],
        compiler_params=params(18),
        cost_estimate=cost(20 * rows * width * width, 16 * width * width),
    )(store, segment[:, None], segment[None, :], grad_answer)


def normal_parts(values):
    center = values - jnp.mean(values, axis=-1, keepdims=True)
    spread = jnp.mean(center * center, axis=-1, keepdims=True)
    return center, lax.rsqrt(spread + norm_eps)


def forward_kernel(*refs):
    tokens, placing, returned, gates, vectors = refs[:5]
    parts = refs[5:9]
    hidden_ref, second_ref, active_ref, slope_ref, w_up = refs[9:14]
    step = pl.program_id(0)

    @pl.when(step == 0)
    def prepare():
        values = tokens[...].astype(wide) + gates[:, 0:1] * dot(placing[...], returned[...])
        hidden_ref[...] = values
        center, inverse = normal_parts(values)
        second_ref[...] = (center * inverse * vectors[3:4] + vectors[4:5]).astype(low)

    place_block(parts, step, w_up.at[step])
    before = dot(second_ref[...], w_up[step])
    share = 0.5 + 0.5 * lax.erf(before * (0.5**0.5))
    density = jnp.exp(before * before * -0.5) * (0.5 / math.pi) ** 0.5
    active_ref[step] = (before * share).astype(low)
    slope_ref[step] = (share + before * density).astype(low)


def token_forward(tokens, placing, returned, gates, vectors, parts):
    count, width = tokens.shape
    blocks = parts[0].shape[2] // 2
    by_block = jax.ShapeDtypeStruct((blocks, count, width), low)
    fetched = (tokens, placing, returned, gates, vectors)
    return pl.pallas_call(
        forward_kernel,
        grid=(blocks,),
        out_shape=(
            jax.ShapeDtypeStruct((count, width), wide),
            jax.ShapeDtypeStruct((count, width), low),
            by_block,
            by_block,
            jax.ShapeDtypeStruct((blocks, width, width), low),
        ),
        in_specs=[whole(value) for value in fetched] + [on_chip()] * 4,
        out_specs=(on_chip(),) * 5,
        compiler_params=params(18),
        cost_estimate=cost(8 * blocks * count * width * width, 8 * blocks * width * width),
    )(*fetched, *parts)


def backward_kernel(*refs):
    above, placing, returned, gates, vectors = refs[:5]
    hidden, active, slope, w_up, w_down = refs[5:10]
    mixed_ref, packed_ref, grad_hidden_ref, logit_ref, vector_ref, inner_ref = refs[10:16]
    result, grad_second = refs[16:]
    step = pl.program_id(0)

    @pl.when(step == 0)
    def prepare():
        result[...] = hidden[...]
        grad_second[...] = jnp.zeros_like(grad_second)

    grad_active = dot(above[...], w_down[step], 1, 1)
    grad_inner = (grad_active * slope[step].astype(wide)).astype(low)
    inner_ref[step] = grad_inner
    result[...] += dot(active[step], w_down[step])
    grad_second[...] += dot(grad_inner, w_up[step], 1, 1)

    @pl.when(step == pl.num_programs(0) - 1)
    def complete():
        mixed_ref[...] = result[...].astype(low)
        center, inverse = normal_parts(hidden[...])
        scaled = center * inverse
        grads = grad_second[...]
        vector_ref[0:1] = jnp.sum(grads * scaled, axis=0, keepdims=True)
        vector_ref[1:2] = jnp.sum(grads, axis=0, keepdims=True)
        pulled = grads * vectors[3:4]
        pulled = (
            pulled
            - jnp.mean(pulled, axis=-1, keepdims=True)
            - scaled * jnp.mean(pulled * scaled, axis=-1, keepdims=True)
        )
        grad_hidden = above[...].astype(wide) + inverse * pulled
        grad_hidden_ref[...] = grad_hidden
        weighted = (grad_hidden * gates[:, 0:1]).astype(low)
        packed_ref[...] = dot(placing[...], weighted, 0, 0).astype(low)
        unpacked = dot(placing[...], returned[...])
        logit_ref[...] = gates[:, 1:2] * jnp.sum(grad_hidden * unpacked, axis=-1, keepdims=True)


def token_backward(above, hidden, active, slope, placing, returned, gates, vectors, w_up, w_down):
    count, width = above.shape
    slots = placing.shape[1]
    blocks = w_up.shape[0]
    fetched = (above, placing, returned, gates, vectors)
    return pl.pallas_call(
        backward_kernel,
        grid=(blocks,),
        out_shape=(
            jax.ShapeDtypeStruct((count, width), low),
            jax.ShapeDtypeStruct((slots, width), low),
            jax.ShapeDtypeStruct((count, width), wide),
            jax.ShapeDtypeStruct((count, 1), wide),
            jax.ShapeDtypeStruct((2, width), wide),
            jax.ShapeDtypeStruct((blocks, count, width), low),
        ),
        in_specs=[whole(value) for value in fetched] + [on_chip()] * 5,
        out_specs=(on_chip(),) * 6,
        scratch_shapes=[
            pltpu.VMEM((count, width), wide),
            pltpu.VMEM((count, width), wide),
        ],
        compiler_params=params(30),
        cost_estimate=cost(8 * blocks * count * width * width, 8 * blocks * width * width),
    )(*fetched, hidden, active, slope, w_up, w_down)


def outer_kernel(left, right, theirs_ref):
    core = lax.axis_index("own")
    step = pl.program_id(0)
    columns = theirs_ref.shape[2]
    left_step = step if left.shape[0] > 1 else 0
    right_step = step if right.shape[0] > 1 else 0
    part = pl.ds(pl.multiple_of((1 - core) * columns, columns), columns)
    theirs_ref[step] = dot(left[left_step], right[right_step, :, part], 0, 0).astype(low)


def outer_theirs(left, right):
    count, width = left.shape[1:]
    blocks = max(left.shape[0], right.shape[0])
    return pl.pallas_call(
        outer_kernel,
        grid=(blocks,),
        out_shape=jax.ShapeDtypeStruct((blocks, width, width // 2), low),
        in_specs=[on_chip()] * 2,
        out_specs=on_chip(),
        compiler_params=params(8),
        cost_estimate=cost(blocks * count * width * width, 3 * blocks * width * width),
    )(left, right)


def column(values):
    return values[:, None]


def pack_kernel(
    tokens, chosen, packing, vectors, placing_ref, packed_ref, gates_ref
):
    count = tokens.shape[0]
    capacity = packing.shape[0]
    center, inverse = normal_parts(tokens[...].astype(wide))
    first = (center * inverse * vectors[0:1] + vectors[1:2]).astype(low)
    gate = jax.nn.sigmoid(jnp.sum(first.astype(wide) * vectors[2:3], axis=-1, keepdims=True))
    weighting = jnp.where(chosen[...] == 1, gate, 0.0)
    gates_ref[:, 0:1] = weighting
    gates_ref[:, 1:2] = weighting * (1.0 - gate)
    above = lax.broadcasted_iota(jnp.int32, (count, count), 0)
    below = lax.broadcasted_iota(jnp.int32, (count, count), 1)
    earlier = (below <= above).astype(wide).astype(low)
    flags = jnp.broadcast_to(chosen[...].astype(wide), (count, capacity))
    rank = dot(earlier, flags.astype(low))
    place_of = lax.broadcasted_iota(jnp.int32, (count, capacity), 1).astype(wide) + 1.0
    ranked = jnp.where(rank == place_of, flags, 0.0).astype(low)
    slots = lax.broadcasted_iota(jnp.int32, (capacity, capacity), 1)
    slot_of = (packing[...] == slots).astype(wide).astype(low)
    placing = dot(ranked, slot_of).astype(low)
    placing_ref[...] = placing
    packed_ref[...] = dot(placing, first, 0, 0).astype(low)


def pack_tokens(tokens, chosen, packing, vectors):
    count, width = tokens.shape
    capacity = packing.shape[0]
    return pl.pallas_call(
        pack_kernel,
        out_shape=(
            jax.ShapeDtypeStruct((count, capacity), low),
            jax.ShapeDtypeStruct((capacity, width), low),
            jax.ShapeDtypeStruct((count, 2), wide),
        ),
        in_specs=[on_chip()] * 4,
        out_specs=(on_chip(),) * 3,
        compiler_params=params(10),
        cost_estimate=cost(4 * count * capacity * width, 8 * count * width),
    )(tokens, column(chosen), column(packing), vectors)


def token_back_kernel(*refs):
    sources, (out_ref, vector_ref), fetched, sems = refs[:6], refs[6:8], refs[8:14], refs[14]
    finish(fetch(sources, fetched, sems))
    tokens, placing, grad_sent, grad_hidden, grad_logit, vectors = fetched
    grad_first = dot(placing[...], grad_sent[...]) + grad_logit[...] * vectors[2:3]
    center, inverse = normal_parts(tokens[...].astype(wide))
    scaled = center * inverse
    vector_ref[0:1] = jnp.sum(grad_first * scaled, axis=0, keepdims=True)
    vector_ref[1:2] = jnp.sum(grad_first, axis=0, keepdims=True)
    first = (scaled * vectors[0:1] + vectors[1:2]).astype(low).astype(wide)
    vector_ref[2:3] = jnp.sum(grad_logit[...] * first, axis=0, keepdims=True)
    pulled = grad_first * vectors[0:1]
    pulled = (
        pulled
        - jnp.mean(pulled, axis=-1, keepdims=True)
        - scaled * jnp.mean(pulled * scaled, axis=-1, keepdims=True)
    )
    out_ref[...] = (grad_hidden[...] + inverse * pulled).astype(low)


def token_back(tokens, placing, grad_sent, grad_hidden, grad_logit, vectors):
    count, width = tokens.shape
    return pl.pallas_call(
        token_back_kernel,
        out_shape=(
            jax.ShapeDtypeStruct((count, width), low),
            jax.ShapeDtypeStruct((3, width), wide),
        ),
        in_specs=[in_hbm()] * 6,
        out_specs=(on_chip(),) * 2,
        scratch_shapes=fetch_scratch(
            (tokens, placing, grad_sent, grad_hidden, grad_logit, vectors)
        ),
        compiler_params=params(17),
        cost_estimate=cost(2 * count * width * placing.shape[1], 12 * count * width),
    )(tokens, placing, grad_sent, grad_hidden, grad_logit, vectors)


def flip_pairs(flip):
    return [(i, i ^ flip) for i in range(32)]


def all_sum(value):
    value = value + send(value, swap_pairs())
    for one, two in ((2, 4), (8, 16)):
        near = value + send(value, flip_pairs(one))
        far = send(value, flip_pairs(two)) + send(value, flip_pairs(one + two))
        value = near + far
    return value


def exchange(value, n_data):
    capacity, width = value.shape
    moved = lax.all_to_all(
        value.reshape(n_data, capacity // n_data, width), "dp", split_axis=0, concat_axis=0, tiled=True
    )
    return moved.reshape(capacity, width)


def block_shards(
    tokens,
    cotangent,
    selected,
    packing,
    segments,
    blocks,
    left_stat,
    right_stat,
    left_root,
    right_root,
    vectors,
    moment,
):
    model_width = tokens.shape[2]
    token_count = tokens.shape[0] * tokens.shape[1]
    n_data = lax.axis_size("dp")
    capacity = packing.shape[1]
    line, place, core = here()
    own_tokens = tokens.reshape(token_count, model_width)
    above = cotangent.reshape(token_count, model_width)
    segment = segments[0]

    every = columns_by_core(jnp.transpose(blocks, (1, 0, 2)).astype(low))
    placing, packed, gates = pack_tokens(
        own_tokens, selected.reshape(token_count), packing[0], vectors
    )
    buffer = exchange(packed, n_data)
    attn_two = send(every[:4], line_pairs(2))
    ffn_got = send(after(every[4:], attn_two), line_pairs(2))
    attn_pair = jnp.stack([every[:4], attn_two])
    attn_got = send(attn_pair, line_pairs(1))
    line_attn = after(jnp.concatenate([attn_pair, attn_got]), packed)
    ffn_two = jnp.stack([every[4:], after(ffn_got, attn_got)])
    near_attn = send(line_attn, plane_pairs(0))
    every_root = roots_by_core(after(left_root, ffn_two), right_root)
    first_attn = after(jnp.stack([line_attn, near_attn]), every_root, buffer)
    far_attn = send(first_attn, plane_pairs(1))
    line_ffn = gather_far(ffn_two)
    near_ffn = send(after(line_ffn, far_attn), plane_pairs(0))
    root_given = lax.optimization_barrier((*roots_given(every_root), buffer, line_ffn))[:4]
    root_parts = [root_given[0]]
    for flip in (1, 2, 3):
        root_parts.append(send(root_given[flip], line_pairs(flip)))
    w_parts = with_other(first_attn, far_attn)
    answer, store = attend(buffer, w_parts, segment)
    first_ffn = jnp.stack([line_ffn, after(near_ffn, answer)])
    left_line, right_line = (jnp.stack([part[:, kind] for part in root_parts]) for kind in range(2))
    returned = exchange(answer, n_data)
    far_ffn = after(send(after(first_ffn, *root_parts[1:]), plane_pairs(1)), returned, right_line, left_line)
    ffn_parts = with_other(first_ffn, far_ffn)

    near_right = send(after(right_line, far_ffn), plane_pairs(0))
    first_right = jnp.stack([right_line, near_right])
    hidden, second_low, active, slope, w_up = token_forward(
        own_tokens, placing, returned, gates, vectors, ffn_parts
    )
    down_theirs = outer_theirs(after(active, near_right), above[None])
    far_right = send(first_right, plane_pairs(1))
    roots = (left_line, send(left_line, swap_pairs()), first_right, far_right)
    w_down = place_weights(ffn_parts, 4, 4)
    down_got = send(down_theirs, swap_pairs())
    down_give, *down_kept = sum_start(
        lambda step: step, active, above[None], after(down_got, w_down)
    )
    down_got = send(down_give, plane_pairs(0))
    mixed, grad_packed, grad_hidden, grad_logit, vector_two, grad_inner = token_backward(
        above,
        hidden,
        active,
        slope,
        placing,
        returned,
        gates,
        vectors,
        w_up,
        after(w_down, down_give),
    )
    grad_answer = exchange(grad_packed, n_data)
    up_theirs = outer_theirs(after(second_low, down_got, far_right)[None], grad_inner)

    down_kept, down_give = add_first(down_got, *down_kept)
    down_got = send(down_give, plane_pairs(1))
    up_got = send(after(up_theirs, grad_answer), swap_pairs())
    attn_theirs, grads, grad_buffer, sides = attend_back(store, segment, grad_answer)
    attn_got = send(after(attn_theirs, down_got), swap_pairs())
    up_give, *up_kept = sum_start(
        lambda step: 0, second_low[None], grad_inner, after(up_got, attn_theirs)
    )
    up_got = send(up_give, plane_pairs(0))
    down_own, down_two, down_give = cut_line((down_kept + down_got.astype(wide))[None])
    down_got = send(down_give, line_pairs(1))
    attn_give, *attn_kept = sum_start(
        lambda step: step // 3, sides, grads, after(attn_got, up_give)
    )
    attn_got = send(attn_give, plane_pairs(0))
    grad_sent = exchange(after(grad_buffer, attn_give), n_data)
    down_own, down_give = add_line(down_own, down_two, down_got)
    down_got = send(down_give, line_pairs(2))
    down_own = (down_own + down_got.astype(wide)).astype(low)
    down_near = send(down_own, plane_pairs(0))
    down_first = jnp.stack([down_own, down_near])
    down_far = send(down_first, plane_pairs(1))
    down_mine = jnp.concatenate([down_first, down_far])
    down_theirs = send(down_mine, swap_pairs())

    up_kept, up_give = add_first(up_got, *up_kept)
    attn_kept, attn_give = add_first(after(attn_got, down_near), *attn_kept)
    pair_got = send(jnp.stack([attn_give, up_give]), plane_pairs(1))
    down_made, down_square = step_chunks(down_mine, down_theirs, roots, 2)
    down_parts = return_chunks(down_made)
    pair_kept = jnp.stack([attn_kept, up_kept]) + pair_got.astype(wide)
    pair_own, pair_two, pair_give = cut_line(pair_kept)
    pair_got = send(pair_give, line_pairs(1))
    grad_tokens, vector_one = token_back(
        own_tokens, placing, grad_sent, grad_hidden, grad_logit, vectors
    )
    pair_own, pair_give = add_line(pair_own, pair_two, pair_got)
    pair_got = send(after(pair_give, vector_one, down_made), line_pairs(2))
    down = jnp.stack(down_parts)
    down_other = send(down, [(i, i ^ 1) for i in range(0, 32, 2)])
    pair_own = (pair_own + pair_got.astype(wide)).astype(low)
    pair_near = send(pair_own, plane_pairs(0))
    pair_first = jnp.stack([pair_own, pair_near])
    pair_far = send(pair_first, plane_pairs(1))
    pair_mine = jnp.concatenate([pair_first, pair_far])
    pair_theirs = send(after(pair_mine, *down_parts[1:]), swap_pairs())
    pair_made, pair_square = step_chunks(pair_mine, pair_theirs, roots, 0)
    pair = jnp.stack(return_chunks(pair_made))
    pair_other = send(pair, swap_pairs())
    squares = jnp.concatenate([jnp.sum(pair_square, axis=2), jnp.sum(down_square, axis=2)])
    lane = lax.broadcasted_iota(jnp.int32, (1, model_width), 1)
    square_row = sum(
        jnp.where(lane == 4 * chunk + line, squares[chunk], 0.0) for chunk in range(3)
    )
    sums = all_sum(jnp.concatenate([vector_one, vector_two, square_row]))
    vector_grad = sums[:5]
    size = model_width * model_width
    scales = block_rate * lax.rsqrt(sums[5, :12] / size + norm_eps)
    grad_own, left_new, right_new, new_blocks = update_blocks(
        pair, pair_other, down, down_other, blocks, left_stat, right_stat, scales
    )
    moment_new = 0.5 * moment + 0.5 * vector_grad
    row_squares = jnp.mean(moment_new * moment_new, axis=1, keepdims=True)
    vector_new = vectors - vector_rate * moment_new * lax.rsqrt(row_squares + norm_eps)
    return (
        mixed.reshape(tokens.shape),
        grad_tokens.reshape(tokens.shape),
        grad_own,
        left_new,
        right_new,
        new_blocks,
        vector_grad,
        moment_new,
        vector_new,
    )


def shards(
    tokens,
    cotangent,
    selected,
    packing,
    segments,
    blocks,
    left_stat,
    right_stat,
    left_root,
    right_root,
    vectors,
    moment,
):
    model_width = tokens.shape[2]
    token_count = tokens.shape[0] * tokens.shape[1]
    n_data = lax.axis_size("dp")
    n_owner = lax.axis_size("own")
    shard_rows = blocks.shape[0]
    own_blocks = blocks.shape[1]
    up_blocks = (own_blocks * n_owner - 4) // 2
    capacity = packing.shape[1]
    per_peer = capacity // n_data
    head_count = model_width // HEAD_DIM
    score_scale = HEAD_DIM ** (-0.5)
    flat_weights = blocks.astype(jnp.bfloat16).reshape(1, shard_rows * own_blocks * model_width)
    gathered = lax.all_gather(flat_weights, ("dp", "own"), axis=0, tiled=True)
    gathered = gathered.reshape(n_data, n_owner, shard_rows, own_blocks, model_width)

    def matrix(number):
        return gathered[:, number // own_blocks, :, number % own_blocks, :].reshape(
            model_width, model_width
        )

    w_query = matrix(0)
    w_key = matrix(1)
    w_value = matrix(2)
    w_out = matrix(3)
    w_up = jnp.concatenate([matrix(4 + position) for position in range(up_blocks)], axis=1)
    w_down = jnp.concatenate(
        [matrix(4 + up_blocks + position) for position in range(up_blocks)], axis=0
    )
    inputs = tokens.reshape(token_count, model_width).astype(jnp.float32)
    chosen = selected.reshape(token_count)
    normed_one, norm_one_back = jax.vjp(layer_norm, inputs, vectors[0], vectors[1])
    first_low = normed_one.astype(jnp.bfloat16)
    first_wide = first_low.astype(jnp.float32)
    gate_values = jax.nn.sigmoid(jnp.dot(first_wide, vectors[2], precision=highest))
    before = jnp.cumsum(chosen) - 1
    slot_index = jnp.where(chosen == 1, packing[0][jnp.clip(before, 0, capacity - 1)], -1)
    placing = (slot_index[None, :] == jnp.arange(capacity, dtype=jnp.int32)[:, None]).astype(
        jnp.bfloat16
    )
    packed = jnp.dot(placing, first_low, preferred_element_type=jnp.float32).astype(jnp.bfloat16)
    buffer = lax.all_to_all(
        packed.reshape(n_data, per_peer, model_width), "dp", split_axis=0, concat_axis=0, tiled=True
    )
    buffer = buffer.reshape(capacity, model_width)

    def project(matrix_in):
        made = jnp.dot(buffer, matrix_in, preferred_element_type=jnp.float32).astype(jnp.bfloat16)
        return made.reshape(capacity, head_count, HEAD_DIM)

    query_rows = project(w_query)
    key_rows = project(w_key)
    value_rows = project(w_value)
    segment = segments[0]
    block_rows = math.gcd(capacity, 512)
    starts = jnp.arange(capacity // block_rows, dtype=jnp.int32) * block_rows

    def masked_scores():
        scores = (
            jnp.einsum("qhd,khd->hqk", query_rows, key_rows, preferred_element_type=jnp.float32)
            * score_scale
        )
        same_segment = segment[:, None] == segment[None, :]
        return (jnp.where(same_segment[None, :, :], scores, -1e30), query_rows)

    def forward_block(first_row):
        scores, unused_block = masked_scores()
        largest = jnp.max(scores, axis=-1, keepdims=True)
        raised = jnp.exp(scores - largest)
        row_total = jnp.sum(raised, axis=-1, keepdims=True)
        shares = (raised / row_total).astype(jnp.bfloat16)
        context_part = jnp.einsum(
            "hqk,khd->qhd", shares, value_rows, preferred_element_type=jnp.float32
        )
        return (context_part.astype(jnp.bfloat16), largest[..., 0] + jnp.log(row_total[..., 0]))

    context_blocks, lse_blocks = lax.map(forward_block, starts)
    context = context_blocks.reshape(capacity, model_width)
    answer = jnp.dot(context, w_out, preferred_element_type=jnp.float32).astype(jnp.bfloat16)
    returned = lax.all_to_all(
        answer.reshape(n_data, per_peer, model_width), "dp", split_axis=0, concat_axis=0, tiled=True
    )
    returned = returned.reshape(capacity, model_width)
    unpacked = jnp.einsum("mt,md->td", placing, returned, preferred_element_type=jnp.float32)
    weighting = jnp.where(chosen == 1, gate_values, 0.0)
    hidden = inputs + weighting[:, None] * unpacked
    normed_two, norm_two_back = jax.vjp(layer_norm, hidden, vectors[3], vectors[4])
    second_low = normed_two.astype(jnp.bfloat16)
    pre_active = jnp.dot(second_low, w_up, preferred_element_type=jnp.float32)
    active_wide, gelu_back = jax.vjp(gelu_exact, pre_active)
    active = active_wide.astype(jnp.bfloat16)
    result = hidden + jnp.dot(active, w_down, preferred_element_type=jnp.float32)
    mixed = result.astype(jnp.bfloat16).reshape(tokens.shape)
    upstream = cotangent.reshape(token_count, model_width)
    grad_down = jnp.einsum("tf,td->fd", active, upstream, preferred_element_type=jnp.float32)
    grad_active = jnp.einsum("td,fd->tf", upstream, w_down, preferred_element_type=jnp.float32)
    grad_inner = gelu_back(grad_active)[0].astype(jnp.bfloat16)
    grad_up = jnp.einsum("td,tf->df", second_low, grad_inner, preferred_element_type=jnp.float32)
    grad_second = jnp.einsum("tf,df->td", grad_inner, w_up, preferred_element_type=jnp.float32)
    grad_hidden_part, grad_gain_two, grad_bias_two = norm_two_back(grad_second)
    grad_hidden = upstream.astype(jnp.float32) + grad_hidden_part
    grad_token_back = (grad_hidden * weighting[:, None]).astype(jnp.bfloat16)
    grad_packed = jnp.dot(placing, grad_token_back, preferred_element_type=jnp.float32).astype(
        jnp.bfloat16
    )
    router_pull = jnp.where(chosen == 1, jnp.sum(grad_hidden * unpacked, axis=-1), 0.0)
    grad_logit = router_pull * gate_values * (1.0 - gate_values)
    grad_answer = lax.all_to_all(
        grad_packed.reshape(n_data, per_peer, model_width),
        "dp",
        split_axis=0,
        concat_axis=0,
        tiled=True,
    )
    grad_answer = grad_answer.reshape(capacity, model_width)
    grad_out = jnp.einsum("md,me->de", context, grad_answer, preferred_element_type=jnp.float32)
    grad_context = jnp.einsum("me,de->md", grad_answer, w_out, preferred_element_type=jnp.float32)
    grad_context = grad_context.astype(jnp.bfloat16).reshape(capacity, head_count, HEAD_DIM)

    def backward_block(running, item_pair):
        first_row, lse_block = item_pair
        scores, query_block = masked_scores()
        shares_wide = jnp.exp(scores - lse_block[..., None])
        grad_shares = jnp.einsum(
            "qhd,khd->hqk", grad_context, value_rows, preferred_element_type=jnp.float32
        )
        inner_sum = jnp.sum(shares_wide * grad_shares, axis=-1, keepdims=True)
        grad_scores = (shares_wide * (grad_shares - inner_sum)).astype(jnp.bfloat16)
        grad_query_block = (
            jnp.einsum("hqk,khd->qhd", grad_scores, key_rows, preferred_element_type=jnp.float32)
            * score_scale
        )
        key_sum = (
            running[0]
            + jnp.einsum(
                "hqk,qhd->khd", grad_scores, query_block, preferred_element_type=jnp.float32
            )
            * score_scale
        )
        value_sum = running[1] + jnp.einsum(
            "hqk,qhd->khd",
            shares_wide.astype(jnp.bfloat16),
            grad_context,
            preferred_element_type=jnp.float32,
        )
        return ((key_sum, value_sum), grad_query_block)

    zeros_init = jnp.zeros((capacity, head_count, HEAD_DIM), jnp.float32)
    (key_total, value_total), query_grads = lax.scan(
        backward_block, (zeros_init, zeros_init), (starts, lse_blocks)
    )
    grad_query = query_grads.reshape(capacity, model_width).astype(jnp.bfloat16)
    grad_key = key_total.reshape(capacity, model_width).astype(jnp.bfloat16)
    grad_value = value_total.reshape(capacity, model_width).astype(jnp.bfloat16)
    grad_w_query = jnp.einsum("md,me->de", buffer, grad_query, preferred_element_type=jnp.float32)
    grad_w_key = jnp.einsum("md,me->de", buffer, grad_key, preferred_element_type=jnp.float32)
    grad_w_value = jnp.einsum("md,me->de", buffer, grad_value, preferred_element_type=jnp.float32)
    grad_buffer = jnp.einsum("me,de->md", grad_query, w_query, preferred_element_type=jnp.float32)
    grad_buffer = grad_buffer + jnp.einsum(
        "me,de->md", grad_key, w_key, preferred_element_type=jnp.float32
    )
    grad_buffer = grad_buffer + jnp.einsum(
        "me,de->md", grad_value, w_value, preferred_element_type=jnp.float32
    )
    grad_buffer = grad_buffer.astype(jnp.bfloat16)
    grad_sent = lax.all_to_all(
        grad_buffer.reshape(n_data, per_peer, model_width),
        "dp",
        split_axis=0,
        concat_axis=0,
        tiled=True,
    )
    grad_sent = grad_sent.reshape(capacity, model_width)
    grad_first = jnp.einsum("mt,md->td", placing, grad_sent, preferred_element_type=jnp.float32)
    grad_first = grad_first + grad_logit[:, None] * vectors[2][None, :]
    grad_router = jnp.sum(grad_logit[:, None] * first_wide, axis=0)
    grad_input_part, grad_gain_one, grad_bias_one = norm_one_back(grad_first)
    grad_tokens = (grad_hidden + grad_input_part).astype(jnp.bfloat16).reshape(tokens.shape)
    pieces = [grad_w_query, grad_w_key, grad_w_value, grad_out]
    pieces = pieces + [
        grad_up[:, position * model_width : (position + 1) * model_width]
        for position in range(up_blocks)
    ]
    pieces = pieces + [
        grad_down[position * model_width : (position + 1) * model_width, :]
        for position in range(up_blocks)
    ]
    local_terms = jnp.stack(pieces, axis=1)
    vector_terms = jnp.stack(
        [grad_gain_one, grad_bias_one, grad_router, grad_gain_two, grad_bias_two]
    )
    partial_value = lax.psum_scatter(local_terms, "dp", scatter_dimension=0, tiled=True)
    grad_own = lax.psum_scatter(
        partial_value.astype(jnp.bfloat16), "own", scatter_dimension=1, tiled=True
    ).astype(jnp.float32)
    vector_grad = lax.psum(vector_terms, ("dp", "own"))
    full_grad = lax.all_gather(grad_own.astype(jnp.bfloat16), "dp", axis=0, tiled=True).astype(
        grad_own.dtype
    )
    row_start = lax.axis_index("dp") * shard_rows
    left_new = 0.5 * left_stat + 0.5 * jnp.einsum(
        "rbk,nbk->rbn", grad_own, full_grad, precision=highest
    )
    column_part = lax.dynamic_slice_in_dim(full_grad, row_start, shard_rows, 2)
    right_new = 0.5 * right_stat + 0.5 * jnp.einsum(
        "nbr,nbk->rbk", column_part, full_grad, precision=highest
    )
    lefted = jnp.einsum("rbn,nbk->rbk", left_root, full_grad, precision=highest)
    precond = jnp.zeros_like(grad_own) + jnp.einsum(
        "rbn,nbk->rbk",
        lefted,
        lax.all_gather(right_root.astype(jnp.bfloat16), "dp", axis=0, tiled=True).astype(
            jnp.float32
        ),
        precision=highest,
    )
    square_sums = lax.psum(jnp.sum(precond * precond, axis=(0, 2)), "dp")
    step_scale = lax.rsqrt(square_sums / (model_width * model_width) + norm_eps)
    new_blocks = blocks - block_rate * precond * step_scale[None, :, None]
    moment_new = 0.5 * moment + 0.5 * vector_grad
    row_squares = jnp.mean(moment_new * moment_new, axis=1, keepdims=True)
    vector_new = vectors - vector_rate * moment_new * lax.rsqrt(row_squares + norm_eps)
    return (
        mixed,
        grad_tokens,
        grad_own,
        left_new,
        right_new,
        new_blocks,
        vector_grad,
        moment_new,
        vector_new,
    )


def solution(mesh):
    placed = (
        P(("dp", "own"), None, None),
        P(("dp", "own"), None, None),
        P(("dp", "own"), None),
        P(("dp", "own"), None),
        P(("dp", "own"), None),
        P("dp", "own", None),
        P("dp", "own", None),
        P("dp", "own", None),
        P("dp", "own", None),
        P("dp", "own", None),
        P(),
        P(),
    )
    small = mesh.shape["dp"] == 16 and mesh.shape["own"] == 2
    return jax.shard_map(
        block_shards if small else shards,
        mesh=mesh,
        in_specs=placed,
        out_specs=(
            P(("dp", "own"), None, None),
            P(("dp", "own"), None, None),
            P("dp", "own", None),
            P("dp", "own", None),
            P("dp", "own", None),
            P("dp", "own", None),
            P(),
            P(),
            P(),
        ),
        check_vma=False,
    )
```

```python
import functools
import math

import jax
import jax.numpy as jnp
from jax import lax
from jax.experimental import pallas as pl
from jax.experimental.pallas import tpu as pltpu
from jax.sharding import PartitionSpec as P

HEAD_DIM = 64


norm_eps = 1e-06
block_rate = 0.03
vector_rate = 0.04
highest = lax.Precision.HIGHEST


def layer_norm(values, norm_gain, norm_bias):
    center = values - jnp.mean(values, axis=-1, keepdims=True)
    spread = jnp.mean(center * center, axis=-1, keepdims=True)
    return center * lax.rsqrt(spread + norm_eps) * norm_gain + norm_bias


def gelu_exact(values):
    return jax.nn.gelu(values, approximate=False)


BOTH = ("dp", "own")
low = jnp.bfloat16
wide = jnp.float32
MIB = 2**20


def swap_pairs():
    return [(i, i ^ 1) for i in range(32)]


def plane_pairs(step):
    pairs = []
    for i in range(32):
        place, core = i // 2, i % 2
        flip = (1, 2)[step ^ core]
        pairs.append((i, (place ^ flip) * 2 + core))
    return pairs


def line_pairs(flip):
    return [(i, i ^ (8 * flip)) for i in range(32)]


def send(value, pairs):
    return lax.ppermute(value, BOTH, pairs)


def after(value, *others):
    return lax.optimization_barrier((value,) + others)[0]


def pick(value, index, axis):
    return lax.dynamic_index_in_dim(value, index, axis, keepdims=False)


def first_core():
    return lax.axis_index("own") == 0


def halves(value):
    middle = value.shape[-1] // 2
    lower, upper = value[..., :middle], value[..., middle:]
    return jnp.where(first_core(), lower, upper), jnp.where(first_core(), upper, lower)


def in_core_order(mine, theirs, axis):
    return jnp.where(
        first_core(),
        jnp.concatenate([mine, theirs], axis=axis),
        jnp.concatenate([theirs, mine], axis=axis),
    )


LINE_FLIPS = (0, 2, 1, 3)


def flipped(index, flip):
    return jnp.bitwise_xor(index, flip)


def spots(place, half):
    first, second = half + 1, 2 - half
    return [
        place,
        flipped(place, first),
        flipped(place, second),
        flipped(place, 3),
    ]


def here():
    device = lax.axis_index("dp")
    return device // 4, device % 4, lax.axis_index("own")


def dot(left, right, left_axis=1, right_axis=0):
    return lax.dot_general(
        left, right, (((left_axis,), (right_axis,)), ((), ())), preferred_element_type=wide
    )


def on_chip():
    return pl.BlockSpec(memory_space=pltpu.VMEM)


def whole(value):
    return pl.BlockSpec(value.shape, lambda *steps: (0,) * value.ndim)


def in_hbm():
    return pl.BlockSpec(memory_space=pltpu.HBM)


def fetch_scratch(values):
    return [pltpu.VMEM(value.shape, value.dtype) for value in values] + [
        pltpu.SemaphoreType.DMA((len(values),))
    ]


def fetch(sources, targets, sems):
    copies = [
        pltpu.make_async_copy(source, target, sems.at[number])
        for number, (source, target) in enumerate(zip(sources, targets))
    ]
    for copy in copies:
        copy.start()
    return copies


def finish(copies):
    for copy in copies:
        copy.wait()


def params(limit):
    return pltpu.CompilerParams(vmem_limit_bytes=limit * MIB)


def cost(flops, moved):
    return pl.CostEstimate(flops=flops, bytes_accessed=moved, transcendentals=0)


def place_block(parts, block, target):
    line, place, core = here()
    rows, columns = parts[0].shape[3:]
    for other in range(2):
        half = core if other == 0 else 1 - core
        column_slice = pl.ds(pl.multiple_of(half * columns, columns), columns)
        for number, spot in enumerate(spots(place, half)):
            for index, flip in enumerate(LINE_FLIPS):
                start = (flipped(line, flip) * 4 + spot) * rows
                row_slice = pl.ds(pl.multiple_of(start, rows), rows)
                piece = parts[2 * other + number // 2][number % 2, index, block]
                target[row_slice, column_slice] = piece


def weight_kernel(first_block, one, two, three, four, out_ref):
    for block in range(out_ref.shape[0]):
        place_block((one, two, three, four), first_block + block, out_ref.at[block])


def place_weights(parts, first_block, blocks):
    rows, columns = parts[0].shape[3:]
    full = rows * 16
    return pl.pallas_call(
        functools.partial(weight_kernel, first_block),
        out_shape=jax.ShapeDtypeStruct((blocks, full, 2 * columns), low),
        in_specs=[on_chip()] * 4,
        out_specs=on_chip(),
        compiler_params=params(10),
        cost_estimate=cost(0, 8 * blocks * full * columns),
    )(*parts)


def columns_by_core(value):
    keep, give = halves(value)
    return in_core_order(keep, send(give, swap_pairs()), 0)


def gather_far(pair):
    return jnp.concatenate([pair, send(pair, line_pairs(1))])


def with_other(first, far):
    return [first, far, send(first, swap_pairs()), send(far, swap_pairs())]


def roots_by_core(left_root, right_root):
    both = [jnp.transpose(root, (1, 0, 2)).astype(low) for root in (left_root, right_root)]
    every = columns_by_core(jnp.stack(both, axis=1))
    return every.reshape((3, 4) + every.shape[1:])


def roots_given(every):
    line, place, core = here()
    return [pick(every, flipped(line, flip), 1) for flip in range(4)]


def sum_kernel(left_of, left, right, got, give_ref, kept_ref, passed_ref, total):
    line, place, core = here()
    step = pl.program_id(0)
    columns = got.shape[2]
    rows = kept_ref.shape[2]
    part = pl.ds(pl.multiple_of(core * columns, columns), columns)
    right_step = step if right.shape[0] > 1 else 0
    made = dot(left[left_of(step)], right[right_step, :, part], 0, 0)
    total[...] = made + got[step].astype(wide)
    own, first, second, both = spots(place, core)
    for row_line in range(4):

        def piece(spot):
            return total[pl.ds(pl.multiple_of((row_line * 4 + spot) * rows, rows), rows), :]

        give_ref[0, step, row_line] = piece(first).astype(low)
        give_ref[1, step, row_line] = piece(both).astype(low)
        kept_ref[step, row_line] = piece(own).astype(low)
        passed_ref[step, row_line] = piece(second).astype(low)


def sum_start(left_of, left, right, got):
    count, width = left.shape[1:]
    blocks, full, columns = got.shape
    shape = (blocks, 4, full // 16, columns)
    return pl.pallas_call(
        functools.partial(sum_kernel, left_of),
        grid=(blocks,),
        out_shape=(
            jax.ShapeDtypeStruct((2,) + shape, low),
            jax.ShapeDtypeStruct(shape, low),
            jax.ShapeDtypeStruct(shape, low),
        ),
        in_specs=[on_chip()] * 3,
        out_specs=(on_chip(),) * 3,
        scratch_shapes=[pltpu.VMEM((full, columns), wide)],
        compiler_params=params(12),
        cost_estimate=cost(blocks * count * width * width, 5 * blocks * width * width),
    )(left, right, got)


def add_first(got, kept, passed):
    kept = kept.astype(wide) + got[0].astype(wide)
    return kept, (passed.astype(wide) + got[1].astype(wide)).astype(low)


def cut_line(kept):
    line, place, core = here()
    given = jnp.stack([pick(kept, flipped(line, flip), 1) for flip in (1, 3)]).astype(low)
    return pick(kept, line, 1), pick(kept, flipped(line, 2), 1), given


def add_line(own, two, got):
    return own + got[0].astype(wide), (two + got[1].astype(wide)).astype(low)


def step_kernel(
    number,
    mine,
    theirs,
    left_mine_from,
    left_theirs_from,
    right_first_from,
    right_far_from,
    out_ref,
    square_ref,
    grad_ref,
    rows_ref,
    left_ref,
    right_ref,
    cross_ref,
    left_mine,
    left_theirs,
    right_first,
    right_far,
    sems,
):
    chunk = number + pl.program_id(0)
    copies = fetch(
        [
            left_mine_from.at[:, chunk],
            left_theirs_from.at[:, chunk],
            right_first_from.at[:, :, chunk],
            right_far_from.at[:, :, chunk],
        ],
        [left_mine, left_theirs, right_first, right_far],
        sems,
    )
    line, place, core = here()
    rows, columns = mine.shape[3:]

    def rows_of(row_line, spot):
        return pl.ds(pl.multiple_of((row_line * 4 + spot) * rows, rows), rows)

    def column_half(half):
        return pl.ds(pl.multiple_of(half * columns, columns), columns)

    for half, group in ((core, mine), (1 - core, theirs)):
        for number, spot in enumerate(spots(place, half)):
            for step in range(4):
                grad_ref[rows_of(step, spot), column_half(half)] = group[number, 0, step]
    finish(copies)
    for half, left in ((core, left_mine), (1 - core, left_theirs)):
        for flip in range(4):
            target = pl.ds(pl.multiple_of(flipped(line, flip) * rows, rows), rows)
            left_ref[target, column_half(half)] = left[flip]
    for number, spot in enumerate(spots(place, core)):
        source = right_far if number > 1 else right_first
        for flip in range(4):
            right_ref[rows_of(flipped(line, flip), spot), :] = source[number % 2, flip]
    for row_line in range(4):
        rows_ref[row_line * rows : (row_line + 1) * rows, :] = grad_ref[rows_of(row_line, place), :]
    left = dot(rows_ref[...], grad_ref[column_half(core), :], 1, 1)
    cross_ref[...] = dot(grad_ref[...], grad_ref[:, column_half(core)], 0, 0)
    lefted = dot(left_ref[...], grad_ref[...]).astype(low)
    stepped = dot(lefted, right_ref[...])
    squares = jnp.sum(jnp.sum(stepped * stepped, axis=0, keepdims=True), axis=1, keepdims=True)
    lane = lax.broadcasted_iota(jnp.int32, (1, 2 * columns), 1)
    square_ref[0] = jnp.where(lane == 4 * chunk + line, squares, 0.0)
    for row_line in range(4):
        part = slice(row_line * rows, (row_line + 1) * rows)
        out_ref[0, row_line, 0] = mine[0, 0, row_line]
        out_ref[0, row_line, 1] = left[part].astype(low)
        out_ref[0, row_line, 2] = cross_ref[rows_of(row_line, place), :].astype(low)
        out_ref[0, row_line, 3] = stepped[part].astype(low)


def step_chunks(mine, theirs, roots, number):
    chunks, lines, rows, columns = mine.shape[1:]
    full = rows * 16
    grad_spec = pl.BlockSpec((4, 1, lines, rows, columns), lambda step: (0, step, 0, 0, 0))
    return pl.pallas_call(
        functools.partial(step_kernel, number),
        grid=(chunks,),
        out_shape=(
            jax.ShapeDtypeStruct((chunks, lines, 4, rows, columns), low),
            jax.ShapeDtypeStruct((chunks, 1, 2 * columns), wide),
        ),
        in_specs=[grad_spec] * 2 + [in_hbm()] * 4,
        out_specs=(
            pl.BlockSpec((1, lines, 4, rows, columns), lambda step: (step, 0, 0, 0, 0)),
            pl.BlockSpec((1, 1, 2 * columns), lambda step: (step, 0, 0)),
        ),
        scratch_shapes=[
            pltpu.VMEM((full, columns * 2), low),
            pltpu.VMEM((lines * rows, columns * 2), low),
            pltpu.VMEM((lines * rows, columns * 2), low),
            pltpu.VMEM((full, columns), low),
            pltpu.VMEM((full, columns), wide),
            pltpu.VMEM((lines, rows, columns), low),
            pltpu.VMEM((lines, rows, columns), low),
            pltpu.VMEM((2, lines, rows, columns), low),
            pltpu.VMEM((2, lines, rows, columns), low),
            pltpu.SemaphoreType.DMA((4,)),
        ],
        compiler_params=params(15),
        cost_estimate=cost(3 * chunks * full**3, 16 * chunks * full * full),
    )(mine, theirs, *roots)


def return_chunks(made):
    line, place, core = here()
    parts = [pick(made, line, 1)]
    for flip in (1, 2, 3):
        parts.append(send(pick(made, flipped(line, flip), 1), line_pairs(flip)))
    return parts


def last_kernel(
    pair, pair_other, down, down_other, blocks, left_stat, right_stat, scales, *outs
):
    grad_out, left_out, right_out, block_out = outs
    line, place, core = here()
    columns = pair.shape[4]

    def update(number, which, mine, theirs):
        for (source, index), half in ((mine, which), (theirs, 1 - which)):
            part = slice(half * columns, (half + 1) * columns)
            pieces = [source[index + (kind,)].astype(wide) for kind in range(4)]
            grad_out[number, :, part] = pieces[0]
            left_out[number, :, part] = 0.5 * left_stat[number, :, part] + 0.5 * pieces[1]
            right_out[number, :, part] = 0.5 * right_stat[number, :, part] + 0.5 * pieces[2]
            step = pieces[3] * scales[6 * which + number]
            block_out[number, :, part] = blocks[number, :, part] - step

    @pl.when(core == 0)
    def first():
        for number in range(6):
            index = (flipped(line, number % 4), number // 4)
            update(number, 0, (pair, index), (pair_other, index))

    @pl.when(core == 1)
    def second():
        for number in range(6):
            source, other = (pair, pair_other) if number < 2 else (down, down_other)
            index = (flipped(line, (number + 2) % 4), 1 if number < 2 else 0)
            update(number, 1, (source, index), (other, index))


def update_blocks(pair, pair_other, down, down_other, blocks, left_stat, right_stat, scales):
    turned = [jnp.transpose(value, (1, 0, 2)) for value in (blocks, left_stat, right_stat)]
    shape = jax.ShapeDtypeStruct(turned[0].shape, wide)
    outs = pl.pallas_call(
        last_kernel,
        out_shape=(shape,) * 4,
        in_specs=[on_chip()] * 7 + [pl.BlockSpec(memory_space=pltpu.SMEM)],
        out_specs=(on_chip(),) * 4,
        compiler_params=params(10),
        cost_estimate=cost(0, 32 * shape.size),
    )(pair, pair_other, down, down_other, *turned, scales)
    return [jnp.transpose(value, (1, 0, 2)) for value in outs]


def head_masks():
    lane = lax.broadcasted_iota(jnp.int32, (1, 2 * HEAD_DIM), 1)
    return [(lane < HEAD_DIM).astype(wide).astype(low), (lane >= HEAD_DIM).astype(wide).astype(low)]


def head_shares(query, key, same):
    scores = dot(query, key, 1, 1) * HEAD_DIM ** (-0.5)
    scores = jnp.where(same, scores, -1e30)
    raised = jnp.exp(scores - jnp.max(scores, axis=-1, keepdims=True))
    return raised / jnp.sum(raised, axis=-1, keepdims=True)


STORE_ROWS = 32768


def store_views(store, rows, width):
    weights = [store.at[pl.ds(block * width, width)] for block in range(4)]
    made = [store.at[pl.ds(4 * width + kind * rows, rows)] for kind in range(3)]
    sides = [store.at[pl.ds(4 * width + (3 + side) * rows, rows)] for side in range(2)]
    return weights, made, sides


def attend_kernel(
    buffer, one, two, three, four, seg_column, seg_row, answer_ref, store, weights, made, sides, sems
):
    rows, width = buffer.shape
    weights_out, made_out, sides_out = store_views(store, rows, width)
    for block in range(4):
        place_block((one, two, three, four), block, weights.at[block])
    copies = fetch([weights.at[block] for block in range(4)], weights_out, sems)
    same = seg_column[...] == seg_row[...]
    for kind in range(3):
        made[kind] = dot(buffer[...], weights[kind]).astype(low)
    copies += fetch([made.at[kind] for kind in range(3)], made_out, sems.at[pl.ds(4, 3)])
    pair_width = 2 * HEAD_DIM
    for pair in range(width // pair_width):
        part = slice(pair * pair_width, (pair + 1) * pair_width)
        query, key, value = (made[kind, :, part] for kind in range(3))
        context = None
        for mask in head_masks():
            shares = head_shares(query, key * mask, same).astype(low)
            term = dot(shares, value * mask)
            context = term if context is None else context + term
        sides[1, :, part] = context.astype(low)
    sides[0] = buffer[...]
    copies += fetch([sides.at[side] for side in range(2)], sides_out, sems.at[pl.ds(7, 2)])
    answer_ref[...] = dot(sides[1], weights[3]).astype(low)
    finish(copies)


def attend_scratch(rows, width):
    return [
        pltpu.VMEM((4, width, width), low),
        pltpu.VMEM((3, rows, width), low),
        pltpu.VMEM((2, rows, width), low),
        pltpu.SemaphoreType.DMA((9,)),
    ]


def attend(buffer, parts, segment):
    rows, width = buffer.shape
    return pl.pallas_call(
        attend_kernel,
        out_shape=(
            jax.ShapeDtypeStruct((rows, width), low),
            jax.ShapeDtypeStruct((STORE_ROWS, width), low),
        ),
        in_specs=[on_chip()] * 7,
        out_specs=(on_chip(), in_hbm()),
        scratch_shapes=attend_scratch(rows, width),
        compiler_params=params(20),
        cost_estimate=cost(12 * rows * width * width, 12 * width * width),
    )(buffer, *parts, segment[:, None], segment[None, :])


def attend_back_kernel(
    store,
    seg_column,
    seg_row,
    grad_answer,
    theirs_ref,
    grads_ref,
    grad_buffer_ref,
    sides,
    grad_context_ref,
    weights,
    made,
    sems,
):
    rows, width = grad_answer.shape
    weights_from, made_from, sides_from = store_views(store, rows, width)
    out_copy, *copies = fetch(
        [weights_from[3]] + made_from + sides_from + weights_from[:3],
        [weights.at[3]]
        + [made.at[kind] for kind in range(3)]
        + [sides.at[side] for side in range(2)]
        + [weights.at[block] for block in range(3)],
        sems,
    )
    same = seg_column[...] == seg_row[...]
    core = lax.axis_index("own")
    out_copy.wait()
    grad_context_ref[...] = dot(grad_answer[...], weights[3], 1, 1).astype(low)
    finish(copies[:3])
    grads_ref[3] = grad_answer[...]
    pair_width = 2 * HEAD_DIM
    for pair in range(width // pair_width):
        part = slice(pair * pair_width, (pair + 1) * pair_width)
        query, key, value = (made[kind, :, part] for kind in range(3))
        above = grad_context_ref[:, part]
        sums = [None] * 3
        for mask in head_masks():
            key_head = key * mask
            shares = head_shares(query, key_head, same)
            grad_shares = dot(above, value * mask, 1, 1)
            inner = jnp.sum(shares * grad_shares, axis=-1, keepdims=True)
            grad_scores = (shares * (grad_shares - inner)).astype(low)
            terms = (
                dot(grad_scores, key_head),
                dot(grad_scores, query * mask, 0, 0),
                dot(shares.astype(low), above * mask, 0, 0),
            )
            sums = [
                term if total is None else total + term for term, total in zip(terms, sums)
            ]
        for kind, factor in enumerate((HEAD_DIM ** (-0.5), HEAD_DIM ** (-0.5), 1.0)):
            grads_ref[kind, :, part] = (sums[kind] * factor).astype(low)
    finish(copies[3:5])
    columns = theirs_ref.shape[2]
    part = pl.ds(pl.multiple_of((1 - core) * columns, columns), columns)
    for kind in range(4):
        theirs_ref[kind] = dot(sides[kind // 3], grads_ref[kind, :, part], 0, 0).astype(low)
    finish(copies[5:])
    total = dot(grads_ref[0], weights[0], 1, 1)
    total = total + dot(grads_ref[1], weights[1], 1, 1)
    total = total + dot(grads_ref[2], weights[2], 1, 1)
    grad_buffer_ref[...] = total.astype(low)


def attend_back(store, segment, grad_answer):
    rows, width = grad_answer.shape
    weights, made, sides, sems = attend_scratch(rows, width)
    return pl.pallas_call(
        attend_back_kernel,
        out_shape=(
            jax.ShapeDtypeStruct((4, width, width // 2), low),
            jax.ShapeDtypeStruct((4, rows, width), low),
            jax.ShapeDtypeStruct((rows, width), low),
            jax.ShapeDtypeStruct((2, rows, width), low),
        ),
        in_specs=[in_hbm()] + [on_chip()] * 3,
        out_specs=(on_chip(),) * 4,
        scratch_shapes=[pltpu.VMEM((rows, width), low), weights, made, sems],
        compiler_params=params(18),
        cost_estimate=cost(20 * rows * width * width, 16 * width * width),
    )(store, segment[:, None], segment[None, :], grad_answer)


def normal_parts(values):
    center = values - jnp.mean(values, axis=-1, keepdims=True)
    spread = jnp.mean(center * center, axis=-1, keepdims=True)
    return center, lax.rsqrt(spread + norm_eps)


def forward_kernel(*refs):
    tokens, placing, returned, gates, vectors = refs[:5]
    parts = refs[5:9]
    hidden_ref, second_ref, active_ref, slope_ref, w_up = refs[9:14]
    step = pl.program_id(0)

    @pl.when(step == 0)
    def prepare():
        values = tokens[...].astype(wide) + gates[:, 0:1] * dot(placing[...], returned[...])
        hidden_ref[...] = values
        center, inverse = normal_parts(values)
        second_ref[...] = (center * inverse * vectors[3:4] + vectors[4:5]).astype(low)

    place_block(parts, step, w_up.at[step])
    before = dot(second_ref[...], w_up[step])
    share = 0.5 + 0.5 * lax.erf(before * (0.5**0.5))
    density = jnp.exp(before * before * -0.5) * (0.5 / math.pi) ** 0.5
    active_ref[step] = (before * share).astype(low)
    slope_ref[step] = (share + before * density).astype(low)


def token_forward(tokens, placing, returned, gates, vectors, parts):
    count, width = tokens.shape
    blocks = parts[0].shape[2] // 2
    by_block = jax.ShapeDtypeStruct((blocks, count, width), low)
    fetched = (tokens, placing, returned, gates, vectors)
    return pl.pallas_call(
        forward_kernel,
        grid=(blocks,),
        out_shape=(
            jax.ShapeDtypeStruct((count, width), wide),
            jax.ShapeDtypeStruct((count, width), low),
            by_block,
            by_block,
            jax.ShapeDtypeStruct((blocks, width, width), low),
        ),
        in_specs=[whole(value) for value in fetched] + [on_chip()] * 4,
        out_specs=(on_chip(),) * 5,
        compiler_params=params(18),
        cost_estimate=cost(8 * blocks * count * width * width, 8 * blocks * width * width),
    )(*fetched, *parts)


def backward_kernel(*refs):
    above, placing, returned, gates, vectors = refs[:5]
    hidden, active, slope, w_up, w_down = refs[5:10]
    mixed_ref, packed_ref, grad_hidden_ref, logit_ref, vector_ref, inner_ref = refs[10:16]
    result, grad_second = refs[16:]
    step = pl.program_id(0)

    @pl.when(step == 0)
    def prepare():
        result[...] = hidden[...]
        grad_second[...] = jnp.zeros_like(grad_second)

    grad_active = dot(above[...], w_down[step], 1, 1)
    grad_inner = (grad_active * slope[step].astype(wide)).astype(low)
    inner_ref[step] = grad_inner
    result[...] += dot(active[step], w_down[step])
    grad_second[...] += dot(grad_inner, w_up[step], 1, 1)

    @pl.when(step == pl.num_programs(0) - 1)
    def complete():
        mixed_ref[...] = result[...].astype(low)
        center, inverse = normal_parts(hidden[...])
        scaled = center * inverse
        grads = grad_second[...]
        vector_ref[0:1] = jnp.sum(grads * scaled, axis=0, keepdims=True)
        vector_ref[1:2] = jnp.sum(grads, axis=0, keepdims=True)
        pulled = grads * vectors[3:4]
        pulled = (
            pulled
            - jnp.mean(pulled, axis=-1, keepdims=True)
            - scaled * jnp.mean(pulled * scaled, axis=-1, keepdims=True)
        )
        grad_hidden = above[...].astype(wide) + inverse * pulled
        grad_hidden_ref[...] = grad_hidden
        weighted = (grad_hidden * gates[:, 0:1]).astype(low)
        packed_ref[...] = dot(placing[...], weighted, 0, 0).astype(low)
        unpacked = dot(placing[...], returned[...])
        logit_ref[...] = gates[:, 1:2] * jnp.sum(grad_hidden * unpacked, axis=-1, keepdims=True)


def token_backward(above, hidden, active, slope, placing, returned, gates, vectors, w_up, w_down):
    count, width = above.shape
    slots = placing.shape[1]
    blocks = w_up.shape[0]
    fetched = (above, placing, returned, gates, vectors)
    return pl.pallas_call(
        backward_kernel,
        grid=(blocks,),
        out_shape=(
            jax.ShapeDtypeStruct((count, width), low),
            jax.ShapeDtypeStruct((slots, width), low),
            jax.ShapeDtypeStruct((count, width), wide),
            jax.ShapeDtypeStruct((count, 1), wide),
            jax.ShapeDtypeStruct((2, width), wide),
            jax.ShapeDtypeStruct((blocks, count, width), low),
        ),
        in_specs=[whole(value) for value in fetched] + [on_chip()] * 5,
        out_specs=(on_chip(),) * 6,
        scratch_shapes=[
            pltpu.VMEM((count, width), wide),
            pltpu.VMEM((count, width), wide),
        ],
        compiler_params=params(30),
        cost_estimate=cost(8 * blocks * count * width * width, 8 * blocks * width * width),
    )(*fetched, hidden, active, slope, w_up, w_down)


def outer_kernel(left, right, theirs_ref):
    core = lax.axis_index("own")
    step = pl.program_id(0)
    columns = theirs_ref.shape[2]
    left_step = step if left.shape[0] > 1 else 0
    right_step = step if right.shape[0] > 1 else 0
    part = pl.ds(pl.multiple_of((1 - core) * columns, columns), columns)
    theirs_ref[step] = dot(left[left_step], right[right_step, :, part], 0, 0).astype(low)


def outer_theirs(left, right):
    count, width = left.shape[1:]
    blocks = max(left.shape[0], right.shape[0])
    return pl.pallas_call(
        outer_kernel,
        grid=(blocks,),
        out_shape=jax.ShapeDtypeStruct((blocks, width, width // 2), low),
        in_specs=[on_chip()] * 2,
        out_specs=on_chip(),
        compiler_params=params(8),
        cost_estimate=cost(blocks * count * width * width, 3 * blocks * width * width),
    )(left, right)


def column(values):
    return values[:, None]


def pack_kernel(
    tokens, chosen, packing, vectors, placing_ref, packed_ref, gates_ref
):
    count = tokens.shape[0]
    capacity = packing.shape[0]
    center, inverse = normal_parts(tokens[...].astype(wide))
    first = (center * inverse * vectors[0:1] + vectors[1:2]).astype(low)
    gate = jax.nn.sigmoid(jnp.sum(first.astype(wide) * vectors[2:3], axis=-1, keepdims=True))
    weighting = jnp.where(chosen[...] == 1, gate, 0.0)
    gates_ref[:, 0:1] = weighting
    gates_ref[:, 1:2] = weighting * (1.0 - gate)
    above = lax.broadcasted_iota(jnp.int32, (count, count), 0)
    below = lax.broadcasted_iota(jnp.int32, (count, count), 1)
    earlier = (below <= above).astype(wide).astype(low)
    flags = jnp.broadcast_to(chosen[...].astype(wide), (count, capacity))
    rank = dot(earlier, flags.astype(low))
    place_of = lax.broadcasted_iota(jnp.int32, (count, capacity), 1).astype(wide) + 1.0
    ranked = jnp.where(rank == place_of, flags, 0.0).astype(low)
    slots = lax.broadcasted_iota(jnp.int32, (capacity, capacity), 1)
    slot_of = (packing[...] == slots).astype(wide).astype(low)
    placing = dot(ranked, slot_of).astype(low)
    placing_ref[...] = placing
    packed_ref[...] = dot(placing, first, 0, 0).astype(low)


def pack_tokens(tokens, chosen, packing, vectors):
    count, width = tokens.shape
    capacity = packing.shape[0]
    return pl.pallas_call(
        pack_kernel,
        out_shape=(
            jax.ShapeDtypeStruct((count, capacity), low),
            jax.ShapeDtypeStruct((capacity, width), low),
            jax.ShapeDtypeStruct((count, 2), wide),
        ),
        in_specs=[on_chip()] * 4,
        out_specs=(on_chip(),) * 3,
        compiler_params=params(10),
        cost_estimate=cost(4 * count * capacity * width, 8 * count * width),
    )(tokens, column(chosen), column(packing), vectors)


def token_back_kernel(*refs):
    sources, (out_ref, vector_ref), fetched, sems = refs[:6], refs[6:8], refs[8:14], refs[14]
    finish(fetch(sources, fetched, sems))
    tokens, placing, grad_sent, grad_hidden, grad_logit, vectors = fetched
    grad_first = dot(placing[...], grad_sent[...]) + grad_logit[...] * vectors[2:3]
    center, inverse = normal_parts(tokens[...].astype(wide))
    scaled = center * inverse
    vector_ref[0:1] = jnp.sum(grad_first * scaled, axis=0, keepdims=True)
    vector_ref[1:2] = jnp.sum(grad_first, axis=0, keepdims=True)
    first = (scaled * vectors[0:1] + vectors[1:2]).astype(low).astype(wide)
    vector_ref[2:3] = jnp.sum(grad_logit[...] * first, axis=0, keepdims=True)
    pulled = grad_first * vectors[0:1]
    pulled = (
        pulled
        - jnp.mean(pulled, axis=-1, keepdims=True)
        - scaled * jnp.mean(pulled * scaled, axis=-1, keepdims=True)
    )
    out_ref[...] = (grad_hidden[...] + inverse * pulled).astype(low)


def token_back(tokens, placing, grad_sent, grad_hidden, grad_logit, vectors):
    count, width = tokens.shape
    return pl.pallas_call(
        token_back_kernel,
        out_shape=(
            jax.ShapeDtypeStruct((count, width), low),
            jax.ShapeDtypeStruct((3, width), wide),
        ),
        in_specs=[in_hbm()] * 6,
        out_specs=(on_chip(),) * 2,
        scratch_shapes=fetch_scratch(
            (tokens, placing, grad_sent, grad_hidden, grad_logit, vectors)
        ),
        compiler_params=params(17),
        cost_estimate=cost(2 * count * width * placing.shape[1], 12 * count * width),
    )(tokens, placing, grad_sent, grad_hidden, grad_logit, vectors)


def flip_pairs(flip):
    return [(i, i ^ flip) for i in range(32)]


def all_sum(value):
    value = value + send(value, swap_pairs())
    for one, two in ((2, 4), (8, 16)):
        near = value + send(value, flip_pairs(one))
        far = send(value, flip_pairs(two)) + send(value, flip_pairs(one + two))
        value = near + far
    return value


def exchange(value, n_data):
    capacity, width = value.shape
    moved = lax.all_to_all(
        value.reshape(n_data, capacity // n_data, width), "dp", split_axis=0, concat_axis=0, tiled=True
    )
    return moved.reshape(capacity, width)


def block_shards(
    tokens,
    cotangent,
    selected,
    packing,
    segments,
    blocks,
    left_stat,
    right_stat,
    left_root,
    right_root,
    vectors,
    moment,
):
    model_width = tokens.shape[2]
    token_count = tokens.shape[0] * tokens.shape[1]
    n_data = lax.axis_size("dp")
    capacity = packing.shape[1]
    line, place, core = here()
    own_tokens = tokens.reshape(token_count, model_width)
    above = cotangent.reshape(token_count, model_width)
    segment = segments[0]

    every = columns_by_core(jnp.transpose(blocks, (1, 0, 2)).astype(low))
    placing, packed, gates = pack_tokens(
        own_tokens, selected.reshape(token_count), packing[0], vectors
    )
    buffer = exchange(packed, n_data)
    attn_two = send(every[:4], line_pairs(2))
    ffn_got = send(after(every[4:], attn_two), line_pairs(2))
    attn_pair = jnp.stack([every[:4], attn_two])
    attn_got = send(attn_pair, line_pairs(1))
    line_attn = after(jnp.concatenate([attn_pair, attn_got]), packed)
    ffn_two = jnp.stack([every[4:], after(ffn_got, attn_got)])
    near_attn = send(line_attn, plane_pairs(0))
    every_root = roots_by_core(after(left_root, ffn_two), right_root)
    first_attn = after(jnp.stack([line_attn, near_attn]), every_root, buffer)
    far_attn = send(first_attn, plane_pairs(1))
    line_ffn = gather_far(ffn_two)
    near_ffn = send(after(line_ffn, far_attn), plane_pairs(0))
    root_given = lax.optimization_barrier((*roots_given(every_root), buffer, line_ffn))[:4]
    root_parts = [root_given[0]]
    for flip in (1, 2, 3):
        root_parts.append(send(root_given[flip], line_pairs(flip)))
    w_parts = with_other(first_attn, far_attn)
    answer, store = attend(buffer, w_parts, segment)
    first_ffn = jnp.stack([line_ffn, near_ffn])
    left_line, right_line = (jnp.stack([part[:, kind] for part in root_parts]) for kind in range(2))
    returned = exchange(answer, n_data)
    far_ffn = after(send(after(first_ffn, *root_parts[1:]), plane_pairs(1)), returned, right_line, left_line)
    ffn_parts = with_other(first_ffn, far_ffn)

    near_right = send(after(right_line, far_ffn), plane_pairs(0))
    first_right = jnp.stack([right_line, near_right])
    hidden, second_low, active, slope, w_up = token_forward(
        own_tokens, placing, returned, gates, vectors, ffn_parts
    )
    down_theirs = outer_theirs(after(active, near_right), above[None])
    far_right = send(first_right, plane_pairs(1))
    roots = (left_line, send(left_line, swap_pairs()), first_right, far_right)
    w_down = place_weights(ffn_parts, 4, 4)
    down_got = send(down_theirs, swap_pairs())
    down_give, *down_kept = sum_start(
        lambda step: step, active, above[None], after(down_got, w_down)
    )
    down_got = send(down_give, plane_pairs(0))
    mixed, grad_packed, grad_hidden, grad_logit, vector_two, grad_inner = token_backward(
        above,
        hidden,
        active,
        slope,
        placing,
        returned,
        gates,
        vectors,
        w_up,
        after(w_down, down_give),
    )
    grad_answer = exchange(grad_packed, n_data)
    up_theirs = outer_theirs(after(second_low, down_got, far_right)[None], grad_inner)

    down_kept, down_give = add_first(down_got, *down_kept)
    down_got = send(down_give, plane_pairs(1))
    up_got = send(after(up_theirs, grad_answer), swap_pairs())
    attn_theirs, grads, grad_buffer, sides = attend_back(store, segment, grad_answer)
    attn_got = send(after(attn_theirs, down_got), swap_pairs())
    up_give, *up_kept = sum_start(
        lambda step: 0, second_low[None], grad_inner, after(up_got, attn_theirs)
    )
    up_got = send(up_give, plane_pairs(0))
    down_own, down_two, down_give = cut_line((down_kept + down_got.astype(wide))[None])
    down_got = send(down_give, line_pairs(1))
    attn_give, *attn_kept = sum_start(
        lambda step: step // 3, sides, grads, after(attn_got, up_give)
    )
    attn_got = send(attn_give, plane_pairs(0))
    grad_sent = exchange(after(grad_buffer, attn_give), n_data)
    down_own, down_give = add_line(down_own, down_two, down_got)
    down_got = send(down_give, line_pairs(2))
    down_own = (down_own + down_got.astype(wide)).astype(low)
    down_near = send(down_own, plane_pairs(0))
    down_first = jnp.stack([down_own, down_near])

    up_kept, up_give = add_first(up_got, *up_kept)
    attn_kept, attn_give = add_first(after(attn_got, down_near), *attn_kept)
    rows, columns = down_own.shape[2:]
    given = jnp.stack([attn_give, up_give])
    both = jnp.concatenate(
        [given.reshape(-1, rows, columns), down_first.reshape(-1, rows, columns)]
    )
    both = send(both, plane_pairs(1))
    cut = given.shape[0] * given.shape[1] * given.shape[2]
    pair_got = both[:cut].reshape(given.shape)
    down_mine = jnp.concatenate([down_first, both[cut:].reshape(down_first.shape)])
    down_theirs = send(down_mine, swap_pairs())
    down_made, down_square = step_chunks(down_mine, down_theirs, roots, 2)
    down_parts = return_chunks(down_made)
    pair_kept = jnp.stack([attn_kept, up_kept]) + pair_got.astype(wide)
    pair_own, pair_two, pair_give = cut_line(pair_kept)
    pair_got = send(pair_give, line_pairs(1))
    grad_tokens, vector_one = token_back(
        own_tokens, placing, grad_sent, grad_hidden, grad_logit, vectors
    )
    pair_own, pair_give = add_line(pair_own, pair_two, pair_got)
    pair_got = send(after(pair_give, vector_one), line_pairs(2))
    down = jnp.stack(down_parts)
    down_other = send(down, [(i, i ^ 1) for i in range(0, 32, 2)])
    pair_own = (pair_own + pair_got.astype(wide)).astype(low)
    pair_near = send(after(pair_own, down_made), plane_pairs(0))
    pair_first = jnp.stack([pair_own, pair_near])
    pair_far = send(pair_first, plane_pairs(1))
    pair_mine = jnp.concatenate([pair_first, pair_far])
    pair_theirs = send(after(pair_mine, *down_parts[1:]), swap_pairs())
    pair_made, pair_square = step_chunks(pair_mine, pair_theirs, roots, 0)
    pair = jnp.stack(return_chunks(pair_made))
    pair_other = send(pair, swap_pairs())
    square_row = pair_square[0] + pair_square[1] + down_square[0]
    sums = all_sum(jnp.concatenate([vector_one, vector_two, square_row]))
    vector_grad = sums[:5]
    size = model_width * model_width
    scales = block_rate * lax.rsqrt(sums[5, :12] / size + norm_eps)
    grad_own, left_new, right_new, new_blocks = update_blocks(
        pair, pair_other, down, down_other, blocks, left_stat, right_stat, scales
    )
    moment_new = 0.5 * moment + 0.5 * vector_grad
    row_squares = jnp.mean(moment_new * moment_new, axis=1, keepdims=True)
    vector_new = vectors - vector_rate * moment_new * lax.rsqrt(row_squares + norm_eps)
    return (
        mixed.reshape(tokens.shape),
        grad_tokens.reshape(tokens.shape),
        grad_own,
        left_new,
        right_new,
        new_blocks,
        vector_grad,
        moment_new,
        vector_new,
    )


def shards(
    tokens,
    cotangent,
    selected,
    packing,
    segments,
    blocks,
    left_stat,
    right_stat,
    left_root,
    right_root,
    vectors,
    moment,
):
    model_width = tokens.shape[2]
    token_count = tokens.shape[0] * tokens.shape[1]
    n_data = lax.axis_size("dp")
    n_owner = lax.axis_size("own")
    shard_rows = blocks.shape[0]
    own_blocks = blocks.shape[1]
    up_blocks = (own_blocks * n_owner - 4) // 2
    capacity = packing.shape[1]
    per_peer = capacity // n_data
    head_count = model_width // HEAD_DIM
    score_scale = HEAD_DIM ** (-0.5)
    flat_weights = blocks.astype(jnp.bfloat16).reshape(1, shard_rows * own_blocks * model_width)
    gathered = lax.all_gather(flat_weights, ("dp", "own"), axis=0, tiled=True)
    gathered = gathered.reshape(n_data, n_owner, shard_rows, own_blocks, model_width)

    def matrix(number):
        return gathered[:, number // own_blocks, :, number % own_blocks, :].reshape(
            model_width, model_width
        )

    w_query = matrix(0)
    w_key = matrix(1)
    w_value = matrix(2)
    w_out = matrix(3)
    w_up = jnp.concatenate([matrix(4 + position) for position in range(up_blocks)], axis=1)
    w_down = jnp.concatenate(
        [matrix(4 + up_blocks + position) for position in range(up_blocks)], axis=0
    )
    inputs = tokens.reshape(token_count, model_width).astype(jnp.float32)
    chosen = selected.reshape(token_count)
    normed_one, norm_one_back = jax.vjp(layer_norm, inputs, vectors[0], vectors[1])
    first_low = normed_one.astype(jnp.bfloat16)
    first_wide = first_low.astype(jnp.float32)
    gate_values = jax.nn.sigmoid(jnp.dot(first_wide, vectors[2], precision=highest))
    before = jnp.cumsum(chosen) - 1
    slot_index = jnp.where(chosen == 1, packing[0][jnp.clip(before, 0, capacity - 1)], -1)
    placing = (slot_index[None, :] == jnp.arange(capacity, dtype=jnp.int32)[:, None]).astype(
        jnp.bfloat16
    )
    packed = jnp.dot(placing, first_low, preferred_element_type=jnp.float32).astype(jnp.bfloat16)
    buffer = lax.all_to_all(
        packed.reshape(n_data, per_peer, model_width), "dp", split_axis=0, concat_axis=0, tiled=True
    )
    buffer = buffer.reshape(capacity, model_width)

    def project(matrix_in):
        made = jnp.dot(buffer, matrix_in, preferred_element_type=jnp.float32).astype(jnp.bfloat16)
        return made.reshape(capacity, head_count, HEAD_DIM)

    query_rows = project(w_query)
    key_rows = project(w_key)
    value_rows = project(w_value)
    segment = segments[0]
    block_rows = math.gcd(capacity, 512)
    starts = jnp.arange(capacity // block_rows, dtype=jnp.int32) * block_rows

    def masked_scores():
        scores = (
            jnp.einsum("qhd,khd->hqk", query_rows, key_rows, preferred_element_type=jnp.float32)
            * score_scale
        )
        same_segment = segment[:, None] == segment[None, :]
        return (jnp.where(same_segment[None, :, :], scores, -1e30), query_rows)

    def forward_block(first_row):
        scores, unused_block = masked_scores()
        largest = jnp.max(scores, axis=-1, keepdims=True)
        raised = jnp.exp(scores - largest)
        row_total = jnp.sum(raised, axis=-1, keepdims=True)
        shares = (raised / row_total).astype(jnp.bfloat16)
        context_part = jnp.einsum(
            "hqk,khd->qhd", shares, value_rows, preferred_element_type=jnp.float32
        )
        return (context_part.astype(jnp.bfloat16), largest[..., 0] + jnp.log(row_total[..., 0]))

    context_blocks, lse_blocks = lax.map(forward_block, starts)
    context = context_blocks.reshape(capacity, model_width)
    answer = jnp.dot(context, w_out, preferred_element_type=jnp.float32).astype(jnp.bfloat16)
    returned = lax.all_to_all(
        answer.reshape(n_data, per_peer, model_width), "dp", split_axis=0, concat_axis=0, tiled=True
    )
    returned = returned.reshape(capacity, model_width)
    unpacked = jnp.einsum("mt,md->td", placing, returned, preferred_element_type=jnp.float32)
    weighting = jnp.where(chosen == 1, gate_values, 0.0)
    hidden = inputs + weighting[:, None] * unpacked
    normed_two, norm_two_back = jax.vjp(layer_norm, hidden, vectors[3], vectors[4])
    second_low = normed_two.astype(jnp.bfloat16)
    pre_active = jnp.dot(second_low, w_up, preferred_element_type=jnp.float32)
    active_wide, gelu_back = jax.vjp(gelu_exact, pre_active)
    active = active_wide.astype(jnp.bfloat16)
    result = hidden + jnp.dot(active, w_down, preferred_element_type=jnp.float32)
    mixed = result.astype(jnp.bfloat16).reshape(tokens.shape)
    upstream = cotangent.reshape(token_count, model_width)
    grad_down = jnp.einsum("tf,td->fd", active, upstream, preferred_element_type=jnp.float32)
    grad_active = jnp.einsum("td,fd->tf", upstream, w_down, preferred_element_type=jnp.float32)
    grad_inner = gelu_back(grad_active)[0].astype(jnp.bfloat16)
    grad_up = jnp.einsum("td,tf->df", second_low, grad_inner, preferred_element_type=jnp.float32)
    grad_second = jnp.einsum("tf,df->td", grad_inner, w_up, preferred_element_type=jnp.float32)
    grad_hidden_part, grad_gain_two, grad_bias_two = norm_two_back(grad_second)
    grad_hidden = upstream.astype(jnp.float32) + grad_hidden_part
    grad_token_back = (grad_hidden * weighting[:, None]).astype(jnp.bfloat16)
    grad_packed = jnp.dot(placing, grad_token_back, preferred_element_type=jnp.float32).astype(
        jnp.bfloat16
    )
    router_pull = jnp.where(chosen == 1, jnp.sum(grad_hidden * unpacked, axis=-1), 0.0)
    grad_logit = router_pull * gate_values * (1.0 - gate_values)
    grad_answer = lax.all_to_all(
        grad_packed.reshape(n_data, per_peer, model_width),
        "dp",
        split_axis=0,
        concat_axis=0,
        tiled=True,
    )
    grad_answer = grad_answer.reshape(capacity, model_width)
    grad_out = jnp.einsum("md,me->de", context, grad_answer, preferred_element_type=jnp.float32)
    grad_context = jnp.einsum("me,de->md", grad_answer, w_out, preferred_element_type=jnp.float32)
    grad_context = grad_context.astype(jnp.bfloat16).reshape(capacity, head_count, HEAD_DIM)

    def backward_block(running, item_pair):
        first_row, lse_block = item_pair
        scores, query_block = masked_scores()
        shares_wide = jnp.exp(scores - lse_block[..., None])
        grad_shares = jnp.einsum(
            "qhd,khd->hqk", grad_context, value_rows, preferred_element_type=jnp.float32
        )
        inner_sum = jnp.sum(shares_wide * grad_shares, axis=-1, keepdims=True)
        grad_scores = (shares_wide * (grad_shares - inner_sum)).astype(jnp.bfloat16)
        grad_query_block = (
            jnp.einsum("hqk,khd->qhd", grad_scores, key_rows, preferred_element_type=jnp.float32)
            * score_scale
        )
        key_sum = (
            running[0]
            + jnp.einsum(
                "hqk,qhd->khd", grad_scores, query_block, preferred_element_type=jnp.float32
            )
            * score_scale
        )
        value_sum = running[1] + jnp.einsum(
            "hqk,qhd->khd",
            shares_wide.astype(jnp.bfloat16),
            grad_context,
            preferred_element_type=jnp.float32,
        )
        return ((key_sum, value_sum), grad_query_block)

    zeros_init = jnp.zeros((capacity, head_count, HEAD_DIM), jnp.float32)
    (key_total, value_total), query_grads = lax.scan(
        backward_block, (zeros_init, zeros_init), (starts, lse_blocks)
    )
    grad_query = query_grads.reshape(capacity, model_width).astype(jnp.bfloat16)
    grad_key = key_total.reshape(capacity, model_width).astype(jnp.bfloat16)
    grad_value = value_total.reshape(capacity, model_width).astype(jnp.bfloat16)
    grad_w_query = jnp.einsum("md,me->de", buffer, grad_query, preferred_element_type=jnp.float32)
    grad_w_key = jnp.einsum("md,me->de", buffer, grad_key, preferred_element_type=jnp.float32)
    grad_w_value = jnp.einsum("md,me->de", buffer, grad_value, preferred_element_type=jnp.float32)
    grad_buffer = jnp.einsum("me,de->md", grad_query, w_query, preferred_element_type=jnp.float32)
    grad_buffer = grad_buffer + jnp.einsum(
        "me,de->md", grad_key, w_key, preferred_element_type=jnp.float32
    )
    grad_buffer = grad_buffer + jnp.einsum(
        "me,de->md", grad_value, w_value, preferred_element_type=jnp.float32
    )
    grad_buffer = grad_buffer.astype(jnp.bfloat16)
    grad_sent = lax.all_to_all(
        grad_buffer.reshape(n_data, per_peer, model_width),
        "dp",
        split_axis=0,
        concat_axis=0,
        tiled=True,
    )
    grad_sent = grad_sent.reshape(capacity, model_width)
    grad_first = jnp.einsum("mt,md->td", placing, grad_sent, preferred_element_type=jnp.float32)
    grad_first = grad_first + grad_logit[:, None] * vectors[2][None, :]
    grad_router = jnp.sum(grad_logit[:, None] * first_wide, axis=0)
    grad_input_part, grad_gain_one, grad_bias_one = norm_one_back(grad_first)
    grad_tokens = (grad_hidden + grad_input_part).astype(jnp.bfloat16).reshape(tokens.shape)
    pieces = [grad_w_query, grad_w_key, grad_w_value, grad_out]
    pieces = pieces + [
        grad_up[:, position * model_width : (position + 1) * model_width]
        for position in range(up_blocks)
    ]
    pieces = pieces + [
        grad_down[position * model_width : (position + 1) * model_width, :]
        for position in range(up_blocks)
    ]
    local_terms = jnp.stack(pieces, axis=1)
    vector_terms = jnp.stack(
        [grad_gain_one, grad_bias_one, grad_router, grad_gain_two, grad_bias_two]
    )
    partial_value = lax.psum_scatter(local_terms, "dp", scatter_dimension=0, tiled=True)
    grad_own = lax.psum_scatter(
        partial_value.astype(jnp.bfloat16), "own", scatter_dimension=1, tiled=True
    ).astype(jnp.float32)
    vector_grad = lax.psum(vector_terms, ("dp", "own"))
    full_grad = lax.all_gather(grad_own.astype(jnp.bfloat16), "dp", axis=0, tiled=True).astype(
        grad_own.dtype
    )
    row_start = lax.axis_index("dp") * shard_rows
    left_new = 0.5 * left_stat + 0.5 * jnp.einsum(
        "rbk,nbk->rbn", grad_own, full_grad, precision=highest
    )
    column_part = lax.dynamic_slice_in_dim(full_grad, row_start, shard_rows, 2)
    right_new = 0.5 * right_stat + 0.5 * jnp.einsum(
        "nbr,nbk->rbk", column_part, full_grad, precision=highest
    )
    lefted = jnp.einsum("rbn,nbk->rbk", left_root, full_grad, precision=highest)
    precond = jnp.zeros_like(grad_own) + jnp.einsum(
        "rbn,nbk->rbk",
        lefted,
        lax.all_gather(right_root.astype(jnp.bfloat16), "dp", axis=0, tiled=True).astype(
            jnp.float32
        ),
        precision=highest,
    )
    square_sums = lax.psum(jnp.sum(precond * precond, axis=(0, 2)), "dp")
    step_scale = lax.rsqrt(square_sums / (model_width * model_width) + norm_eps)
    new_blocks = blocks - block_rate * precond * step_scale[None, :, None]
    moment_new = 0.5 * moment + 0.5 * vector_grad
    row_squares = jnp.mean(moment_new * moment_new, axis=1, keepdims=True)
    vector_new = vectors - vector_rate * moment_new * lax.rsqrt(row_squares + norm_eps)
    return (
        mixed,
        grad_tokens,
        grad_own,
        left_new,
        right_new,
        new_blocks,
        vector_grad,
        moment_new,
        vector_new,
    )


def solution(mesh):
    placed = (
        P(("dp", "own"), None, None),
        P(("dp", "own"), None, None),
        P(("dp", "own"), None),
        P(("dp", "own"), None),
        P(("dp", "own"), None),
        P("dp", "own", None),
        P("dp", "own", None),
        P("dp", "own", None),
        P("dp", "own", None),
        P("dp", "own", None),
        P(),
        P(),
    )
    small = mesh.shape["dp"] == 16 and mesh.shape["own"] == 2
    return jax.shard_map(
        block_shards if small else shards,
        mesh=mesh,
        in_specs=placed,
        out_specs=(
            P(("dp", "own"), None, None),
            P(("dp", "own"), None, None),
            P("dp", "own", None),
            P("dp", "own", None),
            P("dp", "own", None),
            P("dp", "own", None),
            P(),
            P(),
            P(),
        ),
        check_vma=False,
    )
```

```python
import functools
import math

import jax
import jax.numpy as jnp
from jax import lax
from jax.experimental import pallas as pl
from jax.experimental.pallas import tpu as pltpu
from jax.sharding import PartitionSpec as P

HEAD_DIM = 64


norm_eps = 1e-06
block_rate = 0.03
vector_rate = 0.04
highest = lax.Precision.HIGHEST


def layer_norm(values, norm_gain, norm_bias):
    center = values - jnp.mean(values, axis=-1, keepdims=True)
    spread = jnp.mean(center * center, axis=-1, keepdims=True)
    return center * lax.rsqrt(spread + norm_eps) * norm_gain + norm_bias


def gelu_exact(values):
    return jax.nn.gelu(values, approximate=False)


BOTH = ("dp", "own")
low = jnp.bfloat16
wide = jnp.float32
MIB = 2**20


def swap_pairs():
    return [(i, i ^ 1) for i in range(32)]


def plane_pairs(step):
    pairs = []
    for i in range(32):
        place, core = i // 2, i % 2
        flip = (1, 2)[step ^ core]
        pairs.append((i, (place ^ flip) * 2 + core))
    return pairs


def line_pairs(flip):
    return [(i, i ^ (8 * flip)) for i in range(32)]


def send(value, pairs):
    return lax.ppermute(value, BOTH, pairs)


def after(value, *others):
    return lax.optimization_barrier((value,) + others)[0]


def pick(value, index, axis):
    return lax.dynamic_index_in_dim(value, index, axis, keepdims=False)


def first_core():
    return lax.axis_index("own") == 0


def halves(value):
    middle = value.shape[-1] // 2
    lower, upper = value[..., :middle], value[..., middle:]
    return jnp.where(first_core(), lower, upper), jnp.where(first_core(), upper, lower)


def in_core_order(mine, theirs, axis):
    return jnp.where(
        first_core(),
        jnp.concatenate([mine, theirs], axis=axis),
        jnp.concatenate([theirs, mine], axis=axis),
    )


LINE_FLIPS = (0, 2, 1, 3)


def flipped(index, flip):
    return jnp.bitwise_xor(index, flip)


def spots(place, half):
    first, second = half + 1, 2 - half
    return [
        place,
        flipped(place, first),
        flipped(place, second),
        flipped(place, 3),
    ]


def here():
    device = lax.axis_index("dp")
    return device // 4, device % 4, lax.axis_index("own")


def dot(left, right, left_axis=1, right_axis=0):
    return lax.dot_general(
        left, right, (((left_axis,), (right_axis,)), ((), ())), preferred_element_type=wide
    )


def on_chip():
    return pl.BlockSpec(memory_space=pltpu.VMEM)


def whole(value):
    return pl.BlockSpec(value.shape, lambda *steps: (0,) * value.ndim)


def in_hbm():
    return pl.BlockSpec(memory_space=pltpu.HBM)


def fetch_scratch(values):
    return [pltpu.VMEM(value.shape, value.dtype) for value in values] + [
        pltpu.SemaphoreType.DMA((len(values),))
    ]


def fetch(sources, targets, sems):
    copies = [
        pltpu.make_async_copy(source, target, sems.at[number])
        for number, (source, target) in enumerate(zip(sources, targets))
    ]
    for copy in copies:
        copy.start()
    return copies


def finish(copies):
    for copy in copies:
        copy.wait()


def params(limit):
    return pltpu.CompilerParams(vmem_limit_bytes=limit * MIB)


def cost(flops, moved):
    return pl.CostEstimate(flops=flops, bytes_accessed=moved, transcendentals=0)


def place_block(parts, block, target):
    line, place, core = here()
    rows, columns = parts[0].shape[3:]
    for other in range(2):
        half = core if other == 0 else 1 - core
        column_slice = pl.ds(pl.multiple_of(half * columns, columns), columns)
        for number, spot in enumerate(spots(place, half)):
            for index, flip in enumerate(LINE_FLIPS):
                start = (flipped(line, flip) * 4 + spot) * rows
                row_slice = pl.ds(pl.multiple_of(start, rows), rows)
                piece = parts[2 * other + number // 2][number % 2, index, block]
                target[row_slice, column_slice] = piece


def weight_kernel(first_block, one, two, three, four, out_ref):
    for block in range(out_ref.shape[0]):
        place_block((one, two, three, four), first_block + block, out_ref.at[block])


def place_weights(parts, first_block, blocks):
    rows, columns = parts[0].shape[3:]
    full = rows * 16
    return pl.pallas_call(
        functools.partial(weight_kernel, first_block),
        out_shape=jax.ShapeDtypeStruct((blocks, full, 2 * columns), low),
        in_specs=[on_chip()] * 4,
        out_specs=on_chip(),
        compiler_params=params(10),
        cost_estimate=cost(0, 8 * blocks * full * columns),
    )(*parts)


def columns_by_core(value):
    keep, give = halves(value)
    return in_core_order(keep, send(give, swap_pairs()), 0)


def gather_far(pair):
    return jnp.concatenate([pair, send(pair, line_pairs(1))])


def with_other(first, far):
    return [first, far, send(first, swap_pairs()), send(far, swap_pairs())]


def roots_by_core(left_root, right_root):
    both = [jnp.transpose(root, (1, 0, 2)).astype(low) for root in (left_root, right_root)]
    every = columns_by_core(jnp.stack(both, axis=1))
    return every.reshape((3, 4) + every.shape[1:])


def roots_given(every):
    line, place, core = here()
    return [pick(every, flipped(line, flip), 1) for flip in range(4)]


def sum_kernel(left_of, left, right, got, give_ref, kept_ref, passed_ref, total):
    line, place, core = here()
    step = pl.program_id(0)
    columns = got.shape[2]
    rows = kept_ref.shape[2]
    part = pl.ds(pl.multiple_of(core * columns, columns), columns)
    right_step = step if right.shape[0] > 1 else 0
    made = dot(left[left_of(step)], right[right_step, :, part], 0, 0)
    total[...] = made + got[step].astype(wide)
    own, first, second, both = spots(place, core)
    for row_line in range(4):

        def piece(spot):
            return total[pl.ds(pl.multiple_of((row_line * 4 + spot) * rows, rows), rows), :]

        give_ref[0, step, row_line] = piece(first).astype(low)
        give_ref[1, step, row_line] = piece(both).astype(low)
        kept_ref[step, row_line] = piece(own).astype(low)
        passed_ref[step, row_line] = piece(second).astype(low)


def sum_start(left_of, left, right, got):
    count, width = left.shape[1:]
    blocks, full, columns = got.shape
    shape = (blocks, 4, full // 16, columns)
    return pl.pallas_call(
        functools.partial(sum_kernel, left_of),
        grid=(blocks,),
        out_shape=(
            jax.ShapeDtypeStruct((2,) + shape, low),
            jax.ShapeDtypeStruct(shape, low),
            jax.ShapeDtypeStruct(shape, low),
        ),
        in_specs=[on_chip()] * 3,
        out_specs=(on_chip(),) * 3,
        scratch_shapes=[pltpu.VMEM((full, columns), wide)],
        compiler_params=params(12),
        cost_estimate=cost(blocks * count * width * width, 5 * blocks * width * width),
    )(left, right, got)


def add_first(got, kept, passed):
    kept = kept.astype(wide) + got[0].astype(wide)
    return kept, (passed.astype(wide) + got[1].astype(wide)).astype(low)


def cut_line(kept):
    line, place, core = here()
    given = jnp.stack([pick(kept, flipped(line, flip), 1) for flip in (1, 3)]).astype(low)
    return pick(kept, line, 1), pick(kept, flipped(line, 2), 1), given


def add_line(own, two, got):
    return own + got[0].astype(wide), (two + got[1].astype(wide)).astype(low)


def step_kernel(
    number,
    mine,
    theirs,
    left_mine_from,
    left_theirs_from,
    right_first_from,
    right_far_from,
    out_ref,
    square_ref,
    grad_ref,
    rows_ref,
    left_ref,
    right_ref,
    cross_ref,
    left_mine,
    left_theirs,
    right_first,
    right_far,
    sems,
):
    chunk = number + pl.program_id(0)
    copies = fetch(
        [
            left_mine_from.at[:, chunk],
            left_theirs_from.at[:, chunk],
            right_first_from.at[:, :, chunk],
            right_far_from.at[:, :, chunk],
        ],
        [left_mine, left_theirs, right_first, right_far],
        sems,
    )
    line, place, core = here()
    rows, columns = mine.shape[3:]

    def rows_of(row_line, spot):
        return pl.ds(pl.multiple_of((row_line * 4 + spot) * rows, rows), rows)

    def column_half(half):
        return pl.ds(pl.multiple_of(half * columns, columns), columns)

    for half, group in ((core, mine), (1 - core, theirs)):
        for number, spot in enumerate(spots(place, half)):
            for step in range(4):
                grad_ref[rows_of(step, spot), column_half(half)] = group[number, 0, step]
    finish(copies)
    for half, left in ((core, left_mine), (1 - core, left_theirs)):
        for flip in range(4):
            target = pl.ds(pl.multiple_of(flipped(line, flip) * rows, rows), rows)
            left_ref[target, column_half(half)] = left[flip]
    for number, spot in enumerate(spots(place, core)):
        source = right_far if number > 1 else right_first
        for flip in range(4):
            right_ref[rows_of(flipped(line, flip), spot), :] = source[number % 2, flip]
    for row_line in range(4):
        rows_ref[row_line * rows : (row_line + 1) * rows, :] = grad_ref[rows_of(row_line, place), :]
    left = dot(rows_ref[...], grad_ref[column_half(core), :], 1, 1)
    cross_ref[...] = dot(grad_ref[...], grad_ref[:, column_half(core)], 0, 0)
    lefted = dot(left_ref[...], grad_ref[...]).astype(low)
    stepped = dot(lefted, right_ref[...])
    squares = jnp.sum(jnp.sum(stepped * stepped, axis=0, keepdims=True), axis=1, keepdims=True)
    lane = lax.broadcasted_iota(jnp.int32, (1, 2 * columns), 1)
    square_ref[0] = jnp.where(lane == 4 * chunk + line, squares, 0.0)
    for row_line in range(4):
        part = slice(row_line * rows, (row_line + 1) * rows)
        out_ref[0, row_line, 0] = mine[0, 0, row_line]
        out_ref[0, row_line, 1] = left[part].astype(low)
        out_ref[0, row_line, 2] = cross_ref[rows_of(row_line, place), :].astype(low)
        out_ref[0, row_line, 3] = stepped[part].astype(low)


def step_chunks(mine, theirs, roots, number):
    chunks, lines, rows, columns = mine.shape[1:]
    full = rows * 16
    grad_spec = pl.BlockSpec((4, 1, lines, rows, columns), lambda step: (0, step, 0, 0, 0))
    return pl.pallas_call(
        functools.partial(step_kernel, number),
        grid=(chunks,),
        out_shape=(
            jax.ShapeDtypeStruct((chunks, lines, 4, rows, columns), low),
            jax.ShapeDtypeStruct((chunks, 1, 2 * columns), wide),
        ),
        in_specs=[grad_spec] * 2 + [in_hbm()] * 4,
        out_specs=(
            pl.BlockSpec((1, lines, 4, rows, columns), lambda step: (step, 0, 0, 0, 0)),
            pl.BlockSpec((1, 1, 2 * columns), lambda step: (step, 0, 0)),
        ),
        scratch_shapes=[
            pltpu.VMEM((full, columns * 2), low),
            pltpu.VMEM((lines * rows, columns * 2), low),
            pltpu.VMEM((lines * rows, columns * 2), low),
            pltpu.VMEM((full, columns), low),
            pltpu.VMEM((full, columns), wide),
            pltpu.VMEM((lines, rows, columns), low),
            pltpu.VMEM((lines, rows, columns), low),
            pltpu.VMEM((2, lines, rows, columns), low),
            pltpu.VMEM((2, lines, rows, columns), low),
            pltpu.SemaphoreType.DMA((4,)),
        ],
        compiler_params=params(15),
        cost_estimate=cost(3 * chunks * full**3, 16 * chunks * full * full),
    )(mine, theirs, *roots)


def return_chunks(made):
    line, place, core = here()
    parts = [pick(made, line, 1)]
    for flip in (1, 2, 3):
        parts.append(send(pick(made, flipped(line, flip), 1), line_pairs(flip)))
    return parts


def last_kernel(
    pair, pair_other, down, down_other, blocks, left_stat, right_stat, scales, *outs
):
    grad_out, left_out, right_out, block_out = outs
    line, place, core = here()
    columns = pair.shape[4]

    def update(number, which, mine, theirs):
        for (source, index), half in ((mine, which), (theirs, 1 - which)):
            part = slice(half * columns, (half + 1) * columns)
            pieces = [source[index + (kind,)].astype(wide) for kind in range(4)]
            grad_out[number, :, part] = pieces[0]
            left_out[number, :, part] = 0.5 * left_stat[number, :, part] + 0.5 * pieces[1]
            right_out[number, :, part] = 0.5 * right_stat[number, :, part] + 0.5 * pieces[2]
            step = pieces[3] * scales[6 * which + number]
            block_out[number, :, part] = blocks[number, :, part] - step

    @pl.when(core == 0)
    def first():
        for number in range(6):
            index = (flipped(line, number % 4), number // 4)
            update(number, 0, (pair, index), (pair_other, index))

    @pl.when(core == 1)
    def second():
        for number in range(6):
            source, other = (pair, pair_other) if number < 2 else (down, down_other)
            index = (flipped(line, (number + 2) % 4), 1 if number < 2 else 0)
            update(number, 1, (source, index), (other, index))


def update_blocks(pair, pair_other, down, down_other, blocks, left_stat, right_stat, scales):
    turned = [jnp.transpose(value, (1, 0, 2)) for value in (blocks, left_stat, right_stat)]
    shape = jax.ShapeDtypeStruct(turned[0].shape, wide)
    outs = pl.pallas_call(
        last_kernel,
        out_shape=(shape,) * 4,
        in_specs=[on_chip()] * 7 + [pl.BlockSpec(memory_space=pltpu.SMEM)],
        out_specs=(on_chip(),) * 4,
        compiler_params=params(10),
        cost_estimate=cost(0, 32 * shape.size),
    )(pair, pair_other, down, down_other, *turned, scales)
    return [jnp.transpose(value, (1, 0, 2)) for value in outs]


def head_masks():
    lane = lax.broadcasted_iota(jnp.int32, (1, 2 * HEAD_DIM), 1)
    return [(lane < HEAD_DIM).astype(wide).astype(low), (lane >= HEAD_DIM).astype(wide).astype(low)]


def head_shares(query, key, same):
    scores = dot(query, key, 1, 1) * HEAD_DIM ** (-0.5)
    scores = jnp.where(same, scores, -1e30)
    raised = jnp.exp(scores - jnp.max(scores, axis=-1, keepdims=True))
    return raised / jnp.sum(raised, axis=-1, keepdims=True)


STORE_ROWS = 32768


def store_views(store, rows, width):
    weights = [store.at[pl.ds(block * width, width)] for block in range(4)]
    made = [store.at[pl.ds(4 * width + kind * rows, rows)] for kind in range(3)]
    sides = [store.at[pl.ds(4 * width + (3 + side) * rows, rows)] for side in range(2)]
    return weights, made, sides


def attend_kernel(
    buffer, one, two, three, four, seg_column, seg_row, answer_ref, store, weights, made, sides, sems
):
    rows, width = buffer.shape
    weights_out, made_out, sides_out = store_views(store, rows, width)
    for block in range(4):
        place_block((one, two, three, four), block, weights.at[block])
    copies = fetch([weights.at[block] for block in range(4)], weights_out, sems)
    same = seg_column[...] == seg_row[...]
    for kind in range(3):
        made[kind] = dot(buffer[...], weights[kind]).astype(low)
    copies += fetch([made.at[kind] for kind in range(3)], made_out, sems.at[pl.ds(4, 3)])
    pair_width = 2 * HEAD_DIM
    for pair in range(width // pair_width):
        part = slice(pair * pair_width, (pair + 1) * pair_width)
        query, key, value = (made[kind, :, part] for kind in range(3))
        context = None
        for mask in head_masks():
            shares = head_shares(query, key * mask, same).astype(low)
            term = dot(shares, value * mask)
            context = term if context is None else context + term
        sides[1, :, part] = context.astype(low)
    sides[0] = buffer[...]
    copies += fetch([sides.at[side] for side in range(2)], sides_out, sems.at[pl.ds(7, 2)])
    answer_ref[...] = dot(sides[1], weights[3]).astype(low)
    finish(copies)


def attend_scratch(rows, width):
    return [
        pltpu.VMEM((4, width, width), low),
        pltpu.VMEM((3, rows, width), low),
        pltpu.VMEM((2, rows, width), low),
        pltpu.SemaphoreType.DMA((9,)),
    ]


def attend(buffer, parts, segment):
    rows, width = buffer.shape
    return pl.pallas_call(
        attend_kernel,
        out_shape=(
            jax.ShapeDtypeStruct((rows, width), low),
            jax.ShapeDtypeStruct((STORE_ROWS, width), low),
        ),
        in_specs=[on_chip()] * 7,
        out_specs=(on_chip(), in_hbm()),
        scratch_shapes=attend_scratch(rows, width),
        compiler_params=params(20),
        cost_estimate=cost(12 * rows * width * width, 12 * width * width),
    )(buffer, *parts, segment[:, None], segment[None, :])


def attend_back_kernel(
    store,
    seg_column,
    seg_row,
    grad_answer,
    theirs_ref,
    grads_ref,
    grad_buffer_ref,
    sides,
    grad_context_ref,
    weights,
    made,
    sems,
):
    rows, width = grad_answer.shape
    weights_from, made_from, sides_from = store_views(store, rows, width)
    out_copy, *copies = fetch(
        [weights_from[3]] + made_from + sides_from + weights_from[:3],
        [weights.at[3]]
        + [made.at[kind] for kind in range(3)]
        + [sides.at[side] for side in range(2)]
        + [weights.at[block] for block in range(3)],
        sems,
    )
    same = seg_column[...] == seg_row[...]
    core = lax.axis_index("own")
    out_copy.wait()
    grad_context_ref[...] = dot(grad_answer[...], weights[3], 1, 1).astype(low)
    finish(copies[:3])
    grads_ref[3] = grad_answer[...]
    pair_width = 2 * HEAD_DIM
    for pair in range(width // pair_width):
        part = slice(pair * pair_width, (pair + 1) * pair_width)
        query, key, value = (made[kind, :, part] for kind in range(3))
        above = grad_context_ref[:, part]
        sums = [None] * 3
        for mask in head_masks():
            key_head = key * mask
            shares = head_shares(query, key_head, same)
            grad_shares = dot(above, value * mask, 1, 1)
            inner = jnp.sum(shares * grad_shares, axis=-1, keepdims=True)
            grad_scores = (shares * (grad_shares - inner)).astype(low)
            terms = (
                dot(grad_scores, key_head),
                dot(grad_scores, query * mask, 0, 0),
                dot(shares.astype(low), above * mask, 0, 0),
            )
            sums = [
                term if total is None else total + term for term, total in zip(terms, sums)
            ]
        for kind, factor in enumerate((HEAD_DIM ** (-0.5), HEAD_DIM ** (-0.5), 1.0)):
            grads_ref[kind, :, part] = (sums[kind] * factor).astype(low)
    finish(copies[3:5])
    columns = theirs_ref.shape[2]
    part = pl.ds(pl.multiple_of((1 - core) * columns, columns), columns)
    for kind in range(4):
        theirs_ref[kind] = dot(sides[kind // 3], grads_ref[kind, :, part], 0, 0).astype(low)
    finish(copies[5:])
    total = dot(grads_ref[0], weights[0], 1, 1)
    total = total + dot(grads_ref[1], weights[1], 1, 1)
    total = total + dot(grads_ref[2], weights[2], 1, 1)
    grad_buffer_ref[...] = total.astype(low)


def attend_back(store, segment, grad_answer):
    rows, width = grad_answer.shape
    weights, made, sides, sems = attend_scratch(rows, width)
    return pl.pallas_call(
        attend_back_kernel,
        out_shape=(
            jax.ShapeDtypeStruct((4, width, width // 2), low),
            jax.ShapeDtypeStruct((4, rows, width), low),
            jax.ShapeDtypeStruct((rows, width), low),
            jax.ShapeDtypeStruct((2, rows, width), low),
        ),
        in_specs=[in_hbm()] + [on_chip()] * 3,
        out_specs=(on_chip(),) * 4,
        scratch_shapes=[pltpu.VMEM((rows, width), low), weights, made, sems],
        compiler_params=params(18),
        cost_estimate=cost(20 * rows * width * width, 16 * width * width),
    )(store, segment[:, None], segment[None, :], grad_answer)


def normal_parts(values):
    center = values - jnp.mean(values, axis=-1, keepdims=True)
    spread = jnp.mean(center * center, axis=-1, keepdims=True)
    return center, lax.rsqrt(spread + norm_eps)


def forward_kernel(*refs):
    tokens, placing, returned, gates, vectors = refs[:5]
    parts = refs[5:9]
    hidden_ref, second_ref, active_ref, slope_ref, w_up = refs[9:14]
    step = pl.program_id(0)

    @pl.when(step == 0)
    def prepare():
        values = tokens[...].astype(wide) + gates[:, 0:1] * dot(placing[...], returned[...])
        hidden_ref[...] = values
        center, inverse = normal_parts(values)
        second_ref[...] = (center * inverse * vectors[3:4] + vectors[4:5]).astype(low)

    place_block(parts, step, w_up.at[step])
    before = dot(second_ref[...], w_up[step])
    share = 0.5 + 0.5 * lax.erf(before * (0.5**0.5))
    density = jnp.exp(before * before * -0.5) * (0.5 / math.pi) ** 0.5
    active_ref[step] = (before * share).astype(low)
    slope_ref[step] = (share + before * density).astype(low)


def token_forward(tokens, placing, returned, gates, vectors, parts):
    count, width = tokens.shape
    blocks = parts[0].shape[2] // 2
    by_block = jax.ShapeDtypeStruct((blocks, count, width), low)
    fetched = (tokens, placing, returned, gates, vectors)
    return pl.pallas_call(
        forward_kernel,
        grid=(blocks,),
        out_shape=(
            jax.ShapeDtypeStruct((count, width), wide),
            jax.ShapeDtypeStruct((count, width), low),
            by_block,
            by_block,
            jax.ShapeDtypeStruct((blocks, width, width), low),
        ),
        in_specs=[whole(value) for value in fetched] + [on_chip()] * 4,
        out_specs=(on_chip(),) * 5,
        compiler_params=params(18),
        cost_estimate=cost(8 * blocks * count * width * width, 8 * blocks * width * width),
    )(*fetched, *parts)


def backward_kernel(*refs):
    above, placing, returned, gates, vectors = refs[:5]
    hidden, active, slope, w_up, w_down = refs[5:10]
    mixed_ref, packed_ref, grad_hidden_ref, logit_ref, vector_ref, inner_ref = refs[10:16]
    result, grad_second = refs[16:]
    step = pl.program_id(0)

    @pl.when(step == 0)
    def prepare():
        result[...] = hidden[...]
        grad_second[...] = jnp.zeros_like(grad_second)

    grad_active = dot(above[...], w_down[step], 1, 1)
    grad_inner = (grad_active * slope[step].astype(wide)).astype(low)
    inner_ref[step] = grad_inner
    result[...] += dot(active[step], w_down[step])
    grad_second[...] += dot(grad_inner, w_up[step], 1, 1)

    @pl.when(step == pl.num_programs(0) - 1)
    def complete():
        mixed_ref[...] = result[...].astype(low)
        center, inverse = normal_parts(hidden[...])
        scaled = center * inverse
        grads = grad_second[...]
        vector_ref[0:1] = jnp.sum(grads * scaled, axis=0, keepdims=True)
        vector_ref[1:2] = jnp.sum(grads, axis=0, keepdims=True)
        pulled = grads * vectors[3:4]
        pulled = (
            pulled
            - jnp.mean(pulled, axis=-1, keepdims=True)
            - scaled * jnp.mean(pulled * scaled, axis=-1, keepdims=True)
        )
        grad_hidden = above[...].astype(wide) + inverse * pulled
        grad_hidden_ref[...] = grad_hidden
        weighted = (grad_hidden * gates[:, 0:1]).astype(low)
        packed_ref[...] = dot(placing[...], weighted, 0, 0).astype(low)
        unpacked = dot(placing[...], returned[...])
        logit_ref[...] = gates[:, 1:2] * jnp.sum(grad_hidden * unpacked, axis=-1, keepdims=True)


def token_backward(above, hidden, active, slope, placing, returned, gates, vectors, w_up, w_down):
    count, width = above.shape
    slots = placing.shape[1]
    blocks = w_up.shape[0]
    fetched = (above, placing, returned, gates, vectors)
    return pl.pallas_call(
        backward_kernel,
        grid=(blocks,),
        out_shape=(
            jax.ShapeDtypeStruct((count, width), low),
            jax.ShapeDtypeStruct((slots, width), low),
            jax.ShapeDtypeStruct((count, width), wide),
            jax.ShapeDtypeStruct((count, 1), wide),
            jax.ShapeDtypeStruct((2, width), wide),
            jax.ShapeDtypeStruct((blocks, count, width), low),
        ),
        in_specs=[whole(value) for value in fetched] + [on_chip()] * 5,
        out_specs=(on_chip(),) * 6,
        scratch_shapes=[
            pltpu.VMEM((count, width), wide),
            pltpu.VMEM((count, width), wide),
        ],
        compiler_params=params(30),
        cost_estimate=cost(8 * blocks * count * width * width, 8 * blocks * width * width),
    )(*fetched, hidden, active, slope, w_up, w_down)


def outer_kernel(left, right, theirs_ref):
    core = lax.axis_index("own")
    step = pl.program_id(0)
    columns = theirs_ref.shape[2]
    left_step = step if left.shape[0] > 1 else 0
    right_step = step if right.shape[0] > 1 else 0
    part = pl.ds(pl.multiple_of((1 - core) * columns, columns), columns)
    theirs_ref[step] = dot(left[left_step], right[right_step, :, part], 0, 0).astype(low)


def outer_theirs(left, right):
    count, width = left.shape[1:]
    blocks = max(left.shape[0], right.shape[0])
    return pl.pallas_call(
        outer_kernel,
        grid=(blocks,),
        out_shape=jax.ShapeDtypeStruct((blocks, width, width // 2), low),
        in_specs=[on_chip()] * 2,
        out_specs=on_chip(),
        compiler_params=params(8),
        cost_estimate=cost(blocks * count * width * width, 3 * blocks * width * width),
    )(left, right)


def column(values):
    return values[:, None]


def pack_kernel(
    tokens, chosen, packing, vectors, placing_ref, packed_ref, gates_ref
):
    count = tokens.shape[0]
    capacity = packing.shape[0]
    center, inverse = normal_parts(tokens[...].astype(wide))
    first = (center * inverse * vectors[0:1] + vectors[1:2]).astype(low)
    gate = jax.nn.sigmoid(jnp.sum(first.astype(wide) * vectors[2:3], axis=-1, keepdims=True))
    weighting = jnp.where(chosen[...] == 1, gate, 0.0)
    gates_ref[:, 0:1] = weighting
    gates_ref[:, 1:2] = weighting * (1.0 - gate)
    above = lax.broadcasted_iota(jnp.int32, (count, count), 0)
    below = lax.broadcasted_iota(jnp.int32, (count, count), 1)
    earlier = (below <= above).astype(wide).astype(low)
    flags = jnp.broadcast_to(chosen[...].astype(wide), (count, capacity))
    rank = dot(earlier, flags.astype(low))
    place_of = lax.broadcasted_iota(jnp.int32, (count, capacity), 1).astype(wide) + 1.0
    ranked = jnp.where(rank == place_of, flags, 0.0).astype(low)
    slots = lax.broadcasted_iota(jnp.int32, (capacity, capacity), 1)
    slot_of = (packing[...] == slots).astype(wide).astype(low)
    placing = dot(ranked, slot_of).astype(low)
    placing_ref[...] = placing
    packed_ref[...] = dot(placing, first, 0, 0).astype(low)


def pack_tokens(tokens, chosen, packing, vectors):
    count, width = tokens.shape
    capacity = packing.shape[0]
    return pl.pallas_call(
        pack_kernel,
        out_shape=(
            jax.ShapeDtypeStruct((count, capacity), low),
            jax.ShapeDtypeStruct((capacity, width), low),
            jax.ShapeDtypeStruct((count, 2), wide),
        ),
        in_specs=[on_chip()] * 4,
        out_specs=(on_chip(),) * 3,
        compiler_params=params(10),
        cost_estimate=cost(4 * count * capacity * width, 8 * count * width),
    )(tokens, column(chosen), column(packing), vectors)


def token_back_kernel(*refs):
    sources, (out_ref, vector_ref), fetched, sems = refs[:6], refs[6:8], refs[8:14], refs[14]
    finish(fetch(sources, fetched, sems))
    tokens, placing, grad_sent, grad_hidden, grad_logit, vectors = fetched
    grad_first = dot(placing[...], grad_sent[...]) + grad_logit[...] * vectors[2:3]
    center, inverse = normal_parts(tokens[...].astype(wide))
    scaled = center * inverse
    vector_ref[0:1] = jnp.sum(grad_first * scaled, axis=0, keepdims=True)
    vector_ref[1:2] = jnp.sum(grad_first, axis=0, keepdims=True)
    first = (scaled * vectors[0:1] + vectors[1:2]).astype(low).astype(wide)
    vector_ref[2:3] = jnp.sum(grad_logit[...] * first, axis=0, keepdims=True)
    pulled = grad_first * vectors[0:1]
    pulled = (
        pulled
        - jnp.mean(pulled, axis=-1, keepdims=True)
        - scaled * jnp.mean(pulled * scaled, axis=-1, keepdims=True)
    )
    out_ref[...] = (grad_hidden[...] + inverse * pulled).astype(low)


def token_back(tokens, placing, grad_sent, grad_hidden, grad_logit, vectors):
    count, width = tokens.shape
    return pl.pallas_call(
        token_back_kernel,
        out_shape=(
            jax.ShapeDtypeStruct((count, width), low),
            jax.ShapeDtypeStruct((3, width), wide),
        ),
        in_specs=[in_hbm()] * 6,
        out_specs=(on_chip(),) * 2,
        scratch_shapes=fetch_scratch(
            (tokens, placing, grad_sent, grad_hidden, grad_logit, vectors)
        ),
        compiler_params=params(17),
        cost_estimate=cost(2 * count * width * placing.shape[1], 12 * count * width),
    )(tokens, placing, grad_sent, grad_hidden, grad_logit, vectors)


def flip_pairs(flip):
    return [(i, i ^ flip) for i in range(32)]


def all_sum(value):
    value = value + send(value, swap_pairs())
    for one, two in ((2, 4), (8, 16)):
        near = value + send(value, flip_pairs(one))
        far = send(value, flip_pairs(two)) + send(value, flip_pairs(one + two))
        value = near + far
    return value


def exchange(value, n_data):
    capacity, width = value.shape
    moved = lax.all_to_all(
        value.reshape(n_data, capacity // n_data, width), "dp", split_axis=0, concat_axis=0, tiled=True
    )
    return moved.reshape(capacity, width)


def block_shards(
    tokens,
    cotangent,
    selected,
    packing,
    segments,
    blocks,
    left_stat,
    right_stat,
    left_root,
    right_root,
    vectors,
    moment,
):
    model_width = tokens.shape[2]
    token_count = tokens.shape[0] * tokens.shape[1]
    n_data = lax.axis_size("dp")
    capacity = packing.shape[1]
    line, place, core = here()
    own_tokens = tokens.reshape(token_count, model_width)
    above = cotangent.reshape(token_count, model_width)
    segment = segments[0]

    every = columns_by_core(jnp.transpose(blocks, (1, 0, 2)).astype(low))
    placing, packed, gates = pack_tokens(
        own_tokens, selected.reshape(token_count), packing[0], vectors
    )
    buffer = exchange(packed, n_data)
    attn_two = send(every[:4], line_pairs(2))
    ffn_got = send(after(every[4:], attn_two), line_pairs(2))
    attn_pair = jnp.stack([every[:4], attn_two])
    attn_got = send(attn_pair, line_pairs(1))
    line_attn = after(jnp.concatenate([attn_pair, attn_got]), packed)
    ffn_two = jnp.stack([every[4:], after(ffn_got, attn_got)])
    near_attn = send(line_attn, plane_pairs(0))
    every_root = roots_by_core(after(left_root, ffn_two), right_root)
    first_attn = after(jnp.stack([line_attn, near_attn]), every_root, buffer)
    far_attn = send(first_attn, plane_pairs(1))
    line_ffn = gather_far(ffn_two)
    near_ffn = send(after(line_ffn, far_attn), plane_pairs(0))
    root_given = lax.optimization_barrier((*roots_given(every_root), buffer, line_ffn))[:4]
    root_parts = [root_given[0]]
    for flip in (1, 2, 3):
        root_parts.append(send(root_given[flip], line_pairs(flip)))
    w_parts = with_other(first_attn, far_attn)
    answer, store = attend(buffer, w_parts, segment)
    first_ffn = jnp.stack([line_ffn, near_ffn])
    left_line, right_line = (jnp.stack([part[:, kind] for part in root_parts]) for kind in range(2))
    returned = exchange(answer, n_data)
    far_ffn = after(send(after(first_ffn, *root_parts[1:]), plane_pairs(1)), answer, right_line, left_line)
    ffn_parts = with_other(first_ffn, far_ffn)

    near_right = send(after(right_line, far_ffn), plane_pairs(0))
    first_right = jnp.stack([right_line, near_right])
    hidden, second_low, active, slope, w_up = token_forward(
        own_tokens, placing, returned, gates, vectors, ffn_parts
    )
    down_theirs = outer_theirs(after(active, near_right), above[None])
    far_right = send(first_right, plane_pairs(1))
    roots = (left_line, send(left_line, swap_pairs()), first_right, far_right)
    w_down = place_weights(ffn_parts, 4, 4)
    down_got = send(down_theirs, swap_pairs())
    down_give, *down_kept = sum_start(
        lambda step: step, active, above[None], after(down_got, w_down)
    )
    down_got = send(down_give, plane_pairs(0))
    mixed, grad_packed, grad_hidden, grad_logit, vector_two, grad_inner = token_backward(
        above,
        hidden,
        active,
        slope,
        placing,
        returned,
        gates,
        vectors,
        w_up,
        after(w_down, down_give),
    )
    grad_answer = exchange(grad_packed, n_data)
    up_theirs = outer_theirs(after(second_low, down_got, far_right)[None], grad_inner)

    down_kept, down_give = add_first(down_got, *down_kept)
    down_got = send(down_give, plane_pairs(1))
    up_got = send(after(up_theirs, grad_answer), swap_pairs())
    attn_theirs, grads, grad_buffer, sides = attend_back(store, segment, grad_answer)
    attn_got = send(after(attn_theirs, down_got), swap_pairs())
    up_give, *up_kept = sum_start(
        lambda step: 0, second_low[None], grad_inner, after(up_got, attn_theirs)
    )
    up_got = send(up_give, plane_pairs(0))
    down_own, down_two, down_give = cut_line((down_kept + down_got.astype(wide))[None])
    down_got = send(down_give, line_pairs(1))
    attn_give, *attn_kept = sum_start(
        lambda step: step // 3, sides, grads, after(attn_got, up_give)
    )
    attn_got = send(attn_give, plane_pairs(0))
    grad_sent = exchange(after(grad_buffer, attn_give), n_data)
    down_own, down_give = add_line(down_own, down_two, down_got)
    down_got = send(down_give, line_pairs(2))
    down_own = (down_own + down_got.astype(wide)).astype(low)
    down_near = send(down_own, plane_pairs(0))
    down_first = jnp.stack([down_own, down_near])

    up_kept, up_give = add_first(up_got, *up_kept)
    attn_kept, attn_give = add_first(after(attn_got, down_near), *attn_kept)
    rows, columns = down_own.shape[2:]
    given = jnp.stack([attn_give, up_give])
    both = jnp.concatenate(
        [given.reshape(-1, rows, columns), down_first.reshape(-1, rows, columns)]
    )
    both = send(both, plane_pairs(1))
    cut = given.shape[0] * given.shape[1] * given.shape[2]
    pair_got = both[:cut].reshape(given.shape)
    down_mine = jnp.concatenate([down_first, both[cut:].reshape(down_first.shape)])
    down_theirs = send(down_mine, swap_pairs())
    down_made, down_square = step_chunks(down_mine, down_theirs, roots, 2)
    down_parts = return_chunks(down_made)
    pair_kept = jnp.stack([attn_kept, up_kept]) + pair_got.astype(wide)
    pair_own, pair_two, pair_give = cut_line(pair_kept)
    pair_got = send(pair_give, line_pairs(1))
    grad_tokens, vector_one = token_back(
        own_tokens, placing, grad_sent, grad_hidden, grad_logit, vectors
    )
    pair_own, pair_give = add_line(pair_own, pair_two, pair_got)
    pair_got = send(after(pair_give, vector_one), line_pairs(2))
    down = jnp.stack(down_parts)
    down_other = send(down, [(i, i ^ 1) for i in range(0, 32, 2)])
    pair_own = (pair_own + pair_got.astype(wide)).astype(low)
    pair_near = send(after(pair_own, down_made), plane_pairs(0))
    pair_first = jnp.stack([pair_own, pair_near])
    pair_far = send(pair_first, plane_pairs(1))
    pair_mine = jnp.concatenate([pair_first, pair_far])
    pair_theirs = send(after(pair_mine, *down_parts[1:]), swap_pairs())
    pair_made, pair_square = step_chunks(pair_mine, pair_theirs, roots, 0)
    pair = jnp.stack(return_chunks(pair_made))
    pair_other = send(pair, swap_pairs())
    square_row = pair_square[0] + pair_square[1] + down_square[0]
    sums = all_sum(jnp.concatenate([vector_one, vector_two, square_row]))
    vector_grad = sums[:5]
    size = model_width * model_width
    scales = block_rate * lax.rsqrt(sums[5, :12] / size + norm_eps)
    grad_own, left_new, right_new, new_blocks = update_blocks(
        pair, pair_other, down, down_other, blocks, left_stat, right_stat, scales
    )
    moment_new = 0.5 * moment + 0.5 * vector_grad
    row_squares = jnp.mean(moment_new * moment_new, axis=1, keepdims=True)
    vector_new = vectors - vector_rate * moment_new * lax.rsqrt(row_squares + norm_eps)
    return (
        mixed.reshape(tokens.shape),
        grad_tokens.reshape(tokens.shape),
        grad_own,
        left_new,
        right_new,
        new_blocks,
        vector_grad,
        moment_new,
        vector_new,
    )


def shards(
    tokens,
    cotangent,
    selected,
    packing,
    segments,
    blocks,
    left_stat,
    right_stat,
    left_root,
    right_root,
    vectors,
    moment,
):
    model_width = tokens.shape[2]
    token_count = tokens.shape[0] * tokens.shape[1]
    n_data = lax.axis_size("dp")
    n_owner = lax.axis_size("own")
    shard_rows = blocks.shape[0]
    own_blocks = blocks.shape[1]
    up_blocks = (own_blocks * n_owner - 4) // 2
    capacity = packing.shape[1]
    per_peer = capacity // n_data
    head_count = model_width // HEAD_DIM
    score_scale = HEAD_DIM ** (-0.5)
    flat_weights = blocks.astype(jnp.bfloat16).reshape(1, shard_rows * own_blocks * model_width)
    gathered = lax.all_gather(flat_weights, ("dp", "own"), axis=0, tiled=True)
    gathered = gathered.reshape(n_data, n_owner, shard_rows, own_blocks, model_width)

    def matrix(number):
        return gathered[:, number // own_blocks, :, number % own_blocks, :].reshape(
            model_width, model_width
        )

    w_query = matrix(0)
    w_key = matrix(1)
    w_value = matrix(2)
    w_out = matrix(3)
    w_up = jnp.concatenate([matrix(4 + position) for position in range(up_blocks)], axis=1)
    w_down = jnp.concatenate(
        [matrix(4 + up_blocks + position) for position in range(up_blocks)], axis=0
    )
    inputs = tokens.reshape(token_count, model_width).astype(jnp.float32)
    chosen = selected.reshape(token_count)
    normed_one, norm_one_back = jax.vjp(layer_norm, inputs, vectors[0], vectors[1])
    first_low = normed_one.astype(jnp.bfloat16)
    first_wide = first_low.astype(jnp.float32)
    gate_values = jax.nn.sigmoid(jnp.dot(first_wide, vectors[2], precision=highest))
    before = jnp.cumsum(chosen) - 1
    slot_index = jnp.where(chosen == 1, packing[0][jnp.clip(before, 0, capacity - 1)], -1)
    placing = (slot_index[None, :] == jnp.arange(capacity, dtype=jnp.int32)[:, None]).astype(
        jnp.bfloat16
    )
    packed = jnp.dot(placing, first_low, preferred_element_type=jnp.float32).astype(jnp.bfloat16)
    buffer = lax.all_to_all(
        packed.reshape(n_data, per_peer, model_width), "dp", split_axis=0, concat_axis=0, tiled=True
    )
    buffer = buffer.reshape(capacity, model_width)

    def project(matrix_in):
        made = jnp.dot(buffer, matrix_in, preferred_element_type=jnp.float32).astype(jnp.bfloat16)
        return made.reshape(capacity, head_count, HEAD_DIM)

    query_rows = project(w_query)
    key_rows = project(w_key)
    value_rows = project(w_value)
    segment = segments[0]
    block_rows = math.gcd(capacity, 512)
    starts = jnp.arange(capacity // block_rows, dtype=jnp.int32) * block_rows

    def masked_scores():
        scores = (
            jnp.einsum("qhd,khd->hqk", query_rows, key_rows, preferred_element_type=jnp.float32)
            * score_scale
        )
        same_segment = segment[:, None] == segment[None, :]
        return (jnp.where(same_segment[None, :, :], scores, -1e30), query_rows)

    def forward_block(first_row):
        scores, unused_block = masked_scores()
        largest = jnp.max(scores, axis=-1, keepdims=True)
        raised = jnp.exp(scores - largest)
        row_total = jnp.sum(raised, axis=-1, keepdims=True)
        shares = (raised / row_total).astype(jnp.bfloat16)
        context_part = jnp.einsum(
            "hqk,khd->qhd", shares, value_rows, preferred_element_type=jnp.float32
        )
        return (context_part.astype(jnp.bfloat16), largest[..., 0] + jnp.log(row_total[..., 0]))

    context_blocks, lse_blocks = lax.map(forward_block, starts)
    context = context_blocks.reshape(capacity, model_width)
    answer = jnp.dot(context, w_out, preferred_element_type=jnp.float32).astype(jnp.bfloat16)
    returned = lax.all_to_all(
        answer.reshape(n_data, per_peer, model_width), "dp", split_axis=0, concat_axis=0, tiled=True
    )
    returned = returned.reshape(capacity, model_width)
    unpacked = jnp.einsum("mt,md->td", placing, returned, preferred_element_type=jnp.float32)
    weighting = jnp.where(chosen == 1, gate_values, 0.0)
    hidden = inputs + weighting[:, None] * unpacked
    normed_two, norm_two_back = jax.vjp(layer_norm, hidden, vectors[3], vectors[4])
    second_low = normed_two.astype(jnp.bfloat16)
    pre_active = jnp.dot(second_low, w_up, preferred_element_type=jnp.float32)
    active_wide, gelu_back = jax.vjp(gelu_exact, pre_active)
    active = active_wide.astype(jnp.bfloat16)
    result = hidden + jnp.dot(active, w_down, preferred_element_type=jnp.float32)
    mixed = result.astype(jnp.bfloat16).reshape(tokens.shape)
    upstream = cotangent.reshape(token_count, model_width)
    grad_down = jnp.einsum("tf,td->fd", active, upstream, preferred_element_type=jnp.float32)
    grad_active = jnp.einsum("td,fd->tf", upstream, w_down, preferred_element_type=jnp.float32)
    grad_inner = gelu_back(grad_active)[0].astype(jnp.bfloat16)
    grad_up = jnp.einsum("td,tf->df", second_low, grad_inner, preferred_element_type=jnp.float32)
    grad_second = jnp.einsum("tf,df->td", grad_inner, w_up, preferred_element_type=jnp.float32)
    grad_hidden_part, grad_gain_two, grad_bias_two = norm_two_back(grad_second)
    grad_hidden = upstream.astype(jnp.float32) + grad_hidden_part
    grad_token_back = (grad_hidden * weighting[:, None]).astype(jnp.bfloat16)
    grad_packed = jnp.dot(placing, grad_token_back, preferred_element_type=jnp.float32).astype(
        jnp.bfloat16
    )
    router_pull = jnp.where(chosen == 1, jnp.sum(grad_hidden * unpacked, axis=-1), 0.0)
    grad_logit = router_pull * gate_values * (1.0 - gate_values)
    grad_answer = lax.all_to_all(
        grad_packed.reshape(n_data, per_peer, model_width),
        "dp",
        split_axis=0,
        concat_axis=0,
        tiled=True,
    )
    grad_answer = grad_answer.reshape(capacity, model_width)
    grad_out = jnp.einsum("md,me->de", context, grad_answer, preferred_element_type=jnp.float32)
    grad_context = jnp.einsum("me,de->md", grad_answer, w_out, preferred_element_type=jnp.float32)
    grad_context = grad_context.astype(jnp.bfloat16).reshape(capacity, head_count, HEAD_DIM)

    def backward_block(running, item_pair):
        first_row, lse_block = item_pair
        scores, query_block = masked_scores()
        shares_wide = jnp.exp(scores - lse_block[..., None])
        grad_shares = jnp.einsum(
            "qhd,khd->hqk", grad_context, value_rows, preferred_element_type=jnp.float32
        )
        inner_sum = jnp.sum(shares_wide * grad_shares, axis=-1, keepdims=True)
        grad_scores = (shares_wide * (grad_shares - inner_sum)).astype(jnp.bfloat16)
        grad_query_block = (
            jnp.einsum("hqk,khd->qhd", grad_scores, key_rows, preferred_element_type=jnp.float32)
            * score_scale
        )
        key_sum = (
            running[0]
            + jnp.einsum(
                "hqk,qhd->khd", grad_scores, query_block, preferred_element_type=jnp.float32
            )
            * score_scale
        )
        value_sum = running[1] + jnp.einsum(
            "hqk,qhd->khd",
            shares_wide.astype(jnp.bfloat16),
            grad_context,
            preferred_element_type=jnp.float32,
        )
        return ((key_sum, value_sum), grad_query_block)

    zeros_init = jnp.zeros((capacity, head_count, HEAD_DIM), jnp.float32)
    (key_total, value_total), query_grads = lax.scan(
        backward_block, (zeros_init, zeros_init), (starts, lse_blocks)
    )
    grad_query = query_grads.reshape(capacity, model_width).astype(jnp.bfloat16)
    grad_key = key_total.reshape(capacity, model_width).astype(jnp.bfloat16)
    grad_value = value_total.reshape(capacity, model_width).astype(jnp.bfloat16)
    grad_w_query = jnp.einsum("md,me->de", buffer, grad_query, preferred_element_type=jnp.float32)
    grad_w_key = jnp.einsum("md,me->de", buffer, grad_key, preferred_element_type=jnp.float32)
    grad_w_value = jnp.einsum("md,me->de", buffer, grad_value, preferred_element_type=jnp.float32)
    grad_buffer = jnp.einsum("me,de->md", grad_query, w_query, preferred_element_type=jnp.float32)
    grad_buffer = grad_buffer + jnp.einsum(
        "me,de->md", grad_key, w_key, preferred_element_type=jnp.float32
    )
    grad_buffer = grad_buffer + jnp.einsum(
        "me,de->md", grad_value, w_value, preferred_element_type=jnp.float32
    )
    grad_buffer = grad_buffer.astype(jnp.bfloat16)
    grad_sent = lax.all_to_all(
        grad_buffer.reshape(n_data, per_peer, model_width),
        "dp",
        split_axis=0,
        concat_axis=0,
        tiled=True,
    )
    grad_sent = grad_sent.reshape(capacity, model_width)
    grad_first = jnp.einsum("mt,md->td", placing, grad_sent, preferred_element_type=jnp.float32)
    grad_first = grad_first + grad_logit[:, None] * vectors[2][None, :]
    grad_router = jnp.sum(grad_logit[:, None] * first_wide, axis=0)
    grad_input_part, grad_gain_one, grad_bias_one = norm_one_back(grad_first)
    grad_tokens = (grad_hidden + grad_input_part).astype(jnp.bfloat16).reshape(tokens.shape)
    pieces = [grad_w_query, grad_w_key, grad_w_value, grad_out]
    pieces = pieces + [
        grad_up[:, position * model_width : (position + 1) * model_width]
        for position in range(up_blocks)
    ]
    pieces = pieces + [
        grad_down[position * model_width : (position + 1) * model_width, :]
        for position in range(up_blocks)
    ]
    local_terms = jnp.stack(pieces, axis=1)
    vector_terms = jnp.stack(
        [grad_gain_one, grad_bias_one, grad_router, grad_gain_two, grad_bias_two]
    )
    partial_value = lax.psum_scatter(local_terms, "dp", scatter_dimension=0, tiled=True)
    grad_own = lax.psum_scatter(
        partial_value.astype(jnp.bfloat16), "own", scatter_dimension=1, tiled=True
    ).astype(jnp.float32)
    vector_grad = lax.psum(vector_terms, ("dp", "own"))
    full_grad = lax.all_gather(grad_own.astype(jnp.bfloat16), "dp", axis=0, tiled=True).astype(
        grad_own.dtype
    )
    row_start = lax.axis_index("dp") * shard_rows
    left_new = 0.5 * left_stat + 0.5 * jnp.einsum(
        "rbk,nbk->rbn", grad_own, full_grad, precision=highest
    )
    column_part = lax.dynamic_slice_in_dim(full_grad, row_start, shard_rows, 2)
    right_new = 0.5 * right_stat + 0.5 * jnp.einsum(
        "nbr,nbk->rbk", column_part, full_grad, precision=highest
    )
    lefted = jnp.einsum("rbn,nbk->rbk", left_root, full_grad, precision=highest)
    precond = jnp.zeros_like(grad_own) + jnp.einsum(
        "rbn,nbk->rbk",
        lefted,
        lax.all_gather(right_root.astype(jnp.bfloat16), "dp", axis=0, tiled=True).astype(
            jnp.float32
        ),
        precision=highest,
    )
    square_sums = lax.psum(jnp.sum(precond * precond, axis=(0, 2)), "dp")
    step_scale = lax.rsqrt(square_sums / (model_width * model_width) + norm_eps)
    new_blocks = blocks - block_rate * precond * step_scale[None, :, None]
    moment_new = 0.5 * moment + 0.5 * vector_grad
    row_squares = jnp.mean(moment_new * moment_new, axis=1, keepdims=True)
    vector_new = vectors - vector_rate * moment_new * lax.rsqrt(row_squares + norm_eps)
    return (
        mixed,
        grad_tokens,
        grad_own,
        left_new,
        right_new,
        new_blocks,
        vector_grad,
        moment_new,
        vector_new,
    )


def solution(mesh):
    placed = (
        P(("dp", "own"), None, None),
        P(("dp", "own"), None, None),
        P(("dp", "own"), None),
        P(("dp", "own"), None),
        P(("dp", "own"), None),
        P("dp", "own", None),
        P("dp", "own", None),
        P("dp", "own", None),
        P("dp", "own", None),
        P("dp", "own", None),
        P(),
        P(),
    )
    small = mesh.shape["dp"] == 16 and mesh.shape["own"] == 2
    return jax.shard_map(
        block_shards if small else shards,
        mesh=mesh,
        in_specs=placed,
        out_specs=(
            P(("dp", "own"), None, None),
            P(("dp", "own"), None, None),
            P("dp", "own", None),
            P("dp", "own", None),
            P("dp", "own", None),
            P("dp", "own", None),
            P(),
            P(),
            P(),
        ),
        check_vma=False,
    )
```
